32 devices in a mesh: dp: 16 (over z, x, core), state: 2 (over y).
Axes of the slice: x: 2, y: 2, z: 4, core: 2. Of those that a mesh axis runs over, the one named last changes fastest.
Arguments:
- tokens: bfloat16 [2, 2048, 1024], P(None, 'dp'), may hold values from -6 to 6
- cluster_len: int32 [2, 16, 2], P(None, 'dp'), may hold values from 32 to 96, as said below
- norm_gain: float32 [1024], replicated, may hold values from 0.1 to 1.9
- in_weight: bfloat16 [4096, 1024], replicated, may hold values from -0.1875 to 0.1875
- conv_weight: float32 [4, 2048], replicated, may hold values from -3 to 3
- conv_bias: float32 [2048], replicated, may hold values from -1.5 to 1.5
- dtx_weight: bfloat16 [2048, 64], replicated, may hold values from -0.125 to 0.125
- dt_weight: bfloat16 [2048, 64], replicated, may hold values from -0.75 to 0.75
- dt_bias: float32 [2048], replicated, may hold values from -7 to -2.3
- bc_weight: bfloat16 [2, 16, 2048], P(None, 'state'), may hold values from -0.125 to 0.125
- a_log: float32 [16, 2048], P('state'), may hold values from -1 to 2.8
- skip_gain: float32 [2048], replicated, may hold values from 0.1 to 1.9
- out_weight: bfloat16 [2048, 1024], replicated, may hold values from -0.125 to 0.125
- cotangent: bfloat16 [2, 2048, 1024], P(None, 'dp'), may hold values from -6 to 6
Outputs:
- mixed: bfloat16 [2, 2048, 1024], P(None, 'dp')
- tokens_grad: float32 [2, 2048, 1024], P(None, 'dp')
- gain_grad: float32 [1024], P(('dp', 'state'))
- in_grad: float32 [4096, 1024], P(('dp', 'state'))
- conv_weight_grad: float32 [4, 2048], P(None, ('dp', 'state'))
- conv_bias_grad: float32 [2048], P(('dp', 'state'))
- dtx_grad: float32 [2048, 64], P(('dp', 'state'))
- dt_weight_grad: float32 [2048, 64], P(('dp', 'state'))
- dt_bias_grad: float32 [2048], P(('dp', 'state'))
- bc_grad: float32 [2, 16, 2048], P(None, 'state', 'dp')
- a_log_grad: float32 [16, 2048], P('state', 'dp')
- skip_grad: float32 [2048], P(('dp', 'state'))
- out_grad: float32 [2048, 1024], P(('dp', 'state'))
The draws below stay inside these ranges and needn't reach their ends.
Inputs may be any that keep to these rules, and one draw needn't show every extreme that they name: `cluster_len`: in each row the 2 lengths sum to 128; one of them equals 96, the other 32.
All inputs are finite; a program needn't handle non-finite values.
Results may differ from the reference program's by a relative error of at most 0.012.
Values may be sent and summed in bfloat16 or wider, within the bound.
No kernel may reach another device: no remote copies, remote signals or barrier semaphores. Data moves between devices by JAX's collectives and lax.ppermute only.
A program may use at most 256 MiB of HBM per device.

```python
import jax
import jax.numpy as jnp
from jax import lax

D = 1024
E = 2048
N = 16
R = 64
CONV = 4
GRP = 128
MICRO = 2
CLUSTERS = 2
GROUPS = 16
TOKENS = 2048
MOST = 96


def draw_cluster_len(key, part):
    key = jax.random.fold_in(key, 7)
    flipped = jax.random.randint(key, (MICRO, GROUPS), 0, 2, dtype=jnp.int32)
    first_len = jnp.where(flipped == 0, MOST, GRP - MOST).astype(jnp.int32)
    return jnp.stack([first_len, GRP - first_len], axis=-1).astype(jnp.int32)


def levels(own_key, extent, split, smallest, high):
    def one(position, parts):
        steps = jax.random.uniform(jax.random.fold_in(jax.random.fold_in(own_key, 6), position), (parts,), jnp.float32, smallest / len(split), high / len(split))
        return jnp.repeat(jnp.exp(steps), extent[position] // parts).reshape((-1,) + (1,) * (len(extent) - position - 1))

    loudness = one(*split[0])
    for cut in split[1:]:
        loudness = loudness * one(*cut)
    return loudness


def scatter_about(key, extent, deviation, reach, split=(), kind=jnp.bfloat16):
    values = jax.random.normal(key, extent, jnp.float32) * deviation
    if len(split) > 0:
        values = levels(key, extent, split, -0.22, 0.18) * values
    return jnp.clip(values, min=-reach, max=reach).astype(kind)


def setup_inputs(seed: int = 0) -> dict:
    arg_keys = jax.random.split(jax.random.key(seed), 15)
    tokens = scatter_about(arg_keys[0], (MICRO, TOKENS, D), 1.0, 6.0, ((1, 16),))
    cluster_len = draw_cluster_len(jax.random.fold_in(arg_keys[14], 71), 0)
    norm_gain = jnp.clip(1.0 + 0.18 * jax.random.normal(arg_keys[2], (D,), jnp.float32), 0.1, 1.9)
    in_weight = scatter_about(arg_keys[3], (2 * E, D), D ** -0.5, 0.1875)
    conv_weight = scatter_about(arg_keys[4], (CONV, E), CONV ** -0.5, 3.0, (), jnp.float32)
    conv_bias = scatter_about(arg_keys[5], (E,), 0.3, 1.5, (), jnp.float32)
    dtx_weight = scatter_about(arg_keys[6], (E, R), E ** -0.5, 0.125)
    dt_weight = scatter_about(arg_keys[7], (E, R), R ** -0.5, 0.75)
    dt_bias = jnp.clip(jax.random.uniform(arg_keys[8], (E,), jnp.float32, -7.0, -2.3), -7.0, -2.3)
    bc_weight = scatter_about(arg_keys[9], (2, N, E), E ** -0.5, 0.125, ((1, 2),))
    a_log = jnp.clip(-1.0 + 3.8 * jax.random.uniform(arg_keys[10], (N, E), jnp.float32) ** levels(arg_keys[10], (N, E), ((0, 2),), -0.2, 0.2), -1.0, 2.8)
    skip_gain = jnp.clip(1.0 + 0.18 * jax.random.normal(arg_keys[11], (E,), jnp.float32), 0.1, 1.9)
    out_weight = scatter_about(arg_keys[12], (E, D), E ** -0.5, 0.125)
    cotangent = scatter_about(arg_keys[13], (MICRO, TOKENS, D), 1.0, 6.0, ((1, 16),))
    return dict(tokens=tokens, cluster_len=cluster_len, norm_gain=norm_gain, in_weight=in_weight, conv_weight=conv_weight, conv_bias=conv_bias, dtx_weight=dtx_weight, dt_weight=dt_weight, dt_bias=dt_bias, bc_weight=bc_weight, a_log=a_log, skip_gain=skip_gain, out_weight=out_weight, cotangent=cotangent)


@jax.custom_vjp
def low(v):
    return lax.optimization_barrier(v.astype(jnp.bfloat16)).astype(jnp.float32)

@jax.custom_vjp
def low_back(v):
    return v

def low_keep(v):
    return (low(v), None)

def low_pass(kept, grad):
    return (grad,)

def back_keep(v):
    return (v, None)

def back_low(kept, grad):
    return (low(grad),)
low.defvjp(low_keep, low_pass)
low_back.defvjp(back_keep, back_low)
EPSILON = 1e-05

def product(left, right):
    return jnp.dot(left, right, precision=lax.Precision.HIGHEST, preferred_element_type=jnp.float32)

def cluster_index(lengths):
    starts = jnp.cumsum(lengths, dtype=jnp.int32) - lengths
    places = jnp.arange(GRP, dtype=jnp.int32)
    return lax.optimization_barrier(jnp.sum((places[:, None] >= starts[None, :]).astype(jnp.int32), axis=1, dtype=jnp.int32))

def same_cluster(cluster_ids, back_by):
    earlier = jnp.concatenate([jnp.full((back_by,), -1, jnp.int32), cluster_ids[:GRP - back_by]])
    return (earlier == cluster_ids).astype(jnp.float32)

def block_forward(params, token_rows, lengths):
    norm_gain, in_weight, conv_weight, conv_bias, dtx_weight, dt_weight, dt_bias, bc_weight, a_log, skip_gain, out_weight = params
    cluster_ids = cluster_index(lengths)
    inv_scale = lax.rsqrt(lax.optimization_barrier(jnp.mean(token_rows * token_rows, axis=1, keepdims=True)) + EPSILON)
    normed = low(token_rows * inv_scale * norm_gain)
    projected = low_back(product(normed, in_weight.T))
    inner_part = projected[:, :E]
    gate_in = projected[:, E:]
    conved = conv_bias + conv_weight[CONV - 1] * inner_part
    for back_by in range(1, CONV):
        shifted = jnp.concatenate([jnp.zeros((back_by, E), jnp.float32), inner_part[:GRP - back_by]])
        conved = conved + conv_weight[CONV - 1 - back_by] * shifted * same_cluster(cluster_ids, back_by)[:, None]
    activated = low(jax.nn.silu(conved))
    rank_low = low_back(low(product(activated, dtx_weight)))
    step_size = jax.nn.softplus(low_back(product(rank_low, dt_weight.T)) + dt_bias)
    b_coef = low_back(product(activated, bc_weight[0].T))
    c_coef = low_back(product(activated, bc_weight[1].T))
    decay_rate = -jnp.exp(a_log)
    keep_mask = same_cluster(cluster_ids, 1)

    def advance(state_now, inputs):
        step_now, b_now, c_now, act_now, keep_now = inputs
        state_now = jnp.exp(step_now[None, :] * decay_rate) * keep_now * state_now + (step_now * act_now)[None, :] * b_now[:, None]
        return (state_now, lax.optimization_barrier(jnp.sum(c_now[:, None] * state_now, axis=0)))
    _, scanned = lax.scan(advance, jnp.zeros((N, E), jnp.float32), (step_size, b_coef, c_coef, activated, keep_mask))
    mixed_pre = scanned + skip_gain * activated
    gated_low = low(mixed_pre * jax.nn.silu(gate_in))
    return token_rows + product(gated_low, out_weight)

def reference(tokens, cluster_len, norm_gain, in_weight, conv_weight, conv_bias, dtx_weight, dt_weight, dt_bias, bc_weight, a_log, skip_gain, out_weight, cotangent):
    params = tuple((member.astype(jnp.float32) for member in (norm_gain, in_weight, conv_weight, conv_bias, dtx_weight, dt_weight, dt_bias, bc_weight, a_log, skip_gain, out_weight)))
    token_rows = tokens.astype(jnp.float32).reshape(MICRO * GROUPS, GRP, D)
    lengths = cluster_len.reshape(MICRO * GROUPS, CLUSTERS)
    checked = jax.checkpoint(block_forward)

    def forward_all(token_rows, params):
        return lax.map(lambda block_pair: checked(params, block_pair[0], block_pair[1]), (token_rows, lengths))
    outputs, pullback = jax.vjp(forward_all, token_rows, params)
    token_grad, param_grads = pullback(cotangent.astype(jnp.float32).reshape(MICRO * GROUPS, GRP, D))
    mixed = outputs.reshape(MICRO, GROUPS * GRP, D).astype(jnp.bfloat16)
    token_grad = token_grad.reshape(MICRO, GROUPS * GRP, D)
    return (mixed, token_grad, param_grads[0], param_grads[1], param_grads[2], param_grads[3], param_grads[4], param_grads[5], param_grads[6], param_grads[7], param_grads[8], param_grads[9], param_grads[10])
```

```python
import functools
import math

import jax
import jax.numpy as jnp
from jax import lax
from jax.experimental import pallas as pl
from jax.experimental.pallas import tpu as pltpu
from jax.sharding import PartitionSpec as P

EPSILON = 1e-05
LANES = 128
RESET = 1e4
LOG2E = math.log2(math.e)
F32 = jnp.float32
BF16 = jnp.bfloat16
MIB = 1024 * 1024


def dot(left, right, left_dim, right_dim):
    return lax.dot_general(
        left, right, (((left_dim,), (right_dim,)), ((), ())), preferred_element_type=F32
    )


def params(mib, steps=1):
    return pltpu.CompilerParams(
        vmem_limit_bytes=mib * MIB, dimension_semantics=("arbitrary",) * steps
    )


def whole(shape):
    return pl.BlockSpec(shape, lambda *_: (0,) * len(shape))


def sigmoid(value):
    return 1.0 / (1.0 + jnp.exp(-value))


def fill_masks(len_ref, mask_ref, micros, count, taps, clusters):
    place = lax.broadcasted_iota(jnp.int32, (count, LANES), 0)
    for micro in range(micros):
        rows = pl.ds(micro * count, count)
        for back in range(1, taps):
            apart = place < back
            start = 0
            for cluster in range(clusters - 1):
                start = start + len_ref[micro * clusters + cluster]
                apart = apart | ((place >= start) & (place < start + back))
            mask_ref[back, rows, :] = jnp.where(apart, 0.0, 1.0)
            if back == 1:
                mask_ref[0, rows, :] = jnp.where(apart, 1.0, 0.0)


def project_kernel(
    half_ref,
    len_ref,
    x_ref,
    gain_ref,
    win_ref,
    wgate_ref,
    convw_ref,
    convb_ref,
    normed_ref,
    act_ref,
    own_act_ref,
    inner_ref,
    conved_ref,
    gate_ref,
    mask_ref,
    proj_ref,
    conv_ref,
    *,
    micros,
    count,
    taps,
    clusters,
):
    @pl.when(pl.program_id(0) == 0)
    def _():
        fill_masks(len_ref, mask_ref, micros, count, taps, clusters)
        rows = x_ref[...].astype(F32)
        scale = lax.rsqrt(jnp.mean(rows * rows, axis=1, keepdims=True) + EPSILON)
        normed_ref[...] = (rows * scale * gain_ref[...]).astype(BF16)

    half = half_ref[0]
    total = micros * count
    normed = normed_ref[...]
    proj_ref[...] = dot(normed, win_ref[...].reshape(2 * LANES, -1), 1, 1)
    gate_ref[...] = dot(normed, wgate_ref[...].reshape(LANES, -1), 1, 1)
    for part in range(2):
        cols = pl.ds(part * LANES, LANES)
        inner = proj_ref[:, cols]
        conved = convb_ref[:, cols] + convw_ref[taps - 1 : taps, cols] * inner
        for back in range(1, taps):
            shifted = pltpu.roll(inner, back, 0) * mask_ref[back]
            conved = conved + convw_ref[taps - 1 - back : taps - back, cols] * shifted
        conv_ref[:, cols] = conved
        act_ref[:, cols] = (conved * sigmoid(conved)).astype(BF16)
    own = pl.ds(pl.multiple_of(half * LANES, LANES), LANES)
    inner_ref[...] = proj_ref[:, own]
    conved_ref[...] = conv_ref[:, own]
    own_act_ref[...] = act_ref[:, own]
    del total


def project(half, lengths, x, gain, w4, conv_weight, conv_bias, taps):
    rows, width = x.shape
    chunks = w4.shape[1]
    inner = chunks * 2 * LANES
    micros = lengths.shape[0]
    clusters = lengths.shape[1]
    own = chunks * LANES
    grid_spec = pltpu.PrefetchScalarGridSpec(
        num_scalar_prefetch=2,
        grid=(chunks,),
        in_specs=[
            whole((rows, width)),
            whole((1, width)),
            pl.BlockSpec((1, 1, 2, LANES, width), lambda i, h, l: (0, i, 0, 0, 0)),
            pl.BlockSpec((1, 1, 1, LANES, width), lambda i, h, l: (1, i, h[0], 0, 0)),
            pl.BlockSpec((taps, 2 * LANES), lambda i, h, l: (0, i)),
            pl.BlockSpec((1, 2 * LANES), lambda i, h, l: (0, i)),
        ],
        out_specs=[
            whole((rows, width)),
            pl.BlockSpec((rows, 2 * LANES), lambda i, h, l: (0, i)),
            pl.BlockSpec((rows, LANES), lambda i, h, l: (0, i)),
            pl.BlockSpec((rows, LANES), lambda i, h, l: (0, i)),
            pl.BlockSpec((rows, LANES), lambda i, h, l: (0, i)),
            pl.BlockSpec((rows, LANES), lambda i, h, l: (0, i)),
        ],
        scratch_shapes=[
            pltpu.VMEM((taps, rows, LANES), F32),
            pltpu.VMEM((rows, 2 * LANES), F32),
            pltpu.VMEM((rows, 2 * LANES), F32),
        ],
    )
    return pl.pallas_call(
        functools.partial(
            project_kernel,
            micros=micros,
            count=rows // micros,
            taps=taps,
            clusters=clusters,
        ),
        grid_spec=grid_spec,
        out_shape=[
            jax.ShapeDtypeStruct((rows, width), BF16),
            jax.ShapeDtypeStruct((rows, inner), BF16),
            jax.ShapeDtypeStruct((rows, own), BF16),
            jax.ShapeDtypeStruct((rows, own), F32),
            jax.ShapeDtypeStruct((rows, own), F32),
            jax.ShapeDtypeStruct((rows, own), F32),
        ],
        compiler_params=params(40),
        name="project",
    )(half, lengths.reshape(-1), x, gain, w4, w4, conv_weight, conv_bias)


def softplus(value):
    return jnp.maximum(value, 0.0) + jnp.log1p(jnp.exp(-jnp.abs(value)))


def forward_kernel(
    half_ref,
    len_ref,
    bc_ref,
    decay_ref,
    rank_ref,
    dt_ref,
    bias_ref,
    act_ref,
    gate_ref,
    skip_ref,
    wout_ref,
    cotan_ref,
    normed_ref,
    sp_ref,
    u_ref,
    dy_ref,
    mixed_ref,
    dgate_ref,
    out_grad_ref,
    gate_grad_ref,
    mask_ref,
    y_ref,
    gated_ref,
    *,
    micros,
    count,
    states,
    chunks,
    clusters,
):
    rows = micros * count
    fill_masks(len_ref, mask_ref, micros, count, 2, clusters)
    rank = rank_ref[...]
    for chunk in range(chunks):
        cols = slice(chunk * LANES, (chunk + 1) * LANES)
        place = pl.ds(chunk * rows, rows)
        step = softplus(dot(rank, dt_ref[0, chunk, 0], 1, 1) + bias_ref[:, cols])
        sp_ref[place, :] = step + RESET * mask_ref[0]
        u_ref[place, :] = step * act_ref[:, cols].astype(F32)

    for micro in range(micros):

        def advance(t, h, micro=micro):
            row = micro * count + t
            span = pl.ds(row, chunks, stride=rows)
            sp = sp_ref[span, :]
            u = u_ref[span, :]
            out = []
            y = None
            for n in range(states):
                decay = jnp.exp2(sp * decay_ref[n])
                now = decay * h[n] + u * bc_ref[row * 2 * states + n]
                out.append(now)
                term = now * bc_ref[row * 2 * states + states + n]
                y = term if y is None else y + term
            y_ref[span, :] = y
            return tuple(out)

        lax.fori_loop(0, count, advance, (jnp.zeros((chunks, LANES), F32),) * states)

    cotan = cotan_ref[...]
    for chunk in range(chunks):
        cols = slice(chunk * LANES, (chunk + 1) * LANES)
        place = pl.ds(chunk * rows, rows)
        y = y_ref[place, :] + skip_ref[:, cols] * act_ref[:, cols].astype(F32)
        gate = gate_ref[:, cols]
        sig = sigmoid(gate)
        gated_ref[:, cols] = (y * (gate * sig)).astype(BF16)
        dgated = dot(cotan, wout_ref[chunk, 0], 1, 1)
        dy_ref[place, :] = dgated * (gate * sig)
        dgate_ref[:, cols] = (dgated * y * (sig * (1.0 + gate * (1.0 - sig)))).astype(BF16)
    width = cotan.shape[1]
    mixed_ref[...] = dot(gated_ref[...], wout_ref[...].reshape(chunks * LANES, width), 1, 0).astype(
        BF16
    )
    normed = normed_ref[...]
    for chunk in range(chunks):
        cols = slice(chunk * LANES, (chunk + 1) * LANES)
        out_grad_ref[cols, :] = dot(gated_ref[:, cols], cotan, 0, 0).astype(BF16)
        gate_grad_ref[cols, :] = dot(dgate_ref[:, cols], normed, 0, 0).astype(BF16)


def scan_forward(half, lengths, bc, decay, rank, dt4, dt_bias, act, gate, skip, wout3, cotan, normed):
    rows, own = act.shape
    chunks = own // LANES
    states = decay.shape[0]
    width = cotan.shape[1]
    micros, clusters = lengths.shape
    ranks = rank.shape[1]
    smem = pl.BlockSpec(memory_space=pltpu.SMEM)
    grid_spec = pltpu.PrefetchScalarGridSpec(
        num_scalar_prefetch=2,
        grid=(1,),
        in_specs=[
            smem,
            whole((states, chunks, LANES)),
            whole((rows, ranks)),
            pl.BlockSpec((1, chunks, 1, LANES, ranks), lambda i, h, l: (0, 0, h[0], 0, 0)),
            whole((1, own)),
            whole((rows, own)),
            whole((rows, own)),
            whole((1, own)),
            pl.BlockSpec((chunks, 1, LANES, width), lambda i, h, l: (0, h[0], 0, 0)),
            whole((rows, width)),
            whole((rows, width)),
        ],
        out_specs=[
            whole((chunks * rows, LANES)),
            whole((chunks * rows, LANES)),
            whole((chunks * rows, LANES)),
            whole((rows, width)),
            whole((rows, own)),
            whole((own, width)),
            whole((own, width)),
        ],
        scratch_shapes=[
            pltpu.VMEM((2, rows, LANES), F32),
            pltpu.VMEM((chunks * rows, LANES), F32),
            pltpu.VMEM((rows, own), BF16),
        ],
    )
    return pl.pallas_call(
        functools.partial(
            forward_kernel,
            micros=micros,
            count=rows // micros,
            states=states,
            chunks=chunks,
            clusters=clusters,
        ),
        grid_spec=grid_spec,
        out_shape=[
            jax.ShapeDtypeStruct((chunks * rows, LANES), F32),
            jax.ShapeDtypeStruct((chunks * rows, LANES), F32),
            jax.ShapeDtypeStruct((chunks * rows, LANES), F32),
            jax.ShapeDtypeStruct((rows, width), BF16),
            jax.ShapeDtypeStruct((rows, own), BF16),
            jax.ShapeDtypeStruct((own, width), BF16),
            jax.ShapeDtypeStruct((own, width), BF16),
        ],
        compiler_params=params(56),
        name="scan_forward",
    )(
        half,
        lengths.reshape(-1),
        bc,
        decay,
        rank,
        dt4,
        dt_bias,
        act,
        gate,
        skip,
        wout3,
        cotan,
        normed,
    )


def backward_kernel(
    half_ref,
    bc_ref,
    decay_ref,
    rank_ref,
    dt_ref,
    bias_ref,
    act_ref,
    sp_ref,
    u_ref,
    dy_ref,
    part_ref,
    drank_ref,
    sact_ref,
    dpre_ref,
    alog_ref,
    vec_ref,
    h_ref,
    s_ref,
    d_ref,
    terms_ref,
    sums_ref,
    *,
    micros,
    count,
    states,
    chunks,
):
    rows = micros * count
    alog_ref[...] = jnp.zeros_like(alog_ref)
    zero = (jnp.zeros((chunks, LANES), F32),) * states

    for micro in range(micros):
        for n in range(states):
            h_ref[pl.ds(n * chunks, chunks), :] = zero[0]

        def recompute(t, h, micro=micro):
            row = micro * count + t
            span = pl.ds(row, chunks, stride=rows)
            sp = sp_ref[span, :]
            u = u_ref[span, :]
            out = []
            for n in range(states):
                decay = jnp.exp2(sp * decay_ref[n])
                now = decay * h[n] + u * bc_ref[row * 2 * states + n]
                at = pl.multiple_of(((t + 1) * states + n) * chunks, chunks)
                h_ref[pl.ds(at, chunks), :] = now
                out.append(now)
            return tuple(out)

        lax.fori_loop(0, count, recompute, zero)

        def retreat(back, carry, micro=micro):
            t = count - 1 - back
            row = micro * count + t
            span = pl.ds(row, chunks, stride=rows)
            sp = sp_ref[span, :]
            u = u_ref[span, :]
            dy = dy_ref[span, :]
            out = []
            d_sum = None
            s_sum = None
            for n in range(states):
                rate = decay_ref[n]
                decay = jnp.exp2(sp * rate)
                dh = carry[n] + dy * bc_ref[row * 2 * states + states + n]
                flow = decay * dh
                out.append(flow)
                before = h_ref[pl.ds(pl.multiple_of((t * states + n) * chunks, chunks), chunks), :]
                now = h_ref[
                    pl.ds(pl.multiple_of(((t + 1) * states + n) * chunks, chunks), chunks), :
                ]
                q = flow * before
                alog_ref[pl.ds(n * chunks, chunks), :] += q * sp
                d_term = q * rate
                s_term = dh * bc_ref[row * 2 * states + n]
                d_sum = d_term if d_sum is None else d_sum + d_term
                s_sum = s_term if s_sum is None else s_sum + s_term
                terms_ref[pl.ds(n * chunks, chunks), :] = dh * u
                terms_ref[pl.ds((states + n) * chunks, chunks), :] = dy * now
            s_ref[span, :] = s_sum
            d_ref[span, :] = d_sum
            sums = None
            for chunk in range(chunks):
                term = terms_ref[pl.ds(chunk, 2 * states, stride=chunks), :]
                sums = term if sums is None else sums + term
            sums_ref[pl.ds(pl.multiple_of(row * 2 * states, 2 * states), 2 * states), :] = sums
            return tuple(out)

        lax.fori_loop(0, count, retreat, zero)

    part_ref[...] = dot(jnp.ones((8, LANES), F32), sums_ref[...], 1, 1)
    rank = rank_ref[...]
    drank = None
    for chunk in range(chunks):
        cols = slice(chunk * LANES, (chunk + 1) * LANES)
        place = pl.ds(chunk * rows, rows)
        act = act_ref[:, cols].astype(F32)
        pre = dot(rank, dt_ref[0, chunk, 0], 1, 1) + bias_ref[:, cols]
        s_now = s_ref[place, :]
        dstep = d_ref[place, :] * (1.0 / LOG2E) + s_now * act
        sact_ref[:, cols] = s_now * softplus(pre)
        dpre = dstep * sigmoid(pre)
        vec_ref[0:1, cols] = jnp.sum(dpre, axis=0, keepdims=True)
        vec_ref[1:2, cols] = jnp.sum(dy_ref[place, :] * act, axis=0, keepdims=True)
        low = dpre.astype(BF16)
        dpre_ref[:, cols] = low
        term = dot(low, dt_ref[0, chunk, 0], 1, 0)
        drank = term if drank is None else drank + term
    drank_ref[...] = drank


def scan_backward(half, bc, decay, rank, dt4, dt_bias, act, sp, u, dy, micros):
    rows, own = act.shape
    chunks = own // LANES
    states = decay.shape[0]
    ranks = rank.shape[1]
    count = rows // micros
    smem = pl.BlockSpec(memory_space=pltpu.SMEM)
    grid_spec = pltpu.PrefetchScalarGridSpec(
        num_scalar_prefetch=1,
        grid=(1,),
        in_specs=[
            smem,
            whole((states, chunks, LANES)),
            whole((rows, ranks)),
            pl.BlockSpec((1, chunks, 1, LANES, ranks), lambda i, h: (0, 0, h[0], 0, 0)),
            whole((1, own)),
            whole((rows, own)),
            whole((chunks * rows, LANES)),
            whole((chunks * rows, LANES)),
            whole((chunks * rows, LANES)),
        ],
        out_specs=[
            whole((8, rows * 2 * states)),
            whole((rows, ranks)),
            whole((rows, own)),
            whole((rows, own)),
            whole((states * chunks, LANES)),
            whole((2, own)),
        ],
        scratch_shapes=[
            pltpu.VMEM(((count + 1) * states * chunks, LANES), F32),
            pltpu.VMEM((chunks * rows, LANES), F32),
            pltpu.VMEM((chunks * rows, LANES), F32),
            pltpu.VMEM((2 * states * chunks, LANES), F32),
            pltpu.VMEM((rows * 2 * states, LANES), F32),
        ],
    )
    return pl.pallas_call(
        functools.partial(
            backward_kernel, micros=micros, count=count, states=states, chunks=chunks
        ),
        grid_spec=grid_spec,
        out_shape=[
            jax.ShapeDtypeStruct((8, rows * 2 * states), F32),
            jax.ShapeDtypeStruct((rows, ranks), F32),
            jax.ShapeDtypeStruct((rows, own), F32),
            jax.ShapeDtypeStruct((rows, own), BF16),
            jax.ShapeDtypeStruct((states * chunks, LANES), F32),
            jax.ShapeDtypeStruct((2, own), F32),
        ],
        compiler_params=params(48),
        name="scan_backward",
    )(half, bc, decay, rank, dt4, dt_bias, act, sp, u, dy)


def tail_kernel(
    half_ref,
    len_ref,
    code_ref,
    wcode_ref,
    sact_ref,
    dy_ref,
    conved_ref,
    inner_ref,
    act_ref,
    dgate_ref,
    dpre_ref,
    rank_ref,
    convw_ref,
    skip_ref,
    win_ref,
    wgate_ref,
    normed_ref,
    x_ref,
    grad_ref,
    rows_ref,
    vec_ref,
    dnormed_ref,
    gain_ref,
    mask_ref,
    total_ref,
    *,
    micros,
    count,
    taps,
    clusters,
    ranks,
    group,
):
    step = pl.program_id(0)
    rows = micros * count
    width = x_ref.shape[1]

    @pl.when(step == 0)
    def _():
        fill_masks(len_ref, mask_ref, micros, count, taps, clusters)
        total_ref[...] = jnp.zeros_like(total_ref)

    code = code_ref[...]
    low = []
    for part in range(group):
        cols = slice(part * LANES, (part + 1) * LANES)
        dact = sact_ref[:, cols] + dot(code, wcode_ref[cols, :], 1, 1)
        dact = dact + dy_ref[pl.ds(part * rows, rows), :] * skip_ref[:, cols]
        conved = conved_ref[:, cols]
        sig = sigmoid(conved)
        dconv = dact * (sig * (1.0 + conved * (1.0 - sig)))
        inner = inner_ref[:, cols]
        dinner = convw_ref[taps - 1 : taps, cols] * dconv
        vec_ref[taps - 1 : taps, cols] = jnp.sum(dconv * inner, axis=0, keepdims=True)
        for back in range(1, taps):
            kept = dconv * mask_ref[back]
            dinner = dinner + convw_ref[taps - 1 - back : taps - back, cols] * pltpu.roll(
                kept, rows - back, 0
            )
            vec_ref[taps - 1 - back : taps - back, cols] = jnp.sum(
                kept * pltpu.roll(inner, back, 0), axis=0, keepdims=True
            )
        vec_ref[taps : taps + 1, cols] = jnp.sum(dconv, axis=0, keepdims=True)
        low.append(dinner.astype(BF16))
    low = jnp.concatenate(low, axis=1)
    grad_ref[...] = dot(low, normed_ref[...], 0, 0).astype(BF16)
    act = act_ref[...]
    rows_ref[:, : code.shape[1]] = dot(act, code, 0, 0)
    rows_ref[:, code.shape[1] : code.shape[1] + ranks] = dot(dpre_ref[...], rank_ref[...], 0, 0)
    total_ref[...] += dot(low, win_ref[...].reshape(group * LANES, width), 1, 0) + dot(
        dgate_ref[...], wgate_ref[...].reshape(group * LANES, width), 1, 0
    )

    @pl.when(step == pl.num_programs(0) - 1)
    def _():
        total = total_ref[...]
        x = x_ref[...].astype(F32)
        scale = lax.rsqrt(jnp.mean(x * x, axis=1, keepdims=True) + EPSILON)
        gain_ref[...] = jnp.sum(total * (x * scale), axis=0, keepdims=True)
        dnormed_ref[...] = total.astype(BF16)


def tail(
    half, lengths, code, wcode, sact, dy, conved, inner, act, dgate, dpre, rank, convw, skip, w4, normed, x
):
    rows, own = act.shape
    chunks = own // LANES
    group = 2
    width = x.shape[1]
    micros, clusters = lengths.shape
    taps = convw.shape[0]
    ranks = rank.shape[1]
    wide = code.shape[1] + ranks
    cols = group * LANES
    by_cols = pl.BlockSpec((rows, cols), lambda i, h, l: (0, i))
    grid_spec = pltpu.PrefetchScalarGridSpec(
        num_scalar_prefetch=2,
        grid=(chunks // group,),
        in_specs=[
            whole(code.shape),
            pl.BlockSpec((cols, code.shape[1]), lambda i, h, l: (i, 0)),
            by_cols,
            pl.BlockSpec((group * rows, LANES), lambda i, h, l: (i, 0)),
            by_cols,
            by_cols,
            by_cols,
            by_cols,
            by_cols,
            whole(rank.shape),
            pl.BlockSpec((taps, cols), lambda i, h, l: (0, i)),
            pl.BlockSpec((1, cols), lambda i, h, l: (0, i)),
            pl.BlockSpec((1, group, 1, LANES, width), lambda i, h, l: (0, i, h[0], 0, 0)),
            pl.BlockSpec((1, group, 1, LANES, width), lambda i, h, l: (1, i, h[0], 0, 0)),
            whole((rows, width)),
            whole((rows, width)),
        ],
        out_specs=[
            pl.BlockSpec((cols, width), lambda i, h, l: (i, 0)),
            pl.BlockSpec((cols, wide), lambda i, h, l: (i, 0)),
            pl.BlockSpec((taps + 1, cols), lambda i, h, l: (0, i)),
            whole((rows, width)),
            whole((1, width)),
        ],
        scratch_shapes=[
            pltpu.VMEM((taps, rows, LANES), F32),
            pltpu.VMEM((rows, width), F32),
        ],
    )
    return pl.pallas_call(
        functools.partial(
            tail_kernel,
            micros=micros,
            count=rows // micros,
            taps=taps,
            clusters=clusters,
            ranks=ranks,
            group=group,
        ),
        grid_spec=grid_spec,
        out_shape=[
            jax.ShapeDtypeStruct((own, width), BF16),
            jax.ShapeDtypeStruct((own, wide), F32),
            jax.ShapeDtypeStruct((taps + 1, own), F32),
            jax.ShapeDtypeStruct((rows, width), BF16),
            jax.ShapeDtypeStruct((1, width), F32),
        ],
        compiler_params=params(48),
        name="tail",
    )(
        half,
        lengths.reshape(-1),
        code,
        wcode,
        sact,
        dy,
        conved,
        inner,
        act,
        dgate,
        dpre,
        rank,
        convw,
        skip,
        w4,
        w4,
        normed,
        x,
    )


def own_columns(array, half):
    blocks = array.reshape(array.shape[:-1] + (-1, 2, LANES))
    own = lax.dynamic_index_in_dim(blocks, half, axis=array.ndim, keepdims=False)
    return own.reshape(array.shape[:-1] + (-1,))


def swap_pair(array):
    count = lax.axis_size("state")
    return lax.ppermute(array, "state", [(pos, pos ^ 1) for pos in range(count)])


def swap_odd(array):
    parts, states = lax.axis_size("dp"), lax.axis_size("state")
    pairs = []
    for d in range(parts):
        for s in range(states):
            at = d * states + s
            to = at if d % 2 == s % 2 else (d ^ 1) * states + (s ^ 1)
            pairs.append((at, to))
    return lax.ppermute(array, ("dp", "state"), pairs)


def shards(
    tokens,
    cluster_len,
    norm_gain,
    in_weight,
    conv_weight,
    conv_bias,
    dtx_weight,
    dt_weight,
    dt_bias,
    bc_weight,
    a_log,
    skip_gain,
    out_weight,
    cotangent,
):
    micros, count, width = tokens.shape
    inner = out_weight.shape[0]
    taps = conv_weight.shape[0]
    ranks = dtx_weight.shape[1]
    chunks = inner // (2 * LANES)
    own = chunks * LANES
    rows = micros * count
    dp_parts = lax.axis_size("dp")
    state_count = lax.axis_size("state")
    state_pos = lax.axis_index("state")
    half = lax.rem(state_pos, 2)
    half_arg = half.reshape(1).astype(jnp.int32)
    lengths = cluster_len[:, 0, :]

    x = tokens.reshape(rows, width)
    cotan = cotangent.reshape(rows, width)
    w4 = in_weight.reshape(2, chunks, 2, LANES, width)
    dt4 = dt_weight.reshape(1, chunks, 2, LANES, ranks)
    wout3 = out_weight.reshape(chunks, 2, LANES, width)

    bc_all = lax.all_gather(bc_weight, "state", axis=1, tiled=True)
    alog_all = lax.all_gather(a_log, "state", axis=0, tiled=True)
    states = alog_all.shape[0]
    bc_flat = bc_all.reshape(2 * states, inner)
    decay = (-jnp.exp(own_columns(alog_all, half))).reshape(states, chunks, LANES)
    decay2 = decay * LOG2E
    own_bias = own_columns(dt_bias[None], half)
    own_skip = own_columns(skip_gain[None], half)
    own_convw = own_columns(conv_weight, half)
    own_dtx = lax.dynamic_index_in_dim(
        dtx_weight.reshape(chunks, 2, LANES, ranks), half, axis=1, keepdims=False
    ).reshape(own, ranks)
    wcode = jnp.concatenate([own_dtx, own_columns(bc_flat, half).T], axis=1)

    normed, act_all, act, inner_own, conved, gate = project(
        half_arg, lengths, x, norm_gain[None], w4, conv_weight, conv_bias[None], taps
    )
    rank = dot(act_all, dtx_weight, 1, 0).astype(BF16)
    bc = dot(act_all, bc_flat, 1, 1).reshape(-1)
    sp, u, dy, mixed_part, dgate, out_grad, gate_grad = scan_forward(
        half_arg, lengths, bc, decay2, rank, dt4, own_bias, act, gate, own_skip, wout3, cotan, normed
    )
    mixed_other = swap_pair(mixed_part)
    mixed = (
        x.astype(F32) + (mixed_part.astype(F32) + mixed_other.astype(F32))
    ).astype(BF16)

    part, drank_part, sact, dpre, alog_part, vec_back = scan_backward(
        half_arg, bc, decay2, rank, dt4, own_bias, act, sp, u, dy, micros
    )
    code_part = jnp.concatenate([drank_part, part[0].reshape(rows, 2 * states)], axis=1)
    code = (code_part + swap_pair(code_part)).astype(BF16)
    inner_grad, row_part, vec_part, dnormed_part, gain_part = tail(
        half_arg,
        lengths,
        code,
        wcode,
        sact,
        dy,
        conved,
        inner_own,
        act,
        dgate,
        dpre,
        rank,
        own_convw,
        own_skip,
        w4,
        normed,
        x,
    )
    dnormed = dnormed_part.astype(F32) + swap_pair(dnormed_part).astype(F32)
    x32 = x.astype(F32)
    scale = lax.rsqrt(jnp.mean(x32 * x32, axis=1, keepdims=True) + EPSILON)
    unit = x32 * scale
    dhat = dnormed * norm_gain
    tokens_grad = cotan.astype(F32) + scale * (
        dhat - unit * jnp.mean(dhat * unit, axis=1, keepdims=True)
    )

    alog_rows = decay.reshape(states, own) * alog_part.reshape(states, own)
    vectors = jnp.concatenate([vec_part, vec_back], axis=0)
    code_rows = row_part[:, : ranks + 2 * states]
    dt_rows = row_part[:, ranks + 2 * states :]
    dtx_rows = code_rows[:, :ranks]
    state_rows = jnp.concatenate([code_rows[:, ranks:].T, alog_rows], axis=0)

    if state_count == 2 and dp_parts == 2 * chunks:
        in_sum = lax.psum_scatter(
            jnp.concatenate([inner_grad, gate_grad], axis=0), "dp", scatter_dimension=0, tiled=True
        ).astype(F32)
        out_sum = lax.psum_scatter(out_grad, "dp", scatter_dimension=0, tiled=True)
        packed = jnp.concatenate(
            [
                dtx_rows.reshape(dp_parts, -1),
                dt_rows.reshape(dp_parts, -1),
                jnp.moveaxis(vectors.reshape(-1, dp_parts, LANES // 2), 1, 0).reshape(dp_parts, -1),
                jnp.transpose(
                    state_rows.reshape(3, 2, states // 2, chunks, LANES), (3, 1, 0, 2, 4)
                ).reshape(dp_parts, -1),
                gain_part.reshape(dp_parts, -1),
            ],
            axis=1,
        )
        small = lax.psum_scatter(packed, "dp", scatter_dimension=0, tiled=True)
        gain_both = small[0, -(width // dp_parts) :].reshape(2, -1)
        gain_own = lax.dynamic_index_in_dim(gain_both, half, 0, keepdims=False)
        gain_send = lax.dynamic_index_in_dim(gain_both, 1 - half, 0, keepdims=False)
        gain_grad = gain_own + swap_pair(gain_send)
        out_own = swap_odd(out_sum).astype(F32)
        small = swap_odd(small)[0]
        edge = LANES // 2
        at = 0
        dtx_grad = small[at : at + edge * ranks].reshape(edge, ranks)
        at += edge * ranks
        dt_grad = small[at : at + edge * ranks].reshape(edge, ranks)
        at += edge * ranks
        vec = small[at : at + (taps + 3) * edge].reshape(taps + 3, edge)
        at += (taps + 3) * edge
        state_part = small[at : at + 3 * states // 2 * LANES].reshape(3, states // 2, LANES)
        return (
            mixed.reshape(micros, count, width),
            tokens_grad.reshape(micros, count, width),
            gain_grad,
            in_sum,
            vec[:taps],
            vec[taps],
            dtx_grad,
            dt_grad,
            vec[taps + 1],
            state_part[:2],
            state_part[2],
            vec[taps + 2],
            out_own,
        )

    def total(array):
        return lax.psum(array.astype(F32), "dp")

    def both_rows(array):
        mine = array.reshape(chunks, 1, LANES, -1)
        other = swap_pair(mine)
        order = jnp.where(half == 0, jnp.arange(2), 1 - jnp.arange(2))
        pair = jnp.concatenate([mine, other], axis=1)
        return jnp.take(pair, order, axis=1).reshape(2 * own, -1)

    every = dp_parts * state_count
    place = lax.axis_index("dp") * state_count + state_pos

    def cut(array):
        extent = array.shape[0] // every
        return lax.dynamic_slice_in_dim(array, place * extent, extent, 0)

    in_grad = cut(jnp.concatenate([both_rows(total(inner_grad)), both_rows(total(gate_grad))]))
    out_own = cut(both_rows(total(out_grad)))
    small = both_rows(
        total(jnp.concatenate([dtx_rows, dt_rows, vectors.T, state_rows.T], axis=1))
    )
    gain_sum = total(gain_part[0])
    gain_grad = cut(gain_sum + swap_pair(gain_sum))
    mine = cut(small)
    dtx_grad, dt_grad = mine[:, :ranks], mine[:, ranks : 2 * ranks]
    vec = mine[:, 2 * ranks : 2 * ranks + taps + 3].T
    extent = inner // dp_parts
    state_part = lax.dynamic_slice_in_dim(small, lax.axis_index("dp") * extent, extent, 0)
    state_part = state_part[:, 2 * ranks + taps + 3 :].T.reshape(3, state_count, -1, extent)
    state_part = lax.dynamic_index_in_dim(state_part, state_pos, 1, keepdims=False)
    return (
        mixed.reshape(micros, count, width),
        tokens_grad.reshape(micros, count, width),
        gain_grad,
        in_grad,
        vec[:taps],
        vec[taps],
        dtx_grad,
        dt_grad,
        vec[taps + 1],
        state_part[:2],
        state_part[2],
        vec[taps + 2],
        out_own,
    )


def solution(mesh):
    return jax.shard_map(
        shards,
        mesh=mesh,
        in_specs=(
            P(None, "dp", None),
            P(None, "dp", None),
            P(),
            P(),
            P(),
            P(),
            P(),
            P(),
            P(),
            P(None, "state", None),
            P("state", None),
            P(),
            P(),
            P(None, "dp", None),
        ),
        out_specs=(
            P(None, "dp", None),
            P(None, "dp", None),
            P(("dp", "state")),
            P(("dp", "state"), None),
            P(None, ("dp", "state")),
            P(("dp", "state")),
            P(("dp", "state"), None),
            P(("dp", "state"), None),
            P(("dp", "state")),
            P(None, "state", "dp"),
            P("state", "dp"),
            P(("dp", "state")),
            P(("dp", "state"), None),
        ),
        check_vma=False,
    )
```

```python
import functools
import math

import jax
import jax.numpy as jnp
from jax import lax
from jax.experimental import pallas as pl
from jax.experimental.pallas import tpu as pltpu
from jax.sharding import PartitionSpec as P

EPSILON = 1e-05
LANES = 128
RESET = 1e4
LOG2E = math.log2(math.e)
F32 = jnp.float32
BF16 = jnp.bfloat16
MIB = 1024 * 1024


def dot(left, right, left_dim, right_dim):
    return lax.dot_general(
        left, right, (((left_dim,), (right_dim,)), ((), ())), preferred_element_type=F32
    )


def params(mib):
    return pltpu.CompilerParams(
        vmem_limit_bytes=mib * MIB, dimension_semantics=("arbitrary",)
    )


def cost(micros):
    return pl.CostEstimate(
        flops=int(micros * 1e9), bytes_accessed=int(micros * 1e6), transcendentals=0
    )


def whole(shape):
    return pl.BlockSpec(shape, lambda *_: (0,) * len(shape))


sigmoid = jax.nn.sigmoid


def softplus(value):
    return jnp.maximum(value, 0.0) + jnp.log1p(jnp.exp(-jnp.abs(value)))


def lanes(index):
    return pl.ds(pl.multiple_of(index * LANES, LANES), LANES)


def aligned(start, size, to=8):
    return pl.ds(pl.multiple_of(start, to), size)


HALF, CORE, CUBE, FACE = range(4)


def fill_masks(len_ref, mask_ref, micros, count, taps, clusters):
    place = lax.broadcasted_iota(jnp.int32, (count, LANES), 0)
    for micro in range(micros):
        rows = pl.ds(micro * count, count)
        for back in range(1, taps):
            apart = place < back
            start = 0
            for cluster in range(clusters - 1):
                start = start + len_ref[micro, 0, cluster]
                apart = apart | ((place >= start) & (place < start + back))
            mask_ref[back, rows, :] = jnp.where(apart, 0.0, 1.0)
            if back == 1:
                mask_ref[0, rows, :] = jnp.where(apart, 1.0, 0.0)


def project_kernel(
    place_ref,
    len_ref,
    x_ref,
    gain_ref,
    win_ref,
    wgate_ref,
    convw_ref,
    convb_ref,
    normed_ref,
    act_ref,
    own_act_ref,
    inner_ref,
    conved_ref,
    gate_ref,
    mask_ref,
    proj_ref,
    conv_ref,
    *,
    micros,
    count,
    taps,
    clusters,
):
    chunk = pl.program_id(0)

    @pl.when(chunk == 0)
    def _():
        fill_masks(len_ref, mask_ref, micros, count, taps, clusters)
        rows = x_ref[...].astype(F32)
        scale = lax.rsqrt(jnp.mean(rows * rows, axis=1, keepdims=True) + EPSILON)
        normed_ref[...] = (rows * scale * gain_ref[...]).astype(BF16)

    half = place_ref[HALF]
    normed = normed_ref[...]
    proj_ref[...] = dot(normed, win_ref[...].reshape(2 * LANES, -1), 1, 1)
    gate_ref[...] = dot(normed, wgate_ref[...].reshape(LANES, -1), 1, 1)
    for part in range(2):
        cols = pl.ds(part * LANES, LANES)
        inner = proj_ref[:, cols]
        conved = convb_ref[pl.ds(2 * chunk + part, 1), :] + convw_ref[taps - 1 : taps, cols] * inner
        for back in range(1, taps):
            shifted = pltpu.roll(inner, back, 0) * mask_ref[back]
            conved = conved + convw_ref[taps - 1 - back : taps - back, cols] * shifted
        conv_ref[:, cols] = conved
        act_ref[:, cols] = (conved * sigmoid(conved)).astype(BF16)
    own = lanes(half)
    inner_ref[...] = proj_ref[:, own]
    conved_ref[...] = conv_ref[:, own]
    own_act_ref[...] = act_ref[:, own]


def project(place, lengths, x, gain, w4, conv_weight, conv_bias):
    rows, width = x.shape
    chunks = w4.shape[1]
    inner = chunks * 2 * LANES
    micros, _, clusters = lengths.shape
    taps = conv_weight.shape[0]
    own = chunks * LANES
    by_chunk = pl.BlockSpec((rows, LANES), lambda i, p: (0, i))
    return pl.pallas_call(
        functools.partial(
            project_kernel, micros=micros, count=rows // micros, taps=taps, clusters=clusters
        ),
        grid_spec=pltpu.PrefetchScalarGridSpec(
            num_scalar_prefetch=1,
            grid=(chunks,),
            in_specs=[
                pl.BlockSpec(memory_space=pltpu.SMEM),
                whole((rows, width)),
                whole((1, width)),
                pl.BlockSpec((1, 1, 2, LANES, width), lambda i, p: (0, i, 0, 0, 0)),
                pl.BlockSpec((1, 1, 1, LANES, width), lambda i, p: (1, i, p[HALF], 0, 0)),
                pl.BlockSpec((taps, 2 * LANES), lambda i, p: (0, i)),
                whole(conv_bias.shape),
            ],
            out_specs=[
                whole((rows, width)),
                pl.BlockSpec((rows, 2 * LANES), lambda i, p: (0, i)),
                by_chunk,
                by_chunk,
                by_chunk,
                by_chunk,
            ],
            scratch_shapes=[
                pltpu.VMEM((taps, rows, LANES), F32),
                pltpu.VMEM((rows, 2 * LANES), F32),
                pltpu.VMEM((rows, 2 * LANES), F32),
            ],
        ),
        out_shape=[
            jax.ShapeDtypeStruct((rows, width), BF16),
            jax.ShapeDtypeStruct((rows, inner), BF16),
            jax.ShapeDtypeStruct((rows, own), BF16),
            jax.ShapeDtypeStruct((rows, own), F32),
            jax.ShapeDtypeStruct((rows, own), F32),
            jax.ShapeDtypeStruct((rows, own), F32),
        ],
        compiler_params=params(16),
        cost_estimate=cost(6),
        name="project",
    )(place, lengths, x, gain, w4, w4, conv_weight, conv_bias)


def b_at(n, eighth):
    return (n // eighth) * 2 * eighth + n % eighth


def c_at(n, eighth):
    return b_at(n, eighth) + eighth


def forward_kernel(
    place_ref,
    len_ref,
    act_all_ref,
    bc_own_ref,
    bc_other_ref,
    alog_own_ref,
    alog_other_ref,
    dtx_ref,
    dt_ref,
    bias_ref,
    skip_ref,
    act_ref,
    gate_ref,
    wout_ref,
    cotan_ref,
    normed_ref,
    bc_ref,
    rank_ref,
    rank_high_ref,
    decay_ref,
    sp_ref,
    u_ref,
    dy_ref,
    mixed_ref,
    dgate_ref,
    keep_ref,
    send_ref,
    mask_ref,
    y_ref,
    gated_ref,
    tmp_ref,
    scalar_ref,
    sem,
    *,
    micros,
    count,
    states,
    chunks,
    clusters,
):
    rows = micros * count
    eighth = states // 2
    half, core, cube, face = (place_ref[k] for k in range(4))
    first = half == 0
    act_all = act_all_ref[...]
    own = dot(act_all, bc_own_ref[...].reshape(states, -1), 1, 1)
    other = dot(act_all, bc_other_ref[...].reshape(states, -1), 1, 1)
    bc_ref[:, :states] = jnp.where(first, own, other)
    bc_ref[:, states:] = jnp.where(first, other, own)
    copy = pltpu.make_async_copy(bc_ref, scalar_ref, sem)
    copy.start()

    fill_masks(len_ref, mask_ref, micros, count, 2, clusters)
    for chunk in range(chunks):
        cols = lanes(2 * chunk + half)
        own, other = alog_own_ref[:, cols], alog_other_ref[:, cols]
        tmp_ref[pl.ds(chunk * states, eighth), :] = jnp.where(first, own, other)
        tmp_ref[pl.ds(chunk * states + eighth, eighth), :] = jnp.where(first, other, own)
    for n in range(states):
        decay_ref[pl.ds(n * chunks, chunks), :] = -LOG2E * jnp.exp(
            tmp_ref[pl.ds(n, chunks, stride=states), :]
        )

    rank = dot(act_all, dtx_ref[...], 1, 1).astype(BF16)
    rank_ref[...] = rank
    rank_high_ref[...] = jnp.concatenate([jnp.zeros_like(rank), rank], axis=1)
    for chunk in range(chunks):
        cols = slice(chunk * LANES, (chunk + 1) * LANES)
        bias = bias_ref[pl.ds(2 * chunk + half, 1), :]
        step = softplus(dot(rank, dt_ref[:, lanes(2 * chunk + half)], 1, 0) + bias)
        held = step + RESET * mask_ref[0]
        source = step * act_ref[:, cols].astype(F32)
        for micro in range(micros):
            span = slice(micro * count, (micro + 1) * count)
            place = pl.ds((micro * chunks + chunk) * count, count)
            sp_ref[place, :] = held[span]
            u_ref[place, :] = source[span]
    copy.wait()

    for micro in range(micros):

        def advance(t, h, micro=micro):
            row = micro * count + t
            span = pl.ds(micro * chunks * count + t, chunks, stride=count)
            sp = sp_ref[span, :]
            u = u_ref[span, :]
            out = []
            y = None
            for n in range(states):
                decay = jnp.exp2(sp * decay_ref[pl.ds(n * chunks, chunks), :])
                now = decay * h[n] + u * scalar_ref[row, b_at(n, eighth)]
                out.append(now)
                term = now * scalar_ref[row, c_at(n, eighth)]
                y = term if y is None else y + term
            y_ref[span, :] = y
            return tuple(out)

        lax.fori_loop(0, count, advance, (jnp.zeros((chunks, LANES), F32),) * states)

    cotan = cotan_ref[...]
    for chunk in range(chunks):
        cols = slice(chunk * LANES, (chunk + 1) * LANES)
        places = [pl.ds((micro * chunks + chunk) * count, count) for micro in range(micros)]
        y = jnp.concatenate([y_ref[place, :] for place in places])
        y = y + skip_ref[pl.ds(2 * chunk + half, 1), :] * act_ref[:, cols].astype(F32)
        gate = gate_ref[:, cols]
        sig = sigmoid(gate)
        gated_ref[:, cols] = (y * (gate * sig)).astype(BF16)
        dgated = dot(cotan, wout_ref[chunk, 0], 1, 1)
        dy = dgated * (gate * sig)
        for micro in range(micros):
            dy_ref[places[micro], :] = dy[micro * count : (micro + 1) * count]
        dgate_ref[:, cols] = (dgated * y * (sig * (1.0 + gate * (1.0 - sig)))).astype(BF16)
    normed = normed_ref[...]
    edge = LANES // 2
    for j in range(chunks):
        relative = ((j & 1) << 2) | (((j >> 1) & 1) << 1) | (j >> 2)
        grad = dot(gated_ref[:, lanes(relative ^ cube)], cotan, 0, 0).astype(BF16)
        top, bottom = grad[:edge], grad[edge:]
        keep_ref[pl.ds(j * edge, edge), :] = jnp.where(core == 0, top, bottom)
        send_ref[pl.ds(j * edge, edge), :] = jnp.where(core == 0, bottom, top)
    for j in range(chunks // 2):
        place = pl.ds(chunks * edge + j * LANES, LANES)
        pair = 2 * (j ^ face)
        keep_ref[place, :] = dot(dgate_ref[:, lanes(pair + core)], normed, 0, 0).astype(BF16)
        send_ref[place, :] = dot(dgate_ref[:, lanes(pair + 1 - core)], normed, 0, 0).astype(BF16)
    width = cotan.shape[1]
    mixed_ref[...] = dot(gated_ref[...], wout_ref[...].reshape(chunks * LANES, width), 1, 0).astype(
        BF16
    )


def scan_forward(
    place,
    lengths,
    act_all,
    bc_own,
    bc_other,
    alog_own,
    alog_other,
    dtx,
    dt,
    bias,
    skip,
    act,
    gate,
    wout3,
    cotan,
    normed,
):
    rows, own = act.shape
    chunks = own // LANES
    states = 2 * alog_own.shape[0]
    width = cotan.shape[1]
    micros, _, clusters = lengths.shape
    ranks = dtx.shape[0]
    outs = [
        ((rows, 2 * states), F32),
        ((rows, ranks), BF16),
        ((rows, 2 * ranks), BF16),
        ((states * chunks, LANES), F32),
        ((chunks * rows, LANES), F32),
        ((chunks * rows, LANES), F32),
        ((chunks * rows, LANES), F32),
        ((rows, width), BF16),
        ((rows, own), BF16),
        ((own, width), BF16),
        ((own, width), BF16),
    ]
    operands = (
        act_all, bc_own, bc_other, alog_own, alog_other, dtx, dt, bias, skip, act, gate
    )
    return pl.pallas_call(
        functools.partial(
            forward_kernel,
            micros=micros,
            count=rows // micros,
            states=states,
            chunks=chunks,
            clusters=clusters,
        ),
        grid_spec=pltpu.PrefetchScalarGridSpec(
            num_scalar_prefetch=1,
            grid=(1,),
            in_specs=[pl.BlockSpec(memory_space=pltpu.SMEM)]
            + [whole(operand.shape) for operand in operands]
            + [
                pl.BlockSpec((chunks, 1, LANES, width), lambda i, p: (0, p[HALF], 0, 0)),
                whole((rows, width)),
                whole((rows, width)),
            ],
            out_specs=[whole(shape) for shape, _ in outs],
            scratch_shapes=[
                pltpu.VMEM((2, rows, LANES), F32),
                pltpu.VMEM((chunks * rows, LANES), F32),
                pltpu.VMEM((rows, own), BF16),
                pltpu.VMEM((states * chunks, LANES), F32),
                pltpu.SMEM((rows, 2 * states), F32),
                pltpu.SemaphoreType.DMA,
            ],
        ),
        out_shape=[jax.ShapeDtypeStruct(*out) for out in outs],
        compiler_params=params(48),
        cost_estimate=cost(19),
        name="scan_forward",
    )(place, lengths, *operands, wout3, cotan, normed)


def backward_kernel(
    place_ref,
    bc_ref,
    decay_ref,
    rank_ref,
    dt_ref,
    bias_ref,
    act_ref,
    sp_ref,
    u_ref,
    dy_ref,
    code_ref,
    sact_ref,
    dpre_ref,
    alog_ref,
    vec_ref,
    h_ref,
    s_ref,
    d_ref,
    terms_ref,
    sums_ref,
    scalar_ref,
    sem,
    *,
    count,
    states,
    chunks,
):
    copy = pltpu.make_async_copy(bc_ref, scalar_ref, sem)
    copy.start()
    half = place_ref[HALF]
    eighth = states // 2
    alog_ref[...] = jnp.zeros_like(alog_ref)
    zero = (jnp.zeros((chunks, LANES), F32),) * states
    for n in range(states):
        h_ref[pl.ds(n * chunks, chunks), :] = zero[0]
    copy.wait()

    def recompute(t, h):
        span = pl.ds(t, chunks, stride=count)
        sp = sp_ref[span, :]
        u = u_ref[span, :]
        out = []
        for n in range(states):
            decay = jnp.exp2(sp * decay_ref[pl.ds(n * chunks, chunks), :])
            now = decay * h[n] + u * scalar_ref[t, b_at(n, eighth)]
            h_ref[aligned(((t + 1) * states + n) * chunks, chunks), :] = now
            out.append(now)
        return tuple(out)

    lax.fori_loop(0, count, recompute, zero)

    def retreat(back, carry):
        t = count - 1 - back
        span = pl.ds(t, chunks, stride=count)
        sp = sp_ref[span, :]
        u = u_ref[span, :]
        dy = dy_ref[span, :]
        out = []
        d_sum = None
        s_sum = None
        for n in range(states):
            rate = decay_ref[pl.ds(n * chunks, chunks), :]
            decay = jnp.exp2(sp * rate)
            dh = carry[n] + dy * scalar_ref[t, c_at(n, eighth)]
            flow = decay * dh
            out.append(flow)
            before = h_ref[aligned((t * states + n) * chunks, chunks), :]
            now = h_ref[aligned(((t + 1) * states + n) * chunks, chunks), :]
            q = flow * before
            alog_ref[pl.ds(n * chunks, chunks), :] += q * sp
            d_term = q * rate
            s_term = dh * scalar_ref[t, b_at(n, eighth)]
            d_sum = d_term if d_sum is None else d_sum + d_term
            s_sum = s_term if s_sum is None else s_sum + s_term
            terms_ref[pl.ds(b_at(n, eighth) * chunks, chunks), :] = dh * u
            terms_ref[pl.ds(c_at(n, eighth) * chunks, chunks), :] = dy * now
        s_ref[span, :] = s_sum
        d_ref[span, :] = d_sum
        sums = None
        for chunk in range(chunks):
            term = terms_ref[pl.ds(chunk, 2 * states, stride=chunks), :]
            sums = term if sums is None else sums + term
        sums_ref[aligned(t * 2 * states, 2 * states), :] = sums
        return tuple(out)

    lax.fori_loop(0, count, retreat, zero)

    rank = rank_ref[...]
    ranks = rank.shape[1]
    drank = None
    for chunk in range(chunks):
        cols = slice(chunk * LANES, (chunk + 1) * LANES)
        place = pl.ds(chunk * count, count)
        act = act_ref[:, cols].astype(F32)
        weight = dt_ref[:, lanes(2 * chunk + half)]
        pre = dot(rank, weight, 1, 0) + bias_ref[pl.ds(2 * chunk + half, 1), :]
        s_now = s_ref[place, :]
        dstep = d_ref[place, :] * (1.0 / LOG2E) + s_now * act
        sact_ref[:, cols] = s_now * softplus(pre)
        dpre = dstep * sigmoid(pre)
        vec_ref[0:1, cols] = jnp.sum(dpre, axis=0, keepdims=True)
        vec_ref[1:2, cols] = jnp.sum(dy_ref[place, :] * act, axis=0, keepdims=True)
        low = dpre.astype(BF16)
        dpre_ref[:, cols] = low
        term = dot(low, weight, 1, 1)
        drank = term if drank is None else drank + term
    source = lax.broadcasted_iota(jnp.int32, (2 * LANES, LANES), 0) // LANES
    target = lax.broadcasted_iota(jnp.int32, (2 * LANES, LANES), 1)
    code = None
    for k in range(states):
        pair = jnp.concatenate(
            [sums_ref[pl.ds(2 * k + j, count, stride=2 * states), :] for j in range(2)], axis=1
        )
        pick = jnp.where(target == source + (ranks + 2 * k), 1.0, 0.0).astype(BF16)
        term = dot(pair.astype(BF16), pick, 1, 0)
        code = term if code is None else code + term
    code_ref[...] = code + jnp.concatenate([drank, jnp.zeros((count, LANES - ranks), F32)], axis=1)


def scan_backward(place, micro, count, bc, decay, rank, dt, bias, act, sp, u, dy):
    rows, own = act.shape
    chunks = own // LANES
    states = bc.shape[1] // 2
    ranks = rank.shape[1]
    outs = [
        ((count, LANES), F32),
        ((count, own), F32),
        ((count, own), BF16),
        ((states * chunks, LANES), F32),
        ((2, own), F32),
    ]

    def block(*shape):
        return pl.BlockSpec(shape, lambda i, p: (micro, 0))

    return pl.pallas_call(
        functools.partial(backward_kernel, count=count, states=states, chunks=chunks),
        grid_spec=pltpu.PrefetchScalarGridSpec(
            num_scalar_prefetch=1,
            grid=(1,),
            in_specs=[
                block(count, 2 * states),
                whole(decay.shape),
                block(count, ranks),
                whole(dt.shape),
                whole(bias.shape),
                block(count, own),
                block(chunks * count, LANES),
                block(chunks * count, LANES),
                block(chunks * count, LANES),
            ],
            out_specs=[whole(shape) for shape, _ in outs],
            scratch_shapes=[
                pltpu.VMEM(((count + 1) * states * chunks, LANES), F32),
                pltpu.VMEM((chunks * count, LANES), F32),
                pltpu.VMEM((chunks * count, LANES), F32),
                pltpu.VMEM((2 * states * chunks, LANES), F32),
                pltpu.VMEM((count * 2 * states, LANES), F32),
                pltpu.SMEM((count, 2 * states), F32),
                pltpu.SemaphoreType.DMA,
            ],
        ),
        out_shape=[jax.ShapeDtypeStruct(*out) for out in outs],
        compiler_params=params(26),
        cost_estimate=cost(14),
        name="scan_backward",
    )(place, bc, decay, rank, dt, bias, act, sp, u, dy)


def tail_kernel(
    place_ref,
    len_ref,
    *refs,
    micros,
    count,
    taps,
    clusters,
    ranks,
    chunks,
    states,
):
    def take(number):
        nonlocal refs
        taken, refs = refs[:number], refs[number:]
        return taken

    code_own, code_other, sact_refs, dpre_refs, alog_refs, back_refs = (
        take(micros) for _ in range(6)
    )
    dtx_ref, bc_own_ref, bc_other_ref, decay_ref = take(4)
    dy_refs = take(micros)
    conved_ref, inner_ref, act_ref, dgate_ref, high_ref, convw_ref, skip_ref = take(7)
    win_ref, wgate_ref, normed_ref, x_ref = take(4)
    keep_ref, send_ref, dnormed_ref = take(3)
    mask_ref, total_ref, code_ref, wcode_ref, low_ref, vec_ref, alog_ref = refs

    step = pl.program_id(0)
    rows = micros * count
    eighth = states // 2
    edge = LANES // 2
    half, core, cube, face = (place_ref[k] for k in range(4))
    pair = step ^ face
    width = x_ref.shape[1]
    span = 3 * edge // 2

    def pack_row(chunk):
        relative = chunk ^ cube
        zh, zl, x = relative >> 2, (relative >> 1) & 1, relative & 1
        return (2 * x + zl) * span + edge + zh * 16

    def place_pair(start, size, cols, even, odd):
        keep_ref[aligned(start, size, 16), cols] = jnp.where(core == 0, even, odd).astype(BF16)
        send_ref[aligned(start, size, 16), cols] = jnp.where(core == 0, odd, even).astype(BF16)

    @pl.when(step == 0)
    def _():
        fill_masks(len_ref, mask_ref, micros, count, taps, clusters)
        total_ref[...] = jnp.zeros_like(total_ref)
        for micro in range(micros):
            code_ref[pl.ds(micro * count, count), :] = (
                code_own[micro][...] + code_other[micro][...]
            ).astype(BF16)
        total = None
        for micro in range(micros):
            term = alog_refs[micro][...]
            total = term if total is None else total + term
        alog_ref[...] = total * (decay_ref[...] * (1.0 / LOG2E))

    code = code_ref[...]
    lane = lax.broadcasted_iota(jnp.int32, (1, LANES), 1)
    code_rank = jnp.where(lane < ranks, code, jnp.zeros_like(code))
    dpre = jnp.concatenate([ref[...] for ref in dpre_refs], axis=0)
    wide = 2 * LANES
    for part in range(2):
        source = lanes(2 * (2 * pair + part) + half)
        cols = slice(part * LANES, (part + 1) * LANES)
        wcode_ref[:ranks, cols] = dtx_ref[:, source]
        own = bc_own_ref[:, :, source].reshape(states, LANES)
        other = bc_other_ref[:, :, source].reshape(states, LANES)
        wcode_ref[ranks : ranks + states, cols] = jnp.where(half == 0, own, other)
        wcode_ref[ranks + states : ranks + 2 * states, cols] = jnp.where(half == 0, other, own)
        wcode_ref[ranks + 2 * states :, cols] = jnp.zeros(
            (LANES - ranks - 2 * states, LANES), BF16
        )
    for part in range(2):
        cols = slice(part * LANES, (part + 1) * LANES)
        chunk = 2 * pair + part
        source = 2 * chunk + half
        weights = convw_ref[:, lanes(source)]
        sact = jnp.concatenate([ref[:, cols] for ref in sact_refs], axis=0)
        dy = jnp.concatenate([ref[pl.ds(part * count, count), :] for ref in dy_refs], axis=0)
        dact = sact + dot(code, wcode_ref[:, cols], 1, 0)
        dact = dact + dy * skip_ref[pl.ds(source, 1), :]
        conved = conved_ref[:, cols]
        sig = sigmoid(conved)
        dconv = dact * (sig * (1.0 + conved * (1.0 - sig)))
        inner = inner_ref[:, cols]
        dinner = weights[taps - 1 : taps] * dconv
        sums = [None] * (taps + 1)
        sums[taps - 1] = jnp.sum(dconv * inner, axis=0, keepdims=True)
        sums[taps] = jnp.sum(dconv, axis=0, keepdims=True)
        for back in range(1, taps):
            kept = dconv * mask_ref[back]
            dinner = dinner + weights[taps - 1 - back : taps - back] * pltpu.roll(
                kept, rows - back, 0
            )
            sums[taps - 1 - back] = jnp.sum(
                kept * pltpu.roll(inner, back, 0), axis=0, keepdims=True
            )
        for k in range(taps + 1):
            vec_ref[k : k + 1, lanes(chunk)] = sums[k]
        for k in range(2):
            total = None
            for ref in back_refs:
                term = ref[k : k + 1, lanes(chunk)]
                total = term if total is None else total + term
            vec_ref[taps + 1 + k : taps + 2 + k, lanes(chunk)] = total
        low_ref[:, cols] = dinner.astype(BF16)

        act = act_ref[:, cols]
        start = pack_row(chunk)
        rows_now = dot(act, code_rank, 0, 0) + dot(dpre[:, cols], high_ref[...], 0, 0)
        for k in range(4):
            place_pair(
                start,
                16,
                slice(k * LANES, (k + 1) * LANES),
                rows_now[k * 16 : (k + 1) * 16],
                rows_now[edge + k * 16 : edge + (k + 1) * 16],
            )
        state_rows = dot(code, act, 0, 0)[ranks : ranks + 2 * states]
        place_pair(
            start, 16, slice(4 * LANES, 5 * LANES), state_rows[:states], state_rows[states:]
        )

    zl, x_bit = step >> 1, step & 1
    normed = normed_ref[...]
    for part in range(2):
        grad = dot(low_ref[:, lanes(core ^ part)], normed, 0, 0).astype(BF16)
        out_ref = (keep_ref, send_ref)[part]
        out_ref[aligned((2 * x_bit + zl) * span, edge, 16), :] = grad[:edge]
        out_ref[aligned(4 * span + step * edge, edge, 16), :] = grad[edge:]
    total_ref[...] += dot(low_ref[...], win_ref[...].reshape(wide, width), 1, 0) + dot(
        dgate_ref[...], wgate_ref[...].reshape(wide, width), 1, 0
    )

    @pl.when(step == pl.num_programs(0) - 1)
    def _():
        total = total_ref[...]
        x = x_ref[...].astype(F32)
        scale = lax.rsqrt(jnp.mean(x * x, axis=1, keepdims=True) + EPSILON)
        vec_ref[taps + 3 : taps + 4, :] = jnp.sum(total * (x * scale), axis=0, keepdims=True)
        dnormed_ref[...] = total.astype(BF16)
        for chunk in range(chunks):
            start = pack_row(chunk)
            vec = vec_ref[:, chunk * LANES : (chunk + 1) * LANES]
            alog = [
                alog_ref[pl.ds(q * eighth * chunks + chunk, eighth, stride=chunks), :]
                for q in range(2)
            ]
            place_pair(
                start,
                16,
                slice(5 * LANES, 6 * LANES),
                jnp.concatenate([alog[0], vec]),
                jnp.concatenate([alog[1], pltpu.roll(vec, edge, 1)]),
            )
            blank = jnp.zeros((16, 2 * LANES), F32)
            place_pair(start, 16, slice(6 * LANES, 8 * LANES), blank, blank)


def tail(
    place,
    lengths,
    code_own,
    code_other,
    sact,
    dpre,
    alog,
    back,
    dtx,
    bc_own,
    bc_other,
    decay,
    dy,
    conved,
    inner,
    act,
    dgate,
    high,
    convw,
    skip,
    w4,
    normed,
    x,
):
    rows, own = act.shape
    chunks = own // LANES
    width = x.shape[1]
    micros, _, clusters = lengths.shape
    count = rows // micros
    taps = convw.shape[0]
    ranks = dtx.shape[0]
    states = decay.shape[0] // chunks
    cols = 2 * LANES
    extent = chunks * LANES // 2 + 2 * chunks * 8

    def by_cols(height):
        return pl.BlockSpec((height, cols), lambda i, p: (0, i ^ p[FACE]))

    def dy_spec(micro):
        return pl.BlockSpec(
            (2 * count, LANES), lambda i, p: (micro * (chunks // 2) + (i ^ p[FACE]), 0)
        )

    def weight_spec(which):
        return pl.BlockSpec(
            (1, 2, 1, LANES, width), lambda i, p: (which, i ^ p[FACE], p[HALF], 0, 0)
        )

    in_specs = (
        [pl.BlockSpec(memory_space=pltpu.SMEM)]
        + [whole((count, LANES))] * (2 * micros)
        + [by_cols(count)] * (2 * micros)
        + [whole(alog[0].shape)] * micros
        + [whole(back[0].shape)] * micros
        + [whole(array.shape) for array in (dtx, bc_own, bc_other, decay)]
        + [dy_spec(micro) for micro in range(micros)]
        + [by_cols(rows)] * 4
        + [whole(array.shape) for array in (high, convw, skip)]
        + [weight_spec(0), weight_spec(1)]
        + [whole((rows, width))] * 2
    )
    return pl.pallas_call(
        functools.partial(
            tail_kernel,
            micros=micros,
            count=count,
            taps=taps,
            clusters=clusters,
            ranks=ranks,
            chunks=chunks,
            states=states,
        ),
        grid_spec=pltpu.PrefetchScalarGridSpec(
            num_scalar_prefetch=1,
            grid=(chunks // 2,),
            in_specs=in_specs,
            out_specs=[whole((extent, width)), whole((extent, width)), whole((rows, width))],
            scratch_shapes=[
                pltpu.VMEM((taps, rows, LANES), F32),
                pltpu.VMEM((rows, width), F32),
                pltpu.VMEM((rows, LANES), BF16),
                pltpu.VMEM((LANES, cols), BF16),
                pltpu.VMEM((rows, cols), BF16),
                pltpu.VMEM((8, own), F32),
                pltpu.VMEM((states * chunks, LANES), F32),
            ],
        ),
        out_shape=[
            jax.ShapeDtypeStruct((extent, width), BF16),
            jax.ShapeDtypeStruct((extent, width), BF16),
            jax.ShapeDtypeStruct((rows, width), BF16),
        ],
        compiler_params=params(32),
        cost_estimate=cost(9),
        name="tail",
    )(
        place,
        lengths,
        *code_own,
        *code_other,
        *sact,
        *dpre,
        *alog,
        *back,
        dtx,
        bc_own,
        bc_other,
        decay,
        *([dy] * micros),
        conved,
        inner,
        act,
        dgate,
        high,
        convw,
        skip,
        w4,
        w4,
        normed,
        x,
    )


def swap_pair(array):
    count = lax.axis_size("state")
    return lax.ppermute(array, "state", [(pos, pos ^ 1) for pos in range(count)])


def swap_bit(array, bit, source=None):
    pairs = [
        (pos, pos ^ bit)
        for pos in range(lax.axis_size("dp"))
        if source is None or bool(pos & bit) == source
    ]
    return lax.ppermute(array, "dp", pairs)


def swap_odd(array):
    parts, states = lax.axis_size("dp"), lax.axis_size("state")
    pairs = []
    for d in range(parts):
        for s in range(states):
            at = d * states + s
            to = at if d % 2 == s % 2 else (d ^ 1) * states + (s ^ 1)
            pairs.append((at, to))
    return lax.ppermute(array, ("dp", "state"), pairs)


def halves(kept, got):
    middle = kept.shape[0] // 2
    return kept[:middle] + got[:middle], kept[middle:] + got[middle:]


CORE_BIT, X_BIT, ZL_BIT, ZH_BIT = 1, 2, 4, 8


def shards(
    tokens,
    cluster_len,
    norm_gain,
    in_weight,
    conv_weight,
    conv_bias,
    dtx_weight,
    dt_weight,
    dt_bias,
    bc_weight,
    a_log,
    skip_gain,
    out_weight,
    cotangent,
):
    micros, count, width = tokens.shape
    inner = out_weight.shape[0]
    taps = conv_weight.shape[0]
    ranks = dtx_weight.shape[1]
    chunks = inner // (2 * LANES)
    own = chunks * LANES
    rows = micros * count
    edge = LANES // 2
    span = 3 * edge // 2
    dp_parts = lax.axis_size("dp")
    state_count = lax.axis_size("state")
    dp_pos = lax.axis_index("dp")
    state_pos = lax.axis_index("state")
    half = state_pos % 2
    fast = state_count == 2 and dp_parts == 2 * chunks == 16
    if fast:
        place = jnp.stack([half, dp_pos & 1, dp_pos >> 1, (dp_pos >> 1) & 3])
        bc_own, alog_own = bc_weight, a_log
        bc_other, alog_other = swap_pair(bc_weight), swap_pair(a_log)
    else:
        place = jnp.stack([half, 0, 0, 0])
        bc_all = lax.all_gather(bc_weight, "state", axis=1, tiled=True)
        alog_all = lax.all_gather(a_log, "state", axis=0, tiled=True)
        eighth = alog_all.shape[0] // 2
        bc_own, bc_other = (
            lax.dynamic_slice_in_dim(bc_all, which * eighth, eighth, 1)
            for which in (half, 1 - half)
        )
        alog_own, alog_other = (
            lax.dynamic_slice_in_dim(alog_all, which * eighth, eighth, 0)
            for which in (half, 1 - half)
        )
    place = place.astype(jnp.int32)
    eighth = alog_own.shape[0]
    states = 2 * eighth

    x = tokens.reshape(rows, width)
    cotan = cotangent.reshape(rows, width)
    w4 = in_weight.reshape(2, chunks, 2, LANES, width)
    wout3 = out_weight.reshape(chunks, 2, LANES, width)
    dtx, dt = dtx_weight.T, dt_weight.T
    bias = dt_bias.reshape(-1, LANES)
    skip = skip_gain.reshape(-1, LANES)

    normed, act_all, act, inner_own, conved, gate = project(
        place, cluster_len, x, norm_gain[None], w4, conv_weight, conv_bias.reshape(-1, LANES)
    )
    bc, rank, high, decay, sp, u, dy, mixed_part, dgate, keep, send = scan_forward(
        place,
        cluster_len,
        act_all,
        bc_own,
        bc_other,
        alog_own,
        alog_other,
        dtx,
        dt,
        bias,
        skip,
        act,
        gate,
        wout3,
        cotan,
        normed,
    )
    early = None
    if fast:
        early = swap_bit(send, CORE_BIT)
    mixed_other = swap_pair(mixed_part)

    results = []
    for micro in range(micros):
        if fast and micro == micros - 1:
            cut = chunks * edge
            out_keep, out_send = halves(keep[:cut], early[:cut])
            gate_keep, gate_send = halves(keep[cut:], early[cut:])
            out_send, gate_send, sp = lax.optimization_barrier((out_send, gate_send, sp))
            out_got = swap_bit(out_send, X_BIT)
            gate_got = swap_bit(gate_send, ZL_BIT)
        results.append(
            scan_backward(place, micro, count, bc, decay, rank, dt, bias, act, sp, u, dy)
        )
    code_own, sact, dpre, alog, back = zip(*results)
    code_other = [swap_pair(code) for code in code_own]
    if fast:
        out_keep, out_send = halves(out_keep, out_got)
        gate_keep, gate_send = halves(gate_keep, gate_got)
        out_send, gate_send, dgate = lax.optimization_barrier((out_send, gate_send, dgate))
        out_got = swap_bit(out_send, ZL_BIT)
        gate_got = swap_bit(gate_send, X_BIT)
    late_keep, late_send, dnormed_part = tail(
        place,
        cluster_len,
        code_own,
        code_other,
        sact,
        dpre,
        alog,
        back,
        dtx,
        bc_own,
        bc_other,
        decay,
        dy,
        conved,
        inner_own,
        act,
        dgate,
        high,
        conv_weight,
        skip,
        w4,
        normed,
        x,
    )
    if fast:
        late = swap_bit(late_send, CORE_BIT)
        dnormed_other = swap_pair(dnormed_part)
        out_keep, out_send = halves(out_keep, out_got)
        gate_sum = gate_keep + gate_got
        out_got = swap_bit(out_send, ZH_BIT)
        gate_got = swap_bit(gate_sum, ZH_BIT, False)
        cut = 4 * span
        a_keep, a_send = halves(late_keep[:cut], late[:cut])
        b_keep, b_send = halves(late_keep[cut:], late[cut:])
        a_got = swap_bit(a_send, X_BIT)
        b_got = swap_bit(b_send, ZL_BIT)
        a_keep, a_send = halves(a_keep, a_got)
        b_keep, b_send = halves(b_keep, b_got)
        a_got = swap_bit(a_send, ZL_BIT)
        b_got = swap_bit(b_send, X_BIT)
        inner_sum = jnp.concatenate([a_keep[:edge] + a_got[:edge], b_keep + b_got])
        pack_keep, pack_send = halves(a_keep[edge:], a_got[edge:])
        inner_got = swap_bit(inner_sum, ZH_BIT, True)
        pack_got = swap_bit(pack_send, ZH_BIT)
        out_own = swap_odd(out_keep + out_got).astype(F32)
        upper = dp_pos >= dp_parts // 2
        in_grad = jnp.where(
            upper,
            gate_sum.astype(F32) + gate_got.astype(F32),
            inner_sum.astype(F32) + inner_got.astype(F32),
        )
        pack = pack_keep + pack_got
        gain_row = pack[:, 5 * LANES : 6 * LANES]
        gain_rows = gain_row.astype(F32) + swap_pair(gain_row).astype(F32)
        gain_both = gain_rows[-1, : 2 * (width // (dp_parts * 2))].reshape(2, -1)
        gain_grad = lax.dynamic_index_in_dim(gain_both, half, 0, keepdims=False)
        pack = swap_odd(pack).astype(F32)
        small = jnp.concatenate([pack[:, k * LANES : (k + 1) * LANES] for k in range(4)])
        dtx_grad, dt_grad = small[:, :ranks], small[:, ranks:]
        bc_grad = pack[:, 4 * LANES : 5 * LANES].reshape(2, eighth, LANES)
        alog_grad = pack[:eighth, 5 * LANES : 6 * LANES]
        vec = pack[eighth:, 5 * LANES : 5 * LANES + edge]
    else:
        dnormed_other = swap_pair(dnormed_part)

    mixed = (x.astype(F32) + (mixed_part.astype(F32) + mixed_other.astype(F32))).astype(BF16)
    dnormed = dnormed_part.astype(F32) + dnormed_other.astype(F32)
    x32 = x.astype(F32)
    scale = lax.rsqrt(jnp.mean(x32 * x32, axis=1, keepdims=True) + EPSILON)
    unit = x32 * scale
    dhat = dnormed * norm_gain
    tokens_grad = cotan.astype(F32) + scale * (
        dhat - unit * jnp.mean(dhat * unit, axis=1, keepdims=True)
    )
    mixed = mixed.reshape(micros, count, width)
    tokens_grad = tokens_grad.reshape(micros, count, width)

    if not fast:
        def total(array):
            return lax.psum(array.astype(F32), "dp")

        def both_rows(array):
            mine = array.reshape(chunks, 1, LANES, -1)
            other = swap_pair(mine)
            low = jnp.where(half == 0, mine, other)
            high = jnp.where(half == 0, other, mine)
            return jnp.concatenate([low, high], axis=1).reshape(2 * own, -1)

        every = dp_parts * state_count
        at = dp_pos * state_count + state_pos

        def cut_own(array):
            extent = array.shape[0] // every
            return lax.dynamic_slice_in_dim(array, at * extent, extent, 0)

        pair = total(jnp.stack([keep, send]))
        outs = pair[:, : chunks * edge].reshape(2, 2, 2, 2, edge, width)
        outs = jnp.transpose(outs, (3, 2, 1, 0, 4, 5)).reshape(own, width)
        gates = pair[:, chunks * edge :].reshape(2, chunks // 2, LANES, width)
        gates = jnp.moveaxis(gates, 0, 1).reshape(own, width)
        pair = total(jnp.stack([late_keep, late_send]))
        a_part = pair[:, : 4 * span].reshape(2, 2, 2, span, width)
        b_part = pair[:, 4 * span :].reshape(2, 2, 2, edge, width)
        inners = jnp.concatenate(
            [jnp.transpose(a_part[:, :, :, :edge], (2, 1, 0, 3, 4)), jnp.moveaxis(b_part, 0, 2)],
            axis=3,
        ).reshape(own, width)
        packs = a_part[:, :, :, edge:].reshape(2, 2, 2, 2, 16, width // LANES, LANES)
        packs = jnp.transpose(packs, (3, 2, 1, 0, 5, 4, 6)).reshape(chunks, 2, -1, 16, LANES)
        small = both_rows(packs[:, :, :4].reshape(own, LANES))
        in_grad = cut_own(jnp.concatenate([both_rows(inners), both_rows(gates)]))
        out_own = cut_own(both_rows(outs))
        mine = cut_own(small)
        dtx_grad, dt_grad = mine[:, :ranks], mine[:, ranks:]
        vec_rows = jnp.swapaxes(packs[:, :, 5, eighth:, :edge], 2, 3).reshape(own, -1)
        gain_sum = vec_rows[:, -1]
        gain_grad = cut_own(gain_sum + swap_pair(gain_sum))
        vec = cut_own(both_rows(vec_rows)).T
        state_rows = jnp.concatenate([packs[:, :, 4], packs[:, :, 5, :eighth]], axis=2)
        state_rows = state_rows.reshape(chunks, 2, 3, eighth, LANES)
        state_rows = jnp.transpose(state_rows, (0, 4, 2, 1, 3)).reshape(own, -1)
        extent = inner // dp_parts
        state_part = lax.dynamic_slice_in_dim(both_rows(state_rows), dp_pos * extent, extent, 0)
        state_part = state_part.T.reshape(3, state_count, -1, extent)
        state_part = lax.dynamic_index_in_dim(state_part, state_pos, 1, keepdims=False)
        bc_grad, alog_grad = state_part[:2], state_part[2]

    return (
        mixed,
        tokens_grad,
        gain_grad,
        in_grad,
        vec[:taps],
        vec[taps],
        dtx_grad,
        dt_grad,
        vec[taps + 1],
        bc_grad,
        alog_grad,
        vec[taps + 2],
        out_own,
    )


def solution(mesh):
    return jax.shard_map(
        shards,
        mesh=mesh,
        in_specs=(
            P(None, "dp", None),
            P(None, "dp", None),
            P(),
            P(),
            P(),
            P(),
            P(),
            P(),
            P(),
            P(None, "state", None),
            P("state", None),
            P(),
            P(),
            P(None, "dp", None),
        ),
        out_specs=(
            P(None, "dp", None),
            P(None, "dp", None),
            P(("dp", "state")),
            P(("dp", "state"), None),
            P(None, ("dp", "state")),
            P(("dp", "state")),
            P(("dp", "state"), None),
            P(("dp", "state"), None),
            P(("dp", "state")),
            P(None, "state", "dp"),
            P("state", "dp"),
            P(("dp", "state")),
            P(("dp", "state"), None),
        ),
        check_vma=False,
    )
```

```python
import functools
import math

import jax
import jax.numpy as jnp
from jax import lax
from jax.experimental import pallas as pl
from jax.experimental.pallas import tpu as pltpu
from jax.sharding import PartitionSpec as P

EPSILON = 1e-05
LANES = 128
RESET = 1e4
LOG2E = math.log2(math.e)
F32 = jnp.float32
BF16 = jnp.bfloat16
MIB = 1024 * 1024


def dot(left, right, left_dim, right_dim):
    return lax.dot_general(
        left, right, (((left_dim,), (right_dim,)), ((), ())), preferred_element_type=F32
    )


def params(mib):
    return pltpu.CompilerParams(
        vmem_limit_bytes=mib * MIB, dimension_semantics=("arbitrary",)
    )


def cost(micros):
    return pl.CostEstimate(
        flops=int(micros * 1e9), bytes_accessed=int(micros * 1e6), transcendentals=0
    )


def whole(shape):
    return pl.BlockSpec(shape, lambda *_: (0,) * len(shape))


sigmoid = jax.nn.sigmoid


def softplus(value):
    return jnp.maximum(value, 0.0) + jnp.log1p(jnp.exp(-jnp.abs(value)))


def lanes(index):
    return pl.ds(pl.multiple_of(index * LANES, LANES), LANES)


def in_hbm(array):
    return pltpu.with_memory_space_constraint(array, pltpu.HBM)


def aligned(start, size, to=8):
    return pl.ds(pl.multiple_of(start, to), size)


HALF, CORE, CUBE, FACE = range(4)


def fill_masks(len_ref, mask_ref, micros, count, taps, clusters):
    place = lax.broadcasted_iota(jnp.int32, (count, LANES), 0)
    for micro in range(micros):
        rows = pl.ds(micro * count, count)
        for back in range(1, taps):
            apart = place < back
            start = 0
            for cluster in range(clusters - 1):
                start = start + len_ref[micro, 0, cluster]
                apart = apart | ((place >= start) & (place < start + back))
            mask_ref[back, rows, :] = jnp.where(apart, 0.0, 1.0)
            if back == 1:
                mask_ref[0, rows, :] = jnp.where(apart, 1.0, 0.0)


def project_kernel(
    place_ref,
    len_ref,
    x_ref,
    gain_ref,
    win_ref,
    wgate_ref,
    convw_ref,
    convb_ref,
    normed_ref,
    act_ref,
    own_act_ref,
    inner_ref,
    conved_ref,
    gate_ref,
    mask_ref,
    proj_ref,
    conv_ref,
    *,
    micros,
    count,
    taps,
    clusters,
):
    chunk = pl.program_id(0)

    @pl.when(chunk == 0)
    def _():
        fill_masks(len_ref, mask_ref, micros, count, taps, clusters)
        rows = x_ref[...].astype(F32)
        scale = lax.rsqrt(jnp.mean(rows * rows, axis=1, keepdims=True) + EPSILON)
        normed_ref[...] = (rows * scale * gain_ref[...]).astype(BF16)

    half = place_ref[HALF]
    normed = normed_ref[...]
    proj_ref[...] = dot(normed, win_ref[...].reshape(2 * LANES, -1), 1, 1)
    gate_ref[...] = dot(normed, wgate_ref[...].reshape(LANES, -1), 1, 1)
    for part in range(2):
        cols = pl.ds(part * LANES, LANES)
        inner = proj_ref[:, cols]
        conved = convb_ref[pl.ds(2 * chunk + part, 1), :] + convw_ref[taps - 1 : taps, cols] * inner
        for back in range(1, taps):
            shifted = pltpu.roll(inner, back, 0) * mask_ref[back]
            conved = conved + convw_ref[taps - 1 - back : taps - back, cols] * shifted
        conv_ref[:, cols] = conved
        act_ref[:, cols] = (conved * sigmoid(conved)).astype(BF16)
    own = lanes(half)
    inner_ref[...] = proj_ref[:, own]
    conved_ref[...] = conv_ref[:, own]
    own_act_ref[...] = act_ref[:, own]


def project(place, lengths, x, gain, w4, conv_weight, conv_bias):
    rows, width = x.shape
    chunks = w4.shape[1]
    inner = chunks * 2 * LANES
    micros, _, clusters = lengths.shape
    taps = conv_weight.shape[0]
    own = chunks * LANES
    by_chunk = pl.BlockSpec((rows, LANES), lambda i, p: (0, i))
    return pl.pallas_call(
        functools.partial(
            project_kernel, micros=micros, count=rows // micros, taps=taps, clusters=clusters
        ),
        grid_spec=pltpu.PrefetchScalarGridSpec(
            num_scalar_prefetch=1,
            grid=(chunks,),
            in_specs=[
                pl.BlockSpec(memory_space=pltpu.SMEM),
                whole((rows, width)),
                whole((1, width)),
                pl.BlockSpec((1, 1, 2, LANES, width), lambda i, p: (0, i, 0, 0, 0)),
                pl.BlockSpec((1, 1, 1, LANES, width), lambda i, p: (1, i, p[HALF], 0, 0)),
                pl.BlockSpec((taps, 2 * LANES), lambda i, p: (0, i)),
                whole(conv_bias.shape),
            ],
            out_specs=[
                whole((rows, width)),
                pl.BlockSpec((rows, 2 * LANES), lambda i, p: (0, i)),
                by_chunk,
                by_chunk,
                by_chunk,
                by_chunk,
            ],
            scratch_shapes=[
                pltpu.VMEM((taps, rows, LANES), F32),
                pltpu.VMEM((rows, 2 * LANES), F32),
                pltpu.VMEM((rows, 2 * LANES), F32),
            ],
        ),
        out_shape=[
            jax.ShapeDtypeStruct((rows, width), BF16),
            jax.ShapeDtypeStruct((rows, inner), BF16),
            jax.ShapeDtypeStruct((rows, own), BF16),
            jax.ShapeDtypeStruct((rows, own), F32),
            jax.ShapeDtypeStruct((rows, own), F32),
            jax.ShapeDtypeStruct((rows, own), F32),
        ],
        compiler_params=params(16),
        cost_estimate=cost(6),
        name="project",
    )(place, *map(in_hbm, (lengths, x, gain, w4, w4, conv_weight, conv_bias)))


def b_at(n, eighth):
    return (n // eighth) * 2 * eighth + n % eighth


def c_at(n, eighth):
    return b_at(n, eighth) + eighth


def forward_kernel(
    place_ref,
    len_ref,
    act_all_ref,
    bc_own_ref,
    bc_other_ref,
    alog_own_ref,
    alog_other_ref,
    dtx_ref,
    dt_ref,
    bias_ref,
    skip_ref,
    act_ref,
    gate_ref,
    wout_ref,
    cotan_ref,
    normed_ref,
    bc_ref,
    rank_ref,
    rank_high_ref,
    decay_ref,
    sp_ref,
    u_ref,
    dy_ref,
    mixed_ref,
    dgate_ref,
    keep_ref,
    send_ref,
    mask_ref,
    y_ref,
    gated_ref,
    tmp_ref,
    scalar_ref,
    sem,
    *,
    micros,
    count,
    states,
    chunks,
    clusters,
):
    rows = micros * count
    eighth = states // 2
    half, core, cube, face = (place_ref[k] for k in range(4))
    first = half == 0
    act_all = act_all_ref[...]
    own = dot(act_all, bc_own_ref[...].reshape(states, -1), 1, 1)
    other = dot(act_all, bc_other_ref[...].reshape(states, -1), 1, 1)
    bc_ref[:, :states] = jnp.where(first, own, other)
    bc_ref[:, states:] = jnp.where(first, other, own)
    copy = pltpu.make_async_copy(bc_ref, scalar_ref, sem)
    copy.start()

    fill_masks(len_ref, mask_ref, micros, count, 2, clusters)
    for chunk in range(chunks):
        cols = lanes(2 * chunk + half)
        own, other = alog_own_ref[:, cols], alog_other_ref[:, cols]
        tmp_ref[pl.ds(chunk * states, eighth), :] = jnp.where(first, own, other)
        tmp_ref[pl.ds(chunk * states + eighth, eighth), :] = jnp.where(first, other, own)
    for n in range(states):
        decay_ref[pl.ds(n * chunks, chunks), :] = -LOG2E * jnp.exp(
            tmp_ref[pl.ds(n, chunks, stride=states), :]
        )

    rank = dot(act_all, dtx_ref[...], 1, 1).astype(BF16)
    rank_ref[...] = rank
    rank_high_ref[...] = jnp.concatenate([jnp.zeros_like(rank), rank], axis=1)
    for chunk in range(chunks):
        cols = slice(chunk * LANES, (chunk + 1) * LANES)
        bias = bias_ref[pl.ds(2 * chunk + half, 1), :]
        step = softplus(dot(rank, dt_ref[:, lanes(2 * chunk + half)], 1, 0) + bias)
        held = step + RESET * mask_ref[0]
        source = step * act_ref[:, cols].astype(F32)
        for micro in range(micros):
            span = slice(micro * count, (micro + 1) * count)
            place = pl.ds((micro * chunks + chunk) * count, count)
            sp_ref[place, :] = held[span]
            u_ref[place, :] = source[span]
    copy.wait()

    for micro in range(micros):

        def advance(t, h, micro=micro):
            row = micro * count + t
            span = pl.ds(micro * chunks * count + t, chunks, stride=count)
            sp = sp_ref[span, :]
            u = u_ref[span, :]
            out = []
            y = None
            for n in range(states):
                decay = jnp.exp2(sp * decay_ref[pl.ds(n * chunks, chunks), :])
                now = decay * h[n] + u * scalar_ref[row, b_at(n, eighth)]
                out.append(now)
                term = now * scalar_ref[row, c_at(n, eighth)]
                y = term if y is None else y + term
            y_ref[span, :] = y
            return tuple(out)

        lax.fori_loop(0, count, advance, (jnp.zeros((chunks, LANES), F32),) * states, unroll=2)

    cotan = cotan_ref[...]
    for chunk in range(chunks):
        cols = slice(chunk * LANES, (chunk + 1) * LANES)
        places = [pl.ds((micro * chunks + chunk) * count, count) for micro in range(micros)]
        y = jnp.concatenate([y_ref[place, :] for place in places])
        y = y + skip_ref[pl.ds(2 * chunk + half, 1), :] * act_ref[:, cols].astype(F32)
        gate = gate_ref[:, cols]
        sig = sigmoid(gate)
        gated_ref[:, cols] = (y * (gate * sig)).astype(BF16)
        dgated = dot(cotan, wout_ref[chunk, 0], 1, 1)
        dy = dgated * (gate * sig)
        for micro in range(micros):
            dy_ref[places[micro], :] = dy[micro * count : (micro + 1) * count]
        dgate_ref[:, cols] = (dgated * y * (sig * (1.0 + gate * (1.0 - sig)))).astype(BF16)
    normed = normed_ref[...]
    edge = LANES // 2
    for j in range(chunks):
        relative = ((j & 1) << 2) | (((j >> 1) & 1) << 1) | (j >> 2)
        grad = dot(gated_ref[:, lanes(relative ^ cube)], cotan, 0, 0).astype(BF16)
        top, bottom = grad[:edge], grad[edge:]
        keep_ref[pl.ds(j * edge, edge), :] = jnp.where(core == 0, top, bottom)
        send_ref[pl.ds(j * edge, edge), :] = jnp.where(core == 0, bottom, top)
    for j in range(chunks // 2):
        place = pl.ds(chunks * edge + j * LANES, LANES)
        pair = 2 * (j ^ face)
        keep_ref[place, :] = dot(dgate_ref[:, lanes(pair + core)], normed, 0, 0).astype(BF16)
        send_ref[place, :] = dot(dgate_ref[:, lanes(pair + 1 - core)], normed, 0, 0).astype(BF16)
    width = cotan.shape[1]
    mixed_ref[...] = dot(gated_ref[...], wout_ref[...].reshape(chunks * LANES, width), 1, 0).astype(
        BF16
    )


def scan_forward(
    place,
    lengths,
    act_all,
    bc_own,
    bc_other,
    alog_own,
    alog_other,
    dtx,
    dt,
    bias,
    skip,
    act,
    gate,
    wout3,
    cotan,
    normed,
):
    rows, own = act.shape
    chunks = own // LANES
    states = 2 * alog_own.shape[0]
    width = cotan.shape[1]
    micros, _, clusters = lengths.shape
    ranks = dtx.shape[0]
    outs = [
        ((rows, 2 * states), F32),
        ((rows, ranks), BF16),
        ((rows, 2 * ranks), BF16),
        ((states * chunks, LANES), F32),
        ((chunks * rows, LANES), F32),
        ((chunks * rows, LANES), F32),
        ((chunks * rows, LANES), F32),
        ((rows, width), BF16),
        ((rows, own), BF16),
        ((own, width), BF16),
        ((own, width), BF16),
    ]
    operands = (
        act_all, bc_own, bc_other, alog_own, alog_other, dtx, dt, bias, skip, act, gate
    )
    return pl.pallas_call(
        functools.partial(
            forward_kernel,
            micros=micros,
            count=rows // micros,
            states=states,
            chunks=chunks,
            clusters=clusters,
        ),
        grid_spec=pltpu.PrefetchScalarGridSpec(
            num_scalar_prefetch=1,
            grid=(1,),
            in_specs=[pl.BlockSpec(memory_space=pltpu.SMEM)]
            + [whole(operand.shape) for operand in operands]
            + [
                pl.BlockSpec((chunks, 1, LANES, width), lambda i, p: (0, p[HALF], 0, 0)),
                whole((rows, width)),
                whole((rows, width)),
            ],
            out_specs=[whole(shape) for shape, _ in outs],
            scratch_shapes=[
                pltpu.VMEM((2, rows, LANES), F32),
                pltpu.VMEM((chunks * rows, LANES), F32),
                pltpu.VMEM((rows, own), BF16),
                pltpu.VMEM((states * chunks, LANES), F32),
                pltpu.SMEM((rows, 2 * states), F32),
                pltpu.SemaphoreType.DMA,
            ],
        ),
        out_shape=[jax.ShapeDtypeStruct(*out) for out in outs],
        compiler_params=params(48),
        cost_estimate=cost(19),
        name="scan_forward",
    )(place, lengths, *operands, wout3, cotan, normed)


def backward_kernel(
    place_ref,
    bc_ref,
    decay_ref,
    rank_ref,
    dt_ref,
    bias_ref,
    act_ref,
    sp_ref,
    u_ref,
    dy_ref,
    code_ref,
    sact_ref,
    dpre_ref,
    alog_ref,
    vec_ref,
    h_ref,
    s_ref,
    d_ref,
    terms_ref,
    sums_ref,
    scalar_ref,
    sem,
    *,
    count,
    states,
    chunks,
):
    copy = pltpu.make_async_copy(bc_ref, scalar_ref, sem)
    copy.start()
    half = place_ref[HALF]
    eighth = states // 2
    alog_ref[...] = jnp.zeros_like(alog_ref)
    zero = (jnp.zeros((chunks, LANES), F32),) * states
    for n in range(states):
        h_ref[pl.ds(n * chunks, chunks), :] = zero[0]
    copy.wait()

    def recompute(t, h):
        span = pl.ds(t, chunks, stride=count)
        sp = sp_ref[span, :]
        u = u_ref[span, :]
        out = []
        for n in range(states):
            decay = jnp.exp2(sp * decay_ref[pl.ds(n * chunks, chunks), :])
            now = decay * h[n] + u * scalar_ref[t, b_at(n, eighth)]
            h_ref[aligned(((t + 1) * states + n) * chunks, chunks), :] = now
            out.append(now)
        return tuple(out)

    lax.fori_loop(0, count, recompute, zero, unroll=2)

    def retreat(back, carry):
        t = count - 1 - back
        span = pl.ds(t, chunks, stride=count)
        sp = sp_ref[span, :]
        u = u_ref[span, :]
        dy = dy_ref[span, :]
        out = []
        d_sum = None
        s_sum = None
        for n in range(states):
            rate = decay_ref[pl.ds(n * chunks, chunks), :]
            decay = jnp.exp2(sp * rate)
            dh = carry[n] + dy * scalar_ref[t, c_at(n, eighth)]
            flow = decay * dh
            out.append(flow)
            before = h_ref[aligned((t * states + n) * chunks, chunks), :]
            now = h_ref[aligned(((t + 1) * states + n) * chunks, chunks), :]
            q = flow * before
            alog_ref[pl.ds(n * chunks, chunks), :] += q * sp
            d_term = q * rate
            s_term = dh * scalar_ref[t, b_at(n, eighth)]
            d_sum = d_term if d_sum is None else d_sum + d_term
            s_sum = s_term if s_sum is None else s_sum + s_term
            terms_ref[pl.ds(b_at(n, eighth) * chunks, chunks), :] = dh * u
            terms_ref[pl.ds(c_at(n, eighth) * chunks, chunks), :] = dy * now
        s_ref[span, :] = s_sum
        d_ref[span, :] = d_sum
        sums = None
        for chunk in range(chunks):
            term = terms_ref[pl.ds(chunk, 2 * states, stride=chunks), :]
            sums = term if sums is None else sums + term
        sums_ref[aligned(t * 2 * states, 2 * states), :] = sums
        return tuple(out)

    lax.fori_loop(0, count, retreat, zero, unroll=2)

    rank = rank_ref[...]
    ranks = rank.shape[1]
    drank = None
    for chunk in range(chunks):
        cols = slice(chunk * LANES, (chunk + 1) * LANES)
        place = pl.ds(chunk * count, count)
        act = act_ref[:, cols].astype(F32)
        weight = dt_ref[:, lanes(2 * chunk + half)]
        pre = dot(rank, weight, 1, 0) + bias_ref[pl.ds(2 * chunk + half, 1), :]
        s_now = s_ref[place, :]
        dstep = d_ref[place, :] * (1.0 / LOG2E) + s_now * act
        sact_ref[:, cols] = s_now * softplus(pre)
        dpre = dstep * sigmoid(pre)
        vec_ref[0:1, cols] = jnp.sum(dpre, axis=0, keepdims=True)
        vec_ref[1:2, cols] = jnp.sum(dy_ref[place, :] * act, axis=0, keepdims=True)
        low = dpre.astype(BF16)
        dpre_ref[:, cols] = low
        term = dot(low, weight, 1, 1)
        drank = term if drank is None else drank + term
    source = lax.broadcasted_iota(jnp.int32, (2 * LANES, LANES), 0) // LANES
    target = lax.broadcasted_iota(jnp.int32, (2 * LANES, LANES), 1)
    code = None
    for k in range(states):
        pair = jnp.concatenate(
            [sums_ref[pl.ds(2 * k + j, count, stride=2 * states), :] for j in range(2)], axis=1
        )
        pick = jnp.where(target == source + (ranks + 2 * k), 1.0, 0.0).astype(BF16)
        term = dot(pair.astype(BF16), pick, 1, 0)
        code = term if code is None else code + term
    code_ref[...] = code + jnp.concatenate([drank, jnp.zeros((count, LANES - ranks), F32)], axis=1)


def scan_backward(place, micro, count, bc, decay, rank, dt, bias, act, sp, u, dy):
    rows, own = act.shape
    chunks = own // LANES
    states = bc.shape[1] // 2
    ranks = rank.shape[1]
    outs = [
        ((count, LANES), F32),
        ((count, own), F32),
        ((count, own), BF16),
        ((states * chunks, LANES), F32),
        ((2, own), F32),
    ]

    def block(*shape):
        return pl.BlockSpec(shape, lambda i, p: (micro, 0))

    return pl.pallas_call(
        functools.partial(backward_kernel, count=count, states=states, chunks=chunks),
        grid_spec=pltpu.PrefetchScalarGridSpec(
            num_scalar_prefetch=1,
            grid=(1,),
            in_specs=[
                block(count, 2 * states),
                whole(decay.shape),
                block(count, ranks),
                whole(dt.shape),
                whole(bias.shape),
                block(count, own),
                block(chunks * count, LANES),
                block(chunks * count, LANES),
                block(chunks * count, LANES),
            ],
            out_specs=[whole(shape) for shape, _ in outs],
            scratch_shapes=[
                pltpu.VMEM(((count + 1) * states * chunks, LANES), F32),
                pltpu.VMEM((chunks * count, LANES), F32),
                pltpu.VMEM((chunks * count, LANES), F32),
                pltpu.VMEM((2 * states * chunks, LANES), F32),
                pltpu.VMEM((count * 2 * states, LANES), F32),
                pltpu.SMEM((count, 2 * states), F32),
                pltpu.SemaphoreType.DMA,
            ],
        ),
        out_shape=[jax.ShapeDtypeStruct(*out) for out in outs],
        compiler_params=params(26),
        cost_estimate=cost(14),
        name="scan_backward",
    )(place, bc, decay, rank, dt, bias, act, sp, u, dy)


def tail_kernel(
    place_ref,
    len_ref,
    *refs,
    micros,
    count,
    taps,
    clusters,
    ranks,
    chunks,
    states,
):
    def take(number):
        nonlocal refs
        taken, refs = refs[:number], refs[number:]
        return taken

    code_own, code_other, sact_refs, dpre_refs, alog_refs, back_refs = (
        take(micros) for _ in range(6)
    )
    dtx_ref, bc_own_ref, bc_other_ref, decay_ref = take(4)
    dy_refs = take(micros)
    conved_ref, inner_ref, act_ref, dgate_ref, high_ref, convw_ref, skip_ref = take(7)
    (normed_ref,) = take(1)
    keep_ref, send_ref, low_ref = take(3)
    mask_ref, code_ref, wcode_ref, vec_ref, alog_ref = refs

    step = pl.program_id(0)
    rows = micros * count
    eighth = states // 2
    edge = LANES // 2
    half, core, cube, face = (place_ref[k] for k in range(4))
    pair = step ^ face
    span = 3 * edge // 2

    def pack_row(chunk):
        relative = chunk ^ cube
        zh, zl, x = relative >> 2, (relative >> 1) & 1, relative & 1
        return (2 * x + zl) * span + edge + zh * 16

    def place_pair(start, size, cols, even, odd):
        keep_ref[aligned(start, size, 16), cols] = jnp.where(core == 0, even, odd).astype(BF16)
        send_ref[aligned(start, size, 16), cols] = jnp.where(core == 0, odd, even).astype(BF16)

    @pl.when(step == 0)
    def _():
        fill_masks(len_ref, mask_ref, micros, count, taps, clusters)
        for micro in range(micros):
            code_ref[pl.ds(micro * count, count), :] = (
                code_own[micro][...] + code_other[micro][...]
            ).astype(BF16)
        total = None
        for micro in range(micros):
            term = alog_refs[micro][...]
            total = term if total is None else total + term
        alog_ref[...] = total * (decay_ref[...] * (1.0 / LOG2E))

    code = code_ref[...]
    lane = lax.broadcasted_iota(jnp.int32, (1, LANES), 1)
    code_rank = jnp.where(lane < ranks, code, jnp.zeros_like(code))
    dpre = jnp.concatenate([ref[...] for ref in dpre_refs], axis=0)
    for part in range(2):
        source = lanes(2 * (2 * pair + part) + half)
        cols = slice(part * LANES, (part + 1) * LANES)
        wcode_ref[:ranks, cols] = dtx_ref[:, source]
        own = bc_own_ref[:, :, source].reshape(states, LANES)
        other = bc_other_ref[:, :, source].reshape(states, LANES)
        wcode_ref[ranks : ranks + states, cols] = jnp.where(half == 0, own, other)
        wcode_ref[ranks + states : ranks + 2 * states, cols] = jnp.where(half == 0, other, own)
        wcode_ref[ranks + 2 * states :, cols] = jnp.zeros(
            (LANES - ranks - 2 * states, LANES), BF16
        )
    for part in range(2):
        cols = slice(part * LANES, (part + 1) * LANES)
        chunk = 2 * pair + part
        source = 2 * chunk + half
        weights = convw_ref[:, lanes(source)]
        sact = jnp.concatenate([ref[:, cols] for ref in sact_refs], axis=0)
        dy = jnp.concatenate([ref[pl.ds(part * count, count), :] for ref in dy_refs], axis=0)
        dact = sact + dot(code, wcode_ref[:, cols], 1, 0)
        dact = dact + dy * skip_ref[pl.ds(source, 1), :]
        conved = conved_ref[:, cols]
        sig = sigmoid(conved)
        dconv = dact * (sig * (1.0 + conved * (1.0 - sig)))
        inner = inner_ref[:, cols]
        dinner = weights[taps - 1 : taps] * dconv
        sums = [None] * (taps + 1)
        sums[taps - 1] = jnp.sum(dconv * inner, axis=0, keepdims=True)
        sums[taps] = jnp.sum(dconv, axis=0, keepdims=True)
        for back in range(1, taps):
            kept = dconv * mask_ref[back]
            dinner = dinner + weights[taps - 1 - back : taps - back] * pltpu.roll(
                kept, rows - back, 0
            )
            sums[taps - 1 - back] = jnp.sum(
                kept * pltpu.roll(inner, back, 0), axis=0, keepdims=True
            )
        for k in range(taps + 1):
            vec_ref[k : k + 1, lanes(chunk)] = sums[k]
        for k in range(2):
            total = None
            for ref in back_refs:
                term = ref[k : k + 1, lanes(chunk)]
                total = term if total is None else total + term
            vec_ref[taps + 1 + k : taps + 2 + k, lanes(chunk)] = total
        low_ref[:, cols] = dinner.astype(BF16)

        act = act_ref[:, cols]
        start = pack_row(chunk)
        rows_now = dot(act, code_rank, 0, 0) + dot(dpre[:, cols], high_ref[...], 0, 0)
        for k in range(4):
            place_pair(
                start,
                16,
                slice(k * LANES, (k + 1) * LANES),
                rows_now[k * 16 : (k + 1) * 16],
                rows_now[edge + k * 16 : edge + (k + 1) * 16],
            )
        state_rows = dot(code, act, 0, 0)[ranks : ranks + 2 * states]
        place_pair(
            start, 16, slice(4 * LANES, 5 * LANES), state_rows[:states], state_rows[states:]
        )

    zl, x_bit = step >> 1, step & 1
    normed = normed_ref[...]
    for part in range(2):
        grad = dot(low_ref[:, lanes(core ^ part)], normed, 0, 0).astype(BF16)
        out_ref = (keep_ref, send_ref)[part]
        out_ref[aligned((2 * x_bit + zl) * span, edge, 16), :] = grad[:edge]
        out_ref[aligned(4 * span + step * edge, edge, 16), :] = grad[edge:]

    @pl.when(step == pl.num_programs(0) - 1)
    def _():
        vec_ref[taps + 3 : taps + 4, :] = jnp.zeros_like(vec_ref[taps + 3 : taps + 4, :])
        for chunk in range(chunks):
            start = pack_row(chunk)
            vec = vec_ref[:, chunk * LANES : (chunk + 1) * LANES]
            alog = [
                alog_ref[pl.ds(q * eighth * chunks + chunk, eighth, stride=chunks), :]
                for q in range(2)
            ]
            place_pair(
                start,
                16,
                slice(5 * LANES, 6 * LANES),
                jnp.concatenate([alog[0], vec]),
                jnp.concatenate([alog[1], pltpu.roll(vec, edge, 1)]),
            )
            blank = jnp.zeros((16, 2 * LANES), F32)
            place_pair(start, 16, slice(6 * LANES, 8 * LANES), blank, blank)


def tail(
    place,
    lengths,
    code_own,
    code_other,
    sact,
    dpre,
    alog,
    back,
    dtx,
    bc_own,
    bc_other,
    decay,
    dy,
    conved,
    inner,
    act,
    dgate,
    high,
    convw,
    skip,
    normed,
):
    rows, own = act.shape
    chunks = own // LANES
    width = normed.shape[1]
    micros, _, clusters = lengths.shape
    count = rows // micros
    taps = convw.shape[0]
    ranks = dtx.shape[0]
    states = decay.shape[0] // chunks
    cols = 2 * LANES
    extent = chunks * LANES // 2 + 2 * chunks * 8

    def by_cols(height):
        return pl.BlockSpec((height, cols), lambda i, p: (0, i ^ p[FACE]))

    def dy_spec(micro):
        return pl.BlockSpec(
            (2 * count, LANES), lambda i, p: (micro * (chunks // 2) + (i ^ p[FACE]), 0)
        )

    in_specs = (
        [pl.BlockSpec(memory_space=pltpu.SMEM)]
        + [whole((count, LANES))] * (2 * micros)
        + [by_cols(count)] * (2 * micros)
        + [whole(alog[0].shape)] * micros
        + [whole(back[0].shape)] * micros
        + [whole(array.shape) for array in (dtx, bc_own, bc_other, decay)]
        + [dy_spec(micro) for micro in range(micros)]
        + [by_cols(rows)] * 4
        + [whole(array.shape) for array in (high, convw, skip)]
        + [whole((rows, width))]
    )
    return pl.pallas_call(
        functools.partial(
            tail_kernel,
            micros=micros,
            count=count,
            taps=taps,
            clusters=clusters,
            ranks=ranks,
            chunks=chunks,
            states=states,
        ),
        grid_spec=pltpu.PrefetchScalarGridSpec(
            num_scalar_prefetch=1,
            grid=(chunks // 2,),
            in_specs=in_specs,
            out_specs=[whole((extent, width)), whole((extent, width)), by_cols(rows)],
            scratch_shapes=[
                pltpu.VMEM((taps, rows, LANES), F32),
                pltpu.VMEM((rows, LANES), BF16),
                pltpu.VMEM((LANES, cols), BF16),
                pltpu.VMEM((8, own), F32),
                pltpu.VMEM((states * chunks, LANES), F32),
            ],
        ),
        out_shape=[
            jax.ShapeDtypeStruct((extent, width), BF16),
            jax.ShapeDtypeStruct((extent, width), BF16),
            jax.ShapeDtypeStruct((rows, own), BF16),
        ],
        compiler_params=params(24),
        cost_estimate=cost(7),
        name="tail",
    )(
        place,
        lengths,
        *code_own,
        *code_other,
        *sact,
        *dpre,
        *alog,
        *back,
        dtx,
        bc_own,
        bc_other,
        decay,
        *([dy] * micros),
        conved,
        inner,
        act,
        dgate,
        high,
        convw,
        skip,
        normed,
    )


def spread_kernel(
    place_ref, low_ref, dgate_ref, win_ref, wgate_ref, x_ref, dnormed_ref, gain_ref, total_ref
):
    step = pl.program_id(0)
    width = x_ref.shape[1]

    @pl.when(step == 0)
    def _():
        total_ref[...] = jnp.zeros_like(total_ref)

    total_ref[...] += dot(low_ref[...], win_ref[...].reshape(-1, width), 1, 0) + dot(
        dgate_ref[...], wgate_ref[...].reshape(-1, width), 1, 0
    )

    @pl.when(step == pl.num_programs(0) - 1)
    def _():
        total = total_ref[...]
        x = x_ref[...].astype(F32)
        scale = lax.rsqrt(jnp.mean(x * x, axis=1, keepdims=True) + EPSILON)
        gain_ref[...] = jnp.sum(total * (x * scale), axis=0, keepdims=True)
        dnormed_ref[...] = total.astype(BF16)


def spread(place, low, dgate, w4, x):
    rows, own = low.shape
    width = x.shape[1]
    pairs = own // (2 * LANES)
    by_cols = pl.BlockSpec((rows, 2 * LANES), lambda i, p: (0, i))

    def weight_spec(which):
        return pl.BlockSpec((1, 2, 1, LANES, width), lambda i, p: (which, i, p[HALF], 0, 0))

    return pl.pallas_call(
        spread_kernel,
        grid_spec=pltpu.PrefetchScalarGridSpec(
            num_scalar_prefetch=1,
            grid=(pairs,),
            in_specs=[by_cols, by_cols, weight_spec(0), weight_spec(1), whole((rows, width))],
            out_specs=[whole((rows, width)), whole((1, width))],
            scratch_shapes=[pltpu.VMEM((rows, width), F32)],
        ),
        out_shape=[
            jax.ShapeDtypeStruct((rows, width), BF16),
            jax.ShapeDtypeStruct((1, width), F32),
        ],
        compiler_params=params(16),
        cost_estimate=cost(4),
        name="spread",
    )(place, low, dgate, w4, w4, x)


def swap_pair(array):
    count = lax.axis_size("state")
    return lax.ppermute(array, "state", [(pos, pos ^ 1) for pos in range(count)])


def swap_bit(array, bit, source=None):
    pairs = [
        (pos, pos ^ bit)
        for pos in range(lax.axis_size("dp"))
        if source is None or bool(pos & bit) == source
    ]
    return lax.ppermute(array, "dp", pairs)


def swap_odd(array):
    parts, states = lax.axis_size("dp"), lax.axis_size("state")
    pairs = []
    for d in range(parts):
        for s in range(states):
            at = d * states + s
            to = at if d % 2 == s % 2 else (d ^ 1) * states + (s ^ 1)
            pairs.append((at, to))
    return lax.ppermute(array, ("dp", "state"), pairs)


def halves(kept, got):
    middle = kept.shape[0] // 2
    return kept[:middle] + got[:middle], kept[middle:] + got[middle:]


CORE_BIT, X_BIT, ZL_BIT, ZH_BIT = 1, 2, 4, 8


def shards(
    tokens,
    cluster_len,
    norm_gain,
    in_weight,
    conv_weight,
    conv_bias,
    dtx_weight,
    dt_weight,
    dt_bias,
    bc_weight,
    a_log,
    skip_gain,
    out_weight,
    cotangent,
):
    micros, count, width = tokens.shape
    inner = out_weight.shape[0]
    taps = conv_weight.shape[0]
    ranks = dtx_weight.shape[1]
    chunks = inner // (2 * LANES)
    own = chunks * LANES
    rows = micros * count
    edge = LANES // 2
    span = 3 * edge // 2
    dp_parts = lax.axis_size("dp")
    state_count = lax.axis_size("state")
    dp_pos = lax.axis_index("dp")
    state_pos = lax.axis_index("state")
    half = state_pos & 1
    fast = state_count == 2 and dp_parts == 2 * chunks == 16
    if fast:
        place = jnp.stack([half, dp_pos & 1, dp_pos >> 1, (dp_pos >> 1) & 3])
        bc_own, alog_own = bc_weight, a_log
        bc_other, alog_other = swap_pair(bc_weight), swap_pair(a_log)
    else:
        place = jnp.stack([half, 0, 0, 0])
        bc_all = lax.all_gather(bc_weight, "state", axis=1, tiled=True)
        alog_all = lax.all_gather(a_log, "state", axis=0, tiled=True)
        eighth = alog_all.shape[0] // 2
        bc_own, bc_other = (
            lax.dynamic_slice_in_dim(bc_all, which * eighth, eighth, 1)
            for which in (half, 1 - half)
        )
        alog_own, alog_other = (
            lax.dynamic_slice_in_dim(alog_all, which * eighth, eighth, 0)
            for which in (half, 1 - half)
        )
    place = place.astype(jnp.int32)
    eighth = alog_own.shape[0]
    states = 2 * eighth

    x = tokens.reshape(rows, width)
    cotan = cotangent.reshape(rows, width)
    w4 = in_weight.reshape(2, chunks, 2, LANES, width)
    wout3 = out_weight.reshape(chunks, 2, LANES, width)
    dtx, dt = dtx_weight.T, dt_weight.T
    bias = dt_bias.reshape(-1, LANES)
    skip = skip_gain.reshape(-1, LANES)

    normed, act_all, act, inner_own, conved, gate = project(
        place, cluster_len, x, norm_gain[None], w4, conv_weight, conv_bias.reshape(-1, LANES)
    )
    bc, rank, high, decay, sp, u, dy, mixed_part, dgate, keep, send = scan_forward(
        place,
        cluster_len,
        act_all,
        bc_own,
        bc_other,
        alog_own,
        alog_other,
        dtx,
        dt,
        bias,
        skip,
        act,
        gate,
        wout3,
        cotan,
        normed,
    )
    early = None
    if fast:
        early = swap_bit(send, CORE_BIT)
    mixed_other = swap_pair(mixed_part)

    results = []
    for micro in range(micros):
        if fast and micro == micros - 1:
            cut = chunks * edge
            out_keep, out_send = halves(keep[:cut], early[:cut])
            gate_keep, gate_send = halves(keep[cut:], early[cut:])
            out_send, gate_send, mixed_other, sp = lax.optimization_barrier(
                (out_send, gate_send, mixed_other, sp)
            )
            out_got = swap_bit(out_send, X_BIT)
            gate_got = swap_bit(gate_send, ZL_BIT)
        results.append(
            scan_backward(place, micro, count, bc, decay, rank, dt, bias, act, sp, u, dy)
        )
    code_own, sact, dpre, alog, back = zip(*results)
    code_other = [swap_pair(code) for code in code_own]
    if fast:
        out_keep, out_send = halves(out_keep, out_got)
        gate_keep, gate_send = halves(gate_keep, gate_got)
        out_send, gate_send, dgate = lax.optimization_barrier((out_send, gate_send, dgate))
        out_got = swap_bit(out_send, ZL_BIT)
        gate_got = swap_bit(gate_send, X_BIT)
    late_keep, late_send, low = tail(
        place,
        cluster_len,
        code_own,
        code_other,
        sact,
        dpre,
        alog,
        back,
        dtx,
        bc_own,
        bc_other,
        decay,
        dy,
        conved,
        inner_own,
        act,
        dgate,
        high,
        conv_weight,
        skip,
        normed,
    )
    if fast:
        late = swap_bit(late_send, CORE_BIT)
        out_keep, out_send = halves(out_keep, out_got)
        gate_sum = gate_keep + gate_got
        out_send, gate_sum, low = lax.optimization_barrier((out_send, gate_sum, low))
    dnormed_part, gain_part = spread(place, low, dgate, w4, x)
    dnormed_other = swap_pair(dnormed_part)
    gain_sum = lax.psum(gain_part[0], ("dp", "state") if fast else "dp")
    if fast:
        out_got = swap_bit(out_send, ZH_BIT)
        gate_got = swap_bit(gate_sum, ZH_BIT, False)
        cut = 4 * span
        a_keep, a_send = halves(late_keep[:cut], late[:cut])
        b_keep, b_send = halves(late_keep[cut:], late[cut:])
        a_got = swap_bit(a_send, X_BIT)
        b_got = swap_bit(b_send, ZL_BIT)
        _, dnormed_other = lax.optimization_barrier((b_got, dnormed_other))
        a_keep, a_send = halves(a_keep, a_got)
        b_keep, b_send = halves(b_keep, b_got)
        a_got = swap_bit(a_send, ZL_BIT)
        b_got = swap_bit(b_send, X_BIT)
        inner_sum = jnp.concatenate([a_keep[:edge] + a_got[:edge], b_keep + b_got])
        pack_keep, pack_send = halves(a_keep[edge:], a_got[edge:])
        inner_got = swap_bit(inner_sum, ZH_BIT, True)
        pack_got = swap_bit(pack_send, ZH_BIT)
        out_own = swap_odd(out_keep + out_got).astype(F32)
        upper = dp_pos >= dp_parts // 2
        in_grad = jnp.where(
            upper,
            gate_sum.astype(F32) + gate_got.astype(F32),
            inner_sum.astype(F32) + inner_got.astype(F32),
        )
        pack = pack_keep + pack_got
        extent = width // (dp_parts * state_count)
        gain_grad = lax.dynamic_slice_in_dim(
            gain_sum, (dp_pos * state_count + state_pos) * extent, extent, 0
        )
        pack = swap_odd(pack).astype(F32)
        small = jnp.concatenate([pack[:, k * LANES : (k + 1) * LANES] for k in range(4)])
        dtx_grad, dt_grad = small[:, :ranks], small[:, ranks:]
        bc_grad = pack[:, 4 * LANES : 5 * LANES].reshape(2, eighth, LANES)
        alog_grad = pack[:eighth, 5 * LANES : 6 * LANES]
        vec = pack[eighth:, 5 * LANES : 5 * LANES + edge]

    mixed = (x.astype(F32) + (mixed_part.astype(F32) + mixed_other.astype(F32))).astype(BF16)
    dnormed = dnormed_part.astype(F32) + dnormed_other.astype(F32)
    x32 = x.astype(F32)
    scale = lax.rsqrt(jnp.mean(x32 * x32, axis=1, keepdims=True) + EPSILON)
    unit = x32 * scale
    dhat = dnormed * norm_gain
    tokens_grad = cotan.astype(F32) + scale * (
        dhat - unit * jnp.mean(dhat * unit, axis=1, keepdims=True)
    )
    mixed = mixed.reshape(micros, count, width)
    tokens_grad = tokens_grad.reshape(micros, count, width)

    if not fast:
        def total(array):
            return lax.psum(array.astype(F32), "dp")

        def both_rows(array):
            mine = array.reshape(chunks, 1, LANES, -1)
            other = swap_pair(mine)
            low = jnp.where(half == 0, mine, other)
            high = jnp.where(half == 0, other, mine)
            return jnp.concatenate([low, high], axis=1).reshape(2 * own, -1)

        every = dp_parts * state_count
        at = dp_pos * state_count + state_pos

        def cut_own(array):
            extent = array.shape[0] // every
            return lax.dynamic_slice_in_dim(array, at * extent, extent, 0)

        pair = total(jnp.stack([keep, send]))
        outs = pair[:, : chunks * edge].reshape(2, 2, 2, 2, edge, width)
        outs = jnp.transpose(outs, (3, 2, 1, 0, 4, 5)).reshape(own, width)
        gates = pair[:, chunks * edge :].reshape(2, chunks // 2, LANES, width)
        gates = jnp.moveaxis(gates, 0, 1).reshape(own, width)
        pair = total(jnp.stack([late_keep, late_send]))
        a_part = pair[:, : 4 * span].reshape(2, 2, 2, span, width)
        b_part = pair[:, 4 * span :].reshape(2, 2, 2, edge, width)
        inners = jnp.concatenate(
            [jnp.transpose(a_part[:, :, :, :edge], (2, 1, 0, 3, 4)), jnp.moveaxis(b_part, 0, 2)],
            axis=3,
        ).reshape(own, width)
        packs = a_part[:, :, :, edge:].reshape(2, 2, 2, 2, 16, width // LANES, LANES)
        packs = jnp.transpose(packs, (3, 2, 1, 0, 5, 4, 6)).reshape(chunks, 2, -1, 16, LANES)
        small = both_rows(packs[:, :, :4].reshape(own, LANES))
        in_grad = cut_own(jnp.concatenate([both_rows(inners), both_rows(gates)]))
        out_own = cut_own(both_rows(outs))
        mine = cut_own(small)
        dtx_grad, dt_grad = mine[:, :ranks], mine[:, ranks:]
        vec_rows = jnp.swapaxes(packs[:, :, 5, eighth:, :edge], 2, 3).reshape(own, -1)
        gain_grad = cut_own(gain_sum + swap_pair(gain_sum))
        vec = cut_own(both_rows(vec_rows)).T
        state_rows = jnp.concatenate([packs[:, :, 4], packs[:, :, 5, :eighth]], axis=2)
        state_rows = state_rows.reshape(chunks, 2, 3, eighth, LANES)
        state_rows = jnp.transpose(state_rows, (0, 4, 2, 1, 3)).reshape(own, -1)
        extent = inner // dp_parts
        state_part = lax.dynamic_slice_in_dim(both_rows(state_rows), dp_pos * extent, extent, 0)
        state_part = state_part.T.reshape(3, state_count, -1, extent)
        state_part = lax.dynamic_index_in_dim(state_part, state_pos, 1, keepdims=False)
        bc_grad, alog_grad = state_part[:2], state_part[2]

    return (
        mixed,
        tokens_grad,
        gain_grad,
        in_grad,
        vec[:taps],
        vec[taps],
        dtx_grad,
        dt_grad,
        vec[taps + 1],
        bc_grad,
        alog_grad,
        vec[taps + 2],
        out_own,
    )


def solution(mesh):
    return jax.shard_map(
        shards,
        mesh=mesh,
        in_specs=(
            P(None, "dp", None),
            P(None, "dp", None),
            P(),
            P(),
            P(),
            P(),
            P(),
            P(),
            P(),
            P(None, "state", None),
            P("state", None),
            P(),
            P(),
            P(None, "dp", None),
        ),
        out_specs=(
            P(None, "dp", None),
            P(None, "dp", None),
            P(("dp", "state")),
            P(("dp", "state"), None),
            P(None, ("dp", "state")),
            P(("dp", "state")),
            P(("dp", "state"), None),
            P(("dp", "state"), None),
            P(("dp", "state")),
            P(None, "state", "dp"),
            P("state", "dp"),
            P(("dp", "state")),
            P(("dp", "state"), None),
        ),
        check_vma=False,
    )
```

```python
import functools
import math

import jax
import jax.numpy as jnp
from jax import lax
from jax.experimental import pallas as pl
from jax.experimental.pallas import tpu as pltpu
from jax.sharding import PartitionSpec as P

EPSILON = 1e-05
LANES = 128
RESET = 1e4
LOG2E = math.log2(math.e)
F32 = jnp.float32
BF16 = jnp.bfloat16
MIB = 1024 * 1024


def dot(left, right, left_dim, right_dim):
    return lax.dot_general(
        left, right, (((left_dim,), (right_dim,)), ((), ())), preferred_element_type=F32
    )


def params(mib):
    return pltpu.CompilerParams(
        vmem_limit_bytes=mib * MIB, dimension_semantics=("arbitrary",)
    )


def cost(micros):
    return pl.CostEstimate(
        flops=int(micros * 1e9), bytes_accessed=int(micros * 1e6), transcendentals=0
    )


def whole(shape):
    return pl.BlockSpec(shape, lambda *_: (0,) * len(shape))


sigmoid = jax.nn.sigmoid


def softplus(value):
    return jnp.maximum(value, 0.0) + jnp.log1p(jnp.exp(-jnp.abs(value)))


def lanes(index):
    return pl.ds(pl.multiple_of(index * LANES, LANES), LANES)


def in_hbm(arrays):
    return [pltpu.with_memory_space_constraint(array, pltpu.HBM) for array in arrays]


def aligned(start, size, to=8):
    return pl.ds(pl.multiple_of(start, to), size)


HALF, CORE, CUBE, FACE = range(4)


def fill_masks(len_ref, mask_ref, micros, count, taps, clusters):
    place = lax.broadcasted_iota(jnp.int32, (count, LANES), 0)
    for micro in range(micros):
        rows = pl.ds(micro * count, count)
        for back in range(1, taps):
            apart = place < back
            start = 0
            for cluster in range(clusters - 1):
                start = start + len_ref[micro, 0, cluster]
                apart = apart | ((place >= start) & (place < start + back))
            mask_ref[back, rows, :] = jnp.where(apart, 0.0, 1.0)
            if back == 1:
                mask_ref[0, rows, :] = jnp.where(apart, 1.0, 0.0)


def project_kernel(
    place_ref,
    len_ref,
    x_ref,
    gain_ref,
    win_ref,
    wgate_ref,
    convw_ref,
    convb_ref,
    normed_ref,
    act_ref,
    own_act_ref,
    inner_ref,
    conved_ref,
    gate_ref,
    mask_ref,
    proj_ref,
    conv_ref,
    *,
    micros,
    count,
    taps,
    clusters,
):
    chunk = pl.program_id(0)

    @pl.when(chunk == 0)
    def _():
        fill_masks(len_ref, mask_ref, micros, count, taps, clusters)
        rows = x_ref[...].astype(F32)
        scale = lax.rsqrt(jnp.mean(rows * rows, axis=1, keepdims=True) + EPSILON)
        normed_ref[...] = (rows * scale * gain_ref[...]).astype(BF16)

    half = place_ref[HALF]
    normed = normed_ref[...]
    proj_ref[...] = dot(normed, win_ref[...].reshape(2 * LANES, -1), 1, 1)
    gate_ref[...] = dot(normed, wgate_ref[...].reshape(LANES, -1), 1, 1)
    for part in range(2):
        cols = pl.ds(part * LANES, LANES)
        inner = proj_ref[:, cols]
        conved = convb_ref[pl.ds(2 * chunk + part, 1), :] + convw_ref[taps - 1 : taps, cols] * inner
        for back in range(1, taps):
            shifted = pltpu.roll(inner, back, 0) * mask_ref[back]
            conved = conved + convw_ref[taps - 1 - back : taps - back, cols] * shifted
        conv_ref[:, cols] = conved
        act_ref[:, cols] = (conved * sigmoid(conved)).astype(BF16)
    own = lanes(half)
    inner_ref[...] = proj_ref[:, own]
    conved_ref[...] = conv_ref[:, own]
    own_act_ref[...] = act_ref[:, own]


def project(place, lengths, x, gain, w4, conv_weight, conv_bias):
    rows, width = x.shape
    chunks = w4.shape[1]
    inner = chunks * 2 * LANES
    micros, _, clusters = lengths.shape
    taps = conv_weight.shape[0]
    own = chunks * LANES
    by_chunk = pl.BlockSpec((rows, LANES), lambda i, p: (0, i))
    return pl.pallas_call(
        functools.partial(
            project_kernel, micros=micros, count=rows // micros, taps=taps, clusters=clusters
        ),
        grid_spec=pltpu.PrefetchScalarGridSpec(
            num_scalar_prefetch=1,
            grid=(chunks,),
            in_specs=[
                pl.BlockSpec(memory_space=pltpu.SMEM),
                whole((rows, width)),
                whole((1, width)),
                pl.BlockSpec((1, 1, 2, LANES, width), lambda i, p: (0, i, 0, 0, 0)),
                pl.BlockSpec((1, 1, 1, LANES, width), lambda i, p: (1, i, p[HALF], 0, 0)),
                pl.BlockSpec((taps, 2 * LANES), lambda i, p: (0, i)),
                whole(conv_bias.shape),
            ],
            out_specs=[
                whole((rows, width)),
                pl.BlockSpec((rows, 2 * LANES), lambda i, p: (0, i)),
                by_chunk,
                by_chunk,
                by_chunk,
                by_chunk,
            ],
            scratch_shapes=[
                pltpu.VMEM((taps, rows, LANES), F32),
                pltpu.VMEM((rows, 2 * LANES), F32),
                pltpu.VMEM((rows, 2 * LANES), F32),
            ],
        ),
        out_shape=[
            jax.ShapeDtypeStruct((rows, width), BF16),
            jax.ShapeDtypeStruct((rows, inner), BF16),
            jax.ShapeDtypeStruct((rows, own), BF16),
            jax.ShapeDtypeStruct((rows, own), F32),
            jax.ShapeDtypeStruct((rows, own), F32),
            jax.ShapeDtypeStruct((rows, own), F32),
        ],
        compiler_params=params(16),
        cost_estimate=cost(6),
        name="project",
    )(place, *in_hbm((lengths, x, gain, w4, w4, conv_weight, conv_bias)))


def eight_rows(array):
    return jnp.sum(array.reshape(-1, 8, array.shape[1]), axis=0)


def b_at(n, eighth):
    return (n // eighth) * 2 * eighth + n % eighth


def c_at(n, eighth):
    return b_at(n, eighth) + eighth


def forward_kernel(
    place_ref,
    len_ref,
    act_all_ref,
    bc_own_ref,
    bc_other_ref,
    alog_own_ref,
    alog_other_ref,
    dtx_ref,
    dt_ref,
    bias_ref,
    skip_ref,
    act_ref,
    gate_ref,
    wout_ref,
    cotan_ref,
    normed_ref,
    wgate_ref,
    bc_ref,
    rank_ref,
    rank_high_ref,
    decay_ref,
    sp_ref,
    u_ref,
    dy_ref,
    mixed_ref,
    dgate_ref,
    keep_ref,
    send_ref,
    share_ref,
    mask_ref,
    y_ref,
    gated_ref,
    tmp_ref,
    scalar_ref,
    sem,
    *,
    micros,
    count,
    states,
    chunks,
    clusters,
):
    rows = micros * count
    eighth = states // 2
    half, core, cube, face = (place_ref[k] for k in range(4))
    first = half == 0
    act_all = act_all_ref[...]
    own = dot(act_all, bc_own_ref[...].reshape(states, -1), 1, 1)
    other = dot(act_all, bc_other_ref[...].reshape(states, -1), 1, 1)
    bc_ref[:, :states] = jnp.where(first, own, other)
    bc_ref[:, states:] = jnp.where(first, other, own)
    copy = pltpu.make_async_copy(bc_ref, scalar_ref, sem)
    copy.start()

    fill_masks(len_ref, mask_ref, micros, count, 2, clusters)
    for chunk in range(chunks):
        cols = lanes(2 * chunk + half)
        own, other = alog_own_ref[:, cols], alog_other_ref[:, cols]
        tmp_ref[pl.ds(chunk * states, eighth), :] = jnp.where(first, own, other)
        tmp_ref[pl.ds(chunk * states + eighth, eighth), :] = jnp.where(first, other, own)
    for n in range(states):
        decay_ref[pl.ds(n * chunks, chunks), :] = -LOG2E * jnp.exp(
            tmp_ref[pl.ds(n, chunks, stride=states), :]
        )

    rank = dot(act_all, dtx_ref[...], 1, 1).astype(BF16)
    rank_ref[...] = rank
    rank_high_ref[...] = jnp.concatenate([jnp.zeros_like(rank), rank], axis=1)
    for chunk in range(chunks):
        cols = slice(chunk * LANES, (chunk + 1) * LANES)
        bias = bias_ref[pl.ds(2 * chunk + half, 1), :]
        step = softplus(dot(rank, dt_ref[:, lanes(2 * chunk + half)], 1, 0) + bias)
        held = step + RESET * mask_ref[0]
        source = step * act_ref[:, cols].astype(F32)
        for micro in range(micros):
            span = slice(micro * count, (micro + 1) * count)
            place = pl.ds((micro * chunks + chunk) * count, count)
            sp_ref[place, :] = held[span]
            u_ref[place, :] = source[span]
    copy.wait()

    for micro in range(micros):

        def advance(t, h, micro=micro):
            row = micro * count + t
            span = pl.ds(micro * chunks * count + t, chunks, stride=count)
            sp = sp_ref[span, :]
            u = u_ref[span, :]
            out = []
            y = None
            for n in range(states):
                decay = jnp.exp2(sp * decay_ref[pl.ds(n * chunks, chunks), :])
                now = decay * h[n] + u * scalar_ref[row, b_at(n, eighth)]
                out.append(now)
                term = now * scalar_ref[row, c_at(n, eighth)]
                y = term if y is None else y + term
            y_ref[span, :] = y
            return tuple(out)

        lax.fori_loop(0, count, advance, (jnp.zeros((chunks, LANES), F32),) * states, unroll=2)

    cotan = cotan_ref[...]
    for chunk in range(chunks):
        cols = slice(chunk * LANES, (chunk + 1) * LANES)
        places = [pl.ds((micro * chunks + chunk) * count, count) for micro in range(micros)]
        y = jnp.concatenate([y_ref[place, :] for place in places])
        y = y + skip_ref[pl.ds(2 * chunk + half, 1), :] * act_ref[:, cols].astype(F32)
        gate = gate_ref[:, cols]
        sig = sigmoid(gate)
        gated_ref[:, cols] = (y * (gate * sig)).astype(BF16)
        dgated = dot(cotan, wout_ref[chunk, 0], 1, 1)
        dy = dgated * (gate * sig)
        for micro in range(micros):
            dy_ref[places[micro], :] = dy[micro * count : (micro + 1) * count]
        dgate_ref[:, cols] = (dgated * y * (sig * (1.0 + gate * (1.0 - sig)))).astype(BF16)
    normed = normed_ref[...]
    edge = LANES // 2
    for j in range(chunks):
        relative = ((j & 1) << 2) | (((j >> 1) & 1) << 1) | (j >> 2)
        grad = dot(gated_ref[:, lanes(relative ^ cube)], cotan, 0, 0).astype(BF16)
        top, bottom = grad[:edge], grad[edge:]
        keep_ref[pl.ds(j * edge, edge), :] = jnp.where(core == 0, top, bottom)
        send_ref[pl.ds(j * edge, edge), :] = jnp.where(core == 0, bottom, top)
    share = jnp.zeros(share_ref.shape, F32)
    for j in range(chunks // 2):
        place = pl.ds(chunks * edge + j * LANES, LANES)
        pair = 2 * (j ^ face)
        for chunk, out_ref in ((pair + core, keep_ref), (pair + 1 - core, send_ref)):
            grad = dot(dgate_ref[:, lanes(chunk)], normed, 0, 0)
            share = share + eight_rows(grad * wgate_ref[0, chunk, 0].astype(F32))
            out_ref[place, :] = grad.astype(BF16)
    share_ref[...] = share
    width = cotan.shape[1]
    mixed_ref[...] = dot(gated_ref[...], wout_ref[...].reshape(chunks * LANES, width), 1, 0).astype(
        BF16
    )


def scan_forward(
    place,
    lengths,
    act_all,
    bc_own,
    bc_other,
    alog_own,
    alog_other,
    dtx,
    dt,
    bias,
    skip,
    act,
    gate,
    wout3,
    cotan,
    normed,
    w4,
):
    rows, own = act.shape
    chunks = own // LANES
    states = 2 * alog_own.shape[0]
    width = cotan.shape[1]
    micros, _, clusters = lengths.shape
    ranks = dtx.shape[0]
    outs = [
        ((rows, 2 * states), F32),
        ((rows, ranks), BF16),
        ((rows, 2 * ranks), BF16),
        ((states * chunks, LANES), F32),
        ((chunks * rows, LANES), F32),
        ((chunks * rows, LANES), F32),
        ((chunks * rows, LANES), F32),
        ((rows, width), BF16),
        ((rows, own), BF16),
        ((own, width), BF16),
        ((own, width), BF16),
        ((8, width), F32),
    ]
    operands = (
        act_all, bc_own, bc_other, alog_own, alog_other, dtx, dt, bias, skip, act, gate
    )
    return pl.pallas_call(
        functools.partial(
            forward_kernel,
            micros=micros,
            count=rows // micros,
            states=states,
            chunks=chunks,
            clusters=clusters,
        ),
        grid_spec=pltpu.PrefetchScalarGridSpec(
            num_scalar_prefetch=1,
            grid=(1,),
            in_specs=[pl.BlockSpec(memory_space=pltpu.SMEM)]
            + [whole(operand.shape) for operand in operands]
            + [
                pl.BlockSpec((chunks, 1, LANES, width), lambda i, p: (0, p[HALF], 0, 0)),
                whole((rows, width)),
                whole((rows, width)),
                pl.BlockSpec((1, chunks, 1, LANES, width), lambda i, p: (1, 0, p[HALF], 0, 0)),
            ],
            out_specs=[whole(shape) for shape, _ in outs],
            scratch_shapes=[
                pltpu.VMEM((2, rows, LANES), F32),
                pltpu.VMEM((chunks * rows, LANES), F32),
                pltpu.VMEM((rows, own), BF16),
                pltpu.VMEM((states * chunks, LANES), F32),
                pltpu.SMEM((rows, 2 * states), F32),
                pltpu.SemaphoreType.DMA,
            ],
        ),
        out_shape=[jax.ShapeDtypeStruct(*out) for out in outs],
        compiler_params=params(48),
        cost_estimate=cost(19),
        name="scan_forward",
    )(place, *in_hbm((lengths, *operands, wout3, cotan, normed, w4)))


def backward_kernel(
    place_ref,
    bc_ref,
    decay_ref,
    rank_ref,
    dt_ref,
    bias_ref,
    act_ref,
    sp_ref,
    u_ref,
    dy_ref,
    code_ref,
    sact_ref,
    dpre_ref,
    alog_ref,
    vec_ref,
    h_ref,
    s_ref,
    d_ref,
    terms_ref,
    sums_ref,
    scalar_ref,
    sem,
    *,
    count,
    states,
    chunks,
):
    copy = pltpu.make_async_copy(bc_ref, scalar_ref, sem)
    copy.start()
    half = place_ref[HALF]
    eighth = states // 2
    alog_ref[...] = jnp.zeros_like(alog_ref)
    zero = (jnp.zeros((chunks, LANES), F32),) * states
    for n in range(states):
        h_ref[pl.ds(n * chunks, chunks), :] = zero[0]
    copy.wait()

    def recompute(t, h):
        span = pl.ds(t, chunks, stride=count)
        sp = sp_ref[span, :]
        u = u_ref[span, :]
        out = []
        for n in range(states):
            decay = jnp.exp2(sp * decay_ref[pl.ds(n * chunks, chunks), :])
            now = decay * h[n] + u * scalar_ref[t, b_at(n, eighth)]
            h_ref[aligned(((t + 1) * states + n) * chunks, chunks), :] = now
            out.append(now)
        return tuple(out)

    lax.fori_loop(0, count, recompute, zero, unroll=2)

    def retreat(back, carry):
        t = count - 1 - back
        span = pl.ds(t, chunks, stride=count)
        sp = sp_ref[span, :]
        u = u_ref[span, :]
        dy = dy_ref[span, :]
        out = []
        d_sum = None
        s_sum = None
        for n in range(states):
            rate = decay_ref[pl.ds(n * chunks, chunks), :]
            decay = jnp.exp2(sp * rate)
            dh = carry[n] + dy * scalar_ref[t, c_at(n, eighth)]
            flow = decay * dh
            out.append(flow)
            before = h_ref[aligned((t * states + n) * chunks, chunks), :]
            now = h_ref[aligned(((t + 1) * states + n) * chunks, chunks), :]
            q = flow * before
            alog_ref[pl.ds(n * chunks, chunks), :] += q * sp
            d_term = q * rate
            s_term = dh * scalar_ref[t, b_at(n, eighth)]
            d_sum = d_term if d_sum is None else d_sum + d_term
            s_sum = s_term if s_sum is None else s_sum + s_term
            terms_ref[pl.ds(b_at(n, eighth) * chunks, chunks), :] = dh * u
            terms_ref[pl.ds(c_at(n, eighth) * chunks, chunks), :] = dy * now
        s_ref[span, :] = s_sum
        d_ref[span, :] = d_sum
        sums = None
        for chunk in range(chunks):
            term = terms_ref[pl.ds(chunk, 2 * states, stride=chunks), :]
            sums = term if sums is None else sums + term
        sums_ref[aligned(t * 2 * states, 2 * states), :] = sums
        return tuple(out)

    lax.fori_loop(0, count, retreat, zero, unroll=2)

    rank = rank_ref[...]
    ranks = rank.shape[1]
    drank = None
    for chunk in range(chunks):
        cols = slice(chunk * LANES, (chunk + 1) * LANES)
        place = pl.ds(chunk * count, count)
        act = act_ref[:, cols].astype(F32)
        weight = dt_ref[:, lanes(2 * chunk + half)]
        pre = dot(rank, weight, 1, 0) + bias_ref[pl.ds(2 * chunk + half, 1), :]
        s_now = s_ref[place, :]
        dstep = d_ref[place, :] * (1.0 / LOG2E) + s_now * act
        sact_ref[:, cols] = s_now * softplus(pre)
        dpre = dstep * sigmoid(pre)
        vec_ref[0:1, cols] = jnp.sum(dpre, axis=0, keepdims=True)
        vec_ref[1:2, cols] = jnp.sum(dy_ref[place, :] * act, axis=0, keepdims=True)
        low = dpre.astype(BF16)
        dpre_ref[:, cols] = low
        term = dot(low, weight, 1, 1)
        drank = term if drank is None else drank + term
    source = lax.broadcasted_iota(jnp.int32, (2 * LANES, LANES), 0) // LANES
    target = lax.broadcasted_iota(jnp.int32, (2 * LANES, LANES), 1)
    code = None
    for k in range(states):
        pair = jnp.concatenate(
            [sums_ref[pl.ds(2 * k + j, count, stride=2 * states), :] for j in range(2)], axis=1
        )
        pick = jnp.where(target == source + (ranks + 2 * k), 1.0, 0.0).astype(BF16)
        term = dot(pair.astype(BF16), pick, 1, 0)
        code = term if code is None else code + term
    code_ref[...] = code + jnp.concatenate([drank, jnp.zeros((count, LANES - ranks), F32)], axis=1)


def scan_backward(place, micro, count, bc, decay, rank, dt, bias, act, sp, u, dy):
    rows, own = act.shape
    chunks = own // LANES
    states = bc.shape[1] // 2
    ranks = rank.shape[1]
    outs = [
        ((count, LANES), F32),
        ((count, own), F32),
        ((count, own), BF16),
        ((states * chunks, LANES), F32),
        ((2, own), F32),
    ]

    def block(*shape):
        return pl.BlockSpec(shape, lambda i, p: (micro, 0))

    return pl.pallas_call(
        functools.partial(backward_kernel, count=count, states=states, chunks=chunks),
        grid_spec=pltpu.PrefetchScalarGridSpec(
            num_scalar_prefetch=1,
            grid=(1,),
            in_specs=[
                block(count, 2 * states),
                whole(decay.shape),
                block(count, ranks),
                whole(dt.shape),
                whole(bias.shape),
                block(count, own),
                block(chunks * count, LANES),
                block(chunks * count, LANES),
                block(chunks * count, LANES),
            ],
            out_specs=[whole(shape) for shape, _ in outs],
            scratch_shapes=[
                pltpu.VMEM(((count + 1) * states * chunks, LANES), F32),
                pltpu.VMEM((chunks * count, LANES), F32),
                pltpu.VMEM((chunks * count, LANES), F32),
                pltpu.VMEM((2 * states * chunks, LANES), F32),
                pltpu.VMEM((count * 2 * states, LANES), F32),
                pltpu.SMEM((count, 2 * states), F32),
                pltpu.SemaphoreType.DMA,
            ],
        ),
        out_shape=[jax.ShapeDtypeStruct(*out) for out in outs],
        compiler_params=params(26),
        cost_estimate=cost(14),
        name="scan_backward",
    )(place, *in_hbm((bc, decay, rank, dt, bias, act, sp, u, dy)))


def tail_kernel(
    place_ref,
    len_ref,
    *refs,
    micros,
    count,
    taps,
    clusters,
    ranks,
    chunks,
    states,
):
    def take(number):
        nonlocal refs
        taken, refs = refs[:number], refs[number:]
        return taken

    code_own, code_other, sact_refs, dpre_refs, alog_refs, back_refs = (
        take(micros) for _ in range(6)
    )
    dtx_ref, bc_own_ref, bc_other_ref, decay_ref = take(4)
    dy_refs = take(micros)
    conved_ref, inner_ref, act_ref, high_ref, convw_ref, skip_ref = take(6)
    normed_ref, win_ref, share_ref, gain_ref = take(4)
    keep_ref, send_ref, low_ref = take(3)
    mask_ref, code_ref, wcode_ref, vec_ref, alog_ref, total_ref = refs

    step = pl.program_id(0)
    rows = micros * count
    eighth = states // 2
    edge = LANES // 2
    half, core, cube, face = (place_ref[k] for k in range(4))
    pair = step ^ face
    span = 3 * edge // 2

    def pack_row(chunk):
        relative = chunk ^ cube
        zh, zl, x = relative >> 2, (relative >> 1) & 1, relative & 1
        return (2 * x + zl) * span + edge + zh * 16

    def place_pair(start, size, cols, even, odd):
        keep_ref[aligned(start, size, 16), cols] = jnp.where(core == 0, even, odd).astype(BF16)
        send_ref[aligned(start, size, 16), cols] = jnp.where(core == 0, odd, even).astype(BF16)

    @pl.when(step == 0)
    def _():
        fill_masks(len_ref, mask_ref, micros, count, taps, clusters)
        total_ref[...] = share_ref[...]
        for micro in range(micros):
            code_ref[pl.ds(micro * count, count), :] = (
                code_own[micro][...] + code_other[micro][...]
            ).astype(BF16)
        total = None
        for micro in range(micros):
            term = alog_refs[micro][...]
            total = term if total is None else total + term
        alog_ref[...] = total * (decay_ref[...] * (1.0 / LOG2E))

    code = code_ref[...]
    lane = lax.broadcasted_iota(jnp.int32, (1, LANES), 1)
    code_rank = jnp.where(lane < ranks, code, jnp.zeros_like(code))
    dpre = jnp.concatenate([ref[...] for ref in dpre_refs], axis=0)
    for part in range(2):
        source = lanes(2 * (2 * pair + part) + half)
        cols = slice(part * LANES, (part + 1) * LANES)
        wcode_ref[:ranks, cols] = dtx_ref[:, source]
        own = bc_own_ref[:, :, source].reshape(states, LANES)
        other = bc_other_ref[:, :, source].reshape(states, LANES)
        wcode_ref[ranks : ranks + states, cols] = jnp.where(half == 0, own, other)
        wcode_ref[ranks + states : ranks + 2 * states, cols] = jnp.where(half == 0, other, own)
        wcode_ref[ranks + 2 * states :, cols] = jnp.zeros(
            (LANES - ranks - 2 * states, LANES), BF16
        )
    for part in range(2):
        cols = slice(part * LANES, (part + 1) * LANES)
        chunk = 2 * pair + part
        source = 2 * chunk + half
        weights = convw_ref[:, lanes(source)]
        sact = jnp.concatenate([ref[:, cols] for ref in sact_refs], axis=0)
        dy = jnp.concatenate([ref[pl.ds(part * count, count), :] for ref in dy_refs], axis=0)
        dact = sact + dot(code, wcode_ref[:, cols], 1, 0)
        dact = dact + dy * skip_ref[pl.ds(source, 1), :]
        conved = conved_ref[:, cols]
        sig = sigmoid(conved)
        dconv = dact * (sig * (1.0 + conved * (1.0 - sig)))
        inner = inner_ref[:, cols]
        dinner = weights[taps - 1 : taps] * dconv
        sums = [None] * (taps + 1)
        sums[taps - 1] = jnp.sum(dconv * inner, axis=0, keepdims=True)
        sums[taps] = jnp.sum(dconv, axis=0, keepdims=True)
        for back in range(1, taps):
            kept = dconv * mask_ref[back]
            dinner = dinner + weights[taps - 1 - back : taps - back] * pltpu.roll(
                kept, rows - back, 0
            )
            sums[taps - 1 - back] = jnp.sum(
                kept * pltpu.roll(inner, back, 0), axis=0, keepdims=True
            )
        for k in range(taps + 1):
            vec_ref[k : k + 1, lanes(chunk)] = sums[k]
        for k in range(2):
            total = None
            for ref in back_refs:
                term = ref[k : k + 1, lanes(chunk)]
                total = term if total is None else total + term
            vec_ref[taps + 1 + k : taps + 2 + k, lanes(chunk)] = total
        low_ref[:, cols] = dinner.astype(BF16)

        act = act_ref[:, cols]
        start = pack_row(chunk)
        rows_now = dot(act, code_rank, 0, 0) + dot(dpre[:, cols], high_ref[...], 0, 0)
        for k in range(4):
            place_pair(
                start,
                16,
                slice(k * LANES, (k + 1) * LANES),
                rows_now[k * 16 : (k + 1) * 16],
                rows_now[edge + k * 16 : edge + (k + 1) * 16],
            )
        state_rows = dot(code, act, 0, 0)[ranks : ranks + 2 * states]
        place_pair(
            start, 16, slice(4 * LANES, 5 * LANES), state_rows[:states], state_rows[states:]
        )

    zl, x_bit = step >> 1, step & 1
    normed = normed_ref[...]
    for part in range(2):
        grad = dot(low_ref[:, lanes(core ^ part)], normed, 0, 0)
        total_ref[...] += eight_rows(grad * win_ref[0, core ^ part, 0].astype(F32))
        grad = grad.astype(BF16)
        out_ref = (keep_ref, send_ref)[part]
        out_ref[aligned((2 * x_bit + zl) * span, edge, 16), :] = grad[:edge]
        out_ref[aligned(4 * span + step * edge, edge, 16), :] = grad[edge:]

    @pl.when(step == pl.num_programs(0) - 1)
    def _():
        vec_ref[taps + 3 : taps + 4, :] = (
            jnp.sum(total_ref[...], axis=0, keepdims=True) / gain_ref[...]
        )
        for chunk in range(chunks):
            start = pack_row(chunk)
            vec = vec_ref[:, chunk * LANES : (chunk + 1) * LANES]
            alog = [
                alog_ref[pl.ds(q * eighth * chunks + chunk, eighth, stride=chunks), :]
                for q in range(2)
            ]
            place_pair(
                start,
                16,
                slice(5 * LANES, 6 * LANES),
                jnp.concatenate([alog[0], vec]),
                jnp.concatenate([alog[1], pltpu.roll(vec, edge, 1)]),
            )
            blank = jnp.zeros((16, 2 * LANES), F32)
            place_pair(start, 16, slice(6 * LANES, 8 * LANES), blank, blank)


def tail(
    place,
    lengths,
    code_own,
    code_other,
    sact,
    dpre,
    alog,
    back,
    dtx,
    bc_own,
    bc_other,
    decay,
    dy,
    conved,
    inner,
    act,
    high,
    convw,
    skip,
    normed,
    w4,
    share,
    gain,
):
    rows, own = act.shape
    chunks = own // LANES
    width = normed.shape[1]
    micros, _, clusters = lengths.shape
    count = rows // micros
    taps = convw.shape[0]
    ranks = dtx.shape[0]
    states = decay.shape[0] // chunks
    cols = 2 * LANES
    extent = chunks * LANES // 2 + 2 * chunks * 8

    def by_cols(height):
        return pl.BlockSpec((height, cols), lambda i, p: (0, i ^ p[FACE]))

    def dy_spec(micro):
        return pl.BlockSpec(
            (2 * count, LANES), lambda i, p: (micro * (chunks // 2) + (i ^ p[FACE]), 0)
        )

    in_specs = (
        [pl.BlockSpec(memory_space=pltpu.SMEM)]
        + [whole((count, LANES))] * (2 * micros)
        + [by_cols(count)] * (2 * micros)
        + [whole(alog[0].shape)] * micros
        + [whole(back[0].shape)] * micros
        + [whole(array.shape) for array in (dtx, bc_own, bc_other, decay)]
        + [dy_spec(micro) for micro in range(micros)]
        + [by_cols(rows)] * 3
        + [whole(array.shape) for array in (high, convw, skip, normed)]
        + [
            pl.BlockSpec(
                (1, 2, 1, LANES, width), lambda i, p: (0, i ^ p[FACE], p[HALF], 0, 0)
            ),
            whole(share.shape),
            whole(gain.shape),
        ]
    )
    return pl.pallas_call(
        functools.partial(
            tail_kernel,
            micros=micros,
            count=count,
            taps=taps,
            clusters=clusters,
            ranks=ranks,
            chunks=chunks,
            states=states,
        ),
        grid_spec=pltpu.PrefetchScalarGridSpec(
            num_scalar_prefetch=1,
            grid=(chunks // 2,),
            in_specs=in_specs,
            out_specs=[whole((extent, width)), whole((extent, width)), by_cols(rows)],
            scratch_shapes=[
                pltpu.VMEM((taps, rows, LANES), F32),
                pltpu.VMEM((rows, LANES), BF16),
                pltpu.VMEM((LANES, cols), BF16),
                pltpu.VMEM((8, own), F32),
                pltpu.VMEM((states * chunks, LANES), F32),
                pltpu.VMEM((8, width), F32),
            ],
        ),
        out_shape=[
            jax.ShapeDtypeStruct((extent, width), BF16),
            jax.ShapeDtypeStruct((extent, width), BF16),
            jax.ShapeDtypeStruct((rows, own), BF16),
        ],
        compiler_params=params(24),
        cost_estimate=cost(7),
        name="tail",
    )(
        place,
        *in_hbm(
            (
                lengths,
                *code_own,
                *code_other,
                *sact,
                *dpre,
                *alog,
                *back,
                dtx,
                bc_own,
                bc_other,
                decay,
                *([dy] * micros),
                conved,
                inner,
                act,
                high,
                convw,
                skip,
                normed,
                w4,
                share,
                gain,
            )
        ),
    )


def spread_kernel(
    place_ref, low_ref, dgate_ref, win_ref, wgate_ref, dnormed_ref, total_ref
):
    step = pl.program_id(0)
    width = total_ref.shape[1]

    @pl.when(step == 0)
    def _():
        total_ref[...] = jnp.zeros_like(total_ref)

    total_ref[...] += dot(low_ref[...], win_ref[...].reshape(-1, width), 1, 0) + dot(
        dgate_ref[...], wgate_ref[...].reshape(-1, width), 1, 0
    )

    @pl.when(step == pl.num_programs(0) - 1)
    def _():
        dnormed_ref[...] = total_ref[...].astype(BF16)


def spread(place, low, dgate, w4):
    rows, own = low.shape
    width = w4.shape[-1]
    pairs = own // (2 * LANES)
    by_cols = pl.BlockSpec((rows, 2 * LANES), lambda i, p: (0, i))

    def weight_spec(which):
        return pl.BlockSpec((1, 2, 1, LANES, width), lambda i, p: (which, i, p[HALF], 0, 0))

    return pl.pallas_call(
        spread_kernel,
        grid_spec=pltpu.PrefetchScalarGridSpec(
            num_scalar_prefetch=1,
            grid=(pairs,),
            in_specs=[by_cols, by_cols, weight_spec(0), weight_spec(1)],
            out_specs=whole((rows, width)),
            scratch_shapes=[pltpu.VMEM((rows, width), F32)],
        ),
        out_shape=jax.ShapeDtypeStruct((rows, width), BF16),
        compiler_params=params(16),
        cost_estimate=cost(0),
        name="spread",
    )(place, *in_hbm((low, dgate, w4, w4)))


def add_kernel(*refs, pieces, pairs):
    outs = refs[2 * pairs :]
    for pair, start, size, out, at in pieces:
        left, right = refs[2 * pair], refs[2 * pair + 1]
        outs[out][pl.ds(at, size), :] = left[pl.ds(start, size), :] + right[pl.ds(start, size), :]


def add(arrays, heights, pieces):
    width = arrays[0].shape[1]
    vmem = pl.BlockSpec(memory_space=pltpu.VMEM)
    return pl.pallas_call(
        functools.partial(add_kernel, pieces=pieces, pairs=len(arrays) // 2),
        in_specs=[vmem] * len(arrays),
        out_specs=[vmem] * len(heights),
        out_shape=[jax.ShapeDtypeStruct((height, width), BF16) for height in heights],
        cost_estimate=cost(0),
        name="add",
    )(*arrays)


def finish_kernel(
    x_ref, mine_ref, theirs_ref, dn_mine_ref, dn_theirs_ref, cotan_ref, gain_ref, mixed_ref, grad_ref
):
    x = x_ref[...].astype(F32)
    mixed_ref[...] = (
        x + (mine_ref[...].astype(F32) + theirs_ref[...].astype(F32))
    ).astype(BF16)
    scale = lax.rsqrt(jnp.mean(x * x, axis=1, keepdims=True) + EPSILON)
    unit = x * scale
    dhat = (dn_mine_ref[...].astype(F32) + dn_theirs_ref[...].astype(F32)) * gain_ref[...]
    grad_ref[...] = cotan_ref[...].astype(F32) + scale * (
        dhat - unit * jnp.mean(dhat * unit, axis=1, keepdims=True)
    )


def finish(x, mixed_mine, mixed_theirs, dn_mine, dn_theirs, cotan, gain):
    rows, width = x.shape
    block = rows // 4
    by_rows = pl.BlockSpec((block, width), lambda i: (i, 0))
    return pl.pallas_call(
        finish_kernel,
        grid=(4,),
        in_specs=[by_rows] * 6 + [whole(gain.shape)],
        out_specs=[by_rows] * 2,
        out_shape=[
            jax.ShapeDtypeStruct((rows, width), BF16),
            jax.ShapeDtypeStruct((rows, width), F32),
        ],
        compiler_params=params(16),
        cost_estimate=cost(0),
        name="finish",
    )(*in_hbm((x, mixed_mine, mixed_theirs, dn_mine, dn_theirs, cotan, gain)))


def pack_kernel(mine_ref, theirs_ref, pack_ref, gain_ref):
    pack_ref[...] = mine_ref[...] + theirs_ref[...]
    gain_ref[...] = pack_ref[:, 5 * LANES : 6 * LANES]


def sum_pack(mine, theirs):
    vmem = pl.BlockSpec(memory_space=pltpu.VMEM)
    return pl.pallas_call(
        pack_kernel,
        in_specs=[vmem] * 2,
        out_specs=[vmem] * 2,
        out_shape=[
            jax.ShapeDtypeStruct(mine.shape, BF16),
            jax.ShapeDtypeStruct((mine.shape[0], LANES), BF16),
        ],
        cost_estimate=cost(0),
        name="sum_pack",
    )(mine, theirs)


def unpack_kernel(
    place_ref,
    pack_ref,
    mine_ref,
    theirs_ref,
    out_ref,
    dtx_ref,
    dt_ref,
    bc_ref,
    alog_ref,
    convw_ref,
    convb_ref,
    bias_ref,
    skip_ref,
    gain_ref,
    out_grad_ref,
    *,
    eighth,
    taps,
    edge,
):
    pack = pack_ref[...].astype(F32)
    for k in range(4):
        rows = pack[:, k * LANES : (k + 1) * LANES]
        dtx_ref[pl.ds(16 * k, 16), :] = rows[:, :edge]
        dt_ref[pl.ds(16 * k, 16), :] = pltpu.roll(rows, edge, 1)[:, :edge]
    rows = pack[:, 4 * LANES : 5 * LANES]
    bc_ref[0] = rows[:eighth]
    bc_ref[1] = rows[eighth:]
    rows = pack[:, 5 * LANES : 6 * LANES]
    alog_ref[...] = rows[:eighth]
    vec = rows[eighth:, :edge]
    convw_ref[...] = vec[:taps]
    convb_ref[...] = vec[taps : taps + 1]
    bias_ref[...] = vec[taps + 1 : taps + 2]
    skip_ref[...] = vec[taps + 2 : taps + 3]
    gain = mine_ref[...].astype(F32) + theirs_ref[...].astype(F32)
    gain = jnp.where(place_ref[HALF] == 0, gain, pltpu.roll(gain, LANES - edge // 2, 1))
    gain_ref[...] = gain[15:16, : edge // 2]
    out_grad_ref[...] = out_ref[...].astype(F32)


def unpack(place, pack, gain_mine, gain_theirs, out, eighth, taps, ranks):
    edge = LANES // 2
    shapes = [
        (edge, ranks),
        (edge, ranks),
        (2, eighth, LANES),
        (eighth, LANES),
        (taps, edge),
        (1, edge),
        (1, edge),
        (1, edge),
        (1, edge // 2),
        out.shape,
    ]
    return pl.pallas_call(
        functools.partial(unpack_kernel, eighth=eighth, taps=taps, edge=edge),
        grid_spec=pltpu.PrefetchScalarGridSpec(
            num_scalar_prefetch=1,
            grid=(1,),
            in_specs=[whole(array.shape) for array in (pack, gain_mine, gain_theirs, out)],
            out_specs=[whole(shape) for shape in shapes],
        ),
        out_shape=[jax.ShapeDtypeStruct(shape, F32) for shape in shapes],
        cost_estimate=cost(0),
        name="unpack",
    )(place, pack, gain_mine, gain_theirs, out)


def choose_kernel(upper_ref, gate_ref, gate_got_ref, inner_ref, inner_got_ref, out_ref):
    @pl.when(upper_ref[0] == 1)
    def _():
        out_ref[...] = gate_ref[...].astype(F32) + gate_got_ref[...].astype(F32)

    @pl.when(upper_ref[0] == 0)
    def _():
        out_ref[...] = inner_ref[...].astype(F32) + inner_got_ref[...].astype(F32)


def choose(upper, gate, gate_got, inner, inner_got):
    vmem = pl.BlockSpec(memory_space=pltpu.VMEM)
    return pl.pallas_call(
        choose_kernel,
        in_specs=[pl.BlockSpec(memory_space=pltpu.SMEM)] + [vmem] * 4,
        out_specs=vmem,
        out_shape=jax.ShapeDtypeStruct(gate.shape, F32),
        cost_estimate=cost(0),
        name="choose",
    )(upper, gate, gate_got, inner, inner_got)


def swap_pair(array):
    count = lax.axis_size("state")
    return lax.ppermute(array, "state", [(pos, pos ^ 1) for pos in range(count)])


def swap_bit(array, bit, source=None):
    pairs = [
        (pos, pos ^ bit)
        for pos in range(lax.axis_size("dp"))
        if source is None or bool(pos & bit) == source
    ]
    return lax.ppermute(array, "dp", pairs)


def swap_odd(array):
    parts, states = lax.axis_size("dp"), lax.axis_size("state")
    pairs = []
    for d in range(parts):
        for s in range(states):
            at = d * states + s
            to = at if d % 2 == s % 2 else (d ^ 1) * states + (s ^ 1)
            pairs.append((at, to))
    return lax.ppermute(array, ("dp", "state"), pairs)


CORE_BIT, X_BIT, ZL_BIT, ZH_BIT = 1, 2, 4, 8


def shards(
    tokens,
    cluster_len,
    norm_gain,
    in_weight,
    conv_weight,
    conv_bias,
    dtx_weight,
    dt_weight,
    dt_bias,
    bc_weight,
    a_log,
    skip_gain,
    out_weight,
    cotangent,
):
    micros, count, width = tokens.shape
    inner = out_weight.shape[0]
    taps = conv_weight.shape[0]
    ranks = dtx_weight.shape[1]
    chunks = inner // (2 * LANES)
    own = chunks * LANES
    rows = micros * count
    edge = LANES // 2
    span = 3 * edge // 2
    dp_parts = lax.axis_size("dp")
    state_count = lax.axis_size("state")
    dp_pos = lax.axis_index("dp")
    state_pos = lax.axis_index("state")
    half = state_pos & 1
    fast = state_count == 2 and dp_parts == 2 * chunks == 16
    if fast:
        place = jnp.stack([half, dp_pos & 1, dp_pos >> 1, (dp_pos >> 1) & 3])
        bc_own, alog_own = bc_weight, a_log
        bc_other, alog_other = swap_pair(bc_weight), swap_pair(a_log)
    else:
        place = jnp.stack([half, 0, 0, 0])
        bc_all = lax.all_gather(bc_weight, "state", axis=1, tiled=True)
        alog_all = lax.all_gather(a_log, "state", axis=0, tiled=True)
        eighth = alog_all.shape[0] // 2
        bc_own, bc_other = (
            lax.dynamic_slice_in_dim(bc_all, which * eighth, eighth, 1)
            for which in (half, 1 - half)
        )
        alog_own, alog_other = (
            lax.dynamic_slice_in_dim(alog_all, which * eighth, eighth, 0)
            for which in (half, 1 - half)
        )
    place = place.astype(jnp.int32)
    eighth = alog_own.shape[0]
    states = 2 * eighth

    x = tokens.reshape(rows, width)
    cotan = cotangent.reshape(rows, width)
    w4 = in_weight.reshape(2, chunks, 2, LANES, width)
    wout3 = out_weight.reshape(chunks, 2, LANES, width)
    dtx, dt = dtx_weight.T, dt_weight.T
    bias = dt_bias.reshape(-1, LANES)
    skip = skip_gain.reshape(-1, LANES)

    normed, act_all, act, inner_own, conved, gate = project(
        place, cluster_len, x, norm_gain[None], w4, conv_weight, conv_bias.reshape(-1, LANES)
    )
    bc, rank, high, decay, sp, u, dy, mixed_part, dgate, keep, send, share = scan_forward(
        place,
        cluster_len,
        act_all,
        bc_own,
        bc_other,
        alog_own,
        alog_other,
        dtx,
        dt,
        bias,
        skip,
        act,
        gate,
        wout3,
        cotan,
        normed,
        w4,
    )
    early = None
    if fast:
        early = swap_bit(send, CORE_BIT)
    mixed_other = swap_pair(mixed_part)

    results = []
    for micro in range(micros):
        if fast and micro == micros - 1:
            quarter = own // 4
            out_keep, out_send, gate_keep, gate_send = add(
                (keep, early),
                [quarter] * 4,
                [(0, k * quarter, quarter, k, 0) for k in range(4)],
            )
            out_send, gate_send, mixed_other, sp = lax.optimization_barrier(
                (out_send, gate_send, mixed_other, sp)
            )
            out_got = swap_bit(out_send, X_BIT)
            gate_got = swap_bit(gate_send, ZL_BIT)
        results.append(
            scan_backward(place, micro, count, bc, decay, rank, dt, bias, act, sp, u, dy)
        )
    code_own, sact, dpre, alog, back = zip(*results)
    code_other = [swap_pair(code) for code in code_own]
    if fast:
        out_keep, out_send, gate_keep, gate_send = add(
            (out_keep, out_got, gate_keep, gate_got),
            [LANES] * 4,
            [(k // 2, k % 2 * LANES, LANES, k, 0) for k in range(4)],
        )
        out_send, gate_send, conved = lax.optimization_barrier((out_send, gate_send, conved))
        out_got = swap_bit(out_send, ZL_BIT)
        gate_got = swap_bit(gate_send, X_BIT)
    late_keep, late_send, low = tail(
        place,
        cluster_len,
        code_own,
        code_other,
        sact,
        dpre,
        alog,
        back,
        dtx,
        bc_own,
        bc_other,
        decay,
        dy,
        conved,
        inner_own,
        act,
        high,
        conv_weight,
        skip,
        normed,
        w4,
        share,
        norm_gain[None],
    )
    if fast:
        late = swap_bit(late_send, CORE_BIT)
        out_keep, out_send, gate_sum = add(
            (out_keep, out_got, gate_keep, gate_got),
            (edge, edge, LANES),
            ((0, 0, edge, 0, 0), (0, edge, edge, 1, 0), (1, 0, LANES, 2, 0)),
        )
        out_send, gate_sum, low = lax.optimization_barrier((out_send, gate_sum, low))
        out_got = swap_bit(out_send, ZH_BIT)
        gate_got = swap_bit(gate_sum, ZH_BIT, False)
    dnormed_part = spread(place, low, dgate, w4)
    dnormed_other = swap_pair(dnormed_part)
    if fast:
        cut = 4 * span
        a_keep, a_send, b_keep, b_send = add(
            (late_keep, late),
            (2 * span, 2 * span, LANES, LANES),
            (
                (0, 0, 2 * span, 0, 0),
                (0, 2 * span, 2 * span, 1, 0),
                (0, cut, LANES, 2, 0),
                (0, cut + LANES, LANES, 3, 0),
            ),
        )
        a_got = swap_bit(a_send, X_BIT)
        b_got = swap_bit(b_send, ZL_BIT)
        a_keep, a_send, b_keep, b_send = add(
            (a_keep, a_got, b_keep, b_got),
            (span, span, edge, edge),
            (
                (0, 0, span, 0, 0),
                (0, span, span, 1, 0),
                (1, 0, edge, 2, 0),
                (1, edge, edge, 3, 0),
            ),
        )
        a_got = swap_bit(a_send, ZL_BIT)
        b_got = swap_bit(b_send, X_BIT)
        inner_sum, pack_keep, pack_send = add(
            (a_keep, a_got, b_keep, b_got),
            (LANES, 16, 16),
            (
                (0, 0, edge, 0, 0),
                (1, 0, edge, 0, edge),
                (0, edge, 16, 1, 0),
                (0, edge + 16, 16, 2, 0),
            ),
        )
        pack_got = swap_bit(pack_send, ZH_BIT)
        inner_got = swap_bit(inner_sum, ZH_BIT, True)
        out_own = swap_odd(out_keep + out_got)
        upper = (dp_pos // (dp_parts // 2)).reshape(1).astype(jnp.int32)
        pack, gain_mine = sum_pack(pack_keep, pack_got)
        gain_theirs = swap_pair(gain_mine)
        pack = swap_odd(pack)
        (
            dtx_grad,
            dt_grad,
            bc_grad,
            alog_grad,
            convw_grad,
            convb_grad,
            bias_grad,
            skip_grad,
            gain_grad,
            out_own,
        ) = unpack(place, pack, gain_mine, gain_theirs, out_own, eighth, taps, ranks)
        convb_grad, bias_grad, skip_grad, gain_grad = (
            array[0] for array in (convb_grad, bias_grad, skip_grad, gain_grad)
        )
        _, dnormed_other = lax.optimization_barrier((pack_got, dnormed_other))
        in_grad = choose(upper, gate_sum, gate_got, inner_sum, inner_got)
    mixed, tokens_grad = finish(
        x, mixed_part, mixed_other, dnormed_part, dnormed_other, cotan, norm_gain[None]
    )
    mixed = mixed.reshape(micros, count, width)
    tokens_grad = tokens_grad.reshape(micros, count, width)

    if not fast:
        def total(array):
            return lax.psum(array.astype(F32), "dp")

        def both_rows(array):
            mine = array.reshape(chunks, 1, LANES, -1)
            other = swap_pair(mine)
            low = jnp.where(half == 0, mine, other)
            high = jnp.where(half == 0, other, mine)
            return jnp.concatenate([low, high], axis=1).reshape(2 * own, -1)

        every = dp_parts * state_count
        at = dp_pos * state_count + state_pos

        def cut_own(array):
            extent = array.shape[0] // every
            return lax.dynamic_slice_in_dim(array, at * extent, extent, 0)

        pair = total(jnp.stack([keep, send]))
        outs = pair[:, : chunks * edge].reshape(2, 2, 2, 2, edge, width)
        outs = jnp.transpose(outs, (3, 2, 1, 0, 4, 5)).reshape(own, width)
        gates = pair[:, chunks * edge :].reshape(2, chunks // 2, LANES, width)
        gates = jnp.moveaxis(gates, 0, 1).reshape(own, width)
        pair = total(jnp.stack([late_keep, late_send]))
        a_part = pair[:, : 4 * span].reshape(2, 2, 2, span, width)
        b_part = pair[:, 4 * span :].reshape(2, 2, 2, edge, width)
        inners = jnp.concatenate(
            [jnp.transpose(a_part[:, :, :, :edge], (2, 1, 0, 3, 4)), jnp.moveaxis(b_part, 0, 2)],
            axis=3,
        ).reshape(own, width)
        packs = a_part[:, :, :, edge:].reshape(2, 2, 2, 2, 16, width // LANES, LANES)
        packs = jnp.transpose(packs, (3, 2, 1, 0, 5, 4, 6)).reshape(chunks, 2, -1, 16, LANES)
        small = both_rows(packs[:, :, :4].reshape(own, LANES))
        in_grad = cut_own(jnp.concatenate([both_rows(inners), both_rows(gates)]))
        out_own = cut_own(both_rows(outs))
        mine = cut_own(small)
        dtx_grad, dt_grad = mine[:, :ranks], mine[:, ranks:]
        vec_rows = jnp.swapaxes(packs[:, :, 5, eighth:, :edge], 2, 3).reshape(own, -1)
        gain_sum = vec_rows[:, -1]
        gain_grad = cut_own(gain_sum + swap_pair(gain_sum))
        vec = cut_own(both_rows(vec_rows)).T
        state_rows = jnp.concatenate([packs[:, :, 4], packs[:, :, 5, :eighth]], axis=2)
        state_rows = state_rows.reshape(chunks, 2, 3, eighth, LANES)
        state_rows = jnp.transpose(state_rows, (0, 4, 2, 1, 3)).reshape(own, -1)
        extent = inner // dp_parts
        state_part = lax.dynamic_slice_in_dim(both_rows(state_rows), dp_pos * extent, extent, 0)
        state_part = state_part.T.reshape(3, state_count, -1, extent)
        state_part = lax.dynamic_index_in_dim(state_part, state_pos, 1, keepdims=False)
        bc_grad, alog_grad = state_part[:2], state_part[2]
        convw_grad, convb_grad, bias_grad, skip_grad = (
            vec[:taps], vec[taps], vec[taps + 1], vec[taps + 2]
        )

    return (
        mixed,
        tokens_grad,
        gain_grad,
        in_grad,
        convw_grad,
        convb_grad,
        dtx_grad,
        dt_grad,
        bias_grad,
        bc_grad,
        alog_grad,
        skip_grad,
        out_own,
    )


def solution(mesh):
    return jax.shard_map(
        shards,
        mesh=mesh,
        in_specs=(
            P(None, "dp", None),
            P(None, "dp", None),
            P(),
            P(),
            P(),
            P(),
            P(),
            P(),
            P(),
            P(None, "state", None),
            P("state", None),
            P(),
            P(),
            P(None, "dp", None),
        ),
        out_specs=(
            P(None, "dp", None),
            P(None, "dp", None),
            P(("dp", "state")),
            P(("dp", "state"), None),
            P(None, ("dp", "state")),
            P(("dp", "state")),
            P(("dp", "state"), None),
            P(("dp", "state"), None),
            P(("dp", "state")),
            P(None, "state", "dp"),
            P("state", "dp"),
            P(("dp", "state")),
            P(("dp", "state"), None),
        ),
        check_vma=False,
    )
```

```python
import functools
import math

import jax
import jax.numpy as jnp
from jax import lax
from jax.experimental import pallas as pl
from jax.experimental.pallas import tpu as pltpu
from jax.sharding import PartitionSpec as P

EPSILON = 1e-05
LANES = 128
RESET = 1e4
LOG2E = math.log2(math.e)
F32 = jnp.float32
BF16 = jnp.bfloat16
MIB = 1024 * 1024


def dot(left, right, left_dim, right_dim):
    return lax.dot_general(
        left, right, (((left_dim,), (right_dim,)), ((), ())), preferred_element_type=F32
    )


def params(mib):
    return pltpu.CompilerParams(
        vmem_limit_bytes=mib * MIB, dimension_semantics=("arbitrary",)
    )


def whole(shape):
    return pl.BlockSpec(shape, lambda *_: (0,) * len(shape))


sigmoid = jax.nn.sigmoid


def softplus(value):
    return jnp.maximum(value, 0.0) + jnp.log1p(jnp.exp(-jnp.abs(value)))


def lanes(index):
    return pl.ds(pl.multiple_of(index * LANES, LANES), LANES)


def cost(micros):
    return pl.CostEstimate(
        flops=int(micros * 1e9), bytes_accessed=int(micros * 1e6), transcendentals=0
    )


def hbm(shape, dtype):
    return pltpu.HBM(shape, dtype)


def in_hbm(arrays):
    return [pltpu.with_memory_space_constraint(array, pltpu.HBM) for array in arrays]


def aligned(start, size, to=8):
    return pl.ds(pl.multiple_of(start, to), size)


HALF, CORE, CUBE, FACE = range(4)


def fill_masks(len_ref, mask_ref, micros, count, taps, clusters):
    place = lax.broadcasted_iota(jnp.int32, (count, LANES), 0)
    for micro in range(micros):
        rows = pl.ds(micro * count, count)
        for back in range(1, taps):
            apart = place < back
            start = 0
            for cluster in range(clusters - 1):
                start = start + len_ref[micro, 0, cluster]
                apart = apart | ((place >= start) & (place < start + back))
            mask_ref[back, rows, :] = jnp.where(apart, 0.0, 1.0)
            if back == 1:
                mask_ref[0, rows, :] = jnp.where(apart, 1.0, 0.0)


def project_kernel(
    place_ref,
    len_ref,
    x_ref,
    gain_ref,
    win_ref,
    wgate_ref,
    convw_ref,
    convb_ref,
    normed_ref,
    act_ref,
    own_act_ref,
    inner_ref,
    conved_ref,
    gate_ref,
    mask_ref,
    proj_ref,
    conv_ref,
    *,
    micros,
    count,
    taps,
    clusters,
):
    chunk = pl.program_id(0)

    @pl.when(chunk == 0)
    def _():
        fill_masks(len_ref, mask_ref, micros, count, taps, clusters)
        rows = x_ref[...].astype(F32)
        scale = lax.rsqrt(jnp.mean(rows * rows, axis=1, keepdims=True) + EPSILON)
        normed_ref[...] = (rows * scale * gain_ref[...]).astype(BF16)

    half = place_ref[HALF]
    normed = normed_ref[...]
    proj_ref[...] = dot(normed, win_ref[...].reshape(2 * LANES, -1), 1, 1)
    gate_ref[...] = dot(normed, wgate_ref[...].reshape(LANES, -1), 1, 1)
    for part in range(2):
        cols = pl.ds(part * LANES, LANES)
        inner = proj_ref[:, cols]
        conved = convb_ref[pl.ds(2 * chunk + part, 1), :] + convw_ref[taps - 1 : taps, cols] * inner
        for back in range(1, taps):
            shifted = pltpu.roll(inner, back, 0) * mask_ref[back]
            conved = conved + convw_ref[taps - 1 - back : taps - back, cols] * shifted
        conv_ref[:, cols] = conved
        act_ref[:, cols] = (conved * sigmoid(conved)).astype(BF16)
    own = lanes(half)
    inner_ref[...] = proj_ref[:, own]
    conved_ref[...] = conv_ref[:, own]
    own_act_ref[...] = act_ref[:, own]


def project(place, lengths, x, gain, w4, conv_weight, conv_bias):
    rows, width = x.shape
    chunks = w4.shape[1]
    inner = chunks * 2 * LANES
    micros, _, clusters = lengths.shape
    taps = conv_weight.shape[0]
    own = chunks * LANES
    by_chunk = pl.BlockSpec((rows, LANES), lambda i, p: (0, i))
    return pl.pallas_call(
        functools.partial(
            project_kernel, micros=micros, count=rows // micros, taps=taps, clusters=clusters
        ),
        grid_spec=pltpu.PrefetchScalarGridSpec(
            num_scalar_prefetch=1,
            grid=(chunks,),
            in_specs=[
                pl.BlockSpec(memory_space=pltpu.SMEM),
                whole((rows, width)),
                whole((1, width)),
                pl.BlockSpec((1, 1, 2, LANES, width), lambda i, p: (0, i, 0, 0, 0)),
                pl.BlockSpec((1, 1, 1, LANES, width), lambda i, p: (1, i, p[HALF], 0, 0)),
                pl.BlockSpec((taps, 2 * LANES), lambda i, p: (0, i)),
                whole(conv_bias.shape),
            ],
            out_specs=[
                whole((rows, width)),
                pl.BlockSpec((rows, 2 * LANES), lambda i, p: (0, i)),
                by_chunk,
                by_chunk,
                by_chunk,
                by_chunk,
            ],
            scratch_shapes=[
                pltpu.VMEM((taps, rows, LANES), F32),
                pltpu.VMEM((rows, 2 * LANES), F32),
                pltpu.VMEM((rows, 2 * LANES), F32),
            ],
        ),
        out_shape=[
            hbm((rows, width), BF16),
            hbm((rows, inner), BF16),
            hbm((rows, own), BF16),
            hbm((rows, own), F32),
            hbm((rows, own), F32),
            hbm((rows, own), F32),
        ],
        compiler_params=params(16),
        cost_estimate=cost(6),
        name="project",
    )(place, *in_hbm((lengths, x, gain, w4, w4, conv_weight, conv_bias)))


def eight_rows(array):
    return jnp.sum(array.reshape(-1, 8, array.shape[1]), axis=0)


def b_at(n, eighth):
    return (n // eighth) * 2 * eighth + n % eighth


def c_at(n, eighth):
    return b_at(n, eighth) + eighth


def forward_kernel(
    place_ref,
    len_ref,
    act_all_ref,
    bc_own_ref,
    bc_other_ref,
    alog_own_ref,
    alog_other_ref,
    dtx_ref,
    dt_ref,
    bias_ref,
    skip_ref,
    act_ref,
    gate_ref,
    wout_ref,
    cotan_ref,
    normed_ref,
    wgate_ref,
    bc_ref,
    rank_ref,
    rank_high_ref,
    decay_ref,
    sp_ref,
    u_ref,
    dy_ref,
    mixed_ref,
    dgate_ref,
    keep_ref,
    send_ref,
    share_ref,
    mask_ref,
    y_ref,
    gated_ref,
    tmp_ref,
    scalar_ref,
    sem,
    *,
    micros,
    count,
    states,
    chunks,
    clusters,
):
    rows = micros * count
    eighth = states // 2
    half, core, cube, face = (place_ref[k] for k in range(4))
    first = half == 0
    act_all = act_all_ref[...]
    own = dot(act_all, bc_own_ref[...].reshape(states, -1), 1, 1)
    other = dot(act_all, bc_other_ref[...].reshape(states, -1), 1, 1)
    bc_ref[:, :states] = jnp.where(first, own, other)
    bc_ref[:, states:] = jnp.where(first, other, own)
    copy = pltpu.make_async_copy(bc_ref, scalar_ref, sem)
    copy.start()

    fill_masks(len_ref, mask_ref, micros, count, 2, clusters)
    for chunk in range(chunks):
        cols = lanes(2 * chunk + half)
        own, other = alog_own_ref[:, cols], alog_other_ref[:, cols]
        tmp_ref[pl.ds(chunk * states, eighth), :] = jnp.where(first, own, other)
        tmp_ref[pl.ds(chunk * states + eighth, eighth), :] = jnp.where(first, other, own)
    for n in range(states):
        decay_ref[pl.ds(n * chunks, chunks), :] = -LOG2E * jnp.exp(
            tmp_ref[pl.ds(n, chunks, stride=states), :]
        )

    rank = dot(act_all, dtx_ref[...], 1, 1).astype(BF16)
    rank_ref[...] = rank
    rank_high_ref[...] = jnp.concatenate([jnp.zeros_like(rank), rank], axis=1)
    for chunk in range(chunks):
        cols = slice(chunk * LANES, (chunk + 1) * LANES)
        bias = bias_ref[pl.ds(2 * chunk + half, 1), :]
        step = softplus(dot(rank, dt_ref[:, lanes(2 * chunk + half)], 1, 0) + bias)
        held = step + RESET * mask_ref[0]
        source = step * act_ref[:, cols].astype(F32)
        for micro in range(micros):
            span = slice(micro * count, (micro + 1) * count)
            place = pl.ds((micro * chunks + chunk) * count, count)
            sp_ref[place, :] = held[span]
            u_ref[place, :] = source[span]
    copy.wait()

    for micro in range(micros):

        def advance(t, h, micro=micro):
            row = micro * count + t
            span = pl.ds(micro * chunks * count + t, chunks, stride=count)
            sp = sp_ref[span, :]
            u = u_ref[span, :]
            out = []
            y = None
            for n in range(states):
                decay = jnp.exp2(sp * decay_ref[pl.ds(n * chunks, chunks), :])
                now = decay * h[n] + u * scalar_ref[row, b_at(n, eighth)]
                out.append(now)
                term = now * scalar_ref[row, c_at(n, eighth)]
                y = term if y is None else y + term
            y_ref[span, :] = y
            return tuple(out)

        lax.fori_loop(0, count, advance, (jnp.zeros((chunks, LANES), F32),) * states, unroll=2)

    cotan = cotan_ref[...]
    for chunk in range(chunks):
        cols = slice(chunk * LANES, (chunk + 1) * LANES)
        places = [pl.ds((micro * chunks + chunk) * count, count) for micro in range(micros)]
        y = jnp.concatenate([y_ref[place, :] for place in places])
        y = y + skip_ref[pl.ds(2 * chunk + half, 1), :] * act_ref[:, cols].astype(F32)
        gate = gate_ref[:, cols]
        sig = sigmoid(gate)
        gated_ref[:, cols] = (y * (gate * sig)).astype(BF16)
        dgated = dot(cotan, wout_ref[chunk, 0], 1, 1)
        dy = dgated * (gate * sig)
        for micro in range(micros):
            dy_ref[places[micro], :] = dy[micro * count : (micro + 1) * count]
        dgate_ref[:, cols] = (dgated * y * (sig * (1.0 + gate * (1.0 - sig)))).astype(BF16)
    normed = normed_ref[...]
    edge = LANES // 2
    for j in range(chunks):
        grad = dot(gated_ref[:, lanes(j ^ cube)], cotan, 0, 0).astype(BF16)
        top, bottom = grad[:edge], grad[edge:]
        place = pl.ds((j & 3) * 2 * LANES + (j >> 2) * edge, edge)
        keep_ref[place, :] = jnp.where(core == 0, top, bottom)
        send_ref[place, :] = jnp.where(core == 0, bottom, top)
    share = jnp.zeros(share_ref.shape, F32)
    for j in range(chunks // 2):
        place = pl.ds((2 * j + 1) * LANES, LANES)
        pair = 2 * (j ^ face)
        for chunk, out_ref in ((pair + core, keep_ref), (pair + 1 - core, send_ref)):
            grad = dot(dgate_ref[:, lanes(chunk)], normed, 0, 0)
            share = share + eight_rows(grad * wgate_ref[0, chunk, 0].astype(F32))
            out_ref[place, :] = grad.astype(BF16)
    share_ref[...] = share
    width = cotan.shape[1]
    mixed_ref[...] = dot(gated_ref[...], wout_ref[...].reshape(chunks * LANES, width), 1, 0).astype(
        BF16
    )


def scan_forward(
    place,
    lengths,
    act_all,
    bc_own,
    bc_other,
    alog_own,
    alog_other,
    dtx,
    dt,
    bias,
    skip,
    act,
    gate,
    wout3,
    cotan,
    normed,
    w4,
):
    rows, own = act.shape
    chunks = own // LANES
    states = 2 * alog_own.shape[0]
    width = cotan.shape[1]
    micros, _, clusters = lengths.shape
    ranks = dtx.shape[0]
    outs = [
        ((rows, 2 * states), F32),
        ((rows, ranks), BF16),
        ((rows, 2 * ranks), BF16),
        ((states * chunks, LANES), F32),
        ((chunks * rows, LANES), F32),
        ((chunks * rows, LANES), F32),
        ((chunks * rows, LANES), F32),
        ((rows, width), BF16),
        ((rows, own), BF16),
        ((own, width), BF16),
        ((own, width), BF16),
        ((8, width), F32),
    ]
    operands = (
        act_all, bc_own, bc_other, alog_own, alog_other, dtx, dt, bias, skip, act, gate
    )
    return pl.pallas_call(
        functools.partial(
            forward_kernel,
            micros=micros,
            count=rows // micros,
            states=states,
            chunks=chunks,
            clusters=clusters,
        ),
        grid_spec=pltpu.PrefetchScalarGridSpec(
            num_scalar_prefetch=1,
            grid=(1,),
            in_specs=[pl.BlockSpec(memory_space=pltpu.SMEM)]
            + [whole(operand.shape) for operand in operands]
            + [
                pl.BlockSpec((chunks, 1, LANES, width), lambda i, p: (0, p[HALF], 0, 0)),
                whole((rows, width)),
                whole((rows, width)),
                pl.BlockSpec((1, chunks, 1, LANES, width), lambda i, p: (1, 0, p[HALF], 0, 0)),
            ],
            out_specs=[whole(shape) for shape, _ in outs],
            scratch_shapes=[
                pltpu.VMEM((2, rows, LANES), F32),
                pltpu.VMEM((chunks * rows, LANES), F32),
                pltpu.VMEM((rows, own), BF16),
                pltpu.VMEM((states * chunks, LANES), F32),
                pltpu.SMEM((rows, 2 * states), F32),
                pltpu.SemaphoreType.DMA,
            ],
        ),
        out_shape=[hbm(*out) for out in outs],
        compiler_params=params(48),
        cost_estimate=cost(19),
        name="scan_forward",
    )(place, lengths, act_all, bc_own, bc_other, alog_own, alog_other, *in_hbm(operands[5:]), *in_hbm((wout3, cotan, normed, w4)))


def backward_kernel(
    place_ref,
    bc_ref,
    decay_ref,
    rank_ref,
    dt_ref,
    bias_ref,
    act_ref,
    sp_ref,
    u_ref,
    dy_ref,
    code_ref,
    sact_ref,
    dpre_ref,
    alog_ref,
    vec_ref,
    h_ref,
    s_ref,
    d_ref,
    terms_ref,
    sums_ref,
    scalar_ref,
    sem,
    *,
    count,
    states,
    chunks,
):
    copy = pltpu.make_async_copy(bc_ref, scalar_ref, sem)
    copy.start()
    half = place_ref[HALF]
    eighth = states // 2
    alog_ref[...] = jnp.zeros_like(alog_ref)
    zero = (jnp.zeros((chunks, LANES), F32),) * states
    for n in range(states):
        h_ref[pl.ds(n * chunks, chunks), :] = zero[0]
    copy.wait()

    def recompute(t, h):
        span = pl.ds(t, chunks, stride=count)
        sp = sp_ref[span, :]
        u = u_ref[span, :]
        out = []
        for n in range(states):
            decay = jnp.exp2(sp * decay_ref[pl.ds(n * chunks, chunks), :])
            now = decay * h[n] + u * scalar_ref[t, b_at(n, eighth)]
            h_ref[aligned(((t + 1) * states + n) * chunks, chunks), :] = now
            out.append(now)
        return tuple(out)

    lax.fori_loop(0, count, recompute, zero, unroll=2)

    def retreat(back, carry):
        t = count - 1 - back
        span = pl.ds(t, chunks, stride=count)
        sp = sp_ref[span, :]
        u = u_ref[span, :]
        dy = dy_ref[span, :]
        out = []
        d_sum = None
        s_sum = None
        for n in range(states):
            rate = decay_ref[pl.ds(n * chunks, chunks), :]
            decay = jnp.exp2(sp * rate)
            dh = carry[n] + dy * scalar_ref[t, c_at(n, eighth)]
            flow = decay * dh
            out.append(flow)
            before = h_ref[aligned((t * states + n) * chunks, chunks), :]
            now = h_ref[aligned(((t + 1) * states + n) * chunks, chunks), :]
            q = flow * before
            alog_ref[pl.ds(n * chunks, chunks), :] += q * sp
            d_term = q * rate
            s_term = dh * scalar_ref[t, b_at(n, eighth)]
            d_sum = d_term if d_sum is None else d_sum + d_term
            s_sum = s_term if s_sum is None else s_sum + s_term
            terms_ref[pl.ds(b_at(n, eighth) * chunks, chunks), :] = dh * u
            terms_ref[pl.ds(c_at(n, eighth) * chunks, chunks), :] = dy * now
        s_ref[span, :] = s_sum
        d_ref[span, :] = d_sum
        sums = None
        for chunk in range(chunks):
            term = terms_ref[pl.ds(chunk, 2 * states, stride=chunks), :]
            sums = term if sums is None else sums + term
        sums_ref[aligned(t * 2 * states, 2 * states), :] = sums
        return tuple(out)

    lax.fori_loop(0, count, retreat, zero, unroll=2)

    rank = rank_ref[...]
    ranks = rank.shape[1]
    drank = None
    for chunk in range(chunks):
        cols = slice(chunk * LANES, (chunk + 1) * LANES)
        place = pl.ds(chunk * count, count)
        act = act_ref[:, cols].astype(F32)
        weight = dt_ref[:, lanes(2 * chunk + half)]
        pre = dot(rank, weight, 1, 0) + bias_ref[pl.ds(2 * chunk + half, 1), :]
        s_now = s_ref[place, :]
        dstep = d_ref[place, :] * (1.0 / LOG2E) + s_now * act
        sact_ref[:, cols] = s_now * softplus(pre)
        dpre = dstep * sigmoid(pre)
        vec_ref[0:1, cols] = jnp.sum(dpre, axis=0, keepdims=True)
        vec_ref[1:2, cols] = jnp.sum(dy_ref[place, :] * act, axis=0, keepdims=True)
        low = dpre.astype(BF16)
        dpre_ref[:, cols] = low
        term = dot(low, weight, 1, 1)
        drank = term if drank is None else drank + term
    source = lax.broadcasted_iota(jnp.int32, (2 * LANES, LANES), 0) // LANES
    target = lax.broadcasted_iota(jnp.int32, (2 * LANES, LANES), 1)
    code = None
    for k in range(states):
        pair = jnp.concatenate(
            [sums_ref[pl.ds(2 * k + j, count, stride=2 * states), :] for j in range(2)], axis=1
        )
        pick = jnp.where(target == source + (ranks + 2 * k), 1.0, 0.0).astype(BF16)
        term = dot(pair.astype(BF16), pick, 1, 0)
        code = term if code is None else code + term
    code_ref[...] = code + jnp.concatenate([drank, jnp.zeros((count, LANES - ranks), F32)], axis=1)


def scan_backward(place, micro, count, bc, decay, rank, dt, bias, act, sp, u, dy):
    rows, own = act.shape
    chunks = own // LANES
    states = bc.shape[1] // 2
    ranks = rank.shape[1]
    outs = [
        ((count, LANES), F32),
        ((count, own), F32),
        ((count, own), BF16),
        ((states * chunks, LANES), F32),
        ((2, own), F32),
    ]

    def block(*shape):
        return pl.BlockSpec(shape, lambda i, p: (micro, 0))

    return pl.pallas_call(
        functools.partial(backward_kernel, count=count, states=states, chunks=chunks),
        grid_spec=pltpu.PrefetchScalarGridSpec(
            num_scalar_prefetch=1,
            grid=(1,),
            in_specs=[
                block(count, 2 * states),
                whole(decay.shape),
                block(count, ranks),
                whole(dt.shape),
                whole(bias.shape),
                block(count, own),
                block(chunks * count, LANES),
                block(chunks * count, LANES),
                block(chunks * count, LANES),
            ],
            out_specs=[whole(shape) for shape, _ in outs],
            scratch_shapes=[
                pltpu.VMEM(((count + 1) * states * chunks, LANES), F32),
                pltpu.VMEM((chunks * count, LANES), F32),
                pltpu.VMEM((chunks * count, LANES), F32),
                pltpu.VMEM((2 * states * chunks, LANES), F32),
                pltpu.VMEM((count * 2 * states, LANES), F32),
                pltpu.SMEM((count, 2 * states), F32),
                pltpu.SemaphoreType.DMA,
            ],
        ),
        out_shape=[hbm(*out) for out in outs],
        compiler_params=params(26),
        cost_estimate=cost(15),
        name="scan_backward",
    )(place, *in_hbm((bc, decay, rank, dt, bias, act, sp, u, dy)))


def tail_kernel(
    place_ref,
    len_ref,
    *refs,
    micros,
    count,
    taps,
    clusters,
    ranks,
    chunks,
    states,
):
    def take(number):
        nonlocal refs
        taken, refs = refs[:number], refs[number:]
        return taken

    code_own, code_other, sact_refs, dpre_refs, alog_refs, back_refs = (
        take(micros) for _ in range(6)
    )
    dtx_ref, bc_own_ref, bc_other_ref, decay_ref = take(4)
    dy_refs = take(micros)
    conved_ref, inner_ref, act_ref, high_ref, convw_ref, skip_ref = take(6)
    normed_ref, win_ref, share_ref, gain_ref = take(4)
    keep_ref, send_ref, low_ref = take(3)
    mask_ref, code_ref, wcode_ref, vec_ref, alog_ref, total_ref = refs

    step = pl.program_id(0)
    rows = micros * count
    eighth = states // 2
    edge = LANES // 2
    half, core, cube, face = (place_ref[k] for k in range(4))
    pair = step ^ face
    span = LANES + 32

    def pack_row(chunk):
        relative = chunk ^ cube
        return (relative & 3) * span + LANES + (relative >> 2) * 16

    def place_pair(start, size, cols, even, odd):
        keep_ref[aligned(start, size, 16), cols] = jnp.where(core == 0, even, odd).astype(BF16)
        send_ref[aligned(start, size, 16), cols] = jnp.where(core == 0, odd, even).astype(BF16)

    @pl.when(step == 0)
    def _():
        fill_masks(len_ref, mask_ref, micros, count, taps, clusters)
        total_ref[...] = share_ref[...]
        for micro in range(micros):
            code_ref[pl.ds(micro * count, count), :] = (
                code_own[micro][...] + code_other[micro][...]
            ).astype(BF16)
        total = None
        for micro in range(micros):
            term = alog_refs[micro][...]
            total = term if total is None else total + term
        alog_ref[...] = total * (decay_ref[...] * (1.0 / LOG2E))

    code = code_ref[...]
    lane = lax.broadcasted_iota(jnp.int32, (1, LANES), 1)
    code_rank = jnp.where(lane < ranks, code, jnp.zeros_like(code))
    dpre = jnp.concatenate([ref[...] for ref in dpre_refs], axis=0)
    for part in range(2):
        source = lanes(2 * (2 * pair + part) + half)
        cols = slice(part * LANES, (part + 1) * LANES)
        wcode_ref[:ranks, cols] = dtx_ref[:, source]
        own = bc_own_ref[:, :, source].reshape(states, LANES)
        other = bc_other_ref[:, :, source].reshape(states, LANES)
        wcode_ref[ranks : ranks + states, cols] = jnp.where(half == 0, own, other)
        wcode_ref[ranks + states : ranks + 2 * states, cols] = jnp.where(half == 0, other, own)
        wcode_ref[ranks + 2 * states :, cols] = jnp.zeros(
            (LANES - ranks - 2 * states, LANES), BF16
        )
    for part in range(2):
        cols = slice(part * LANES, (part + 1) * LANES)
        chunk = 2 * pair + part
        source = 2 * chunk + half
        weights = convw_ref[:, lanes(source)]
        sact = jnp.concatenate([ref[:, cols] for ref in sact_refs], axis=0)
        dy = jnp.concatenate([ref[pl.ds(part * count, count), :] for ref in dy_refs], axis=0)
        dact = sact + dot(code, wcode_ref[:, cols], 1, 0)
        dact = dact + dy * skip_ref[pl.ds(source, 1), :]
        conved = conved_ref[:, cols]
        sig = sigmoid(conved)
        dconv = dact * (sig * (1.0 + conved * (1.0 - sig)))
        inner = inner_ref[:, cols]
        dinner = weights[taps - 1 : taps] * dconv
        sums = [None] * (taps + 1)
        sums[taps - 1] = jnp.sum(dconv * inner, axis=0, keepdims=True)
        sums[taps] = jnp.sum(dconv, axis=0, keepdims=True)
        for back in range(1, taps):
            kept = dconv * mask_ref[back]
            dinner = dinner + weights[taps - 1 - back : taps - back] * pltpu.roll(
                kept, rows - back, 0
            )
            sums[taps - 1 - back] = jnp.sum(
                kept * pltpu.roll(inner, back, 0), axis=0, keepdims=True
            )
        for k in range(taps + 1):
            vec_ref[k : k + 1, lanes(chunk)] = sums[k]
        for k in range(2):
            total = None
            for ref in back_refs:
                term = ref[k : k + 1, lanes(chunk)]
                total = term if total is None else total + term
            vec_ref[taps + 1 + k : taps + 2 + k, lanes(chunk)] = total
        low_ref[:, cols] = dinner.astype(BF16)

        act = act_ref[:, cols]
        start = pack_row(chunk)
        rows_now = dot(act, code_rank, 0, 0) + dot(dpre[:, cols], high_ref[...], 0, 0)
        for k in range(4):
            place_pair(
                start,
                16,
                slice(k * LANES, (k + 1) * LANES),
                rows_now[k * 16 : (k + 1) * 16],
                rows_now[edge + k * 16 : edge + (k + 1) * 16],
            )
        state_rows = dot(code, act, 0, 0)[ranks : ranks + 2 * states]
        place_pair(
            start, 16, slice(4 * LANES, 5 * LANES), state_rows[:states], state_rows[states:]
        )

    normed = normed_ref[...]
    for part in range(2):
        grad = dot(low_ref[:, lanes(core ^ part)], normed, 0, 0)
        total_ref[...] += eight_rows(grad * win_ref[0, core ^ part, 0].astype(F32))
        out_ref = (keep_ref, send_ref)[part]
        out_ref[aligned(step * span, LANES, 16), :] = grad.astype(BF16)

    @pl.when(step == pl.num_programs(0) - 1)
    def _():
        vec_ref[taps + 3 : taps + 4, :] = (
            jnp.sum(total_ref[...], axis=0, keepdims=True) / gain_ref[...]
        )
        for chunk in range(chunks):
            start = pack_row(chunk)
            vec = vec_ref[:, chunk * LANES : (chunk + 1) * LANES]
            alog = [
                alog_ref[pl.ds(q * eighth * chunks + chunk, eighth, stride=chunks), :]
                for q in range(2)
            ]
            place_pair(
                start,
                16,
                slice(5 * LANES, 6 * LANES),
                jnp.concatenate([alog[0], vec]),
                jnp.concatenate([alog[1], pltpu.roll(vec, edge, 1)]),
            )
            blank = jnp.zeros((16, 2 * LANES), F32)
            place_pair(start, 16, slice(6 * LANES, 8 * LANES), blank, blank)


def tail(
    place,
    lengths,
    code_own,
    code_other,
    sact,
    dpre,
    alog,
    back,
    dtx,
    bc_own,
    bc_other,
    decay,
    dy,
    conved,
    inner,
    act,
    high,
    convw,
    skip,
    normed,
    w4,
    share,
    gain,
):
    rows, own = act.shape
    chunks = own // LANES
    width = normed.shape[1]
    micros, _, clusters = lengths.shape
    count = rows // micros
    taps = convw.shape[0]
    ranks = dtx.shape[0]
    states = decay.shape[0] // chunks
    cols = 2 * LANES
    extent = 4 * (LANES + 32)

    def by_cols(height):
        return pl.BlockSpec((height, cols), lambda i, p: (0, i ^ p[FACE]))

    def dy_spec(micro):
        return pl.BlockSpec(
            (2 * count, LANES), lambda i, p: (micro * (chunks // 2) + (i ^ p[FACE]), 0)
        )

    in_specs = (
        [pl.BlockSpec(memory_space=pltpu.SMEM)]
        + [whole((count, LANES))] * (2 * micros)
        + [by_cols(count)] * (2 * micros)
        + [whole(alog[0].shape)] * micros
        + [whole(back[0].shape)] * micros
        + [whole(array.shape) for array in (dtx, bc_own, bc_other, decay)]
        + [dy_spec(micro) for micro in range(micros)]
        + [by_cols(rows)] * 3
        + [whole(array.shape) for array in (high, convw, skip, normed)]
        + [
            pl.BlockSpec(
                (1, 2, 1, LANES, width), lambda i, p: (0, i ^ p[FACE], p[HALF], 0, 0)
            ),
            whole(share.shape),
            whole(gain.shape),
        ]
    )
    return pl.pallas_call(
        functools.partial(
            tail_kernel,
            micros=micros,
            count=count,
            taps=taps,
            clusters=clusters,
            ranks=ranks,
            chunks=chunks,
            states=states,
        ),
        grid_spec=pltpu.PrefetchScalarGridSpec(
            num_scalar_prefetch=1,
            grid=(chunks // 2,),
            in_specs=in_specs,
            out_specs=[whole((extent, width)), whole((extent, width)), by_cols(rows)],
            scratch_shapes=[
                pltpu.VMEM((taps, rows, LANES), F32),
                pltpu.VMEM((rows, LANES), BF16),
                pltpu.VMEM((LANES, cols), BF16),
                pltpu.VMEM((8, own), F32),
                pltpu.VMEM((states * chunks, LANES), F32),
                pltpu.VMEM((8, width), F32),
            ],
        ),
        out_shape=[
            hbm((extent, width), BF16),
            hbm((extent, width), BF16),
            hbm((rows, own), BF16),
        ],
        compiler_params=params(24),
        cost_estimate=cost(7),
        name="tail",
    )(
        place,
        lengths,
        *code_own,
        *code_other,
        *in_hbm(
            (
                *sact,
                *dpre,
                *alog,
                *back,
                dtx,
                bc_own,
                bc_other,
                decay,
                *([dy] * micros),
                conved,
                inner,
                act,
                high,
                convw,
                skip,
                normed,
                w4,
                share,
                gain,
            )
        ),
    )


def spread_kernel(
    place_ref, low_ref, dgate_ref, win_ref, wgate_ref, dnormed_ref, total_ref
):
    step = pl.program_id(0)
    width = total_ref.shape[1]

    @pl.when(step == 0)
    def _():
        total_ref[...] = jnp.zeros_like(total_ref)

    total_ref[...] += dot(low_ref[...], win_ref[...].reshape(-1, width), 1, 0) + dot(
        dgate_ref[...], wgate_ref[...].reshape(-1, width), 1, 0
    )

    @pl.when(step == pl.num_programs(0) - 1)
    def _():
        dnormed_ref[...] = total_ref[...].astype(BF16)


def spread(place, low, dgate, w4):
    rows, own = low.shape
    width = w4.shape[-1]
    pairs = own // (2 * LANES)
    by_cols = pl.BlockSpec((rows, 2 * LANES), lambda i, p: (0, i))

    def weight_spec(which):
        return pl.BlockSpec((1, 2, 1, LANES, width), lambda i, p: (which, i, p[HALF], 0, 0))

    return pl.pallas_call(
        spread_kernel,
        grid_spec=pltpu.PrefetchScalarGridSpec(
            num_scalar_prefetch=1,
            grid=(pairs,),
            in_specs=[by_cols, by_cols, weight_spec(0), weight_spec(1)],
            out_specs=whole((rows, width)),
            scratch_shapes=[pltpu.VMEM((rows, width), F32)],
        ),
        out_shape=hbm((rows, width), BF16),
        compiler_params=params(16),
        cost_estimate=cost(4),
        name="spread",
    )(place, *in_hbm((low, dgate, w4, w4)))


def finish_kernel(
    x_ref, mine_ref, theirs_ref, dn_mine_ref, dn_theirs_ref, cotan_ref, gain_ref, mixed_ref, grad_ref
):
    x = x_ref[...].astype(F32)
    mixed_ref[...] = (
        x + (mine_ref[...].astype(F32) + theirs_ref[...].astype(F32))
    ).astype(BF16)
    scale = lax.rsqrt(jnp.mean(x * x, axis=1, keepdims=True) + EPSILON)
    unit = x * scale
    dhat = (dn_mine_ref[...].astype(F32) + dn_theirs_ref[...].astype(F32)) * gain_ref[...]
    grad_ref[...] = cotan_ref[...].astype(F32) + scale * (
        dhat - unit * jnp.mean(dhat * unit, axis=1, keepdims=True)
    )


def finish(x, mixed_mine, mixed_theirs, dn_mine, dn_theirs, cotan, gain):
    rows, width = x.shape
    block = rows // 4
    by_rows = pl.BlockSpec((block, width), lambda i: (i, 0))
    return pl.pallas_call(
        finish_kernel,
        grid=(4,),
        in_specs=[by_rows] * 6 + [whole(gain.shape)],
        out_specs=[by_rows] * 2,
        out_shape=[
            jax.ShapeDtypeStruct((rows, width), BF16),
            jax.ShapeDtypeStruct((rows, width), F32),
        ],
        compiler_params=params(16),
        cost_estimate=cost(3),
        name="finish",
    )(*in_hbm((x, mixed_mine, mixed_theirs, dn_mine, dn_theirs, cotan, gain)))


def pack_kernel(mine_ref, theirs_ref, pack_ref, gain_ref):
    pack_ref[...] = mine_ref[...] + theirs_ref[...]
    gain_ref[...] = pack_ref[:, 5 * LANES : 6 * LANES]


def sum_pack(mine, theirs):
    vmem = pl.BlockSpec(memory_space=pltpu.VMEM)
    return pl.pallas_call(
        pack_kernel,
        in_specs=[vmem] * 2,
        out_specs=[vmem] * 2,
        out_shape=[
            jax.ShapeDtypeStruct(mine.shape, BF16),
            jax.ShapeDtypeStruct((mine.shape[0], LANES), BF16),
        ],
        name="sum_pack",
    )(mine, theirs)


def unpack_kernel(
    place_ref,
    pack_ref,
    mine_ref,
    theirs_ref,
    out_ref,
    dtx_ref,
    dt_ref,
    bc_ref,
    alog_ref,
    convw_ref,
    convb_ref,
    bias_ref,
    skip_ref,
    gain_ref,
    out_grad_ref,
    *,
    eighth,
    taps,
    edge,
):
    pack = pack_ref[...].astype(F32)
    for k in range(4):
        rows = pack[:, k * LANES : (k + 1) * LANES]
        dtx_ref[pl.ds(16 * k, 16), :] = rows[:, :edge]
        dt_ref[pl.ds(16 * k, 16), :] = pltpu.roll(rows, edge, 1)[:, :edge]
    rows = pack[:, 4 * LANES : 5 * LANES]
    bc_ref[0] = rows[:eighth]
    bc_ref[1] = rows[eighth:]
    rows = pack[:, 5 * LANES : 6 * LANES]
    alog_ref[...] = rows[:eighth]
    vec = rows[eighth:, :edge]
    convw_ref[...] = vec[:taps]
    convb_ref[...] = vec[taps : taps + 1]
    bias_ref[...] = vec[taps + 1 : taps + 2]
    skip_ref[...] = vec[taps + 2 : taps + 3]
    gain = mine_ref[...].astype(F32) + theirs_ref[...].astype(F32)
    gain = jnp.where(place_ref[HALF] == 0, gain, pltpu.roll(gain, LANES - edge // 2, 1))
    gain_ref[...] = gain[15:16, : edge // 2]
    out_grad_ref[...] = out_ref[...].astype(F32)


def unpack(place, pack, gain_mine, gain_theirs, out, eighth, taps, ranks):
    edge = LANES // 2
    shapes = [
        (edge, ranks),
        (edge, ranks),
        (2, eighth, LANES),
        (eighth, LANES),
        (taps, edge),
        (1, edge),
        (1, edge),
        (1, edge),
        (1, edge // 2),
        out.shape,
    ]
    return pl.pallas_call(
        functools.partial(unpack_kernel, eighth=eighth, taps=taps, edge=edge),
        grid_spec=pltpu.PrefetchScalarGridSpec(
            num_scalar_prefetch=1,
            grid=(1,),
            in_specs=[whole(array.shape) for array in (pack, gain_mine, gain_theirs, out)],
            out_specs=[whole(shape) for shape in shapes],
        ),
        out_shape=[jax.ShapeDtypeStruct(shape, F32) for shape in shapes],
        name="unpack",
    )(place, pack, gain_mine, gain_theirs, out)


def swap_pair(array):
    count = lax.axis_size("state")
    return lax.ppermute(array, "state", [(pos, pos ^ 1) for pos in range(count)])


def swap_bit(array, bits, source=None):
    pairs = [
        (pos, pos ^ bits)
        for pos in range(lax.axis_size("dp"))
        if source is None or bool(pos & bits) == source
    ]
    return lax.ppermute(array, "dp", pairs)


def swap_odd(array):
    parts, states = lax.axis_size("dp"), lax.axis_size("state")
    pairs = []
    for d in range(parts):
        for s in range(states):
            at = d * states + s
            to = at if d % 2 == s % 2 else (d ^ 1) * states + (s ^ 1)
            pairs.append((at, to))
    return lax.ppermute(array, ("dp", "state"), pairs)


def add_quarters(kept, got):
    extent = kept.shape[0] // 4
    return [kept[k * extent :][:extent] + got[k * extent :][:extent] for k in range(4)]


def trade_quarters(quarters):
    return [quarters[0]] + [swap_bit(quarters[k], k * X_BIT) for k in range(1, 4)]


def sum_quarters(quarters):
    left, right = (quarters[k].astype(F32) + quarters[k + 1].astype(F32) for k in (0, 2))
    return (left + right).astype(BF16)


CORE_BIT, X_BIT, ZH_BIT = 1, 2, 8


def shards(
    tokens,
    cluster_len,
    norm_gain,
    in_weight,
    conv_weight,
    conv_bias,
    dtx_weight,
    dt_weight,
    dt_bias,
    bc_weight,
    a_log,
    skip_gain,
    out_weight,
    cotangent,
):
    micros, count, width = tokens.shape
    inner = out_weight.shape[0]
    taps = conv_weight.shape[0]
    ranks = dtx_weight.shape[1]
    chunks = inner // (2 * LANES)
    own = chunks * LANES
    rows = micros * count
    edge = LANES // 2
    span = LANES + 32
    dp_parts = lax.axis_size("dp")
    state_count = lax.axis_size("state")
    dp_pos = lax.axis_index("dp")
    state_pos = lax.axis_index("state")
    half = state_pos & 1
    fast = state_count == 2 and dp_parts == 2 * chunks == 16
    if fast:
        place = jnp.stack([half, dp_pos & 1, dp_pos >> 1, (dp_pos >> 1) & 3])
        bc_own, alog_own = bc_weight, a_log
        bc_other, alog_other = swap_pair(bc_weight), swap_pair(a_log)
    else:
        place = jnp.stack([half, 0, 0, 0])
        bc_all = lax.all_gather(bc_weight, "state", axis=1, tiled=True)
        alog_all = lax.all_gather(a_log, "state", axis=0, tiled=True)
        eighth = alog_all.shape[0] // 2
        bc_own, bc_other = (
            lax.dynamic_slice_in_dim(bc_all, which * eighth, eighth, 1)
            for which in (half, 1 - half)
        )
        alog_own, alog_other = (
            lax.dynamic_slice_in_dim(alog_all, which * eighth, eighth, 0)
            for which in (half, 1 - half)
        )
    place = place.astype(jnp.int32)
    eighth = alog_own.shape[0]
    states = 2 * eighth

    x = tokens.reshape(rows, width)
    cotan = cotangent.reshape(rows, width)
    w4 = in_weight.reshape(2, chunks, 2, LANES, width)
    wout3 = out_weight.reshape(chunks, 2, LANES, width)
    dtx, dt = dtx_weight.T, dt_weight.T
    bias = dt_bias.reshape(-1, LANES)
    skip = skip_gain.reshape(-1, LANES)

    normed, act_all, act, inner_own, conved, gate = project(
        place, cluster_len, x, norm_gain[None], w4, conv_weight, conv_bias.reshape(-1, LANES)
    )
    bc, rank, high, decay, sp, u, dy, mixed_part, dgate, keep, send, share = scan_forward(
        place,
        cluster_len,
        act_all,
        bc_own,
        bc_other,
        alog_own,
        alog_other,
        dtx,
        dt,
        bias,
        skip,
        act,
        gate,
        wout3,
        cotan,
        normed,
        w4,
    )
    early = None
    if fast:
        early = swap_bit(send, CORE_BIT)
    mixed_other = swap_pair(mixed_part)

    results = []
    for micro in range(micros):
        if fast and micro == micros - 1:
            *quarters, mixed_other, sp = lax.optimization_barrier(
                (*add_quarters(keep, early), mixed_other, sp)
            )
            early_got = trade_quarters(quarters)
        results.append(
            scan_backward(place, micro, count, bc, decay, rank, dt, bias, act, sp, u, dy)
        )
    code_own, sact, dpre, alog, back = zip(*results)
    code_other = [swap_pair(code) for code in code_own]
    if fast:
        *early_got, conved = lax.optimization_barrier((*early_got, conved))
    late_keep, late_send, low = tail(
        place,
        cluster_len,
        code_own,
        code_other,
        sact,
        dpre,
        alog,
        back,
        dtx,
        bc_own,
        bc_other,
        decay,
        dy,
        conved,
        inner_own,
        act,
        high,
        conv_weight,
        skip,
        normed,
        w4,
        share,
        norm_gain[None],
    )
    if fast:
        late = swap_bit(late_send, CORE_BIT)
        block = sum_quarters(early_got)
        out_keep, out_send, gate_sum = block[:edge], block[edge:LANES], block[LANES:]
        out_send, gate_sum, low = lax.optimization_barrier((out_send, gate_sum, low))
        out_got = swap_bit(out_send, ZH_BIT)
        gate_got = swap_bit(gate_sum, ZH_BIT, False)
    dnormed_part = spread(place, low, dgate, w4)
    dnormed_other = swap_pair(dnormed_part)
    if fast:
        late_got = trade_quarters(add_quarters(late_keep, late))
        block = sum_quarters(late_got)
        inner_sum, pack_keep, pack_send = block[:LANES], block[LANES:-16], block[-16:]
        pack_got = swap_bit(pack_send, ZH_BIT)
        inner_got = swap_bit(inner_sum, ZH_BIT, True)
        out_own = swap_odd(out_keep + out_got)
        upper = dp_pos >= dp_parts // 2
        pack, gain_mine = sum_pack(pack_keep, pack_got)
        gain_theirs = swap_pair(gain_mine)
        pack = swap_odd(pack)
        (
            dtx_grad,
            dt_grad,
            bc_grad,
            alog_grad,
            convw_grad,
            convb_grad,
            bias_grad,
            skip_grad,
            gain_grad,
            out_own,
        ) = unpack(place, pack, gain_mine, gain_theirs, out_own, eighth, taps, ranks)
        convb_grad, bias_grad, skip_grad, gain_grad = (
            array[0] for array in (convb_grad, bias_grad, skip_grad, gain_grad)
        )
        _, dnormed_other = lax.optimization_barrier((pack_got, dnormed_other))
        in_grad = jnp.where(
            upper,
            gate_sum.astype(F32) + gate_got.astype(F32),
            inner_sum.astype(F32) + inner_got.astype(F32),
        )
    mixed, tokens_grad = finish(
        x, mixed_part, mixed_other, dnormed_part, dnormed_other, cotan, norm_gain[None]
    )
    mixed = mixed.reshape(micros, count, width)
    tokens_grad = tokens_grad.reshape(micros, count, width)

    if not fast:
        def total(array):
            return lax.psum(array.astype(F32), "dp")

        def both_rows(array):
            mine = array.reshape(chunks, 1, LANES, -1)
            other = swap_pair(mine)
            low = jnp.where(half == 0, mine, other)
            high = jnp.where(half == 0, other, mine)
            return jnp.concatenate([low, high], axis=1).reshape(2 * own, -1)

        every = dp_parts * state_count
        at = dp_pos * state_count + state_pos

        def cut_own(array):
            extent = array.shape[0] // every
            return lax.dynamic_slice_in_dim(array, at * extent, extent, 0)

        pair = total(jnp.stack([keep, send])).reshape(2, 2, 2, 2 * LANES, width)
        outs = pair[:, :, :, :LANES].reshape(2, 2, 2, 2, edge, width)
        outs = jnp.transpose(outs, (3, 1, 2, 0, 4, 5)).reshape(own, width)
        gates = jnp.moveaxis(pair[:, :, :, LANES:], 0, 2).reshape(own, width)
        pair = total(jnp.stack([late_keep, late_send])).reshape(2, 2, 2, span, width)
        inners = jnp.moveaxis(pair[:, :, :, :LANES], 0, 2).reshape(own, width)
        packs = pair[:, :, :, LANES:].reshape(2, 2, 2, 2, 16, width // LANES, LANES)
        packs = jnp.transpose(packs, (3, 1, 2, 0, 5, 4, 6)).reshape(chunks, 2, -1, 16, LANES)
        small = both_rows(packs[:, :, :4].reshape(own, LANES))
        in_grad = cut_own(jnp.concatenate([both_rows(inners), both_rows(gates)]))
        out_own = cut_own(both_rows(outs))
        mine = cut_own(small)
        dtx_grad, dt_grad = mine[:, :ranks], mine[:, ranks:]
        vec_rows = jnp.swapaxes(packs[:, :, 5, eighth:, :edge], 2, 3).reshape(own, -1)
        gain_sum = vec_rows[:, -1]
        gain_grad = cut_own(gain_sum + swap_pair(gain_sum))
        vec = cut_own(both_rows(vec_rows)).T
        state_rows = jnp.concatenate([packs[:, :, 4], packs[:, :, 5, :eighth]], axis=2)
        state_rows = state_rows.reshape(chunks, 2, 3, eighth, LANES)
        state_rows = jnp.transpose(state_rows, (0, 4, 2, 1, 3)).reshape(own, -1)
        extent = inner // dp_parts
        state_part = lax.dynamic_slice_in_dim(both_rows(state_rows), dp_pos * extent, extent, 0)
        state_part = state_part.T.reshape(3, state_count, -1, extent)
        state_part = lax.dynamic_index_in_dim(state_part, state_pos, 1, keepdims=False)
        bc_grad, alog_grad = state_part[:2], state_part[2]
        convw_grad, convb_grad, bias_grad, skip_grad = (
            vec[:taps], vec[taps], vec[taps + 1], vec[taps + 2]
        )

    return (
        mixed,
        tokens_grad,
        gain_grad,
        in_grad,
        convw_grad,
        convb_grad,
        dtx_grad,
        dt_grad,
        bias_grad,
        bc_grad,
        alog_grad,
        skip_grad,
        out_own,
    )


def solution(mesh):
    return jax.shard_map(
        shards,
        mesh=mesh,
        in_specs=(
            P(None, "dp", None),
            P(None, "dp", None),
            P(),
            P(),
            P(),
            P(),
            P(),
            P(),
            P(),
            P(None, "state", None),
            P("state", None),
            P(),
            P(),
            P(None, "dp", None),
        ),
        out_specs=(
            P(None, "dp", None),
            P(None, "dp", None),
            P(("dp", "state")),
            P(("dp", "state"), None),
            P(None, ("dp", "state")),
            P(("dp", "state")),
            P(("dp", "state"), None),
            P(("dp", "state"), None),
            P(("dp", "state")),
            P(None, "state", "dp"),
            P("state", "dp"),
            P(("dp", "state")),
            P(("dp", "state"), None),
        ),
        check_vma=False,
    )
```

```python
import functools
import math

import jax
import jax.numpy as jnp
from jax import lax
from jax.experimental import pallas as pl
from jax.experimental.pallas import tpu as pltpu
from jax.sharding import PartitionSpec as P

EPSILON = 1e-05
LANES = 128
RESET = 1e4
LOG2E = math.log2(math.e)
F32 = jnp.float32
BF16 = jnp.bfloat16
MIB = 1024 * 1024


def dot(left, right, left_dim, right_dim):
    return lax.dot_general(
        left, right, (((left_dim,), (right_dim,)), ((), ())), preferred_element_type=F32
    )


def params(mib):
    return pltpu.CompilerParams(
        vmem_limit_bytes=mib * MIB, dimension_semantics=("arbitrary",)
    )


def whole(shape):
    return pl.BlockSpec(shape, lambda *_: (0,) * len(shape))


sigmoid = jax.nn.sigmoid


def softplus(value):
    return jnp.maximum(value, 0.0) + jnp.log1p(jnp.exp(-jnp.abs(value)))


def lanes(index):
    return pl.ds(pl.multiple_of(index * LANES, LANES), LANES)


def cost(micros):
    return pl.CostEstimate(
        flops=int(micros * 1e9), bytes_accessed=int(micros * 1e6), transcendentals=0
    )


def hbm(shape, dtype):
    return pltpu.HBM(shape, dtype)


def in_hbm(arrays):
    return [pltpu.with_memory_space_constraint(array, pltpu.HBM) for array in arrays]


def aligned(start, size, to=8):
    return pl.ds(pl.multiple_of(start, to), size)


HALF, CORE, CUBE, FACE = range(4)


def fill_masks(len_ref, mask_ref, micros, count, taps, clusters):
    place = lax.broadcasted_iota(jnp.int32, (count, LANES), 0)
    for micro in range(micros):
        rows = pl.ds(micro * count, count)
        for back in range(1, taps):
            apart = place < back
            start = 0
            for cluster in range(clusters - 1):
                start = start + len_ref[micro, 0, cluster]
                apart = apart | ((place >= start) & (place < start + back))
            mask_ref[back, rows, :] = jnp.where(apart, 0.0, 1.0)
            if back == 1:
                mask_ref[0, rows, :] = jnp.where(apart, 1.0, 0.0)


def project_kernel(
    place_ref,
    len_ref,
    x_ref,
    gain_ref,
    win_ref,
    wgate_ref,
    convw_ref,
    convb_ref,
    normed_ref,
    act_ref,
    own_act_ref,
    inner_ref,
    conved_ref,
    gate_ref,
    mask_ref,
    proj_ref,
    conv_ref,
    *,
    micros,
    count,
    taps,
    clusters,
):
    chunk = pl.program_id(0)

    @pl.when(chunk == 0)
    def _():
        fill_masks(len_ref, mask_ref, micros, count, taps, clusters)
        rows = x_ref[...].astype(F32)
        scale = lax.rsqrt(jnp.mean(rows * rows, axis=1, keepdims=True) + EPSILON)
        normed_ref[...] = (rows * scale * gain_ref[...]).astype(BF16)

    half = place_ref[HALF]
    normed = normed_ref[...]
    proj_ref[...] = dot(normed, win_ref[...].reshape(2 * LANES, -1), 1, 1)
    gate_ref[...] = dot(normed, wgate_ref[...].reshape(LANES, -1), 1, 1)
    for part in range(2):
        cols = pl.ds(part * LANES, LANES)
        inner = proj_ref[:, cols]
        conved = convb_ref[pl.ds(2 * chunk + part, 1), :] + convw_ref[taps - 1 : taps, cols] * inner
        for back in range(1, taps):
            shifted = pltpu.roll(inner, back, 0) * mask_ref[back]
            conved = conved + convw_ref[taps - 1 - back : taps - back, cols] * shifted
        conv_ref[:, cols] = conved
        act_ref[:, cols] = (conved * sigmoid(conved)).astype(BF16)
    own = lanes(half)
    inner_ref[...] = proj_ref[:, own]
    conved_ref[...] = conv_ref[:, own]
    own_act_ref[...] = act_ref[:, own]


def project(place, lengths, x, gain, w4, conv_weight, conv_bias):
    rows, width = x.shape
    chunks = w4.shape[1]
    inner = chunks * 2 * LANES
    micros, _, clusters = lengths.shape
    taps = conv_weight.shape[0]
    own = chunks * LANES
    by_chunk = pl.BlockSpec((rows, LANES), lambda i, p: (0, i))
    return pl.pallas_call(
        functools.partial(
            project_kernel, micros=micros, count=rows // micros, taps=taps, clusters=clusters
        ),
        grid_spec=pltpu.PrefetchScalarGridSpec(
            num_scalar_prefetch=1,
            grid=(chunks,),
            in_specs=[
                pl.BlockSpec(memory_space=pltpu.SMEM),
                whole((rows, width)),
                whole((1, width)),
                pl.BlockSpec((1, 1, 2, LANES, width), lambda i, p: (0, i, 0, 0, 0)),
                pl.BlockSpec((1, 1, 1, LANES, width), lambda i, p: (1, i, p[HALF], 0, 0)),
                pl.BlockSpec((taps, 2 * LANES), lambda i, p: (0, i)),
                whole(conv_bias.shape),
            ],
            out_specs=[
                whole((rows, width)),
                pl.BlockSpec((rows, 2 * LANES), lambda i, p: (0, i)),
                by_chunk,
                by_chunk,
                by_chunk,
                by_chunk,
            ],
            scratch_shapes=[
                pltpu.VMEM((taps, rows, LANES), F32),
                pltpu.VMEM((rows, 2 * LANES), F32),
                pltpu.VMEM((rows, 2 * LANES), F32),
            ],
        ),
        out_shape=[
            hbm((rows, width), BF16),
            hbm((rows, inner), BF16),
            hbm((rows, own), BF16),
            hbm((rows, own), F32),
            hbm((rows, own), F32),
            hbm((rows, own), F32),
        ],
        compiler_params=params(16),
        cost_estimate=cost(6),
        name="project",
    )(place, *in_hbm((lengths, x, gain, w4, w4, conv_weight, conv_bias)))


def eight_rows(array):
    return jnp.sum(array.reshape(-1, 8, array.shape[1]), axis=0)


def b_at(n, eighth):
    return (n // eighth) * 2 * eighth + n % eighth


def c_at(n, eighth):
    return b_at(n, eighth) + eighth


def forward_kernel(
    place_ref,
    len_ref,
    act_all_ref,
    bc_own_ref,
    bc_other_ref,
    alog_own_ref,
    alog_other_ref,
    dtx_ref,
    dt_ref,
    bias_ref,
    skip_ref,
    act_ref,
    gate_ref,
    wout_ref,
    cotan_ref,
    normed_ref,
    wgate_ref,
    bc_ref,
    rank_ref,
    rank_high_ref,
    decay_ref,
    sp_ref,
    u_ref,
    dy_ref,
    gated_ref,
    dgate_ref,
    keep_ref,
    send_ref,
    share_ref,
    mask_ref,
    y_ref,
    tmp_ref,
    scalar_ref,
    sem,
    *,
    micros,
    count,
    states,
    chunks,
    clusters,
):
    rows = micros * count
    eighth = states // 2
    half, core, cube, face = (place_ref[k] for k in range(4))
    first = half == 0
    act_all = act_all_ref[...]
    own = dot(act_all, bc_own_ref[...].reshape(states, -1), 1, 1)
    other = dot(act_all, bc_other_ref[...].reshape(states, -1), 1, 1)
    bc_ref[:, :states] = jnp.where(first, own, other)
    bc_ref[:, states:] = jnp.where(first, other, own)
    copy = pltpu.make_async_copy(bc_ref, scalar_ref, sem)
    copy.start()

    fill_masks(len_ref, mask_ref, micros, count, 2, clusters)
    for chunk in range(chunks):
        cols = lanes(2 * chunk + half)
        own, other = alog_own_ref[:, cols], alog_other_ref[:, cols]
        tmp_ref[pl.ds(chunk * states, eighth), :] = jnp.where(first, own, other)
        tmp_ref[pl.ds(chunk * states + eighth, eighth), :] = jnp.where(first, other, own)
    for n in range(states):
        decay_ref[pl.ds(n * chunks, chunks), :] = -LOG2E * jnp.exp(
            tmp_ref[pl.ds(n, chunks, stride=states), :]
        )

    rank = dot(act_all, dtx_ref[...], 1, 1).astype(BF16)
    rank_ref[...] = rank
    rank_high_ref[...] = jnp.concatenate([jnp.zeros_like(rank), rank], axis=1)
    for chunk in range(chunks):
        cols = slice(chunk * LANES, (chunk + 1) * LANES)
        bias = bias_ref[pl.ds(2 * chunk + half, 1), :]
        step = softplus(dot(rank, dt_ref[:, lanes(2 * chunk + half)], 1, 0) + bias)
        held = step + RESET * mask_ref[0]
        source = step * act_ref[:, cols].astype(F32)
        for micro in range(micros):
            span = slice(micro * count, (micro + 1) * count)
            place = pl.ds((micro * chunks + chunk) * count, count)
            sp_ref[place, :] = held[span]
            u_ref[place, :] = source[span]
    copy.wait()

    for micro in range(micros):

        def advance(t, h, micro=micro):
            row = micro * count + t
            span = pl.ds(micro * chunks * count + t, chunks, stride=count)
            sp = sp_ref[span, :]
            u = u_ref[span, :]
            out = []
            y = None
            for n in range(states):
                decay = jnp.exp2(sp * decay_ref[pl.ds(n * chunks, chunks), :])
                now = decay * h[n] + u * scalar_ref[row, b_at(n, eighth)]
                out.append(now)
                term = now * scalar_ref[row, c_at(n, eighth)]
                y = term if y is None else y + term
            y_ref[span, :] = y
            return tuple(out)

        lax.fori_loop(0, count, advance, (jnp.zeros((chunks, LANES), F32),) * states, unroll=2)

    cotan = cotan_ref[...]
    for chunk in range(chunks):
        cols = slice(chunk * LANES, (chunk + 1) * LANES)
        places = [pl.ds((micro * chunks + chunk) * count, count) for micro in range(micros)]
        y = jnp.concatenate([y_ref[place, :] for place in places])
        y = y + skip_ref[pl.ds(2 * chunk + half, 1), :] * act_ref[:, cols].astype(F32)
        gate = gate_ref[:, cols]
        sig = sigmoid(gate)
        gated_ref[:, cols] = (y * (gate * sig)).astype(BF16)
        dgated = dot(cotan, wout_ref[chunk, 0], 1, 1)
        dy = dgated * (gate * sig)
        for micro in range(micros):
            dy_ref[places[micro], :] = dy[micro * count : (micro + 1) * count]
        dgate_ref[:, cols] = (dgated * y * (sig * (1.0 + gate * (1.0 - sig)))).astype(BF16)
    normed = normed_ref[...]
    edge = LANES // 2
    for j in range(chunks):
        grad = dot(gated_ref[:, lanes(j ^ cube)], cotan, 0, 0).astype(BF16)
        top, bottom = grad[:edge], grad[edge:]
        place = pl.ds((j & 3) * 2 * LANES + (j >> 2) * edge, edge)
        keep_ref[place, :] = jnp.where(core == 0, top, bottom)
        send_ref[place, :] = jnp.where(core == 0, bottom, top)
    share = jnp.zeros(share_ref.shape, F32)
    for j in range(chunks // 2):
        place = pl.ds((2 * j + 1) * LANES, LANES)
        pair = 2 * (j ^ face)
        for chunk, out_ref in ((pair + core, keep_ref), (pair + 1 - core, send_ref)):
            grad = dot(dgate_ref[:, lanes(chunk)], normed, 0, 0)
            share = share + eight_rows(grad * wgate_ref[0, chunk, 0].astype(F32))
            out_ref[place, :] = grad.astype(BF16)
    share_ref[...] = share


def scan_forward(
    place,
    lengths,
    act_all,
    bc_own,
    bc_other,
    alog_own,
    alog_other,
    dtx,
    dt,
    bias,
    skip,
    act,
    gate,
    wout3,
    cotan,
    normed,
    w4,
):
    rows, own = act.shape
    chunks = own // LANES
    states = 2 * alog_own.shape[0]
    width = cotan.shape[1]
    micros, _, clusters = lengths.shape
    ranks = dtx.shape[0]
    outs = [
        ((rows, 2 * states), F32),
        ((rows, ranks), BF16),
        ((rows, 2 * ranks), BF16),
        ((states * chunks, LANES), F32),
        ((chunks * rows, LANES), F32),
        ((chunks * rows, LANES), F32),
        ((chunks * rows, LANES), F32),
        ((rows, own), BF16),
        ((rows, own), BF16),
        ((own, width), BF16),
        ((own, width), BF16),
        ((8, width), F32),
    ]
    operands = (
        act_all, bc_own, bc_other, alog_own, alog_other, dtx, dt, bias, skip, act, gate
    )
    return pl.pallas_call(
        functools.partial(
            forward_kernel,
            micros=micros,
            count=rows // micros,
            states=states,
            chunks=chunks,
            clusters=clusters,
        ),
        grid_spec=pltpu.PrefetchScalarGridSpec(
            num_scalar_prefetch=1,
            grid=(1,),
            in_specs=[pl.BlockSpec(memory_space=pltpu.SMEM)]
            + [whole(operand.shape) for operand in operands]
            + [
                pl.BlockSpec((chunks, 1, LANES, width), lambda i, p: (0, p[HALF], 0, 0)),
                whole((rows, width)),
                whole((rows, width)),
                pl.BlockSpec((1, chunks, 1, LANES, width), lambda i, p: (1, 0, p[HALF], 0, 0)),
            ],
            out_specs=[whole(shape) for shape, _ in outs],
            scratch_shapes=[
                pltpu.VMEM((2, rows, LANES), F32),
                pltpu.VMEM((chunks * rows, LANES), F32),
                pltpu.VMEM((states * chunks, LANES), F32),
                pltpu.SMEM((rows, 2 * states), F32),
                pltpu.SemaphoreType.DMA,
            ],
        ),
        out_shape=[hbm(*out) for out in outs],
        compiler_params=params(48),
        cost_estimate=cost(19),
        name="scan_forward",
    )(
        place,
        lengths,
        *in_hbm(operands[:1]),
        *operands[1:5],
        *in_hbm((*operands[5:], wout3, cotan, normed, w4)),
    )


def backward_kernel(
    place_ref,
    bc_ref,
    decay_ref,
    rank_ref,
    dt_ref,
    bias_ref,
    act_ref,
    sp_ref,
    u_ref,
    dy_ref,
    code_ref,
    sact_ref,
    dpre_ref,
    alog_ref,
    vec_ref,
    h_ref,
    s_ref,
    d_ref,
    terms_ref,
    sums_ref,
    scalar_ref,
    sem,
    *,
    count,
    states,
    chunks,
):
    copy = pltpu.make_async_copy(bc_ref, scalar_ref, sem)
    copy.start()
    half = place_ref[HALF]
    eighth = states // 2
    alog_ref[...] = jnp.zeros_like(alog_ref)
    zero = (jnp.zeros((chunks, LANES), F32),) * states
    for n in range(states):
        h_ref[pl.ds(n * chunks, chunks), :] = zero[0]
    copy.wait()

    def recompute(t, h):
        span = pl.ds(t, chunks, stride=count)
        sp = sp_ref[span, :]
        u = u_ref[span, :]
        out = []
        for n in range(states):
            decay = jnp.exp2(sp * decay_ref[pl.ds(n * chunks, chunks), :])
            now = decay * h[n] + u * scalar_ref[t, b_at(n, eighth)]
            h_ref[aligned(((t + 1) * states + n) * chunks, chunks), :] = now
            out.append(now)
        return tuple(out)

    lax.fori_loop(0, count, recompute, zero, unroll=2)

    def retreat(back, carry):
        t = count - 1 - back
        span = pl.ds(t, chunks, stride=count)
        sp = sp_ref[span, :]
        u = u_ref[span, :]
        dy = dy_ref[span, :]
        out = []
        d_sum = None
        s_sum = None
        for n in range(states):
            rate = decay_ref[pl.ds(n * chunks, chunks), :]
            decay = jnp.exp2(sp * rate)
            dh = carry[n] + dy * scalar_ref[t, c_at(n, eighth)]
            flow = decay * dh
            out.append(flow)
            before = h_ref[aligned((t * states + n) * chunks, chunks), :]
            now = h_ref[aligned(((t + 1) * states + n) * chunks, chunks), :]
            q = flow * before
            alog_ref[pl.ds(n * chunks, chunks), :] += q * sp
            d_term = q * rate
            s_term = dh * scalar_ref[t, b_at(n, eighth)]
            d_sum = d_term if d_sum is None else d_sum + d_term
            s_sum = s_term if s_sum is None else s_sum + s_term
            terms_ref[pl.ds(b_at(n, eighth) * chunks, chunks), :] = dh * u
            terms_ref[pl.ds(c_at(n, eighth) * chunks, chunks), :] = dy * now
        s_ref[span, :] = s_sum
        d_ref[span, :] = d_sum
        sums = None
        for chunk in range(chunks):
            term = terms_ref[pl.ds(chunk, 2 * states, stride=chunks), :]
            sums = term if sums is None else sums + term
        sums_ref[aligned(t * 2 * states, 2 * states), :] = sums
        return tuple(out)

    lax.fori_loop(0, count, retreat, zero, unroll=2)

    rank = rank_ref[...]
    ranks = rank.shape[1]
    drank = None
    for chunk in range(chunks):
        cols = slice(chunk * LANES, (chunk + 1) * LANES)
        place = pl.ds(chunk * count, count)
        act = act_ref[:, cols].astype(F32)
        weight = dt_ref[:, lanes(2 * chunk + half)]
        pre = dot(rank, weight, 1, 0) + bias_ref[pl.ds(2 * chunk + half, 1), :]
        s_now = s_ref[place, :]
        dstep = d_ref[place, :] * (1.0 / LOG2E) + s_now * act
        sact_ref[:, cols] = s_now * softplus(pre)
        dpre = dstep * sigmoid(pre)
        vec_ref[0:1, cols] = jnp.sum(dpre, axis=0, keepdims=True)
        vec_ref[1:2, cols] = jnp.sum(dy_ref[place, :] * act, axis=0, keepdims=True)
        low = dpre.astype(BF16)
        dpre_ref[:, cols] = low
        term = dot(low, weight, 1, 1)
        drank = term if drank is None else drank + term
    source = lax.broadcasted_iota(jnp.int32, (2 * LANES, LANES), 0) // LANES
    target = lax.broadcasted_iota(jnp.int32, (2 * LANES, LANES), 1)
    code = None
    for k in range(states):
        pair = jnp.concatenate(
            [sums_ref[pl.ds(2 * k + j, count, stride=2 * states), :] for j in range(2)], axis=1
        )
        pick = jnp.where(target == source + (ranks + 2 * k), 1.0, 0.0).astype(BF16)
        term = dot(pair.astype(BF16), pick, 1, 0)
        code = term if code is None else code + term
    code_ref[...] = code + jnp.concatenate([drank, jnp.zeros((count, LANES - ranks), F32)], axis=1)


def scan_backward(place, micro, count, bc, decay, rank, dt, bias, act, sp, u, dy):
    rows, own = act.shape
    chunks = own // LANES
    states = bc.shape[1] // 2
    ranks = rank.shape[1]
    outs = [
        ((count, LANES), F32),
        ((count, own), F32),
        ((count, own), BF16),
        ((states * chunks, LANES), F32),
        ((2, own), F32),
    ]

    def block(*shape):
        return pl.BlockSpec(shape, lambda i, p: (micro, 0))

    return pl.pallas_call(
        functools.partial(backward_kernel, count=count, states=states, chunks=chunks),
        grid_spec=pltpu.PrefetchScalarGridSpec(
            num_scalar_prefetch=1,
            grid=(1,),
            in_specs=[
                block(count, 2 * states),
                whole(decay.shape),
                block(count, ranks),
                whole(dt.shape),
                whole(bias.shape),
                block(count, own),
                block(chunks * count, LANES),
                block(chunks * count, LANES),
                block(chunks * count, LANES),
            ],
            out_specs=[whole(shape) for shape, _ in outs],
            scratch_shapes=[
                pltpu.VMEM(((count + 1) * states * chunks, LANES), F32),
                pltpu.VMEM((chunks * count, LANES), F32),
                pltpu.VMEM((chunks * count, LANES), F32),
                pltpu.VMEM((2 * states * chunks, LANES), F32),
                pltpu.VMEM((count * 2 * states, LANES), F32),
                pltpu.SMEM((count, 2 * states), F32),
                pltpu.SemaphoreType.DMA,
            ],
        ),
        out_shape=[hbm(*out) for out in outs],
        compiler_params=params(26),
        cost_estimate=cost(0),
        name="scan_backward",
    )(place, *in_hbm((bc, decay, rank, dt, bias, act, sp, u, dy)))


def tail_kernel(
    place_ref,
    len_ref,
    *refs,
    micros,
    count,
    taps,
    clusters,
    ranks,
    chunks,
    states,
):
    def take(number):
        nonlocal refs
        taken, refs = refs[:number], refs[number:]
        return taken

    code_own, code_other, sact_refs, dpre_refs, alog_refs, back_refs = (
        take(micros) for _ in range(6)
    )
    dtx_ref, bc_own_ref, bc_other_ref, decay_ref = take(4)
    dy_refs = take(micros)
    conved_ref, inner_ref, act_ref, high_ref, convw_ref, skip_ref = take(6)
    normed_ref, win_ref, share_ref, gain_ref = take(4)
    keep_ref, send_ref, low_ref = take(3)
    mask_ref, code_ref, wcode_ref, vec_ref, alog_ref, total_ref = refs

    step = pl.program_id(0)
    rows = micros * count
    eighth = states // 2
    edge = LANES // 2
    half, core, cube, face = (place_ref[k] for k in range(4))
    pair = step ^ face
    span = LANES + 32

    def pack_row(chunk):
        relative = chunk ^ cube
        return (relative & 3) * span + LANES + (relative >> 2) * 16

    def place_pair(start, size, cols, even, odd):
        keep_ref[aligned(start, size, 16), cols] = jnp.where(core == 0, even, odd).astype(BF16)
        send_ref[aligned(start, size, 16), cols] = jnp.where(core == 0, odd, even).astype(BF16)

    @pl.when(step == 0)
    def _():
        fill_masks(len_ref, mask_ref, micros, count, taps, clusters)
        total_ref[...] = share_ref[...]
        for micro in range(micros):
            code_ref[pl.ds(micro * count, count), :] = (
                code_own[micro][...] + code_other[micro][...]
            ).astype(BF16)
        total = None
        for micro in range(micros):
            term = alog_refs[micro][...]
            total = term if total is None else total + term
        alog_ref[...] = total * (decay_ref[...] * (1.0 / LOG2E))

    code = code_ref[...]
    lane = lax.broadcasted_iota(jnp.int32, (1, LANES), 1)
    code_rank = jnp.where(lane < ranks, code, jnp.zeros_like(code))
    dpre = jnp.concatenate([ref[...] for ref in dpre_refs], axis=0)
    for part in range(2):
        source = lanes(2 * (2 * pair + part) + half)
        cols = slice(part * LANES, (part + 1) * LANES)
        wcode_ref[:ranks, cols] = dtx_ref[:, source]
        own = bc_own_ref[:, :, source].reshape(states, LANES)
        other = bc_other_ref[:, :, source].reshape(states, LANES)
        wcode_ref[ranks : ranks + states, cols] = jnp.where(half == 0, own, other)
        wcode_ref[ranks + states : ranks + 2 * states, cols] = jnp.where(half == 0, other, own)
        wcode_ref[ranks + 2 * states :, cols] = jnp.zeros(
            (LANES - ranks - 2 * states, LANES), BF16
        )
    for part in range(2):
        cols = slice(part * LANES, (part + 1) * LANES)
        chunk = 2 * pair + part
        source = 2 * chunk + half
        weights = convw_ref[:, lanes(source)]
        sact = jnp.concatenate([ref[:, cols] for ref in sact_refs], axis=0)
        dy = jnp.concatenate([ref[pl.ds(part * count, count), :] for ref in dy_refs], axis=0)
        dact = sact + dot(code, wcode_ref[:, cols], 1, 0)
        dact = dact + dy * skip_ref[pl.ds(source, 1), :]
        conved = conved_ref[:, cols]
        sig = sigmoid(conved)
        dconv = dact * (sig * (1.0 + conved * (1.0 - sig)))
        inner = inner_ref[:, cols]
        dinner = weights[taps - 1 : taps] * dconv
        sums = [None] * (taps + 1)
        sums[taps - 1] = jnp.sum(dconv * inner, axis=0, keepdims=True)
        sums[taps] = jnp.sum(dconv, axis=0, keepdims=True)
        for back in range(1, taps):
            kept = dconv * mask_ref[back]
            dinner = dinner + weights[taps - 1 - back : taps - back] * pltpu.roll(
                kept, rows - back, 0
            )
            sums[taps - 1 - back] = jnp.sum(
                kept * pltpu.roll(inner, back, 0), axis=0, keepdims=True
            )
        for k in range(taps + 1):
            vec_ref[k : k + 1, lanes(chunk)] = sums[k]
        for k in range(2):
            total = None
            for ref in back_refs:
                term = ref[k : k + 1, lanes(chunk)]
                total = term if total is None else total + term
            vec_ref[taps + 1 + k : taps + 2 + k, lanes(chunk)] = total
        low_ref[:, cols] = dinner.astype(BF16)

        act = act_ref[:, cols]
        start = pack_row(chunk)
        rows_now = dot(act, code_rank, 0, 0) + dot(dpre[:, cols], high_ref[...], 0, 0)
        for k in range(4):
            place_pair(
                start,
                16,
                slice(k * LANES, (k + 1) * LANES),
                rows_now[k * 16 : (k + 1) * 16],
                rows_now[edge + k * 16 : edge + (k + 1) * 16],
            )
        state_rows = dot(code, act, 0, 0)[ranks : ranks + 2 * states]
        place_pair(
            start, 16, slice(4 * LANES, 5 * LANES), state_rows[:states], state_rows[states:]
        )

    normed = normed_ref[...]
    for part in range(2):
        grad = dot(low_ref[:, lanes(core ^ part)], normed, 0, 0)
        total_ref[...] += eight_rows(grad * win_ref[0, core ^ part, 0].astype(F32))
        out_ref = (keep_ref, send_ref)[part]
        out_ref[aligned(step * span, LANES, 16), :] = grad.astype(BF16)

    @pl.when(step == pl.num_programs(0) - 1)
    def _():
        vec_ref[taps + 3 : taps + 4, :] = (
            jnp.sum(total_ref[...], axis=0, keepdims=True) / gain_ref[...]
        )
        for chunk in range(chunks):
            start = pack_row(chunk)
            vec = vec_ref[:, chunk * LANES : (chunk + 1) * LANES]
            alog = [
                alog_ref[pl.ds(q * eighth * chunks + chunk, eighth, stride=chunks), :]
                for q in range(2)
            ]
            place_pair(
                start,
                16,
                slice(5 * LANES, 6 * LANES),
                jnp.concatenate([alog[0], vec]),
                jnp.concatenate([alog[1], pltpu.roll(vec, edge, 1)]),
            )
            blank = jnp.zeros((16, 2 * LANES), F32)
            place_pair(start, 16, slice(6 * LANES, 8 * LANES), blank, blank)


def tail(
    place,
    lengths,
    code_own,
    code_other,
    sact,
    dpre,
    alog,
    back,
    dtx,
    bc_own,
    bc_other,
    decay,
    dy,
    conved,
    inner,
    act,
    high,
    convw,
    skip,
    normed,
    w4,
    share,
    gain,
):
    rows, own = act.shape
    chunks = own // LANES
    width = normed.shape[1]
    micros, _, clusters = lengths.shape
    count = rows // micros
    taps = convw.shape[0]
    ranks = dtx.shape[0]
    states = decay.shape[0] // chunks
    cols = 2 * LANES
    extent = 4 * (LANES + 32)

    def by_cols(height):
        return pl.BlockSpec((height, cols), lambda i, p: (0, i ^ p[FACE]))

    def dy_spec(micro):
        return pl.BlockSpec(
            (2 * count, LANES), lambda i, p: (micro * (chunks // 2) + (i ^ p[FACE]), 0)
        )

    in_specs = (
        [pl.BlockSpec(memory_space=pltpu.SMEM)]
        + [whole((count, LANES))] * (2 * micros)
        + [by_cols(count)] * (2 * micros)
        + [whole(alog[0].shape)] * micros
        + [whole(back[0].shape)] * micros
        + [whole(array.shape) for array in (dtx, bc_own, bc_other, decay)]
        + [dy_spec(micro) for micro in range(micros)]
        + [by_cols(rows)] * 3
        + [whole(array.shape) for array in (high, convw, skip, normed)]
        + [
            pl.BlockSpec(
                (1, 2, 1, LANES, width), lambda i, p: (0, i ^ p[FACE], p[HALF], 0, 0)
            ),
            whole(share.shape),
            whole(gain.shape),
        ]
    )
    return pl.pallas_call(
        functools.partial(
            tail_kernel,
            micros=micros,
            count=count,
            taps=taps,
            clusters=clusters,
            ranks=ranks,
            chunks=chunks,
            states=states,
        ),
        grid_spec=pltpu.PrefetchScalarGridSpec(
            num_scalar_prefetch=1,
            grid=(chunks // 2,),
            in_specs=in_specs,
            out_specs=[whole((extent, width)), whole((extent, width)), by_cols(rows)],
            scratch_shapes=[
                pltpu.VMEM((taps, rows, LANES), F32),
                pltpu.VMEM((rows, LANES), BF16),
                pltpu.VMEM((LANES, cols), BF16),
                pltpu.VMEM((8, own), F32),
                pltpu.VMEM((states * chunks, LANES), F32),
                pltpu.VMEM((8, width), F32),
            ],
        ),
        out_shape=[
            hbm((extent, width), BF16),
            hbm((extent, width), BF16),
            hbm((rows, own), BF16),
        ],
        compiler_params=params(24),
        cost_estimate=cost(7),
        name="tail",
    )(
        place,
        lengths,
        *code_own,
        *code_other,
        *in_hbm(
            (
                *sact,
                *dpre,
                *alog,
                *back,
                dtx,
                bc_own,
                bc_other,
                decay,
                *([dy] * micros),
                conved,
                inner,
                act,
                high,
                convw,
                skip,
                normed,
                w4,
                share,
                gain,
            )
        ),
    )


def products_kernel(
    place_ref, gated_ref, dgate_ref, wout_ref, wgate_ref, mixed_ref, dnormed_ref, total_ref
):
    step = pl.program_id(0)
    width = total_ref.shape[1]

    @pl.when(step == 0)
    def _():
        total_ref[...] = jnp.zeros_like(total_ref)
        dnormed_ref[...] = jnp.zeros_like(dnormed_ref)

    total_ref[...] += dot(gated_ref[...], wout_ref[...].reshape(-1, width), 1, 0)
    dnormed_ref[...] += dot(dgate_ref[...], wgate_ref[...].reshape(-1, width), 1, 0)

    @pl.when(step == pl.num_programs(0) - 1)
    def _():
        mixed_ref[...] = total_ref[...].astype(BF16)


def products(place, gated, dgate, wout3, w4):
    rows, own = gated.shape
    width = w4.shape[-1]
    by_cols = pl.BlockSpec((rows, 2 * LANES), lambda i, p: (0, i))
    return pl.pallas_call(
        products_kernel,
        grid_spec=pltpu.PrefetchScalarGridSpec(
            num_scalar_prefetch=1,
            grid=(own // (2 * LANES),),
            in_specs=[
                by_cols,
                by_cols,
                pl.BlockSpec((2, 1, LANES, width), lambda i, p: (i, p[HALF], 0, 0)),
                pl.BlockSpec((1, 2, 1, LANES, width), lambda i, p: (1, i, p[HALF], 0, 0)),
            ],
            out_specs=[whole((rows, width))] * 2,
            scratch_shapes=[pltpu.VMEM((rows, width), F32)],
        ),
        out_shape=[hbm((rows, width), BF16), hbm((rows, width), F32)],
        compiler_params=params(16),
        cost_estimate=cost(4),
        name="products",
    )(place, *in_hbm((gated, dgate, wout3, w4)))


def spread_kernel(place_ref, low_ref, win_ref, gate_ref, dnormed_ref, total_ref):
    step = pl.program_id(0)
    width = total_ref.shape[1]

    @pl.when(step == 0)
    def _():
        total_ref[...] = gate_ref[...]

    total_ref[...] += dot(low_ref[...], win_ref[...].reshape(-1, width), 1, 0)

    @pl.when(step == pl.num_programs(0) - 1)
    def _():
        dnormed_ref[...] = total_ref[...].astype(BF16)


def spread(place, low, w4, gate_part):
    rows, own = low.shape
    width = w4.shape[-1]
    return pl.pallas_call(
        spread_kernel,
        grid_spec=pltpu.PrefetchScalarGridSpec(
            num_scalar_prefetch=1,
            grid=(own // (2 * LANES),),
            in_specs=[
                pl.BlockSpec((rows, 2 * LANES), lambda i, p: (0, i)),
                pl.BlockSpec((1, 2, 1, LANES, width), lambda i, p: (0, i, p[HALF], 0, 0)),
                whole((rows, width)),
            ],
            out_specs=whole((rows, width)),
            scratch_shapes=[pltpu.VMEM((rows, width), F32)],
        ),
        out_shape=hbm((rows, width), BF16),
        compiler_params=params(16),
        cost_estimate=cost(3),
        name="spread",
    )(place, *in_hbm((low, w4, gate_part)))


def finish_kernel(x_ref, mine_ref, theirs_ref, cotan_ref, gain_ref, grad_ref):
    x = x_ref[...].astype(F32)
    scale = lax.rsqrt(jnp.mean(x * x, axis=1, keepdims=True) + EPSILON)
    unit = x * scale
    dhat = (mine_ref[...].astype(F32) + theirs_ref[...].astype(F32)) * gain_ref[...]
    grad_ref[...] = cotan_ref[...].astype(F32) + scale * (
        dhat - unit * jnp.mean(dhat * unit, axis=1, keepdims=True)
    )


def finish(x, mine, theirs, cotan, gain):
    rows, width = x.shape
    by_rows = pl.BlockSpec((rows // 4, width), lambda i: (i, 0))
    return pl.pallas_call(
        finish_kernel,
        grid=(4,),
        in_specs=[by_rows] * 4 + [whole(gain.shape)],
        out_specs=by_rows,
        out_shape=jax.ShapeDtypeStruct((rows, width), F32),
        compiler_params=params(16),
        cost_estimate=cost(0),
        name="finish",
    )(*in_hbm((x, mine)), theirs, *in_hbm((cotan, gain)))


def unpack_kernel(
    place_ref,
    pack_near_ref,
    pack_far_ref,
    *refs,
    eighth,
    taps,
    edge,
):
    gain_refs, out_ref, refs = refs[:4], refs[4], refs[5:]
    dtx_ref, dt_ref, bc_ref, alog_ref, convw_ref, convb_ref = refs[:6]
    bias_ref, skip_ref, gain_ref, out_grad_ref = refs[6:]
    pack = pack_near_ref[...].astype(F32) + pack_far_ref[...].astype(F32)
    for k in range(4):
        rows = pack[:, k * LANES : (k + 1) * LANES]
        dtx_ref[pl.ds(16 * k, 16), :] = rows[:, :edge]
        dt_ref[pl.ds(16 * k, 16), :] = pltpu.roll(rows, edge, 1)[:, :edge]
    rows = pack[:, 4 * LANES : 5 * LANES]
    bc_ref[0] = rows[:eighth]
    bc_ref[1] = rows[eighth:]
    rows = pack[:, 5 * LANES : 6 * LANES]
    alog_ref[...] = rows[:eighth]
    vec = rows[eighth:, :edge]
    convw_ref[...] = vec[:taps]
    convb_ref[...] = vec[taps : taps + 1]
    bias_ref[...] = vec[taps + 1 : taps + 2]
    skip_ref[...] = vec[taps + 2 : taps + 3]
    gain = gain_refs[0][...].astype(F32)
    for ref in gain_refs[1:]:
        gain = gain + ref[...].astype(F32)
    gain = jnp.where(place_ref[HALF] == 0, gain, pltpu.roll(gain, LANES - edge // 2, 1))
    gain_ref[...] = gain[15:16, : edge // 2]
    out_grad_ref[...] = out_ref[...].astype(F32)


def unpack(place, packs, gains, out, eighth, taps, ranks):
    edge = LANES // 2
    shapes = [
        (edge, ranks),
        (edge, ranks),
        (2, eighth, LANES),
        (eighth, LANES),
        (taps, edge),
        (1, edge),
        (1, edge),
        (1, edge),
        (1, edge // 2),
        out.shape,
    ]
    return pl.pallas_call(
        functools.partial(unpack_kernel, eighth=eighth, taps=taps, edge=edge),
        grid_spec=pltpu.PrefetchScalarGridSpec(
            num_scalar_prefetch=1,
            grid=(1,),
            in_specs=[whole(array.shape) for array in (*packs, *gains, out)],
            out_specs=[whole(shape) for shape in shapes],
        ),
        out_shape=[jax.ShapeDtypeStruct(shape, F32) for shape in shapes],
        cost_estimate=cost(0),
        name="unpack",
    )(place, *packs, *gains, out)


def swap_pair(array):
    count = lax.axis_size("state")
    return lax.ppermute(array, "state", [(pos, pos ^ 1) for pos in range(count)])


def swap_bit(array, bits):
    return lax.ppermute(array, "dp", [(pos, pos ^ bits) for pos in range(lax.axis_size("dp"))])


def swap_both(array, bits=0, cross=False):
    states = lax.axis_size("state")
    pairs = []
    for d in range(lax.axis_size("dp")):
        for s in range(states):
            to_d, to_s = ((d & ~1) | s, d & 1) if cross else (d, s ^ 1)
            pairs.append((d * states + s, (to_d ^ bits) * states + to_s))
    return lax.ppermute(array, ("dp", "state"), pairs)


def add_quarters(kept, got):
    extent = kept.shape[0] // 4
    return [kept[k * extent :][:extent] + got[k * extent :][:extent] for k in range(4)]


def trade_quarters(quarters):
    return [quarters[0]] + [swap_bit(quarters[k], k * X_BIT) for k in range(1, 4)]


def sum_quarters(quarters):
    left, right = (quarters[k].astype(F32) + quarters[k + 1].astype(F32) for k in (0, 2))
    return (left + right).astype(BF16)


CORE_BIT, X_BIT, ZH_BIT = 1, 2, 8


def shards(
    tokens,
    cluster_len,
    norm_gain,
    in_weight,
    conv_weight,
    conv_bias,
    dtx_weight,
    dt_weight,
    dt_bias,
    bc_weight,
    a_log,
    skip_gain,
    out_weight,
    cotangent,
):
    micros, count, width = tokens.shape
    inner = out_weight.shape[0]
    taps = conv_weight.shape[0]
    ranks = dtx_weight.shape[1]
    chunks = inner // (2 * LANES)
    own = chunks * LANES
    rows = micros * count
    edge = LANES // 2
    span = LANES + 32
    dp_parts = lax.axis_size("dp")
    state_count = lax.axis_size("state")
    dp_pos = lax.axis_index("dp")
    state_pos = lax.axis_index("state")
    half = state_pos & 1
    fast = state_count == 2 and dp_parts == 2 * chunks == 16
    if fast:
        place = jnp.stack([half, dp_pos & 1, dp_pos >> 1, (dp_pos >> 1) & 3])
        bc_own, alog_own = bc_weight, a_log
        bc_other, alog_other = swap_pair(bc_weight), swap_pair(a_log)
    else:
        place = jnp.stack([half, 0, 0, 0])
        bc_all = lax.all_gather(bc_weight, "state", axis=1, tiled=True)
        alog_all = lax.all_gather(a_log, "state", axis=0, tiled=True)
        eighth = alog_all.shape[0] // 2
        bc_own, bc_other = (
            lax.dynamic_slice_in_dim(bc_all, which * eighth, eighth, 1)
            for which in (half, 1 - half)
        )
        alog_own, alog_other = (
            lax.dynamic_slice_in_dim(alog_all, which * eighth, eighth, 0)
            for which in (half, 1 - half)
        )
    place = place.astype(jnp.int32)
    eighth = alog_own.shape[0]
    states = 2 * eighth

    x = tokens.reshape(rows, width)
    cotan = cotangent.reshape(rows, width)
    w4 = in_weight.reshape(2, chunks, 2, LANES, width)
    wout3 = out_weight.reshape(chunks, 2, LANES, width)
    dtx, dt = dtx_weight.T, dt_weight.T
    bias = dt_bias.reshape(-1, LANES)
    skip = skip_gain.reshape(-1, LANES)

    normed, act_all, act, inner_own, conved, gate = project(
        place, cluster_len, x, norm_gain[None], w4, conv_weight, conv_bias.reshape(-1, LANES)
    )
    bc, rank, high, decay, sp, u, dy, gated, dgate, keep, send, share = scan_forward(
        place,
        cluster_len,
        act_all,
        bc_own,
        bc_other,
        alog_own,
        alog_other,
        dtx,
        dt,
        bias,
        skip,
        act,
        gate,
        wout3,
        cotan,
        normed,
        w4,
    )
    if fast:
        early = swap_bit(send, CORE_BIT)
    mixed_part, dn_gate = products(place, gated, dgate, wout3, w4)
    if fast:
        *quarters, mixed_part, dn_gate, sp = lax.optimization_barrier(
            (*add_quarters(keep, early), mixed_part, dn_gate, sp)
        )
        early_got = trade_quarters(quarters)
    mixed_other = swap_pair(mixed_part)
    results = [
        scan_backward(place, micro, count, bc, decay, rank, dt, bias, act, sp, u, dy)
        for micro in range(micros)
    ]
    code_own, sact, dpre, alog, back = zip(*results)
    code_other = [swap_pair(code) for code in code_own]
    if fast:
        *early_got, mixed_other, conved = lax.optimization_barrier(
            (*early_got, mixed_other, conved)
        )
    late_keep, late_send, low = tail(
        place,
        cluster_len,
        code_own,
        code_other,
        sact,
        dpre,
        alog,
        back,
        dtx,
        bc_own,
        bc_other,
        decay,
        dy,
        conved,
        inner_own,
        act,
        high,
        conv_weight,
        skip,
        normed,
        w4,
        share,
        norm_gain[None],
    )
    if fast:
        late = swap_bit(late_send, CORE_BIT)
        block = sum_quarters(early_got)
        out_keep, out_send, gate_sum = block[:edge], block[edge:LANES], block[LANES:]
        out_send, gate_sum, low = lax.optimization_barrier((out_send, gate_sum, low))
        out_got = swap_bit(out_send, ZH_BIT)
        late_got = trade_quarters(add_quarters(late_keep, late))
    dnormed_part = spread(place, low, w4, dn_gate)
    dnormed_other = swap_pair(dnormed_part)
    tokens_grad = finish(x, dnormed_part, dnormed_other, cotan, norm_gain[None])
    mixed = (x.astype(F32) + (mixed_part.astype(F32) + mixed_other.astype(F32))).astype(BF16)
    if fast:
        *late_got, mixed, tokens_grad = lax.optimization_barrier((*late_got, mixed, tokens_grad))
        out_own = swap_both(out_keep + out_got, cross=True)
        block = sum_quarters(late_got)
        inner_sum = block[:LANES]
        pack_near, pack_far = block[LANES:-16], block[-16:]
        upper = dp_pos >= dp_parts // 2
        pack_far_got = swap_both(pack_far, ZH_BIT, True)
        half_got = swap_bit(jnp.where(upper, inner_sum, gate_sum), ZH_BIT)
        pack_near_got = swap_both(pack_near, cross=True)
        near, far = (array[:, 5 * LANES : 6 * LANES] for array in (pack_near, pack_far))
        gains = [near, swap_bit(far, ZH_BIT), swap_both(near), swap_both(far, ZH_BIT)]
        (
            dtx_grad,
            dt_grad,
            bc_grad,
            alog_grad,
            convw_grad,
            convb_grad,
            bias_grad,
            skip_grad,
            gain_grad,
            out_own,
        ) = unpack(
            place, (pack_near_got, pack_far_got), gains, out_own, eighth, taps, ranks
        )
        convb_grad, bias_grad, skip_grad, gain_grad = (
            array[0] for array in (convb_grad, bias_grad, skip_grad, gain_grad)
        )
        in_grad = jnp.where(upper, gate_sum, inner_sum).astype(F32) + half_got.astype(F32)
    mixed = mixed.reshape(micros, count, width)
    tokens_grad = tokens_grad.reshape(micros, count, width)

    if not fast:
        def total(array):
            return lax.psum(array.astype(F32), "dp")

        def both_rows(array):
            mine = array.reshape(chunks, 1, LANES, -1)
            other = swap_pair(mine)
            low = jnp.where(half == 0, mine, other)
            high = jnp.where(half == 0, other, mine)
            return jnp.concatenate([low, high], axis=1).reshape(2 * own, -1)

        every = dp_parts * state_count
        at = dp_pos * state_count + state_pos

        def cut_own(array):
            extent = array.shape[0] // every
            return lax.dynamic_slice_in_dim(array, at * extent, extent, 0)

        pair = total(jnp.stack([keep, send])).reshape(2, 2, 2, 2 * LANES, width)
        outs = pair[:, :, :, :LANES].reshape(2, 2, 2, 2, edge, width)
        outs = jnp.transpose(outs, (3, 1, 2, 0, 4, 5)).reshape(own, width)
        gates = jnp.moveaxis(pair[:, :, :, LANES:], 0, 2).reshape(own, width)
        pair = total(jnp.stack([late_keep, late_send])).reshape(2, 2, 2, span, width)
        inners = jnp.moveaxis(pair[:, :, :, :LANES], 0, 2).reshape(own, width)
        packs = pair[:, :, :, LANES:].reshape(2, 2, 2, 2, 16, width // LANES, LANES)
        packs = jnp.transpose(packs, (3, 1, 2, 0, 5, 4, 6)).reshape(chunks, 2, -1, 16, LANES)
        small = both_rows(packs[:, :, :4].reshape(own, LANES))
        in_grad = cut_own(jnp.concatenate([both_rows(inners), both_rows(gates)]))
        out_own = cut_own(both_rows(outs))
        mine = cut_own(small)
        dtx_grad, dt_grad = mine[:, :ranks], mine[:, ranks:]
        vec_rows = jnp.swapaxes(packs[:, :, 5, eighth:, :edge], 2, 3).reshape(own, -1)
        gain_sum = vec_rows[:, -1]
        gain_grad = cut_own(gain_sum + swap_pair(gain_sum))
        vec = cut_own(both_rows(vec_rows)).T
        state_rows = jnp.concatenate([packs[:, :, 4], packs[:, :, 5, :eighth]], axis=2)
        state_rows = state_rows.reshape(chunks, 2, 3, eighth, LANES)
        state_rows = jnp.transpose(state_rows, (0, 4, 2, 1, 3)).reshape(own, -1)
        extent = inner // dp_parts
        state_part = lax.dynamic_slice_in_dim(both_rows(state_rows), dp_pos * extent, extent, 0)
        state_part = state_part.T.reshape(3, state_count, -1, extent)
        state_part = lax.dynamic_index_in_dim(state_part, state_pos, 1, keepdims=False)
        bc_grad, alog_grad = state_part[:2], state_part[2]
        convw_grad, convb_grad, bias_grad, skip_grad = (
            vec[:taps], vec[taps], vec[taps + 1], vec[taps + 2]
        )

    return (
        mixed,
        tokens_grad,
        gain_grad,
        in_grad,
        convw_grad,
        convb_grad,
        dtx_grad,
        dt_grad,
        bias_grad,
        bc_grad,
        alog_grad,
        skip_grad,
        out_own,
    )


def solution(mesh):
    return jax.shard_map(
        shards,
        mesh=mesh,
        in_specs=(
            P(None, "dp", None),
            P(None, "dp", None),
            P(),
            P(),
            P(),
            P(),
            P(),
            P(),
            P(),
            P(None, "state", None),
            P("state", None),
            P(),
            P(),
            P(None, "dp", None),
        ),
        out_specs=(
            P(None, "dp", None),
            P(None, "dp", None),
            P(("dp", "state")),
            P(("dp", "state"), None),
            P(None, ("dp", "state")),
            P(("dp", "state")),
            P(("dp", "state"), None),
            P(("dp", "state"), None),
            P(("dp", "state")),
            P(None, "state", "dp"),
            P("state", "dp"),
            P(("dp", "state")),
            P(("dp", "state"), None),
        ),
        check_vma=False,
    )
```

```python
import functools
import math

import jax
import jax.numpy as jnp
from jax import lax
from jax.experimental import pallas as pl
from jax.experimental.pallas import tpu as pltpu
from jax.sharding import PartitionSpec as P

EPSILON = 1e-05
LANES = 128
RESET = 1e4
LOG2E = math.log2(math.e)
F32 = jnp.float32
BF16 = jnp.bfloat16
MIB = 1024 * 1024


def dot(left, right, left_dim, right_dim):
    return lax.dot_general(
        left, right, (((left_dim,), (right_dim,)), ((), ())), preferred_element_type=F32
    )


def params(mib):
    return pltpu.CompilerParams(
        vmem_limit_bytes=mib * MIB, dimension_semantics=("arbitrary",)
    )


ANY = pl.BlockSpec(memory_space=pl.ANY)


def stream(step, steps, fetch):
    @pl.when(step == 0)
    def _():
        for k in range(steps):
            for copy in fetch(k):
                copy.start()

    for copy in fetch(step):
        copy.wait()


def whole(shape):
    return pl.BlockSpec(shape, lambda *_: (0,) * len(shape))


sigmoid = jax.nn.sigmoid


def softplus(value):
    return jnp.maximum(value, 0.0) + jnp.log1p(jnp.exp(-jnp.abs(value)))


def lanes(index):
    return pl.ds(pl.multiple_of(index * LANES, LANES), LANES)


def cost(micros):
    return pl.CostEstimate(
        flops=int(micros * 1e9), bytes_accessed=int(micros * 1e6), transcendentals=0
    )


def hbm(shape, dtype):
    return pltpu.HBM(shape, dtype)


def in_hbm(arrays):
    return [pltpu.with_memory_space_constraint(array, pltpu.HBM) for array in arrays]


def aligned(start, size, to=8):
    return pl.ds(pl.multiple_of(start, to), size)


HALF, CORE, CUBE, FACE = range(4)


def fill_masks(len_ref, mask_ref, micros, count, taps, clusters):
    place = lax.broadcasted_iota(jnp.int32, (count, LANES), 0)
    for micro in range(micros):
        rows = pl.ds(micro * count, count)
        for back in range(1, taps):
            apart = place < back
            start = 0
            for cluster in range(clusters - 1):
                start = start + len_ref[micro, 0, cluster]
                apart = apart | ((place >= start) & (place < start + back))
            mask_ref[back, rows, :] = jnp.where(apart, 0.0, 1.0)
            if back == 1:
                mask_ref[0, rows, :] = jnp.where(apart, 1.0, 0.0)


def project_kernel(
    place_ref,
    len_ref,
    x_ref,
    gain_ref,
    weight_ref,
    convw_ref,
    convb_ref,
    normed_ref,
    act_ref,
    own_act_ref,
    inner_ref,
    conved_ref,
    gate_ref,
    mask_ref,
    proj_ref,
    conv_ref,
    win_ref,
    wgate_ref,
    sems,
    *,
    micros,
    count,
    taps,
    clusters,
):
    chunk = pl.program_id(0)

    @pl.when(chunk == 0)
    def _():
        fill_masks(len_ref, mask_ref, micros, count, taps, clusters)
        rows = x_ref[...].astype(F32)
        scale = lax.rsqrt(jnp.mean(rows * rows, axis=1, keepdims=True) + EPSILON)
        normed_ref[...] = (rows * scale * gain_ref[...]).astype(BF16)

    half = place_ref[HALF]

    def fetch(k):
        return (
            pltpu.make_async_copy(weight_ref.at[0, k], win_ref.at[k], sems.at[0, k]),
            pltpu.make_async_copy(weight_ref.at[1, k, half], wgate_ref.at[k], sems.at[1, k]),
        )

    stream(chunk, win_ref.shape[0], fetch)
    normed = normed_ref[...]
    proj_ref[...] = dot(normed, win_ref[chunk].reshape(2 * LANES, -1), 1, 1)
    gate_ref[...] = dot(normed, wgate_ref[chunk], 1, 1)
    for part in range(2):
        cols = pl.ds(part * LANES, LANES)
        inner = proj_ref[:, cols]
        conved = convb_ref[pl.ds(2 * chunk + part, 1), :] + convw_ref[taps - 1 : taps, cols] * inner
        for back in range(1, taps):
            shifted = pltpu.roll(inner, back, 0) * mask_ref[back]
            conved = conved + convw_ref[taps - 1 - back : taps - back, cols] * shifted
        conv_ref[:, cols] = conved
        act_ref[:, cols] = (conved * sigmoid(conved)).astype(BF16)
    own = lanes(half)
    inner_ref[...] = proj_ref[:, own]
    conved_ref[...] = conv_ref[:, own]
    own_act_ref[...] = act_ref[:, own]


def project(place, lengths, x, gain, w4, conv_weight, conv_bias):
    rows, width = x.shape
    chunks = w4.shape[1]
    inner = chunks * 2 * LANES
    micros, _, clusters = lengths.shape
    taps = conv_weight.shape[0]
    own = chunks * LANES
    by_chunk = pl.BlockSpec((rows, LANES), lambda i, p: (0, i))
    return pl.pallas_call(
        functools.partial(
            project_kernel, micros=micros, count=rows // micros, taps=taps, clusters=clusters
        ),
        grid_spec=pltpu.PrefetchScalarGridSpec(
            num_scalar_prefetch=1,
            grid=(chunks,),
            in_specs=[
                pl.BlockSpec(memory_space=pltpu.SMEM),
                whole((rows, width)),
                whole((1, width)),
                ANY,
                pl.BlockSpec((taps, 2 * LANES), lambda i, p: (0, i)),
                whole(conv_bias.shape),
            ],
            out_specs=[
                whole((rows, width)),
                pl.BlockSpec((rows, 2 * LANES), lambda i, p: (0, i)),
                by_chunk,
                by_chunk,
                by_chunk,
                by_chunk,
            ],
            scratch_shapes=[
                pltpu.VMEM((taps, rows, LANES), F32),
                pltpu.VMEM((rows, 2 * LANES), F32),
                pltpu.VMEM((rows, 2 * LANES), F32),
                pltpu.VMEM((chunks, 2, LANES, width), BF16),
                pltpu.VMEM((chunks, LANES, width), BF16),
                pltpu.SemaphoreType.DMA((2, chunks)),
            ],
        ),
        out_shape=[
            hbm((rows, width), BF16),
            hbm((rows, inner), BF16),
            hbm((rows, own), BF16),
            hbm((rows, own), F32),
            hbm((rows, own), F32),
            hbm((rows, own), F32),
        ],
        compiler_params=params(20),
        cost_estimate=cost(6),
        name="project",
    )(place, *in_hbm((lengths, x, gain, w4, conv_weight, conv_bias)))


def eight_rows(array):
    return jnp.sum(array.reshape(-1, 8, array.shape[1]), axis=0)


def b_at(n, eighth):
    return (n // eighth) * 2 * eighth + n % eighth


def c_at(n, eighth):
    return b_at(n, eighth) + eighth


def forward_kernel(
    place_ref,
    len_ref,
    act_all_ref,
    bc_own_ref,
    bc_other_ref,
    alog_own_ref,
    alog_other_ref,
    dtx_ref,
    dt_ref,
    bias_ref,
    skip_ref,
    act_ref,
    gate_ref,
    wout_ref,
    cotan_ref,
    normed_ref,
    wgate_ref,
    bc_ref,
    rank_ref,
    rank_high_ref,
    decay_ref,
    sp_ref,
    u_ref,
    dy_ref,
    gated_ref,
    dgate_ref,
    keep_ref,
    send_ref,
    share_ref,
    mask_ref,
    y_ref,
    tmp_ref,
    scalar_ref,
    sem,
    *,
    micros,
    count,
    states,
    chunks,
    clusters,
):
    rows = micros * count
    eighth = states // 2
    half, core, cube, face = (place_ref[k] for k in range(4))
    first = half == 0
    act_all = act_all_ref[...]
    own = dot(act_all, bc_own_ref[...].reshape(states, -1), 1, 1)
    other = dot(act_all, bc_other_ref[...].reshape(states, -1), 1, 1)
    bc_ref[:, :states] = jnp.where(first, own, other)
    bc_ref[:, states:] = jnp.where(first, other, own)
    copy = pltpu.make_async_copy(bc_ref, scalar_ref, sem)
    copy.start()

    fill_masks(len_ref, mask_ref, micros, count, 2, clusters)
    for chunk in range(chunks):
        cols = lanes(2 * chunk + half)
        own, other = alog_own_ref[:, cols], alog_other_ref[:, cols]
        tmp_ref[pl.ds(chunk * states, eighth), :] = jnp.where(first, own, other)
        tmp_ref[pl.ds(chunk * states + eighth, eighth), :] = jnp.where(first, other, own)
    for n in range(states):
        decay_ref[pl.ds(n * chunks, chunks), :] = -LOG2E * jnp.exp(
            tmp_ref[pl.ds(n, chunks, stride=states), :]
        )

    rank = dot(act_all, dtx_ref[...], 1, 1).astype(BF16)
    rank_ref[...] = rank
    rank_high_ref[...] = jnp.concatenate([jnp.zeros_like(rank), rank], axis=1)
    for chunk in range(chunks):
        cols = slice(chunk * LANES, (chunk + 1) * LANES)
        bias = bias_ref[pl.ds(2 * chunk + half, 1), :]
        step = softplus(dot(rank, dt_ref[:, lanes(2 * chunk + half)], 1, 0) + bias)
        held = step + RESET * mask_ref[0]
        source = step * act_ref[:, cols].astype(F32)
        for micro in range(micros):
            span = slice(micro * count, (micro + 1) * count)
            place = pl.ds((micro * chunks + chunk) * count, count)
            sp_ref[place, :] = held[span]
            u_ref[place, :] = source[span]
    copy.wait()

    for micro in range(micros):

        def advance(t, h, micro=micro):
            row = micro * count + t
            span = pl.ds(micro * chunks * count + t, chunks, stride=count)
            sp = sp_ref[span, :]
            u = u_ref[span, :]
            out = []
            y = None
            for n in range(states):
                decay = jnp.exp2(sp * decay_ref[pl.ds(n * chunks, chunks), :])
                now = decay * h[n] + u * scalar_ref[row, b_at(n, eighth)]
                out.append(now)
                term = now * scalar_ref[row, c_at(n, eighth)]
                y = term if y is None else y + term
            y_ref[span, :] = y
            return tuple(out)

        lax.fori_loop(0, count, advance, (jnp.zeros((chunks, LANES), F32),) * states, unroll=2)

    cotan = cotan_ref[...]
    for chunk in range(chunks):
        cols = slice(chunk * LANES, (chunk + 1) * LANES)
        places = [pl.ds((micro * chunks + chunk) * count, count) for micro in range(micros)]
        y = jnp.concatenate([y_ref[place, :] for place in places])
        y = y + skip_ref[pl.ds(2 * chunk + half, 1), :] * act_ref[:, cols].astype(F32)
        gate = gate_ref[:, cols]
        sig = sigmoid(gate)
        gated_ref[:, cols] = (y * (gate * sig)).astype(BF16)
        dgated = dot(cotan, wout_ref[chunk, 0], 1, 1)
        dy = dgated * (gate * sig)
        for micro in range(micros):
            dy_ref[places[micro], :] = dy[micro * count : (micro + 1) * count]
        dgate_ref[:, cols] = (dgated * y * (sig * (1.0 + gate * (1.0 - sig)))).astype(BF16)
    normed = normed_ref[...]
    edge = LANES // 2
    for j in range(chunks):
        grad = dot(gated_ref[:, lanes(j ^ cube)], cotan, 0, 0).astype(BF16)
        top, bottom = grad[:edge], grad[edge:]
        place = pl.ds((j & 3) * 2 * LANES + (j >> 2) * edge, edge)
        keep_ref[place, :] = jnp.where(core == 0, top, bottom)
        send_ref[place, :] = jnp.where(core == 0, bottom, top)
    share = jnp.zeros(share_ref.shape, F32)
    for j in range(chunks // 2):
        place = pl.ds((2 * j + 1) * LANES, LANES)
        pair = 2 * (j ^ face)
        for chunk, out_ref in ((pair + core, keep_ref), (pair + 1 - core, send_ref)):
            grad = dot(dgate_ref[:, lanes(chunk)], normed, 0, 0)
            share = share + eight_rows(grad * wgate_ref[0, chunk, 0].astype(F32))
            out_ref[place, :] = grad.astype(BF16)
    share_ref[...] = share


def scan_forward(
    place,
    lengths,
    act_all,
    bc_own,
    bc_other,
    alog_own,
    alog_other,
    dtx,
    dt,
    bias,
    skip,
    act,
    gate,
    wout3,
    cotan,
    normed,
    w4,
):
    rows, own = act.shape
    chunks = own // LANES
    states = 2 * alog_own.shape[0]
    width = cotan.shape[1]
    micros, _, clusters = lengths.shape
    ranks = dtx.shape[0]
    outs = [
        ((rows, 2 * states), F32),
        ((rows, ranks), BF16),
        ((rows, 2 * ranks), BF16),
        ((states * chunks, LANES), F32),
        ((chunks * rows, LANES), F32),
        ((chunks * rows, LANES), F32),
        ((chunks * rows, LANES), F32),
        ((rows, own), BF16),
        ((rows, own), BF16),
        ((own, width), BF16),
        ((own, width), BF16),
        ((8, width), F32),
    ]
    operands = (
        act_all, bc_own, bc_other, alog_own, alog_other, dtx, dt, bias, skip, act, gate
    )
    return pl.pallas_call(
        functools.partial(
            forward_kernel,
            micros=micros,
            count=rows // micros,
            states=states,
            chunks=chunks,
            clusters=clusters,
        ),
        grid_spec=pltpu.PrefetchScalarGridSpec(
            num_scalar_prefetch=1,
            grid=(1,),
            in_specs=[pl.BlockSpec(memory_space=pltpu.SMEM)]
            + [whole(operand.shape) for operand in operands]
            + [
                pl.BlockSpec((chunks, 1, LANES, width), lambda i, p: (0, p[HALF], 0, 0)),
                whole((rows, width)),
                whole((rows, width)),
                pl.BlockSpec((1, chunks, 1, LANES, width), lambda i, p: (1, 0, p[HALF], 0, 0)),
            ],
            out_specs=[whole(shape) for shape, _ in outs],
            scratch_shapes=[
                pltpu.VMEM((2, rows, LANES), F32),
                pltpu.VMEM((chunks * rows, LANES), F32),
                pltpu.VMEM((states * chunks, LANES), F32),
                pltpu.SMEM((rows, 2 * states), F32),
                pltpu.SemaphoreType.DMA,
            ],
        ),
        out_shape=[hbm(*out) for out in outs],
        compiler_params=params(48),
        cost_estimate=cost(19),
        name="scan_forward",
    )(
        place,
        lengths,
        *in_hbm(operands[:1]),
        *operands[1:5],
        *in_hbm((*operands[5:], wout3, cotan, normed, w4)),
    )


def reduce_terms(terms_ref, slot, states, chunks):
    sums = None
    for chunk in range(chunks):
        term = terms_ref[slot, pl.ds(chunk, states, stride=chunks), :]
        sums = term if sums is None else sums + term
    return sums


def backward_kernel(
    place_ref,
    bc_ref,
    decay_ref,
    rank_ref,
    dt_ref,
    bias_ref,
    act_ref,
    sp_ref,
    u_ref,
    dy_ref,
    *refs,
    count,
    states,
    chunks,
):
    code_ref, sact_ref, dpre_ref, alog_ref, vec_ref = refs[-13:-8]
    h_ref, s_ref, d_ref, terms_ref, sums_b_ref, sums_c_ref, scalar_ref, sem = refs[-8:]
    copy = pltpu.make_async_copy(bc_ref, scalar_ref, sem)
    copy.start()
    half = place_ref[HALF]
    eighth = states // 2
    zero = (jnp.zeros((chunks, LANES), F32),) * states
    for n in range(states):
        h_ref[pl.ds(n * chunks, chunks), :] = zero[0]
    copy.wait()

    def recompute(pair, h):
        for slot in range(2):
            t = 2 * pair + slot
            span = pl.ds(t, chunks, stride=count)
            sp = sp_ref[span, :]
            u = u_ref[span, :]
            dy = dy_ref[span, :]
            out = []
            for n in range(states):
                decay = jnp.exp2(sp * decay_ref[pl.ds(n * chunks, chunks), :])
                now = decay * h[n] + u * scalar_ref[t, b_at(n, eighth)]
                h_ref[aligned(((t + 1) * states + n) * chunks, chunks), :] = now
                terms_ref[slot, pl.ds(n * chunks, chunks), :] = dy * now
                out.append(now)
            sums_c_ref[aligned(t * states, states), :] = reduce_terms(
                terms_ref, slot, states, chunks
            )
            h = tuple(out)
        return h

    lax.fori_loop(0, count // 2, recompute, zero)

    def retreat(back, carry):
        flows, totals = carry
        for slot in range(2):
            t = count - 1 - (2 * back + slot)
            span = pl.ds(t, chunks, stride=count)
            sp = sp_ref[span, :]
            u = u_ref[span, :]
            dy = dy_ref[span, :]
            out_flows = []
            out_totals = []
            d_sum = None
            s_sum = None
            for n in range(states):
                rate = decay_ref[pl.ds(n * chunks, chunks), :]
                dh = flows[n] + dy * scalar_ref[t, c_at(n, eighth)]
                flow = jnp.exp2(sp * rate) * dh
                out_flows.append(flow)
                q = flow * h_ref[aligned((t * states + n) * chunks, chunks), :]
                out_totals.append(totals[n] + q * sp)
                d_term = q * rate
                s_term = dh * scalar_ref[t, b_at(n, eighth)]
                d_sum = d_term if d_sum is None else d_sum + d_term
                s_sum = s_term if s_sum is None else s_sum + s_term
                terms_ref[slot, pl.ds(n * chunks, chunks), :] = dh * u
            s_ref[span, :] = s_sum
            d_ref[span, :] = d_sum
            sums_b_ref[aligned(t * states, states), :] = reduce_terms(
                terms_ref, slot, states, chunks
            )
            flows, totals = tuple(out_flows), tuple(out_totals)
        return flows, totals

    _, totals = lax.fori_loop(0, count // 2, retreat, (zero, zero))
    for n in range(states):
        alog_ref[pl.ds(n * chunks, chunks), :] = totals[n]

    rank = rank_ref[...]
    ranks = rank.shape[1]
    drank = None
    for chunk in range(chunks):
        cols = slice(chunk * LANES, (chunk + 1) * LANES)
        place = pl.ds(chunk * count, count)
        act = act_ref[:, cols].astype(F32)
        weight = dt_ref[:, lanes(2 * chunk + half)]
        pre = dot(rank, weight, 1, 0) + bias_ref[pl.ds(2 * chunk + half, 1), :]
        s_now = s_ref[place, :]
        dstep = d_ref[place, :] * (1.0 / LOG2E) + s_now * act
        sact_ref[:, cols] = s_now * softplus(pre)
        dpre = dstep * sigmoid(pre)
        vec_ref[0:1, cols] = jnp.sum(dpre, axis=0, keepdims=True)
        vec_ref[1:2, cols] = jnp.sum(dy_ref[place, :] * act, axis=0, keepdims=True)
        low = dpre.astype(BF16)
        dpre_ref[:, cols] = low
        term = dot(low, weight, 1, 1)
        drank = term if drank is None else drank + term
    source = lax.broadcasted_iota(jnp.int32, (2 * LANES, LANES), 0)
    target = lax.broadcasted_iota(jnp.int32, (2 * LANES, LANES), 1)
    code = None
    for n in range(states):
        pair = jnp.concatenate(
            [ref[pl.ds(n, count, stride=states), :] for ref in (sums_b_ref, sums_c_ref)], axis=1
        )
        column = ranks + jnp.where(source < LANES, b_at(n, eighth), c_at(n, eighth))
        pick = jnp.where(target == column, 1.0, 0.0).astype(BF16)
        term = dot(pair.astype(BF16), pick, 1, 0)
        code = term if code is None else code + term
    code_ref[...] = code + jnp.concatenate([drank, jnp.zeros((count, LANES - ranks), F32)], axis=1)


def scan_backward(place, micro, count, bc, decay, rank, dt, bias, act, sp, u, dy, code):
    rows, own = act.shape
    chunks = own // LANES
    states = bc.shape[1] // 2
    ranks = rank.shape[1]
    outs = [
        ((rows, LANES), F32),
        ((count, own), F32),
        ((count, own), BF16),
        ((states * chunks, LANES), F32),
        ((2, own), F32),
    ]

    def block(*shape):
        return pl.BlockSpec(shape, lambda i, p: (micro, 0))

    operands = (bc, decay, rank, dt, bias, act, sp, u, dy) + (() if code is None else (code,))
    return pl.pallas_call(
        functools.partial(backward_kernel, count=count, states=states, chunks=chunks),
        grid_spec=pltpu.PrefetchScalarGridSpec(
            num_scalar_prefetch=1,
            grid=(1,),
            in_specs=[
                block(count, 2 * states),
                whole(decay.shape),
                block(count, ranks),
                whole(dt.shape),
                whole(bias.shape),
                block(count, own),
                block(chunks * count, LANES),
                block(chunks * count, LANES),
                block(chunks * count, LANES),
            ]
            + [ANY] * (code is not None),
            out_specs=[block(count, LANES)] + [whole(shape) for shape, _ in outs[1:]],
            scratch_shapes=[
                pltpu.VMEM(((count + 1) * states * chunks, LANES), F32),
                pltpu.VMEM((chunks * count, LANES), F32),
                pltpu.VMEM((chunks * count, LANES), F32),
                pltpu.VMEM((2, states * chunks, LANES), F32),
                pltpu.VMEM((count * states, LANES), F32),
                pltpu.VMEM((count * states, LANES), F32),
                pltpu.SMEM((count, 2 * states), F32),
                pltpu.SemaphoreType.DMA,
            ],
        ),
        out_shape=[hbm(*out) for out in outs],
        input_output_aliases={} if code is None else {len(operands): 0},
        compiler_params=params(26),
        cost_estimate=cost(0),
        name="scan_backward",
    )(place, *in_hbm(operands))


def tail_kernel(
    place_ref,
    len_ref,
    *refs,
    micros,
    count,
    taps,
    clusters,
    ranks,
    chunks,
    states,
):
    def take(number):
        nonlocal refs
        taken, refs = refs[:number], refs[number:]
        return taken

    code_own_ref, code_other_ref = take(2)
    sact_refs, dpre_refs, alog_refs, back_refs = (take(micros) for _ in range(4))
    dtx_ref, bc_own_ref, bc_other_ref, decay_ref = take(4)
    dy_refs = take(micros)
    conved_ref, inner_ref, act_ref, high_ref, convw_ref, skip_ref = take(6)
    normed_ref, weight_ref, share_ref, gain_ref = take(4)
    keep_ref, send_ref, low_ref = take(3)
    mask_ref, code_ref, wcode_ref, vec_ref, alog_ref, total_ref, win_ref, sems = refs

    step = pl.program_id(0)
    rows = micros * count
    eighth = states // 2
    edge = LANES // 2
    half, core, cube, face = (place_ref[k] for k in range(4))
    pair = step ^ face
    span = LANES + 32

    def fetch(k):
        source = weight_ref.at[0, pl.ds(2 * (k ^ face), 2), half]
        return (pltpu.make_async_copy(source, win_ref.at[k], sems.at[k]),)

    stream(step, win_ref.shape[0], fetch)

    def pack_row(chunk):
        relative = chunk ^ cube
        return (relative & 3) * span + LANES + (relative >> 2) * 16

    def place_pair(start, size, cols, even, odd):
        keep_ref[aligned(start, size, 16), cols] = jnp.where(core == 0, even, odd).astype(BF16)
        send_ref[aligned(start, size, 16), cols] = jnp.where(core == 0, odd, even).astype(BF16)

    @pl.when(step == 0)
    def _():
        fill_masks(len_ref, mask_ref, micros, count, taps, clusters)
        total_ref[...] = share_ref[...]
        code_ref[...] = (code_own_ref[...] + code_other_ref[...]).astype(BF16)
        total = None
        for micro in range(micros):
            term = alog_refs[micro][...]
            total = term if total is None else total + term
        alog_ref[...] = total * (decay_ref[...] * (1.0 / LOG2E))

    code = code_ref[...]
    lane = lax.broadcasted_iota(jnp.int32, (1, LANES), 1)
    code_rank = jnp.where(lane < ranks, code, jnp.zeros_like(code))
    dpre = jnp.concatenate([ref[...] for ref in dpre_refs], axis=0)
    for part in range(2):
        source = lanes(2 * (2 * pair + part) + half)
        cols = slice(part * LANES, (part + 1) * LANES)
        wcode_ref[:ranks, cols] = dtx_ref[:, source]
        own = bc_own_ref[:, :, source].reshape(states, LANES)
        other = bc_other_ref[:, :, source].reshape(states, LANES)
        wcode_ref[ranks : ranks + states, cols] = jnp.where(half == 0, own, other)
        wcode_ref[ranks + states : ranks + 2 * states, cols] = jnp.where(half == 0, other, own)
        wcode_ref[ranks + 2 * states :, cols] = jnp.zeros(
            (LANES - ranks - 2 * states, LANES), BF16
        )
    for part in range(2):
        cols = slice(part * LANES, (part + 1) * LANES)
        chunk = 2 * pair + part
        source = 2 * chunk + half
        weights = convw_ref[:, lanes(source)]
        sact = jnp.concatenate([ref[:, cols] for ref in sact_refs], axis=0)
        dy = jnp.concatenate([ref[pl.ds(part * count, count), :] for ref in dy_refs], axis=0)
        dact = sact + dot(code, wcode_ref[:, cols], 1, 0)
        dact = dact + dy * skip_ref[pl.ds(source, 1), :]
        conved = conved_ref[:, cols]
        sig = sigmoid(conved)
        dconv = dact * (sig * (1.0 + conved * (1.0 - sig)))
        inner = inner_ref[:, cols]
        dinner = weights[taps - 1 : taps] * dconv
        sums = [None] * (taps + 1)
        sums[taps - 1] = jnp.sum(dconv * inner, axis=0, keepdims=True)
        sums[taps] = jnp.sum(dconv, axis=0, keepdims=True)
        for back in range(1, taps):
            kept = dconv * mask_ref[back]
            dinner = dinner + weights[taps - 1 - back : taps - back] * pltpu.roll(
                kept, rows - back, 0
            )
            sums[taps - 1 - back] = jnp.sum(
                kept * pltpu.roll(inner, back, 0), axis=0, keepdims=True
            )
        for k in range(taps + 1):
            vec_ref[k : k + 1, lanes(chunk)] = sums[k]
        for k in range(2):
            total = None
            for ref in back_refs:
                term = ref[k : k + 1, lanes(chunk)]
                total = term if total is None else total + term
            vec_ref[taps + 1 + k : taps + 2 + k, lanes(chunk)] = total
        low_ref[:, cols] = dinner.astype(BF16)

        act = act_ref[:, cols]
        start = pack_row(chunk)
        rows_now = dot(act, code_rank, 0, 0) + dot(dpre[:, cols], high_ref[...], 0, 0)
        for k in range(4):
            place_pair(
                start,
                16,
                slice(k * LANES, (k + 1) * LANES),
                rows_now[k * 16 : (k + 1) * 16],
                rows_now[edge + k * 16 : edge + (k + 1) * 16],
            )
        state_rows = dot(code, act, 0, 0)[ranks : ranks + 2 * states]
        place_pair(
            start, 16, slice(4 * LANES, 5 * LANES), state_rows[:states], state_rows[states:]
        )

    normed = normed_ref[...]
    for part in range(2):
        grad = dot(low_ref[:, lanes(core ^ part)], normed, 0, 0)
        total_ref[...] += eight_rows(grad * win_ref[step, core ^ part].astype(F32))
        out_ref = (keep_ref, send_ref)[part]
        out_ref[aligned(step * span, LANES, 16), :] = grad.astype(BF16)

    @pl.when(step == pl.num_programs(0) - 1)
    def _():
        vec_ref[taps + 3 : taps + 4, :] = (
            jnp.sum(total_ref[...], axis=0, keepdims=True) / gain_ref[...]
        )
        is_gain = lax.broadcasted_iota(jnp.int32, (8, LANES), 0) == taps + 3
        for chunk in range(chunks):
            start = pack_row(chunk)
            vec = vec_ref[:, chunk * LANES : (chunk + 1) * LANES]
            far, farther = (pltpu.roll(vec, LANES - k * edge // 2, 1) for k in (1, 2))
            even = jnp.where(is_gain & (lane >= edge // 2), far, vec)
            odd = jnp.where(is_gain & (lane < edge // 2), far, farther)
            alog = [
                alog_ref[pl.ds(q * eighth * chunks + chunk, eighth, stride=chunks), :]
                for q in range(2)
            ]
            place_pair(
                start,
                16,
                slice(5 * LANES, 6 * LANES),
                jnp.concatenate([alog[0], even]),
                jnp.concatenate([alog[1], odd]),
            )
            blank = jnp.zeros((16, 2 * LANES), F32)
            place_pair(start, 16, slice(6 * LANES, 8 * LANES), blank, blank)


def tail(
    place,
    lengths,
    code_own,
    code_other,
    sact,
    dpre,
    alog,
    back,
    dtx,
    bc_own,
    bc_other,
    decay,
    dy,
    conved,
    inner,
    act,
    high,
    convw,
    skip,
    normed,
    w4,
    share,
    gain,
):
    rows, own = act.shape
    chunks = own // LANES
    width = normed.shape[1]
    micros, _, clusters = lengths.shape
    count = rows // micros
    taps = convw.shape[0]
    ranks = dtx.shape[0]
    states = decay.shape[0] // chunks
    cols = 2 * LANES
    extent = 4 * (LANES + 32)

    def by_cols(height):
        return pl.BlockSpec((height, cols), lambda i, p: (0, i ^ p[FACE]))

    def dy_spec(micro):
        return pl.BlockSpec(
            (2 * count, LANES), lambda i, p: (micro * (chunks // 2) + (i ^ p[FACE]), 0)
        )

    in_specs = (
        [pl.BlockSpec(memory_space=pltpu.SMEM)]
        + [whole((rows, LANES))] * 2
        + [by_cols(count)] * (2 * micros)
        + [whole(alog[0].shape)] * micros
        + [whole(back[0].shape)] * micros
        + [whole(array.shape) for array in (dtx, bc_own, bc_other, decay)]
        + [dy_spec(micro) for micro in range(micros)]
        + [by_cols(rows)] * 3
        + [whole(array.shape) for array in (high, convw, skip, normed)]
        + [
            ANY,
            whole(share.shape),
            whole(gain.shape),
        ]
    )
    return pl.pallas_call(
        functools.partial(
            tail_kernel,
            micros=micros,
            count=count,
            taps=taps,
            clusters=clusters,
            ranks=ranks,
            chunks=chunks,
            states=states,
        ),
        grid_spec=pltpu.PrefetchScalarGridSpec(
            num_scalar_prefetch=1,
            grid=(chunks // 2,),
            in_specs=in_specs,
            out_specs=[
                whole((extent, width)),
                whole((extent, width)),
                pl.BlockSpec((rows, cols), lambda i, p: (0, i ^ p[FACE])),
            ],
            scratch_shapes=[
                pltpu.VMEM((taps, rows, LANES), F32),
                pltpu.VMEM((rows, LANES), BF16),
                pltpu.VMEM((LANES, cols), BF16),
                pltpu.VMEM((8, own), F32),
                pltpu.VMEM((states * chunks, LANES), F32),
                pltpu.VMEM((8, width), F32),
                pltpu.VMEM((chunks // 2, 2, LANES, width), BF16),
                pltpu.SemaphoreType.DMA((chunks // 2,)),
            ],
        ),
        out_shape=[
            hbm((extent, width), BF16),
            hbm((extent, width), BF16),
            hbm((rows, own), BF16),
        ],
        compiler_params=params(30),
        cost_estimate=cost(7),
        name="tail",
    )(
        place,
        lengths,
        *in_hbm([code_own]),
        code_other,
        *in_hbm(
            (
                *sact,
                *dpre,
                *alog,
                *back,
                dtx,
                bc_own,
                bc_other,
                decay,
                *([dy] * micros),
                conved,
                inner,
                act,
                high,
                convw,
                skip,
                normed,
                w4,
                share,
                gain,
            )
        ),
    )


def products_kernel(
    place_ref,
    gated_ref,
    dgate_ref,
    out_ref,
    weight_ref,
    mixed_ref,
    dnormed_ref,
    total_ref,
    wout_ref,
    wgate_ref,
    sems,
):
    step = pl.program_id(0)
    half = place_ref[HALF]

    def fetch(k):
        pair = pl.ds(2 * k, 2)
        return (
            pltpu.make_async_copy(out_ref.at[pair, half], wout_ref.at[k], sems.at[0, k]),
            pltpu.make_async_copy(weight_ref.at[1, pair, half], wgate_ref.at[k], sems.at[1, k]),
        )

    stream(step, wout_ref.shape[0], fetch)
    width = total_ref.shape[1]

    @pl.when(step == 0)
    def _():
        total_ref[...] = jnp.zeros_like(total_ref)
        dnormed_ref[...] = jnp.zeros_like(dnormed_ref)

    total_ref[...] += dot(gated_ref[...], wout_ref[step].reshape(-1, width), 1, 0)
    dnormed_ref[...] += dot(dgate_ref[...], wgate_ref[step].reshape(-1, width), 1, 0)

    @pl.when(step == pl.num_programs(0) - 1)
    def _():
        mixed_ref[...] = total_ref[...].astype(BF16)


def products(place, gated, dgate, wout3, w4):
    rows, own = gated.shape
    width = w4.shape[-1]
    pairs = own // (2 * LANES)
    by_cols = pl.BlockSpec((rows, 2 * LANES), lambda i, p: (0, i))
    return pl.pallas_call(
        products_kernel,
        grid_spec=pltpu.PrefetchScalarGridSpec(
            num_scalar_prefetch=1,
            grid=(pairs,),
            in_specs=[by_cols, by_cols, ANY, ANY],
            out_specs=[whole((rows, width))] * 2,
            scratch_shapes=[
                pltpu.VMEM((rows, width), F32),
                pltpu.VMEM((pairs, 2, LANES, width), BF16),
                pltpu.VMEM((pairs, 2, LANES, width), BF16),
                pltpu.SemaphoreType.DMA((2, pairs)),
            ],
        ),
        out_shape=[hbm((rows, width), BF16), hbm((rows, width), F32)],
        compiler_params=params(16),
        cost_estimate=cost(4),
        name="products",
    )(place, *in_hbm((gated, dgate, wout3, w4)))


def spread_kernel(
    place_ref, low_ref, weight_ref, gate_ref, dnormed_ref, total_ref, win_ref, sems
):
    step = pl.program_id(0)

    def fetch(k):
        return (
            pltpu.make_async_copy(
                weight_ref.at[0, pl.ds(2 * k, 2), place_ref[HALF]], win_ref.at[k], sems.at[k]
            ),
        )

    stream(step, win_ref.shape[0], fetch)
    width = total_ref.shape[1]

    @pl.when(step == 0)
    def _():
        total_ref[...] = gate_ref[...]

    total_ref[...] += dot(low_ref[...], win_ref[step].reshape(-1, width), 1, 0)

    @pl.when(step == pl.num_programs(0) - 1)
    def _():
        dnormed_ref[...] = total_ref[...].astype(BF16)


def spread(place, low, w4, gate_part):
    rows, own = low.shape
    pairs = own // (2 * LANES)
    width = w4.shape[-1]
    return pl.pallas_call(
        spread_kernel,
        grid_spec=pltpu.PrefetchScalarGridSpec(
            num_scalar_prefetch=1,
            grid=(pairs,),
            in_specs=[
                pl.BlockSpec((rows, 2 * LANES), lambda i, p: (0, i)),
                ANY,
                whole((rows, width)),
            ],
            out_specs=whole((rows, width)),
            scratch_shapes=[
                pltpu.VMEM((rows, width), F32),
                pltpu.VMEM((pairs, 2, LANES, width), BF16),
                pltpu.SemaphoreType.DMA((pairs,)),
            ],
        ),
        out_shape=hbm((rows, width), BF16),
        compiler_params=params(16),
        cost_estimate=cost(0),
        name="spread",
    )(place, *in_hbm((low, w4, gate_part)))


def finish_kernel(x_ref, mine_ref, theirs_ref, cotan_ref, gain_ref, grad_ref):
    x = x_ref[...].astype(F32)
    scale = lax.rsqrt(jnp.mean(x * x, axis=1, keepdims=True) + EPSILON)
    unit = x * scale
    dhat = (mine_ref[...].astype(F32) + theirs_ref[...].astype(F32)) * gain_ref[...]
    grad_ref[...] = cotan_ref[...].astype(F32) + scale * (
        dhat - unit * jnp.mean(dhat * unit, axis=1, keepdims=True)
    )


def finish(x, mine, theirs, cotan, gain):
    rows, width = x.shape
    by_rows = pl.BlockSpec((rows // 4, width), lambda i: (i, 0))
    return pl.pallas_call(
        finish_kernel,
        grid=(4,),
        in_specs=[by_rows] * 4 + [whole(gain.shape)],
        out_specs=by_rows,
        out_shape=jax.ShapeDtypeStruct((rows, width), F32),
        compiler_params=params(16),
        cost_estimate=cost(0),
        name="finish",
    )(*in_hbm((x, mine)), theirs, *in_hbm((cotan, gain)))


def unpack_kernel(
    place_ref,
    pack_near_ref,
    pack_far_ref,
    *refs,
    eighth,
    taps,
    edge,
):
    gain_mine_ref, gain_theirs_ref, out_ref, *refs = refs
    dtx_ref, dt_ref, bc_ref, alog_ref, convw_ref, convb_ref = refs[:6]
    bias_ref, skip_ref, gain_ref, out_grad_ref = refs[6:]
    pack = pack_near_ref[...].astype(F32) + pack_far_ref[...].astype(F32)
    for k in range(4):
        rows = pack[:, k * LANES : (k + 1) * LANES]
        dtx_ref[pl.ds(16 * k, 16), :] = rows[:, :edge]
        dt_ref[pl.ds(16 * k, 16), :] = pltpu.roll(rows, edge, 1)[:, :edge]
    rows = pack[:, 4 * LANES : 5 * LANES]
    bc_ref[0] = rows[:eighth]
    bc_ref[1] = rows[eighth:]
    rows = pack[:, 5 * LANES : 6 * LANES]
    alog_ref[...] = rows[:eighth]
    vec = rows[eighth:, :edge]
    convw_ref[...] = vec[:taps]
    convb_ref[...] = vec[taps : taps + 1]
    bias_ref[...] = vec[taps + 1 : taps + 2]
    skip_ref[...] = vec[taps + 2 : taps + 3]
    gain = gain_mine_ref[...].astype(F32) + gain_theirs_ref[...].astype(F32)
    gain = jnp.where(place_ref[CORE] == 0, gain, pltpu.roll(gain, LANES - edge // 2, 1))
    gain_ref[...] = gain[15:16, : edge // 2]
    out_grad_ref[...] = out_ref[...].astype(F32)


def unpack(place, packs, gains, out, eighth, taps, ranks):
    edge = LANES // 2
    shapes = [
        (edge, ranks),
        (edge, ranks),
        (2, eighth, LANES),
        (eighth, LANES),
        (taps, edge),
        (1, edge),
        (1, edge),
        (1, edge),
        (1, edge // 2),
        out.shape,
    ]
    return pl.pallas_call(
        functools.partial(unpack_kernel, eighth=eighth, taps=taps, edge=edge),
        grid_spec=pltpu.PrefetchScalarGridSpec(
            num_scalar_prefetch=1,
            grid=(1,),
            in_specs=[whole(array.shape) for array in (*packs, *gains, out)],
            out_specs=[whole(shape) for shape in shapes],
        ),
        out_shape=[jax.ShapeDtypeStruct(shape, F32) for shape in shapes],
        cost_estimate=cost(0),
        name="unpack",
    )(place, *packs, *gains, out)


def swap_pair(array):
    count = lax.axis_size("state")
    return lax.ppermute(array, "state", [(pos, pos ^ 1) for pos in range(count)])


def swap_bit(array, bits):
    return lax.ppermute(array, "dp", [(pos, pos ^ bits) for pos in range(lax.axis_size("dp"))])


def swap_both(array, bits=0):
    states = lax.axis_size("state")
    pairs = []
    for d in range(lax.axis_size("dp")):
        for s in range(states):
            pairs.append((d * states + s, (((d & ~1) | s) ^ bits) * states + (d & 1)))
    return lax.ppermute(array, ("dp", "state"), pairs)


def add_quarters(kept, got):
    extent = kept.shape[0] // 4
    return [kept[k * extent :][:extent] + got[k * extent :][:extent] for k in range(4)]


def trade_quarters(quarters):
    return [quarters[0]] + [swap_bit(quarters[k], k * X_BIT) for k in range(1, 4)]


def sum_quarters(quarters):
    left, right = (quarters[k].astype(F32) + quarters[k + 1].astype(F32) for k in (0, 2))
    return (left + right).astype(BF16)


CORE_BIT, X_BIT, ZH_BIT = 1, 2, 8


def shards(
    tokens,
    cluster_len,
    norm_gain,
    in_weight,
    conv_weight,
    conv_bias,
    dtx_weight,
    dt_weight,
    dt_bias,
    bc_weight,
    a_log,
    skip_gain,
    out_weight,
    cotangent,
):
    micros, count, width = tokens.shape
    inner = out_weight.shape[0]
    taps = conv_weight.shape[0]
    ranks = dtx_weight.shape[1]
    chunks = inner // (2 * LANES)
    own = chunks * LANES
    rows = micros * count
    edge = LANES // 2
    span = LANES + 32
    dp_parts = lax.axis_size("dp")
    state_count = lax.axis_size("state")
    dp_pos = lax.axis_index("dp")
    state_pos = lax.axis_index("state")
    half = state_pos & 1
    fast = state_count == 2 and dp_parts == 2 * chunks == 16
    if fast:
        place = jnp.stack([half, dp_pos & 1, dp_pos >> 1, (dp_pos >> 1) & 3])
        bc_own, alog_own = bc_weight, a_log
        bc_other, alog_other = swap_pair(bc_weight), swap_pair(a_log)
    else:
        place = jnp.stack([half, 0, 0, 0])
        bc_all = lax.all_gather(bc_weight, "state", axis=1, tiled=True)
        alog_all = lax.all_gather(a_log, "state", axis=0, tiled=True)
        eighth = alog_all.shape[0] // 2
        bc_own, bc_other = (
            lax.dynamic_slice_in_dim(bc_all, which * eighth, eighth, 1)
            for which in (half, 1 - half)
        )
        alog_own, alog_other = (
            lax.dynamic_slice_in_dim(alog_all, which * eighth, eighth, 0)
            for which in (half, 1 - half)
        )
    place = place.astype(jnp.int32)
    eighth = alog_own.shape[0]
    states = 2 * eighth

    x = tokens.reshape(rows, width)
    cotan = cotangent.reshape(rows, width)
    w4 = in_weight.reshape(2, chunks, 2, LANES, width)
    wout3 = out_weight.reshape(chunks, 2, LANES, width)
    dtx, dt = dtx_weight.T, dt_weight.T
    bias = dt_bias.reshape(-1, LANES)
    skip = skip_gain.reshape(-1, LANES)

    normed, act_all, act, inner_own, conved, gate = project(
        place, cluster_len, x, norm_gain[None], w4, conv_weight, conv_bias.reshape(-1, LANES)
    )
    bc, rank, high, decay, sp, u, dy, gated, dgate, keep, send, share = scan_forward(
        place,
        cluster_len,
        act_all,
        bc_own,
        bc_other,
        alog_own,
        alog_other,
        dtx,
        dt,
        bias,
        skip,
        act,
        gate,
        wout3,
        cotan,
        normed,
        w4,
    )
    if fast:
        early = swap_bit(send, CORE_BIT)
    mixed_part, dn_gate = products(place, gated, dgate, wout3, w4)
    if fast:
        *quarters, mixed_part, dn_gate, sp = lax.optimization_barrier(
            (*add_quarters(keep, early), mixed_part, dn_gate, sp)
        )
        early_got = trade_quarters(quarters)
    mixed_other = swap_pair(mixed_part)
    code_own = None
    results = []
    for micro in range(micros):
        code_own, *rest = scan_backward(
            place, micro, count, bc, decay, rank, dt, bias, act, sp, u, dy, code_own
        )
        results.append(rest)
    sact, dpre, alog, back = zip(*results)
    code_other = swap_pair(code_own)
    if fast:
        *early_got, mixed_other, conved = lax.optimization_barrier(
            (*early_got, mixed_other, conved)
        )
    late_keep, late_send, low = tail(
        place,
        cluster_len,
        code_own,
        code_other,
        sact,
        dpre,
        alog,
        back,
        dtx,
        bc_own,
        bc_other,
        decay,
        dy,
        conved,
        inner_own,
        act,
        high,
        conv_weight,
        skip,
        normed,
        w4,
        share,
        norm_gain[None],
    )
    if fast:
        late = swap_bit(late_send, CORE_BIT)
        block = sum_quarters(early_got)
        out_keep, out_send, gate_sum = block[:edge], block[edge:LANES], block[LANES:]
        out_send, gate_sum, low = lax.optimization_barrier((out_send, gate_sum, low))
        out_got = swap_bit(out_send, ZH_BIT)
        *quarters, low = lax.optimization_barrier((*add_quarters(late_keep, late), low))
        late_got = trade_quarters(quarters)
    dnormed_part = spread(place, low, w4, dn_gate)
    dnormed_other = swap_pair(dnormed_part)
    mixed = (x.astype(F32) + (mixed_part.astype(F32) + mixed_other.astype(F32))).astype(BF16)
    if fast:
        *late_got, mixed = lax.optimization_barrier((*late_got, mixed))
        out_own = swap_both(out_keep + out_got)
        block = sum_quarters(late_got)
        inner_sum = block[:LANES]
        pack_far = swap_both(block[-16:], ZH_BIT)
        pack_near = swap_both(block[LANES:-16])
        upper = dp_pos >= dp_parts // 2
        half_got = swap_bit(jnp.where(upper, inner_sum, gate_sum), ZH_BIT)
        gain_mine = (
            pack_near[:, 5 * LANES : 6 * LANES].astype(F32)
            + pack_far[:, 5 * LANES : 6 * LANES].astype(F32)
        ).astype(BF16)
        gains = (gain_mine, swap_bit(gain_mine, CORE_BIT))
        (
            dtx_grad,
            dt_grad,
            bc_grad,
            alog_grad,
            convw_grad,
            convb_grad,
            bias_grad,
            skip_grad,
            gain_grad,
            out_own,
        ) = unpack(
            place, (pack_near, pack_far), gains, out_own, eighth, taps, ranks
        )
        convb_grad, bias_grad, skip_grad, gain_grad = (
            array[0] for array in (convb_grad, bias_grad, skip_grad, gain_grad)
        )
        in_grad = jnp.where(upper, gate_sum, inner_sum).astype(F32) + half_got.astype(F32)
        _, dnormed_other = lax.optimization_barrier((inner_sum, dnormed_other))
    tokens_grad = finish(x, dnormed_part, dnormed_other, cotan, norm_gain[None])
    mixed = mixed.reshape(micros, count, width)
    tokens_grad = tokens_grad.reshape(micros, count, width)

    if not fast:
        def total(array):
            return lax.psum(array.astype(F32), "dp")

        def both_rows(array):
            mine = array.reshape(chunks, 1, LANES, -1)
            other = swap_pair(mine)
            low = jnp.where(half == 0, mine, other)
            high = jnp.where(half == 0, other, mine)
            return jnp.concatenate([low, high], axis=1).reshape(2 * own, -1)

        every = dp_parts * state_count
        at = dp_pos * state_count + state_pos

        def cut_own(array):
            extent = array.shape[0] // every
            return lax.dynamic_slice_in_dim(array, at * extent, extent, 0)

        pair = total(jnp.stack([keep, send])).reshape(2, 2, 2, 2 * LANES, width)
        outs = pair[:, :, :, :LANES].reshape(2, 2, 2, 2, edge, width)
        outs = jnp.transpose(outs, (3, 1, 2, 0, 4, 5)).reshape(own, width)
        gates = jnp.moveaxis(pair[:, :, :, LANES:], 0, 2).reshape(own, width)
        pair = total(jnp.stack([late_keep, late_send])).reshape(2, 2, 2, span, width)
        inners = jnp.moveaxis(pair[:, :, :, :LANES], 0, 2).reshape(own, width)
        packs = pair[:, :, :, LANES:].reshape(2, 2, 2, 2, 16, width // LANES, LANES)
        packs = jnp.transpose(packs, (3, 1, 2, 0, 5, 4, 6)).reshape(chunks, 2, -1, 16, LANES)
        small = both_rows(packs[:, :, :4].reshape(own, LANES))
        in_grad = cut_own(jnp.concatenate([both_rows(inners), both_rows(gates)]))
        out_own = cut_own(both_rows(outs))
        mine = cut_own(small)
        dtx_grad, dt_grad = mine[:, :ranks], mine[:, ranks:]
        vec_rows = jnp.swapaxes(packs[:, :, 5, eighth:, :edge], 2, 3).reshape(own, -1)
        gain_sum = vec_rows[:, -1].reshape(chunks, 2, 2, -1).swapaxes(1, 2).reshape(-1)
        gain_grad = cut_own(gain_sum + swap_pair(gain_sum))
        vec = cut_own(both_rows(vec_rows)).T
        state_rows = jnp.concatenate([packs[:, :, 4], packs[:, :, 5, :eighth]], axis=2)
        state_rows = state_rows.reshape(chunks, 2, 3, eighth, LANES)
        state_rows = jnp.transpose(state_rows, (0, 4, 2, 1, 3)).reshape(own, -1)
        extent = inner // dp_parts
        state_part = lax.dynamic_slice_in_dim(both_rows(state_rows), dp_pos * extent, extent, 0)
        state_part = state_part.T.reshape(3, state_count, -1, extent)
        state_part = lax.dynamic_index_in_dim(state_part, state_pos, 1, keepdims=False)
        bc_grad, alog_grad = state_part[:2], state_part[2]
        convw_grad, convb_grad, bias_grad, skip_grad = (
            vec[:taps], vec[taps], vec[taps + 1], vec[taps + 2]
        )

    return (
        mixed,
        tokens_grad,
        gain_grad,
        in_grad,
        convw_grad,
        convb_grad,
        dtx_grad,
        dt_grad,
        bias_grad,
        bc_grad,
        alog_grad,
        skip_grad,
        out_own,
    )


def solution(mesh):
    return jax.shard_map(
        shards,
        mesh=mesh,
        in_specs=(
            P(None, "dp", None),
            P(None, "dp", None),
            P(),
            P(),
            P(),
            P(),
            P(),
            P(),
            P(),
            P(None, "state", None),
            P("state", None),
            P(),
            P(),
            P(None, "dp", None),
        ),
        out_specs=(
            P(None, "dp", None),
            P(None, "dp", None),
            P(("dp", "state")),
            P(("dp", "state"), None),
            P(None, ("dp", "state")),
            P(("dp", "state")),
            P(("dp", "state"), None),
            P(("dp", "state"), None),
            P(("dp", "state")),
            P(None, "state", "dp"),
            P("state", "dp"),
            P(("dp", "state")),
            P(("dp", "state"), None),
        ),
        check_vma=False,
    )
```

```python
import functools
import math

import jax
import jax.numpy as jnp
from jax import lax
from jax.experimental import pallas as pl
from jax.experimental.pallas import tpu as pltpu
from jax.sharding import PartitionSpec as P

EPSILON = 1e-05
LANES = 128
RESET = 1e4
LOG2E = math.log2(math.e)
F32 = jnp.float32
BF16 = jnp.bfloat16
MIB = 1024 * 1024


def dot(left, right, left_dim, right_dim):
    return lax.dot_general(
        left, right, (((left_dim,), (right_dim,)), ((), ())), preferred_element_type=F32
    )


def params(mib):
    return pltpu.CompilerParams(
        vmem_limit_bytes=mib * MIB, dimension_semantics=("arbitrary",)
    )


ANY = pl.BlockSpec(memory_space=pl.ANY)


def stream(step, steps, fetch):
    @pl.when(step == 0)
    def _():
        for k in range(steps):
            for copy in fetch(k):
                copy.start()

    for copy in fetch(step):
        copy.wait()


def whole(shape):
    return pl.BlockSpec(shape, lambda *_: (0,) * len(shape))


sigmoid = jax.nn.sigmoid


def softplus(value):
    return jnp.maximum(value, 0.0) + jnp.log1p(jnp.exp(-jnp.abs(value)))


def lanes(index):
    return pl.ds(pl.multiple_of(index * LANES, LANES), LANES)


def cost(micros):
    return pl.CostEstimate(
        flops=int(micros * 1e9), bytes_accessed=int(micros * 1e6), transcendentals=0
    )


def hbm(shape, dtype):
    return pltpu.HBM(shape, dtype)


def in_hbm(arrays):
    return [pltpu.with_memory_space_constraint(array, pltpu.HBM) for array in arrays]


def aligned(start, size, to=8):
    return pl.ds(pl.multiple_of(start, to), size)


HALF, CORE, CUBE, FACE = range(4)


def fill_masks(len_ref, mask_ref, micros, count, taps, clusters):
    place = lax.broadcasted_iota(jnp.int32, (count, LANES), 0)
    for micro in range(micros):
        rows = pl.ds(micro * count, count)
        for back in range(1, taps):
            apart = place < back
            start = 0
            for cluster in range(clusters - 1):
                start = start + len_ref[micro, 0, cluster]
                apart = apart | ((place >= start) & (place < start + back))
            mask_ref[back, rows, :] = jnp.where(apart, 0.0, 1.0)
            if back == 1:
                mask_ref[0, rows, :] = jnp.where(apart, 1.0, 0.0)


def project_kernel(
    place_ref,
    len_ref,
    x_ref,
    gain_ref,
    weight_ref,
    convw_ref,
    convb_ref,
    normed_ref,
    act_ref,
    own_act_ref,
    inner_ref,
    conved_ref,
    gate_ref,
    mask_ref,
    proj_ref,
    conv_ref,
    win_ref,
    wgate_ref,
    sems,
    *,
    micros,
    count,
    taps,
    clusters,
):
    chunk = pl.program_id(0)

    @pl.when(chunk == 0)
    def _():
        fill_masks(len_ref, mask_ref, micros, count, taps, clusters)
        rows = x_ref[...].astype(F32)
        scale = lax.rsqrt(jnp.mean(rows * rows, axis=1, keepdims=True) + EPSILON)
        normed_ref[...] = (rows * scale * gain_ref[...]).astype(BF16)

    half = place_ref[HALF]

    def fetch(k):
        return (
            pltpu.make_async_copy(weight_ref.at[0, k], win_ref.at[k], sems.at[0, k]),
            pltpu.make_async_copy(weight_ref.at[1, k, half], wgate_ref.at[k], sems.at[1, k]),
        )

    stream(chunk, win_ref.shape[0], fetch)
    normed = normed_ref[...]
    proj_ref[...] = dot(normed, win_ref[chunk].reshape(2 * LANES, -1), 1, 1)
    gate_ref[...] = dot(normed, wgate_ref[chunk], 1, 1)
    for part in range(2):
        cols = pl.ds(part * LANES, LANES)
        inner = proj_ref[:, cols]
        conved = convb_ref[pl.ds(2 * chunk + part, 1), :] + convw_ref[taps - 1 : taps, cols] * inner
        for back in range(1, taps):
            shifted = pltpu.roll(inner, back, 0) * mask_ref[back]
            conved = conved + convw_ref[taps - 1 - back : taps - back, cols] * shifted
        conv_ref[:, cols] = conved
        act_ref[:, cols] = (conved * sigmoid(conved)).astype(BF16)
    own = lanes(half)
    inner_ref[...] = proj_ref[:, own]
    conved_ref[...] = conv_ref[:, own]
    own_act_ref[...] = act_ref[:, own]


def project(place, lengths, x, gain, w4, conv_weight, conv_bias):
    rows, width = x.shape
    chunks = w4.shape[1]
    inner = chunks * 2 * LANES
    micros, _, clusters = lengths.shape
    taps = conv_weight.shape[0]
    own = chunks * LANES
    by_chunk = pl.BlockSpec((rows, LANES), lambda i, p: (0, i))
    return pl.pallas_call(
        functools.partial(
            project_kernel, micros=micros, count=rows // micros, taps=taps, clusters=clusters
        ),
        grid_spec=pltpu.PrefetchScalarGridSpec(
            num_scalar_prefetch=1,
            grid=(chunks,),
            in_specs=[
                pl.BlockSpec(memory_space=pltpu.SMEM),
                whole((rows, width)),
                whole((1, width)),
                ANY,
                pl.BlockSpec((taps, 2 * LANES), lambda i, p: (0, i)),
                whole(conv_bias.shape),
            ],
            out_specs=[
                whole((rows, width)),
                pl.BlockSpec((rows, 2 * LANES), lambda i, p: (0, i)),
                by_chunk,
                by_chunk,
                by_chunk,
                by_chunk,
            ],
            scratch_shapes=[
                pltpu.VMEM((taps, rows, LANES), F32),
                pltpu.VMEM((rows, 2 * LANES), F32),
                pltpu.VMEM((rows, 2 * LANES), F32),
                pltpu.VMEM((chunks, 2, LANES, width), BF16),
                pltpu.VMEM((chunks, LANES, width), BF16),
                pltpu.SemaphoreType.DMA((2, chunks)),
            ],
        ),
        out_shape=[
            hbm((rows, width), BF16),
            hbm((rows, inner), BF16),
            hbm((rows, own), BF16),
            hbm((rows, own), F32),
            hbm((rows, own), F32),
            hbm((rows, own), F32),
        ],
        compiler_params=params(20),
        cost_estimate=cost(6),
        name="project",
    )(place, *in_hbm((lengths, x, gain, w4, conv_weight, conv_bias)))


def eight_rows(array):
    return jnp.sum(array.reshape(-1, 8, array.shape[1]), axis=0)


def b_at(n, eighth):
    return (n // eighth) * 2 * eighth + n % eighth


def c_at(n, eighth):
    return b_at(n, eighth) + eighth


def forward_kernel(
    place_ref,
    len_ref,
    act_all_ref,
    bc_own_ref,
    bc_other_ref,
    alog_own_ref,
    alog_other_ref,
    dtx_ref,
    dt_ref,
    bias_ref,
    skip_ref,
    act_ref,
    gate_ref,
    wout_ref,
    cotan_ref,
    normed_ref,
    wgate_ref,
    bc_ref,
    rank_ref,
    rank_high_ref,
    decay_ref,
    sp_ref,
    u_ref,
    dy_ref,
    gated_ref,
    dgate_ref,
    keep_ref,
    send_ref,
    share_ref,
    mask_ref,
    y_ref,
    tmp_ref,
    scalar_ref,
    sem,
    *,
    micros,
    count,
    states,
    chunks,
    clusters,
):
    rows = micros * count
    eighth = states // 2
    half, core, cube, face = (place_ref[k] for k in range(4))
    first = half == 0
    act_all = act_all_ref[...]
    own = dot(act_all, bc_own_ref[...].reshape(states, -1), 1, 1)
    other = dot(act_all, bc_other_ref[...].reshape(states, -1), 1, 1)
    bc_ref[:, :states] = jnp.where(first, own, other)
    bc_ref[:, states:] = jnp.where(first, other, own)
    copy = pltpu.make_async_copy(bc_ref, scalar_ref, sem)
    copy.start()

    fill_masks(len_ref, mask_ref, micros, count, 2, clusters)
    for chunk in range(chunks):
        cols = lanes(2 * chunk + half)
        own, other = alog_own_ref[:, cols], alog_other_ref[:, cols]
        tmp_ref[pl.ds(chunk * states, eighth), :] = jnp.where(first, own, other)
        tmp_ref[pl.ds(chunk * states + eighth, eighth), :] = jnp.where(first, other, own)
    for n in range(states):
        decay_ref[pl.ds(n * chunks, chunks), :] = -LOG2E * jnp.exp(
            tmp_ref[pl.ds(n, chunks, stride=states), :]
        )

    rank = dot(act_all, dtx_ref[...], 1, 1).astype(BF16)
    rank_ref[...] = rank
    rank_high_ref[...] = jnp.concatenate([jnp.zeros_like(rank), rank], axis=1)
    for chunk in range(chunks):
        cols = slice(chunk * LANES, (chunk + 1) * LANES)
        bias = bias_ref[pl.ds(2 * chunk + half, 1), :]
        step = softplus(dot(rank, dt_ref[:, lanes(2 * chunk + half)], 1, 0) + bias)
        held = step + RESET * mask_ref[0]
        source = step * act_ref[:, cols].astype(F32)
        for micro in range(micros):
            span = slice(micro * count, (micro + 1) * count)
            place = pl.ds((micro * chunks + chunk) * count, count)
            sp_ref[place, :] = held[span]
            u_ref[place, :] = source[span]
    copy.wait()

    for micro in range(micros):

        def advance(t, h, micro=micro):
            row = micro * count + t
            span = pl.ds(micro * chunks * count + t, chunks, stride=count)
            sp = sp_ref[span, :]
            u = u_ref[span, :]
            out = []
            y = None
            for n in range(states):
                decay = jnp.exp2(sp * decay_ref[pl.ds(n * chunks, chunks), :])
                now = decay * h[n] + u * scalar_ref[row, b_at(n, eighth)]
                out.append(now)
                term = now * scalar_ref[row, c_at(n, eighth)]
                y = term if y is None else y + term
            y_ref[span, :] = y
            return tuple(out)

        lax.fori_loop(0, count, advance, (jnp.zeros((chunks, LANES), F32),) * states, unroll=2)

    cotan = cotan_ref[...]
    for chunk in range(chunks):
        cols = slice(chunk * LANES, (chunk + 1) * LANES)
        places = [pl.ds((micro * chunks + chunk) * count, count) for micro in range(micros)]
        y = jnp.concatenate([y_ref[place, :] for place in places])
        y = y + skip_ref[pl.ds(2 * chunk + half, 1), :] * act_ref[:, cols].astype(F32)
        gate = gate_ref[:, cols]
        sig = sigmoid(gate)
        gated_ref[:, cols] = (y * (gate * sig)).astype(BF16)
        dgated = dot(cotan, wout_ref[chunk, 0], 1, 1)
        dy = dgated * (gate * sig)
        for micro in range(micros):
            dy_ref[places[micro], :] = dy[micro * count : (micro + 1) * count]
        dgate_ref[:, cols] = (dgated * y * (sig * (1.0 + gate * (1.0 - sig)))).astype(BF16)
    normed = normed_ref[...]
    edge = LANES // 2
    for j in range(chunks):
        grad = dot(gated_ref[:, lanes(j ^ cube)], cotan, 0, 0).astype(BF16)
        top, bottom = grad[:edge], grad[edge:]
        place = pl.ds((j & 3) * 2 * LANES + (j >> 2) * edge, edge)
        keep_ref[place, :] = jnp.where(core == 0, top, bottom)
        send_ref[place, :] = jnp.where(core == 0, bottom, top)
    share = jnp.zeros(share_ref.shape, F32)
    for j in range(chunks // 2):
        place = pl.ds((2 * j + 1) * LANES, LANES)
        pair = 2 * (j ^ face)
        for chunk, out_ref in ((pair + core, keep_ref), (pair + 1 - core, send_ref)):
            grad = dot(dgate_ref[:, lanes(chunk)], normed, 0, 0)
            share = share + eight_rows(grad * wgate_ref[0, chunk, 0].astype(F32))
            out_ref[place, :] = grad.astype(BF16)
    share_ref[...] = share


def scan_forward(
    place,
    lengths,
    act_all,
    bc_own,
    bc_other,
    alog_own,
    alog_other,
    dtx,
    dt,
    bias,
    skip,
    act,
    gate,
    wout3,
    cotan,
    normed,
    w4,
):
    rows, own = act.shape
    chunks = own // LANES
    states = 2 * alog_own.shape[0]
    width = cotan.shape[1]
    micros, _, clusters = lengths.shape
    ranks = dtx.shape[0]
    outs = [
        ((rows, 2 * states), F32),
        ((rows, ranks), BF16),
        ((rows, 2 * ranks), BF16),
        ((states * chunks, LANES), F32),
        ((chunks * rows, LANES), F32),
        ((chunks * rows, LANES), F32),
        ((chunks * rows, LANES), F32),
        ((rows, own), BF16),
        ((rows, own), BF16),
        ((own, width), BF16),
        ((own, width), BF16),
        ((8, width), F32),
    ]
    operands = (
        act_all, bc_own, bc_other, alog_own, alog_other, dtx, dt, bias, skip, act, gate
    )
    return pl.pallas_call(
        functools.partial(
            forward_kernel,
            micros=micros,
            count=rows // micros,
            states=states,
            chunks=chunks,
            clusters=clusters,
        ),
        grid_spec=pltpu.PrefetchScalarGridSpec(
            num_scalar_prefetch=1,
            grid=(1,),
            in_specs=[pl.BlockSpec(memory_space=pltpu.SMEM)]
            + [whole(operand.shape) for operand in operands]
            + [
                pl.BlockSpec((chunks, 1, LANES, width), lambda i, p: (0, p[HALF], 0, 0)),
                whole((rows, width)),
                whole((rows, width)),
                pl.BlockSpec((1, chunks, 1, LANES, width), lambda i, p: (1, 0, p[HALF], 0, 0)),
            ],
            out_specs=[whole(shape) for shape, _ in outs],
            scratch_shapes=[
                pltpu.VMEM((2, rows, LANES), F32),
                pltpu.VMEM((chunks * rows, LANES), F32),
                pltpu.VMEM((states * chunks, LANES), F32),
                pltpu.SMEM((rows, 2 * states), F32),
                pltpu.SemaphoreType.DMA,
            ],
        ),
        out_shape=[hbm(*out) for out in outs],
        compiler_params=params(48),
        cost_estimate=cost(19),
        name="scan_forward",
    )(
        place,
        lengths,
        *in_hbm(operands[:1]),
        *operands[1:5],
        *in_hbm((*operands[5:], wout3, cotan, normed, w4)),
    )


def sum_chunks(terms, chunks):
    count = len(terms)
    shape = (count, count * chunks)
    group = lax.broadcasted_iota(jnp.int32, shape, 1) // chunks
    pick = jnp.where(group == lax.broadcasted_iota(jnp.int32, shape, 0), 1.0, 0.0).astype(BF16)
    return dot(pick, jnp.concatenate(terms).astype(BF16), 1, 0)


def backward_kernel(
    place_ref,
    bc_ref,
    decay_ref,
    rank_ref,
    dt_ref,
    bias_ref,
    act_ref,
    sp_ref,
    u_ref,
    dy_ref,
    *refs,
    count,
    states,
    chunks,
):
    code_ref, sact_ref, dpre_ref, alog_ref, vec_ref = refs[-12:-7]
    h_ref, s_ref, d_ref, sums_b_ref, sums_c_ref, scalar_ref, sem = refs[-7:]
    copy = pltpu.make_async_copy(bc_ref, scalar_ref, sem)
    copy.start()
    half = place_ref[HALF]
    eighth = states // 2
    zero = (jnp.zeros((chunks, LANES), F32),) * states
    for n in range(states):
        h_ref[pl.ds(n * chunks, chunks), :] = zero[0]
    copy.wait()

    def recompute(pair, h):
        terms = []
        for slot in range(2):
            t = 2 * pair + slot
            span = pl.ds(t, chunks, stride=count)
            sp = sp_ref[span, :]
            u = u_ref[span, :]
            dy = dy_ref[span, :]
            out = []
            for n in range(states):
                decay = jnp.exp2(sp * decay_ref[pl.ds(n * chunks, chunks), :])
                now = decay * h[n] + u * scalar_ref[t, b_at(n, eighth)]
                h_ref[aligned(((t + 1) * states + n) * chunks, chunks), :] = now
                terms.append(dy * now)
                out.append(now)
            h = tuple(out)
        place = aligned(2 * pair * states, 2 * states)
        sums_c_ref[place, :] = sum_chunks(terms, chunks)
        return h

    lax.fori_loop(0, count // 2, recompute, zero)

    def retreat(back, carry):
        flows, totals = carry
        terms = []
        for slot in range(2):
            t = count - 1 - (2 * back + slot)
            span = pl.ds(t, chunks, stride=count)
            sp = sp_ref[span, :]
            u = u_ref[span, :]
            dy = dy_ref[span, :]
            out_flows = []
            out_totals = []
            out_terms = []
            d_sum = None
            s_sum = None
            for n in range(states):
                rate = decay_ref[pl.ds(n * chunks, chunks), :]
                dh = flows[n] + dy * scalar_ref[t, c_at(n, eighth)]
                flow = jnp.exp2(sp * rate) * dh
                out_flows.append(flow)
                q = flow * h_ref[aligned((t * states + n) * chunks, chunks), :]
                out_totals.append(totals[n] + q * sp)
                d_term = q * rate
                s_term = dh * scalar_ref[t, b_at(n, eighth)]
                d_sum = d_term if d_sum is None else d_sum + d_term
                s_sum = s_term if s_sum is None else s_sum + s_term
                out_terms.append(dh * u)
            s_ref[span, :] = s_sum
            d_ref[span, :] = d_sum
            terms = out_terms + terms
            flows, totals = tuple(out_flows), tuple(out_totals)
        place = aligned((count - 2 - 2 * back) * states, 2 * states)
        sums_b_ref[place, :] = sum_chunks(terms, chunks)
        return flows, totals

    _, totals = lax.fori_loop(0, count // 2, retreat, (zero, zero))
    for n in range(states):
        alog_ref[pl.ds(n * chunks, chunks), :] = totals[n]

    rank = rank_ref[...]
    ranks = rank.shape[1]
    drank = None
    for chunk in range(chunks):
        cols = slice(chunk * LANES, (chunk + 1) * LANES)
        place = pl.ds(chunk * count, count)
        act = act_ref[:, cols].astype(F32)
        weight = dt_ref[:, lanes(2 * chunk + half)]
        pre = dot(rank, weight, 1, 0) + bias_ref[pl.ds(2 * chunk + half, 1), :]
        s_now = s_ref[place, :]
        dstep = d_ref[place, :] * (1.0 / LOG2E) + s_now * act
        sact_ref[:, cols] = s_now * softplus(pre)
        dpre = dstep * sigmoid(pre)
        vec_ref[0:1, cols] = jnp.sum(dpre, axis=0, keepdims=True)
        vec_ref[1:2, cols] = jnp.sum(dy_ref[place, :] * act, axis=0, keepdims=True)
        low = dpre.astype(BF16)
        dpre_ref[:, cols] = low
        term = dot(low, weight, 1, 1)
        drank = term if drank is None else drank + term
    source = lax.broadcasted_iota(jnp.int32, (2 * LANES, LANES), 0)
    target = lax.broadcasted_iota(jnp.int32, (2 * LANES, LANES), 1)
    code = None
    for n in range(states):
        pair = jnp.concatenate(
            [ref[pl.ds(n, count, stride=states), :] for ref in (sums_b_ref, sums_c_ref)], axis=1
        )
        column = ranks + jnp.where(source < LANES, b_at(n, eighth), c_at(n, eighth))
        pick = jnp.where(target == column, 1.0, 0.0).astype(BF16)
        term = dot(pair.astype(BF16), pick, 1, 0)
        code = term if code is None else code + term
    code_ref[...] = code + jnp.concatenate([drank, jnp.zeros((count, LANES - ranks), F32)], axis=1)


def scan_backward(place, micro, count, bc, decay, rank, dt, bias, act, sp, u, dy, code):
    rows, own = act.shape
    chunks = own // LANES
    states = bc.shape[1] // 2
    ranks = rank.shape[1]
    outs = [
        ((rows, LANES), F32),
        ((count, own), F32),
        ((count, own), BF16),
        ((states * chunks, LANES), F32),
        ((2, own), F32),
    ]

    def block(*shape):
        return pl.BlockSpec(shape, lambda i, p: (micro, 0))

    operands = (bc, decay, rank, dt, bias, act, sp, u, dy) + (() if code is None else (code,))
    return pl.pallas_call(
        functools.partial(backward_kernel, count=count, states=states, chunks=chunks),
        grid_spec=pltpu.PrefetchScalarGridSpec(
            num_scalar_prefetch=1,
            grid=(1,),
            in_specs=[
                block(count, 2 * states),
                whole(decay.shape),
                block(count, ranks),
                whole(dt.shape),
                whole(bias.shape),
                block(count, own),
                block(chunks * count, LANES),
                block(chunks * count, LANES),
                block(chunks * count, LANES),
            ]
            + [ANY] * (code is not None),
            out_specs=[block(count, LANES)] + [whole(shape) for shape, _ in outs[1:]],
            scratch_shapes=[
                pltpu.VMEM(((count + 1) * states * chunks, LANES), F32),
                pltpu.VMEM((chunks * count, LANES), F32),
                pltpu.VMEM((chunks * count, LANES), F32),
                pltpu.VMEM((count * states, LANES), F32),
                pltpu.VMEM((count * states, LANES), F32),
                pltpu.SMEM((count, 2 * states), F32),
                pltpu.SemaphoreType.DMA,
            ],
        ),
        out_shape=[hbm(*out) for out in outs],
        input_output_aliases={} if code is None else {len(operands): 0},
        compiler_params=params(26),
        cost_estimate=cost(0),
        name="scan_backward",
    )(place, *in_hbm(operands))


def tail_kernel(
    place_ref,
    len_ref,
    *refs,
    micros,
    count,
    taps,
    clusters,
    ranks,
    chunks,
    states,
):
    def take(number):
        nonlocal refs
        taken, refs = refs[:number], refs[number:]
        return taken

    code_own_ref, code_other_ref = take(2)
    sact_refs, dpre_refs, alog_refs, back_refs = (take(micros) for _ in range(4))
    dtx_ref, bc_own_ref, bc_other_ref, decay_ref = take(4)
    dy_refs = take(micros)
    conved_ref, inner_ref, act_ref, high_ref, convw_ref, skip_ref = take(6)
    normed_ref, weight_ref, share_ref, gain_ref = take(4)
    keep_ref, send_ref, low_ref = take(3)
    mask_ref, code_ref, wcode_ref, vec_ref, alog_ref, total_ref, win_ref, sems = refs

    step = pl.program_id(0)
    rows = micros * count
    eighth = states // 2
    edge = LANES // 2
    half, core, cube, face = (place_ref[k] for k in range(4))
    pair = step ^ face
    span = LANES + 32

    def fetch(k):
        source = weight_ref.at[0, pl.ds(2 * (k ^ face), 2), half]
        return (pltpu.make_async_copy(source, win_ref.at[k], sems.at[k]),)

    stream(step, win_ref.shape[0], fetch)

    def pack_row(chunk):
        relative = chunk ^ cube
        return (relative & 3) * span + LANES + (relative >> 2) * 16

    def place_pair(start, size, cols, even, odd):
        keep_ref[aligned(start, size, 16), cols] = jnp.where(core == 0, even, odd).astype(BF16)
        send_ref[aligned(start, size, 16), cols] = jnp.where(core == 0, odd, even).astype(BF16)

    @pl.when(step == 0)
    def _():
        fill_masks(len_ref, mask_ref, micros, count, taps, clusters)
        total_ref[...] = share_ref[...]
        code_ref[...] = (code_own_ref[...] + code_other_ref[...]).astype(BF16)
        total = None
        for micro in range(micros):
            term = alog_refs[micro][...]
            total = term if total is None else total + term
        alog_ref[...] = total * (decay_ref[...] * (1.0 / LOG2E))

    code = code_ref[...]
    lane = lax.broadcasted_iota(jnp.int32, (1, LANES), 1)
    code_rank = jnp.where(lane < ranks, code, jnp.zeros_like(code))
    dpre = jnp.concatenate([ref[...] for ref in dpre_refs], axis=0)
    for part in range(2):
        source = lanes(2 * (2 * pair + part) + half)
        cols = slice(part * LANES, (part + 1) * LANES)
        wcode_ref[:ranks, cols] = dtx_ref[:, source]
        own = bc_own_ref[:, :, source].reshape(states, LANES)
        other = bc_other_ref[:, :, source].reshape(states, LANES)
        wcode_ref[ranks : ranks + states, cols] = jnp.where(half == 0, own, other)
        wcode_ref[ranks + states : ranks + 2 * states, cols] = jnp.where(half == 0, other, own)
        wcode_ref[ranks + 2 * states :, cols] = jnp.zeros(
            (LANES - ranks - 2 * states, LANES), BF16
        )
    for part in range(2):
        cols = slice(part * LANES, (part + 1) * LANES)
        chunk = 2 * pair + part
        source = 2 * chunk + half
        weights = convw_ref[:, lanes(source)]
        sact = jnp.concatenate([ref[:, cols] for ref in sact_refs], axis=0)
        dy = jnp.concatenate([ref[pl.ds(part * count, count), :] for ref in dy_refs], axis=0)
        dact = sact + dot(code, wcode_ref[:, cols], 1, 0)
        dact = dact + dy * skip_ref[pl.ds(source, 1), :]
        conved = conved_ref[:, cols]
        sig = sigmoid(conved)
        dconv = dact * (sig * (1.0 + conved * (1.0 - sig)))
        inner = inner_ref[:, cols]
        dinner = weights[taps - 1 : taps] * dconv
        sums = [None] * (taps + 1)
        sums[taps - 1] = jnp.sum(dconv * inner, axis=0, keepdims=True)
        sums[taps] = jnp.sum(dconv, axis=0, keepdims=True)
        for back in range(1, taps):
            kept = dconv * mask_ref[back]
            dinner = dinner + weights[taps - 1 - back : taps - back] * pltpu.roll(
                kept, rows - back, 0
            )
            sums[taps - 1 - back] = jnp.sum(
                kept * pltpu.roll(inner, back, 0), axis=0, keepdims=True
            )
        for k in range(taps + 1):
            vec_ref[k : k + 1, lanes(chunk)] = sums[k]
        for k in range(2):
            total = None
            for ref in back_refs:
                term = ref[k : k + 1, lanes(chunk)]
                total = term if total is None else total + term
            vec_ref[taps + 1 + k : taps + 2 + k, lanes(chunk)] = total
        low_ref[:, cols] = dinner.astype(BF16)

        act = act_ref[:, cols]
        start = pack_row(chunk)
        rows_now = dot(act, code_rank, 0, 0) + dot(dpre[:, cols], high_ref[...], 0, 0)
        for k in range(4):
            place_pair(
                start,
                16,
                slice(k * LANES, (k + 1) * LANES),
                rows_now[k * 16 : (k + 1) * 16],
                rows_now[edge + k * 16 : edge + (k + 1) * 16],
            )
        state_rows = dot(code, act, 0, 0)[ranks : ranks + 2 * states]
        place_pair(
            start, 16, slice(4 * LANES, 5 * LANES), state_rows[:states], state_rows[states:]
        )

    normed = normed_ref[...]
    for part in range(2):
        grad = dot(low_ref[:, lanes(core ^ part)], normed, 0, 0)
        total_ref[...] += eight_rows(grad * win_ref[step, core ^ part].astype(F32))
        out_ref = (keep_ref, send_ref)[part]
        out_ref[aligned(step * span, LANES, 16), :] = grad.astype(BF16)

    @pl.when(step == pl.num_programs(0) - 1)
    def _():
        vec_ref[taps + 3 : taps + 4, :] = (
            jnp.sum(total_ref[...], axis=0, keepdims=True) / gain_ref[...]
        )
        is_gain = lax.broadcasted_iota(jnp.int32, (8, LANES), 0) == taps + 3
        for chunk in range(chunks):
            start = pack_row(chunk)
            vec = vec_ref[:, chunk * LANES : (chunk + 1) * LANES]
            far, farther = (pltpu.roll(vec, LANES - k * edge // 2, 1) for k in (1, 2))
            even = jnp.where(is_gain & (lane >= edge // 2), far, vec)
            odd = jnp.where(is_gain & (lane < edge // 2), far, farther)
            alog = [
                alog_ref[pl.ds(q * eighth * chunks + chunk, eighth, stride=chunks), :]
                for q in range(2)
            ]
            place_pair(
                start,
                16,
                slice(5 * LANES, 6 * LANES),
                jnp.concatenate([alog[0], even]),
                jnp.concatenate([alog[1], odd]),
            )
            blank = jnp.zeros((16, 2 * LANES), F32)
            place_pair(start, 16, slice(6 * LANES, 8 * LANES), blank, blank)


def tail(
    place,
    lengths,
    code_own,
    code_other,
    sact,
    dpre,
    alog,
    back,
    dtx,
    bc_own,
    bc_other,
    decay,
    dy,
    conved,
    inner,
    act,
    high,
    convw,
    skip,
    normed,
    w4,
    share,
    gain,
):
    rows, own = act.shape
    chunks = own // LANES
    width = normed.shape[1]
    micros, _, clusters = lengths.shape
    count = rows // micros
    taps = convw.shape[0]
    ranks = dtx.shape[0]
    states = decay.shape[0] // chunks
    cols = 2 * LANES
    extent = 4 * (LANES + 32)

    def by_cols(height):
        return pl.BlockSpec((height, cols), lambda i, p: (0, i ^ p[FACE]))

    def dy_spec(micro):
        return pl.BlockSpec(
            (2 * count, LANES), lambda i, p: (micro * (chunks // 2) + (i ^ p[FACE]), 0)
        )

    in_specs = (
        [pl.BlockSpec(memory_space=pltpu.SMEM)]
        + [whole((rows, LANES))] * 2
        + [by_cols(count)] * (2 * micros)
        + [whole(alog[0].shape)] * micros
        + [whole(back[0].shape)] * micros
        + [whole(array.shape) for array in (dtx, bc_own, bc_other, decay)]
        + [dy_spec(micro) for micro in range(micros)]
        + [by_cols(rows)] * 3
        + [whole(array.shape) for array in (high, convw, skip, normed)]
        + [
            ANY,
            whole(share.shape),
            whole(gain.shape),
        ]
    )
    return pl.pallas_call(
        functools.partial(
            tail_kernel,
            micros=micros,
            count=count,
            taps=taps,
            clusters=clusters,
            ranks=ranks,
            chunks=chunks,
            states=states,
        ),
        grid_spec=pltpu.PrefetchScalarGridSpec(
            num_scalar_prefetch=1,
            grid=(chunks // 2,),
            in_specs=in_specs,
            out_specs=[
                whole((extent, width)),
                whole((extent, width)),
                pl.BlockSpec((rows, cols), lambda i, p: (0, i ^ p[FACE])),
            ],
            scratch_shapes=[
                pltpu.VMEM((taps, rows, LANES), F32),
                pltpu.VMEM((rows, LANES), BF16),
                pltpu.VMEM((LANES, cols), BF16),
                pltpu.VMEM((8, own), F32),
                pltpu.VMEM((states * chunks, LANES), F32),
                pltpu.VMEM((8, width), F32),
                pltpu.VMEM((chunks // 2, 2, LANES, width), BF16),
                pltpu.SemaphoreType.DMA((chunks // 2,)),
            ],
        ),
        out_shape=[
            hbm((extent, width), BF16),
            hbm((extent, width), BF16),
            hbm((rows, own), BF16),
        ],
        compiler_params=params(30),
        cost_estimate=cost(7),
        name="tail",
    )(
        place,
        lengths,
        *in_hbm([code_own]),
        code_other,
        *in_hbm(
            (
                *sact,
                *dpre,
                *alog,
                *back,
                dtx,
                bc_own,
                bc_other,
                decay,
                *([dy] * micros),
                conved,
                inner,
                act,
                high,
                convw,
                skip,
                normed,
                w4,
                share,
                gain,
            )
        ),
    )


def fetch_halves(source, which, half, target_ref, sems):
    copies = []
    for k in range(target_ref.shape[0]):
        pair = pl.ds(2 * k, 2)
        block = source.at[pair, half] if which is None else source.at[which, pair, half]
        copies.append(pltpu.make_async_copy(block, target_ref.at[k], sems.at[k]))
    for copy in copies:
        copy.start()
    return copies


def products_kernel(
    place_ref,
    gated_ref,
    dgate_ref,
    out_ref,
    weight_ref,
    mixed_ref,
    dnormed_ref,
    wout_ref,
    wgate_ref,
    out_sems,
    gate_sems,
):
    half = place_ref[HALF]
    width = mixed_ref.shape[1]
    jobs = (
        (fetch_halves(out_ref, None, half, wout_ref, out_sems), gated_ref, wout_ref, mixed_ref),
        (fetch_halves(weight_ref, 1, half, wgate_ref, gate_sems), dgate_ref, wgate_ref, dnormed_ref),
    )
    for copies, left_ref, right_ref, result_ref in jobs:
        total = None
        for k, copy in enumerate(copies):
            copy.wait()
            left = left_ref[:, 2 * k * LANES : 2 * (k + 1) * LANES]
            term = dot(left, right_ref[k].reshape(-1, width), 1, 0)
            total = term if total is None else total + term
        result_ref[...] = total.astype(BF16)


def products(place, gated, dgate, wout3, w4):
    rows, own = gated.shape
    width = w4.shape[-1]
    pairs = own // (2 * LANES)
    return pl.pallas_call(
        products_kernel,
        grid_spec=pltpu.PrefetchScalarGridSpec(
            num_scalar_prefetch=1,
            grid=(1,),
            in_specs=[whole((rows, own)), whole((rows, own)), ANY, ANY],
            out_specs=[whole((rows, width))] * 2,
            scratch_shapes=[
                pltpu.VMEM((pairs, 2, LANES, width), BF16),
                pltpu.VMEM((pairs, 2, LANES, width), BF16),
                pltpu.SemaphoreType.DMA((pairs,)),
                pltpu.SemaphoreType.DMA((pairs,)),
            ],
        ),
        out_shape=[hbm((rows, width), BF16)] * 2,
        compiler_params=params(20),
        cost_estimate=cost(4),
        name="products",
    )(place, *in_hbm((gated, dgate, wout3, w4)))


def spread_kernel(place_ref, low_ref, weight_ref, gate_ref, dnormed_ref, win_ref, sems):
    width = gate_ref.shape[1]
    total = gate_ref[...].astype(F32)
    for k, copy in enumerate(fetch_halves(weight_ref, 0, place_ref[HALF], win_ref, sems)):
        copy.wait()
        left = low_ref[:, 2 * k * LANES : 2 * (k + 1) * LANES]
        total = total + dot(left, win_ref[k].reshape(-1, width), 1, 0)
    dnormed_ref[...] = total.astype(BF16)


def spread(place, low, w4, gate_part):
    rows, own = low.shape
    width = w4.shape[-1]
    pairs = own // (2 * LANES)
    return pl.pallas_call(
        spread_kernel,
        grid_spec=pltpu.PrefetchScalarGridSpec(
            num_scalar_prefetch=1,
            grid=(1,),
            in_specs=[whole((rows, own)), ANY, whole((rows, width))],
            out_specs=whole((rows, width)),
            scratch_shapes=[
                pltpu.VMEM((pairs, 2, LANES, width), BF16),
                pltpu.SemaphoreType.DMA((pairs,)),
            ],
        ),
        out_shape=hbm((rows, width), BF16),
        compiler_params=params(16),
        cost_estimate=cost(3),
        name="spread",
    )(place, *in_hbm((low, w4, gate_part)))


def finish_kernel(x_ref, mine_ref, theirs_ref, cotan_ref, gain_ref, grad_ref):
    x = x_ref[...].astype(F32)
    scale = lax.rsqrt(jnp.mean(x * x, axis=1, keepdims=True) + EPSILON)
    unit = x * scale
    dhat = (mine_ref[...].astype(F32) + theirs_ref[...].astype(F32)) * gain_ref[...]
    grad_ref[...] = cotan_ref[...].astype(F32) + scale * (
        dhat - unit * jnp.mean(dhat * unit, axis=1, keepdims=True)
    )


def finish(x, mine, theirs, cotan, gain):
    rows, width = x.shape
    by_rows = pl.BlockSpec((rows // 4, width), lambda i: (i, 0))
    return pl.pallas_call(
        finish_kernel,
        grid=(4,),
        in_specs=[by_rows] * 4 + [whole(gain.shape)],
        out_specs=by_rows,
        out_shape=jax.ShapeDtypeStruct((rows, width), F32),
        compiler_params=params(16),
        cost_estimate=cost(0),
        name="finish",
    )(*in_hbm((x, mine)), theirs, *in_hbm((cotan, gain)))


def unpack_kernel(
    near_ref,
    far_ref,
    out_ref,
    dtx_ref,
    dt_ref,
    bc_ref,
    alog_ref,
    convw_ref,
    convb_ref,
    bias_ref,
    skip_ref,
    out_grad_ref,
    *,
    eighth,
    taps,
    edge,
):
    pack = near_ref[...].astype(F32) + far_ref[...].astype(F32)
    for k in range(4):
        rows = pack[:, k * LANES : (k + 1) * LANES]
        dtx_ref[pl.ds(16 * k, 16), :] = rows[:, :edge]
        dt_ref[pl.ds(16 * k, 16), :] = pltpu.roll(rows, edge, 1)[:, :edge]
    rows = pack[:, 4 * LANES : 5 * LANES]
    bc_ref[0] = rows[:eighth]
    bc_ref[1] = rows[eighth:]
    rows = pack[:, 5 * LANES : 6 * LANES]
    alog_ref[...] = rows[:eighth]
    vec = rows[eighth:, :edge]
    convw_ref[...] = vec[:taps]
    convb_ref[...] = vec[taps : taps + 1]
    bias_ref[...] = vec[taps + 1 : taps + 2]
    skip_ref[...] = vec[taps + 2 : taps + 3]
    out_grad_ref[...] = out_ref[...].astype(F32)


def unpack(near, far, out, eighth, taps, ranks):
    edge = LANES // 2
    shapes = [
        (edge, ranks),
        (edge, ranks),
        (2, eighth, LANES),
        (eighth, LANES),
        (taps, edge),
        (1, edge),
        (1, edge),
        (1, edge),
        out.shape,
    ]
    return pl.pallas_call(
        functools.partial(unpack_kernel, eighth=eighth, taps=taps, edge=edge),
        grid=(1,),
        in_specs=[whole(array.shape) for array in (near, far, out)],
        out_specs=[whole(shape) for shape in shapes],
        out_shape=[jax.ShapeDtypeStruct(shape, F32) for shape in shapes],
        cost_estimate=cost(0),
        name="unpack",
    )(near, far, out)


def swap_pair(array):
    count = lax.axis_size("state")
    return lax.ppermute(array, "state", [(pos, pos ^ 1) for pos in range(count)])


def swap_bit(array, bits):
    return lax.ppermute(array, "dp", [(pos, pos ^ bits) for pos in range(lax.axis_size("dp"))])


def swap_both(array, bits=0):
    states = lax.axis_size("state")
    pairs = []
    for d in range(lax.axis_size("dp")):
        for s in range(states):
            pairs.append((d * states + s, (((d & ~1) | s) ^ bits) * states + (d & 1)))
    return lax.ppermute(array, ("dp", "state"), pairs)


def add_quarters(kept, got):
    extent = kept.shape[0] // 4
    return [kept[k * extent :][:extent] + got[k * extent :][:extent] for k in range(4)]


def trade_quarters(quarters):
    return [quarters[0]] + [swap_bit(quarters[k], k * X_BIT) for k in range(1, 4)]


def sum_quarters(quarters):
    left, right = (quarters[k].astype(F32) + quarters[k + 1].astype(F32) for k in (0, 2))
    return (left + right).astype(BF16)


CORE_BIT, X_BIT, ZH_BIT = 1, 2, 8


def shards(
    tokens,
    cluster_len,
    norm_gain,
    in_weight,
    conv_weight,
    conv_bias,
    dtx_weight,
    dt_weight,
    dt_bias,
    bc_weight,
    a_log,
    skip_gain,
    out_weight,
    cotangent,
):
    micros, count, width = tokens.shape
    inner = out_weight.shape[0]
    taps = conv_weight.shape[0]
    ranks = dtx_weight.shape[1]
    chunks = inner // (2 * LANES)
    own = chunks * LANES
    rows = micros * count
    edge = LANES // 2
    span = LANES + 32
    dp_parts = lax.axis_size("dp")
    state_count = lax.axis_size("state")
    dp_pos = lax.axis_index("dp")
    state_pos = lax.axis_index("state")
    half = state_pos & 1
    fast = state_count == 2 and dp_parts == 2 * chunks == 16
    if fast:
        place = jnp.stack([half, dp_pos & 1, dp_pos >> 1, (dp_pos >> 1) & 3])
        bc_own, alog_own = bc_weight, a_log
        bc_other, alog_other = swap_pair(bc_weight), swap_pair(a_log)
    else:
        place = jnp.stack([half, 0, 0, 0])
        bc_all = lax.all_gather(bc_weight, "state", axis=1, tiled=True)
        alog_all = lax.all_gather(a_log, "state", axis=0, tiled=True)
        eighth = alog_all.shape[0] // 2
        bc_own, bc_other = (
            lax.dynamic_slice_in_dim(bc_all, which * eighth, eighth, 1)
            for which in (half, 1 - half)
        )
        alog_own, alog_other = (
            lax.dynamic_slice_in_dim(alog_all, which * eighth, eighth, 0)
            for which in (half, 1 - half)
        )
    place = place.astype(jnp.int32)
    eighth = alog_own.shape[0]
    states = 2 * eighth

    x = tokens.reshape(rows, width)
    cotan = cotangent.reshape(rows, width)
    w4 = in_weight.reshape(2, chunks, 2, LANES, width)
    wout3 = out_weight.reshape(chunks, 2, LANES, width)
    dtx, dt = dtx_weight.T, dt_weight.T
    bias = dt_bias.reshape(-1, LANES)
    skip = skip_gain.reshape(-1, LANES)

    normed, act_all, act, inner_own, conved, gate = project(
        place, cluster_len, x, norm_gain[None], w4, conv_weight, conv_bias.reshape(-1, LANES)
    )
    bc, rank, high, decay, sp, u, dy, gated, dgate, keep, send, share = scan_forward(
        place,
        cluster_len,
        act_all,
        bc_own,
        bc_other,
        alog_own,
        alog_other,
        dtx,
        dt,
        bias,
        skip,
        act,
        gate,
        wout3,
        cotan,
        normed,
        w4,
    )
    if fast:
        early = swap_bit(send, CORE_BIT)
    mixed_part, dn_gate = products(place, gated, dgate, wout3, w4)
    if fast:
        *quarters, mixed_part, dn_gate, sp = lax.optimization_barrier(
            (*add_quarters(keep, early), mixed_part, dn_gate, sp)
        )
        early_got = trade_quarters(quarters)
    mixed_other = swap_pair(mixed_part)
    code_own = None
    results = []
    for micro in range(micros):
        if fast and micro == micros - 1:
            block = sum_quarters(early_got)
            out_keep, out_send, gate_sum = block[:edge], block[edge:LANES], block[LANES:]
            out_send, gate_sum, sp = lax.optimization_barrier((out_send, gate_sum, sp))
            out_got = swap_bit(out_send, ZH_BIT)
        code_own, *rest = scan_backward(
            place, micro, count, bc, decay, rank, dt, bias, act, sp, u, dy, code_own
        )
        results.append(rest)
    sact, dpre, alog, back = zip(*results)
    code_other = swap_pair(code_own)
    if fast:
        out_got, mixed_other, conved = lax.optimization_barrier((out_got, mixed_other, conved))
    late_keep, late_send, low = tail(
        place,
        cluster_len,
        code_own,
        code_other,
        sact,
        dpre,
        alog,
        back,
        dtx,
        bc_own,
        bc_other,
        decay,
        dy,
        conved,
        inner_own,
        act,
        high,
        conv_weight,
        skip,
        normed,
        w4,
        share,
        norm_gain[None],
    )
    if fast:
        late = swap_bit(late_send, CORE_BIT)
        out_own = swap_both(out_keep + out_got)
        late_got = trade_quarters(add_quarters(late_keep, late))
    dnormed_part = spread(place, low, w4, dn_gate)
    dnormed_other = swap_pair(dnormed_part)
    mixed = (x.astype(F32) + (mixed_part.astype(F32) + mixed_other.astype(F32))).astype(BF16)
    if fast:
        *late_got, mixed, out_own, dnormed_other = lax.optimization_barrier(
            (*late_got, mixed, out_own, dnormed_other)
        )
        block = sum_quarters(late_got)
        inner_sum = block[:LANES]
        upper = dp_pos >= dp_parts // 2
        crossing = jnp.where(upper, inner_sum, gate_sum)
        first, second = crossing[:edge], crossing[edge:]
        first, pack_far, pack_near = lax.optimization_barrier(
            (first, block[-16:], block[LANES:-16])
        )
        pack_far = swap_both(pack_far, ZH_BIT)
        first_got = swap_bit(first, ZH_BIT)
        pack_near = swap_both(pack_near)
        first_got, pack_far, pack_near = lax.optimization_barrier((first_got, pack_far, pack_near))
        second_got = swap_bit(second, ZH_BIT)
        tokens_grad = finish(x, dnormed_part, dnormed_other, cotan, norm_gain[None])
        gain_mine = (
            pack_near[:, 5 * LANES : 6 * LANES].astype(F32)
            + pack_far[:, 5 * LANES : 6 * LANES].astype(F32)
        ).astype(BF16)
        gain_both = gain_mine[-1].astype(F32) + swap_bit(gain_mine, CORE_BIT)[-1].astype(F32)
        extent = width // (dp_parts * state_count)
        gain_grad = lax.dynamic_slice_in_dim(gain_both, (dp_pos & 1) * extent, extent, 0)
        (
            dtx_grad,
            dt_grad,
            bc_grad,
            alog_grad,
            convw_grad,
            convb_grad,
            bias_grad,
            skip_grad,
            out_own,
        ) = unpack(pack_near, pack_far, out_own, eighth, taps, ranks)
        convb_grad, bias_grad, skip_grad = (
            array[0] for array in (convb_grad, bias_grad, skip_grad)
        )
        in_grad = jnp.where(upper, gate_sum, inner_sum).astype(F32) + jnp.concatenate(
            [first_got, second_got]
        ).astype(F32)
    else:
        tokens_grad = finish(x, dnormed_part, dnormed_other, cotan, norm_gain[None])
    mixed = mixed.reshape(micros, count, width)
    tokens_grad = tokens_grad.reshape(micros, count, width)

    if not fast:
        def total(array):
            return lax.psum(array.astype(F32), "dp")

        def both_rows(array):
            mine = array.reshape(chunks, 1, LANES, -1)
            other = swap_pair(mine)
            low = jnp.where(half == 0, mine, other)
            high = jnp.where(half == 0, other, mine)
            return jnp.concatenate([low, high], axis=1).reshape(2 * own, -1)

        every = dp_parts * state_count
        at = dp_pos * state_count + state_pos

        def cut_own(array):
            extent = array.shape[0] // every
            return lax.dynamic_slice_in_dim(array, at * extent, extent, 0)

        pair = total(jnp.stack([keep, send])).reshape(2, 2, 2, 2 * LANES, width)
        outs = pair[:, :, :, :LANES].reshape(2, 2, 2, 2, edge, width)
        outs = jnp.transpose(outs, (3, 1, 2, 0, 4, 5)).reshape(own, width)
        gates = jnp.moveaxis(pair[:, :, :, LANES:], 0, 2).reshape(own, width)
        pair = total(jnp.stack([late_keep, late_send])).reshape(2, 2, 2, span, width)
        inners = jnp.moveaxis(pair[:, :, :, :LANES], 0, 2).reshape(own, width)
        packs = pair[:, :, :, LANES:].reshape(2, 2, 2, 2, 16, width // LANES, LANES)
        packs = jnp.transpose(packs, (3, 1, 2, 0, 5, 4, 6)).reshape(chunks, 2, -1, 16, LANES)
        small = both_rows(packs[:, :, :4].reshape(own, LANES))
        in_grad = cut_own(jnp.concatenate([both_rows(inners), both_rows(gates)]))
        out_own = cut_own(both_rows(outs))
        mine = cut_own(small)
        dtx_grad, dt_grad = mine[:, :ranks], mine[:, ranks:]
        vec_rows = jnp.swapaxes(packs[:, :, 5, eighth:, :edge], 2, 3).reshape(own, -1)
        gain_sum = vec_rows[:, -1].reshape(chunks, 2, 2, -1).swapaxes(1, 2).reshape(-1)
        gain_grad = cut_own(gain_sum + swap_pair(gain_sum))
        vec = cut_own(both_rows(vec_rows)).T
        state_rows = jnp.concatenate([packs[:, :, 4], packs[:, :, 5, :eighth]], axis=2)
        state_rows = state_rows.reshape(chunks, 2, 3, eighth, LANES)
        state_rows = jnp.transpose(state_rows, (0, 4, 2, 1, 3)).reshape(own, -1)
        extent = inner // dp_parts
        state_part = lax.dynamic_slice_in_dim(both_rows(state_rows), dp_pos * extent, extent, 0)
        state_part = state_part.T.reshape(3, state_count, -1, extent)
        state_part = lax.dynamic_index_in_dim(state_part, state_pos, 1, keepdims=False)
        bc_grad, alog_grad = state_part[:2], state_part[2]
        convw_grad, convb_grad, bias_grad, skip_grad = (
            vec[:taps], vec[taps], vec[taps + 1], vec[taps + 2]
        )

    return (
        mixed,
        tokens_grad,
        gain_grad,
        in_grad,
        convw_grad,
        convb_grad,
        dtx_grad,
        dt_grad,
        bias_grad,
        bc_grad,
        alog_grad,
        skip_grad,
        out_own,
    )


def solution(mesh):
    return jax.shard_map(
        shards,
        mesh=mesh,
        in_specs=(
            P(None, "dp", None),
            P(None, "dp", None),
            P(),
            P(),
            P(),
            P(),
            P(),
            P(),
            P(),
            P(None, "state", None),
            P("state", None),
            P(),
            P(),
            P(None, "dp", None),
        ),
        out_specs=(
            P(None, "dp", None),
            P(None, "dp", None),
            P(("dp", "state")),
            P(("dp", "state"), None),
            P(None, ("dp", "state")),
            P(("dp", "state")),
            P(("dp", "state"), None),
            P(("dp", "state"), None),
            P(("dp", "state")),
            P(None, "state", "dp"),
            P("state", "dp"),
            P(("dp", "state")),
            P(("dp", "state"), None),
        ),
        check_vma=False,
    )
```

```python
import functools
import math

import jax
import jax.numpy as jnp
from jax import lax
from jax.experimental import pallas as pl
from jax.experimental.pallas import tpu as pltpu
from jax.sharding import PartitionSpec as P

EPSILON = 1e-05
LANES = 128
RESET = 1e4
LOG2E = math.log2(math.e)
F32 = jnp.float32
BF16 = jnp.bfloat16
MIB = 1024 * 1024


def dot(left, right, left_dim, right_dim):
    return lax.dot_general(
        left, right, (((left_dim,), (right_dim,)), ((), ())), preferred_element_type=F32
    )


def params(mib):
    return pltpu.CompilerParams(
        vmem_limit_bytes=mib * MIB, dimension_semantics=("arbitrary",)
    )


ANY = pl.BlockSpec(memory_space=pl.ANY)


def stream(step, steps, fetch):
    @pl.when(step == 0)
    def _():
        for k in range(steps):
            for copy in fetch(k):
                copy.start()

    for copy in fetch(step):
        copy.wait()


def whole(shape):
    return pl.BlockSpec(shape, lambda *_: (0,) * len(shape))


sigmoid = jax.nn.sigmoid


def softplus(value):
    return jnp.maximum(value, 0.0) + jnp.log1p(jnp.exp(-jnp.abs(value)))


def lanes(index):
    return pl.ds(pl.multiple_of(index * LANES, LANES), LANES)


def cost(micros):
    return pl.CostEstimate(
        flops=int(micros * 1e9), bytes_accessed=int(micros * 1e6), transcendentals=0
    )


def hbm(shape, dtype):
    return pltpu.HBM(shape, dtype)


def in_hbm(arrays):
    return [pltpu.with_memory_space_constraint(array, pltpu.HBM) for array in arrays]


def aligned(start, size, to=8):
    return pl.ds(pl.multiple_of(start, to), size)


HALF, CORE, CUBE, FACE = range(4)


def fill_masks(len_ref, mask_ref, micros, count, taps, clusters):
    place = lax.broadcasted_iota(jnp.int32, (count, LANES), 0)
    for micro in range(micros):
        rows = pl.ds(micro * count, count)
        for back in range(1, taps):
            apart = place < back
            start = 0
            for cluster in range(clusters - 1):
                start = start + len_ref[micro, 0, cluster]
                apart = apart | ((place >= start) & (place < start + back))
            mask_ref[back, rows, :] = jnp.where(apart, 0.0, 1.0)
            if back == 1:
                mask_ref[0, rows, :] = jnp.where(apart, 1.0, 0.0)


def project_kernel(
    place_ref,
    len_ref,
    x_ref,
    gain_ref,
    weight_ref,
    convw_ref,
    convb_ref,
    normed_ref,
    act_ref,
    own_act_ref,
    inner_ref,
    conved_ref,
    gate_ref,
    mask_ref,
    proj_ref,
    conv_ref,
    win_ref,
    wgate_ref,
    sems,
    *,
    micros,
    count,
    taps,
    clusters,
):
    chunk = pl.program_id(0)

    @pl.when(chunk == 0)
    def _():
        fill_masks(len_ref, mask_ref, micros, count, taps, clusters)
        rows = x_ref[...].astype(F32)
        scale = lax.rsqrt(jnp.mean(rows * rows, axis=1, keepdims=True) + EPSILON)
        normed_ref[...] = (rows * scale * gain_ref[...]).astype(BF16)

    half = place_ref[HALF]

    def fetch(k):
        return (
            pltpu.make_async_copy(weight_ref.at[0, k], win_ref.at[k], sems.at[0, k]),
            pltpu.make_async_copy(weight_ref.at[1, k, half], wgate_ref.at[k], sems.at[1, k]),
        )

    stream(chunk, win_ref.shape[0], fetch)
    normed = normed_ref[...]
    proj_ref[...] = dot(normed, win_ref[chunk].reshape(2 * LANES, -1), 1, 1)
    gate_ref[...] = dot(normed, wgate_ref[chunk], 1, 1)
    for part in range(2):
        cols = pl.ds(part * LANES, LANES)
        inner = proj_ref[:, cols]
        conved = convb_ref[pl.ds(2 * chunk + part, 1), :] + convw_ref[taps - 1 : taps, cols] * inner
        for back in range(1, taps):
            shifted = pltpu.roll(inner, back, 0) * mask_ref[back]
            conved = conved + convw_ref[taps - 1 - back : taps - back, cols] * shifted
        conv_ref[:, cols] = conved
        act_ref[:, cols] = (conved * sigmoid(conved)).astype(BF16)
    own = lanes(half)
    inner_ref[...] = proj_ref[:, own]
    conved_ref[...] = conv_ref[:, own]
    own_act_ref[...] = act_ref[:, own]


def project(place, lengths, x, gain, w4, conv_weight, conv_bias):
    rows, width = x.shape
    chunks = w4.shape[1]
    inner = chunks * 2 * LANES
    micros, _, clusters = lengths.shape
    taps = conv_weight.shape[0]
    own = chunks * LANES
    by_chunk = pl.BlockSpec((rows, LANES), lambda i, p: (0, i))
    return pl.pallas_call(
        functools.partial(
            project_kernel, micros=micros, count=rows // micros, taps=taps, clusters=clusters
        ),
        grid_spec=pltpu.PrefetchScalarGridSpec(
            num_scalar_prefetch=1,
            grid=(chunks,),
            in_specs=[
                pl.BlockSpec(memory_space=pltpu.SMEM),
                whole((rows, width)),
                whole((1, width)),
                ANY,
                pl.BlockSpec((taps, 2 * LANES), lambda i, p: (0, i)),
                whole(conv_bias.shape),
            ],
            out_specs=[
                whole((rows, width)),
                pl.BlockSpec((rows, 2 * LANES), lambda i, p: (0, i)),
                by_chunk,
                by_chunk,
                by_chunk,
                by_chunk,
            ],
            scratch_shapes=[
                pltpu.VMEM((taps, rows, LANES), F32),
                pltpu.VMEM((rows, 2 * LANES), F32),
                pltpu.VMEM((rows, 2 * LANES), F32),
                pltpu.VMEM((chunks, 2, LANES, width), BF16),
                pltpu.VMEM((chunks, LANES, width), BF16),
                pltpu.SemaphoreType.DMA((2, chunks)),
            ],
        ),
        out_shape=[
            hbm((rows, width), BF16),
            hbm((rows, inner), BF16),
            hbm((rows, own), BF16),
            hbm((rows, own), F32),
            hbm((rows, own), F32),
            hbm((rows, own), F32),
        ],
        compiler_params=params(20),
        cost_estimate=cost(6),
        name="project",
    )(place, *in_hbm((lengths, x, gain, w4, conv_weight, conv_bias)))


def eight_rows(array):
    return jnp.sum(array.reshape(-1, 8, array.shape[1]), axis=0)


def b_at(n, eighth):
    return (n // eighth) * 2 * eighth + n % eighth


def c_at(n, eighth):
    return b_at(n, eighth) + eighth


def forward_kernel(
    place_ref,
    len_ref,
    act_all_ref,
    bc_own_ref,
    bc_other_ref,
    alog_own_ref,
    alog_other_ref,
    dtx_ref,
    dt_ref,
    bias_ref,
    skip_ref,
    act_ref,
    gate_ref,
    wout_ref,
    cotan_ref,
    normed_ref,
    wgate_ref,
    bc_ref,
    rank_ref,
    rank_high_ref,
    decay_ref,
    sp_ref,
    u_ref,
    dy_ref,
    gated_ref,
    dgate_ref,
    keep_ref,
    send_ref,
    share_ref,
    mask_ref,
    y_ref,
    tmp_ref,
    scalar_ref,
    sem,
    *,
    micros,
    count,
    states,
    chunks,
    clusters,
):
    rows = micros * count
    eighth = states // 2
    half, core, cube, face = (place_ref[k] for k in range(4))
    first = half == 0
    act_all = act_all_ref[...]
    own = dot(act_all, bc_own_ref[...].reshape(states, -1), 1, 1)
    other = dot(act_all, bc_other_ref[...].reshape(states, -1), 1, 1)
    bc_ref[:, :states] = jnp.where(first, own, other)
    bc_ref[:, states:] = jnp.where(first, other, own)
    copy = pltpu.make_async_copy(bc_ref, scalar_ref, sem)
    copy.start()

    fill_masks(len_ref, mask_ref, micros, count, 2, clusters)
    for chunk in range(chunks):
        cols = lanes(2 * chunk + half)
        own, other = alog_own_ref[:, cols], alog_other_ref[:, cols]
        tmp_ref[pl.ds(chunk * states, eighth), :] = jnp.where(first, own, other)
        tmp_ref[pl.ds(chunk * states + eighth, eighth), :] = jnp.where(first, other, own)
    for n in range(states):
        decay_ref[pl.ds(n * chunks, chunks), :] = -LOG2E * jnp.exp(
            tmp_ref[pl.ds(n, chunks, stride=states), :]
        )

    rank = dot(act_all, dtx_ref[...], 1, 1).astype(BF16)
    rank_ref[...] = rank
    rank_high_ref[...] = jnp.concatenate([jnp.zeros_like(rank), rank], axis=1)
    for chunk in range(chunks):
        cols = slice(chunk * LANES, (chunk + 1) * LANES)
        bias = bias_ref[pl.ds(2 * chunk + half, 1), :]
        step = softplus(dot(rank, dt_ref[:, lanes(2 * chunk + half)], 1, 0) + bias)
        held = step + RESET * mask_ref[0]
        source = step * act_ref[:, cols].astype(F32)
        for micro in range(micros):
            span = slice(micro * count, (micro + 1) * count)
            place = pl.ds((micro * chunks + chunk) * count, count)
            sp_ref[place, :] = held[span]
            u_ref[place, :] = source[span]
    copy.wait()

    for micro in range(micros):

        def advance(t, h, micro=micro):
            row = micro * count + t
            span = pl.ds(micro * chunks * count + t, chunks, stride=count)
            sp = sp_ref[span, :]
            u = u_ref[span, :]
            out = []
            y = None
            for n in range(states):
                decay = jnp.exp2(sp * decay_ref[pl.ds(n * chunks, chunks), :])
                now = decay * h[n] + u * scalar_ref[row, b_at(n, eighth)]
                out.append(now)
                term = now * scalar_ref[row, c_at(n, eighth)]
                y = term if y is None else y + term
            y_ref[span, :] = y
            return tuple(out)

        lax.fori_loop(0, count, advance, (jnp.zeros((chunks, LANES), F32),) * states, unroll=2)

    cotan = cotan_ref[...]
    for chunk in range(chunks):
        cols = slice(chunk * LANES, (chunk + 1) * LANES)
        places = [pl.ds((micro * chunks + chunk) * count, count) for micro in range(micros)]
        y = jnp.concatenate([y_ref[place, :] for place in places])
        y = y + skip_ref[pl.ds(2 * chunk + half, 1), :] * act_ref[:, cols].astype(F32)
        gate = gate_ref[:, cols]
        sig = sigmoid(gate)
        gated_ref[:, cols] = (y * (gate * sig)).astype(BF16)
        dgated = dot(cotan, wout_ref[chunk, 0], 1, 1)
        dy = dgated * (gate * sig)
        for micro in range(micros):
            dy_ref[places[micro], :] = dy[micro * count : (micro + 1) * count]
        dgate_ref[:, cols] = (dgated * y * (sig * (1.0 + gate * (1.0 - sig)))).astype(BF16)
    normed = normed_ref[...]
    edge = LANES // 2
    for j in range(chunks):
        grad = dot(gated_ref[:, lanes(j ^ cube)], cotan, 0, 0).astype(BF16)
        top, bottom = grad[:edge], grad[edge:]
        place = pl.ds((j & 3) * 2 * LANES + (j >> 2) * edge, edge)
        keep_ref[place, :] = jnp.where(core == 0, top, bottom)
        send_ref[place, :] = jnp.where(core == 0, bottom, top)
    share = jnp.zeros(share_ref.shape, F32)
    for j in range(chunks // 2):
        place = pl.ds((2 * j + 1) * LANES, LANES)
        pair = 2 * (j ^ face)
        for chunk, out_ref in ((pair + core, keep_ref), (pair + 1 - core, send_ref)):
            grad = dot(dgate_ref[:, lanes(chunk)], normed, 0, 0)
            share = share + eight_rows(grad * wgate_ref[0, chunk, 0].astype(F32))
            out_ref[place, :] = grad.astype(BF16)
    share_ref[...] = share


def scan_forward(
    place,
    lengths,
    act_all,
    bc_own,
    bc_other,
    alog_own,
    alog_other,
    dtx,
    dt,
    bias,
    skip,
    act,
    gate,
    wout3,
    cotan,
    normed,
    w4,
):
    rows, own = act.shape
    chunks = own // LANES
    states = 2 * alog_own.shape[0]
    width = cotan.shape[1]
    micros, _, clusters = lengths.shape
    ranks = dtx.shape[0]
    outs = [
        ((rows, 2 * states), F32),
        ((rows, ranks), BF16),
        ((rows, 2 * ranks), BF16),
        ((states * chunks, LANES), F32),
        ((chunks * rows, LANES), F32),
        ((chunks * rows, LANES), F32),
        ((chunks * rows, LANES), F32),
        ((rows, own), BF16),
        ((rows, own), BF16),
        ((own, width), BF16),
        ((own, width), BF16),
        ((8, width), F32),
    ]
    operands = (
        act_all, bc_own, bc_other, alog_own, alog_other, dtx, dt, bias, skip, act, gate
    )
    return pl.pallas_call(
        functools.partial(
            forward_kernel,
            micros=micros,
            count=rows // micros,
            states=states,
            chunks=chunks,
            clusters=clusters,
        ),
        grid_spec=pltpu.PrefetchScalarGridSpec(
            num_scalar_prefetch=1,
            grid=(1,),
            in_specs=[pl.BlockSpec(memory_space=pltpu.SMEM)]
            + [whole(operand.shape) for operand in operands]
            + [
                pl.BlockSpec((chunks, 1, LANES, width), lambda i, p: (0, p[HALF], 0, 0)),
                whole((rows, width)),
                whole((rows, width)),
                pl.BlockSpec((1, chunks, 1, LANES, width), lambda i, p: (1, 0, p[HALF], 0, 0)),
            ],
            out_specs=[whole(shape) for shape, _ in outs],
            scratch_shapes=[
                pltpu.VMEM((2, rows, LANES), F32),
                pltpu.VMEM((chunks * rows, LANES), F32),
                pltpu.VMEM((states * chunks, LANES), F32),
                pltpu.SMEM((rows, 2 * states), F32),
                pltpu.SemaphoreType.DMA,
            ],
        ),
        out_shape=[hbm(*out) for out in outs],
        compiler_params=params(48),
        cost_estimate=cost(19),
        name="scan_forward",
    )(
        place,
        lengths,
        *in_hbm(operands[:1]),
        *operands[1:5],
        *in_hbm((*operands[5:], wout3, cotan, normed, w4)),
    )


def fold(terms):
    size = len(terms)
    row = lax.broadcasted_iota(jnp.int32, terms[0].shape, 0)
    shift = 1
    while shift < size:
        first = row % (2 * shift) < shift
        merged = []
        for left, right in zip(terms[::2], terms[1::2]):
            crossed = jnp.where(first, right, left)
            merged.append(jnp.where(first, left, right) + pltpu.roll(crossed, size - shift, 0))
        terms = merged
        shift = 2 * shift
    return terms[0]


def backward_kernel(
    place_ref,
    bc_ref,
    decay_ref,
    rank_ref,
    dt_ref,
    bias_ref,
    act_ref,
    sp_ref,
    u_ref,
    dy_ref,
    *refs,
    count,
    states,
    chunks,
):
    code_ref, sact_ref, dpre_ref, alog_ref, vec_ref = refs[-11:-6]
    h_ref, s_ref, d_ref, sums_ref, scalar_ref, sem = refs[-6:]
    copy = pltpu.make_async_copy(bc_ref, scalar_ref, sem)
    copy.start()
    half = place_ref[HALF]
    eighth = states // 2
    zero = (jnp.zeros((chunks, LANES), F32),) * states
    for n in range(states):
        h_ref[pl.ds(n * chunks, chunks), :] = zero[0]
    copy.wait()
    pitch = count + 1

    def put_sums(t, start, terms):
        for k in range(0, states, chunks):
            place = pl.ds((start + k) * pitch + t, chunks, stride=pitch)
            sums_ref[place, :] = fold(terms[k : k + chunks])

    def recompute(pair, h):
        for slot in range(2):
            t = 2 * pair + slot
            span = pl.ds(t, chunks, stride=count)
            sp = sp_ref[span, :]
            u = u_ref[span, :]
            dy = dy_ref[span, :]
            out = []
            terms = []
            for n in range(states):
                decay = jnp.exp2(sp * decay_ref[pl.ds(n * chunks, chunks), :])
                now = decay * h[n] + u * scalar_ref[t, b_at(n, eighth)]
                h_ref[aligned(((t + 1) * states + n) * chunks, chunks), :] = now
                terms.append(dy * now)
                out.append(now)
            h = tuple(out)
            put_sums(t, states, terms)
        return h

    lax.fori_loop(0, count // 2, recompute, zero)

    def retreat(back, carry):
        flows, totals = carry
        for slot in range(2):
            t = count - 1 - (2 * back + slot)
            span = pl.ds(t, chunks, stride=count)
            sp = sp_ref[span, :]
            u = u_ref[span, :]
            dy = dy_ref[span, :]
            out_flows = []
            out_totals = []
            terms = []
            d_sum = None
            s_sum = None
            for n in range(states):
                rate = decay_ref[pl.ds(n * chunks, chunks), :]
                dh = flows[n] + dy * scalar_ref[t, c_at(n, eighth)]
                flow = jnp.exp2(sp * rate) * dh
                out_flows.append(flow)
                q = flow * h_ref[aligned((t * states + n) * chunks, chunks), :]
                out_totals.append(totals[n] + q * sp)
                d_term = q * rate
                s_term = dh * scalar_ref[t, b_at(n, eighth)]
                d_sum = d_term if d_sum is None else d_sum + d_term
                s_sum = s_term if s_sum is None else s_sum + s_term
                terms.append(dh * u)
            s_ref[span, :] = s_sum
            d_ref[span, :] = d_sum
            put_sums(t, 0, terms)
            flows, totals = tuple(out_flows), tuple(out_totals)
        return flows, totals

    _, totals = lax.fori_loop(0, count // 2, retreat, (zero, zero))
    for n in range(states):
        alog_ref[pl.ds(n * chunks, chunks), :] = totals[n]

    rank = rank_ref[...]
    ranks = rank.shape[1]
    drank = None
    for chunk in range(chunks):
        cols = slice(chunk * LANES, (chunk + 1) * LANES)
        place = pl.ds(chunk * count, count)
        act = act_ref[:, cols].astype(F32)
        weight = dt_ref[:, lanes(2 * chunk + half)]
        pre = dot(rank, weight, 1, 0) + bias_ref[pl.ds(2 * chunk + half, 1), :]
        s_now = s_ref[place, :]
        dstep = d_ref[place, :] * (1.0 / LOG2E) + s_now * act
        sact_ref[:, cols] = s_now * softplus(pre)
        dpre = dstep * sigmoid(pre)
        vec_ref[0:1, cols] = jnp.sum(dpre, axis=0, keepdims=True)
        vec_ref[1:2, cols] = jnp.sum(dy_ref[place, :] * act, axis=0, keepdims=True)
        low = dpre.astype(BF16)
        dpre_ref[:, cols] = low
        term = dot(low, weight, 1, 1)
        drank = term if drank is None else drank + term
    source = lax.broadcasted_iota(jnp.int32, (2 * LANES, LANES), 0)
    target = lax.broadcasted_iota(jnp.int32, (2 * LANES, LANES), 1)
    code = None
    for n in range(states):
        pair = jnp.concatenate(
            [sums_ref[pl.ds((start + n) * pitch, count), :] for start in (0, states)], axis=1
        )
        column = ranks + jnp.where(source < LANES, b_at(n, eighth), c_at(n, eighth))
        pick = jnp.where(target == column, 1.0, 0.0).astype(BF16)
        term = dot(pair.astype(BF16), pick, 1, 0)
        code = term if code is None else code + term
    code_ref[...] = code + jnp.concatenate([drank, jnp.zeros((count, LANES - ranks), F32)], axis=1)


def scan_backward(place, micro, count, bc, decay, rank, dt, bias, act, sp, u, dy, code):
    rows, own = act.shape
    chunks = own // LANES
    states = bc.shape[1] // 2
    ranks = rank.shape[1]
    outs = [
        ((rows, LANES), F32),
        ((count, own), F32),
        ((count, own), BF16),
        ((states * chunks, LANES), F32),
        ((2, own), F32),
    ]

    def block(*shape):
        return pl.BlockSpec(shape, lambda i, p: (micro, 0))

    operands = (bc, decay, rank, dt, bias, act, sp, u, dy) + (() if code is None else (code,))
    return pl.pallas_call(
        functools.partial(backward_kernel, count=count, states=states, chunks=chunks),
        grid_spec=pltpu.PrefetchScalarGridSpec(
            num_scalar_prefetch=1,
            grid=(1,),
            in_specs=[
                block(count, 2 * states),
                whole(decay.shape),
                block(count, ranks),
                whole(dt.shape),
                whole(bias.shape),
                block(count, own),
                block(chunks * count, LANES),
                block(chunks * count, LANES),
                block(chunks * count, LANES),
            ]
            + [ANY] * (code is not None),
            out_specs=[block(count, LANES)] + [whole(shape) for shape, _ in outs[1:]],
            scratch_shapes=[
                pltpu.VMEM(((count + 1) * states * chunks, LANES), F32),
                pltpu.VMEM((chunks * count, LANES), F32),
                pltpu.VMEM((chunks * count, LANES), F32),
                pltpu.VMEM((2 * states * (count + 1), LANES), F32),
                pltpu.SMEM((count, 2 * states), F32),
                pltpu.SemaphoreType.DMA,
            ],
        ),
        out_shape=[hbm(*out) for out in outs],
        input_output_aliases={} if code is None else {len(operands): 0},
        compiler_params=params(26),
        cost_estimate=cost(0),
        name="scan_backward",
    )(place, *in_hbm(operands))


def tail_kernel(
    place_ref,
    len_ref,
    *refs,
    micros,
    count,
    taps,
    clusters,
    ranks,
    chunks,
    states,
):
    def take(number):
        nonlocal refs
        taken, refs = refs[:number], refs[number:]
        return taken

    code_own_ref, code_other_ref = take(2)
    sact_refs, dpre_refs, alog_refs, back_refs = (take(micros) for _ in range(4))
    dtx_ref, bc_own_ref, bc_other_ref, decay_ref = take(4)
    dy_refs = take(micros)
    conved_ref, inner_ref, act_ref, high_ref, convw_ref, skip_ref = take(6)
    normed_ref, weight_ref, share_ref, gain_ref = take(4)
    keep_ref, send_ref, low_ref = take(3)
    mask_ref, code_ref, wcode_ref, vec_ref, alog_ref, total_ref, win_ref, sems = refs

    step = pl.program_id(0)
    rows = micros * count
    eighth = states // 2
    edge = LANES // 2
    half, core, cube, face = (place_ref[k] for k in range(4))
    pair = step ^ face
    span = LANES + 32

    def fetch(k):
        source = weight_ref.at[0, pl.ds(2 * (k ^ face), 2), half]
        return (pltpu.make_async_copy(source, win_ref.at[k], sems.at[k]),)

    stream(step, win_ref.shape[0], fetch)

    def pack_row(chunk):
        relative = chunk ^ cube
        return (relative & 3) * span + LANES + (relative >> 2) * 16

    def place_pair(start, size, cols, even, odd):
        keep_ref[aligned(start, size, 16), cols] = jnp.where(core == 0, even, odd).astype(BF16)
        send_ref[aligned(start, size, 16), cols] = jnp.where(core == 0, odd, even).astype(BF16)

    @pl.when(step == 0)
    def _():
        fill_masks(len_ref, mask_ref, micros, count, taps, clusters)
        total_ref[...] = share_ref[...]
        code_ref[...] = (code_own_ref[...] + code_other_ref[...]).astype(BF16)
        total = None
        for micro in range(micros):
            term = alog_refs[micro][...]
            total = term if total is None else total + term
        alog_ref[...] = total * (decay_ref[...] * (1.0 / LOG2E))

    code = code_ref[...]
    lane = lax.broadcasted_iota(jnp.int32, (1, LANES), 1)
    code_rank = jnp.where(lane < ranks, code, jnp.zeros_like(code))
    dpre = jnp.concatenate([ref[...] for ref in dpre_refs], axis=0)
    for part in range(2):
        source = lanes(2 * (2 * pair + part) + half)
        cols = slice(part * LANES, (part + 1) * LANES)
        wcode_ref[:ranks, cols] = dtx_ref[:, source]
        own = bc_own_ref[:, :, source].reshape(states, LANES)
        other = bc_other_ref[:, :, source].reshape(states, LANES)
        wcode_ref[ranks : ranks + states, cols] = jnp.where(half == 0, own, other)
        wcode_ref[ranks + states : ranks + 2 * states, cols] = jnp.where(half == 0, other, own)
        wcode_ref[ranks + 2 * states :, cols] = jnp.zeros(
            (LANES - ranks - 2 * states, LANES), BF16
        )
    for part in range(2):
        cols = slice(part * LANES, (part + 1) * LANES)
        chunk = 2 * pair + part
        source = 2 * chunk + half
        weights = convw_ref[:, lanes(source)]
        sact = jnp.concatenate([ref[:, cols] for ref in sact_refs], axis=0)
        dy = jnp.concatenate([ref[pl.ds(part * count, count), :] for ref in dy_refs], axis=0)
        dact = sact + dot(code, wcode_ref[:, cols], 1, 0)
        dact = dact + dy * skip_ref[pl.ds(source, 1), :]
        conved = conved_ref[:, cols]
        sig = sigmoid(conved)
        dconv = dact * (sig * (1.0 + conved * (1.0 - sig)))
        inner = inner_ref[:, cols]
        dinner = weights[taps - 1 : taps] * dconv
        sums = [None] * (taps + 1)
        sums[taps - 1] = jnp.sum(dconv * inner, axis=0, keepdims=True)
        sums[taps] = jnp.sum(dconv, axis=0, keepdims=True)
        for back in range(1, taps):
            kept = dconv * mask_ref[back]
            dinner = dinner + weights[taps - 1 - back : taps - back] * pltpu.roll(
                kept, rows - back, 0
            )
            sums[taps - 1 - back] = jnp.sum(
                kept * pltpu.roll(inner, back, 0), axis=0, keepdims=True
            )
        for k in range(taps + 1):
            vec_ref[k : k + 1, lanes(chunk)] = sums[k]
        for k in range(2):
            total = None
            for ref in back_refs:
                term = ref[k : k + 1, lanes(chunk)]
                total = term if total is None else total + term
            vec_ref[taps + 1 + k : taps + 2 + k, lanes(chunk)] = total
        low_ref[:, cols] = dinner.astype(BF16)

        act = act_ref[:, cols]
        start = pack_row(chunk)
        rows_now = dot(act, code_rank, 0, 0) + dot(dpre[:, cols], high_ref[...], 0, 0)
        for k in range(4):
            place_pair(
                start,
                16,
                slice(k * LANES, (k + 1) * LANES),
                rows_now[k * 16 : (k + 1) * 16],
                rows_now[edge + k * 16 : edge + (k + 1) * 16],
            )
        state_rows = dot(code, act, 0, 0)[ranks : ranks + 2 * states]
        place_pair(
            start, 16, slice(4 * LANES, 5 * LANES), state_rows[:states], state_rows[states:]
        )

    normed = normed_ref[...]
    for part in range(2):
        grad = dot(low_ref[:, lanes(core ^ part)], normed, 0, 0)
        total_ref[...] += eight_rows(grad * win_ref[step, core ^ part].astype(F32))
        out_ref = (keep_ref, send_ref)[part]
        out_ref[aligned(step * span, LANES, 16), :] = grad.astype(BF16)

    @pl.when(step == pl.num_programs(0) - 1)
    def _():
        vec_ref[taps + 3 : taps + 4, :] = (
            jnp.sum(total_ref[...], axis=0, keepdims=True) / gain_ref[...]
        )
        is_gain = lax.broadcasted_iota(jnp.int32, (8, LANES), 0) == taps + 3
        for chunk in range(chunks):
            start = pack_row(chunk)
            vec = vec_ref[:, chunk * LANES : (chunk + 1) * LANES]
            far, farther = (pltpu.roll(vec, LANES - k * edge // 2, 1) for k in (1, 2))
            even = jnp.where(is_gain & (lane >= edge // 2), far, vec)
            odd = jnp.where(is_gain & (lane < edge // 2), far, farther)
            alog = [
                alog_ref[pl.ds(q * eighth * chunks + chunk, eighth, stride=chunks), :]
                for q in range(2)
            ]
            place_pair(
                start,
                16,
                slice(5 * LANES, 6 * LANES),
                jnp.concatenate([alog[0], even]),
                jnp.concatenate([alog[1], odd]),
            )
            blank = jnp.zeros((16, 2 * LANES), F32)
            place_pair(start, 16, slice(6 * LANES, 8 * LANES), blank, blank)


def tail(
    place,
    lengths,
    code_own,
    code_other,
    sact,
    dpre,
    alog,
    back,
    dtx,
    bc_own,
    bc_other,
    decay,
    dy,
    conved,
    inner,
    act,
    high,
    convw,
    skip,
    normed,
    w4,
    share,
    gain,
):
    rows, own = act.shape
    chunks = own // LANES
    width = normed.shape[1]
    micros, _, clusters = lengths.shape
    count = rows // micros
    taps = convw.shape[0]
    ranks = dtx.shape[0]
    states = decay.shape[0] // chunks
    cols = 2 * LANES
    extent = 4 * (LANES + 32)

    def by_cols(height):
        return pl.BlockSpec((height, cols), lambda i, p: (0, i ^ p[FACE]))

    def dy_spec(micro):
        return pl.BlockSpec(
            (2 * count, LANES), lambda i, p: (micro * (chunks // 2) + (i ^ p[FACE]), 0)
        )

    in_specs = (
        [pl.BlockSpec(memory_space=pltpu.SMEM)]
        + [whole((rows, LANES))] * 2
        + [by_cols(count)] * (2 * micros)
        + [whole(alog[0].shape)] * micros
        + [whole(back[0].shape)] * micros
        + [whole(array.shape) for array in (dtx, bc_own, bc_other, decay)]
        + [dy_spec(micro) for micro in range(micros)]
        + [by_cols(rows)] * 3
        + [whole(array.shape) for array in (high, convw, skip, normed)]
        + [
            ANY,
            whole(share.shape),
            whole(gain.shape),
        ]
    )
    return pl.pallas_call(
        functools.partial(
            tail_kernel,
            micros=micros,
            count=count,
            taps=taps,
            clusters=clusters,
            ranks=ranks,
            chunks=chunks,
            states=states,
        ),
        grid_spec=pltpu.PrefetchScalarGridSpec(
            num_scalar_prefetch=1,
            grid=(chunks // 2,),
            in_specs=in_specs,
            out_specs=[
                whole((extent, width)),
                whole((extent, width)),
                pl.BlockSpec((rows, cols), lambda i, p: (0, i ^ p[FACE])),
            ],
            scratch_shapes=[
                pltpu.VMEM((taps, rows, LANES), F32),
                pltpu.VMEM((rows, LANES), BF16),
                pltpu.VMEM((LANES, cols), BF16),
                pltpu.VMEM((8, own), F32),
                pltpu.VMEM((states * chunks, LANES), F32),
                pltpu.VMEM((8, width), F32),
                pltpu.VMEM((chunks // 2, 2, LANES, width), BF16),
                pltpu.SemaphoreType.DMA((chunks // 2,)),
            ],
        ),
        out_shape=[
            hbm((extent, width), BF16),
            hbm((extent, width), BF16),
            hbm((rows, own), BF16),
        ],
        compiler_params=params(30),
        cost_estimate=cost(7),
        name="tail",
    )(
        place,
        lengths,
        *in_hbm([code_own]),
        code_other,
        *in_hbm(
            (
                *sact,
                *dpre,
                *alog,
                *back,
                dtx,
                bc_own,
                bc_other,
                decay,
                *([dy] * micros),
                conved,
                inner,
                act,
                high,
                convw,
                skip,
                normed,
                w4,
                share,
                gain,
            )
        ),
    )


def fetch_halves(source, which, half, target_ref, sems):
    copies = []
    for k in range(target_ref.shape[0]):
        pair = pl.ds(2 * k, 2)
        block = source.at[pair, half] if which is None else source.at[which, pair, half]
        copies.append(pltpu.make_async_copy(block, target_ref.at[k], sems.at[k]))
    for copy in copies:
        copy.start()
    return copies


def products_kernel(
    place_ref,
    gated_ref,
    dgate_ref,
    out_ref,
    weight_ref,
    mixed_ref,
    dnormed_ref,
    wout_ref,
    wgate_ref,
    out_sems,
    gate_sems,
):
    half = place_ref[HALF]
    width = mixed_ref.shape[1]
    jobs = (
        (fetch_halves(out_ref, None, half, wout_ref, out_sems), gated_ref, wout_ref, mixed_ref),
        (fetch_halves(weight_ref, 1, half, wgate_ref, gate_sems), dgate_ref, wgate_ref, dnormed_ref),
    )
    for copies, left_ref, right_ref, result_ref in jobs:
        total = None
        for k, copy in enumerate(copies):
            copy.wait()
            left = left_ref[:, 2 * k * LANES : 2 * (k + 1) * LANES]
            term = dot(left, right_ref[k].reshape(-1, width), 1, 0)
            total = term if total is None else total + term
        result_ref[...] = total.astype(BF16)


def products(place, gated, dgate, wout3, w4):
    rows, own = gated.shape
    width = w4.shape[-1]
    pairs = own // (2 * LANES)
    return pl.pallas_call(
        products_kernel,
        grid_spec=pltpu.PrefetchScalarGridSpec(
            num_scalar_prefetch=1,
            grid=(1,),
            in_specs=[whole((rows, own)), whole((rows, own)), ANY, ANY],
            out_specs=[whole((rows, width))] * 2,
            scratch_shapes=[
                pltpu.VMEM((pairs, 2, LANES, width), BF16),
                pltpu.VMEM((pairs, 2, LANES, width), BF16),
                pltpu.SemaphoreType.DMA((pairs,)),
                pltpu.SemaphoreType.DMA((pairs,)),
            ],
        ),
        out_shape=[hbm((rows, width), BF16)] * 2,
        compiler_params=params(20),
        cost_estimate=cost(4),
        name="products",
    )(place, *in_hbm((gated, dgate, wout3, w4)))


def spread_kernel(place_ref, low_ref, weight_ref, gate_ref, dnormed_ref, win_ref, sems):
    width = gate_ref.shape[1]
    total = gate_ref[...].astype(F32)
    for k, copy in enumerate(fetch_halves(weight_ref, 0, place_ref[HALF], win_ref, sems)):
        copy.wait()
        left = low_ref[:, 2 * k * LANES : 2 * (k + 1) * LANES]
        total = total + dot(left, win_ref[k].reshape(-1, width), 1, 0)
    dnormed_ref[...] = total.astype(BF16)


def spread(place, low, w4, gate_part):
    rows, own = low.shape
    width = w4.shape[-1]
    pairs = own // (2 * LANES)
    return pl.pallas_call(
        spread_kernel,
        grid_spec=pltpu.PrefetchScalarGridSpec(
            num_scalar_prefetch=1,
            grid=(1,),
            in_specs=[whole((rows, own)), ANY, whole((rows, width))],
            out_specs=whole((rows, width)),
            scratch_shapes=[
                pltpu.VMEM((pairs, 2, LANES, width), BF16),
                pltpu.SemaphoreType.DMA((pairs,)),
            ],
        ),
        out_shape=hbm((rows, width), BF16),
        compiler_params=params(16),
        cost_estimate=cost(3),
        name="spread",
    )(place, *in_hbm((low, w4, gate_part)))


def finish_kernel(x_ref, mine_ref, theirs_ref, cotan_ref, gain_ref, grad_ref):
    x = x_ref[...].astype(F32)
    scale = lax.rsqrt(jnp.mean(x * x, axis=1, keepdims=True) + EPSILON)
    unit = x * scale
    dhat = (mine_ref[...].astype(F32) + theirs_ref[...].astype(F32)) * gain_ref[...]
    grad_ref[...] = cotan_ref[...].astype(F32) + scale * (
        dhat - unit * jnp.mean(dhat * unit, axis=1, keepdims=True)
    )


def finish(x, mine, theirs, cotan, gain):
    rows, width = x.shape
    by_rows = pl.BlockSpec((rows // 4, width), lambda i: (i, 0))
    return pl.pallas_call(
        finish_kernel,
        grid=(4,),
        in_specs=[by_rows] * 4 + [whole(gain.shape)],
        out_specs=by_rows,
        out_shape=jax.ShapeDtypeStruct((rows, width), F32),
        compiler_params=params(16),
        cost_estimate=cost(0),
        name="finish",
    )(*in_hbm((x, mine)), theirs, *in_hbm((cotan, gain)))


def unpack_kernel(
    near_ref,
    far_ref,
    out_ref,
    dtx_ref,
    dt_ref,
    bc_ref,
    alog_ref,
    convw_ref,
    convb_ref,
    bias_ref,
    skip_ref,
    out_grad_ref,
    *,
    eighth,
    taps,
    edge,
):
    pack = near_ref[...].astype(F32) + far_ref[...].astype(F32)
    for k in range(4):
        rows = pack[:, k * LANES : (k + 1) * LANES]
        dtx_ref[pl.ds(16 * k, 16), :] = rows[:, :edge]
        dt_ref[pl.ds(16 * k, 16), :] = pltpu.roll(rows, edge, 1)[:, :edge]
    rows = pack[:, 4 * LANES : 5 * LANES]
    bc_ref[0] = rows[:eighth]
    bc_ref[1] = rows[eighth:]
    rows = pack[:, 5 * LANES : 6 * LANES]
    alog_ref[...] = rows[:eighth]
    vec = rows[eighth:, :edge]
    convw_ref[...] = vec[:taps]
    convb_ref[...] = vec[taps : taps + 1]
    bias_ref[...] = vec[taps + 1 : taps + 2]
    skip_ref[...] = vec[taps + 2 : taps + 3]
    out_grad_ref[...] = out_ref[...].astype(F32)


def unpack(near, far, out, eighth, taps, ranks):
    edge = LANES // 2
    shapes = [
        (edge, ranks),
        (edge, ranks),
        (2, eighth, LANES),
        (eighth, LANES),
        (taps, edge),
        (1, edge),
        (1, edge),
        (1, edge),
        out.shape,
    ]
    return pl.pallas_call(
        functools.partial(unpack_kernel, eighth=eighth, taps=taps, edge=edge),
        grid=(1,),
        in_specs=[whole(array.shape) for array in (near, far, out)],
        out_specs=[whole(shape) for shape in shapes],
        out_shape=[jax.ShapeDtypeStruct(shape, F32) for shape in shapes],
        cost_estimate=cost(0),
        name="unpack",
    )(near, far, out)


def swap_pair(array):
    count = lax.axis_size("state")
    return lax.ppermute(array, "state", [(pos, pos ^ 1) for pos in range(count)])


def swap_bit(array, bits):
    return lax.ppermute(array, "dp", [(pos, pos ^ bits) for pos in range(lax.axis_size("dp"))])


def swap_both(array, bits=0):
    states = lax.axis_size("state")
    pairs = []
    for d in range(lax.axis_size("dp")):
        for s in range(states):
            pairs.append((d * states + s, (((d & ~1) | s) ^ bits) * states + (d & 1)))
    return lax.ppermute(array, ("dp", "state"), pairs)


def add_quarters(kept, got):
    extent = kept.shape[0] // 4
    return [kept[k * extent :][:extent] + got[k * extent :][:extent] for k in range(4)]


def trade_quarters(quarters):
    return [quarters[0]] + [swap_bit(quarters[k], k * X_BIT) for k in range(1, 4)]


def sum_quarters(quarters):
    left, right = (quarters[k].astype(F32) + quarters[k + 1].astype(F32) for k in (0, 2))
    return (left + right).astype(BF16)


CORE_BIT, X_BIT, ZH_BIT = 1, 2, 8


def shards(
    tokens,
    cluster_len,
    norm_gain,
    in_weight,
    conv_weight,
    conv_bias,
    dtx_weight,
    dt_weight,
    dt_bias,
    bc_weight,
    a_log,
    skip_gain,
    out_weight,
    cotangent,
):
    micros, count, width = tokens.shape
    inner = out_weight.shape[0]
    taps = conv_weight.shape[0]
    ranks = dtx_weight.shape[1]
    chunks = inner // (2 * LANES)
    own = chunks * LANES
    rows = micros * count
    edge = LANES // 2
    span = LANES + 32
    dp_parts = lax.axis_size("dp")
    state_count = lax.axis_size("state")
    dp_pos = lax.axis_index("dp")
    state_pos = lax.axis_index("state")
    half = state_pos & 1
    fast = state_count == 2 and dp_parts == 2 * chunks == 16
    if fast:
        place = jnp.stack([half, dp_pos & 1, dp_pos >> 1, (dp_pos >> 1) & 3])
        bc_own, alog_own = bc_weight, a_log
        bc_other, alog_other = swap_pair(bc_weight), swap_pair(a_log)
    else:
        place = jnp.stack([half, 0, 0, 0])
        bc_all = lax.all_gather(bc_weight, "state", axis=1, tiled=True)
        alog_all = lax.all_gather(a_log, "state", axis=0, tiled=True)
        eighth = alog_all.shape[0] // 2
        bc_own, bc_other = (
            lax.dynamic_slice_in_dim(bc_all, which * eighth, eighth, 1)
            for which in (half, 1 - half)
        )
        alog_own, alog_other = (
            lax.dynamic_slice_in_dim(alog_all, which * eighth, eighth, 0)
            for which in (half, 1 - half)
        )
    place = place.astype(jnp.int32)
    eighth = alog_own.shape[0]
    states = 2 * eighth

    x = tokens.reshape(rows, width)
    cotan = cotangent.reshape(rows, width)
    w4 = in_weight.reshape(2, chunks, 2, LANES, width)
    wout3 = out_weight.reshape(chunks, 2, LANES, width)
    dtx, dt = dtx_weight.T, dt_weight.T
    bias = dt_bias.reshape(-1, LANES)
    skip = skip_gain.reshape(-1, LANES)

    normed, act_all, act, inner_own, conved, gate = project(
        place, cluster_len, x, norm_gain[None], w4, conv_weight, conv_bias.reshape(-1, LANES)
    )
    bc, rank, high, decay, sp, u, dy, gated, dgate, keep, send, share = scan_forward(
        place,
        cluster_len,
        act_all,
        bc_own,
        bc_other,
        alog_own,
        alog_other,
        dtx,
        dt,
        bias,
        skip,
        act,
        gate,
        wout3,
        cotan,
        normed,
        w4,
    )
    if fast:
        early = swap_bit(send, CORE_BIT)
    mixed_part, dn_gate = products(place, gated, dgate, wout3, w4)
    if fast:
        *quarters, mixed_part, dn_gate, sp = lax.optimization_barrier(
            (*add_quarters(keep, early), mixed_part, dn_gate, sp)
        )
        early_got = trade_quarters(quarters)
    mixed_other = swap_pair(mixed_part)
    code_own = None
    results = []
    for micro in range(micros):
        if fast and micro == micros - 1:
            block = sum_quarters(early_got)
            out_keep, out_send, gate_sum = block[:edge], block[edge:LANES], block[LANES:]
            out_send, gate_sum, sp = lax.optimization_barrier((out_send, gate_sum, sp))
            out_got = swap_bit(out_send, ZH_BIT)
        code_own, *rest = scan_backward(
            place, micro, count, bc, decay, rank, dt, bias, act, sp, u, dy, code_own
        )
        results.append(rest)
    sact, dpre, alog, back = zip(*results)
    code_other = swap_pair(code_own)
    if fast:
        out_got, mixed_other, conved = lax.optimization_barrier((out_got, mixed_other, conved))
    late_keep, late_send, low = tail(
        place,
        cluster_len,
        code_own,
        code_other,
        sact,
        dpre,
        alog,
        back,
        dtx,
        bc_own,
        bc_other,
        decay,
        dy,
        conved,
        inner_own,
        act,
        high,
        conv_weight,
        skip,
        normed,
        w4,
        share,
        norm_gain[None],
    )
    if fast:
        late = swap_bit(late_send, CORE_BIT)
        out_own = swap_both(out_keep + out_got)
        late_got = trade_quarters(add_quarters(late_keep, late))
    dnormed_part = spread(place, low, w4, dn_gate)
    dnormed_other = swap_pair(dnormed_part)
    mixed = (x.astype(F32) + (mixed_part.astype(F32) + mixed_other.astype(F32))).astype(BF16)
    if fast:
        *late_got, mixed, out_own, dnormed_other = lax.optimization_barrier(
            (*late_got, mixed, out_own, dnormed_other)
        )
        block = sum_quarters(late_got)
        inner_sum = block[:LANES]
        upper = dp_pos >= dp_parts // 2
        crossing = jnp.where(upper, inner_sum, gate_sum)
        first, second = crossing[:edge], crossing[edge:]
        first, pack_far, pack_near = lax.optimization_barrier(
            (first, block[-16:], block[LANES:-16])
        )
        pack_far = swap_both(pack_far, ZH_BIT)
        first_got = swap_bit(first, ZH_BIT)
        pack_near = swap_both(pack_near)
        first_got, pack_far, pack_near = lax.optimization_barrier((first_got, pack_far, pack_near))
        second_got = swap_bit(second, ZH_BIT)
        tokens_grad = finish(x, dnormed_part, dnormed_other, cotan, norm_gain[None])
        gain_mine = (
            pack_near[:, 5 * LANES : 6 * LANES].astype(F32)
            + pack_far[:, 5 * LANES : 6 * LANES].astype(F32)
        ).astype(BF16)
        gain_both = gain_mine[-1].astype(F32) + swap_bit(gain_mine, CORE_BIT)[-1].astype(F32)
        extent = width // (dp_parts * state_count)
        gain_grad = lax.dynamic_slice_in_dim(gain_both, (dp_pos & 1) * extent, extent, 0)
        (
            dtx_grad,
            dt_grad,
            bc_grad,
            alog_grad,
            convw_grad,
            convb_grad,
            bias_grad,
            skip_grad,
            out_own,
        ) = unpack(pack_near, pack_far, out_own, eighth, taps, ranks)
        convb_grad, bias_grad, skip_grad = (
            array[0] for array in (convb_grad, bias_grad, skip_grad)
        )
        in_grad = jnp.where(upper, gate_sum, inner_sum).astype(F32) + jnp.concatenate(
            [first_got, second_got]
        ).astype(F32)
    else:
        tokens_grad = finish(x, dnormed_part, dnormed_other, cotan, norm_gain[None])
    mixed = mixed.reshape(micros, count, width)
    tokens_grad = tokens_grad.reshape(micros, count, width)

    if not fast:
        def total(array):
            return lax.psum(array.astype(F32), "dp")

        def both_rows(array):
            mine = array.reshape(chunks, 1, LANES, -1)
            other = swap_pair(mine)
            low = jnp.where(half == 0, mine, other)
            high = jnp.where(half == 0, other, mine)
            return jnp.concatenate([low, high], axis=1).reshape(2 * own, -1)

        every = dp_parts * state_count
        at = dp_pos * state_count + state_pos

        def cut_own(array):
            extent = array.shape[0] // every
            return lax.dynamic_slice_in_dim(array, at * extent, extent, 0)

        pair = total(jnp.stack([keep, send])).reshape(2, 2, 2, 2 * LANES, width)
        outs = pair[:, :, :, :LANES].reshape(2, 2, 2, 2, edge, width)
        outs = jnp.transpose(outs, (3, 1, 2, 0, 4, 5)).reshape(own, width)
        gates = jnp.moveaxis(pair[:, :, :, LANES:], 0, 2).reshape(own, width)
        pair = total(jnp.stack([late_keep, late_send])).reshape(2, 2, 2, span, width)
        inners = jnp.moveaxis(pair[:, :, :, :LANES], 0, 2).reshape(own, width)
        packs = pair[:, :, :, LANES:].reshape(2, 2, 2, 2, 16, width // LANES, LANES)
        packs = jnp.transpose(packs, (3, 1, 2, 0, 5, 4, 6)).reshape(chunks, 2, -1, 16, LANES)
        small = both_rows(packs[:, :, :4].reshape(own, LANES))
        in_grad = cut_own(jnp.concatenate([both_rows(inners), both_rows(gates)]))
        out_own = cut_own(both_rows(outs))
        mine = cut_own(small)
        dtx_grad, dt_grad = mine[:, :ranks], mine[:, ranks:]
        vec_rows = jnp.swapaxes(packs[:, :, 5, eighth:, :edge], 2, 3).reshape(own, -1)
        gain_sum = vec_rows[:, -1].reshape(chunks, 2, 2, -1).swapaxes(1, 2).reshape(-1)
        gain_grad = cut_own(gain_sum + swap_pair(gain_sum))
        vec = cut_own(both_rows(vec_rows)).T
        state_rows = jnp.concatenate([packs[:, :, 4], packs[:, :, 5, :eighth]], axis=2)
        state_rows = state_rows.reshape(chunks, 2, 3, eighth, LANES)
        state_rows = jnp.transpose(state_rows, (0, 4, 2, 1, 3)).reshape(own, -1)
        extent = inner // dp_parts
        state_part = lax.dynamic_slice_in_dim(both_rows(state_rows), dp_pos * extent, extent, 0)
        state_part = state_part.T.reshape(3, state_count, -1, extent)
        state_part = lax.dynamic_index_in_dim(state_part, state_pos, 1, keepdims=False)
        bc_grad, alog_grad = state_part[:2], state_part[2]
        convw_grad, convb_grad, bias_grad, skip_grad = (
            vec[:taps], vec[taps], vec[taps + 1], vec[taps + 2]
        )

    return (
        mixed,
        tokens_grad,
        gain_grad,
        in_grad,
        convw_grad,
        convb_grad,
        dtx_grad,
        dt_grad,
        bias_grad,
        bc_grad,
        alog_grad,
        skip_grad,
        out_own,
    )


def solution(mesh):
    return jax.shard_map(
        shards,
        mesh=mesh,
        in_specs=(
            P(None, "dp", None),
            P(None, "dp", None),
            P(),
            P(),
            P(),
            P(),
            P(),
            P(),
            P(),
            P(None, "state", None),
            P("state", None),
            P(),
            P(),
            P(None, "dp", None),
        ),
        out_specs=(
            P(None, "dp", None),
            P(None, "dp", None),
            P(("dp", "state")),
            P(("dp", "state"), None),
            P(None, ("dp", "state")),
            P(("dp", "state")),
            P(("dp", "state"), None),
            P(("dp", "state"), None),
            P(("dp", "state")),
            P(None, "state", "dp"),
            P("state", "dp"),
            P(("dp", "state")),
            P(("dp", "state"), None),
        ),
        check_vma=False,
    )
```

```python
import functools
import math

import jax
import jax.numpy as jnp
from jax import lax
from jax.experimental import pallas as pl
from jax.experimental.pallas import tpu as pltpu
from jax.sharding import PartitionSpec as P

EPSILON = 1e-05
LANES = 128
RESET = 1e4
LOG2E = math.log2(math.e)
F32 = jnp.float32
BF16 = jnp.bfloat16
MIB = 1024 * 1024


def dot(left, right, left_dim, right_dim):
    return lax.dot_general(
        left, right, (((left_dim,), (right_dim,)), ((), ())), preferred_element_type=F32
    )


def params(mib):
    return pltpu.CompilerParams(
        vmem_limit_bytes=mib * MIB, dimension_semantics=("arbitrary",)
    )


ANY = pl.BlockSpec(memory_space=pl.ANY)


def stream(step, steps, fetch):
    @pl.when(step == 0)
    def _():
        for k in range(steps):
            for copy in fetch(k):
                copy.start()

    for copy in fetch(step):
        copy.wait()


def whole(shape):
    return pl.BlockSpec(shape, lambda *_: (0,) * len(shape))


sigmoid = jax.nn.sigmoid


def softplus(value):
    return jnp.maximum(value, 0.0) + jnp.log1p(jnp.exp(-jnp.abs(value)))


def lanes(index):
    return pl.ds(pl.multiple_of(index * LANES, LANES), LANES)


def cost(micros):
    return pl.CostEstimate(
        flops=int(micros * 1e9), bytes_accessed=int(micros * 1e6), transcendentals=0
    )


def hbm(shape, dtype):
    return pltpu.HBM(shape, dtype)


def in_hbm(arrays):
    return [pltpu.with_memory_space_constraint(array, pltpu.HBM) for array in arrays]


def aligned(start, size, to=8):
    return pl.ds(pl.multiple_of(start, to), size)


HALF, CORE, CUBE, FACE = range(4)


def fill_masks(len_ref, mask_ref, micros, count, taps, clusters):
    place = lax.broadcasted_iota(jnp.int32, (count, LANES), 0)
    for micro in range(micros):
        rows = pl.ds(micro * count, count)
        for back in range(1, taps):
            apart = place < back
            start = 0
            for cluster in range(clusters - 1):
                start = start + len_ref[micro, 0, cluster]
                apart = apart | ((place >= start) & (place < start + back))
            mask_ref[back, rows, :] = jnp.where(apart, 0.0, 1.0)
            if back == 1:
                mask_ref[0, rows, :] = jnp.where(apart, 1.0, 0.0)


def project_kernel(
    place_ref,
    len_ref,
    x_ref,
    gain_ref,
    weight_ref,
    convw_ref,
    convb_ref,
    normed_ref,
    act_ref,
    own_act_ref,
    inner_ref,
    conved_ref,
    gate_ref,
    mask_ref,
    proj_ref,
    conv_ref,
    win_ref,
    wgate_ref,
    sems,
    *,
    micros,
    count,
    taps,
    clusters,
):
    chunk = pl.program_id(0)

    @pl.when(chunk == 0)
    def _():
        fill_masks(len_ref, mask_ref, micros, count, taps, clusters)
        rows = x_ref[...].astype(F32)
        scale = lax.rsqrt(jnp.mean(rows * rows, axis=1, keepdims=True) + EPSILON)
        normed_ref[...] = (rows * scale * gain_ref[...]).astype(BF16)

    half = place_ref[HALF]

    def fetch(k):
        return (
            pltpu.make_async_copy(weight_ref.at[0, k], win_ref.at[k], sems.at[0, k]),
            pltpu.make_async_copy(weight_ref.at[1, k, half], wgate_ref.at[k], sems.at[1, k]),
        )

    stream(chunk, win_ref.shape[0], fetch)
    normed = normed_ref[...]
    proj_ref[...] = dot(normed, win_ref[chunk].reshape(2 * LANES, -1), 1, 1)
    gate_ref[...] = dot(normed, wgate_ref[chunk], 1, 1)
    for part in range(2):
        cols = pl.ds(part * LANES, LANES)
        inner = proj_ref[:, cols]
        conved = convb_ref[pl.ds(2 * chunk + part, 1), :] + convw_ref[taps - 1 : taps, cols] * inner
        for back in range(1, taps):
            shifted = pltpu.roll(inner, back, 0) * mask_ref[back]
            conved = conved + convw_ref[taps - 1 - back : taps - back, cols] * shifted
        conv_ref[:, cols] = conved
        act_ref[:, cols] = (conved * sigmoid(conved)).astype(BF16)
    own = lanes(half)
    inner_ref[...] = proj_ref[:, own]
    conved_ref[...] = conv_ref[:, own]
    own_act_ref[...] = act_ref[:, own]


def project(place, lengths, x, gain, w4, conv_weight, conv_bias):
    rows, width = x.shape
    chunks = w4.shape[1]
    inner = chunks * 2 * LANES
    micros, _, clusters = lengths.shape
    taps = conv_weight.shape[0]
    own = chunks * LANES
    by_chunk = pl.BlockSpec((rows, LANES), lambda i, p: (0, i))
    return pl.pallas_call(
        functools.partial(
            project_kernel, micros=micros, count=rows // micros, taps=taps, clusters=clusters
        ),
        grid_spec=pltpu.PrefetchScalarGridSpec(
            num_scalar_prefetch=1,
            grid=(chunks,),
            in_specs=[
                pl.BlockSpec(memory_space=pltpu.SMEM),
                whole((rows, width)),
                whole((1, width)),
                ANY,
                pl.BlockSpec((taps, 2 * LANES), lambda i, p: (0, i)),
                whole(conv_bias.shape),
            ],
            out_specs=[
                whole((rows, width)),
                pl.BlockSpec((rows, 2 * LANES), lambda i, p: (0, i)),
                by_chunk,
                by_chunk,
                by_chunk,
                by_chunk,
            ],
            scratch_shapes=[
                pltpu.VMEM((taps, rows, LANES), F32),
                pltpu.VMEM((rows, 2 * LANES), F32),
                pltpu.VMEM((rows, 2 * LANES), F32),
                pltpu.VMEM((chunks, 2, LANES, width), BF16),
                pltpu.VMEM((chunks, LANES, width), BF16),
                pltpu.SemaphoreType.DMA((2, chunks)),
            ],
        ),
        out_shape=[
            hbm((rows, width), BF16),
            hbm((rows, inner), BF16),
            hbm((rows, own), BF16),
            hbm((rows, own), F32),
            hbm((rows, own), F32),
            hbm((rows, own), F32),
        ],
        compiler_params=params(20),
        cost_estimate=cost(6),
        name="project",
    )(place, *in_hbm((lengths, x, gain, w4, conv_weight, conv_bias)))


def eight_rows(array):
    return jnp.sum(array.reshape(-1, 8, array.shape[1]), axis=0)


def every_row(ref, row, height):
    return ref[pl.ds(row, height, stride=0), :]


def b_at(n, eighth):
    return (n // eighth) * 2 * eighth + n % eighth


def c_at(n, eighth):
    return b_at(n, eighth) + eighth


def forward_kernel(
    place_ref,
    len_ref,
    act_all_ref,
    bc_own_ref,
    bc_other_ref,
    alog_own_ref,
    alog_other_ref,
    dtx_ref,
    dt_ref,
    bias_ref,
    skip_ref,
    act_ref,
    gate_ref,
    wout_ref,
    cotan_ref,
    normed_ref,
    wgate_ref,
    bc_ref,
    rank_ref,
    rank_high_ref,
    decay_ref,
    sp_ref,
    u_ref,
    dy_ref,
    gated_ref,
    dgate_ref,
    keep_ref,
    send_ref,
    share_ref,
    mask_ref,
    y_ref,
    tmp_ref,
    wide_ref,
    *,
    micros,
    count,
    states,
    chunks,
    clusters,
):
    rows = micros * count
    eighth = states // 2
    half, core, cube, face = (place_ref[k] for k in range(4))
    first = half == 0
    act_all = act_all_ref[...]
    own = dot(act_all, bc_own_ref[...].reshape(states, -1), 1, 1)
    other = dot(act_all, bc_other_ref[...].reshape(states, -1), 1, 1)
    bc_ref[:, :states] = jnp.where(first, own, other)
    bc_ref[:, states:] = jnp.where(first, other, own)
    spread_lanes(bc_ref, wide_ref)

    fill_masks(len_ref, mask_ref, micros, count, 2, clusters)
    for chunk in range(chunks):
        cols = lanes(2 * chunk + half)
        own, other = alog_own_ref[:, cols], alog_other_ref[:, cols]
        tmp_ref[pl.ds(chunk * states, eighth), :] = jnp.where(first, own, other)
        tmp_ref[pl.ds(chunk * states + eighth, eighth), :] = jnp.where(first, other, own)
    for n in range(states):
        decay_ref[pl.ds(n * chunks, chunks), :] = -LOG2E * jnp.exp(
            tmp_ref[pl.ds(n, chunks, stride=states), :]
        )

    rank = dot(act_all, dtx_ref[...], 1, 1).astype(BF16)
    rank_ref[...] = rank
    rank_high_ref[...] = jnp.concatenate([jnp.zeros_like(rank), rank], axis=1)
    for chunk in range(chunks):
        cols = slice(chunk * LANES, (chunk + 1) * LANES)
        bias = bias_ref[pl.ds(2 * chunk + half, 1), :]
        step = softplus(dot(rank, dt_ref[:, lanes(2 * chunk + half)], 1, 0) + bias)
        held = step + RESET * mask_ref[0]
        source = step * act_ref[:, cols].astype(F32)
        for micro in range(micros):
            span = slice(micro * count, (micro + 1) * count)
            place = pl.ds((micro * chunks + chunk) * count, count)
            sp_ref[place, :] = held[span]
            u_ref[place, :] = source[span]

    for micro in range(micros):

        def advance(t, h, micro=micro):
            row = micro * count + t
            span = pl.ds(micro * chunks * count + t, chunks, stride=count)
            sp = sp_ref[span, :]
            u = u_ref[span, :]
            out = []
            y = None
            for n in range(states):
                decay = jnp.exp2(sp * decay_ref[pl.ds(n * chunks, chunks), :])
                now = decay * h[n] + u * every_row(wide_ref, b_at(n, eighth) * rows + row, chunks)
                out.append(now)
                term = now * every_row(wide_ref, c_at(n, eighth) * rows + row, chunks)
                y = term if y is None else y + term
            y_ref[span, :] = y
            return tuple(out)

        lax.fori_loop(0, count, advance, (jnp.zeros((chunks, LANES), F32),) * states, unroll=2)

    cotan = cotan_ref[...]
    for chunk in range(chunks):
        cols = slice(chunk * LANES, (chunk + 1) * LANES)
        places = [pl.ds((micro * chunks + chunk) * count, count) for micro in range(micros)]
        y = jnp.concatenate([y_ref[place, :] for place in places])
        y = y + skip_ref[pl.ds(2 * chunk + half, 1), :] * act_ref[:, cols].astype(F32)
        gate = gate_ref[:, cols]
        sig = sigmoid(gate)
        gated_ref[:, cols] = (y * (gate * sig)).astype(BF16)
        dgated = dot(cotan, wout_ref[chunk, 0], 1, 1)
        dy = dgated * (gate * sig)
        for micro in range(micros):
            dy_ref[places[micro], :] = dy[micro * count : (micro + 1) * count]
        dgate_ref[:, cols] = (dgated * y * (sig * (1.0 + gate * (1.0 - sig)))).astype(BF16)
    normed = normed_ref[...]
    edge = LANES // 2
    for j in range(chunks):
        grad = dot(gated_ref[:, lanes(j ^ cube)], cotan, 0, 0).astype(BF16)
        top, bottom = grad[:edge], grad[edge:]
        place = pl.ds((j & 3) * 2 * LANES + (j >> 2) * edge, edge)
        keep_ref[place, :] = jnp.where(core == 0, top, bottom)
        send_ref[place, :] = jnp.where(core == 0, bottom, top)
    share = jnp.zeros(share_ref.shape, F32)
    for j in range(chunks // 2):
        place = pl.ds((2 * j + 1) * LANES, LANES)
        pair = 2 * (j ^ face)
        for chunk, out_ref in ((pair + core, keep_ref), (pair + 1 - core, send_ref)):
            grad = dot(dgate_ref[:, lanes(chunk)], normed, 0, 0)
            share = share + eight_rows(grad * wgate_ref[0, chunk, 0].astype(F32))
            out_ref[place, :] = grad.astype(BF16)
    share_ref[...] = share


def scan_forward(
    place,
    lengths,
    act_all,
    bc_own,
    bc_other,
    alog_own,
    alog_other,
    dtx,
    dt,
    bias,
    skip,
    act,
    gate,
    wout3,
    cotan,
    normed,
    w4,
):
    rows, own = act.shape
    chunks = own // LANES
    states = 2 * alog_own.shape[0]
    width = cotan.shape[1]
    micros, _, clusters = lengths.shape
    ranks = dtx.shape[0]
    outs = [
        ((rows, 2 * states), F32),
        ((rows, ranks), BF16),
        ((rows, 2 * ranks), BF16),
        ((states * chunks, LANES), F32),
        ((chunks * rows, LANES), F32),
        ((chunks * rows, LANES), F32),
        ((chunks * rows, LANES), F32),
        ((rows, own), BF16),
        ((rows, own), BF16),
        ((own, width), BF16),
        ((own, width), BF16),
        ((8, width), F32),
    ]
    operands = (
        act_all, bc_own, bc_other, alog_own, alog_other, dtx, dt, bias, skip, act, gate
    )
    return pl.pallas_call(
        functools.partial(
            forward_kernel,
            micros=micros,
            count=rows // micros,
            states=states,
            chunks=chunks,
            clusters=clusters,
        ),
        grid_spec=pltpu.PrefetchScalarGridSpec(
            num_scalar_prefetch=1,
            grid=(1,),
            in_specs=[pl.BlockSpec(memory_space=pltpu.SMEM)]
            + [whole(operand.shape) for operand in operands]
            + [
                pl.BlockSpec((chunks, 1, LANES, width), lambda i, p: (0, p[HALF], 0, 0)),
                whole((rows, width)),
                whole((rows, width)),
                pl.BlockSpec((1, chunks, 1, LANES, width), lambda i, p: (1, 0, p[HALF], 0, 0)),
            ],
            out_specs=[whole(shape) for shape, _ in outs],
            scratch_shapes=[
                pltpu.VMEM((2, rows, LANES), F32),
                pltpu.VMEM((chunks * rows, LANES), F32),
                pltpu.VMEM((states * chunks, LANES), F32),
                pltpu.VMEM((2 * states * rows, LANES), F32),
            ],
        ),
        out_shape=[hbm(*out) for out in outs],
        compiler_params=params(52),
        cost_estimate=cost(19),
        name="scan_forward",
    )(
        place,
        lengths,
        *in_hbm(operands[:1]),
        *operands[1:5],
        *in_hbm((*operands[5:], wout3, cotan, normed, w4)),
    )


def spread_lanes(values_ref, wide_ref):
    rows, count = values_ref.shape
    for k in range(count):
        wide_ref[pl.ds(k * rows, rows), :] = jnp.broadcast_to(
            values_ref[:, k : k + 1], (rows, LANES)
        )


def backward_kernel(
    place_ref,
    bc_ref,
    decay_ref,
    rank_ref,
    dt_ref,
    bias_ref,
    act_ref,
    sp_ref,
    u_ref,
    dy_ref,
    *refs,
    count,
    states,
    chunks,
):
    code_ref, sact_ref, dpre_ref, alog_ref, vec_ref = refs[-13:-8]
    h_ref, keep_ref, s_ref, d_ref, terms_ref, sums_b_ref, sums_c_ref, wide_ref = refs[-8:]
    half = place_ref[HALF]
    eighth = states // 2
    zero = (jnp.zeros((chunks, LANES), F32),) * states
    for n in range(states):
        h_ref[pl.ds(n * chunks, chunks), :] = zero[0]
    spread_lanes(bc_ref, wide_ref)
    block = states * chunks

    def put_terms(which, t, terms):
        for n in range(0, states, 2):
            pair = jnp.concatenate(terms[n : n + 2]).astype(BF16)
            terms_ref[which, aligned(t * block + n * chunks, 2 * chunks, 16), :] = pair

    def recompute(pair, h):
        for slot in range(2):
            t = 2 * pair + slot
            span = pl.ds(t, chunks, stride=count)
            sp = sp_ref[span, :]
            u = u_ref[span, :]
            dy = dy_ref[span, :]
            out = []
            terms = []
            for n in range(states):
                decay = jnp.exp2(sp * decay_ref[pl.ds(n * chunks, chunks), :])
                keep_ref[aligned(t * block + n * chunks, chunks), :] = decay
                now = decay * h[n] + u * every_row(wide_ref, b_at(n, eighth) * count + t, chunks)
                h_ref[aligned((t + 1) * block + n * chunks, chunks), :] = now
                terms.append(dy * now)
                out.append(now)
            h = tuple(out)
            put_terms(1, t, terms)
        return h

    lax.fori_loop(0, count // 2, recompute, zero)

    def retreat(back, carry):
        flows, totals = carry
        for slot in range(2):
            t = count - 1 - (2 * back + slot)
            span = pl.ds(t, chunks, stride=count)
            sp = sp_ref[span, :]
            u = u_ref[span, :]
            dy = dy_ref[span, :]
            out_flows = []
            out_totals = []
            terms = []
            d_sum = None
            s_sum = None
            for n in range(states):
                dh = flows[n] + dy * every_row(wide_ref, c_at(n, eighth) * count + t, chunks)
                place = aligned(t * block + n * chunks, chunks)
                flow = keep_ref[place, :] * dh
                out_flows.append(flow)
                q = flow * h_ref[place, :]
                out_totals.append(totals[n] + q * sp)
                d_term = q * decay_ref[pl.ds(n * chunks, chunks), :]
                s_term = dh * every_row(wide_ref, b_at(n, eighth) * count + t, chunks)
                d_sum = d_term if d_sum is None else d_sum + d_term
                s_sum = s_term if s_sum is None else s_sum + s_term
                terms.append(dh * u)
            s_ref[span, :] = s_sum
            d_ref[span, :] = d_sum
            put_terms(0, t, terms)
            flows, totals = tuple(out_flows), tuple(out_totals)
        return flows, totals

    _, totals = lax.fori_loop(0, count // 2, retreat, (zero, zero))
    for n in range(states):
        alog_ref[pl.ds(n * chunks, chunks), :] = totals[n]

    shape = (2 * states, 2 * block)
    group = lax.broadcasted_iota(jnp.int32, shape, 1) // chunks
    gather = jnp.where(group == lax.broadcasted_iota(jnp.int32, shape, 0), 1.0, 0.0).astype(BF16)

    @pl.loop(0, count // 16)
    def _(step):
        for which, sums_ref in ((0, sums_b_ref), (1, sums_c_ref)):
            for k in range(8):
                at = 8 * step + k
                terms = terms_ref[which, aligned(at * 2 * block, 2 * block, 16), :]
                sums_ref[aligned(at * 2 * states, 2 * states), :] = dot(gather, terms, 1, 0)

    rank = rank_ref[...]
    ranks = rank.shape[1]
    drank = None
    for chunk in range(chunks):
        cols = slice(chunk * LANES, (chunk + 1) * LANES)
        place = pl.ds(chunk * count, count)
        act = act_ref[:, cols].astype(F32)
        weight = dt_ref[:, lanes(2 * chunk + half)]
        pre = dot(rank, weight, 1, 0) + bias_ref[pl.ds(2 * chunk + half, 1), :]
        s_now = s_ref[place, :]
        dstep = d_ref[place, :] * (1.0 / LOG2E) + s_now * act
        sact_ref[:, cols] = s_now * softplus(pre)
        dpre = dstep * sigmoid(pre)
        vec_ref[0:1, cols] = jnp.sum(dpre, axis=0, keepdims=True)
        vec_ref[1:2, cols] = jnp.sum(dy_ref[place, :] * act, axis=0, keepdims=True)
        low = dpre.astype(BF16)
        dpre_ref[:, cols] = low
        term = dot(low, weight, 1, 1)
        drank = term if drank is None else drank + term
    source = lax.broadcasted_iota(jnp.int32, (2 * LANES, LANES), 0)
    target = lax.broadcasted_iota(jnp.int32, (2 * LANES, LANES), 1)
    code = None
    for n in range(states):
        pair = jnp.concatenate(
            [ref[pl.ds(n, count, stride=states), :] for ref in (sums_b_ref, sums_c_ref)], axis=1
        )
        column = ranks + jnp.where(source < LANES, b_at(n, eighth), c_at(n, eighth))
        pick = jnp.where(target == column, 1.0, 0.0).astype(BF16)
        term = dot(pair.astype(BF16), pick, 1, 0)
        code = term if code is None else code + term
    code_ref[...] = code + jnp.concatenate([drank, jnp.zeros((count, LANES - ranks), F32)], axis=1)


def scan_backward(place, micro, count, bc, decay, rank, dt, bias, act, sp, u, dy, code):
    rows, own = act.shape
    chunks = own // LANES
    states = bc.shape[1] // 2
    ranks = rank.shape[1]
    outs = [
        ((rows, LANES), F32),
        ((count, own), F32),
        ((count, own), BF16),
        ((states * chunks, LANES), F32),
        ((2, own), F32),
    ]

    def block(*shape):
        return pl.BlockSpec(shape, lambda i, p: (micro, 0))

    operands = (bc, decay, rank, dt, bias, act, sp, u, dy) + (() if code is None else (code,))
    return pl.pallas_call(
        functools.partial(backward_kernel, count=count, states=states, chunks=chunks),
        grid_spec=pltpu.PrefetchScalarGridSpec(
            num_scalar_prefetch=1,
            grid=(1,),
            in_specs=[
                block(count, 2 * states),
                whole(decay.shape),
                block(count, ranks),
                whole(dt.shape),
                whole(bias.shape),
                block(count, own),
                block(chunks * count, LANES),
                block(chunks * count, LANES),
                block(chunks * count, LANES),
            ]
            + [ANY] * (code is not None),
            out_specs=[block(count, LANES)] + [whole(shape) for shape, _ in outs[1:]],
            scratch_shapes=[
                pltpu.VMEM(((count + 1) * states * chunks, LANES), F32),
                pltpu.VMEM((count * states * chunks, LANES), F32),
                pltpu.VMEM((chunks * count, LANES), F32),
                pltpu.VMEM((chunks * count, LANES), F32),
                pltpu.VMEM((2, count * states * chunks, LANES), BF16),
                pltpu.VMEM((count * states, LANES), F32),
                pltpu.VMEM((count * states, LANES), F32),
                pltpu.VMEM((2 * states * count, LANES), F32),
            ],
        ),
        out_shape=[hbm(*out) for out in outs],
        input_output_aliases={} if code is None else {len(operands): 0},
        compiler_params=params(48),
        cost_estimate=cost(0),
        name="scan_backward",
    )(place, *in_hbm(operands))


def tail_kernel(
    place_ref,
    len_ref,
    *refs,
    micros,
    count,
    taps,
    clusters,
    ranks,
    chunks,
    states,
):
    def take(number):
        nonlocal refs
        taken, refs = refs[:number], refs[number:]
        return taken

    code_own_ref, code_other_ref = take(2)
    sact_refs, dpre_refs, alog_refs, back_refs = (take(micros) for _ in range(4))
    dtx_ref, bc_own_ref, bc_other_ref, decay_ref = take(4)
    dy_refs = take(micros)
    conved_ref, inner_ref, act_ref, high_ref, convw_ref, skip_ref = take(6)
    normed_ref, weight_ref, share_ref, gain_ref = take(4)
    keep_ref, send_ref, low_ref = take(3)
    mask_ref, code_ref, wcode_ref, vec_ref, alog_ref, total_ref, win_ref, sems = refs

    step = pl.program_id(0)
    rows = micros * count
    eighth = states // 2
    edge = LANES // 2
    half, core, cube, face = (place_ref[k] for k in range(4))
    pair = step ^ face
    span = LANES + 32

    def fetch(k):
        source = weight_ref.at[0, pl.ds(2 * (k ^ face), 2), half]
        return (pltpu.make_async_copy(source, win_ref.at[k], sems.at[k]),)

    stream(step, win_ref.shape[0], fetch)

    def pack_row(chunk):
        relative = chunk ^ cube
        return (relative & 3) * span + LANES + (relative >> 2) * 16

    def place_pair(start, size, cols, even, odd):
        keep_ref[aligned(start, size, 16), cols] = jnp.where(core == 0, even, odd).astype(BF16)
        send_ref[aligned(start, size, 16), cols] = jnp.where(core == 0, odd, even).astype(BF16)

    @pl.when(step == 0)
    def _():
        fill_masks(len_ref, mask_ref, micros, count, taps, clusters)
        total_ref[...] = share_ref[...]
        code_ref[...] = (code_own_ref[...] + code_other_ref[...]).astype(BF16)
        total = None
        for micro in range(micros):
            term = alog_refs[micro][...]
            total = term if total is None else total + term
        alog_ref[...] = total * (decay_ref[...] * (1.0 / LOG2E))

    code = code_ref[...]
    lane = lax.broadcasted_iota(jnp.int32, (1, LANES), 1)
    code_rank = jnp.where(lane < ranks, code, jnp.zeros_like(code))
    dpre = jnp.concatenate([ref[...] for ref in dpre_refs], axis=0)
    for part in range(2):
        source = lanes(2 * (2 * pair + part) + half)
        cols = slice(part * LANES, (part + 1) * LANES)
        wcode_ref[:ranks, cols] = dtx_ref[:, source]
        own = bc_own_ref[:, :, source].reshape(states, LANES)
        other = bc_other_ref[:, :, source].reshape(states, LANES)
        wcode_ref[ranks : ranks + states, cols] = jnp.where(half == 0, own, other)
        wcode_ref[ranks + states : ranks + 2 * states, cols] = jnp.where(half == 0, other, own)
        wcode_ref[ranks + 2 * states :, cols] = jnp.zeros(
            (LANES - ranks - 2 * states, LANES), BF16
        )
    for part in range(2):
        cols = slice(part * LANES, (part + 1) * LANES)
        chunk = 2 * pair + part
        source = 2 * chunk + half
        weights = convw_ref[:, lanes(source)]
        sact = jnp.concatenate([ref[:, cols] for ref in sact_refs], axis=0)
        dy = jnp.concatenate([ref[pl.ds(part * count, count), :] for ref in dy_refs], axis=0)
        dact = sact + dot(code, wcode_ref[:, cols], 1, 0)
        dact = dact + dy * skip_ref[pl.ds(source, 1), :]
        conved = conved_ref[:, cols]
        sig = sigmoid(conved)
        dconv = dact * (sig * (1.0 + conved * (1.0 - sig)))
        inner = inner_ref[:, cols]
        dinner = weights[taps - 1 : taps] * dconv
        sums = [None] * (taps + 1)
        sums[taps - 1] = jnp.sum(dconv * inner, axis=0, keepdims=True)
        sums[taps] = jnp.sum(dconv, axis=0, keepdims=True)
        for back in range(1, taps):
            kept = dconv * mask_ref[back]
            dinner = dinner + weights[taps - 1 - back : taps - back] * pltpu.roll(
                kept, rows - back, 0
            )
            sums[taps - 1 - back] = jnp.sum(
                kept * pltpu.roll(inner, back, 0), axis=0, keepdims=True
            )
        for k in range(taps + 1):
            vec_ref[k : k + 1, lanes(chunk)] = sums[k]
        for k in range(2):
            total = None
            for ref in back_refs:
                term = ref[k : k + 1, lanes(chunk)]
                total = term if total is None else total + term
            vec_ref[taps + 1 + k : taps + 2 + k, lanes(chunk)] = total
        low_ref[:, cols] = dinner.astype(BF16)

        act = act_ref[:, cols]
        start = pack_row(chunk)
        rows_now = dot(act, code_rank, 0, 0) + dot(dpre[:, cols], high_ref[...], 0, 0)
        for k in range(4):
            place_pair(
                start,
                16,
                slice(k * LANES, (k + 1) * LANES),
                rows_now[k * 16 : (k + 1) * 16],
                rows_now[edge + k * 16 : edge + (k + 1) * 16],
            )
        state_rows = dot(code, act, 0, 0)[ranks : ranks + 2 * states]
        place_pair(
            start, 16, slice(4 * LANES, 5 * LANES), state_rows[:states], state_rows[states:]
        )

    normed = normed_ref[...]
    for part in range(2):
        grad = dot(low_ref[:, lanes(core ^ part)], normed, 0, 0)
        total_ref[...] += eight_rows(grad * win_ref[step, core ^ part].astype(F32))
        out_ref = (keep_ref, send_ref)[part]
        out_ref[aligned(step * span, LANES, 16), :] = grad.astype(BF16)

    @pl.when(step == pl.num_programs(0) - 1)
    def _():
        vec_ref[taps + 3 : taps + 4, :] = (
            jnp.sum(total_ref[...], axis=0, keepdims=True) / gain_ref[...]
        )
        is_gain = lax.broadcasted_iota(jnp.int32, (8, LANES), 0) == taps + 3
        for chunk in range(chunks):
            start = pack_row(chunk)
            vec = vec_ref[:, chunk * LANES : (chunk + 1) * LANES]
            far, farther = (pltpu.roll(vec, LANES - k * edge // 2, 1) for k in (1, 2))
            even = jnp.where(is_gain & (lane >= edge // 2), far, vec)
            odd = jnp.where(is_gain & (lane < edge // 2), far, farther)
            alog = [
                alog_ref[pl.ds(q * eighth * chunks + chunk, eighth, stride=chunks), :]
                for q in range(2)
            ]
            place_pair(
                start,
                16,
                slice(5 * LANES, 6 * LANES),
                jnp.concatenate([alog[0], even]),
                jnp.concatenate([alog[1], odd]),
            )
            blank = jnp.zeros((16, 2 * LANES), F32)
            place_pair(start, 16, slice(6 * LANES, 8 * LANES), blank, blank)


def tail(
    place,
    lengths,
    code_own,
    code_other,
    sact,
    dpre,
    alog,
    back,
    dtx,
    bc_own,
    bc_other,
    decay,
    dy,
    conved,
    inner,
    act,
    high,
    convw,
    skip,
    normed,
    w4,
    share,
    gain,
):
    rows, own = act.shape
    chunks = own // LANES
    width = normed.shape[1]
    micros, _, clusters = lengths.shape
    count = rows // micros
    taps = convw.shape[0]
    ranks = dtx.shape[0]
    states = decay.shape[0] // chunks
    cols = 2 * LANES
    extent = 4 * (LANES + 32)

    def by_cols(height):
        return pl.BlockSpec((height, cols), lambda i, p: (0, i ^ p[FACE]))

    def dy_spec(micro):
        return pl.BlockSpec(
            (2 * count, LANES), lambda i, p: (micro * (chunks // 2) + (i ^ p[FACE]), 0)
        )

    in_specs = (
        [pl.BlockSpec(memory_space=pltpu.SMEM)]
        + [whole((rows, LANES))] * 2
        + [by_cols(count)] * (2 * micros)
        + [whole(alog[0].shape)] * micros
        + [whole(back[0].shape)] * micros
        + [whole(array.shape) for array in (dtx, bc_own, bc_other, decay)]
        + [dy_spec(micro) for micro in range(micros)]
        + [by_cols(rows)] * 3
        + [whole(array.shape) for array in (high, convw, skip, normed)]
        + [
            ANY,
            whole(share.shape),
            whole(gain.shape),
        ]
    )
    return pl.pallas_call(
        functools.partial(
            tail_kernel,
            micros=micros,
            count=count,
            taps=taps,
            clusters=clusters,
            ranks=ranks,
            chunks=chunks,
            states=states,
        ),
        grid_spec=pltpu.PrefetchScalarGridSpec(
            num_scalar_prefetch=1,
            grid=(chunks // 2,),
            in_specs=in_specs,
            out_specs=[
                whole((extent, width)),
                whole((extent, width)),
                pl.BlockSpec((rows, cols), lambda i, p: (0, i ^ p[FACE])),
            ],
            scratch_shapes=[
                pltpu.VMEM((taps, rows, LANES), F32),
                pltpu.VMEM((rows, LANES), BF16),
                pltpu.VMEM((LANES, cols), BF16),
                pltpu.VMEM((8, own), F32),
                pltpu.VMEM((states * chunks, LANES), F32),
                pltpu.VMEM((8, width), F32),
                pltpu.VMEM((chunks // 2, 2, LANES, width), BF16),
                pltpu.SemaphoreType.DMA((chunks // 2,)),
            ],
        ),
        out_shape=[
            hbm((extent, width), BF16),
            hbm((extent, width), BF16),
            hbm((rows, own), BF16),
        ],
        compiler_params=params(30),
        cost_estimate=cost(7),
        name="tail",
    )(
        place,
        lengths,
        *in_hbm([code_own]),
        code_other,
        *in_hbm(
            (
                *sact,
                *dpre,
                *alog,
                *back,
                dtx,
                bc_own,
                bc_other,
                decay,
                *([dy] * micros),
                conved,
                inner,
                act,
                high,
                convw,
                skip,
                normed,
                w4,
                share,
                gain,
            )
        ),
    )


def fetch_halves(source, which, half, target_ref, sems):
    copies = []
    for k in range(target_ref.shape[0]):
        pair = pl.ds(2 * k, 2)
        block = source.at[pair, half] if which is None else source.at[which, pair, half]
        copies.append(pltpu.make_async_copy(block, target_ref.at[k], sems.at[k]))
    for copy in copies:
        copy.start()
    return copies


def products_kernel(
    place_ref,
    gated_ref,
    dgate_ref,
    out_ref,
    weight_ref,
    mixed_ref,
    dnormed_ref,
    wout_ref,
    wgate_ref,
    out_sems,
    gate_sems,
):
    half = place_ref[HALF]
    width = mixed_ref.shape[1]
    jobs = (
        (fetch_halves(out_ref, None, half, wout_ref, out_sems), gated_ref, wout_ref, mixed_ref),
        (fetch_halves(weight_ref, 1, half, wgate_ref, gate_sems), dgate_ref, wgate_ref, dnormed_ref),
    )
    for copies, left_ref, right_ref, result_ref in jobs:
        total = None
        for k, copy in enumerate(copies):
            copy.wait()
            left = left_ref[:, 2 * k * LANES : 2 * (k + 1) * LANES]
            term = dot(left, right_ref[k].reshape(-1, width), 1, 0)
            total = term if total is None else total + term
        result_ref[...] = total.astype(BF16)


def products(place, gated, dgate, wout3, w4):
    rows, own = gated.shape
    width = w4.shape[-1]
    pairs = own // (2 * LANES)
    return pl.pallas_call(
        products_kernel,
        grid_spec=pltpu.PrefetchScalarGridSpec(
            num_scalar_prefetch=1,
            grid=(1,),
            in_specs=[whole((rows, own)), whole((rows, own)), ANY, ANY],
            out_specs=[whole((rows, width))] * 2,
            scratch_shapes=[
                pltpu.VMEM((pairs, 2, LANES, width), BF16),
                pltpu.VMEM((pairs, 2, LANES, width), BF16),
                pltpu.SemaphoreType.DMA((pairs,)),
                pltpu.SemaphoreType.DMA((pairs,)),
            ],
        ),
        out_shape=[hbm((rows, width), BF16)] * 2,
        compiler_params=params(20),
        cost_estimate=cost(4),
        name="products",
    )(place, *in_hbm((gated, dgate, wout3, w4)))


def spread_kernel(place_ref, low_ref, weight_ref, gate_ref, dnormed_ref, win_ref, sems):
    width = gate_ref.shape[1]
    total = gate_ref[...].astype(F32)
    for k, copy in enumerate(fetch_halves(weight_ref, 0, place_ref[HALF], win_ref, sems)):
        copy.wait()
        left = low_ref[:, 2 * k * LANES : 2 * (k + 1) * LANES]
        total = total + dot(left, win_ref[k].reshape(-1, width), 1, 0)
    dnormed_ref[...] = total.astype(BF16)


def spread(place, low, w4, gate_part):
    rows, own = low.shape
    width = w4.shape[-1]
    pairs = own // (2 * LANES)
    return pl.pallas_call(
        spread_kernel,
        grid_spec=pltpu.PrefetchScalarGridSpec(
            num_scalar_prefetch=1,
            grid=(1,),
            in_specs=[whole((rows, own)), ANY, whole((rows, width))],
            out_specs=whole((rows, width)),
            scratch_shapes=[
                pltpu.VMEM((pairs, 2, LANES, width), BF16),
                pltpu.SemaphoreType.DMA((pairs,)),
            ],
        ),
        out_shape=hbm((rows, width), BF16),
        compiler_params=params(16),
        cost_estimate=cost(3),
        name="spread",
    )(place, *in_hbm((low, w4, gate_part)))


def finish_kernel(x_ref, mine_ref, theirs_ref, cotan_ref, gain_ref, grad_ref):
    x = x_ref[...].astype(F32)
    scale = lax.rsqrt(jnp.mean(x * x, axis=1, keepdims=True) + EPSILON)
    unit = x * scale
    dhat = (mine_ref[...].astype(F32) + theirs_ref[...].astype(F32)) * gain_ref[...]
    grad_ref[...] = cotan_ref[...].astype(F32) + scale * (
        dhat - unit * jnp.mean(dhat * unit, axis=1, keepdims=True)
    )


def finish(x, mine, theirs, cotan, gain):
    rows, width = x.shape
    by_rows = pl.BlockSpec((rows // 4, width), lambda i: (i, 0))
    return pl.pallas_call(
        finish_kernel,
        grid=(4,),
        in_specs=[by_rows] * 4 + [whole(gain.shape)],
        out_specs=by_rows,
        out_shape=jax.ShapeDtypeStruct((rows, width), F32),
        compiler_params=params(16),
        cost_estimate=cost(0),
        name="finish",
    )(*in_hbm((x, mine)), theirs, *in_hbm((cotan, gain)))


def unpack_kernel(
    near_ref,
    far_ref,
    out_ref,
    dtx_ref,
    dt_ref,
    bc_ref,
    alog_ref,
    convw_ref,
    convb_ref,
    bias_ref,
    skip_ref,
    out_grad_ref,
    *,
    eighth,
    taps,
    edge,
):
    pack = near_ref[...].astype(F32) + far_ref[...].astype(F32)
    for k in range(4):
        rows = pack[:, k * LANES : (k + 1) * LANES]
        dtx_ref[pl.ds(16 * k, 16), :] = rows[:, :edge]
        dt_ref[pl.ds(16 * k, 16), :] = pltpu.roll(rows, edge, 1)[:, :edge]
    rows = pack[:, 4 * LANES : 5 * LANES]
    bc_ref[0] = rows[:eighth]
    bc_ref[1] = rows[eighth:]
    rows = pack[:, 5 * LANES : 6 * LANES]
    alog_ref[...] = rows[:eighth]
    vec = rows[eighth:, :edge]
    convw_ref[...] = vec[:taps]
    convb_ref[...] = vec[taps : taps + 1]
    bias_ref[...] = vec[taps + 1 : taps + 2]
    skip_ref[...] = vec[taps + 2 : taps + 3]
    out_grad_ref[...] = out_ref[...].astype(F32)


def unpack(near, far, out, eighth, taps, ranks):
    edge = LANES // 2
    shapes = [
        (edge, ranks),
        (edge, ranks),
        (2, eighth, LANES),
        (eighth, LANES),
        (taps, edge),
        (1, edge),
        (1, edge),
        (1, edge),
        out.shape,
    ]
    return pl.pallas_call(
        functools.partial(unpack_kernel, eighth=eighth, taps=taps, edge=edge),
        grid=(1,),
        in_specs=[whole(array.shape) for array in (near, far, out)],
        out_specs=[whole(shape) for shape in shapes],
        out_shape=[jax.ShapeDtypeStruct(shape, F32) for shape in shapes],
        cost_estimate=cost(0),
        name="unpack",
    )(near, far, out)


def swap_pair(array):
    count = lax.axis_size("state")
    return lax.ppermute(array, "state", [(pos, pos ^ 1) for pos in range(count)])


def swap_bit(array, bits):
    return lax.ppermute(array, "dp", [(pos, pos ^ bits) for pos in range(lax.axis_size("dp"))])


def swap_both(array, bits=0):
    states = lax.axis_size("state")
    pairs = []
    for d in range(lax.axis_size("dp")):
        for s in range(states):
            pairs.append((d * states + s, (((d & ~1) | s) ^ bits) * states + (d & 1)))
    return lax.ppermute(array, ("dp", "state"), pairs)


def add_quarters(kept, got):
    extent = kept.shape[0] // 4
    return [kept[k * extent :][:extent] + got[k * extent :][:extent] for k in range(4)]


def trade_quarters(quarters):
    return [quarters[0]] + [swap_bit(quarters[k], k * X_BIT) for k in range(1, 4)]


def sum_quarters(quarters):
    left, right = (quarters[k].astype(F32) + quarters[k + 1].astype(F32) for k in (0, 2))
    return (left + right).astype(BF16)


CORE_BIT, X_BIT, ZH_BIT = 1, 2, 8


def shards(
    tokens,
    cluster_len,
    norm_gain,
    in_weight,
    conv_weight,
    conv_bias,
    dtx_weight,
    dt_weight,
    dt_bias,
    bc_weight,
    a_log,
    skip_gain,
    out_weight,
    cotangent,
):
    micros, count, width = tokens.shape
    inner = out_weight.shape[0]
    taps = conv_weight.shape[0]
    ranks = dtx_weight.shape[1]
    chunks = inner // (2 * LANES)
    own = chunks * LANES
    rows = micros * count
    edge = LANES // 2
    span = LANES + 32
    dp_parts = lax.axis_size("dp")
    state_count = lax.axis_size("state")
    dp_pos = lax.axis_index("dp")
    state_pos = lax.axis_index("state")
    half = state_pos & 1
    fast = state_count == 2 and dp_parts == 2 * chunks == 16
    if fast:
        place = jnp.stack([half, dp_pos & 1, dp_pos >> 1, (dp_pos >> 1) & 3])
        bc_own, alog_own = bc_weight, a_log
        bc_other, alog_other = swap_pair(bc_weight), swap_pair(a_log)
    else:
        place = jnp.stack([half, 0, 0, 0])
        bc_all = lax.all_gather(bc_weight, "state", axis=1, tiled=True)
        alog_all = lax.all_gather(a_log, "state", axis=0, tiled=True)
        eighth = alog_all.shape[0] // 2
        bc_own, bc_other = (
            lax.dynamic_slice_in_dim(bc_all, which * eighth, eighth, 1)
            for which in (half, 1 - half)
        )
        alog_own, alog_other = (
            lax.dynamic_slice_in_dim(alog_all, which * eighth, eighth, 0)
            for which in (half, 1 - half)
        )
    place = place.astype(jnp.int32)
    eighth = alog_own.shape[0]
    states = 2 * eighth

    x = tokens.reshape(rows, width)
    cotan = cotangent.reshape(rows, width)
    w4 = in_weight.reshape(2, chunks, 2, LANES, width)
    wout3 = out_weight.reshape(chunks, 2, LANES, width)
    dtx, dt = dtx_weight.T, dt_weight.T
    bias = dt_bias.reshape(-1, LANES)
    skip = skip_gain.reshape(-1, LANES)

    normed, act_all, act, inner_own, conved, gate = project(
        place, cluster_len, x, norm_gain[None], w4, conv_weight, conv_bias.reshape(-1, LANES)
    )
    bc, rank, high, decay, sp, u, dy, gated, dgate, keep, send, share = scan_forward(
        place,
        cluster_len,
        act_all,
        bc_own,
        bc_other,
        alog_own,
        alog_other,
        dtx,
        dt,
        bias,
        skip,
        act,
        gate,
        wout3,
        cotan,
        normed,
        w4,
    )
    if fast:
        early = swap_bit(send, CORE_BIT)
    mixed_part, dn_gate = products(place, gated, dgate, wout3, w4)
    if fast:
        *quarters, mixed_part, dn_gate, sp = lax.optimization_barrier(
            (*add_quarters(keep, early), mixed_part, dn_gate, sp)
        )
        early_got = trade_quarters(quarters)
    mixed_other = swap_pair(mixed_part)
    code_own = None
    results = []
    for micro in range(micros):
        code_own, *rest = scan_backward(
            place, micro, count, bc, decay, rank, dt, bias, act, sp, u, dy, code_own
        )
        results.append(rest)
    sact, dpre, alog, back = zip(*results)
    code_other = swap_pair(code_own)
    if fast:
        block = sum_quarters(early_got)
        out_keep, out_send, gate_sum = block[:edge], block[edge:LANES], block[LANES:]
        out_send, gate_sum, mixed_other, conved = lax.optimization_barrier(
            (out_send, gate_sum, mixed_other, conved)
        )
        out_got = swap_bit(out_send, ZH_BIT)
    late_keep, late_send, low = tail(
        place,
        cluster_len,
        code_own,
        code_other,
        sact,
        dpre,
        alog,
        back,
        dtx,
        bc_own,
        bc_other,
        decay,
        dy,
        conved,
        inner_own,
        act,
        high,
        conv_weight,
        skip,
        normed,
        w4,
        share,
        norm_gain[None],
    )
    if fast:
        late = swap_bit(late_send, CORE_BIT)
        out_own = swap_both(out_keep + out_got)
        late_got = trade_quarters(add_quarters(late_keep, late))
    dnormed_part = spread(place, low, w4, dn_gate)
    dnormed_other = swap_pair(dnormed_part)
    mixed = (x.astype(F32) + (mixed_part.astype(F32) + mixed_other.astype(F32))).astype(BF16)
    if fast:
        *late_got, mixed, out_own, dnormed_other = lax.optimization_barrier(
            (*late_got, mixed, out_own, dnormed_other)
        )
        block = sum_quarters(late_got)
        inner_sum = block[:LANES]
        upper = dp_pos >= dp_parts // 2
        crossing = jnp.where(upper, inner_sum, gate_sum)
        first, second = crossing[:edge], crossing[edge:]
        first, pack_far, pack_near = lax.optimization_barrier(
            (first, block[-16:], block[LANES:-16])
        )
        pack_far = swap_both(pack_far, ZH_BIT)
        first_got = swap_bit(first, ZH_BIT)
        pack_near = swap_both(pack_near)
        first_got, pack_far, pack_near = lax.optimization_barrier((first_got, pack_far, pack_near))
        second_got = swap_bit(second, ZH_BIT)
        tokens_grad = finish(x, dnormed_part, dnormed_other, cotan, norm_gain[None])
        gain_mine = (
            pack_near[:, 5 * LANES : 6 * LANES].astype(F32)
            + pack_far[:, 5 * LANES : 6 * LANES].astype(F32)
        ).astype(BF16)
        gain_both = gain_mine[-1].astype(F32) + swap_bit(gain_mine, CORE_BIT)[-1].astype(F32)
        extent = width // (dp_parts * state_count)
        gain_grad = lax.dynamic_slice_in_dim(gain_both, (dp_pos & 1) * extent, extent, 0)
        (
            dtx_grad,
            dt_grad,
            bc_grad,
            alog_grad,
            convw_grad,
            convb_grad,
            bias_grad,
            skip_grad,
            out_own,
        ) = unpack(pack_near, pack_far, out_own, eighth, taps, ranks)
        convb_grad, bias_grad, skip_grad = (
            array[0] for array in (convb_grad, bias_grad, skip_grad)
        )
        in_grad = jnp.where(upper, gate_sum, inner_sum).astype(F32) + jnp.concatenate(
            [first_got, second_got]
        ).astype(F32)
    else:
        tokens_grad = finish(x, dnormed_part, dnormed_other, cotan, norm_gain[None])
    mixed = mixed.reshape(micros, count, width)
    tokens_grad = tokens_grad.reshape(micros, count, width)

    if not fast:
        def total(array):
            return lax.psum(array.astype(F32), "dp")

        def both_rows(array):
            mine = array.reshape(chunks, 1, LANES, -1)
            other = swap_pair(mine)
            low = jnp.where(half == 0, mine, other)
            high = jnp.where(half == 0, other, mine)
            return jnp.concatenate([low, high], axis=1).reshape(2 * own, -1)

        every = dp_parts * state_count
        at = dp_pos * state_count + state_pos

        def cut_own(array):
            extent = array.shape[0] // every
            return lax.dynamic_slice_in_dim(array, at * extent, extent, 0)

        pair = total(jnp.stack([keep, send])).reshape(2, 2, 2, 2 * LANES, width)
        outs = pair[:, :, :, :LANES].reshape(2, 2, 2, 2, edge, width)
        outs = jnp.transpose(outs, (3, 1, 2, 0, 4, 5)).reshape(own, width)
        gates = jnp.moveaxis(pair[:, :, :, LANES:], 0, 2).reshape(own, width)
        pair = total(jnp.stack([late_keep, late_send])).reshape(2, 2, 2, span, width)
        inners = jnp.moveaxis(pair[:, :, :, :LANES], 0, 2).reshape(own, width)
        packs = pair[:, :, :, LANES:].reshape(2, 2, 2, 2, 16, width // LANES, LANES)
        packs = jnp.transpose(packs, (3, 1, 2, 0, 5, 4, 6)).reshape(chunks, 2, -1, 16, LANES)
        small = both_rows(packs[:, :, :4].reshape(own, LANES))
        in_grad = cut_own(jnp.concatenate([both_rows(inners), both_rows(gates)]))
        out_own = cut_own(both_rows(outs))
        mine = cut_own(small)
        dtx_grad, dt_grad = mine[:, :ranks], mine[:, ranks:]
        vec_rows = jnp.swapaxes(packs[:, :, 5, eighth:, :edge], 2, 3).reshape(own, -1)
        gain_sum = vec_rows[:, -1].reshape(chunks, 2, 2, -1).swapaxes(1, 2).reshape(-1)
        gain_grad = cut_own(gain_sum + swap_pair(gain_sum))
        vec = cut_own(both_rows(vec_rows)).T
        state_rows = jnp.concatenate([packs[:, :, 4], packs[:, :, 5, :eighth]], axis=2)
        state_rows = state_rows.reshape(chunks, 2, 3, eighth, LANES)
        state_rows = jnp.transpose(state_rows, (0, 4, 2, 1, 3)).reshape(own, -1)
        extent = inner // dp_parts
        state_part = lax.dynamic_slice_in_dim(both_rows(state_rows), dp_pos * extent, extent, 0)
        state_part = state_part.T.reshape(3, state_count, -1, extent)
        state_part = lax.dynamic_index_in_dim(state_part, state_pos, 1, keepdims=False)
        bc_grad, alog_grad = state_part[:2], state_part[2]
        convw_grad, convb_grad, bias_grad, skip_grad = (
            vec[:taps], vec[taps], vec[taps + 1], vec[taps + 2]
        )

    return (
        mixed,
        tokens_grad,
        gain_grad,
        in_grad,
        convw_grad,
        convb_grad,
        dtx_grad,
        dt_grad,
        bias_grad,
        bc_grad,
        alog_grad,
        skip_grad,
        out_own,
    )


def solution(mesh):
    return jax.shard_map(
        shards,
        mesh=mesh,
        in_specs=(
            P(None, "dp", None),
            P(None, "dp", None),
            P(),
            P(),
            P(),
            P(),
            P(),
            P(),
            P(),
            P(None, "state", None),
            P("state", None),
            P(),
            P(),
            P(None, "dp", None),
        ),
        out_specs=(
            P(None, "dp", None),
            P(None, "dp", None),
            P(("dp", "state")),
            P(("dp", "state"), None),
            P(None, ("dp", "state")),
            P(("dp", "state")),
            P(("dp", "state"), None),
            P(("dp", "state"), None),
            P(("dp", "state")),
            P(None, "state", "dp"),
            P("state", "dp"),
            P(("dp", "state")),
            P(("dp", "state"), None),
        ),
        check_vma=False,
    )
```

```python
import functools
import math

import jax
import jax.numpy as jnp
from jax import lax
from jax.experimental import pallas as pl
from jax.experimental.pallas import tpu as pltpu
from jax.sharding import PartitionSpec as P

EPSILON = 1e-05
LANES = 128
RESET = 1e4
LOG2E = math.log2(math.e)
F32 = jnp.float32
BF16 = jnp.bfloat16
MIB = 1024 * 1024


def dot(left, right, left_dim, right_dim):
    return lax.dot_general(
        left, right, (((left_dim,), (right_dim,)), ((), ())), preferred_element_type=F32
    )


def params(mib):
    return pltpu.CompilerParams(
        vmem_limit_bytes=mib * MIB, dimension_semantics=("arbitrary",)
    )


ANY = pl.BlockSpec(memory_space=pl.ANY)


def stream(step, steps, fetch):
    @pl.when(step == 0)
    def _():
        for k in range(steps):
            for copy in fetch(k):
                copy.start()

    for copy in fetch(step):
        copy.wait()


def whole(shape):
    return pl.BlockSpec(shape, lambda *_: (0,) * len(shape))


sigmoid = jax.nn.sigmoid


def softplus(value):
    return jnp.maximum(value, 0.0) + jnp.log1p(jnp.exp(-jnp.abs(value)))


def lanes(index):
    return pl.ds(pl.multiple_of(index * LANES, LANES), LANES)


def cost(micros):
    return pl.CostEstimate(
        flops=int(micros * 1e9), bytes_accessed=int(micros * 1e6), transcendentals=0
    )


def hbm(shape, dtype):
    return pltpu.HBM(shape, dtype)


def in_hbm(arrays):
    return [pltpu.with_memory_space_constraint(array, pltpu.HBM) for array in arrays]


def aligned(start, size, to=8):
    return pl.ds(pl.multiple_of(start, to), size)


HALF, CORE, CUBE, FACE = range(4)


def fill_masks(len_ref, mask_ref, micros, count, taps, clusters):
    place = lax.broadcasted_iota(jnp.int32, (count, LANES), 0)
    for micro in range(micros):
        rows = pl.ds(micro * count, count)
        for back in range(1, taps):
            apart = place < back
            start = 0
            for cluster in range(clusters - 1):
                start = start + len_ref[micro, 0, cluster]
                apart = apart | ((place >= start) & (place < start + back))
            mask_ref[back, rows, :] = jnp.where(apart, 0.0, 1.0)
            if back == 1:
                mask_ref[0, rows, :] = jnp.where(apart, 1.0, 0.0)


def project_kernel(
    place_ref,
    len_ref,
    gain_ref,
    convw_ref,
    convb_ref,
    x_far,
    weight_far,
    normed_far,
    act_far,
    own_act_far,
    inner_far,
    conved_far,
    gate_far,
    mask_ref,
    x_ref,
    win_ref,
    wgate_ref,
    normed_ref,
    act_ref,
    own_act_ref,
    inner_ref,
    conved_ref,
    gate_ref,
    in_sems,
    out_sems,
    *,
    micros,
    count,
    taps,
    clusters,
):
    half = place_ref[HALF]
    chunks = win_ref.shape[0]
    inward = [pltpu.make_async_copy(x_far, x_ref, in_sems.at[2 * chunks])]
    for k in range(chunks):
        inward.append(pltpu.make_async_copy(weight_far.at[0, k], win_ref.at[k], in_sems.at[2 * k]))
        inward.append(
            pltpu.make_async_copy(
                weight_far.at[1, k, half], wgate_ref.at[k], in_sems.at[2 * k + 1]
            )
        )
    for copy in inward:
        copy.start()
    outward = []

    def put(source, target):
        outward.append(pltpu.make_async_copy(source, target, out_sems.at[len(outward)]))
        outward[-1].start()

    fill_masks(len_ref, mask_ref, micros, count, taps, clusters)
    inward[0].wait()
    rows = x_ref[...].astype(F32)
    scale = lax.rsqrt(jnp.mean(rows * rows, axis=1, keepdims=True) + EPSILON)
    normed = (rows * scale * gain_ref[...]).astype(BF16)
    normed_ref[...] = normed
    put(normed_ref, normed_far)
    for k in range(chunks):
        inward[2 * k + 1].wait()
        inward[2 * k + 2].wait()
        proj = dot(normed, win_ref[k].reshape(2 * LANES, -1), 1, 1)
        own = slice(k * LANES, (k + 1) * LANES)
        gate_ref[:, own] = dot(normed, wgate_ref[k], 1, 1)
        inners, conveds, acts = [], [], []
        for part in range(2):
            cols = slice((2 * k + part) * LANES, (2 * k + part + 1) * LANES)
            inner = proj[:, part * LANES : (part + 1) * LANES]
            conved = convb_ref[2 * k + part : 2 * k + part + 1, :]
            conved = conved + convw_ref[taps - 1 : taps, cols] * inner
            for back in range(1, taps):
                shifted = pltpu.roll(inner, back, 0) * mask_ref[back]
                conved = conved + convw_ref[taps - 1 - back : taps - back, cols] * shifted
            act = conved * sigmoid(conved)
            act_ref[:, cols] = act.astype(BF16)
            inners.append(inner)
            conveds.append(conved)
            acts.append(act)
        inner_ref[:, own] = jnp.where(half == 0, *inners)
        conved_ref[:, own] = jnp.where(half == 0, *conveds)
        own_act_ref[:, own] = jnp.where(half == 0, *acts).astype(BF16)
        if k % 2:
            group = pl.ds((k - 1) * LANES, 2 * LANES)
            wide = pl.ds(2 * (k - 1) * LANES, 4 * LANES)
            put(act_ref.at[:, wide], act_far.at[:, wide])
            for near, far in (
                (gate_ref, gate_far),
                (inner_ref, inner_far),
                (conved_ref, conved_far),
                (own_act_ref, own_act_far),
            ):
                put(near.at[:, group], far.at[:, group])
    for copy in outward:
        copy.wait()


def project(place, lengths, x, gain, w4, conv_weight, conv_bias):
    rows, width = x.shape
    chunks = w4.shape[1]
    micros, _, clusters = lengths.shape
    taps = conv_weight.shape[0]
    own = chunks * LANES
    outs = [
        ((rows, width), BF16),
        ((rows, 2 * own), BF16),
        ((rows, own), BF16),
        ((rows, own), F32),
        ((rows, own), F32),
        ((rows, own), F32),
    ]
    return pl.pallas_call(
        functools.partial(
            project_kernel, micros=micros, count=rows // micros, taps=taps, clusters=clusters
        ),
        grid_spec=pltpu.PrefetchScalarGridSpec(
            num_scalar_prefetch=1,
            grid=(1,),
            in_specs=[
                pl.BlockSpec(memory_space=pltpu.SMEM),
                whole(gain.shape),
                whole(conv_weight.shape),
                whole(conv_bias.shape),
                ANY,
                ANY,
            ],
            out_specs=[ANY] * len(outs),
            scratch_shapes=[
                pltpu.VMEM((taps, rows, LANES), F32),
                pltpu.VMEM((rows, width), BF16),
                pltpu.VMEM((chunks, 2, LANES, width), BF16),
                pltpu.VMEM((chunks, LANES, width), BF16),
            ]
            + [pltpu.VMEM(*out) for out in outs]
            + [
                pltpu.SemaphoreType.DMA((2 * chunks + 1,)),
                pltpu.SemaphoreType.DMA((1 + 5 * chunks // 2,)),
            ],
        ),
        out_shape=[hbm(*out) for out in outs],
        compiler_params=params(30),
        cost_estimate=cost(6),
        name="project",
    )(place, *in_hbm((lengths, gain, conv_weight, conv_bias, x, w4)))


def eight_rows(array):
    return jnp.sum(array.reshape(-1, 8, array.shape[1]), axis=0)


def every_row(ref, row, height):
    return ref[pl.ds(row, height, stride=0), :]


def b_at(n, eighth):
    return (n // eighth) * 2 * eighth + n % eighth


def c_at(n, eighth):
    return b_at(n, eighth) + eighth


def forward_kernel(
    place_ref,
    len_ref,
    act_all_ref,
    bc_own_ref,
    bc_other_ref,
    alog_own_ref,
    alog_other_ref,
    dtx_ref,
    dt_ref,
    bias_ref,
    skip_ref,
    act_ref,
    *refs,
    micros,
    count,
    states,
    chunks,
    clusters,
):
    gate_far, wout_far, cotan_far, normed_far, weight_far = refs[:5]
    bc_ref, rank_ref, rank_high_ref, decay_ref, share_ref = refs[5:10]
    sp_far, u_far, dy_far, gated_far, dgate_far, keep_far, send_far = refs[10:17]
    mask_ref, y_ref, tmp_ref, wide_ref = refs[17:21]
    gate_ref, wout_ref, cotan_ref, normed_ref, wgate_ref = refs[21:26]
    sp_ref, u_ref, dy_ref, gated_ref, dgate_ref, keep_ref, send_ref = refs[26:33]
    in_sems, out_sems = refs[33:]
    rows = micros * count
    eighth = states // 2
    half, core, cube, face = (place_ref[k] for k in range(4))
    first = half == 0
    inward = [
        pltpu.make_async_copy(source, target, in_sems.at[k])
        for k, (source, target) in enumerate(
            (
                (gate_far, gate_ref),
                (wout_far.at[:, half], wout_ref),
                (cotan_far, cotan_ref),
                (normed_far, normed_ref),
                (weight_far.at[1, :, half], wgate_ref),
            )
        )
    ]
    for copy in inward:
        copy.start()
    outward = []

    def put(source, target):
        outward.append(pltpu.make_async_copy(source, target, out_sems.at[len(outward)]))
        outward[-1].start()

    act_all = act_all_ref[...]
    own = dot(act_all, bc_own_ref[...].reshape(states, -1), 1, 1)
    other = dot(act_all, bc_other_ref[...].reshape(states, -1), 1, 1)
    bc_ref[:, :states] = jnp.where(first, own, other)
    bc_ref[:, states:] = jnp.where(first, other, own)
    spread_lanes(bc_ref, wide_ref)

    fill_masks(len_ref, mask_ref, micros, count, 2, clusters)
    for chunk in range(chunks):
        cols = lanes(2 * chunk + half)
        own, other = alog_own_ref[:, cols], alog_other_ref[:, cols]
        tmp_ref[pl.ds(chunk * states, eighth), :] = jnp.where(first, own, other)
        tmp_ref[pl.ds(chunk * states + eighth, eighth), :] = jnp.where(first, other, own)
    for n in range(states):
        decay_ref[pl.ds(n * chunks, chunks), :] = -LOG2E * jnp.exp(
            tmp_ref[pl.ds(n, chunks, stride=states), :]
        )

    rank = dot(act_all, dtx_ref[...], 1, 1).astype(BF16)
    rank_ref[...] = rank
    rank_high_ref[...] = jnp.concatenate([jnp.zeros_like(rank), rank], axis=1)
    for chunk in range(chunks):
        cols = slice(chunk * LANES, (chunk + 1) * LANES)
        bias = bias_ref[pl.ds(2 * chunk + half, 1), :]
        step = softplus(dot(rank, dt_ref[:, lanes(2 * chunk + half)], 1, 0) + bias)
        held = step + RESET * mask_ref[0]
        source = step * act_ref[:, cols].astype(F32)
        for micro in range(micros):
            span = slice(micro * count, (micro + 1) * count)
            place = pl.ds((micro * chunks + chunk) * count, count)
            sp_ref[place, :] = held[span]
            u_ref[place, :] = source[span]
    put(sp_ref, sp_far)
    put(u_ref, u_far)

    for micro in range(micros):

        def advance(t, h, micro=micro):
            row = micro * count + t
            span = pl.ds(micro * chunks * count + t, chunks, stride=count)
            sp = sp_ref[span, :]
            u = u_ref[span, :]
            out = []
            y = None
            for n in range(states):
                decay = jnp.exp2(sp * decay_ref[pl.ds(n * chunks, chunks), :])
                now = decay * h[n] + u * every_row(wide_ref, b_at(n, eighth) * rows + row, chunks)
                out.append(now)
                term = now * every_row(wide_ref, c_at(n, eighth) * rows + row, chunks)
                y = term if y is None else y + term
            y_ref[span, :] = y
            return tuple(out)

        lax.fori_loop(0, count, advance, (jnp.zeros((chunks, LANES), F32),) * states, unroll=2)

    for copy in inward:
        copy.wait()
    cotan = cotan_ref[...]
    for chunk in range(chunks):
        cols = slice(chunk * LANES, (chunk + 1) * LANES)
        places = [pl.ds((micro * chunks + chunk) * count, count) for micro in range(micros)]
        y = jnp.concatenate([y_ref[place, :] for place in places])
        y = y + skip_ref[pl.ds(2 * chunk + half, 1), :] * act_ref[:, cols].astype(F32)
        gate = gate_ref[:, cols]
        sig = sigmoid(gate)
        gated_ref[:, cols] = (y * (gate * sig)).astype(BF16)
        dgated = dot(cotan, wout_ref[chunk], 1, 1)
        dy = dgated * (gate * sig)
        for micro in range(micros):
            dy_ref[places[micro], :] = dy[micro * count : (micro + 1) * count]
        dgate_ref[:, cols] = (dgated * y * (sig * (1.0 + gate * (1.0 - sig)))).astype(BF16)
    put(dy_ref, dy_far)
    put(gated_ref, gated_far)
    put(dgate_ref, dgate_far)
    normed = normed_ref[...]
    edge = LANES // 2
    share = jnp.zeros(share_ref.shape, F32)
    for r in range(chunks // 2):
        for zh in range(2):
            grad = dot(gated_ref[:, lanes((r + 4 * zh) ^ cube)], cotan, 0, 0).astype(BF16)
            top, bottom = grad[:edge], grad[edge:]
            place = pl.ds(r * 2 * LANES + zh * edge, edge)
            keep_ref[place, :] = jnp.where(core == 0, top, bottom)
            send_ref[place, :] = jnp.where(core == 0, bottom, top)
        place = pl.ds((2 * r + 1) * LANES, LANES)
        pair = 2 * (r ^ face)
        for chunk, out_ref in ((pair + core, keep_ref), (pair + 1 - core, send_ref)):
            grad = dot(dgate_ref[:, lanes(chunk)], normed, 0, 0)
            share = share + eight_rows(grad * wgate_ref[chunk].astype(F32))
            out_ref[place, :] = grad.astype(BF16)
        place = pl.ds(r * 2 * LANES, 2 * LANES)
        put(send_ref.at[place], send_far.at[place])
        put(keep_ref.at[place], keep_far.at[place])
    share_ref[...] = share
    for copy in outward:
        copy.wait()


def scan_forward(
    place,
    lengths,
    act_all,
    bc_own,
    bc_other,
    alog_own,
    alog_other,
    dtx,
    dt,
    bias,
    skip,
    act,
    gate,
    wout3,
    cotan,
    normed,
    w4,
):
    rows, own = act.shape
    chunks = own // LANES
    states = 2 * alog_own.shape[0]
    width = cotan.shape[1]
    micros, _, clusters = lengths.shape
    ranks = dtx.shape[0]
    small = [
        ((rows, 2 * states), F32),
        ((rows, ranks), BF16),
        ((rows, 2 * ranks), BF16),
        ((states * chunks, LANES), F32),
        ((8, width), F32),
    ]
    large = [
        ((chunks * rows, LANES), F32),
        ((chunks * rows, LANES), F32),
        ((chunks * rows, LANES), F32),
        ((rows, own), BF16),
        ((rows, own), BF16),
        ((own, width), BF16),
        ((own, width), BF16),
    ]
    operands = (act_all, bc_own, bc_other, alog_own, alog_other, dtx, dt, bias, skip, act)
    streamed = (gate, wout3, cotan, normed, w4)
    return pl.pallas_call(
        functools.partial(
            forward_kernel,
            micros=micros,
            count=rows // micros,
            states=states,
            chunks=chunks,
            clusters=clusters,
        ),
        grid_spec=pltpu.PrefetchScalarGridSpec(
            num_scalar_prefetch=1,
            grid=(1,),
            in_specs=[pl.BlockSpec(memory_space=pltpu.SMEM)]
            + [whole(operand.shape) for operand in operands]
            + [ANY] * len(streamed),
            out_specs=[whole(shape) for shape, _ in small] + [ANY] * len(large),
            scratch_shapes=[
                pltpu.VMEM((2, rows, LANES), F32),
                pltpu.VMEM((chunks * rows, LANES), F32),
                pltpu.VMEM((states * chunks, LANES), F32),
                pltpu.VMEM((2 * states * rows, LANES), F32),
                pltpu.VMEM((rows, own), F32),
                pltpu.VMEM((chunks, LANES, width), BF16),
                pltpu.VMEM((rows, width), BF16),
                pltpu.VMEM((rows, width), BF16),
                pltpu.VMEM((chunks, LANES, width), BF16),
            ]
            + [pltpu.VMEM(*out) for out in large]
            + [pltpu.SemaphoreType.DMA((5,)), pltpu.SemaphoreType.DMA((5 + chunks,))],
        ),
        out_shape=[hbm(*out) for out in small + large],
        compiler_params=params(52),
        cost_estimate=cost(19),
        name="scan_forward",
    )(
        place,
        lengths,
        *in_hbm(operands[:1]),
        *operands[1:5],
        *in_hbm((*operands[5:], *streamed)),
    )


def spread_lanes(values_ref, wide_ref):
    rows, count = values_ref.shape
    for k in range(count):
        wide_ref[pl.ds(k * rows, rows), :] = jnp.broadcast_to(
            values_ref[:, k : k + 1], (rows, LANES)
        )


def backward_kernel(
    place_ref,
    bc_ref,
    decay_ref,
    rank_ref,
    dt_ref,
    bias_ref,
    act_ref,
    sp_ref,
    u_ref,
    dy_ref,
    code_ref,
    sact_ref,
    dpre_ref,
    alog_ref,
    vec_ref,
    h_ref,
    keep_ref,
    s_ref,
    d_ref,
    terms_ref,
    sums_b_ref,
    sums_c_ref,
    wide_ref,
    *,
    count,
    states,
    chunks,
):
    @pl.when(pl.program_id(0) == 0)
    def _():
        alog_ref[...] = jnp.zeros_like(alog_ref)
        vec_ref[...] = jnp.zeros_like(vec_ref)

    half = place_ref[HALF]
    eighth = states // 2
    zero = (jnp.zeros((chunks, LANES), F32),) * states
    for n in range(states):
        h_ref[pl.ds(n * chunks, chunks), :] = zero[0]
    spread_lanes(bc_ref, wide_ref)
    block = states * chunks

    def put_terms(which, t, terms):
        for n in range(0, states, 2):
            pair = jnp.concatenate(terms[n : n + 2]).astype(BF16)
            terms_ref[which, aligned(t * block + n * chunks, 2 * chunks, 16), :] = pair

    def recompute(pair, h):
        for slot in range(2):
            t = 2 * pair + slot
            span = pl.ds(t, chunks, stride=count)
            sp = sp_ref[span, :]
            u = u_ref[span, :]
            dy = dy_ref[span, :]
            out = []
            terms = []
            for n in range(states):
                decay = jnp.exp2(sp * decay_ref[pl.ds(n * chunks, chunks), :])
                keep_ref[aligned(t * block + n * chunks, chunks), :] = decay
                now = decay * h[n] + u * every_row(wide_ref, b_at(n, eighth) * count + t, chunks)
                h_ref[aligned((t + 1) * block + n * chunks, chunks), :] = now
                terms.append(dy * now)
                out.append(now)
            h = tuple(out)
            put_terms(1, t, terms)
        return h

    lax.fori_loop(0, count // 2, recompute, zero)

    def retreat(back, carry):
        flows, totals = carry
        for slot in range(2):
            t = count - 1 - (2 * back + slot)
            span = pl.ds(t, chunks, stride=count)
            sp = sp_ref[span, :]
            u = u_ref[span, :]
            dy = dy_ref[span, :]
            out_flows = []
            out_totals = []
            terms = []
            d_sum = None
            s_sum = None
            for n in range(states):
                dh = flows[n] + dy * every_row(wide_ref, c_at(n, eighth) * count + t, chunks)
                place = aligned(t * block + n * chunks, chunks)
                flow = keep_ref[place, :] * dh
                out_flows.append(flow)
                q = flow * h_ref[place, :]
                out_totals.append(totals[n] + q * sp)
                d_term = q * decay_ref[pl.ds(n * chunks, chunks), :]
                s_term = dh * every_row(wide_ref, b_at(n, eighth) * count + t, chunks)
                d_sum = d_term if d_sum is None else d_sum + d_term
                s_sum = s_term if s_sum is None else s_sum + s_term
                terms.append(dh * u)
            s_ref[span, :] = s_sum
            d_ref[span, :] = d_sum
            put_terms(0, t, terms)
            flows, totals = tuple(out_flows), tuple(out_totals)
        return flows, totals

    _, totals = lax.fori_loop(0, count // 2, retreat, (zero, zero))
    for n in range(states):
        alog_ref[pl.ds(n * chunks, chunks), :] += totals[n]

    shape = (2 * states, 2 * block)
    group = lax.broadcasted_iota(jnp.int32, shape, 1) // chunks
    gather = jnp.where(group == lax.broadcasted_iota(jnp.int32, shape, 0), 1.0, 0.0).astype(BF16)

    @pl.loop(0, count // 16)
    def _(step):
        for which, sums_ref in ((0, sums_b_ref), (1, sums_c_ref)):
            for k in range(8):
                at = 8 * step + k
                terms = terms_ref[which, aligned(at * 2 * block, 2 * block, 16), :]
                sums_ref[aligned(at * 2 * states, 2 * states), :] = dot(gather, terms, 1, 0)

    rank = rank_ref[...]
    ranks = rank.shape[1]
    drank = None
    for chunk in range(chunks):
        cols = slice(chunk * LANES, (chunk + 1) * LANES)
        place = pl.ds(chunk * count, count)
        act = act_ref[:, cols].astype(F32)
        weight = dt_ref[:, lanes(2 * chunk + half)]
        pre = dot(rank, weight, 1, 0) + bias_ref[pl.ds(2 * chunk + half, 1), :]
        s_now = s_ref[place, :]
        dstep = d_ref[place, :] * (1.0 / LOG2E) + s_now * act
        sact_ref[:, cols] = s_now * softplus(pre)
        dpre = dstep * sigmoid(pre)
        vec_ref[0:1, cols] += jnp.sum(dpre, axis=0, keepdims=True)
        vec_ref[1:2, cols] += jnp.sum(dy_ref[place, :] * act, axis=0, keepdims=True)
        low = dpre.astype(BF16)
        dpre_ref[:, cols] = low
        term = dot(low, weight, 1, 1)
        drank = term if drank is None else drank + term
    source = lax.broadcasted_iota(jnp.int32, (2 * LANES, LANES), 0)
    target = lax.broadcasted_iota(jnp.int32, (2 * LANES, LANES), 1)
    code = None
    for n in range(states):
        pair = jnp.concatenate(
            [ref[pl.ds(n, count, stride=states), :] for ref in (sums_b_ref, sums_c_ref)], axis=1
        )
        column = ranks + jnp.where(source < LANES, b_at(n, eighth), c_at(n, eighth))
        pick = jnp.where(target == column, 1.0, 0.0).astype(BF16)
        term = dot(pair.astype(BF16), pick, 1, 0)
        code = term if code is None else code + term
    code_ref[...] = code + jnp.concatenate([drank, jnp.zeros((count, LANES - ranks), F32)], axis=1)


def scan_backward(place, micros, bc, decay, rank, dt, bias, act, sp, u, dy):
    rows, own = act.shape
    count = rows // micros
    chunks = own // LANES
    states = bc.shape[1] // 2
    ranks = rank.shape[1]
    outs = [
        ((rows, LANES), F32),
        ((rows, own), F32),
        ((rows, own), BF16),
        ((states * chunks, LANES), F32),
        ((2, own), F32),
    ]

    def block(*shape):
        return pl.BlockSpec(shape, lambda i, p: (i, 0))

    return pl.pallas_call(
        functools.partial(backward_kernel, count=count, states=states, chunks=chunks),
        grid_spec=pltpu.PrefetchScalarGridSpec(
            num_scalar_prefetch=1,
            grid=(micros,),
            in_specs=[
                block(count, 2 * states),
                whole(decay.shape),
                block(count, ranks),
                whole(dt.shape),
                whole(bias.shape),
                block(count, own),
                block(chunks * count, LANES),
                block(chunks * count, LANES),
                block(chunks * count, LANES),
            ],
            out_specs=[block(count, LANES), block(count, own), block(count, own)]
            + [whole(shape) for shape, _ in outs[3:]],
            scratch_shapes=[
                pltpu.VMEM(((count + 1) * states * chunks, LANES), F32),
                pltpu.VMEM((count * states * chunks, LANES), F32),
                pltpu.VMEM((chunks * count, LANES), F32),
                pltpu.VMEM((chunks * count, LANES), F32),
                pltpu.VMEM((2, count * states * chunks, LANES), BF16),
                pltpu.VMEM((count * states, LANES), F32),
                pltpu.VMEM((count * states, LANES), F32),
                pltpu.VMEM((2 * states * count, LANES), F32),
            ],
        ),
        out_shape=[hbm(*out) for out in outs],
        compiler_params=params(48),
        cost_estimate=cost(0),
        name="scan_backward",
    )(place, *in_hbm((bc, decay, rank, dt, bias, act, sp, u, dy)))


def tail_kernel(
    place_ref,
    len_ref,
    *refs,
    micros,
    count,
    taps,
    clusters,
    ranks,
    chunks,
    states,
):
    def take(number):
        nonlocal refs
        taken, refs = refs[:number], refs[number:]
        return taken

    code_own_ref, code_other_ref = take(2)
    sact_ref, dpre_ref, alog_sum_ref, back_ref = take(4)
    dtx_ref, bc_own_ref, bc_other_ref, decay_ref = take(4)
    dy_refs = take(micros)
    conved_ref, inner_ref, act_ref, high_ref, convw_ref, skip_ref = take(6)
    normed_ref, weight_ref, share_ref, gain_ref = take(4)
    keep_ref, send_ref, low_ref = take(3)
    mask_ref, code_ref, wcode_ref, vec_ref, alog_ref, total_ref, win_ref, sems = refs

    step = pl.program_id(0)
    rows = micros * count
    eighth = states // 2
    edge = LANES // 2
    half, core, cube, face = (place_ref[k] for k in range(4))
    pair = step ^ face
    span = LANES + 32

    def fetch(k):
        source = weight_ref.at[0, pl.ds(2 * (k ^ face), 2), half]
        return (pltpu.make_async_copy(source, win_ref.at[k], sems.at[k]),)

    stream(step, win_ref.shape[0], fetch)

    def pack_row(chunk):
        relative = chunk ^ cube
        return (relative & 3) * span + LANES + (relative >> 2) * 16

    def place_pair(start, size, cols, even, odd):
        keep_ref[aligned(start, size, 16), cols] = jnp.where(core == 0, even, odd).astype(BF16)
        send_ref[aligned(start, size, 16), cols] = jnp.where(core == 0, odd, even).astype(BF16)

    @pl.when(step == 0)
    def _():
        fill_masks(len_ref, mask_ref, micros, count, taps, clusters)
        total_ref[...] = share_ref[...]
        code_ref[...] = (code_own_ref[...] + code_other_ref[...]).astype(BF16)
        alog_ref[...] = alog_sum_ref[...] * (decay_ref[...] * (1.0 / LOG2E))

    code = code_ref[...]
    lane = lax.broadcasted_iota(jnp.int32, (1, LANES), 1)
    code_rank = jnp.where(lane < ranks, code, jnp.zeros_like(code))
    dpre = dpre_ref[...]
    for part in range(2):
        source = lanes(2 * (2 * pair + part) + half)
        cols = slice(part * LANES, (part + 1) * LANES)
        wcode_ref[:ranks, cols] = dtx_ref[:, source]
        own = bc_own_ref[:, :, source].reshape(states, LANES)
        other = bc_other_ref[:, :, source].reshape(states, LANES)
        wcode_ref[ranks : ranks + states, cols] = jnp.where(half == 0, own, other)
        wcode_ref[ranks + states : ranks + 2 * states, cols] = jnp.where(half == 0, other, own)
        wcode_ref[ranks + 2 * states :, cols] = jnp.zeros(
            (LANES - ranks - 2 * states, LANES), BF16
        )
    for part in range(2):
        cols = slice(part * LANES, (part + 1) * LANES)
        chunk = 2 * pair + part
        source = 2 * chunk + half
        weights = convw_ref[:, lanes(source)]
        sact = sact_ref[:, cols]
        dy = jnp.concatenate([ref[pl.ds(part * count, count), :] for ref in dy_refs], axis=0)
        dact = sact + dot(code, wcode_ref[:, cols], 1, 0)
        dact = dact + dy * skip_ref[pl.ds(source, 1), :]
        conved = conved_ref[:, cols]
        sig = sigmoid(conved)
        dconv = dact * (sig * (1.0 + conved * (1.0 - sig)))
        inner = inner_ref[:, cols]
        dinner = weights[taps - 1 : taps] * dconv
        sums = [None] * (taps + 1)
        sums[taps - 1] = jnp.sum(dconv * inner, axis=0, keepdims=True)
        sums[taps] = jnp.sum(dconv, axis=0, keepdims=True)
        for back in range(1, taps):
            kept = dconv * mask_ref[back]
            dinner = dinner + weights[taps - 1 - back : taps - back] * pltpu.roll(
                kept, rows - back, 0
            )
            sums[taps - 1 - back] = jnp.sum(
                kept * pltpu.roll(inner, back, 0), axis=0, keepdims=True
            )
        for k in range(taps + 1):
            vec_ref[k : k + 1, lanes(chunk)] = sums[k]
        vec_ref[taps + 1 : taps + 3, lanes(chunk)] = back_ref[:, lanes(chunk)]
        low_ref[:, cols] = dinner.astype(BF16)

        act = act_ref[:, cols]
        start = pack_row(chunk)
        rows_now = dot(act, code_rank, 0, 0) + dot(dpre[:, cols], high_ref[...], 0, 0)
        for k in range(4):
            place_pair(
                start,
                16,
                slice(k * LANES, (k + 1) * LANES),
                rows_now[k * 16 : (k + 1) * 16],
                rows_now[edge + k * 16 : edge + (k + 1) * 16],
            )
        state_rows = dot(code, act, 0, 0)[ranks : ranks + 2 * states]
        place_pair(
            start, 16, slice(4 * LANES, 5 * LANES), state_rows[:states], state_rows[states:]
        )

    normed = normed_ref[...]
    for part in range(2):
        grad = dot(low_ref[:, lanes(core ^ part)], normed, 0, 0)
        total_ref[...] += eight_rows(grad * win_ref[step, core ^ part].astype(F32))
        out_ref = (keep_ref, send_ref)[part]
        out_ref[aligned(step * span, LANES, 16), :] = grad.astype(BF16)

    @pl.when(step == pl.num_programs(0) - 1)
    def _():
        vec_ref[taps + 3 : taps + 4, :] = (
            jnp.sum(total_ref[...], axis=0, keepdims=True) / gain_ref[...]
        )
        is_gain = lax.broadcasted_iota(jnp.int32, (8, LANES), 0) == taps + 3
        for chunk in range(chunks):
            start = pack_row(chunk)
            vec = vec_ref[:, chunk * LANES : (chunk + 1) * LANES]
            far, farther = (pltpu.roll(vec, LANES - k * edge // 2, 1) for k in (1, 2))
            even = jnp.where(is_gain & (lane >= edge // 2), far, vec)
            odd = jnp.where(is_gain & (lane < edge // 2), far, farther)
            alog = [
                alog_ref[pl.ds(q * eighth * chunks + chunk, eighth, stride=chunks), :]
                for q in range(2)
            ]
            place_pair(
                start,
                16,
                slice(5 * LANES, 6 * LANES),
                jnp.concatenate([alog[0], even]),
                jnp.concatenate([alog[1], odd]),
            )
            blank = jnp.zeros((16, 2 * LANES), F32)
            place_pair(start, 16, slice(6 * LANES, 8 * LANES), blank, blank)


def tail(
    place,
    lengths,
    code_own,
    code_other,
    sact,
    dpre,
    alog,
    back,
    dtx,
    bc_own,
    bc_other,
    decay,
    dy,
    conved,
    inner,
    act,
    high,
    convw,
    skip,
    normed,
    w4,
    share,
    gain,
):
    rows, own = act.shape
    chunks = own // LANES
    width = normed.shape[1]
    micros, _, clusters = lengths.shape
    count = rows // micros
    taps = convw.shape[0]
    ranks = dtx.shape[0]
    states = decay.shape[0] // chunks
    cols = 2 * LANES
    extent = 4 * (LANES + 32)

    def by_cols(height):
        return pl.BlockSpec((height, cols), lambda i, p: (0, i ^ p[FACE]))

    def dy_spec(micro):
        return pl.BlockSpec(
            (2 * count, LANES), lambda i, p: (micro * (chunks // 2) + (i ^ p[FACE]), 0)
        )

    in_specs = (
        [pl.BlockSpec(memory_space=pltpu.SMEM)]
        + [whole((rows, LANES))] * 2
        + [by_cols(rows)] * 2
        + [whole(alog.shape), whole(back.shape)]
        + [whole(array.shape) for array in (dtx, bc_own, bc_other, decay)]
        + [dy_spec(micro) for micro in range(micros)]
        + [by_cols(rows)] * 3
        + [whole(array.shape) for array in (high, convw, skip, normed)]
        + [
            ANY,
            whole(share.shape),
            whole(gain.shape),
        ]
    )
    return pl.pallas_call(
        functools.partial(
            tail_kernel,
            micros=micros,
            count=count,
            taps=taps,
            clusters=clusters,
            ranks=ranks,
            chunks=chunks,
            states=states,
        ),
        grid_spec=pltpu.PrefetchScalarGridSpec(
            num_scalar_prefetch=1,
            grid=(chunks // 2,),
            in_specs=in_specs,
            out_specs=[
                whole((extent, width)),
                whole((extent, width)),
                pl.BlockSpec((rows, cols), lambda i, p: (0, i ^ p[FACE])),
            ],
            scratch_shapes=[
                pltpu.VMEM((taps, rows, LANES), F32),
                pltpu.VMEM((rows, LANES), BF16),
                pltpu.VMEM((LANES, cols), BF16),
                pltpu.VMEM((8, own), F32),
                pltpu.VMEM((states * chunks, LANES), F32),
                pltpu.VMEM((8, width), F32),
                pltpu.VMEM((chunks // 2, 2, LANES, width), BF16),
                pltpu.SemaphoreType.DMA((chunks // 2,)),
            ],
        ),
        out_shape=[
            hbm((extent, width), BF16),
            hbm((extent, width), BF16),
            hbm((rows, own), BF16),
        ],
        compiler_params=params(30),
        cost_estimate=cost(7),
        name="tail",
    )(
        place,
        lengths,
        *in_hbm([code_own]),
        code_other,
        *in_hbm(
            (
                sact,
                dpre,
                alog,
                back,
                dtx,
                bc_own,
                bc_other,
                decay,
                *([dy] * micros),
                conved,
                inner,
                act,
                high,
                convw,
                skip,
                normed,
                w4,
                share,
                gain,
            )
        ),
    )


def fetch_halves(source, which, half, target_ref, sems):
    copies = []
    for k in range(target_ref.shape[0]):
        pair = pl.ds(2 * k, 2)
        block = source.at[pair, half] if which is None else source.at[which, pair, half]
        copies.append(pltpu.make_async_copy(block, target_ref.at[k], sems.at[k]))
    for copy in copies:
        copy.start()
    return copies


def products_kernel(
    place_ref,
    gated_ref,
    dgate_ref,
    out_ref,
    weight_ref,
    mixed_ref,
    dnormed_ref,
    wout_ref,
    wgate_ref,
    out_sems,
    gate_sems,
):
    half = place_ref[HALF]
    width = mixed_ref.shape[1]
    jobs = (
        (fetch_halves(out_ref, None, half, wout_ref, out_sems), gated_ref, wout_ref, mixed_ref),
        (fetch_halves(weight_ref, 1, half, wgate_ref, gate_sems), dgate_ref, wgate_ref, dnormed_ref),
    )
    for copies, left_ref, right_ref, result_ref in jobs:
        total = None
        for k, copy in enumerate(copies):
            copy.wait()
            left = left_ref[:, 2 * k * LANES : 2 * (k + 1) * LANES]
            term = dot(left, right_ref[k].reshape(-1, width), 1, 0)
            total = term if total is None else total + term
        result_ref[...] = total.astype(BF16)


def products(place, gated, dgate, wout3, w4):
    rows, own = gated.shape
    width = w4.shape[-1]
    pairs = own // (2 * LANES)
    return pl.pallas_call(
        products_kernel,
        grid_spec=pltpu.PrefetchScalarGridSpec(
            num_scalar_prefetch=1,
            grid=(1,),
            in_specs=[whole((rows, own)), whole((rows, own)), ANY, ANY],
            out_specs=[whole((rows, width))] * 2,
            scratch_shapes=[
                pltpu.VMEM((pairs, 2, LANES, width), BF16),
                pltpu.VMEM((pairs, 2, LANES, width), BF16),
                pltpu.SemaphoreType.DMA((pairs,)),
                pltpu.SemaphoreType.DMA((pairs,)),
            ],
        ),
        out_shape=[hbm((rows, width), BF16)] * 2,
        compiler_params=params(20),
        cost_estimate=cost(4),
        name="products",
    )(place, *in_hbm((gated, dgate, wout3, w4)))


def spread_kernel(place_ref, low_ref, weight_ref, gate_ref, dnormed_ref, win_ref, sems):
    width = gate_ref.shape[1]
    total = gate_ref[...].astype(F32)
    for k, copy in enumerate(fetch_halves(weight_ref, 0, place_ref[HALF], win_ref, sems)):
        copy.wait()
        left = low_ref[:, 2 * k * LANES : 2 * (k + 1) * LANES]
        total = total + dot(left, win_ref[k].reshape(-1, width), 1, 0)
    dnormed_ref[...] = total.astype(BF16)


def spread(place, low, w4, gate_part):
    rows, own = low.shape
    width = w4.shape[-1]
    pairs = own // (2 * LANES)
    return pl.pallas_call(
        spread_kernel,
        grid_spec=pltpu.PrefetchScalarGridSpec(
            num_scalar_prefetch=1,
            grid=(1,),
            in_specs=[whole((rows, own)), ANY, whole((rows, width))],
            out_specs=whole((rows, width)),
            scratch_shapes=[
                pltpu.VMEM((pairs, 2, LANES, width), BF16),
                pltpu.SemaphoreType.DMA((pairs,)),
            ],
        ),
        out_shape=hbm((rows, width), BF16),
        compiler_params=params(16),
        cost_estimate=cost(3),
        name="spread",
    )(place, *in_hbm((low, w4, gate_part)))


def finish_kernel(x_ref, mine_ref, theirs_ref, cotan_ref, gain_ref, grad_ref):
    x = x_ref[...].astype(F32)
    scale = lax.rsqrt(jnp.mean(x * x, axis=1, keepdims=True) + EPSILON)
    unit = x * scale
    dhat = (mine_ref[...].astype(F32) + theirs_ref[...].astype(F32)) * gain_ref[...]
    grad_ref[...] = cotan_ref[...].astype(F32) + scale * (
        dhat - unit * jnp.mean(dhat * unit, axis=1, keepdims=True)
    )


def finish(x, mine, theirs, cotan, gain):
    rows, width = x.shape
    by_rows = pl.BlockSpec((rows // 4, width), lambda i: (i, 0))
    return pl.pallas_call(
        finish_kernel,
        grid=(4,),
        in_specs=[by_rows] * 4 + [whole(gain.shape)],
        out_specs=by_rows,
        out_shape=jax.ShapeDtypeStruct((rows, width), F32),
        compiler_params=params(16),
        cost_estimate=cost(0),
        name="finish",
    )(*in_hbm((x, mine)), theirs, *in_hbm((cotan, gain)))


def unpack_kernel(
    near_ref,
    far_ref,
    out_ref,
    dtx_ref,
    dt_ref,
    bc_ref,
    alog_ref,
    convw_ref,
    convb_ref,
    bias_ref,
    skip_ref,
    out_grad_ref,
    *,
    eighth,
    taps,
    edge,
):
    pack = near_ref[...].astype(F32) + far_ref[...].astype(F32)
    for k in range(4):
        rows = pack[:, k * LANES : (k + 1) * LANES]
        dtx_ref[pl.ds(16 * k, 16), :] = rows[:, :edge]
        dt_ref[pl.ds(16 * k, 16), :] = pltpu.roll(rows, edge, 1)[:, :edge]
    rows = pack[:, 4 * LANES : 5 * LANES]
    bc_ref[0] = rows[:eighth]
    bc_ref[1] = rows[eighth:]
    rows = pack[:, 5 * LANES : 6 * LANES]
    alog_ref[...] = rows[:eighth]
    vec = rows[eighth:, :edge]
    convw_ref[...] = vec[:taps]
    convb_ref[...] = vec[taps : taps + 1]
    bias_ref[...] = vec[taps + 1 : taps + 2]
    skip_ref[...] = vec[taps + 2 : taps + 3]
    out_grad_ref[...] = out_ref[...].astype(F32)


def unpack(near, far, out, eighth, taps, ranks):
    edge = LANES // 2
    shapes = [
        (edge, ranks),
        (edge, ranks),
        (2, eighth, LANES),
        (eighth, LANES),
        (taps, edge),
        (1, edge),
        (1, edge),
        (1, edge),
        out.shape,
    ]
    return pl.pallas_call(
        functools.partial(unpack_kernel, eighth=eighth, taps=taps, edge=edge),
        grid=(1,),
        in_specs=[whole(array.shape) for array in (near, far, out)],
        out_specs=[whole(shape) for shape in shapes],
        out_shape=[jax.ShapeDtypeStruct(shape, F32) for shape in shapes],
        cost_estimate=cost(0),
        name="unpack",
    )(near, far, out)


def swap_pair(array):
    count = lax.axis_size("state")
    return lax.ppermute(array, "state", [(pos, pos ^ 1) for pos in range(count)])


def swap_bit(array, bits):
    return lax.ppermute(array, "dp", [(pos, pos ^ bits) for pos in range(lax.axis_size("dp"))])


def swap_both(array, bits=0):
    states = lax.axis_size("state")
    pairs = []
    for d in range(lax.axis_size("dp")):
        for s in range(states):
            pairs.append((d * states + s, (((d & ~1) | s) ^ bits) * states + (d & 1)))
    return lax.ppermute(array, ("dp", "state"), pairs)


def add_quarters(kept, got):
    extent = kept.shape[0] // 4
    return [kept[k * extent :][:extent] + got[k * extent :][:extent] for k in range(4)]


def trade_quarters(quarters):
    return [quarters[0]] + [swap_bit(quarters[k], k * X_BIT) for k in range(1, 4)]


def sum_quarters(quarters):
    left, right = (quarters[k].astype(F32) + quarters[k + 1].astype(F32) for k in (0, 2))
    return (left + right).astype(BF16)


CORE_BIT, X_BIT, ZH_BIT = 1, 2, 8


def shards(
    tokens,
    cluster_len,
    norm_gain,
    in_weight,
    conv_weight,
    conv_bias,
    dtx_weight,
    dt_weight,
    dt_bias,
    bc_weight,
    a_log,
    skip_gain,
    out_weight,
    cotangent,
):
    micros, count, width = tokens.shape
    inner = out_weight.shape[0]
    taps = conv_weight.shape[0]
    ranks = dtx_weight.shape[1]
    chunks = inner // (2 * LANES)
    own = chunks * LANES
    rows = micros * count
    edge = LANES // 2
    span = LANES + 32
    dp_parts = lax.axis_size("dp")
    state_count = lax.axis_size("state")
    dp_pos = lax.axis_index("dp")
    state_pos = lax.axis_index("state")
    half = state_pos & 1
    fast = state_count == 2 and dp_parts == 2 * chunks == 16
    if fast:
        place = jnp.stack([half, dp_pos & 1, dp_pos >> 1, (dp_pos >> 1) & 3])
        bc_own, alog_own = bc_weight, a_log
        bc_other, alog_other = swap_pair(bc_weight), swap_pair(a_log)
    else:
        place = jnp.stack([half, 0, 0, 0])
        bc_all = lax.all_gather(bc_weight, "state", axis=1, tiled=True)
        alog_all = lax.all_gather(a_log, "state", axis=0, tiled=True)
        eighth = alog_all.shape[0] // 2
        bc_own, bc_other = (
            lax.dynamic_slice_in_dim(bc_all, which * eighth, eighth, 1)
            for which in (half, 1 - half)
        )
        alog_own, alog_other = (
            lax.dynamic_slice_in_dim(alog_all, which * eighth, eighth, 0)
            for which in (half, 1 - half)
        )
    place = place.astype(jnp.int32)
    eighth = alog_own.shape[0]
    states = 2 * eighth

    x = tokens.reshape(rows, width)
    cotan = cotangent.reshape(rows, width)
    w4 = in_weight.reshape(2, chunks, 2, LANES, width)
    wout3 = out_weight.reshape(chunks, 2, LANES, width)
    dtx, dt = dtx_weight.T, dt_weight.T
    bias = dt_bias.reshape(-1, LANES)
    skip = skip_gain.reshape(-1, LANES)

    normed, act_all, act, inner_own, conved, gate = project(
        place, cluster_len, x, norm_gain[None], w4, conv_weight, conv_bias.reshape(-1, LANES)
    )
    bc, rank, high, decay, share, sp, u, dy, gated, dgate, keep, send = scan_forward(
        place,
        cluster_len,
        act_all,
        bc_own,
        bc_other,
        alog_own,
        alog_other,
        dtx,
        dt,
        bias,
        skip,
        act,
        gate,
        wout3,
        cotan,
        normed,
        w4,
    )
    if fast:
        early = swap_bit(send, CORE_BIT)
    mixed_part, dn_gate = products(place, gated, dgate, wout3, w4)
    if fast:
        *quarters, mixed_part, dn_gate, sp = lax.optimization_barrier(
            (*add_quarters(keep, early), mixed_part, dn_gate, sp)
        )
        early_got = trade_quarters(quarters)
    mixed_other = swap_pair(mixed_part)
    code_own, sact, dpre, alog, back = scan_backward(
        place, micros, bc, decay, rank, dt, bias, act, sp, u, dy
    )
    code_other = swap_pair(code_own)
    if fast:
        block = sum_quarters(early_got)
        out_keep, out_send, gate_sum = block[:edge], block[edge:LANES], block[LANES:]
        out_send, gate_sum, mixed_other, conved = lax.optimization_barrier(
            (out_send, gate_sum, mixed_other, conved)
        )
        out_got = swap_bit(out_send, ZH_BIT)
    late_keep, late_send, low = tail(
        place,
        cluster_len,
        code_own,
        code_other,
        sact,
        dpre,
        alog,
        back,
        dtx,
        bc_own,
        bc_other,
        decay,
        dy,
        conved,
        inner_own,
        act,
        high,
        conv_weight,
        skip,
        normed,
        w4,
        share,
        norm_gain[None],
    )
    if fast:
        late = swap_bit(late_send, CORE_BIT)
        out_own = swap_both(out_keep + out_got)
        late_got = trade_quarters(add_quarters(late_keep, late))
    dnormed_part = spread(place, low, w4, dn_gate)
    dnormed_other = swap_pair(dnormed_part)
    mixed = (x.astype(F32) + (mixed_part.astype(F32) + mixed_other.astype(F32))).astype(BF16)
    if fast:
        *late_got, mixed, out_own, dnormed_other = lax.optimization_barrier(
            (*late_got, mixed, out_own, dnormed_other)
        )
        block = sum_quarters(late_got)
        inner_sum = block[:LANES]
        upper = dp_pos >= dp_parts // 2
        crossing = jnp.where(upper, inner_sum, gate_sum)
        first, second = crossing[:edge], crossing[edge:]
        first, pack_far, pack_near = lax.optimization_barrier(
            (first, block[-16:], block[LANES:-16])
        )
        pack_far = swap_both(pack_far, ZH_BIT)
        first_got = swap_bit(first, ZH_BIT)
        pack_near = swap_both(pack_near)
        first_got, pack_far, pack_near = lax.optimization_barrier((first_got, pack_far, pack_near))
        second_got = swap_bit(second, ZH_BIT)
        tokens_grad = finish(x, dnormed_part, dnormed_other, cotan, norm_gain[None])
        gain_mine = (
            pack_near[:, 5 * LANES : 6 * LANES].astype(F32)
            + pack_far[:, 5 * LANES : 6 * LANES].astype(F32)
        ).astype(BF16)
        gain_both = gain_mine[-1].astype(F32) + swap_bit(gain_mine, CORE_BIT)[-1].astype(F32)
        extent = width // (dp_parts * state_count)
        gain_grad = lax.dynamic_slice_in_dim(gain_both, (dp_pos & 1) * extent, extent, 0)
        (
            dtx_grad,
            dt_grad,
            bc_grad,
            alog_grad,
            convw_grad,
            convb_grad,
            bias_grad,
            skip_grad,
            out_own,
        ) = unpack(pack_near, pack_far, out_own, eighth, taps, ranks)
        convb_grad, bias_grad, skip_grad = (
            array[0] for array in (convb_grad, bias_grad, skip_grad)
        )
        in_grad = jnp.where(upper, gate_sum, inner_sum).astype(F32) + jnp.concatenate(
            [first_got, second_got]
        ).astype(F32)
    else:
        tokens_grad = finish(x, dnormed_part, dnormed_other, cotan, norm_gain[None])
    mixed = mixed.reshape(micros, count, width)
    tokens_grad = tokens_grad.reshape(micros, count, width)

    if not fast:
        def total(array):
            return lax.psum(array.astype(F32), "dp")

        def both_rows(array):
            mine = array.reshape(chunks, 1, LANES, -1)
            other = swap_pair(mine)
            low = jnp.where(half == 0, mine, other)
            high = jnp.where(half == 0, other, mine)
            return jnp.concatenate([low, high], axis=1).reshape(2 * own, -1)

        every = dp_parts * state_count
        at = dp_pos * state_count + state_pos

        def cut_own(array):
            extent = array.shape[0] // every
            return lax.dynamic_slice_in_dim(array, at * extent, extent, 0)

        pair = total(jnp.stack([keep, send])).reshape(2, 2, 2, 2 * LANES, width)
        outs = pair[:, :, :, :LANES].reshape(2, 2, 2, 2, edge, width)
        outs = jnp.transpose(outs, (3, 1, 2, 0, 4, 5)).reshape(own, width)
        gates = jnp.moveaxis(pair[:, :, :, LANES:], 0, 2).reshape(own, width)
        pair = total(jnp.stack([late_keep, late_send])).reshape(2, 2, 2, span, width)
        inners = jnp.moveaxis(pair[:, :, :, :LANES], 0, 2).reshape(own, width)
        packs = pair[:, :, :, LANES:].reshape(2, 2, 2, 2, 16, width // LANES, LANES)
        packs = jnp.transpose(packs, (3, 1, 2, 0, 5, 4, 6)).reshape(chunks, 2, -1, 16, LANES)
        small = both_rows(packs[:, :, :4].reshape(own, LANES))
        in_grad = cut_own(jnp.concatenate([both_rows(inners), both_rows(gates)]))
        out_own = cut_own(both_rows(outs))
        mine = cut_own(small)
        dtx_grad, dt_grad = mine[:, :ranks], mine[:, ranks:]
        vec_rows = jnp.swapaxes(packs[:, :, 5, eighth:, :edge], 2, 3).reshape(own, -1)
        gain_sum = vec_rows[:, -1].reshape(chunks, 2, 2, -1).swapaxes(1, 2).reshape(-1)
        gain_grad = cut_own(gain_sum + swap_pair(gain_sum))
        vec = cut_own(both_rows(vec_rows)).T
        state_rows = jnp.concatenate([packs[:, :, 4], packs[:, :, 5, :eighth]], axis=2)
        state_rows = state_rows.reshape(chunks, 2, 3, eighth, LANES)
        state_rows = jnp.transpose(state_rows, (0, 4, 2, 1, 3)).reshape(own, -1)
        extent = inner // dp_parts
        state_part = lax.dynamic_slice_in_dim(both_rows(state_rows), dp_pos * extent, extent, 0)
        state_part = state_part.T.reshape(3, state_count, -1, extent)
        state_part = lax.dynamic_index_in_dim(state_part, state_pos, 1, keepdims=False)
        bc_grad, alog_grad = state_part[:2], state_part[2]
        convw_grad, convb_grad, bias_grad, skip_grad = (
            vec[:taps], vec[taps], vec[taps + 1], vec[taps + 2]
        )

    return (
        mixed,
        tokens_grad,
        gain_grad,
        in_grad,
        convw_grad,
        convb_grad,
        dtx_grad,
        dt_grad,
        bias_grad,
        bc_grad,
        alog_grad,
        skip_grad,
        out_own,
    )


def solution(mesh):
    return jax.shard_map(
        shards,
        mesh=mesh,
        in_specs=(
            P(None, "dp", None),
            P(None, "dp", None),
            P(),
            P(),
            P(),
            P(),
            P(),
            P(),
            P(),
            P(None, "state", None),
            P("state", None),
            P(),
            P(),
            P(None, "dp", None),
        ),
        out_specs=(
            P(None, "dp", None),
            P(None, "dp", None),
            P(("dp", "state")),
            P(("dp", "state"), None),
            P(None, ("dp", "state")),
            P(("dp", "state")),
            P(("dp", "state"), None),
            P(("dp", "state"), None),
            P(("dp", "state")),
            P(None, "state", "dp"),
            P("state", "dp"),
            P(("dp", "state")),
            P(("dp", "state"), None),
        ),
        check_vma=False,
    )
```

```python
import functools
import math

import jax
import jax.numpy as jnp
from jax import lax
from jax.experimental import pallas as pl
from jax.experimental.pallas import tpu as pltpu
from jax.sharding import PartitionSpec as P

EPSILON = 1e-05
LANES = 128
RESET = 1e4
LOG2E = math.log2(math.e)
F32 = jnp.float32
BF16 = jnp.bfloat16
MIB = 1024 * 1024


def dot(left, right, left_dim, right_dim):
    return lax.dot_general(
        left, right, (((left_dim,), (right_dim,)), ((), ())), preferred_element_type=F32
    )


def params(mib):
    return pltpu.CompilerParams(
        vmem_limit_bytes=mib * MIB, dimension_semantics=("arbitrary",)
    )


ANY = pl.BlockSpec(memory_space=pl.ANY)


def stream(step, steps, fetch):
    @pl.when(step == 0)
    def _():
        for k in range(steps):
            for copy in fetch(k):
                copy.start()

    for copy in fetch(step):
        copy.wait()


def whole(shape):
    return pl.BlockSpec(shape, lambda *_: (0,) * len(shape))


sigmoid = jax.nn.sigmoid


def softplus(value):
    return jnp.maximum(value, 0.0) + jnp.log1p(jnp.exp(-jnp.abs(value)))


def lanes(index):
    return pl.ds(pl.multiple_of(index * LANES, LANES), LANES)


def cost(micros):
    return pl.CostEstimate(
        flops=int(micros * 1e9), bytes_accessed=int(micros * 1e6), transcendentals=0
    )


def hbm(shape, dtype):
    return pltpu.HBM(shape, dtype)


def in_hbm(arrays):
    return [pltpu.with_memory_space_constraint(array, pltpu.HBM) for array in arrays]


def aligned(start, size, to=8):
    return pl.ds(pl.multiple_of(start, to), size)


HALF, CORE, CUBE, FACE = range(4)


def fill_masks(len_ref, mask_ref, micros, count, taps, clusters):
    place = lax.broadcasted_iota(jnp.int32, (count, LANES), 0)
    for micro in range(micros):
        rows = pl.ds(micro * count, count)
        for back in range(1, taps):
            apart = place < back
            start = 0
            for cluster in range(clusters - 1):
                start = start + len_ref[micro, 0, cluster]
                apart = apart | ((place >= start) & (place < start + back))
            mask_ref[back, rows, :] = jnp.where(apart, 0.0, 1.0)
            if back == 1:
                mask_ref[0, rows, :] = jnp.where(apart, 1.0, 0.0)


def project_kernel(
    place_ref,
    len_ref,
    gain_ref,
    convw_ref,
    convb_ref,
    x_far,
    weight_far,
    normed_far,
    act_far,
    own_act_far,
    inner_far,
    conved_far,
    gate_far,
    mask_ref,
    x_ref,
    win_ref,
    wgate_ref,
    normed_ref,
    act_ref,
    own_act_ref,
    inner_ref,
    conved_ref,
    gate_ref,
    in_sems,
    out_sems,
    *,
    micros,
    count,
    taps,
    clusters,
):
    half = place_ref[HALF]
    chunks = win_ref.shape[0]
    inward = [pltpu.make_async_copy(x_far, x_ref, in_sems.at[2 * chunks])]
    for k in range(chunks):
        inward.append(pltpu.make_async_copy(weight_far.at[0, k], win_ref.at[k], in_sems.at[2 * k]))
        inward.append(
            pltpu.make_async_copy(
                weight_far.at[1, k, half], wgate_ref.at[k], in_sems.at[2 * k + 1]
            )
        )
    for copy in inward:
        copy.start()
    outward = []

    def put(source, target):
        outward.append(pltpu.make_async_copy(source, target, out_sems.at[len(outward)]))
        outward[-1].start()

    fill_masks(len_ref, mask_ref, micros, count, taps, clusters)
    inward[0].wait()
    rows = x_ref[...].astype(F32)
    scale = lax.rsqrt(jnp.mean(rows * rows, axis=1, keepdims=True) + EPSILON)
    normed = (rows * scale * gain_ref[...]).astype(BF16)
    normed_ref[...] = normed
    put(normed_ref, normed_far)
    for k in range(chunks):
        inward[2 * k + 1].wait()
        inward[2 * k + 2].wait()
        proj = dot(normed, win_ref[k].reshape(2 * LANES, -1), 1, 1)
        own = slice(k * LANES, (k + 1) * LANES)
        gate_ref[:, own] = dot(normed, wgate_ref[k], 1, 1)
        inners, conveds, acts = [], [], []
        for part in range(2):
            cols = slice((2 * k + part) * LANES, (2 * k + part + 1) * LANES)
            inner = proj[:, part * LANES : (part + 1) * LANES]
            conved = convb_ref[2 * k + part : 2 * k + part + 1, :]
            conved = conved + convw_ref[taps - 1 : taps, cols] * inner
            for back in range(1, taps):
                shifted = pltpu.roll(inner, back, 0) * mask_ref[back]
                conved = conved + convw_ref[taps - 1 - back : taps - back, cols] * shifted
            act = conved * sigmoid(conved)
            act_ref[:, cols] = act.astype(BF16)
            inners.append(inner)
            conveds.append(conved)
            acts.append(act)
        inner_ref[:, own] = jnp.where(half == 0, *inners)
        conved_ref[:, own] = jnp.where(half == 0, *conveds)
        own_act_ref[:, own] = jnp.where(half == 0, *acts).astype(BF16)
        if k % 2:
            group = pl.ds((k - 1) * LANES, 2 * LANES)
            wide = pl.ds(2 * (k - 1) * LANES, 4 * LANES)
            put(act_ref.at[:, wide], act_far.at[:, wide])
            for near, far in (
                (gate_ref, gate_far),
                (inner_ref, inner_far),
                (conved_ref, conved_far),
                (own_act_ref, own_act_far),
            ):
                put(near.at[:, group], far.at[:, group])
    for copy in outward:
        copy.wait()


def project(place, lengths, x, gain, w4, conv_weight, conv_bias):
    rows, width = x.shape
    chunks = w4.shape[1]
    micros, _, clusters = lengths.shape
    taps = conv_weight.shape[0]
    own = chunks * LANES
    outs = [
        ((rows, width), BF16),
        ((rows, 2 * own), BF16),
        ((rows, own), BF16),
        ((rows, own), F32),
        ((rows, own), F32),
        ((rows, own), F32),
    ]
    return pl.pallas_call(
        functools.partial(
            project_kernel, micros=micros, count=rows // micros, taps=taps, clusters=clusters
        ),
        grid_spec=pltpu.PrefetchScalarGridSpec(
            num_scalar_prefetch=1,
            grid=(1,),
            in_specs=[
                pl.BlockSpec(memory_space=pltpu.SMEM),
                whole(gain.shape),
                whole(conv_weight.shape),
                whole(conv_bias.shape),
                ANY,
                ANY,
            ],
            out_specs=[ANY] * len(outs),
            scratch_shapes=[
                pltpu.VMEM((taps, rows, LANES), F32),
                pltpu.VMEM((rows, width), BF16),
                pltpu.VMEM((chunks, 2, LANES, width), BF16),
                pltpu.VMEM((chunks, LANES, width), BF16),
            ]
            + [pltpu.VMEM(*out) for out in outs]
            + [
                pltpu.SemaphoreType.DMA((2 * chunks + 1,)),
                pltpu.SemaphoreType.DMA((1 + 5 * chunks // 2,)),
            ],
        ),
        out_shape=[hbm(*out) for out in outs],
        compiler_params=params(30),
        cost_estimate=cost(6),
        name="project",
    )(place, *in_hbm((lengths, gain, conv_weight, conv_bias, x, w4)))


def eight_rows(array):
    return jnp.sum(array.reshape(-1, 8, array.shape[1]), axis=0)


def every_row(ref, row, height):
    return ref[pl.ds(row, height, stride=0), :]


def b_at(n, eighth):
    return (n // eighth) * 2 * eighth + n % eighth


def c_at(n, eighth):
    return b_at(n, eighth) + eighth


def forward_kernel(
    place_ref,
    len_ref,
    act_all_ref,
    bc_own_ref,
    bc_other_ref,
    alog_own_ref,
    alog_other_ref,
    dtx_ref,
    dt_ref,
    bias_ref,
    skip_ref,
    act_ref,
    *refs,
    micros,
    count,
    states,
    chunks,
    clusters,
):
    gate_far, wout_far, cotan_far, normed_far, weight_far = refs[:5]
    bc_ref, rank_ref, rank_high_ref, decay_ref, share_ref = refs[5:10]
    sp_far, u_far, dy_far, gated_far, dgate_far, keep_far, send_far = refs[10:17]
    mask_ref, y_ref, tmp_ref, wide_ref = refs[17:21]
    gate_ref, wout_ref, cotan_ref, normed_ref, wgate_ref = refs[21:26]
    sp_ref, u_ref, dy_ref, gated_ref, dgate_ref, keep_ref, send_ref = refs[26:33]
    in_sems, out_sems = refs[33:]
    rows = micros * count
    eighth = states // 2
    half, core, cube, face = (place_ref[k] for k in range(4))
    first = half == 0
    inward = [
        pltpu.make_async_copy(source, target, in_sems.at[k])
        for k, (source, target) in enumerate(
            (
                (gate_far, gate_ref),
                (wout_far.at[:, half], wout_ref),
                (cotan_far, cotan_ref),
                (normed_far, normed_ref),
                (weight_far.at[1, :, half], wgate_ref),
            )
        )
    ]
    for copy in inward:
        copy.start()
    outward = []

    def put(source, target):
        outward.append(pltpu.make_async_copy(source, target, out_sems.at[len(outward)]))
        outward[-1].start()

    act_all = act_all_ref[...]
    own = dot(act_all, bc_own_ref[...].reshape(states, -1), 1, 1)
    other = dot(act_all, bc_other_ref[...].reshape(states, -1), 1, 1)
    bc_ref[:, :states] = jnp.where(first, own, other)
    bc_ref[:, states:] = jnp.where(first, other, own)
    spread_lanes(bc_ref, wide_ref)

    fill_masks(len_ref, mask_ref, micros, count, 2, clusters)
    for chunk in range(chunks):
        cols = lanes(2 * chunk + half)
        own, other = alog_own_ref[:, cols], alog_other_ref[:, cols]
        tmp_ref[pl.ds(chunk * states, eighth), :] = jnp.where(first, own, other)
        tmp_ref[pl.ds(chunk * states + eighth, eighth), :] = jnp.where(first, other, own)
    for n in range(states):
        decay_ref[pl.ds(n * chunks, chunks), :] = -LOG2E * jnp.exp(
            tmp_ref[pl.ds(n, chunks, stride=states), :]
        )

    rank = dot(act_all, dtx_ref[...], 1, 1).astype(BF16)
    rank_ref[...] = rank
    rank_high_ref[...] = jnp.concatenate([jnp.zeros_like(rank), rank], axis=1)
    for chunk in range(chunks):
        cols = slice(chunk * LANES, (chunk + 1) * LANES)
        bias = bias_ref[pl.ds(2 * chunk + half, 1), :]
        step = softplus(dot(rank, dt_ref[:, lanes(2 * chunk + half)], 1, 0) + bias)
        held = step + RESET * mask_ref[0]
        source = step * act_ref[:, cols].astype(F32)
        for micro in range(micros):
            span = slice(micro * count, (micro + 1) * count)
            place = pl.ds((micro * chunks + chunk) * count, count)
            sp_ref[place, :] = held[span]
            u_ref[place, :] = source[span]
    put(sp_ref, sp_far)
    put(u_ref, u_far)

    for micro in range(micros):

        def advance(t, h, micro=micro):
            row = micro * count + t
            span = pl.ds(micro * chunks * count + t, chunks, stride=count)
            sp = sp_ref[span, :]
            u = u_ref[span, :]
            out = []
            y = None
            for n in range(states):
                decay = jnp.exp2(sp * decay_ref[pl.ds(n * chunks, chunks), :])
                now = decay * h[n] + u * every_row(wide_ref, b_at(n, eighth) * rows + row, chunks)
                out.append(now)
                term = now * every_row(wide_ref, c_at(n, eighth) * rows + row, chunks)
                y = term if y is None else y + term
            y_ref[span, :] = y
            return tuple(out)

        lax.fori_loop(0, count, advance, (jnp.zeros((chunks, LANES), F32),) * states, unroll=2)

    for copy in inward:
        copy.wait()
    cotan = cotan_ref[...]
    for chunk in range(chunks):
        cols = slice(chunk * LANES, (chunk + 1) * LANES)
        places = [pl.ds((micro * chunks + chunk) * count, count) for micro in range(micros)]
        y = jnp.concatenate([y_ref[place, :] for place in places])
        y = y + skip_ref[pl.ds(2 * chunk + half, 1), :] * act_ref[:, cols].astype(F32)
        gate = gate_ref[:, cols]
        sig = sigmoid(gate)
        gated_ref[:, cols] = (y * (gate * sig)).astype(BF16)
        dgated = dot(cotan, wout_ref[chunk], 1, 1)
        dy = dgated * (gate * sig)
        for micro in range(micros):
            dy_ref[places[micro], :] = dy[micro * count : (micro + 1) * count]
        dgate_ref[:, cols] = (dgated * y * (sig * (1.0 + gate * (1.0 - sig)))).astype(BF16)
    put(dy_ref, dy_far)
    put(gated_ref, gated_far)
    put(dgate_ref, dgate_far)
    normed = normed_ref[...]
    edge = LANES // 2
    share = jnp.zeros(share_ref.shape, F32)
    for r in range(chunks // 2):
        for zh in range(2):
            grad = dot(gated_ref[:, lanes((r + 4 * zh) ^ cube)], cotan, 0, 0).astype(BF16)
            top, bottom = grad[:edge], grad[edge:]
            place = pl.ds(r * 2 * LANES + zh * edge, edge)
            keep_ref[place, :] = jnp.where(core == 0, top, bottom)
            send_ref[place, :] = jnp.where(core == 0, bottom, top)
        place = pl.ds((2 * r + 1) * LANES, LANES)
        pair = 2 * (r ^ face)
        for chunk, out_ref in ((pair + core, keep_ref), (pair + 1 - core, send_ref)):
            grad = dot(dgate_ref[:, lanes(chunk)], normed, 0, 0)
            share = share + eight_rows(grad * wgate_ref[chunk].astype(F32))
            out_ref[place, :] = grad.astype(BF16)
        place = pl.ds(r * 2 * LANES, 2 * LANES)
        put(send_ref.at[place], send_far.at[place])
        put(keep_ref.at[place], keep_far.at[place])
    share_ref[...] = share
    for copy in outward:
        copy.wait()


def scan_forward(
    place,
    lengths,
    act_all,
    bc_own,
    bc_other,
    alog_own,
    alog_other,
    dtx,
    dt,
    bias,
    skip,
    act,
    gate,
    wout3,
    cotan,
    normed,
    w4,
):
    rows, own = act.shape
    chunks = own // LANES
    states = 2 * alog_own.shape[0]
    width = cotan.shape[1]
    micros, _, clusters = lengths.shape
    ranks = dtx.shape[0]
    small = [
        ((rows, 2 * states), F32),
        ((rows, ranks), BF16),
        ((rows, 2 * ranks), BF16),
        ((states * chunks, LANES), F32),
        ((8, width), F32),
    ]
    large = [
        ((chunks * rows, LANES), F32),
        ((chunks * rows, LANES), F32),
        ((chunks * rows, LANES), F32),
        ((rows, own), BF16),
        ((rows, own), BF16),
        ((own, width), BF16),
        ((own, width), BF16),
    ]
    operands = (act_all, bc_own, bc_other, alog_own, alog_other, dtx, dt, bias, skip, act)
    streamed = (gate, wout3, cotan, normed, w4)
    return pl.pallas_call(
        functools.partial(
            forward_kernel,
            micros=micros,
            count=rows // micros,
            states=states,
            chunks=chunks,
            clusters=clusters,
        ),
        grid_spec=pltpu.PrefetchScalarGridSpec(
            num_scalar_prefetch=1,
            grid=(1,),
            in_specs=[pl.BlockSpec(memory_space=pltpu.SMEM)]
            + [whole(operand.shape) for operand in operands]
            + [ANY] * len(streamed),
            out_specs=[whole(shape) for shape, _ in small] + [ANY] * len(large),
            scratch_shapes=[
                pltpu.VMEM((2, rows, LANES), F32),
                pltpu.VMEM((chunks * rows, LANES), F32),
                pltpu.VMEM((states * chunks, LANES), F32),
                pltpu.VMEM((2 * states * rows, LANES), F32),
                pltpu.VMEM((rows, own), F32),
                pltpu.VMEM((chunks, LANES, width), BF16),
                pltpu.VMEM((rows, width), BF16),
                pltpu.VMEM((rows, width), BF16),
                pltpu.VMEM((chunks, LANES, width), BF16),
            ]
            + [pltpu.VMEM(*out) for out in large]
            + [pltpu.SemaphoreType.DMA((5,)), pltpu.SemaphoreType.DMA((5 + chunks,))],
        ),
        out_shape=[hbm(*out) for out in small + large],
        compiler_params=params(52),
        cost_estimate=cost(19),
        name="scan_forward",
    )(
        place,
        lengths,
        *in_hbm(operands[:1]),
        *operands[1:5],
        *in_hbm((*operands[5:], *streamed)),
    )


def spread_lanes(values_ref, wide_ref):
    rows, count = values_ref.shape
    for k in range(count):
        wide_ref[pl.ds(k * rows, rows), :] = jnp.broadcast_to(
            values_ref[:, k : k + 1], (rows, LANES)
        )


def backward_kernel(
    place_ref,
    bc_ref,
    decay_ref,
    rank_ref,
    dt_ref,
    bias_ref,
    act_ref,
    sp_ref,
    u_ref,
    dy_ref,
    code_ref,
    sact_ref,
    dpre_ref,
    alog_ref,
    vec_ref,
    h_ref,
    keep_ref,
    s_ref,
    d_ref,
    terms_ref,
    sums_b_ref,
    sums_c_ref,
    wide_ref,
    *,
    count,
    states,
    chunks,
):
    @pl.when(pl.program_id(0) == 0)
    def _():
        alog_ref[...] = jnp.zeros_like(alog_ref)
        vec_ref[...] = jnp.zeros_like(vec_ref)

    half = place_ref[HALF]
    eighth = states // 2
    zero = (jnp.zeros((chunks, LANES), F32),) * states
    for n in range(states):
        h_ref[pl.ds(n * chunks, chunks), :] = zero[0]
    spread_lanes(bc_ref, wide_ref)
    block = states * chunks

    def put_sums(slot, t, sums_ref):
        sums = None
        for chunk in range(chunks):
            term = terms_ref[slot, pl.ds(chunk, states, stride=chunks), :]
            sums = term if sums is None else sums + term
        sums_ref[aligned(t * states, states), :] = sums

    def recompute(pair, h):
        for slot in range(2):
            t = 2 * pair + slot
            span = pl.ds(t, chunks, stride=count)
            sp = sp_ref[span, :]
            u = u_ref[span, :]
            dy = dy_ref[span, :]
            out = []
            for n in range(states):
                decay = jnp.exp2(sp * decay_ref[pl.ds(n * chunks, chunks), :])
                keep_ref[aligned(t * block + n * chunks, chunks), :] = decay
                now = decay * h[n] + u * every_row(wide_ref, b_at(n, eighth) * count + t, chunks)
                h_ref[aligned((t + 1) * block + n * chunks, chunks), :] = now
                terms_ref[slot, pl.ds(n * chunks, chunks), :] = dy * now
                out.append(now)
            h = tuple(out)
            put_sums(slot, t, sums_c_ref)
        return h

    lax.fori_loop(0, count // 2, recompute, zero)

    def retreat(back, carry):
        flows, totals = carry
        for slot in range(2):
            t = count - 1 - (2 * back + slot)
            span = pl.ds(t, chunks, stride=count)
            sp = sp_ref[span, :]
            u = u_ref[span, :]
            dy = dy_ref[span, :]
            out_flows = []
            out_totals = []
            d_sum = None
            s_sum = None
            for n in range(states):
                dh = flows[n] + dy * every_row(wide_ref, c_at(n, eighth) * count + t, chunks)
                place = aligned(t * block + n * chunks, chunks)
                flow = keep_ref[place, :] * dh
                out_flows.append(flow)
                q = flow * h_ref[place, :]
                out_totals.append(totals[n] + q * sp)
                d_term = q * decay_ref[pl.ds(n * chunks, chunks), :]
                s_term = dh * every_row(wide_ref, b_at(n, eighth) * count + t, chunks)
                d_sum = d_term if d_sum is None else d_sum + d_term
                s_sum = s_term if s_sum is None else s_sum + s_term
                terms_ref[slot, pl.ds(n * chunks, chunks), :] = dh * u
            s_ref[span, :] = s_sum
            d_ref[span, :] = d_sum
            put_sums(slot, t, sums_b_ref)
            flows, totals = tuple(out_flows), tuple(out_totals)
        return flows, totals

    _, totals = lax.fori_loop(0, count // 2, retreat, (zero, zero))
    for n in range(states):
        alog_ref[pl.ds(n * chunks, chunks), :] += totals[n]

    rank = rank_ref[...]
    ranks = rank.shape[1]
    drank = None
    for chunk in range(chunks):
        cols = slice(chunk * LANES, (chunk + 1) * LANES)
        place = pl.ds(chunk * count, count)
        act = act_ref[:, cols].astype(F32)
        weight = dt_ref[:, lanes(2 * chunk + half)]
        pre = dot(rank, weight, 1, 0) + bias_ref[pl.ds(2 * chunk + half, 1), :]
        s_now = s_ref[place, :]
        dstep = d_ref[place, :] * (1.0 / LOG2E) + s_now * act
        sact_ref[:, cols] = s_now * softplus(pre)
        dpre = dstep * sigmoid(pre)
        vec_ref[0:1, cols] += jnp.sum(dpre, axis=0, keepdims=True)
        vec_ref[1:2, cols] += jnp.sum(dy_ref[place, :] * act, axis=0, keepdims=True)
        low = dpre.astype(BF16)
        dpre_ref[:, cols] = low
        term = dot(low, weight, 1, 1)
        drank = term if drank is None else drank + term
    source = lax.broadcasted_iota(jnp.int32, (2 * LANES, LANES), 0)
    target = lax.broadcasted_iota(jnp.int32, (2 * LANES, LANES), 1)
    code = None
    for n in range(states):
        pair = jnp.concatenate(
            [ref[pl.ds(n, count, stride=states), :] for ref in (sums_b_ref, sums_c_ref)], axis=1
        )
        column = ranks + jnp.where(source < LANES, b_at(n, eighth), c_at(n, eighth))
        pick = jnp.where(target == column, 1.0, 0.0).astype(BF16)
        term = dot(pair.astype(BF16), pick, 1, 0)
        code = term if code is None else code + term
    code_ref[...] = code + jnp.concatenate([drank, jnp.zeros((count, LANES - ranks), F32)], axis=1)


def scan_backward(place, micros, bc, decay, rank, dt, bias, act, sp, u, dy):
    rows, own = act.shape
    count = rows // micros
    chunks = own // LANES
    states = bc.shape[1] // 2
    ranks = rank.shape[1]
    outs = [
        ((rows, LANES), F32),
        ((rows, own), F32),
        ((rows, own), BF16),
        ((states * chunks, LANES), F32),
        ((2, own), F32),
    ]

    def block(*shape):
        return pl.BlockSpec(shape, lambda i, p: (i, 0))

    return pl.pallas_call(
        functools.partial(backward_kernel, count=count, states=states, chunks=chunks),
        grid_spec=pltpu.PrefetchScalarGridSpec(
            num_scalar_prefetch=1,
            grid=(micros,),
            in_specs=[
                block(count, 2 * states),
                whole(decay.shape),
                block(count, ranks),
                whole(dt.shape),
                whole(bias.shape),
                block(count, own),
                block(chunks * count, LANES),
                block(chunks * count, LANES),
                block(chunks * count, LANES),
            ],
            out_specs=[block(count, LANES), block(count, own), block(count, own)]
            + [whole(shape) for shape, _ in outs[3:]],
            scratch_shapes=[
                pltpu.VMEM(((count + 1) * states * chunks, LANES), F32),
                pltpu.VMEM((count * states * chunks, LANES), F32),
                pltpu.VMEM((chunks * count, LANES), F32),
                pltpu.VMEM((chunks * count, LANES), F32),
                pltpu.VMEM((2, states * chunks, LANES), F32),
                pltpu.VMEM((count * states, LANES), F32),
                pltpu.VMEM((count * states, LANES), F32),
                pltpu.VMEM((2 * states * count, LANES), F32),
            ],
        ),
        out_shape=[hbm(*out) for out in outs],
        compiler_params=params(48),
        cost_estimate=cost(0),
        name="scan_backward",
    )(place, *in_hbm((bc, decay, rank, dt, bias, act, sp, u, dy)))


def tail_kernel(
    place_ref,
    len_ref,
    *refs,
    micros,
    count,
    taps,
    clusters,
    ranks,
    chunks,
    states,
):
    def take(number):
        nonlocal refs
        taken, refs = refs[:number], refs[number:]
        return taken

    code_own_ref, code_other_ref = take(2)
    sact_ref, dpre_ref, alog_sum_ref, back_ref = take(4)
    dtx_ref, bc_own_ref, bc_other_ref, decay_ref = take(4)
    dy_refs = take(micros)
    conved_ref, inner_ref, act_ref, high_ref, convw_ref, skip_ref = take(6)
    normed_ref, weight_ref, share_ref, gain_ref = take(4)
    keep_far, send_far, low_ref = take(3)
    mask_ref, code_ref, wcode_ref, vec_ref, alog_ref, total_ref, win_ref, sems = refs[:8]
    keep_ref, send_ref, out_sems = refs[8:]

    step = pl.program_id(0)
    rows = micros * count
    eighth = states // 2
    edge = LANES // 2
    half, core, cube, face = (place_ref[k] for k in range(4))
    pair = step ^ face
    span = LANES + 32

    def fetch(k):
        source = weight_ref.at[0, pl.ds(2 * (k ^ face), 2), half]
        return (pltpu.make_async_copy(source, win_ref.at[k], sems.at[k]),)

    steps = win_ref.shape[0]
    stream(step, steps, fetch)

    def put(k, start, size, column):
        rows_out = aligned(k * span + start, size, 16)
        return [
            pltpu.make_async_copy(near.at[rows_out], far.at[rows_out], out_sems.at[side, column, k])
            for side, (near, far) in enumerate(((send_ref, send_far), (keep_ref, keep_far)))
        ]

    def pack_row(chunk):
        relative = chunk ^ cube
        return (relative & 3) * span + LANES + (relative >> 2) * 16

    def place_pair(start, size, cols, even, odd):
        keep_ref[aligned(start, size, 16), cols] = jnp.where(core == 0, even, odd).astype(BF16)
        send_ref[aligned(start, size, 16), cols] = jnp.where(core == 0, odd, even).astype(BF16)

    @pl.when(step == 0)
    def _():
        fill_masks(len_ref, mask_ref, micros, count, taps, clusters)
        total_ref[...] = share_ref[...]
        code_ref[...] = (code_own_ref[...] + code_other_ref[...]).astype(BF16)
        alog_ref[...] = alog_sum_ref[...] * (decay_ref[...] * (1.0 / LOG2E))

    code = code_ref[...]
    lane = lax.broadcasted_iota(jnp.int32, (1, LANES), 1)
    code_rank = jnp.where(lane < ranks, code, jnp.zeros_like(code))
    dpre = dpre_ref[...]
    for part in range(2):
        source = lanes(2 * (2 * pair + part) + half)
        cols = slice(part * LANES, (part + 1) * LANES)
        wcode_ref[:ranks, cols] = dtx_ref[:, source]
        own = bc_own_ref[:, :, source].reshape(states, LANES)
        other = bc_other_ref[:, :, source].reshape(states, LANES)
        wcode_ref[ranks : ranks + states, cols] = jnp.where(half == 0, own, other)
        wcode_ref[ranks + states : ranks + 2 * states, cols] = jnp.where(half == 0, other, own)
        wcode_ref[ranks + 2 * states :, cols] = jnp.zeros(
            (LANES - ranks - 2 * states, LANES), BF16
        )
    for part in range(2):
        cols = slice(part * LANES, (part + 1) * LANES)
        chunk = 2 * pair + part
        source = 2 * chunk + half
        weights = convw_ref[:, lanes(source)]
        sact = sact_ref[:, cols]
        dy = jnp.concatenate([ref[pl.ds(part * count, count), :] for ref in dy_refs], axis=0)
        dact = sact + dot(code, wcode_ref[:, cols], 1, 0)
        dact = dact + dy * skip_ref[pl.ds(source, 1), :]
        conved = conved_ref[:, cols]
        sig = sigmoid(conved)
        dconv = dact * (sig * (1.0 + conved * (1.0 - sig)))
        inner = inner_ref[:, cols]
        dinner = weights[taps - 1 : taps] * dconv
        sums = [None] * (taps + 1)
        sums[taps - 1] = jnp.sum(dconv * inner, axis=0, keepdims=True)
        sums[taps] = jnp.sum(dconv, axis=0, keepdims=True)
        for back in range(1, taps):
            kept = dconv * mask_ref[back]
            dinner = dinner + weights[taps - 1 - back : taps - back] * pltpu.roll(
                kept, rows - back, 0
            )
            sums[taps - 1 - back] = jnp.sum(
                kept * pltpu.roll(inner, back, 0), axis=0, keepdims=True
            )
        for k in range(taps + 1):
            vec_ref[k : k + 1, lanes(chunk)] = sums[k]
        vec_ref[taps + 1 : taps + 3, lanes(chunk)] = back_ref[:, lanes(chunk)]
        low_ref[:, cols] = dinner.astype(BF16)

        act = act_ref[:, cols]
        start = pack_row(chunk)
        rows_now = dot(act, code_rank, 0, 0) + dot(dpre[:, cols], high_ref[...], 0, 0)
        for k in range(4):
            place_pair(
                start,
                16,
                slice(k * LANES, (k + 1) * LANES),
                rows_now[k * 16 : (k + 1) * 16],
                rows_now[edge + k * 16 : edge + (k + 1) * 16],
            )
        state_rows = dot(code, act, 0, 0)[ranks : ranks + 2 * states]
        place_pair(
            start, 16, slice(4 * LANES, 5 * LANES), state_rows[:states], state_rows[states:]
        )

    normed = normed_ref[...]
    for part in range(2):
        grad = dot(low_ref[:, lanes(core ^ part)], normed, 0, 0)
        total_ref[...] += eight_rows(grad * win_ref[step, core ^ part].astype(F32))
        out_ref = (keep_ref, send_ref)[part]
        out_ref[aligned(step * span, LANES, 16), :] = grad.astype(BF16)
    for copy in put(step, 0, LANES, 0):
        copy.start()

    @pl.when(step == pl.num_programs(0) - 1)
    def _():
        vec_ref[taps + 3 : taps + 4, :] = (
            jnp.sum(total_ref[...], axis=0, keepdims=True) / gain_ref[...]
        )
        is_gain = lax.broadcasted_iota(jnp.int32, (8, LANES), 0) == taps + 3
        for chunk in range(chunks):
            start = pack_row(chunk)
            vec = vec_ref[:, chunk * LANES : (chunk + 1) * LANES]
            far, farther = (pltpu.roll(vec, LANES - k * edge // 2, 1) for k in (1, 2))
            even = jnp.where(is_gain & (lane >= edge // 2), far, vec)
            odd = jnp.where(is_gain & (lane < edge // 2), far, farther)
            alog = [
                alog_ref[pl.ds(q * eighth * chunks + chunk, eighth, stride=chunks), :]
                for q in range(2)
            ]
            place_pair(
                start,
                16,
                slice(5 * LANES, 6 * LANES),
                jnp.concatenate([alog[0], even]),
                jnp.concatenate([alog[1], odd]),
            )
            blank = jnp.zeros((16, 2 * LANES), F32)
            place_pair(start, 16, slice(6 * LANES, 8 * LANES), blank, blank)
        for k in range(steps):
            for copy in put(k, LANES, span - LANES, 1):
                copy.start()
        for k in range(steps):
            for copy in put(k, 0, LANES, 0) + put(k, LANES, span - LANES, 1):
                copy.wait()


def tail(
    place,
    lengths,
    code_own,
    code_other,
    sact,
    dpre,
    alog,
    back,
    dtx,
    bc_own,
    bc_other,
    decay,
    dy,
    conved,
    inner,
    act,
    high,
    convw,
    skip,
    normed,
    w4,
    share,
    gain,
):
    rows, own = act.shape
    chunks = own // LANES
    width = normed.shape[1]
    micros, _, clusters = lengths.shape
    count = rows // micros
    taps = convw.shape[0]
    ranks = dtx.shape[0]
    states = decay.shape[0] // chunks
    cols = 2 * LANES
    extent = 4 * (LANES + 32)

    def by_cols(height):
        return pl.BlockSpec((height, cols), lambda i, p: (0, i ^ p[FACE]))

    def dy_spec(micro):
        return pl.BlockSpec(
            (2 * count, LANES), lambda i, p: (micro * (chunks // 2) + (i ^ p[FACE]), 0)
        )

    in_specs = (
        [pl.BlockSpec(memory_space=pltpu.SMEM)]
        + [whole((rows, LANES))] * 2
        + [by_cols(rows)] * 2
        + [whole(alog.shape), whole(back.shape)]
        + [whole(array.shape) for array in (dtx, bc_own, bc_other, decay)]
        + [dy_spec(micro) for micro in range(micros)]
        + [by_cols(rows)] * 3
        + [whole(array.shape) for array in (high, convw, skip, normed)]
        + [
            ANY,
            whole(share.shape),
            whole(gain.shape),
        ]
    )
    return pl.pallas_call(
        functools.partial(
            tail_kernel,
            micros=micros,
            count=count,
            taps=taps,
            clusters=clusters,
            ranks=ranks,
            chunks=chunks,
            states=states,
        ),
        grid_spec=pltpu.PrefetchScalarGridSpec(
            num_scalar_prefetch=1,
            grid=(chunks // 2,),
            in_specs=in_specs,
            out_specs=[ANY, ANY, pl.BlockSpec((rows, cols), lambda i, p: (0, i ^ p[FACE]))],
            scratch_shapes=[
                pltpu.VMEM((taps, rows, LANES), F32),
                pltpu.VMEM((rows, LANES), BF16),
                pltpu.VMEM((LANES, cols), BF16),
                pltpu.VMEM((8, own), F32),
                pltpu.VMEM((states * chunks, LANES), F32),
                pltpu.VMEM((8, width), F32),
                pltpu.VMEM((chunks // 2, 2, LANES, width), BF16),
                pltpu.SemaphoreType.DMA((chunks // 2,)),
                pltpu.VMEM((extent, width), BF16),
                pltpu.VMEM((extent, width), BF16),
                pltpu.SemaphoreType.DMA((2, 2, chunks // 2)),
            ],
        ),
        out_shape=[
            hbm((extent, width), BF16),
            hbm((extent, width), BF16),
            hbm((rows, own), BF16),
        ],
        compiler_params=params(30),
        cost_estimate=cost(7),
        name="tail",
    )(
        place,
        lengths,
        *in_hbm([code_own]),
        code_other,
        *in_hbm(
            (
                sact,
                dpre,
                alog,
                back,
                dtx,
                bc_own,
                bc_other,
                decay,
                *([dy] * micros),
                conved,
                inner,
                act,
                high,
                convw,
                skip,
                normed,
                w4,
                share,
                gain,
            )
        ),
    )


def fetch_halves(source, which, half, target_ref, sems):
    copies = []
    for k in range(target_ref.shape[0]):
        pair = pl.ds(2 * k, 2)
        block = source.at[pair, half] if which is None else source.at[which, pair, half]
        copies.append(pltpu.make_async_copy(block, target_ref.at[k], sems.at[k]))
    for copy in copies:
        copy.start()
    return copies


def products_kernel(
    place_ref,
    gated_ref,
    dgate_ref,
    out_ref,
    weight_ref,
    mixed_ref,
    dnormed_ref,
    wout_ref,
    wgate_ref,
    out_sems,
    gate_sems,
):
    half = place_ref[HALF]
    width = mixed_ref.shape[1]
    jobs = (
        (fetch_halves(out_ref, None, half, wout_ref, out_sems), gated_ref, wout_ref, mixed_ref),
        (fetch_halves(weight_ref, 1, half, wgate_ref, gate_sems), dgate_ref, wgate_ref, dnormed_ref),
    )
    for copies, left_ref, right_ref, result_ref in jobs:
        total = None
        for k, copy in enumerate(copies):
            copy.wait()
            left = left_ref[:, 2 * k * LANES : 2 * (k + 1) * LANES]
            term = dot(left, right_ref[k].reshape(-1, width), 1, 0)
            total = term if total is None else total + term
        result_ref[...] = total.astype(BF16)


def products(place, gated, dgate, wout3, w4):
    rows, own = gated.shape
    width = w4.shape[-1]
    pairs = own // (2 * LANES)
    return pl.pallas_call(
        products_kernel,
        grid_spec=pltpu.PrefetchScalarGridSpec(
            num_scalar_prefetch=1,
            grid=(1,),
            in_specs=[whole((rows, own)), whole((rows, own)), ANY, ANY],
            out_specs=[whole((rows, width))] * 2,
            scratch_shapes=[
                pltpu.VMEM((pairs, 2, LANES, width), BF16),
                pltpu.VMEM((pairs, 2, LANES, width), BF16),
                pltpu.SemaphoreType.DMA((pairs,)),
                pltpu.SemaphoreType.DMA((pairs,)),
            ],
        ),
        out_shape=[hbm((rows, width), BF16)] * 2,
        compiler_params=params(20),
        cost_estimate=cost(4),
        name="products",
    )(place, *in_hbm((gated, dgate, wout3, w4)))


def spread_kernel(place_ref, low_ref, weight_ref, gate_ref, dnormed_ref, win_ref, sems):
    width = gate_ref.shape[1]
    total = gate_ref[...].astype(F32)
    for k, copy in enumerate(fetch_halves(weight_ref, 0, place_ref[HALF], win_ref, sems)):
        copy.wait()
        left = low_ref[:, 2 * k * LANES : 2 * (k + 1) * LANES]
        total = total + dot(left, win_ref[k].reshape(-1, width), 1, 0)
    dnormed_ref[...] = total.astype(BF16)


def spread(place, low, w4, gate_part):
    rows, own = low.shape
    width = w4.shape[-1]
    pairs = own // (2 * LANES)
    return pl.pallas_call(
        spread_kernel,
        grid_spec=pltpu.PrefetchScalarGridSpec(
            num_scalar_prefetch=1,
            grid=(1,),
            in_specs=[whole((rows, own)), ANY, whole((rows, width))],
            out_specs=whole((rows, width)),
            scratch_shapes=[
                pltpu.VMEM((pairs, 2, LANES, width), BF16),
                pltpu.SemaphoreType.DMA((pairs,)),
            ],
        ),
        out_shape=hbm((rows, width), BF16),
        compiler_params=params(16),
        cost_estimate=cost(3),
        name="spread",
    )(place, *in_hbm((low, w4, gate_part)))


def finish_kernel(x_ref, mine_ref, theirs_ref, cotan_ref, gain_ref, grad_ref):
    x = x_ref[...].astype(F32)
    scale = lax.rsqrt(jnp.mean(x * x, axis=1, keepdims=True) + EPSILON)
    unit = x * scale
    dhat = (mine_ref[...].astype(F32) + theirs_ref[...].astype(F32)) * gain_ref[...]
    grad_ref[...] = cotan_ref[...].astype(F32) + scale * (
        dhat - unit * jnp.mean(dhat * unit, axis=1, keepdims=True)
    )


def finish(x, mine, theirs, cotan, gain):
    rows, width = x.shape
    by_rows = pl.BlockSpec((rows // 4, width), lambda i: (i, 0))
    return pl.pallas_call(
        finish_kernel,
        grid=(4,),
        in_specs=[by_rows] * 4 + [whole(gain.shape)],
        out_specs=by_rows,
        out_shape=jax.ShapeDtypeStruct((rows, width), F32),
        compiler_params=params(16),
        cost_estimate=cost(0),
        name="finish",
    )(*in_hbm((x, mine)), theirs, *in_hbm((cotan, gain)))


def unpack_kernel(
    near_ref,
    far_ref,
    out_ref,
    dtx_ref,
    dt_ref,
    bc_ref,
    alog_ref,
    convw_ref,
    convb_ref,
    bias_ref,
    skip_ref,
    out_grad_ref,
    *,
    eighth,
    taps,
    edge,
):
    pack = near_ref[...].astype(F32) + far_ref[...].astype(F32)
    for k in range(4):
        rows = pack[:, k * LANES : (k + 1) * LANES]
        dtx_ref[pl.ds(16 * k, 16), :] = rows[:, :edge]
        dt_ref[pl.ds(16 * k, 16), :] = pltpu.roll(rows, edge, 1)[:, :edge]
    rows = pack[:, 4 * LANES : 5 * LANES]
    bc_ref[0] = rows[:eighth]
    bc_ref[1] = rows[eighth:]
    rows = pack[:, 5 * LANES : 6 * LANES]
    alog_ref[...] = rows[:eighth]
    vec = rows[eighth:, :edge]
    convw_ref[...] = vec[:taps]
    convb_ref[...] = vec[taps : taps + 1]
    bias_ref[...] = vec[taps + 1 : taps + 2]
    skip_ref[...] = vec[taps + 2 : taps + 3]
    out_grad_ref[...] = out_ref[...].astype(F32)


def unpack(near, far, out, eighth, taps, ranks):
    edge = LANES // 2
    shapes = [
        (edge, ranks),
        (edge, ranks),
        (2, eighth, LANES),
        (eighth, LANES),
        (taps, edge),
        (1, edge),
        (1, edge),
        (1, edge),
        out.shape,
    ]
    return pl.pallas_call(
        functools.partial(unpack_kernel, eighth=eighth, taps=taps, edge=edge),
        grid=(1,),
        in_specs=[whole(array.shape) for array in (near, far, out)],
        out_specs=[whole(shape) for shape in shapes],
        out_shape=[jax.ShapeDtypeStruct(shape, F32) for shape in shapes],
        cost_estimate=cost(0),
        name="unpack",
    )(near, far, out)


def swap_pair(array):
    count = lax.axis_size("state")
    return lax.ppermute(array, "state", [(pos, pos ^ 1) for pos in range(count)])


def swap_bit(array, bits):
    return lax.ppermute(array, "dp", [(pos, pos ^ bits) for pos in range(lax.axis_size("dp"))])


def swap_both(array, bits=0):
    states = lax.axis_size("state")
    pairs = []
    for d in range(lax.axis_size("dp")):
        for s in range(states):
            pairs.append((d * states + s, (((d & ~1) | s) ^ bits) * states + (d & 1)))
    return lax.ppermute(array, ("dp", "state"), pairs)


def add_quarters(kept, got):
    extent = kept.shape[0] // 4
    return [kept[k * extent :][:extent] + got[k * extent :][:extent] for k in range(4)]


def trade_quarters(quarters):
    return [quarters[0]] + [swap_bit(quarters[k], k * X_BIT) for k in range(1, 4)]


def sum_quarters(quarters):
    left, right = (quarters[k].astype(F32) + quarters[k + 1].astype(F32) for k in (0, 2))
    return (left + right).astype(BF16)


CORE_BIT, X_BIT, ZH_BIT = 1, 2, 8


def shards(
    tokens,
    cluster_len,
    norm_gain,
    in_weight,
    conv_weight,
    conv_bias,
    dtx_weight,
    dt_weight,
    dt_bias,
    bc_weight,
    a_log,
    skip_gain,
    out_weight,
    cotangent,
):
    micros, count, width = tokens.shape
    inner = out_weight.shape[0]
    taps = conv_weight.shape[0]
    ranks = dtx_weight.shape[1]
    chunks = inner // (2 * LANES)
    own = chunks * LANES
    rows = micros * count
    edge = LANES // 2
    span = LANES + 32
    dp_parts = lax.axis_size("dp")
    state_count = lax.axis_size("state")
    dp_pos = lax.axis_index("dp")
    state_pos = lax.axis_index("state")
    half = state_pos & 1
    fast = state_count == 2 and dp_parts == 2 * chunks == 16
    if fast:
        place = jnp.stack([half, dp_pos & 1, dp_pos >> 1, (dp_pos >> 1) & 3])
        bc_own, alog_own = bc_weight, a_log
        bc_other, alog_other = swap_pair(bc_weight), swap_pair(a_log)
    else:
        place = jnp.stack([half, 0, 0, 0])
        bc_all = lax.all_gather(bc_weight, "state", axis=1, tiled=True)
        alog_all = lax.all_gather(a_log, "state", axis=0, tiled=True)
        eighth = alog_all.shape[0] // 2
        bc_own, bc_other = (
            lax.dynamic_slice_in_dim(bc_all, which * eighth, eighth, 1)
            for which in (half, 1 - half)
        )
        alog_own, alog_other = (
            lax.dynamic_slice_in_dim(alog_all, which * eighth, eighth, 0)
            for which in (half, 1 - half)
        )
    place = place.astype(jnp.int32)
    eighth = alog_own.shape[0]
    states = 2 * eighth

    x = tokens.reshape(rows, width)
    cotan = cotangent.reshape(rows, width)
    w4 = in_weight.reshape(2, chunks, 2, LANES, width)
    wout3 = out_weight.reshape(chunks, 2, LANES, width)
    dtx, dt = dtx_weight.T, dt_weight.T
    bias = dt_bias.reshape(-1, LANES)
    skip = skip_gain.reshape(-1, LANES)

    normed, act_all, act, inner_own, conved, gate = project(
        place, cluster_len, x, norm_gain[None], w4, conv_weight, conv_bias.reshape(-1, LANES)
    )
    bc, rank, high, decay, share, sp, u, dy, gated, dgate, keep, send = scan_forward(
        place,
        cluster_len,
        act_all,
        bc_own,
        bc_other,
        alog_own,
        alog_other,
        dtx,
        dt,
        bias,
        skip,
        act,
        gate,
        wout3,
        cotan,
        normed,
        w4,
    )
    if fast:
        early = swap_bit(send, CORE_BIT)
    mixed_part, dn_gate = products(place, gated, dgate, wout3, w4)
    if fast:
        *quarters, mixed_part, dn_gate, sp = lax.optimization_barrier(
            (*add_quarters(keep, early), mixed_part, dn_gate, sp)
        )
        early_got = trade_quarters(quarters)
    mixed_other = swap_pair(mixed_part)
    code_own, sact, dpre, alog, back = scan_backward(
        place, micros, bc, decay, rank, dt, bias, act, sp, u, dy
    )
    if fast:
        *early_got, code_own = lax.optimization_barrier((*early_got, code_own))
    code_other = swap_pair(code_own)
    if fast:
        block = sum_quarters(early_got)
        out_keep, out_send, gate_sum = block[:edge], block[edge:LANES], block[LANES:]
        out_got, gate_sum, mixed_other, conved = lax.optimization_barrier(
            (swap_bit(out_send, ZH_BIT), gate_sum, mixed_other, conved)
        )
    late_keep, late_send, low = tail(
        place,
        cluster_len,
        code_own,
        code_other,
        sact,
        dpre,
        alog,
        back,
        dtx,
        bc_own,
        bc_other,
        decay,
        dy,
        conved,
        inner_own,
        act,
        high,
        conv_weight,
        skip,
        normed,
        w4,
        share,
        norm_gain[None],
    )
    if fast:
        late = swap_bit(late_send, CORE_BIT)
        out_own = swap_both(out_keep + out_got)
        late_got = trade_quarters(add_quarters(late_keep, late))
    dnormed_part = spread(place, low, w4, dn_gate)
    dnormed_other = swap_pair(dnormed_part)
    mixed = (x.astype(F32) + (mixed_part.astype(F32) + mixed_other.astype(F32))).astype(BF16)
    if fast:
        *late_got, mixed, out_own, dnormed_other = lax.optimization_barrier(
            (*late_got, mixed, out_own, dnormed_other)
        )
        block = sum_quarters(late_got)
        inner_sum = block[:LANES]
        upper = dp_pos >= dp_parts // 2
        crossing = jnp.where(upper, inner_sum, gate_sum)
        first, second = crossing[:32], crossing[32:]
        first, pack_far, pack_near = lax.optimization_barrier(
            (first, block[-16:], block[LANES:-16])
        )
        pack_far = swap_both(pack_far, ZH_BIT)
        first_got = swap_bit(first, ZH_BIT)
        pack_near = swap_both(pack_near)
        first_got, pack_far, pack_near = lax.optimization_barrier((first_got, pack_far, pack_near))
        second_got = swap_bit(second, ZH_BIT)
        tokens_grad = finish(x, dnormed_part, dnormed_other, cotan, norm_gain[None])
        gain_mine = (
            pack_near[:, 5 * LANES : 6 * LANES].astype(F32)
            + pack_far[:, 5 * LANES : 6 * LANES].astype(F32)
        ).astype(BF16)
        gain_both = gain_mine[-1].astype(F32) + swap_bit(gain_mine, CORE_BIT)[-1].astype(F32)
        extent = width // (dp_parts * state_count)
        gain_grad = lax.dynamic_slice_in_dim(gain_both, (dp_pos & 1) * extent, extent, 0)
        (
            dtx_grad,
            dt_grad,
            bc_grad,
            alog_grad,
            convw_grad,
            convb_grad,
            bias_grad,
            skip_grad,
            out_own,
        ) = unpack(pack_near, pack_far, out_own, eighth, taps, ranks)
        convb_grad, bias_grad, skip_grad = (
            array[0] for array in (convb_grad, bias_grad, skip_grad)
        )
        in_grad = jnp.where(upper, gate_sum, inner_sum).astype(F32) + jnp.concatenate(
            [first_got, second_got]
        ).astype(F32)
    else:
        tokens_grad = finish(x, dnormed_part, dnormed_other, cotan, norm_gain[None])
    mixed = mixed.reshape(micros, count, width)
    tokens_grad = tokens_grad.reshape(micros, count, width)

    if not fast:
        def total(array):
            return lax.psum(array.astype(F32), "dp")

        def both_rows(array):
            mine = array.reshape(chunks, 1, LANES, -1)
            other = swap_pair(mine)
            low = jnp.where(half == 0, mine, other)
            high = jnp.where(half == 0, other, mine)
            return jnp.concatenate([low, high], axis=1).reshape(2 * own, -1)

        every = dp_parts * state_count
        at = dp_pos * state_count + state_pos

        def cut_own(array):
            extent = array.shape[0] // every
            return lax.dynamic_slice_in_dim(array, at * extent, extent, 0)

        pair = total(jnp.stack([keep, send])).reshape(2, 2, 2, 2 * LANES, width)
        outs = pair[:, :, :, :LANES].reshape(2, 2, 2, 2, edge, width)
        outs = jnp.transpose(outs, (3, 1, 2, 0, 4, 5)).reshape(own, width)
        gates = jnp.moveaxis(pair[:, :, :, LANES:], 0, 2).reshape(own, width)
        pair = total(jnp.stack([late_keep, late_send])).reshape(2, 2, 2, span, width)
        inners = jnp.moveaxis(pair[:, :, :, :LANES], 0, 2).reshape(own, width)
        packs = pair[:, :, :, LANES:].reshape(2, 2, 2, 2, 16, width // LANES, LANES)
        packs = jnp.transpose(packs, (3, 1, 2, 0, 5, 4, 6)).reshape(chunks, 2, -1, 16, LANES)
        small = both_rows(packs[:, :, :4].reshape(own, LANES))
        in_grad = cut_own(jnp.concatenate([both_rows(inners), both_rows(gates)]))
        out_own = cut_own(both_rows(outs))
        mine = cut_own(small)
        dtx_grad, dt_grad = mine[:, :ranks], mine[:, ranks:]
        vec_rows = jnp.swapaxes(packs[:, :, 5, eighth:, :edge], 2, 3).reshape(own, -1)
        gain_sum = vec_rows[:, -1].reshape(chunks, 2, 2, -1).swapaxes(1, 2).reshape(-1)
        gain_grad = cut_own(gain_sum + swap_pair(gain_sum))
        vec = cut_own(both_rows(vec_rows)).T
        state_rows = jnp.concatenate([packs[:, :, 4], packs[:, :, 5, :eighth]], axis=2)
        state_rows = state_rows.reshape(chunks, 2, 3, eighth, LANES)
        state_rows = jnp.transpose(state_rows, (0, 4, 2, 1, 3)).reshape(own, -1)
        extent = inner // dp_parts
        state_part = lax.dynamic_slice_in_dim(both_rows(state_rows), dp_pos * extent, extent, 0)
        state_part = state_part.T.reshape(3, state_count, -1, extent)
        state_part = lax.dynamic_index_in_dim(state_part, state_pos, 1, keepdims=False)
        bc_grad, alog_grad = state_part[:2], state_part[2]
        convw_grad, convb_grad, bias_grad, skip_grad = (
            vec[:taps], vec[taps], vec[taps + 1], vec[taps + 2]
        )

    return (
        mixed,
        tokens_grad,
        gain_grad,
        in_grad,
        convw_grad,
        convb_grad,
        dtx_grad,
        dt_grad,
        bias_grad,
        bc_grad,
        alog_grad,
        skip_grad,
        out_own,
    )


def solution(mesh):
    return jax.shard_map(
        shards,
        mesh=mesh,
        in_specs=(
            P(None, "dp", None),
            P(None, "dp", None),
            P(),
            P(),
            P(),
            P(),
            P(),
            P(),
            P(),
            P(None, "state", None),
            P("state", None),
            P(),
            P(),
            P(None, "dp", None),
        ),
        out_specs=(
            P(None, "dp", None),
            P(None, "dp", None),
            P(("dp", "state")),
            P(("dp", "state"), None),
            P(None, ("dp", "state")),
            P(("dp", "state")),
            P(("dp", "state"), None),
            P(("dp", "state"), None),
            P(("dp", "state")),
            P(None, "state", "dp"),
            P("state", "dp"),
            P(("dp", "state")),
            P(("dp", "state"), None),
        ),
        check_vma=False,
    )
```

```python
import functools
import math

import jax
import jax.numpy as jnp
from jax import lax
from jax.experimental import pallas as pl
from jax.experimental.pallas import tpu as pltpu
from jax.sharding import PartitionSpec as P

EPSILON = 1e-05
LANES = 128
RESET = 1e4
LOG2E = math.log2(math.e)
F32 = jnp.float32
BF16 = jnp.bfloat16
MIB = 1024 * 1024


def dot(left, right, left_dim, right_dim):
    return lax.dot_general(
        left, right, (((left_dim,), (right_dim,)), ((), ())), preferred_element_type=F32
    )


def params(mib):
    return pltpu.CompilerParams(
        vmem_limit_bytes=mib * MIB, dimension_semantics=("arbitrary",)
    )


ANY = pl.BlockSpec(memory_space=pl.ANY)


def stream(step, steps, fetch):
    @pl.when(step == 0)
    def _():
        for k in range(steps):
            for copy in fetch(k):
                copy.start()

    for copy in fetch(step):
        copy.wait()


def whole(shape):
    return pl.BlockSpec(shape, lambda *_: (0,) * len(shape))


sigmoid = jax.nn.sigmoid


def softplus(value):
    return jnp.maximum(value, 0.0) + jnp.log1p(jnp.exp(-jnp.abs(value)))


def lanes(index):
    return pl.ds(pl.multiple_of(index * LANES, LANES), LANES)


def cost(micros):
    return pl.CostEstimate(
        flops=int(micros * 1e9), bytes_accessed=int(micros * 1e6), transcendentals=0
    )


def hbm(shape, dtype):
    return pltpu.HBM(shape, dtype)


def in_hbm(arrays):
    return [pltpu.with_memory_space_constraint(array, pltpu.HBM) for array in arrays]


def aligned(start, size, to=8):
    return pl.ds(pl.multiple_of(start, to), size)


HALF, CORE, CUBE, FACE = range(4)


def fill_masks(len_ref, mask_ref, micros, count, taps, clusters):
    place = lax.broadcasted_iota(jnp.int32, (count, LANES), 0)
    for micro in range(micros):
        rows = pl.ds(micro * count, count)
        for back in range(1, taps):
            apart = place < back
            start = 0
            for cluster in range(clusters - 1):
                start = start + len_ref[micro, 0, cluster]
                apart = apart | ((place >= start) & (place < start + back))
            mask_ref[back, rows, :] = jnp.where(apart, 0.0, 1.0)
            if back == 1:
                mask_ref[0, rows, :] = jnp.where(apart, 1.0, 0.0)


def project_kernel(
    place_ref,
    len_ref,
    gain_ref,
    convw_ref,
    convb_ref,
    x_far,
    weight_far,
    normed_far,
    act_far,
    own_act_far,
    inner_far,
    conved_far,
    gate_far,
    mask_ref,
    x_ref,
    win_ref,
    wgate_ref,
    normed_ref,
    act_ref,
    own_act_ref,
    inner_ref,
    conved_ref,
    gate_ref,
    in_sems,
    out_sems,
    *,
    micros,
    count,
    taps,
    clusters,
):
    half = place_ref[HALF]
    chunks = win_ref.shape[0]
    inward = [pltpu.make_async_copy(x_far, x_ref, in_sems.at[2 * chunks])]
    for k in range(chunks):
        inward.append(pltpu.make_async_copy(weight_far.at[0, k], win_ref.at[k], in_sems.at[2 * k]))
        inward.append(
            pltpu.make_async_copy(
                weight_far.at[1, k, half], wgate_ref.at[k], in_sems.at[2 * k + 1]
            )
        )
    for copy in inward:
        copy.start()
    outward = []

    def put(source, target):
        outward.append(pltpu.make_async_copy(source, target, out_sems.at[len(outward)]))
        outward[-1].start()

    fill_masks(len_ref, mask_ref, micros, count, taps, clusters)
    inward[0].wait()
    rows = x_ref[...].astype(F32)
    scale = lax.rsqrt(jnp.mean(rows * rows, axis=1, keepdims=True) + EPSILON)
    normed = (rows * scale * gain_ref[...]).astype(BF16)
    normed_ref[...] = normed
    put(normed_ref, normed_far)
    for k in range(chunks):
        inward[2 * k + 1].wait()
        inward[2 * k + 2].wait()
        proj = dot(normed, win_ref[k].reshape(2 * LANES, -1), 1, 1)
        own = slice(k * LANES, (k + 1) * LANES)
        gate_ref[:, own] = dot(normed, wgate_ref[k], 1, 1)
        inners, conveds, acts = [], [], []
        for part in range(2):
            cols = slice((2 * k + part) * LANES, (2 * k + part + 1) * LANES)
            inner = proj[:, part * LANES : (part + 1) * LANES]
            conved = convb_ref[2 * k + part : 2 * k + part + 1, :]
            conved = conved + convw_ref[taps - 1 : taps, cols] * inner
            for back in range(1, taps):
                shifted = pltpu.roll(inner, back, 0) * mask_ref[back]
                conved = conved + convw_ref[taps - 1 - back : taps - back, cols] * shifted
            act = conved * sigmoid(conved)
            act_ref[:, cols] = act.astype(BF16)
            inners.append(inner)
            conveds.append(conved)
            acts.append(act)
        inner_ref[:, own] = jnp.where(half == 0, *inners)
        conved_ref[:, own] = jnp.where(half == 0, *conveds)
        own_act_ref[:, own] = jnp.where(half == 0, *acts).astype(BF16)
        if k % 2:
            group = pl.ds((k - 1) * LANES, 2 * LANES)
            wide = pl.ds(2 * (k - 1) * LANES, 4 * LANES)
            put(act_ref.at[:, wide], act_far.at[:, wide])
            for near, far in (
                (gate_ref, gate_far),
                (inner_ref, inner_far),
                (conved_ref, conved_far),
                (own_act_ref, own_act_far),
            ):
                put(near.at[:, group], far.at[:, group])
    for copy in outward:
        copy.wait()


def project(place, lengths, x, gain, w4, conv_weight, conv_bias):
    rows, width = x.shape
    chunks = w4.shape[1]
    micros, _, clusters = lengths.shape
    taps = conv_weight.shape[0]
    own = chunks * LANES
    outs = [
        ((rows, width), BF16),
        ((rows, 2 * own), BF16),
        ((rows, own), BF16),
        ((rows, own), F32),
        ((rows, own), F32),
        ((rows, own), F32),
    ]
    return pl.pallas_call(
        functools.partial(
            project_kernel, micros=micros, count=rows // micros, taps=taps, clusters=clusters
        ),
        grid_spec=pltpu.PrefetchScalarGridSpec(
            num_scalar_prefetch=1,
            grid=(1,),
            in_specs=[
                pl.BlockSpec(memory_space=pltpu.SMEM),
                whole(gain.shape),
                whole(conv_weight.shape),
                whole(conv_bias.shape),
                ANY,
                ANY,
            ],
            out_specs=[ANY] * len(outs),
            scratch_shapes=[
                pltpu.VMEM((taps, rows, LANES), F32),
                pltpu.VMEM((rows, width), BF16),
                pltpu.VMEM((chunks, 2, LANES, width), BF16),
                pltpu.VMEM((chunks, LANES, width), BF16),
            ]
            + [pltpu.VMEM(*out) for out in outs]
            + [
                pltpu.SemaphoreType.DMA((2 * chunks + 1,)),
                pltpu.SemaphoreType.DMA((1 + 5 * chunks // 2,)),
            ],
        ),
        out_shape=[hbm(*out) for out in outs],
        compiler_params=params(30),
        cost_estimate=cost(6),
        name="project",
    )(place, *in_hbm((lengths, gain, conv_weight, conv_bias, x, w4)))


def every_row(ref, row, height):
    return ref[pl.ds(row, height, stride=0), :]


def b_at(n, eighth):
    return (n // eighth) * 2 * eighth + n % eighth


def c_at(n, eighth):
    return b_at(n, eighth) + eighth


def forward_kernel(
    place_ref,
    len_ref,
    act_all_ref,
    bc_own_ref,
    bc_other_ref,
    alog_own_ref,
    alog_other_ref,
    dtx_ref,
    dt_ref,
    bias_ref,
    skip_ref,
    act_ref,
    *refs,
    micros,
    count,
    states,
    chunks,
    clusters,
):
    gate_far, wout_far, cotan_far, normed_far = refs[:4]
    bc_ref, rank_ref, rank_high_ref, decay_ref = refs[4:8]
    sp_far, u_far, dy_far, gated_far, dgate_far, keep_far, send_far = refs[8:15]
    mask_ref, y_ref, tmp_ref, wide_ref = refs[15:19]
    gate_ref, wout_ref, cotan_ref, normed_ref = refs[19:23]
    sp_ref, u_ref, dy_ref, gated_ref, dgate_ref, keep_ref, send_ref = refs[23:30]
    in_sems, out_sems = refs[30:]
    rows = micros * count
    eighth = states // 2
    half, core, cube, face = (place_ref[k] for k in range(4))
    first = half == 0
    inward = [
        pltpu.make_async_copy(source, target, in_sems.at[k])
        for k, (source, target) in enumerate(
            (
                (gate_far, gate_ref),
                (wout_far.at[:, half], wout_ref),
                (cotan_far, cotan_ref),
                (normed_far, normed_ref),
            )
        )
    ]
    for copy in inward:
        copy.start()
    outward = []

    def put(source, target):
        outward.append(pltpu.make_async_copy(source, target, out_sems.at[len(outward)]))
        outward[-1].start()

    act_all = act_all_ref[...]
    own = dot(act_all, bc_own_ref[...].reshape(states, -1), 1, 1)
    other = dot(act_all, bc_other_ref[...].reshape(states, -1), 1, 1)
    bc_ref[:, :states] = jnp.where(first, own, other)
    bc_ref[:, states:] = jnp.where(first, other, own)
    spread_lanes(bc_ref, wide_ref)

    fill_masks(len_ref, mask_ref, micros, count, 2, clusters)
    for chunk in range(chunks):
        cols = lanes(2 * chunk + half)
        own, other = alog_own_ref[:, cols], alog_other_ref[:, cols]
        tmp_ref[pl.ds(chunk * states, eighth), :] = jnp.where(first, own, other)
        tmp_ref[pl.ds(chunk * states + eighth, eighth), :] = jnp.where(first, other, own)
    for n in range(states):
        decay_ref[pl.ds(n * chunks, chunks), :] = -LOG2E * jnp.exp(
            tmp_ref[pl.ds(n, chunks, stride=states), :]
        )

    rank = dot(act_all, dtx_ref[...], 1, 1).astype(BF16)
    rank_ref[...] = rank
    rank_high_ref[...] = jnp.concatenate([jnp.zeros_like(rank), rank], axis=1)
    for chunk in range(chunks):
        cols = slice(chunk * LANES, (chunk + 1) * LANES)
        bias = bias_ref[pl.ds(2 * chunk + half, 1), :]
        step = softplus(dot(rank, dt_ref[:, lanes(2 * chunk + half)], 1, 0) + bias)
        held = step + RESET * mask_ref[0]
        source = step * act_ref[:, cols].astype(F32)
        for micro in range(micros):
            span = slice(micro * count, (micro + 1) * count)
            place = pl.ds((micro * chunks + chunk) * count, count)
            sp_ref[place, :] = held[span]
            u_ref[place, :] = source[span]
    put(sp_ref, sp_far)
    put(u_ref, u_far)

    for micro in range(micros):

        def advance(t, h, micro=micro):
            row = micro * count + t
            span = pl.ds(micro * chunks * count + t, chunks, stride=count)
            sp = sp_ref[span, :]
            u = u_ref[span, :]
            out = []
            y = None
            for n in range(states):
                decay = jnp.exp2(sp * decay_ref[pl.ds(n * chunks, chunks), :])
                now = decay * h[n] + u * every_row(wide_ref, b_at(n, eighth) * rows + row, chunks)
                out.append(now)
                term = now * every_row(wide_ref, c_at(n, eighth) * rows + row, chunks)
                y = term if y is None else y + term
            y_ref[span, :] = y
            return tuple(out)

        lax.fori_loop(0, count, advance, (jnp.zeros((chunks, LANES), F32),) * states, unroll=4)

    for copy in inward:
        copy.wait()
    cotan = cotan_ref[...]
    for chunk in range(chunks):
        cols = slice(chunk * LANES, (chunk + 1) * LANES)
        places = [pl.ds((micro * chunks + chunk) * count, count) for micro in range(micros)]
        y = jnp.concatenate([y_ref[place, :] for place in places])
        y = y + skip_ref[pl.ds(2 * chunk + half, 1), :] * act_ref[:, cols].astype(F32)
        gate = gate_ref[:, cols]
        sig = sigmoid(gate)
        gated_ref[:, cols] = (y * (gate * sig)).astype(BF16)
        dgated = dot(cotan, wout_ref[chunk], 1, 1)
        dy = dgated * (gate * sig)
        for micro in range(micros):
            dy_ref[places[micro], :] = dy[micro * count : (micro + 1) * count]
        dgate_ref[:, cols] = (dgated * y * (sig * (1.0 + gate * (1.0 - sig)))).astype(BF16)
    put(dy_ref, dy_far)
    put(gated_ref, gated_far)
    put(dgate_ref, dgate_far)
    normed = normed_ref[...]
    edge = LANES // 2
    for r in range(chunks // 2):
        for zh in range(2):
            grad = dot(gated_ref[:, lanes((r + 4 * zh) ^ cube)], cotan, 0, 0).astype(BF16)
            top, bottom = grad[:edge], grad[edge:]
            place = pl.ds(r * 2 * LANES + zh * edge, edge)
            keep_ref[place, :] = jnp.where(core == 0, top, bottom)
            send_ref[place, :] = jnp.where(core == 0, bottom, top)
        place = pl.ds((2 * r + 1) * LANES, LANES)
        pair = 2 * (r ^ face)
        for chunk, out_ref in ((pair + core, keep_ref), (pair + 1 - core, send_ref)):
            out_ref[place, :] = dot(dgate_ref[:, lanes(chunk)], normed, 0, 0).astype(BF16)
        place = pl.ds(r * 2 * LANES, 2 * LANES)
        put(send_ref.at[place], send_far.at[place])
        put(keep_ref.at[place], keep_far.at[place])
    for copy in outward:
        copy.wait()


def scan_forward(
    place,
    lengths,
    act_all,
    bc_own,
    bc_other,
    alog_own,
    alog_other,
    dtx,
    dt,
    bias,
    skip,
    act,
    gate,
    wout3,
    cotan,
    normed,
):
    rows, own = act.shape
    chunks = own // LANES
    states = 2 * alog_own.shape[0]
    width = cotan.shape[1]
    micros, _, clusters = lengths.shape
    ranks = dtx.shape[0]
    small = [
        ((rows, 2 * states), F32),
        ((rows, ranks), BF16),
        ((rows, 2 * ranks), BF16),
        ((states * chunks, LANES), F32),
    ]
    large = [
        ((chunks * rows, LANES), F32),
        ((chunks * rows, LANES), F32),
        ((chunks * rows, LANES), F32),
        ((rows, own), BF16),
        ((rows, own), BF16),
        ((own, width), BF16),
        ((own, width), BF16),
    ]
    operands = (act_all, bc_own, bc_other, alog_own, alog_other, dtx, dt, bias, skip, act)
    streamed = (gate, wout3, cotan, normed)
    return pl.pallas_call(
        functools.partial(
            forward_kernel,
            micros=micros,
            count=rows // micros,
            states=states,
            chunks=chunks,
            clusters=clusters,
        ),
        grid_spec=pltpu.PrefetchScalarGridSpec(
            num_scalar_prefetch=1,
            grid=(1,),
            in_specs=[pl.BlockSpec(memory_space=pltpu.SMEM)]
            + [whole(operand.shape) for operand in operands]
            + [ANY] * len(streamed),
            out_specs=[whole(shape) for shape, _ in small] + [ANY] * len(large),
            scratch_shapes=[
                pltpu.VMEM((2, rows, LANES), F32),
                pltpu.VMEM((chunks * rows, LANES), F32),
                pltpu.VMEM((states * chunks, LANES), F32),
                pltpu.VMEM((2 * states * rows, LANES), F32),
                pltpu.VMEM((rows, own), F32),
                pltpu.VMEM((chunks, LANES, width), BF16),
                pltpu.VMEM((rows, width), BF16),
                pltpu.VMEM((rows, width), BF16),
            ]
            + [pltpu.VMEM(*out) for out in large]
            + [pltpu.SemaphoreType.DMA((4,)), pltpu.SemaphoreType.DMA((5 + chunks,))],
        ),
        out_shape=[hbm(*out) for out in small + large],
        compiler_params=params(52),
        cost_estimate=cost(19),
        name="scan_forward",
    )(
        place,
        lengths,
        *in_hbm(operands[:1]),
        *operands[1:5],
        *in_hbm((*operands[5:], *streamed)),
    )


def spread_lanes(values_ref, wide_ref):
    rows, count = values_ref.shape
    for k in range(count):
        wide_ref[pl.ds(k * rows, rows), :] = jnp.broadcast_to(
            values_ref[:, k : k + 1], (rows, LANES)
        )


def backward_kernel(
    place_ref,
    bc_ref,
    decay_ref,
    rank_ref,
    dt_ref,
    bias_ref,
    act_ref,
    sp_ref,
    u_ref,
    dy_ref,
    code_ref,
    sact_ref,
    dpre_ref,
    alog_ref,
    vec_ref,
    h_ref,
    keep_ref,
    s_ref,
    d_ref,
    terms_ref,
    sums_b_ref,
    sums_c_ref,
    wide_ref,
    *,
    count,
    states,
    chunks,
):
    @pl.when(pl.program_id(0) == 0)
    def _():
        alog_ref[...] = jnp.zeros_like(alog_ref)
        vec_ref[...] = jnp.zeros_like(vec_ref)

    half = place_ref[HALF]
    eighth = states // 2
    zero = (jnp.zeros((chunks, LANES), F32),) * states
    for n in range(states):
        h_ref[pl.ds(n * chunks, chunks), :] = zero[0]
    spread_lanes(bc_ref, wide_ref)
    block = states * chunks

    def put_terms(which, t, terms):
        for n in range(0, states, 2):
            pair = jnp.concatenate(terms[n : n + 2]).astype(BF16)
            place = aligned(t * block + n * chunks, 2 * chunks, 16)
            terms_ref[place, which * LANES : (which + 1) * LANES] = pair

    def recompute(pair, h):
        for slot in range(4):
            t = 4 * pair + slot
            span = pl.ds(t, chunks, stride=count)
            sp = sp_ref[span, :]
            u = u_ref[span, :]
            dy = dy_ref[span, :]
            out = []
            terms = []
            for n in range(states):
                decay = jnp.exp2(sp * decay_ref[pl.ds(n * chunks, chunks), :])
                keep_ref[aligned(t * block + n * chunks, chunks), :] = decay
                now = decay * h[n] + u * every_row(wide_ref, b_at(n, eighth) * count + t, chunks)
                h_ref[aligned((t + 1) * block + n * chunks, chunks), :] = now
                terms.append(dy * now)
                out.append(now)
            h = tuple(out)
            put_terms(1, t, terms)
        return h

    lax.fori_loop(0, count // 4, recompute, zero)

    def retreat(back, carry):
        flows, totals = carry
        for slot in range(4):
            t = count - 1 - (4 * back + slot)
            span = pl.ds(t, chunks, stride=count)
            sp = sp_ref[span, :]
            u = u_ref[span, :]
            dy = dy_ref[span, :]
            out_flows = []
            out_totals = []
            terms = []
            d_sum = None
            s_sum = None
            for n in range(states):
                dh = flows[n] + dy * every_row(wide_ref, c_at(n, eighth) * count + t, chunks)
                place = aligned(t * block + n * chunks, chunks)
                flow = keep_ref[place, :] * dh
                out_flows.append(flow)
                q = flow * h_ref[place, :]
                out_totals.append(totals[n] + q * sp)
                d_term = q * decay_ref[pl.ds(n * chunks, chunks), :]
                s_term = dh * every_row(wide_ref, b_at(n, eighth) * count + t, chunks)
                d_sum = d_term if d_sum is None else d_sum + d_term
                s_sum = s_term if s_sum is None else s_sum + s_term
                terms.append(dh * u)
            s_ref[span, :] = s_sum
            d_ref[span, :] = d_sum
            put_terms(0, t, terms)
            flows, totals = tuple(out_flows), tuple(out_totals)
        return flows, totals

    _, totals = lax.fori_loop(0, count // 4, retreat, (zero, zero))
    for n in range(states):
        alog_ref[pl.ds(n * chunks, chunks), :] += totals[n]

    shape = (2 * states, 2 * block)
    group = lax.broadcasted_iota(jnp.int32, shape, 1) // chunks
    gather = jnp.where(group == lax.broadcasted_iota(jnp.int32, shape, 0), 1.0, 0.0).astype(BF16)

    @pl.loop(0, count // 16)
    def _(step):
        for k in range(8):
            at = 8 * step + k
            terms = terms_ref[aligned(at * 2 * block, 2 * block, 16), :]
            sums = dot(gather, terms, 1, 0)
            sums_b_ref[aligned(at * 2 * states, 2 * states), :] = sums[:, :LANES]
            sums_c_ref[aligned(at * 2 * states, 2 * states), :] = sums[:, LANES:]

    rank = rank_ref[...]
    ranks = rank.shape[1]
    drank = None
    for chunk in range(chunks):
        cols = slice(chunk * LANES, (chunk + 1) * LANES)
        place = pl.ds(chunk * count, count)
        act = act_ref[:, cols].astype(F32)
        weight = dt_ref[:, lanes(2 * chunk + half)]
        pre = dot(rank, weight, 1, 0) + bias_ref[pl.ds(2 * chunk + half, 1), :]
        s_now = s_ref[place, :]
        dstep = d_ref[place, :] * (1.0 / LOG2E) + s_now * act
        sact_ref[:, cols] = s_now * softplus(pre)
        dpre = dstep * sigmoid(pre)
        vec_ref[0:1, cols] += jnp.sum(dpre, axis=0, keepdims=True)
        vec_ref[1:2, cols] += jnp.sum(dy_ref[place, :] * act, axis=0, keepdims=True)
        low = dpre.astype(BF16)
        dpre_ref[:, cols] = low
        term = dot(low, weight, 1, 1)
        drank = term if drank is None else drank + term
    source = lax.broadcasted_iota(jnp.int32, (2 * LANES, LANES), 0)
    target = lax.broadcasted_iota(jnp.int32, (2 * LANES, LANES), 1)
    code = None
    for n in range(states):
        pair = jnp.concatenate(
            [ref[pl.ds(n, count, stride=states), :] for ref in (sums_b_ref, sums_c_ref)], axis=1
        )
        column = ranks + jnp.where(source < LANES, b_at(n, eighth), c_at(n, eighth))
        pick = jnp.where(target == column, 1.0, 0.0).astype(BF16)
        term = dot(pair.astype(BF16), pick, 1, 0)
        code = term if code is None else code + term
    code_ref[...] = code + jnp.concatenate([drank, jnp.zeros((count, LANES - ranks), F32)], axis=1)


def scan_backward(place, micros, bc, decay, rank, dt, bias, act, sp, u, dy):
    rows, own = act.shape
    count = rows // micros
    chunks = own // LANES
    states = bc.shape[1] // 2
    ranks = rank.shape[1]
    outs = [
        ((rows, LANES), F32),
        ((rows, own), F32),
        ((rows, own), BF16),
        ((states * chunks, LANES), F32),
        ((2, own), F32),
    ]

    def block(*shape):
        return pl.BlockSpec(shape, lambda i, p: (i, 0))

    return pl.pallas_call(
        functools.partial(backward_kernel, count=count, states=states, chunks=chunks),
        grid_spec=pltpu.PrefetchScalarGridSpec(
            num_scalar_prefetch=1,
            grid=(micros,),
            in_specs=[
                block(count, 2 * states),
                whole(decay.shape),
                block(count, ranks),
                whole(dt.shape),
                whole(bias.shape),
                block(count, own),
                block(chunks * count, LANES),
                block(chunks * count, LANES),
                block(chunks * count, LANES),
            ],
            out_specs=[block(count, LANES), block(count, own), block(count, own)]
            + [whole(shape) for shape, _ in outs[3:]],
            scratch_shapes=[
                pltpu.VMEM(((count + 1) * states * chunks, LANES), F32),
                pltpu.VMEM((count * states * chunks, LANES), F32),
                pltpu.VMEM((chunks * count, LANES), F32),
                pltpu.VMEM((chunks * count, LANES), F32),
                pltpu.VMEM((count * states * chunks, 2 * LANES), BF16),
                pltpu.VMEM((count * states, LANES), F32),
                pltpu.VMEM((count * states, LANES), F32),
                pltpu.VMEM((2 * states * count, LANES), F32),
            ],
        ),
        out_shape=[hbm(*out) for out in outs],
        compiler_params=params(48),
        cost_estimate=cost(0),
        name="scan_backward",
    )(place, *in_hbm((bc, decay, rank, dt, bias, act, sp, u, dy)))


def tail_kernel(
    place_ref,
    len_ref,
    *refs,
    micros,
    count,
    taps,
    clusters,
    ranks,
    chunks,
    states,
):
    def take(number):
        nonlocal refs
        taken, refs = refs[:number], refs[number:]
        return taken

    code_own_ref, code_other_ref = take(2)
    sact_ref, dpre_ref, alog_sum_ref, back_ref = take(4)
    dtx_ref, bc_own_ref, bc_other_ref, decay_ref = take(4)
    dy_refs = take(micros)
    conved_ref, inner_ref, act_ref, high_ref, convw_ref, skip_ref = take(6)
    normed_ref, weight_ref, gate_part_ref, x_ref = take(4)
    keep_ref, send_ref, dnormed_ref = take(3)
    mask_ref, code_ref, wcode_ref, vec_ref, alog_ref, total_ref, win_ref, sems, low_ref = refs

    step = pl.program_id(0)
    rows = micros * count
    eighth = states // 2
    edge = LANES // 2
    half, core, cube, face = (place_ref[k] for k in range(4))
    pair = step ^ face
    span = LANES + 32

    def fetch(k):
        source = weight_ref.at[0, pl.ds(2 * (k ^ face), 2), half]
        return (pltpu.make_async_copy(source, win_ref.at[k], sems.at[k]),)

    stream(step, win_ref.shape[0], fetch)

    def pack_row(chunk):
        relative = chunk ^ cube
        return (relative & 3) * span + LANES + (relative >> 2) * 16

    def place_pair(start, size, cols, even, odd):
        keep_ref[aligned(start, size, 16), cols] = jnp.where(core == 0, even, odd).astype(BF16)
        send_ref[aligned(start, size, 16), cols] = jnp.where(core == 0, odd, even).astype(BF16)

    @pl.when(step == 0)
    def _():
        fill_masks(len_ref, mask_ref, micros, count, taps, clusters)
        total_ref[...] = gate_part_ref[...].astype(F32)
        code_ref[...] = (code_own_ref[...] + code_other_ref[...]).astype(BF16)
        alog_ref[...] = alog_sum_ref[...] * (decay_ref[...] * (1.0 / LOG2E))

    code = code_ref[...]
    lane = lax.broadcasted_iota(jnp.int32, (1, LANES), 1)
    code_rank = jnp.where(lane < ranks, code, jnp.zeros_like(code))
    dpre = dpre_ref[...]
    for part in range(2):
        source = lanes(2 * (2 * pair + part) + half)
        cols = slice(part * LANES, (part + 1) * LANES)
        wcode_ref[:ranks, cols] = dtx_ref[:, source]
        own = bc_own_ref[:, :, source].reshape(states, LANES)
        other = bc_other_ref[:, :, source].reshape(states, LANES)
        wcode_ref[ranks : ranks + states, cols] = jnp.where(half == 0, own, other)
        wcode_ref[ranks + states : ranks + 2 * states, cols] = jnp.where(half == 0, other, own)
        wcode_ref[ranks + 2 * states :, cols] = jnp.zeros(
            (LANES - ranks - 2 * states, LANES), BF16
        )
    for part in range(2):
        cols = slice(part * LANES, (part + 1) * LANES)
        chunk = 2 * pair + part
        source = 2 * chunk + half
        weights = convw_ref[:, lanes(source)]
        sact = sact_ref[:, cols]
        dy = jnp.concatenate([ref[pl.ds(part * count, count), :] for ref in dy_refs], axis=0)
        dact = sact + dot(code, wcode_ref[:, cols], 1, 0)
        dact = dact + dy * skip_ref[pl.ds(source, 1), :]
        conved = conved_ref[:, cols]
        sig = sigmoid(conved)
        dconv = dact * (sig * (1.0 + conved * (1.0 - sig)))
        inner = inner_ref[:, cols]
        dinner = weights[taps - 1 : taps] * dconv
        sums = [None] * (taps + 1)
        sums[taps - 1] = jnp.sum(dconv * inner, axis=0, keepdims=True)
        sums[taps] = jnp.sum(dconv, axis=0, keepdims=True)
        for back in range(1, taps):
            kept = dconv * mask_ref[back]
            dinner = dinner + weights[taps - 1 - back : taps - back] * pltpu.roll(
                kept, rows - back, 0
            )
            sums[taps - 1 - back] = jnp.sum(
                kept * pltpu.roll(inner, back, 0), axis=0, keepdims=True
            )
        for k in range(taps + 1):
            vec_ref[k : k + 1, lanes(chunk)] = sums[k]
        vec_ref[taps + 1 : taps + 3, lanes(chunk)] = back_ref[:, lanes(chunk)]
        low_ref[:, cols] = dinner.astype(BF16)

        act = act_ref[:, cols]
        start = pack_row(chunk)
        rows_now = dot(act, code_rank, 0, 0) + dot(dpre[:, cols], high_ref[...], 0, 0)
        for k in range(4):
            place_pair(
                start,
                16,
                slice(k * LANES, (k + 1) * LANES),
                rows_now[k * 16 : (k + 1) * 16],
                rows_now[edge + k * 16 : edge + (k + 1) * 16],
            )
        state_rows = dot(code, act, 0, 0)[ranks : ranks + 2 * states]
        place_pair(
            start, 16, slice(4 * LANES, 5 * LANES), state_rows[:states], state_rows[states:]
        )

    normed = normed_ref[...]
    for part in range(2):
        grad = dot(low_ref[:, lanes(core ^ part)], normed, 0, 0)
        out_ref = (keep_ref, send_ref)[part]
        out_ref[aligned(step * span, LANES, 16), :] = grad.astype(BF16)
    width = total_ref.shape[1]
    total_ref[...] += dot(low_ref[...], win_ref[step].reshape(2 * LANES, width), 1, 0)

    @pl.when(step == pl.num_programs(0) - 1)
    def _():
        total = total_ref[...]
        dnormed_ref[...] = total.astype(BF16)
        x = x_ref[...].astype(F32)
        unit = x * lax.rsqrt(jnp.mean(x * x, axis=1, keepdims=True) + EPSILON)
        vec_ref[taps + 3 : taps + 4, :] = jnp.sum(total * unit, axis=0, keepdims=True)
        is_gain = lax.broadcasted_iota(jnp.int32, (8, LANES), 0) == taps + 3
        for chunk in range(chunks):
            start = pack_row(chunk)
            vec = vec_ref[:, chunk * LANES : (chunk + 1) * LANES]
            far, farther = (pltpu.roll(vec, LANES - k * edge // 2, 1) for k in (1, 2))
            even = jnp.where(is_gain & (lane >= edge // 2), far, vec)
            odd = jnp.where(is_gain & (lane < edge // 2), far, farther)
            alog = [
                alog_ref[pl.ds(q * eighth * chunks + chunk, eighth, stride=chunks), :]
                for q in range(2)
            ]
            place_pair(
                start,
                16,
                slice(5 * LANES, 6 * LANES),
                jnp.concatenate([alog[0], even]),
                jnp.concatenate([alog[1], odd]),
            )
            blank = jnp.zeros((16, 2 * LANES), F32)
            place_pair(start, 16, slice(6 * LANES, 8 * LANES), blank, blank)


def tail(
    place,
    lengths,
    code_own,
    code_other,
    sact,
    dpre,
    alog,
    back,
    dtx,
    bc_own,
    bc_other,
    decay,
    dy,
    conved,
    inner,
    act,
    high,
    convw,
    skip,
    normed,
    w4,
    gate_part,
    x,
):
    rows, own = act.shape
    chunks = own // LANES
    width = normed.shape[1]
    micros, _, clusters = lengths.shape
    count = rows // micros
    taps = convw.shape[0]
    ranks = dtx.shape[0]
    states = decay.shape[0] // chunks
    cols = 2 * LANES
    extent = 4 * (LANES + 32)

    def by_cols(height):
        return pl.BlockSpec((height, cols), lambda i, p: (0, i ^ p[FACE]))

    def dy_spec(micro):
        return pl.BlockSpec(
            (2 * count, LANES), lambda i, p: (micro * (chunks // 2) + (i ^ p[FACE]), 0)
        )

    in_specs = (
        [pl.BlockSpec(memory_space=pltpu.SMEM)]
        + [whole((rows, LANES))] * 2
        + [by_cols(rows)] * 2
        + [whole(alog.shape), whole(back.shape)]
        + [whole(array.shape) for array in (dtx, bc_own, bc_other, decay)]
        + [dy_spec(micro) for micro in range(micros)]
        + [by_cols(rows)] * 3
        + [whole(array.shape) for array in (high, convw, skip, normed)]
        + [
            ANY,
            whole((rows, width)),
            whole((rows, width)),
        ]
    )
    return pl.pallas_call(
        functools.partial(
            tail_kernel,
            micros=micros,
            count=count,
            taps=taps,
            clusters=clusters,
            ranks=ranks,
            chunks=chunks,
            states=states,
        ),
        grid_spec=pltpu.PrefetchScalarGridSpec(
            num_scalar_prefetch=1,
            grid=(chunks // 2,),
            in_specs=in_specs,
            out_specs=[whole((extent, width)), whole((extent, width)), whole((rows, width))],
            scratch_shapes=[
                pltpu.VMEM((taps, rows, LANES), F32),
                pltpu.VMEM((rows, LANES), BF16),
                pltpu.VMEM((LANES, cols), BF16),
                pltpu.VMEM((8, own), F32),
                pltpu.VMEM((states * chunks, LANES), F32),
                pltpu.VMEM((rows, width), F32),
                pltpu.VMEM((chunks // 2, 2, LANES, width), BF16),
                pltpu.SemaphoreType.DMA((chunks // 2,)),
                pltpu.VMEM((rows, cols), BF16),
            ],
        ),
        out_shape=[
            hbm((extent, width), BF16),
            hbm((extent, width), BF16),
            hbm((rows, width), BF16),
        ],
        compiler_params=params(34),
        cost_estimate=cost(7),
        name="tail",
    )(
        place,
        lengths,
        *in_hbm([code_own]),
        code_other,
        *in_hbm(
            (
                sact,
                dpre,
                alog,
                back,
                dtx,
                bc_own,
                bc_other,
                decay,
                *([dy] * micros),
                conved,
                inner,
                act,
                high,
                convw,
                skip,
                normed,
                w4,
                gate_part,
                x,
            )
        ),
    )


def fetch_halves(source, which, half, target_ref, sems):
    copies = []
    for k in range(target_ref.shape[0]):
        pair = pl.ds(2 * k, 2)
        block = source.at[pair, half] if which is None else source.at[which, pair, half]
        copies.append(pltpu.make_async_copy(block, target_ref.at[k], sems.at[k]))
    for copy in copies:
        copy.start()
    return copies


def products_kernel(
    place_ref,
    gated_ref,
    dgate_ref,
    out_ref,
    weight_ref,
    mixed_ref,
    dnormed_ref,
    wout_ref,
    wgate_ref,
    out_sems,
    gate_sems,
):
    half = place_ref[HALF]
    width = mixed_ref.shape[1]
    jobs = (
        (fetch_halves(out_ref, None, half, wout_ref, out_sems), gated_ref, wout_ref, mixed_ref),
        (fetch_halves(weight_ref, 1, half, wgate_ref, gate_sems), dgate_ref, wgate_ref, dnormed_ref),
    )
    for copies, left_ref, right_ref, result_ref in jobs:
        total = None
        for k, copy in enumerate(copies):
            copy.wait()
            left = left_ref[:, 2 * k * LANES : 2 * (k + 1) * LANES]
            term = dot(left, right_ref[k].reshape(-1, width), 1, 0)
            total = term if total is None else total + term
        result_ref[...] = total.astype(BF16)


def products(place, gated, dgate, wout3, w4):
    rows, own = gated.shape
    width = w4.shape[-1]
    pairs = own // (2 * LANES)
    return pl.pallas_call(
        products_kernel,
        grid_spec=pltpu.PrefetchScalarGridSpec(
            num_scalar_prefetch=1,
            grid=(1,),
            in_specs=[whole((rows, own)), whole((rows, own)), ANY, ANY],
            out_specs=[whole((rows, width))] * 2,
            scratch_shapes=[
                pltpu.VMEM((pairs, 2, LANES, width), BF16),
                pltpu.VMEM((pairs, 2, LANES, width), BF16),
                pltpu.SemaphoreType.DMA((pairs,)),
                pltpu.SemaphoreType.DMA((pairs,)),
            ],
        ),
        out_shape=[hbm((rows, width), BF16)] * 2,
        compiler_params=params(20),
        cost_estimate=cost(4),
        name="products",
    )(place, *in_hbm((gated, dgate, wout3, w4)))


def finish_kernel(x_ref, mine_ref, theirs_ref, cotan_ref, gain_ref, grad_ref):
    x = x_ref[...].astype(F32)
    scale = lax.rsqrt(jnp.mean(x * x, axis=1, keepdims=True) + EPSILON)
    unit = x * scale
    dhat = (mine_ref[...].astype(F32) + theirs_ref[...].astype(F32)) * gain_ref[...]
    grad_ref[...] = cotan_ref[...].astype(F32) + scale * (
        dhat - unit * jnp.mean(dhat * unit, axis=1, keepdims=True)
    )


def finish(x, mine, theirs, cotan, gain):
    rows, width = x.shape
    by_rows = pl.BlockSpec((rows // 4, width), lambda i: (i, 0))
    return pl.pallas_call(
        finish_kernel,
        grid=(4,),
        in_specs=[by_rows] * 4 + [whole(gain.shape)],
        out_specs=by_rows,
        out_shape=jax.ShapeDtypeStruct((rows, width), F32),
        compiler_params=params(16),
        cost_estimate=cost(0),
        name="finish",
    )(*in_hbm((x, mine)), theirs, *in_hbm((cotan, gain)))


def unpack_kernel(
    near_ref,
    far_ref,
    out_ref,
    dtx_ref,
    dt_ref,
    bc_ref,
    alog_ref,
    convw_ref,
    convb_ref,
    bias_ref,
    skip_ref,
    out_grad_ref,
    *,
    eighth,
    taps,
    edge,
):
    pack = near_ref[...].astype(F32) + far_ref[...].astype(F32)
    for k in range(4):
        rows = pack[:, k * LANES : (k + 1) * LANES]
        dtx_ref[pl.ds(16 * k, 16), :] = rows[:, :edge]
        dt_ref[pl.ds(16 * k, 16), :] = pltpu.roll(rows, edge, 1)[:, :edge]
    rows = pack[:, 4 * LANES : 5 * LANES]
    bc_ref[0] = rows[:eighth]
    bc_ref[1] = rows[eighth:]
    rows = pack[:, 5 * LANES : 6 * LANES]
    alog_ref[...] = rows[:eighth]
    vec = rows[eighth:, :edge]
    convw_ref[...] = vec[:taps]
    convb_ref[...] = vec[taps : taps + 1]
    bias_ref[...] = vec[taps + 1 : taps + 2]
    skip_ref[...] = vec[taps + 2 : taps + 3]
    out_grad_ref[...] = out_ref[...].astype(F32)


def unpack(near, far, out, eighth, taps, ranks):
    edge = LANES // 2
    shapes = [
        (edge, ranks),
        (edge, ranks),
        (2, eighth, LANES),
        (eighth, LANES),
        (taps, edge),
        (1, edge),
        (1, edge),
        (1, edge),
        out.shape,
    ]
    return pl.pallas_call(
        functools.partial(unpack_kernel, eighth=eighth, taps=taps, edge=edge),
        grid=(1,),
        in_specs=[whole(array.shape) for array in (near, far, out)],
        out_specs=[whole(shape) for shape in shapes],
        out_shape=[jax.ShapeDtypeStruct(shape, F32) for shape in shapes],
        cost_estimate=cost(0),
        name="unpack",
    )(near, far, out)


def swap_pair(array):
    count = lax.axis_size("state")
    return lax.ppermute(array, "state", [(pos, pos ^ 1) for pos in range(count)])


def swap_bit(array, bits):
    return lax.ppermute(array, "dp", [(pos, pos ^ bits) for pos in range(lax.axis_size("dp"))])


def swap_both(array, bits=0):
    states = lax.axis_size("state")
    pairs = []
    for d in range(lax.axis_size("dp")):
        for s in range(states):
            pairs.append((d * states + s, (((d & ~1) | s) ^ bits) * states + (d & 1)))
    return lax.ppermute(array, ("dp", "state"), pairs)


def add_quarters(kept, got):
    extent = kept.shape[0] // 4
    return [kept[k * extent :][:extent] + got[k * extent :][:extent] for k in range(4)]


def trade_quarters(quarters):
    return [quarters[0]] + [swap_bit(quarters[k], k * X_BIT) for k in range(1, 4)]


def sum_quarters(quarters):
    left, right = (quarters[k].astype(F32) + quarters[k + 1].astype(F32) for k in (0, 2))
    return (left + right).astype(BF16)


CORE_BIT, X_BIT, ZH_BIT = 1, 2, 8


def shards(
    tokens,
    cluster_len,
    norm_gain,
    in_weight,
    conv_weight,
    conv_bias,
    dtx_weight,
    dt_weight,
    dt_bias,
    bc_weight,
    a_log,
    skip_gain,
    out_weight,
    cotangent,
):
    micros, count, width = tokens.shape
    inner = out_weight.shape[0]
    taps = conv_weight.shape[0]
    ranks = dtx_weight.shape[1]
    chunks = inner // (2 * LANES)
    own = chunks * LANES
    rows = micros * count
    edge = LANES // 2
    span = LANES + 32
    dp_parts = lax.axis_size("dp")
    state_count = lax.axis_size("state")
    dp_pos = lax.axis_index("dp")
    state_pos = lax.axis_index("state")
    half = state_pos & 1
    fast = state_count == 2 and dp_parts == 2 * chunks == 16
    if fast:
        place = jnp.stack([half, dp_pos & 1, dp_pos >> 1, (dp_pos >> 1) & 3])
        bc_own, alog_own = bc_weight, a_log
        bc_other, alog_other = swap_pair(bc_weight), swap_pair(a_log)
    else:
        place = jnp.stack([half, 0, 0, 0])
        bc_all = lax.all_gather(bc_weight, "state", axis=1, tiled=True)
        alog_all = lax.all_gather(a_log, "state", axis=0, tiled=True)
        eighth = alog_all.shape[0] // 2
        bc_own, bc_other = (
            lax.dynamic_slice_in_dim(bc_all, which * eighth, eighth, 1)
            for which in (half, 1 - half)
        )
        alog_own, alog_other = (
            lax.dynamic_slice_in_dim(alog_all, which * eighth, eighth, 0)
            for which in (half, 1 - half)
        )
    place = place.astype(jnp.int32)
    eighth = alog_own.shape[0]
    states = 2 * eighth

    x = tokens.reshape(rows, width)
    cotan = cotangent.reshape(rows, width)
    w4 = in_weight.reshape(2, chunks, 2, LANES, width)
    wout3 = out_weight.reshape(chunks, 2, LANES, width)
    dtx, dt = dtx_weight.T, dt_weight.T
    bias = dt_bias.reshape(-1, LANES)
    skip = skip_gain.reshape(-1, LANES)

    normed, act_all, act, inner_own, conved, gate = project(
        place, cluster_len, x, norm_gain[None], w4, conv_weight, conv_bias.reshape(-1, LANES)
    )
    bc, rank, high, decay, sp, u, dy, gated, dgate, keep, send = scan_forward(
        place,
        cluster_len,
        act_all,
        bc_own,
        bc_other,
        alog_own,
        alog_other,
        dtx,
        dt,
        bias,
        skip,
        act,
        gate,
        wout3,
        cotan,
        normed,
    )
    if fast:
        early = swap_bit(send, CORE_BIT)
    mixed_part, dn_gate = products(place, gated, dgate, wout3, w4)
    if fast:
        *quarters, mixed_part, dn_gate, sp = lax.optimization_barrier(
            (*add_quarters(keep, early), mixed_part, dn_gate, sp)
        )
        early_got = trade_quarters(quarters)
    mixed_other = swap_pair(mixed_part)
    code_own, sact, dpre, alog, back = scan_backward(
        place, micros, bc, decay, rank, dt, bias, act, sp, u, dy
    )
    code_other = swap_pair(code_own)
    if fast:
        block = sum_quarters(early_got)
        out_keep, out_send, gate_sum = block[:edge], block[edge:LANES], block[LANES:]
        out_send, gate_sum, mixed_other, conved = lax.optimization_barrier(
            (out_send, gate_sum, mixed_other, conved)
        )
        out_got = swap_bit(out_send, ZH_BIT)
    late_keep, late_send, dnormed_part = tail(
        place,
        cluster_len,
        code_own,
        code_other,
        sact,
        dpre,
        alog,
        back,
        dtx,
        bc_own,
        bc_other,
        decay,
        dy,
        conved,
        inner_own,
        act,
        high,
        conv_weight,
        skip,
        normed,
        w4,
        dn_gate,
        x,
    )
    if fast:
        late = swap_bit(late_send, CORE_BIT)
        out_own = swap_both(out_keep + out_got)
        late_got = trade_quarters(add_quarters(late_keep, late))
    dnormed_other = swap_pair(dnormed_part)
    tokens_grad = finish(x, dnormed_part, dnormed_other, cotan, norm_gain[None])
    mixed = (x.astype(F32) + (mixed_part.astype(F32) + mixed_other.astype(F32))).astype(BF16)
    if fast:
        *late_got, mixed, out_own, tokens_grad = lax.optimization_barrier(
            (*late_got, mixed, out_own, tokens_grad)
        )
        block = sum_quarters(late_got)
        inner_sum = block[:LANES]
        upper = dp_pos >= dp_parts // 2
        crossing = jnp.where(upper, inner_sum, gate_sum)
        first, second = crossing[:edge], crossing[edge:]
        first, pack_far, pack_near = lax.optimization_barrier(
            (first, block[-16:], block[LANES:-16])
        )
        pack_far = swap_both(pack_far, ZH_BIT)
        first_got = swap_bit(first, ZH_BIT)
        pack_near = swap_both(pack_near)
        first_got, pack_far, pack_near = lax.optimization_barrier((first_got, pack_far, pack_near))
        second_got = swap_bit(second, ZH_BIT)
        gain_mine = (
            pack_near[:, 5 * LANES : 6 * LANES].astype(F32)
            + pack_far[:, 5 * LANES : 6 * LANES].astype(F32)
        ).astype(BF16)
        gain_both = gain_mine[-1].astype(F32) + swap_bit(gain_mine, CORE_BIT)[-1].astype(F32)
        extent = width // (dp_parts * state_count)
        gain_grad = lax.dynamic_slice_in_dim(gain_both, (dp_pos & 1) * extent, extent, 0)
        (
            dtx_grad,
            dt_grad,
            bc_grad,
            alog_grad,
            convw_grad,
            convb_grad,
            bias_grad,
            skip_grad,
            out_own,
        ) = unpack(pack_near, pack_far, out_own, eighth, taps, ranks)
        convb_grad, bias_grad, skip_grad = (
            array[0] for array in (convb_grad, bias_grad, skip_grad)
        )
        in_grad = jnp.where(upper, gate_sum, inner_sum).astype(F32) + jnp.concatenate(
            [first_got, second_got]
        ).astype(F32)
    mixed = mixed.reshape(micros, count, width)
    tokens_grad = tokens_grad.reshape(micros, count, width)

    if not fast:
        def total(array):
            return lax.psum(array.astype(F32), "dp")

        def both_rows(array):
            mine = array.reshape(chunks, 1, LANES, -1)
            other = swap_pair(mine)
            low = jnp.where(half == 0, mine, other)
            high = jnp.where(half == 0, other, mine)
            return jnp.concatenate([low, high], axis=1).reshape(2 * own, -1)

        every = dp_parts * state_count
        at = dp_pos * state_count + state_pos

        def cut_own(array):
            extent = array.shape[0] // every
            return lax.dynamic_slice_in_dim(array, at * extent, extent, 0)

        pair = total(jnp.stack([keep, send])).reshape(2, 2, 2, 2 * LANES, width)
        outs = pair[:, :, :, :LANES].reshape(2, 2, 2, 2, edge, width)
        outs = jnp.transpose(outs, (3, 1, 2, 0, 4, 5)).reshape(own, width)
        gates = jnp.moveaxis(pair[:, :, :, LANES:], 0, 2).reshape(own, width)
        pair = total(jnp.stack([late_keep, late_send])).reshape(2, 2, 2, span, width)
        inners = jnp.moveaxis(pair[:, :, :, :LANES], 0, 2).reshape(own, width)
        packs = pair[:, :, :, LANES:].reshape(2, 2, 2, 2, 16, width // LANES, LANES)
        packs = jnp.transpose(packs, (3, 1, 2, 0, 5, 4, 6)).reshape(chunks, 2, -1, 16, LANES)
        small = both_rows(packs[:, :, :4].reshape(own, LANES))
        in_grad = cut_own(jnp.concatenate([both_rows(inners), both_rows(gates)]))
        out_own = cut_own(both_rows(outs))
        mine = cut_own(small)
        dtx_grad, dt_grad = mine[:, :ranks], mine[:, ranks:]
        vec_rows = jnp.swapaxes(packs[:, :, 5, eighth:, :edge], 2, 3).reshape(own, -1)
        gain_sum = vec_rows[:, -1].reshape(chunks, 2, 2, -1).swapaxes(1, 2).reshape(-1)
        gain_grad = cut_own(gain_sum + swap_pair(gain_sum))
        vec = cut_own(both_rows(vec_rows)).T
        state_rows = jnp.concatenate([packs[:, :, 4], packs[:, :, 5, :eighth]], axis=2)
        state_rows = state_rows.reshape(chunks, 2, 3, eighth, LANES)
        state_rows = jnp.transpose(state_rows, (0, 4, 2, 1, 3)).reshape(own, -1)
        extent = inner // dp_parts
        state_part = lax.dynamic_slice_in_dim(both_rows(state_rows), dp_pos * extent, extent, 0)
        state_part = state_part.T.reshape(3, state_count, -1, extent)
        state_part = lax.dynamic_index_in_dim(state_part, state_pos, 1, keepdims=False)
        bc_grad, alog_grad = state_part[:2], state_part[2]
        convw_grad, convb_grad, bias_grad, skip_grad = (
            vec[:taps], vec[taps], vec[taps + 1], vec[taps + 2]
        )

    return (
        mixed,
        tokens_grad,
        gain_grad,
        in_grad,
        convw_grad,
        convb_grad,
        dtx_grad,
        dt_grad,
        bias_grad,
        bc_grad,
        alog_grad,
        skip_grad,
        out_own,
    )


def solution(mesh):
    return jax.shard_map(
        shards,
        mesh=mesh,
        in_specs=(
            P(None, "dp", None),
            P(None, "dp", None),
            P(),
            P(),
            P(),
            P(),
            P(),
            P(),
            P(),
            P(None, "state", None),
            P("state", None),
            P(),
            P(),
            P(None, "dp", None),
        ),
        out_specs=(
            P(None, "dp", None),
            P(None, "dp", None),
            P(("dp", "state")),
            P(("dp", "state"), None),
            P(None, ("dp", "state")),
            P(("dp", "state")),
            P(("dp", "state"), None),
            P(("dp", "state"), None),
            P(("dp", "state")),
            P(None, "state", "dp"),
            P("state", "dp"),
            P(("dp", "state")),
            P(("dp", "state"), None),
        ),
        check_vma=False,
    )
```

```python
import functools
import math

import jax
import jax.numpy as jnp
from jax import lax
from jax.experimental import pallas as pl
from jax.experimental.pallas import tpu as pltpu
from jax.sharding import PartitionSpec as P

EPSILON = 1e-05
LANES = 128
RESET = 1e4
LOG2E = math.log2(math.e)
F32 = jnp.float32
BF16 = jnp.bfloat16
MIB = 1024 * 1024


def dot(left, right, left_dim, right_dim):
    return lax.dot_general(
        left, right, (((left_dim,), (right_dim,)), ((), ())), preferred_element_type=F32
    )


def params(mib):
    return pltpu.CompilerParams(
        vmem_limit_bytes=mib * MIB, dimension_semantics=("arbitrary",)
    )


ANY = pl.BlockSpec(memory_space=pl.ANY)


def stream(step, steps, fetch):
    @pl.when(step == 0)
    def _():
        for k in range(steps):
            for copy in fetch(k):
                copy.start()

    for copy in fetch(step):
        copy.wait()


def whole(shape):
    return pl.BlockSpec(shape, lambda *_: (0,) * len(shape))


sigmoid = jax.nn.sigmoid


def log_one_plus(value):
    series = value * (1.0 - value * (0.5 - value * (1.0 / 3.0)))
    return jnp.where(value < 1e-3, series, jnp.log(1.0 + value))


def lanes(index):
    return pl.ds(pl.multiple_of(index * LANES, LANES), LANES)


def cost(micros):
    return pl.CostEstimate(
        flops=int(micros * 1e9), bytes_accessed=int(micros * 1e6), transcendentals=0
    )


def hbm(shape, dtype):
    return pltpu.HBM(shape, dtype)


def in_hbm(arrays):
    return [pltpu.with_memory_space_constraint(array, pltpu.HBM) for array in arrays]


def aligned(start, size, to=8):
    return pl.ds(pl.multiple_of(start, to), size)


HALF, CORE, CUBE, FACE = range(4)


def fill_masks(len_ref, mask_ref, micros, count, taps, clusters):
    place = lax.broadcasted_iota(jnp.int32, (count, LANES), 0)
    for micro in range(micros):
        rows = pl.ds(micro * count, count)
        for back in range(1, taps):
            apart = place < back
            start = 0
            for cluster in range(clusters - 1):
                start = start + len_ref[micro, 0, cluster]
                apart = apart | ((place >= start) & (place < start + back))
            mask_ref[back, rows, :] = jnp.where(apart, 0.0, 1.0)
            if back == 1:
                mask_ref[0, rows, :] = jnp.where(apart, 1.0, 0.0)


def project_kernel(
    place_ref,
    len_ref,
    gain_ref,
    convw_ref,
    convb_ref,
    x_far,
    weight_far,
    normed_far,
    act_far,
    own_act_far,
    inner_far,
    conved_far,
    gate_far,
    mask_ref,
    x_ref,
    win_ref,
    wgate_ref,
    normed_ref,
    act_ref,
    own_act_ref,
    inner_ref,
    conved_ref,
    gate_ref,
    in_sems,
    out_sems,
    *,
    micros,
    count,
    taps,
    clusters,
):
    half = place_ref[HALF]
    chunks = win_ref.shape[0]
    inward = [pltpu.make_async_copy(x_far, x_ref, in_sems.at[2 * chunks])]
    for k in range(chunks):
        inward.append(pltpu.make_async_copy(weight_far.at[0, k], win_ref.at[k], in_sems.at[2 * k]))
        inward.append(
            pltpu.make_async_copy(
                weight_far.at[1, k, half], wgate_ref.at[k], in_sems.at[2 * k + 1]
            )
        )
    for copy in inward:
        copy.start()
    outward = []

    def put(source, target):
        outward.append(pltpu.make_async_copy(source, target, out_sems.at[len(outward)]))
        outward[-1].start()

    fill_masks(len_ref, mask_ref, micros, count, taps, clusters)
    inward[0].wait()
    rows = x_ref[...].astype(F32)
    scale = lax.rsqrt(jnp.mean(rows * rows, axis=1, keepdims=True) + EPSILON)
    normed = (rows * scale * gain_ref[...]).astype(BF16)
    normed_ref[...] = normed
    put(normed_ref, normed_far)
    for k in range(chunks):
        inward[2 * k + 1].wait()
        inward[2 * k + 2].wait()
        proj = dot(normed, win_ref[k].reshape(2 * LANES, -1), 1, 1)
        own = slice(k * LANES, (k + 1) * LANES)
        gate_ref[:, own] = dot(normed, wgate_ref[k], 1, 1)
        inners, conveds, acts = [], [], []
        for part in range(2):
            cols = slice((2 * k + part) * LANES, (2 * k + part + 1) * LANES)
            inner = proj[:, part * LANES : (part + 1) * LANES]
            conved = convb_ref[2 * k + part : 2 * k + part + 1, :]
            conved = conved + convw_ref[taps - 1 : taps, cols] * inner
            for back in range(1, taps):
                shifted = pltpu.roll(inner, back, 0) * mask_ref[back]
                conved = conved + convw_ref[taps - 1 - back : taps - back, cols] * shifted
            act = conved * sigmoid(conved)
            act_ref[:, cols] = act.astype(BF16)
            inners.append(inner)
            conveds.append(conved)
            acts.append(act)
        inner_ref[:, own] = jnp.where(half == 0, *inners)
        conved_ref[:, own] = jnp.where(half == 0, *conveds)
        own_act_ref[:, own] = jnp.where(half == 0, *acts).astype(BF16)
        if k % 2:
            group = pl.ds((k - 1) * LANES, 2 * LANES)
            wide = pl.ds(2 * (k - 1) * LANES, 4 * LANES)
            put(act_ref.at[:, wide], act_far.at[:, wide])
            for near, far in (
                (gate_ref, gate_far),
                (inner_ref, inner_far),
                (conved_ref, conved_far),
                (own_act_ref, own_act_far),
            ):
                put(near.at[:, group], far.at[:, group])
    for copy in outward:
        copy.wait()


def project(place, lengths, x, gain, w4, conv_weight, conv_bias):
    rows, width = x.shape
    chunks = w4.shape[1]
    micros, _, clusters = lengths.shape
    taps = conv_weight.shape[0]
    own = chunks * LANES
    outs = [
        ((rows, width), BF16),
        ((rows, 2 * own), BF16),
        ((rows, own), BF16),
        ((rows, own), F32),
        ((rows, own), F32),
        ((rows, own), F32),
    ]
    return pl.pallas_call(
        functools.partial(
            project_kernel, micros=micros, count=rows // micros, taps=taps, clusters=clusters
        ),
        grid_spec=pltpu.PrefetchScalarGridSpec(
            num_scalar_prefetch=1,
            grid=(1,),
            in_specs=[
                pl.BlockSpec(memory_space=pltpu.SMEM),
                whole(gain.shape),
                whole(conv_weight.shape),
                whole(conv_bias.shape),
                ANY,
                ANY,
            ],
            out_specs=[ANY] * len(outs),
            scratch_shapes=[
                pltpu.VMEM((taps, rows, LANES), F32),
                pltpu.VMEM((rows, width), BF16),
                pltpu.VMEM((chunks, 2, LANES, width), BF16),
                pltpu.VMEM((chunks, LANES, width), BF16),
            ]
            + [pltpu.VMEM(*out) for out in outs]
            + [
                pltpu.SemaphoreType.DMA((2 * chunks + 1,)),
                pltpu.SemaphoreType.DMA((1 + 5 * chunks // 2,)),
            ],
        ),
        out_shape=[hbm(*out) for out in outs],
        compiler_params=params(30),
        cost_estimate=cost(6),
        name="project",
    )(place, *in_hbm((lengths, gain, conv_weight, conv_bias, x, w4)))


def every_row(ref, row, height):
    return ref[pl.ds(row, height, stride=0), :]


def b_at(n, eighth):
    return (n // eighth) * 2 * eighth + n % eighth


def c_at(n, eighth):
    return b_at(n, eighth) + eighth


def forward_kernel(
    place_ref,
    len_ref,
    act_all_ref,
    bc_own_ref,
    bc_other_ref,
    alog_own_ref,
    alog_other_ref,
    dtx_ref,
    dt_ref,
    bias_ref,
    skip_ref,
    act_ref,
    *refs,
    micros,
    count,
    states,
    chunks,
    clusters,
):
    gate_far, wout_far, cotan_far, normed_far = refs[:4]
    bc_ref, rank_ref, rank_high_ref, decay_ref = refs[4:8]
    sp_far, u_far, step_far, slope_far, dy_far, gated_far, dgate_far, keep_far, send_far = refs[8:17]
    mask_ref, y_ref, tmp_ref, wide_ref = refs[17:21]
    gate_ref, wout_ref, cotan_ref, normed_ref = refs[21:25]
    sp_ref, u_ref, step_ref, slope_ref, dy_ref, gated_ref, dgate_ref, keep_ref, send_ref = refs[25:34]
    in_sems, out_sems = refs[34:]
    rows = micros * count
    eighth = states // 2
    half, core, cube, face = (place_ref[k] for k in range(4))
    first = half == 0
    inward = [
        pltpu.make_async_copy(source, target, in_sems.at[k])
        for k, (source, target) in enumerate(
            (
                (gate_far, gate_ref),
                (wout_far.at[:, half], wout_ref),
                (cotan_far, cotan_ref),
                (normed_far, normed_ref),
            )
        )
    ]
    for copy in inward:
        copy.start()
    outward = []

    def put(source, target):
        outward.append(pltpu.make_async_copy(source, target, out_sems.at[len(outward)]))
        outward[-1].start()

    act_all = act_all_ref[...]
    own = dot(act_all, bc_own_ref[...].reshape(states, -1), 1, 1)
    other = dot(act_all, bc_other_ref[...].reshape(states, -1), 1, 1)
    bc_ref[:, :states] = jnp.where(first, own, other)
    bc_ref[:, states:] = jnp.where(first, other, own)
    spread_lanes(bc_ref, wide_ref)

    fill_masks(len_ref, mask_ref, micros, count, 2, clusters)
    for chunk in range(chunks):
        cols = lanes(2 * chunk + half)
        own, other = alog_own_ref[:, cols], alog_other_ref[:, cols]
        tmp_ref[pl.ds(chunk * states, eighth), :] = jnp.where(first, own, other)
        tmp_ref[pl.ds(chunk * states + eighth, eighth), :] = jnp.where(first, other, own)
    for n in range(states):
        decay_ref[pl.ds(n * chunks, chunks), :] = -LOG2E * jnp.exp(
            tmp_ref[pl.ds(n, chunks, stride=states), :]
        )

    rank = dot(act_all, dtx_ref[...], 1, 1).astype(BF16)
    rank_ref[...] = rank
    rank_high_ref[...] = jnp.concatenate([jnp.zeros_like(rank), rank], axis=1)
    for chunk in range(chunks):
        cols = slice(chunk * LANES, (chunk + 1) * LANES)
        bias = bias_ref[pl.ds(2 * chunk + half, 1), :]
        pre = dot(rank, dt_ref[:, lanes(2 * chunk + half)], 1, 0) + bias
        tail_part = jnp.exp(-jnp.abs(pre))
        step = jnp.maximum(pre, 0.0) + log_one_plus(tail_part)
        slope = jnp.where(pre >= 0.0, 1.0, tail_part) / (1.0 + tail_part)
        step_ref[:, cols] = step
        slope_ref[:, cols] = slope.astype(BF16)
        held = step + RESET * mask_ref[0]
        source = step * act_ref[:, cols].astype(F32)
        for micro in range(micros):
            span = slice(micro * count, (micro + 1) * count)
            place = pl.ds((micro * chunks + chunk) * count, count)
            sp_ref[place, :] = held[span]
            u_ref[place, :] = source[span]
    put(sp_ref, sp_far)
    put(u_ref, u_far)
    put(step_ref, step_far)
    put(slope_ref, slope_far)

    for micro in range(micros):

        def advance(t, h, micro=micro):
            row = micro * count + t
            span = pl.ds(micro * chunks * count + t, chunks, stride=count)
            sp = sp_ref[span, :]
            u = u_ref[span, :]
            out = []
            y = None
            for n in range(states):
                decay = jnp.exp2(sp * decay_ref[pl.ds(n * chunks, chunks), :])
                now = decay * h[n] + u * every_row(wide_ref, b_at(n, eighth) * rows + row, chunks)
                out.append(now)
                term = now * every_row(wide_ref, c_at(n, eighth) * rows + row, chunks)
                y = term if y is None else y + term
            y_ref[span, :] = y
            return tuple(out)

        lax.fori_loop(0, count, advance, (jnp.zeros((chunks, LANES), F32),) * states, unroll=4)

    for copy in inward:
        copy.wait()
    cotan = cotan_ref[...]
    for chunk in range(chunks):
        cols = slice(chunk * LANES, (chunk + 1) * LANES)
        places = [pl.ds((micro * chunks + chunk) * count, count) for micro in range(micros)]
        y = jnp.concatenate([y_ref[place, :] for place in places])
        y = y + skip_ref[pl.ds(2 * chunk + half, 1), :] * act_ref[:, cols].astype(F32)
        gate = gate_ref[:, cols]
        sig = sigmoid(gate)
        gated_ref[:, cols] = (y * (gate * sig)).astype(BF16)
        dgated = dot(cotan, wout_ref[chunk], 1, 1)
        dy = dgated * (gate * sig)
        for micro in range(micros):
            dy_ref[places[micro], :] = dy[micro * count : (micro + 1) * count]
        dgate_ref[:, cols] = (dgated * y * (sig * (1.0 + gate * (1.0 - sig)))).astype(BF16)
    put(dy_ref, dy_far)
    put(gated_ref, gated_far)
    put(dgate_ref, dgate_far)
    normed = normed_ref[...]
    edge = LANES // 2
    for r in range(chunks // 2):
        for zh in range(2):
            grad = dot(gated_ref[:, lanes((r + 4 * zh) ^ cube)], cotan, 0, 0).astype(BF16)
            top, bottom = grad[:edge], grad[edge:]
            place = pl.ds(r * 2 * LANES + zh * edge, edge)
            keep_ref[place, :] = jnp.where(core == 0, top, bottom)
            send_ref[place, :] = jnp.where(core == 0, bottom, top)
        place = pl.ds((2 * r + 1) * LANES, LANES)
        pair = 2 * (r ^ face)
        for chunk, out_ref in ((pair + core, keep_ref), (pair + 1 - core, send_ref)):
            out_ref[place, :] = dot(dgate_ref[:, lanes(chunk)], normed, 0, 0).astype(BF16)
        place = pl.ds(r * 2 * LANES, 2 * LANES)
        put(send_ref.at[place], send_far.at[place])
        put(keep_ref.at[place], keep_far.at[place])
    for copy in outward:
        copy.wait()


def scan_forward(
    place,
    lengths,
    act_all,
    bc_own,
    bc_other,
    alog_own,
    alog_other,
    dtx,
    dt,
    bias,
    skip,
    act,
    gate,
    wout3,
    cotan,
    normed,
):
    rows, own = act.shape
    chunks = own // LANES
    states = 2 * alog_own.shape[0]
    width = cotan.shape[1]
    micros, _, clusters = lengths.shape
    ranks = dtx.shape[0]
    small = [
        ((rows, 2 * states), F32),
        ((rows, ranks), BF16),
        ((rows, 2 * ranks), BF16),
        ((states * chunks, LANES), F32),
    ]
    large = [
        ((chunks * rows, LANES), F32),
        ((chunks * rows, LANES), F32),
        ((rows, own), F32),
        ((rows, own), BF16),
        ((chunks * rows, LANES), F32),
        ((rows, own), BF16),
        ((rows, own), BF16),
        ((own, width), BF16),
        ((own, width), BF16),
    ]
    operands = (act_all, bc_own, bc_other, alog_own, alog_other, dtx, dt, bias, skip, act)
    streamed = (gate, wout3, cotan, normed)
    return pl.pallas_call(
        functools.partial(
            forward_kernel,
            micros=micros,
            count=rows // micros,
            states=states,
            chunks=chunks,
            clusters=clusters,
        ),
        grid_spec=pltpu.PrefetchScalarGridSpec(
            num_scalar_prefetch=1,
            grid=(1,),
            in_specs=[pl.BlockSpec(memory_space=pltpu.SMEM)]
            + [whole(operand.shape) for operand in operands]
            + [ANY] * len(streamed),
            out_specs=[whole(shape) for shape, _ in small] + [ANY] * len(large),
            scratch_shapes=[
                pltpu.VMEM((2, rows, LANES), F32),
                pltpu.VMEM((chunks * rows, LANES), F32),
                pltpu.VMEM((states * chunks, LANES), F32),
                pltpu.VMEM((2 * states * rows, LANES), F32),
                pltpu.VMEM((rows, own), F32),
                pltpu.VMEM((chunks, LANES, width), BF16),
                pltpu.VMEM((rows, width), BF16),
                pltpu.VMEM((rows, width), BF16),
            ]
            + [pltpu.VMEM(*out) for out in large]
            + [pltpu.SemaphoreType.DMA((4,)), pltpu.SemaphoreType.DMA((7 + chunks,))],
        ),
        out_shape=[hbm(*out) for out in small + large],
        compiler_params=params(52),
        cost_estimate=cost(19),
        name="scan_forward",
    )(
        place,
        lengths,
        *in_hbm(operands[:1]),
        *operands[1:5],
        *in_hbm((*operands[5:], *streamed)),
    )


def spread_lanes(values_ref, wide_ref):
    rows, count = values_ref.shape
    for k in range(count):
        wide_ref[pl.ds(k * rows, rows), :] = jnp.broadcast_to(
            values_ref[:, k : k + 1], (rows, LANES)
        )


def backward_kernel(
    place_ref,
    bc_ref,
    decay_ref,
    dt_ref,
    act_ref,
    sp_ref,
    u_ref,
    step_ref,
    slope_ref,
    dy_ref,
    code_ref,
    sact_ref,
    dpre_ref,
    alog_ref,
    vec_ref,
    h_ref,
    keep_ref,
    s_ref,
    d_ref,
    terms_ref,
    sums_b_ref,
    sums_c_ref,
    wide_ref,
    *,
    count,
    states,
    chunks,
):
    @pl.when(pl.program_id(0) == 0)
    def _():
        alog_ref[...] = jnp.zeros_like(alog_ref)
        vec_ref[...] = jnp.zeros_like(vec_ref)

    half = place_ref[HALF]
    eighth = states // 2
    zero = (jnp.zeros((chunks, LANES), F32),) * states
    for n in range(states):
        h_ref[pl.ds(n * chunks, chunks), :] = zero[0]
    spread_lanes(bc_ref, wide_ref)
    block = states * chunks

    def put_terms(which, t, terms):
        for n in range(0, states, 2):
            pair = jnp.concatenate(terms[n : n + 2]).astype(BF16)
            place = aligned(t * block + n * chunks, 2 * chunks, 16)
            terms_ref[place, which * LANES : (which + 1) * LANES] = pair

    def recompute(pair, h):
        for slot in range(4):
            t = 4 * pair + slot
            span = pl.ds(t, chunks, stride=count)
            sp = sp_ref[span, :]
            u = u_ref[span, :]
            dy = dy_ref[span, :]
            out = []
            terms = []
            for n in range(states):
                decay = jnp.exp2(sp * decay_ref[pl.ds(n * chunks, chunks), :])
                keep_ref[aligned(t * block + n * chunks, chunks), :] = decay
                now = decay * h[n] + u * every_row(wide_ref, b_at(n, eighth) * count + t, chunks)
                h_ref[aligned((t + 1) * block + n * chunks, chunks), :] = now
                terms.append(dy * now)
                out.append(now)
            h = tuple(out)
            put_terms(1, t, terms)
        return h

    lax.fori_loop(0, count // 4, recompute, zero)

    def retreat(back, carry):
        flows, totals = carry
        for slot in range(2):
            t = count - 1 - (2 * back + slot)
            span = pl.ds(t, chunks, stride=count)
            sp = sp_ref[span, :]
            u = u_ref[span, :]
            dy = dy_ref[span, :]
            out_flows = []
            out_totals = []
            terms = []
            d_sum = None
            s_sum = None
            for n in range(states):
                dh = flows[n] + dy * every_row(wide_ref, c_at(n, eighth) * count + t, chunks)
                place = aligned(t * block + n * chunks, chunks)
                flow = keep_ref[place, :] * dh
                out_flows.append(flow)
                q = flow * h_ref[place, :]
                out_totals.append(totals[n] + q * sp)
                d_term = q * decay_ref[pl.ds(n * chunks, chunks), :]
                s_term = dh * every_row(wide_ref, b_at(n, eighth) * count + t, chunks)
                d_sum = d_term if d_sum is None else d_sum + d_term
                s_sum = s_term if s_sum is None else s_sum + s_term
                terms.append(dh * u)
            s_ref[span, :] = s_sum
            d_ref[span, :] = d_sum
            put_terms(0, t, terms)
            flows, totals = tuple(out_flows), tuple(out_totals)
        return flows, totals

    _, totals = lax.fori_loop(0, count // 2, retreat, (zero, zero))
    for n in range(states):
        alog_ref[pl.ds(n * chunks, chunks), :] += totals[n]

    shape = (2 * states, 2 * block)
    group = lax.broadcasted_iota(jnp.int32, shape, 1) // chunks
    gather = jnp.where(group == lax.broadcasted_iota(jnp.int32, shape, 0), 1.0, 0.0).astype(BF16)

    @pl.loop(0, count // 16)
    def _(step):
        for k in range(8):
            at = 8 * step + k
            terms = terms_ref[aligned(at * 2 * block, 2 * block, 16), :]
            sums = dot(gather, terms, 1, 0)
            sums_b_ref[aligned(at * 2 * states, 2 * states), :] = sums[:, :LANES]
            sums_c_ref[aligned(at * 2 * states, 2 * states), :] = sums[:, LANES:]

    ranks = dt_ref.shape[0]
    drank = None
    for chunk in range(chunks):
        cols = slice(chunk * LANES, (chunk + 1) * LANES)
        place = pl.ds(chunk * count, count)
        act = act_ref[:, cols].astype(F32)
        weight = dt_ref[:, lanes(2 * chunk + half)]
        s_now = s_ref[place, :]
        dstep = d_ref[place, :] * (1.0 / LOG2E) + s_now * act
        sact_ref[:, cols] = s_now * step_ref[:, cols]
        dpre = dstep * slope_ref[:, cols].astype(F32)
        vec_ref[0:1, cols] += jnp.sum(dpre, axis=0, keepdims=True)
        vec_ref[1:2, cols] += jnp.sum(dy_ref[place, :] * act, axis=0, keepdims=True)
        low = dpre.astype(BF16)
        dpre_ref[:, cols] = low
        term = dot(low, weight, 1, 1)
        drank = term if drank is None else drank + term
    source = lax.broadcasted_iota(jnp.int32, (2 * LANES, LANES), 0)
    target = lax.broadcasted_iota(jnp.int32, (2 * LANES, LANES), 1)
    code = None
    for n in range(states):
        pair = jnp.concatenate(
            [ref[pl.ds(n, count, stride=states), :] for ref in (sums_b_ref, sums_c_ref)], axis=1
        )
        column = ranks + jnp.where(source < LANES, b_at(n, eighth), c_at(n, eighth))
        pick = jnp.where(target == column, 1.0, 0.0).astype(BF16)
        term = dot(pair.astype(BF16), pick, 1, 0)
        code = term if code is None else code + term
    code_ref[...] = code + jnp.concatenate([drank, jnp.zeros((count, LANES - ranks), F32)], axis=1)


def scan_backward(place, micros, bc, decay, dt, act, sp, u, step, slope, dy):
    rows, own = act.shape
    count = rows // micros
    chunks = own // LANES
    states = bc.shape[1] // 2
    outs = [
        ((rows, LANES), F32),
        ((rows, own), F32),
        ((rows, own), BF16),
        ((states * chunks, LANES), F32),
        ((2, own), F32),
    ]

    def block(*shape):
        return pl.BlockSpec(shape, lambda i, p: (i, 0))

    return pl.pallas_call(
        functools.partial(backward_kernel, count=count, states=states, chunks=chunks),
        grid_spec=pltpu.PrefetchScalarGridSpec(
            num_scalar_prefetch=1,
            grid=(micros,),
            in_specs=[
                block(count, 2 * states),
                whole(decay.shape),
                whole(dt.shape),
                block(count, own),
                block(chunks * count, LANES),
                block(chunks * count, LANES),
                block(count, own),
                block(count, own),
                block(chunks * count, LANES),
            ],
            out_specs=[block(count, LANES), block(count, own), block(count, own)]
            + [whole(shape) for shape, _ in outs[3:]],
            scratch_shapes=[
                pltpu.VMEM(((count + 1) * states * chunks, LANES), F32),
                pltpu.VMEM((count * states * chunks, LANES), F32),
                pltpu.VMEM((chunks * count, LANES), F32),
                pltpu.VMEM((chunks * count, LANES), F32),
                pltpu.VMEM((count * states * chunks, 2 * LANES), BF16),
                pltpu.VMEM((count * states, LANES), F32),
                pltpu.VMEM((count * states, LANES), F32),
                pltpu.VMEM((2 * states * count, LANES), F32),
            ],
        ),
        out_shape=[hbm(*out) for out in outs],
        compiler_params=params(48),
        cost_estimate=cost(0),
        name="scan_backward",
    )(place, *in_hbm((bc, decay, dt, act, sp, u, step, slope, dy)))


def tail_kernel(
    place_ref,
    len_ref,
    *refs,
    micros,
    count,
    taps,
    clusters,
    ranks,
    chunks,
    states,
):
    def take(number):
        nonlocal refs
        taken, refs = refs[:number], refs[number:]
        return taken

    code_own_ref, code_other_ref = take(2)
    sact_ref, dpre_ref, alog_sum_ref, back_ref = take(4)
    dtx_ref, bc_own_ref, bc_other_ref, decay_ref = take(4)
    dy_refs = take(micros)
    conved_ref, inner_ref, act_ref, high_ref, convw_ref, skip_ref = take(6)
    normed_ref, weight_ref, gate_part_ref, x_ref = take(4)
    keep_ref, send_ref, dnormed_ref = take(3)
    mask_ref, code_ref, wcode_ref, vec_ref, alog_ref, total_ref, win_ref, sems, low_ref = refs

    step = pl.program_id(0)
    rows = micros * count
    eighth = states // 2
    edge = LANES // 2
    half, core, cube, face = (place_ref[k] for k in range(4))
    pair = step ^ face
    span = LANES + 32

    def fetch(k):
        source = weight_ref.at[0, pl.ds(2 * (k ^ face), 2), half]
        return (pltpu.make_async_copy(source, win_ref.at[k], sems.at[k]),)

    stream(step, win_ref.shape[0], fetch)

    def pack_row(chunk):
        relative = chunk ^ cube
        return (relative & 3) * span + LANES + (relative >> 2) * 16

    def place_pair(start, size, cols, even, odd):
        keep_ref[aligned(start, size, 16), cols] = jnp.where(core == 0, even, odd).astype(BF16)
        send_ref[aligned(start, size, 16), cols] = jnp.where(core == 0, odd, even).astype(BF16)

    @pl.when(step == 0)
    def _():
        fill_masks(len_ref, mask_ref, micros, count, taps, clusters)
        total_ref[...] = gate_part_ref[...].astype(F32)
        code_ref[...] = (code_own_ref[...] + code_other_ref[...]).astype(BF16)
        alog_ref[...] = alog_sum_ref[...] * (decay_ref[...] * (1.0 / LOG2E))

    code = code_ref[...]
    lane = lax.broadcasted_iota(jnp.int32, (1, LANES), 1)
    code_rank = jnp.where(lane < ranks, code, jnp.zeros_like(code))
    dpre = dpre_ref[...]
    for part in range(2):
        source = lanes(2 * (2 * pair + part) + half)
        cols = slice(part * LANES, (part + 1) * LANES)
        wcode_ref[:ranks, cols] = dtx_ref[:, source]
        own = bc_own_ref[:, :, source].reshape(states, LANES)
        other = bc_other_ref[:, :, source].reshape(states, LANES)
        wcode_ref[ranks : ranks + states, cols] = jnp.where(half == 0, own, other)
        wcode_ref[ranks + states : ranks + 2 * states, cols] = jnp.where(half == 0, other, own)
        wcode_ref[ranks + 2 * states :, cols] = jnp.zeros(
            (LANES - ranks - 2 * states, LANES), BF16
        )
    for part in range(2):
        cols = slice(part * LANES, (part + 1) * LANES)
        chunk = 2 * pair + part
        source = 2 * chunk + half
        weights = convw_ref[:, lanes(source)]
        sact = sact_ref[:, cols]
        dy = jnp.concatenate([ref[pl.ds(part * count, count), :] for ref in dy_refs], axis=0)
        dact = sact + dot(code, wcode_ref[:, cols], 1, 0)
        dact = dact + dy * skip_ref[pl.ds(source, 1), :]
        conved = conved_ref[:, cols]
        sig = sigmoid(conved)
        dconv = dact * (sig * (1.0 + conved * (1.0 - sig)))
        inner = inner_ref[:, cols]
        dinner = weights[taps - 1 : taps] * dconv
        sums = [None] * (taps + 1)
        sums[taps - 1] = jnp.sum(dconv * inner, axis=0, keepdims=True)
        sums[taps] = jnp.sum(dconv, axis=0, keepdims=True)
        for back in range(1, taps):
            kept = dconv * mask_ref[back]
            dinner = dinner + weights[taps - 1 - back : taps - back] * pltpu.roll(
                kept, rows - back, 0
            )
            sums[taps - 1 - back] = jnp.sum(
                kept * pltpu.roll(inner, back, 0), axis=0, keepdims=True
            )
        for k in range(taps + 1):
            vec_ref[k : k + 1, lanes(chunk)] = sums[k]
        vec_ref[taps + 1 : taps + 3, lanes(chunk)] = back_ref[:, lanes(chunk)]
        low_ref[:, cols] = dinner.astype(BF16)

        act = act_ref[:, cols]
        start = pack_row(chunk)
        rows_now = dot(act, code_rank, 0, 0) + dot(dpre[:, cols], high_ref[...], 0, 0)
        for k in range(4):
            place_pair(
                start,
                16,
                slice(k * LANES, (k + 1) * LANES),
                rows_now[k * 16 : (k + 1) * 16],
                rows_now[edge + k * 16 : edge + (k + 1) * 16],
            )
        state_rows = dot(code, act, 0, 0)[ranks : ranks + 2 * states]
        place_pair(
            start, 16, slice(4 * LANES, 5 * LANES), state_rows[:states], state_rows[states:]
        )

    normed = normed_ref[...]
    for part in range(2):
        grad = dot(low_ref[:, lanes(core ^ part)], normed, 0, 0)
        out_ref = (keep_ref, send_ref)[part]
        out_ref[aligned(step * span, LANES, 16), :] = grad.astype(BF16)
    width = total_ref.shape[1]
    total_ref[...] += dot(low_ref[...], win_ref[step].reshape(2 * LANES, width), 1, 0)

    @pl.when(step == pl.num_programs(0) - 1)
    def _():
        total = total_ref[...]
        dnormed_ref[...] = total.astype(BF16)
        x = x_ref[...].astype(F32)
        unit = x * lax.rsqrt(jnp.mean(x * x, axis=1, keepdims=True) + EPSILON)
        vec_ref[taps + 3 : taps + 4, :] = jnp.sum(total * unit, axis=0, keepdims=True)
        is_gain = lax.broadcasted_iota(jnp.int32, (8, LANES), 0) == taps + 3
        for chunk in range(chunks):
            start = pack_row(chunk)
            vec = vec_ref[:, chunk * LANES : (chunk + 1) * LANES]
            far, farther = (pltpu.roll(vec, LANES - k * edge // 2, 1) for k in (1, 2))
            even = jnp.where(is_gain & (lane >= edge // 2), far, vec)
            odd = jnp.where(is_gain & (lane < edge // 2), far, farther)
            alog = [
                alog_ref[pl.ds(q * eighth * chunks + chunk, eighth, stride=chunks), :]
                for q in range(2)
            ]
            place_pair(
                start,
                16,
                slice(5 * LANES, 6 * LANES),
                jnp.concatenate([alog[0], even]),
                jnp.concatenate([alog[1], odd]),
            )
            blank = jnp.zeros((16, 2 * LANES), F32)
            place_pair(start, 16, slice(6 * LANES, 8 * LANES), blank, blank)


def tail(
    place,
    lengths,
    code_own,
    code_other,
    sact,
    dpre,
    alog,
    back,
    dtx,
    bc_own,
    bc_other,
    decay,
    dy,
    conved,
    inner,
    act,
    high,
    convw,
    skip,
    normed,
    w4,
    gate_part,
    x,
):
    rows, own = act.shape
    chunks = own // LANES
    width = normed.shape[1]
    micros, _, clusters = lengths.shape
    count = rows // micros
    taps = convw.shape[0]
    ranks = dtx.shape[0]
    states = decay.shape[0] // chunks
    cols = 2 * LANES
    extent = 4 * (LANES + 32)

    def by_cols(height):
        return pl.BlockSpec((height, cols), lambda i, p: (0, i ^ p[FACE]))

    def dy_spec(micro):
        return pl.BlockSpec(
            (2 * count, LANES), lambda i, p: (micro * (chunks // 2) + (i ^ p[FACE]), 0)
        )

    in_specs = (
        [pl.BlockSpec(memory_space=pltpu.SMEM)]
        + [whole((rows, LANES))] * 2
        + [by_cols(rows)] * 2
        + [whole(alog.shape), whole(back.shape)]
        + [whole(array.shape) for array in (dtx, bc_own, bc_other, decay)]
        + [dy_spec(micro) for micro in range(micros)]
        + [by_cols(rows)] * 3
        + [whole(array.shape) for array in (high, convw, skip, normed)]
        + [
            ANY,
            whole((rows, width)),
            whole((rows, width)),
        ]
    )
    return pl.pallas_call(
        functools.partial(
            tail_kernel,
            micros=micros,
            count=count,
            taps=taps,
            clusters=clusters,
            ranks=ranks,
            chunks=chunks,
            states=states,
        ),
        grid_spec=pltpu.PrefetchScalarGridSpec(
            num_scalar_prefetch=1,
            grid=(chunks // 2,),
            in_specs=in_specs,
            out_specs=[whole((extent, width)), whole((extent, width)), whole((rows, width))],
            scratch_shapes=[
                pltpu.VMEM((taps, rows, LANES), F32),
                pltpu.VMEM((rows, LANES), BF16),
                pltpu.VMEM((LANES, cols), BF16),
                pltpu.VMEM((8, own), F32),
                pltpu.VMEM((states * chunks, LANES), F32),
                pltpu.VMEM((rows, width), F32),
                pltpu.VMEM((chunks // 2, 2, LANES, width), BF16),
                pltpu.SemaphoreType.DMA((chunks // 2,)),
                pltpu.VMEM((rows, cols), BF16),
            ],
        ),
        out_shape=[
            hbm((extent, width), BF16),
            hbm((extent, width), BF16),
            hbm((rows, width), BF16),
        ],
        compiler_params=params(34),
        cost_estimate=cost(7),
        name="tail",
    )(
        place,
        lengths,
        *in_hbm([code_own]),
        code_other,
        *in_hbm(
            (
                sact,
                dpre,
                alog,
                back,
                dtx,
                bc_own,
                bc_other,
                decay,
                *([dy] * micros),
                conved,
                inner,
                act,
                high,
                convw,
                skip,
                normed,
                w4,
                gate_part,
                x,
            )
        ),
    )


def fetch_halves(source, which, half, target_ref, sems):
    copies = []
    for k in range(target_ref.shape[0]):
        pair = pl.ds(2 * k, 2)
        block = source.at[pair, half] if which is None else source.at[which, pair, half]
        copies.append(pltpu.make_async_copy(block, target_ref.at[k], sems.at[k]))
    for copy in copies:
        copy.start()
    return copies


def products_kernel(
    place_ref,
    gated_ref,
    dgate_ref,
    out_ref,
    weight_ref,
    mixed_ref,
    dnormed_ref,
    wout_ref,
    wgate_ref,
    out_sems,
    gate_sems,
):
    half = place_ref[HALF]
    width = mixed_ref.shape[1]
    jobs = (
        (fetch_halves(out_ref, None, half, wout_ref, out_sems), gated_ref, wout_ref, mixed_ref),
        (fetch_halves(weight_ref, 1, half, wgate_ref, gate_sems), dgate_ref, wgate_ref, dnormed_ref),
    )
    for copies, left_ref, right_ref, result_ref in jobs:
        total = None
        for k, copy in enumerate(copies):
            copy.wait()
            left = left_ref[:, 2 * k * LANES : 2 * (k + 1) * LANES]
            term = dot(left, right_ref[k].reshape(-1, width), 1, 0)
            total = term if total is None else total + term
        result_ref[...] = total.astype(BF16)


def products(place, gated, dgate, wout3, w4):
    rows, own = gated.shape
    width = w4.shape[-1]
    pairs = own // (2 * LANES)
    return pl.pallas_call(
        products_kernel,
        grid_spec=pltpu.PrefetchScalarGridSpec(
            num_scalar_prefetch=1,
            grid=(1,),
            in_specs=[whole((rows, own)), whole((rows, own)), ANY, ANY],
            out_specs=[whole((rows, width))] * 2,
            scratch_shapes=[
                pltpu.VMEM((pairs, 2, LANES, width), BF16),
                pltpu.VMEM((pairs, 2, LANES, width), BF16),
                pltpu.SemaphoreType.DMA((pairs,)),
                pltpu.SemaphoreType.DMA((pairs,)),
            ],
        ),
        out_shape=[hbm((rows, width), BF16)] * 2,
        compiler_params=params(20),
        cost_estimate=cost(4),
        name="products",
    )(place, *in_hbm((gated, dgate, wout3, w4)))


def finish_kernel(x_ref, mine_ref, theirs_ref, cotan_ref, gain_ref, grad_ref):
    x = x_ref[...].astype(F32)
    scale = lax.rsqrt(jnp.mean(x * x, axis=1, keepdims=True) + EPSILON)
    unit = x * scale
    dhat = (mine_ref[...].astype(F32) + theirs_ref[...].astype(F32)) * gain_ref[...]
    grad_ref[...] = cotan_ref[...].astype(F32) + scale * (
        dhat - unit * jnp.mean(dhat * unit, axis=1, keepdims=True)
    )


def finish(x, mine, theirs, cotan, gain):
    rows, width = x.shape
    by_rows = pl.BlockSpec((rows // 4, width), lambda i: (i, 0))
    return pl.pallas_call(
        finish_kernel,
        grid=(4,),
        in_specs=[by_rows] * 4 + [whole(gain.shape)],
        out_specs=by_rows,
        out_shape=jax.ShapeDtypeStruct((rows, width), F32),
        compiler_params=params(16),
        cost_estimate=cost(0),
        name="finish",
    )(*in_hbm((x, mine)), theirs, *in_hbm((cotan, gain)))


def unpack_kernel(
    near_ref,
    far_ref,
    out_ref,
    dtx_ref,
    dt_ref,
    bc_ref,
    alog_ref,
    convw_ref,
    convb_ref,
    bias_ref,
    skip_ref,
    out_grad_ref,
    *,
    eighth,
    taps,
    edge,
):
    pack = near_ref[...].astype(F32) + far_ref[...].astype(F32)
    for k in range(4):
        rows = pack[:, k * LANES : (k + 1) * LANES]
        dtx_ref[pl.ds(16 * k, 16), :] = rows[:, :edge]
        dt_ref[pl.ds(16 * k, 16), :] = pltpu.roll(rows, edge, 1)[:, :edge]
    rows = pack[:, 4 * LANES : 5 * LANES]
    bc_ref[0] = rows[:eighth]
    bc_ref[1] = rows[eighth:]
    rows = pack[:, 5 * LANES : 6 * LANES]
    alog_ref[...] = rows[:eighth]
    vec = rows[eighth:, :edge]
    convw_ref[...] = vec[:taps]
    convb_ref[...] = vec[taps : taps + 1]
    bias_ref[...] = vec[taps + 1 : taps + 2]
    skip_ref[...] = vec[taps + 2 : taps + 3]
    out_grad_ref[...] = out_ref[...].astype(F32)


def unpack(near, far, out, eighth, taps, ranks):
    edge = LANES // 2
    shapes = [
        (edge, ranks),
        (edge, ranks),
        (2, eighth, LANES),
        (eighth, LANES),
        (taps, edge),
        (1, edge),
        (1, edge),
        (1, edge),
        out.shape,
    ]
    return pl.pallas_call(
        functools.partial(unpack_kernel, eighth=eighth, taps=taps, edge=edge),
        grid=(1,),
        in_specs=[whole(array.shape) for array in (near, far, out)],
        out_specs=[whole(shape) for shape in shapes],
        out_shape=[jax.ShapeDtypeStruct(shape, F32) for shape in shapes],
        cost_estimate=cost(0),
        name="unpack",
    )(near, far, out)


def swap_pair(array):
    count = lax.axis_size("state")
    return lax.ppermute(array, "state", [(pos, pos ^ 1) for pos in range(count)])


def swap_bit(array, bits):
    return lax.ppermute(array, "dp", [(pos, pos ^ bits) for pos in range(lax.axis_size("dp"))])


def swap_both(array, bits=0):
    states = lax.axis_size("state")
    pairs = []
    for d in range(lax.axis_size("dp")):
        for s in range(states):
            pairs.append((d * states + s, (((d & ~1) | s) ^ bits) * states + (d & 1)))
    return lax.ppermute(array, ("dp", "state"), pairs)


def add_mixed(x, mine, theirs):
    return (x.astype(F32) + (mine.astype(F32) + theirs.astype(F32))).astype(BF16)


def add_quarters(kept, got, start=0, stop=None):
    extent = kept.shape[0] // 4
    stop = extent if stop is None else stop
    return [
        kept[k * extent + start : k * extent + stop] + got[k * extent + start : k * extent + stop]
        for k in range(4)
    ]


def trade_quarters(quarters):
    return [quarters[0]] + [swap_bit(quarters[k], k * X_BIT) for k in range(1, 4)]


def sum_quarters(quarters):
    left, right = (quarters[k].astype(F32) + quarters[k + 1].astype(F32) for k in (0, 2))
    return (left + right).astype(BF16)


CORE_BIT, X_BIT, ZH_BIT = 1, 2, 8


def shards(
    tokens,
    cluster_len,
    norm_gain,
    in_weight,
    conv_weight,
    conv_bias,
    dtx_weight,
    dt_weight,
    dt_bias,
    bc_weight,
    a_log,
    skip_gain,
    out_weight,
    cotangent,
):
    micros, count, width = tokens.shape
    inner = out_weight.shape[0]
    taps = conv_weight.shape[0]
    ranks = dtx_weight.shape[1]
    chunks = inner // (2 * LANES)
    own = chunks * LANES
    rows = micros * count
    edge = LANES // 2
    span = LANES + 32
    dp_parts = lax.axis_size("dp")
    state_count = lax.axis_size("state")
    dp_pos = lax.axis_index("dp")
    state_pos = lax.axis_index("state")
    half = state_pos & 1
    fast = state_count == 2 and dp_parts == 2 * chunks == 16
    if fast:
        place = jnp.stack([half, dp_pos & 1, dp_pos >> 1, (dp_pos >> 1) & 3])
        bc_own, alog_own = bc_weight, a_log
        bc_other, alog_other = swap_pair(bc_weight), swap_pair(a_log)
    else:
        place = jnp.stack([half, 0, 0, 0])
        bc_all = lax.all_gather(bc_weight, "state", axis=1, tiled=True)
        alog_all = lax.all_gather(a_log, "state", axis=0, tiled=True)
        eighth = alog_all.shape[0] // 2
        bc_own, bc_other = (
            lax.dynamic_slice_in_dim(bc_all, which * eighth, eighth, 1)
            for which in (half, 1 - half)
        )
        alog_own, alog_other = (
            lax.dynamic_slice_in_dim(alog_all, which * eighth, eighth, 0)
            for which in (half, 1 - half)
        )
    place = place.astype(jnp.int32)
    eighth = alog_own.shape[0]
    states = 2 * eighth

    x = tokens.reshape(rows, width)
    cotan = cotangent.reshape(rows, width)
    w4 = in_weight.reshape(2, chunks, 2, LANES, width)
    wout3 = out_weight.reshape(chunks, 2, LANES, width)
    dtx, dt = dtx_weight.T, dt_weight.T
    bias = dt_bias.reshape(-1, LANES)
    skip = skip_gain.reshape(-1, LANES)

    normed, act_all, act, inner_own, conved, gate = project(
        place, cluster_len, x, norm_gain[None], w4, conv_weight, conv_bias.reshape(-1, LANES)
    )
    bc, rank, high, decay, sp, u, step, slope, dy, gated, dgate, keep, send = scan_forward(
        place,
        cluster_len,
        act_all,
        bc_own,
        bc_other,
        alog_own,
        alog_other,
        dtx,
        dt,
        bias,
        skip,
        act,
        gate,
        wout3,
        cotan,
        normed,
    )
    if fast:
        early = swap_bit(send, CORE_BIT)
    mixed_part, dn_gate = products(place, gated, dgate, wout3, w4)
    if fast:
        *quarters, mixed_part, dn_gate, sp = lax.optimization_barrier(
            (*add_quarters(keep, early), mixed_part, dn_gate, sp)
        )
        early_got = trade_quarters(quarters)
    mixed_other = swap_pair(mixed_part)
    code_own, sact, dpre, alog, back = scan_backward(
        place, micros, bc, decay, dt, act, sp, u, step, slope, dy
    )
    code_other = swap_pair(code_own)
    if fast:
        block = sum_quarters(early_got)
        out_keep, out_send, gate_sum = block[:edge], block[edge:LANES], block[LANES:]
        mixed = add_mixed(x, mixed_part, mixed_other)
        out_send, gate_sum, mixed, conved = lax.optimization_barrier(
            (out_send, gate_sum, mixed, conved)
        )
        out_got = swap_bit(out_send, ZH_BIT)
    late_keep, late_send, dnormed_part = tail(
        place,
        cluster_len,
        code_own,
        code_other,
        sact,
        dpre,
        alog,
        back,
        dtx,
        bc_own,
        bc_other,
        decay,
        dy,
        conved,
        inner_own,
        act,
        high,
        conv_weight,
        skip,
        normed,
        w4,
        dn_gate,
        x,
    )
    if fast:
        late = swap_bit(late_send, CORE_BIT)
        cut = LANES - 32
        a_got = trade_quarters(add_quarters(late_keep, late, cut))
        b_got = trade_quarters(add_quarters(late_keep, late, 0, cut))
    dnormed_other = swap_pair(dnormed_part)
    tokens_grad = finish(x, dnormed_part, dnormed_other, cotan, norm_gain[None])
    if not fast:
        mixed = add_mixed(x, mixed_part, mixed_other)
    if fast:
        upper = dp_pos >= dp_parts // 2
        block = sum_quarters(a_got)
        a_inner = block[:32]
        a_send, pack_far, pack_near = lax.optimization_barrier(
            (jnp.where(upper, a_inner, gate_sum[cut:]), block[-16:], block[32:-16])
        )
        pack_far = swap_both(pack_far, ZH_BIT)
        a_cross = swap_bit(a_send, ZH_BIT)
        pack_near = swap_both(pack_near)
        a_cross, pack_far, pack_near, tokens_grad, out_got, *b_got = lax.optimization_barrier(
            (a_cross, pack_far, pack_near, tokens_grad, out_got, *b_got)
        )
        out_own = swap_both(out_keep + out_got)
        b_inner = sum_quarters(b_got)
        b_cross = swap_bit(jnp.where(upper, b_inner, gate_sum[:cut]), ZH_BIT)
        gain_mine = (
            pack_near[:, 5 * LANES : 6 * LANES].astype(F32)
            + pack_far[:, 5 * LANES : 6 * LANES].astype(F32)
        ).astype(BF16)
        gain_both = gain_mine[-1].astype(F32) + swap_bit(gain_mine, CORE_BIT)[-1].astype(F32)
        extent = width // (dp_parts * state_count)
        gain_grad = lax.dynamic_slice_in_dim(gain_both, (dp_pos & 1) * extent, extent, 0)
        (
            dtx_grad,
            dt_grad,
            bc_grad,
            alog_grad,
            convw_grad,
            convb_grad,
            bias_grad,
            skip_grad,
            out_own,
        ) = unpack(pack_near, pack_far, out_own, eighth, taps, ranks)
        convb_grad, bias_grad, skip_grad = (
            array[0] for array in (convb_grad, bias_grad, skip_grad)
        )
        in_grad = jnp.where(
            upper, gate_sum, jnp.concatenate([b_inner, a_inner])
        ).astype(F32) + jnp.concatenate([b_cross, a_cross]).astype(F32)

    mixed = mixed.reshape(micros, count, width)
    tokens_grad = tokens_grad.reshape(micros, count, width)

    if not fast:
        def total(array):
            return lax.psum(array.astype(F32), "dp")

        def both_rows(array):
            mine = array.reshape(chunks, 1, LANES, -1)
            other = swap_pair(mine)
            low = jnp.where(half == 0, mine, other)
            high = jnp.where(half == 0, other, mine)
            return jnp.concatenate([low, high], axis=1).reshape(2 * own, -1)

        every = dp_parts * state_count
        at = dp_pos * state_count + state_pos

        def cut_own(array):
            extent = array.shape[0] // every
            return lax.dynamic_slice_in_dim(array, at * extent, extent, 0)

        pair = total(jnp.stack([keep, send])).reshape(2, 2, 2, 2 * LANES, width)
        outs = pair[:, :, :, :LANES].reshape(2, 2, 2, 2, edge, width)
        outs = jnp.transpose(outs, (3, 1, 2, 0, 4, 5)).reshape(own, width)
        gates = jnp.moveaxis(pair[:, :, :, LANES:], 0, 2).reshape(own, width)
        pair = total(jnp.stack([late_keep, late_send])).reshape(2, 2, 2, span, width)
        inners = jnp.moveaxis(pair[:, :, :, :LANES], 0, 2).reshape(own, width)
        packs = pair[:, :, :, LANES:].reshape(2, 2, 2, 2, 16, width // LANES, LANES)
        packs = jnp.transpose(packs, (3, 1, 2, 0, 5, 4, 6)).reshape(chunks, 2, -1, 16, LANES)
        small = both_rows(packs[:, :, :4].reshape(own, LANES))
        in_grad = cut_own(jnp.concatenate([both_rows(inners), both_rows(gates)]))
        out_own = cut_own(both_rows(outs))
        mine = cut_own(small)
        dtx_grad, dt_grad = mine[:, :ranks], mine[:, ranks:]
        vec_rows = jnp.swapaxes(packs[:, :, 5, eighth:, :edge], 2, 3).reshape(own, -1)
        gain_sum = vec_rows[:, -1].reshape(chunks, 2, 2, -1).swapaxes(1, 2).reshape(-1)
        gain_grad = cut_own(gain_sum + swap_pair(gain_sum))
        vec = cut_own(both_rows(vec_rows)).T
        state_rows = jnp.concatenate([packs[:, :, 4], packs[:, :, 5, :eighth]], axis=2)
        state_rows = state_rows.reshape(chunks, 2, 3, eighth, LANES)
        state_rows = jnp.transpose(state_rows, (0, 4, 2, 1, 3)).reshape(own, -1)
        extent = inner // dp_parts
        state_part = lax.dynamic_slice_in_dim(both_rows(state_rows), dp_pos * extent, extent, 0)
        state_part = state_part.T.reshape(3, state_count, -1, extent)
        state_part = lax.dynamic_index_in_dim(state_part, state_pos, 1, keepdims=False)
        bc_grad, alog_grad = state_part[:2], state_part[2]
        convw_grad, convb_grad, bias_grad, skip_grad = (
            vec[:taps], vec[taps], vec[taps + 1], vec[taps + 2]
        )

    return (
        mixed,
        tokens_grad,
        gain_grad,
        in_grad,
        convw_grad,
        convb_grad,
        dtx_grad,
        dt_grad,
        bias_grad,
        bc_grad,
        alog_grad,
        skip_grad,
        out_own,
    )


def solution(mesh):
    return jax.shard_map(
        shards,
        mesh=mesh,
        in_specs=(
            P(None, "dp", None),
            P(None, "dp", None),
            P(),
            P(),
            P(),
            P(),
            P(),
            P(),
            P(),
            P(None, "state", None),
            P("state", None),
            P(),
            P(),
            P(None, "dp", None),
        ),
        out_specs=(
            P(None, "dp", None),
            P(None, "dp", None),
            P(("dp", "state")),
            P(("dp", "state"), None),
            P(None, ("dp", "state")),
            P(("dp", "state")),
            P(("dp", "state"), None),
            P(("dp", "state"), None),
            P(("dp", "state")),
            P(None, "state", "dp"),
            P("state", "dp"),
            P(("dp", "state")),
            P(("dp", "state"), None),
        ),
        check_vma=False,
    )
```

```python
import functools
import math

import jax
import jax.numpy as jnp
from jax import lax
from jax.experimental import pallas as pl
from jax.experimental.pallas import tpu as pltpu
from jax.sharding import PartitionSpec as P

EPSILON = 1e-05
LANES = 128
RESET = 1e4
LOG2E = math.log2(math.e)
F32 = jnp.float32
BF16 = jnp.bfloat16
MIB = 1024 * 1024


def dot(left, right, left_dim, right_dim):
    return lax.dot_general(
        left, right, (((left_dim,), (right_dim,)), ((), ())), preferred_element_type=F32
    )


def params(mib):
    return pltpu.CompilerParams(
        vmem_limit_bytes=mib * MIB, dimension_semantics=("arbitrary",)
    )


ANY = pl.BlockSpec(memory_space=pl.ANY)


def stream(step, steps, fetch):
    @pl.when(step == 0)
    def _():
        for k in range(steps):
            for copy in fetch(k):
                copy.start()

    for copy in fetch(step):
        copy.wait()


def whole(shape):
    return pl.BlockSpec(shape, lambda *_: (0,) * len(shape))


sigmoid = jax.nn.sigmoid


def log_one_plus(value):
    series = value * (1.0 - value * (0.5 - value * (1.0 / 3.0)))
    return jnp.where(value < 1e-3, series, jnp.log(1.0 + value))


def lanes(index):
    return pl.ds(pl.multiple_of(index * LANES, LANES), LANES)


def cost(micros):
    return pl.CostEstimate(
        flops=int(micros * 1e9), bytes_accessed=int(micros * 1e6), transcendentals=0
    )


def hbm(shape, dtype):
    return pltpu.HBM(shape, dtype)


def in_hbm(arrays):
    return [pltpu.with_memory_space_constraint(array, pltpu.HBM) for array in arrays]


def aligned(start, size, to=8):
    return pl.ds(pl.multiple_of(start, to), size)


SEGMENTS = 4

HALF, CORE, CUBE, FACE = range(4)


def fill_masks(len_ref, mask_ref, micros, count, taps, clusters):
    place = lax.broadcasted_iota(jnp.int32, (count, LANES), 0)
    for micro in range(micros):
        rows = pl.ds(micro * count, count)
        for back in range(1, taps):
            apart = place < back
            start = 0
            for cluster in range(clusters - 1):
                start = start + len_ref[micro, 0, cluster]
                apart = apart | ((place >= start) & (place < start + back))
            mask_ref[back, rows, :] = jnp.where(apart, 0.0, 1.0)
            if back == 1:
                mask_ref[0, rows, :] = jnp.where(apart, 1.0, 0.0)


def project_kernel(
    place_ref,
    len_ref,
    gain_ref,
    convw_ref,
    convb_ref,
    x_far,
    weight_far,
    normed_far,
    act_far,
    own_act_far,
    inner_far,
    conved_far,
    gate_far,
    mask_ref,
    x_ref,
    win_ref,
    wgate_ref,
    normed_ref,
    act_ref,
    own_act_ref,
    inner_ref,
    conved_ref,
    gate_ref,
    in_sems,
    out_sems,
    *,
    micros,
    count,
    taps,
    clusters,
):
    half = place_ref[HALF]
    chunks = win_ref.shape[0]
    inward = [pltpu.make_async_copy(x_far, x_ref, in_sems.at[2 * chunks])]
    for k in range(chunks):
        inward.append(pltpu.make_async_copy(weight_far.at[0, k], win_ref.at[k], in_sems.at[2 * k]))
        inward.append(
            pltpu.make_async_copy(
                weight_far.at[1, k, half], wgate_ref.at[k], in_sems.at[2 * k + 1]
            )
        )
    for copy in inward:
        copy.start()
    outward = []

    def put(source, target):
        outward.append(pltpu.make_async_copy(source, target, out_sems.at[len(outward)]))
        outward[-1].start()

    fill_masks(len_ref, mask_ref, micros, count, taps, clusters)
    inward[0].wait()
    rows = x_ref[...].astype(F32)
    scale = lax.rsqrt(jnp.mean(rows * rows, axis=1, keepdims=True) + EPSILON)
    normed = (rows * scale * gain_ref[...]).astype(BF16)
    normed_ref[...] = normed
    put(normed_ref, normed_far)
    for k in range(chunks):
        inward[2 * k + 1].wait()
        inward[2 * k + 2].wait()
        proj = dot(normed, win_ref[k].reshape(2 * LANES, -1), 1, 1)
        own = slice(k * LANES, (k + 1) * LANES)
        gate_ref[:, own] = dot(normed, wgate_ref[k], 1, 1)
        inners, conveds, acts = [], [], []
        for part in range(2):
            cols = slice((2 * k + part) * LANES, (2 * k + part + 1) * LANES)
            inner = proj[:, part * LANES : (part + 1) * LANES]
            conved = convb_ref[2 * k + part : 2 * k + part + 1, :]
            conved = conved + convw_ref[taps - 1 : taps, cols] * inner
            for back in range(1, taps):
                shifted = pltpu.roll(inner, back, 0) * mask_ref[back]
                conved = conved + convw_ref[taps - 1 - back : taps - back, cols] * shifted
            act = conved * sigmoid(conved)
            act_ref[:, cols] = act.astype(BF16)
            inners.append(inner)
            conveds.append(conved)
            acts.append(act)
        inner_ref[:, own] = jnp.where(half == 0, *inners)
        conved_ref[:, own] = jnp.where(half == 0, *conveds)
        own_act_ref[:, own] = jnp.where(half == 0, *acts).astype(BF16)
        if k % 2:
            group = pl.ds((k - 1) * LANES, 2 * LANES)
            wide = pl.ds(2 * (k - 1) * LANES, 4 * LANES)
            put(act_ref.at[:, wide], act_far.at[:, wide])
            for near, far in (
                (gate_ref, gate_far),
                (inner_ref, inner_far),
                (conved_ref, conved_far),
                (own_act_ref, own_act_far),
            ):
                put(near.at[:, group], far.at[:, group])
    for copy in outward:
        copy.wait()


def project(place, lengths, x, gain, w4, conv_weight, conv_bias):
    rows, width = x.shape
    chunks = w4.shape[1]
    micros, _, clusters = lengths.shape
    taps = conv_weight.shape[0]
    own = chunks * LANES
    outs = [
        ((rows, width), BF16),
        ((rows, 2 * own), BF16),
        ((rows, own), BF16),
        ((rows, own), F32),
        ((rows, own), F32),
        ((rows, own), F32),
    ]
    return pl.pallas_call(
        functools.partial(
            project_kernel, micros=micros, count=rows // micros, taps=taps, clusters=clusters
        ),
        grid_spec=pltpu.PrefetchScalarGridSpec(
            num_scalar_prefetch=1,
            grid=(1,),
            in_specs=[
                pl.BlockSpec(memory_space=pltpu.SMEM),
                whole(gain.shape),
                whole(conv_weight.shape),
                whole(conv_bias.shape),
                ANY,
                ANY,
            ],
            out_specs=[ANY] * len(outs),
            scratch_shapes=[
                pltpu.VMEM((taps, rows, LANES), F32),
                pltpu.VMEM((rows, width), BF16),
                pltpu.VMEM((chunks, 2, LANES, width), BF16),
                pltpu.VMEM((chunks, LANES, width), BF16),
            ]
            + [pltpu.VMEM(*out) for out in outs]
            + [
                pltpu.SemaphoreType.DMA((2 * chunks + 1,)),
                pltpu.SemaphoreType.DMA((1 + 5 * chunks // 2,)),
            ],
        ),
        out_shape=[hbm(*out) for out in outs],
        compiler_params=params(30),
        cost_estimate=cost(6),
        name="project",
    )(place, *in_hbm((lengths, gain, conv_weight, conv_bias, x, w4)))


def every_row(ref, row, height):
    return ref[pl.ds(row, height, stride=0), :]


def b_at(n, eighth):
    return (n // eighth) * 2 * eighth + n % eighth


def c_at(n, eighth):
    return b_at(n, eighth) + eighth


def forward_kernel(
    place_ref,
    len_ref,
    act_all_ref,
    bc_own_ref,
    bc_other_ref,
    alog_own_ref,
    alog_other_ref,
    dtx_ref,
    dt_ref,
    bias_ref,
    skip_ref,
    act_ref,
    *refs,
    micros,
    count,
    states,
    chunks,
    clusters,
):
    gate_far, wout_far, cotan_far, normed_far = refs[:4]
    bc_ref, rank_ref, rank_high_ref, decay_ref = refs[4:8]
    sp_far, u_far, step_far, slope_far, h_far, dy_far = refs[8:14]
    gated_far, dgate_far, keep_far, send_far = refs[14:18]
    mask_ref, y_ref, tmp_ref, wide_ref = refs[18:22]
    gate_ref, wout_ref, cotan_ref, normed_ref = refs[22:26]
    sp_ref, u_ref, step_ref, slope_ref, h_ref, dy_ref = refs[26:32]
    gated_ref, dgate_ref, keep_ref, send_ref = refs[32:36]
    in_sems, out_sems = refs[36:]
    rows = micros * count
    eighth = states // 2
    half, core, cube, face = (place_ref[k] for k in range(4))
    first = half == 0
    inward = [
        pltpu.make_async_copy(source, target, in_sems.at[k])
        for k, (source, target) in enumerate(
            (
                (gate_far, gate_ref),
                (wout_far.at[:, half], wout_ref),
                (cotan_far, cotan_ref),
                (normed_far, normed_ref),
            )
        )
    ]
    for copy in inward:
        copy.start()
    outward = []

    def put(source, target):
        outward.append(pltpu.make_async_copy(source, target, out_sems.at[len(outward)]))
        outward[-1].start()

    act_all = act_all_ref[...]
    own = dot(act_all, bc_own_ref[...].reshape(states, -1), 1, 1)
    other = dot(act_all, bc_other_ref[...].reshape(states, -1), 1, 1)
    bc_ref[:, :states] = jnp.where(first, own, other)
    bc_ref[:, states:] = jnp.where(first, other, own)
    spread_lanes(bc_ref, wide_ref)

    fill_masks(len_ref, mask_ref, micros, count, 2, clusters)
    for chunk in range(chunks):
        cols = lanes(2 * chunk + half)
        own, other = alog_own_ref[:, cols], alog_other_ref[:, cols]
        tmp_ref[pl.ds(chunk * states, eighth), :] = jnp.where(first, own, other)
        tmp_ref[pl.ds(chunk * states + eighth, eighth), :] = jnp.where(first, other, own)
    for n in range(states):
        decay_ref[pl.ds(n * chunks, chunks), :] = -LOG2E * jnp.exp(
            tmp_ref[pl.ds(n, chunks, stride=states), :]
        )

    rank = dot(act_all, dtx_ref[...], 1, 1).astype(BF16)
    rank_ref[...] = rank
    rank_high_ref[...] = jnp.concatenate([jnp.zeros_like(rank), rank], axis=1)
    for chunk in range(chunks):
        cols = slice(chunk * LANES, (chunk + 1) * LANES)
        bias = bias_ref[pl.ds(2 * chunk + half, 1), :]
        pre = dot(rank, dt_ref[:, lanes(2 * chunk + half)], 1, 0) + bias
        tail_part = jnp.exp(-jnp.abs(pre))
        step = jnp.maximum(pre, 0.0) + log_one_plus(tail_part)
        slope = jnp.where(pre >= 0.0, 1.0, tail_part) / (1.0 + tail_part)
        step_ref[:, cols] = step
        slope_ref[:, cols] = slope.astype(BF16)
        held = step + RESET * mask_ref[0]
        source = step * act_ref[:, cols].astype(F32)
        for micro in range(micros):
            span = slice(micro * count, (micro + 1) * count)
            place = pl.ds((micro * chunks + chunk) * count, count)
            sp_ref[place, :] = held[span]
            u_ref[place, :] = source[span]
    put(sp_ref, sp_far)
    put(u_ref, u_far)
    put(step_ref, step_far)
    put(slope_ref, slope_far)

    for micro in range(micros):

        def advance(t, h, micro=micro):
            row = micro * count + t
            span = pl.ds(micro * chunks * count + t, chunks, stride=count)
            sp = sp_ref[span, :]
            u = u_ref[span, :]
            out = []
            y = None
            for n in range(states):
                decay = jnp.exp2(sp * decay_ref[pl.ds(n * chunks, chunks), :])
                now = decay * h[n] + u * every_row(wide_ref, b_at(n, eighth) * rows + row, chunks)
                h_ref[aligned((row * states + n) * chunks, chunks), :] = now
                out.append(now)
                term = now * every_row(wide_ref, c_at(n, eighth) * rows + row, chunks)
                y = term if y is None else y + term
            y_ref[span, :] = y
            return tuple(out)

        h = (jnp.zeros((chunks, LANES), F32),) * states
        segment = count // SEGMENTS
        for k in range(SEGMENTS):
            h = lax.fori_loop(k * segment, (k + 1) * segment, advance, h, unroll=4)
            extent = segment * states * chunks
            place = pl.ds((micro * SEGMENTS + k) * extent, extent)
            put(h_ref.at[place], h_far.at[place])

    for copy in inward:
        copy.wait()
    cotan = cotan_ref[...]
    for chunk in range(chunks):
        cols = slice(chunk * LANES, (chunk + 1) * LANES)
        places = [pl.ds((micro * chunks + chunk) * count, count) for micro in range(micros)]
        y = jnp.concatenate([y_ref[place, :] for place in places])
        y = y + skip_ref[pl.ds(2 * chunk + half, 1), :] * act_ref[:, cols].astype(F32)
        gate = gate_ref[:, cols]
        sig = sigmoid(gate)
        gated_ref[:, cols] = (y * (gate * sig)).astype(BF16)
        dgated = dot(cotan, wout_ref[chunk], 1, 1)
        dy = dgated * (gate * sig)
        for micro in range(micros):
            dy_ref[places[micro], :] = dy[micro * count : (micro + 1) * count]
        dgate_ref[:, cols] = (dgated * y * (sig * (1.0 + gate * (1.0 - sig)))).astype(BF16)
    put(dy_ref, dy_far)
    put(gated_ref, gated_far)
    put(dgate_ref, dgate_far)
    normed = normed_ref[...]
    edge = LANES // 2
    for r in range(chunks // 2):
        for zh in range(2):
            grad = dot(gated_ref[:, lanes((r + 4 * zh) ^ cube)], cotan, 0, 0).astype(BF16)
            top, bottom = grad[:edge], grad[edge:]
            place = pl.ds(r * 2 * LANES + zh * edge, edge)
            keep_ref[place, :] = jnp.where(core == 0, top, bottom)
            send_ref[place, :] = jnp.where(core == 0, bottom, top)
        place = pl.ds((2 * r + 1) * LANES, LANES)
        pair = 2 * (r ^ face)
        for chunk, out_ref in ((pair + core, keep_ref), (pair + 1 - core, send_ref)):
            out_ref[place, :] = dot(dgate_ref[:, lanes(chunk)], normed, 0, 0).astype(BF16)
        place = pl.ds(r * 2 * LANES, 2 * LANES)
        put(send_ref.at[place], send_far.at[place])
        put(keep_ref.at[place], keep_far.at[place])
    for copy in outward:
        copy.wait()


def scan_forward(
    place,
    lengths,
    act_all,
    bc_own,
    bc_other,
    alog_own,
    alog_other,
    dtx,
    dt,
    bias,
    skip,
    act,
    gate,
    wout3,
    cotan,
    normed,
):
    rows, own = act.shape
    chunks = own // LANES
    states = 2 * alog_own.shape[0]
    width = cotan.shape[1]
    micros, _, clusters = lengths.shape
    ranks = dtx.shape[0]
    small = [
        ((rows, 2 * states), F32),
        ((rows, ranks), BF16),
        ((rows, 2 * ranks), BF16),
        ((states * chunks, LANES), F32),
    ]
    large = [
        ((chunks * rows, LANES), F32),
        ((chunks * rows, LANES), F32),
        ((rows, own), F32),
        ((rows, own), BF16),
        ((rows * states * chunks, LANES), F32),
        ((chunks * rows, LANES), F32),
        ((rows, own), BF16),
        ((rows, own), BF16),
        ((own, width), BF16),
        ((own, width), BF16),
    ]
    operands = (act_all, bc_own, bc_other, alog_own, alog_other, dtx, dt, bias, skip, act)
    streamed = (gate, wout3, cotan, normed)
    return pl.pallas_call(
        functools.partial(
            forward_kernel,
            micros=micros,
            count=rows // micros,
            states=states,
            chunks=chunks,
            clusters=clusters,
        ),
        grid_spec=pltpu.PrefetchScalarGridSpec(
            num_scalar_prefetch=1,
            grid=(1,),
            in_specs=[pl.BlockSpec(memory_space=pltpu.SMEM)]
            + [whole(operand.shape) for operand in operands]
            + [ANY] * len(streamed),
            out_specs=[whole(shape) for shape, _ in small] + [ANY] * len(large),
            scratch_shapes=[
                pltpu.VMEM((2, rows, LANES), F32),
                pltpu.VMEM((chunks * rows, LANES), F32),
                pltpu.VMEM((states * chunks, LANES), F32),
                pltpu.VMEM((2 * states * rows, LANES), F32),
                pltpu.VMEM((rows, own), F32),
                pltpu.VMEM((chunks, LANES, width), BF16),
                pltpu.VMEM((rows, width), BF16),
                pltpu.VMEM((rows, width), BF16),
            ]
            + [pltpu.VMEM(*out) for out in large]
            + [pltpu.SemaphoreType.DMA((4,)), pltpu.SemaphoreType.DMA((7 + chunks + micros * SEGMENTS,))],
        ),
        out_shape=[hbm(*out) for out in small + large],
        compiler_params=params(52),
        cost_estimate=cost(19),
        name="scan_forward",
    )(
        place,
        lengths,
        *in_hbm(operands[:1]),
        *operands[1:5],
        *in_hbm((*operands[5:], *streamed)),
    )


def spread_lanes(values_ref, wide_ref):
    rows, count = values_ref.shape
    for k in range(count):
        wide_ref[pl.ds(k * rows, rows), :] = jnp.broadcast_to(
            values_ref[:, k : k + 1], (rows, LANES)
        )


def backward_kernel(
    place_ref,
    bc_ref,
    decay_ref,
    dt_ref,
    act_ref,
    sp_ref,
    u_ref,
    step_ref,
    slope_ref,
    dy_ref,
    h_far,
    code_ref,
    sact_ref,
    dpre_ref,
    alog_ref,
    vec_ref,
    h_ref,
    s_ref,
    d_ref,
    terms_ref,
    sums_b_ref,
    sums_c_ref,
    wide_ref,
    sems,
    *,
    count,
    states,
    chunks,
):
    micro = pl.program_id(0)
    block = states * chunks
    segment = count // SEGMENTS

    def fetch(which, k):
        extent = segment * block
        buffer = h_ref.at[which % 2]
        return pltpu.make_async_copy(
            h_far.at[aligned((which * SEGMENTS + k) * extent, extent)],
            buffer.at[pl.ds(block + k * extent, extent)],
            sems.at[which % 2, k],
        )

    @pl.when(micro == 0)
    def _():
        for k in reversed(range(SEGMENTS)):
            fetch(0, k).start()
        for which in range(2):
            h_ref[which, pl.ds(0, block), :] = jnp.zeros((block, LANES), F32)
        alog_ref[...] = jnp.zeros_like(alog_ref)
        vec_ref[...] = jnp.zeros_like(vec_ref)

    half = place_ref[HALF]
    eighth = states // 2
    zero = (jnp.zeros((chunks, LANES), F32),) * states
    spread_lanes(bc_ref, wide_ref)

    @pl.when(micro + 1 < pl.num_programs(0))
    def _():
        for k in reversed(range(SEGMENTS)):
            fetch(micro + 1, k).start()

    side = micro % 2

    def put_terms(which, t, terms):
        for n in range(0, states, 2):
            pair = jnp.concatenate(terms[n : n + 2]).astype(BF16)
            place = aligned(t * block + n * chunks, 2 * chunks, 16)
            terms_ref[which, place, :] = pair

    def retreat(back, carry):
        flows, totals = carry
        for slot in range(2):
            t = count - 1 - (2 * back + slot)
            span = pl.ds(t, chunks, stride=count)
            sp = sp_ref[span, :]
            u = u_ref[span, :]
            dy = dy_ref[span, :]
            out_flows = []
            out_totals = []
            b_terms, c_terms = [], []
            d_sum = None
            s_sum = None
            for n in range(states):
                rate = decay_ref[pl.ds(n * chunks, chunks), :]
                dh = flows[n] + dy * every_row(wide_ref, c_at(n, eighth) * count + t, chunks)
                flow = jnp.exp2(sp * rate) * dh
                out_flows.append(flow)
                q = flow * h_ref[side, aligned(t * block + n * chunks, chunks), :]
                now = h_ref[side, aligned((t + 1) * block + n * chunks, chunks), :]
                out_totals.append(totals[n] + q * sp)
                d_term = q * rate
                s_term = dh * every_row(wide_ref, b_at(n, eighth) * count + t, chunks)
                d_sum = d_term if d_sum is None else d_sum + d_term
                s_sum = s_term if s_sum is None else s_sum + s_term
                b_terms.append(dh * u)
                c_terms.append(dy * now)
            s_ref[span, :] = s_sum
            d_ref[span, :] = d_sum
            put_terms(0, t, b_terms)
            put_terms(1, t, c_terms)
            flows, totals = tuple(out_flows), tuple(out_totals)
        return flows, totals

    carry = (zero, zero)
    for k in range(SEGMENTS):
        fetch(micro, SEGMENTS - 1 - k).wait()
        carry = lax.fori_loop(k * segment // 2, (k + 1) * segment // 2, retreat, carry)
    totals = carry[1]
    for n in range(states):
        alog_ref[pl.ds(n * chunks, chunks), :] += totals[n]

    shape = (2 * states, 2 * block)
    group = lax.broadcasted_iota(jnp.int32, shape, 1) // chunks
    gather = jnp.where(group == lax.broadcasted_iota(jnp.int32, shape, 0), 1.0, 0.0).astype(BF16)

    @pl.loop(0, count // 16)
    def _(step):
        for which, sums_ref in ((0, sums_b_ref), (1, sums_c_ref)):
            for k in range(8):
                at = 8 * step + k
                terms = terms_ref[which, aligned(at * 2 * block, 2 * block, 16), :]
                sums_ref[aligned(at * 2 * states, 2 * states), :] = dot(gather, terms, 1, 0)

    ranks = dt_ref.shape[0]
    drank = None
    for chunk in range(chunks):
        cols = slice(chunk * LANES, (chunk + 1) * LANES)
        place = pl.ds(chunk * count, count)
        act = act_ref[:, cols].astype(F32)
        weight = dt_ref[:, lanes(2 * chunk + half)]
        s_now = s_ref[place, :]
        dstep = d_ref[place, :] * (1.0 / LOG2E) + s_now * act
        sact_ref[:, cols] = s_now * step_ref[:, cols]
        dpre = dstep * slope_ref[:, cols].astype(F32)
        vec_ref[0:1, cols] += jnp.sum(dpre, axis=0, keepdims=True)
        vec_ref[1:2, cols] += jnp.sum(dy_ref[place, :] * act, axis=0, keepdims=True)
        low = dpre.astype(BF16)
        dpre_ref[:, cols] = low
        term = dot(low, weight, 1, 1)
        drank = term if drank is None else drank + term
    source = lax.broadcasted_iota(jnp.int32, (2 * LANES, LANES), 0)
    target = lax.broadcasted_iota(jnp.int32, (2 * LANES, LANES), 1)
    code = None
    for n in range(states):
        pair = jnp.concatenate(
            [ref[pl.ds(n, count, stride=states), :] for ref in (sums_b_ref, sums_c_ref)], axis=1
        )
        column = ranks + jnp.where(source < LANES, b_at(n, eighth), c_at(n, eighth))
        pick = jnp.where(target == column, 1.0, 0.0).astype(BF16)
        term = dot(pair.astype(BF16), pick, 1, 0)
        code = term if code is None else code + term
    code_ref[...] = code + jnp.concatenate([drank, jnp.zeros((count, LANES - ranks), F32)], axis=1)


def scan_backward(place, micros, bc, decay, dt, act, sp, u, step, slope, dy, h):
    rows, own = act.shape
    count = rows // micros
    chunks = own // LANES
    states = bc.shape[1] // 2
    outs = [
        ((rows, LANES), F32),
        ((rows, own), F32),
        ((rows, own), BF16),
        ((states * chunks, LANES), F32),
        ((2, own), F32),
    ]

    def block(*shape):
        return pl.BlockSpec(shape, lambda i, p: (i, 0))

    return pl.pallas_call(
        functools.partial(backward_kernel, count=count, states=states, chunks=chunks),
        grid_spec=pltpu.PrefetchScalarGridSpec(
            num_scalar_prefetch=1,
            grid=(micros,),
            in_specs=[
                block(count, 2 * states),
                whole(decay.shape),
                whole(dt.shape),
                block(count, own),
                block(chunks * count, LANES),
                block(chunks * count, LANES),
                block(count, own),
                block(count, own),
                block(chunks * count, LANES),
                ANY,
            ],
            out_specs=[block(count, LANES), block(count, own), block(count, own)]
            + [whole(shape) for shape, _ in outs[3:]],
            scratch_shapes=[
                pltpu.VMEM((2, (count + 1) * states * chunks, LANES), F32),
                pltpu.VMEM((chunks * count, LANES), F32),
                pltpu.VMEM((chunks * count, LANES), F32),
                pltpu.VMEM((2, count * states * chunks, LANES), BF16),
                pltpu.VMEM((count * states, LANES), F32),
                pltpu.VMEM((count * states, LANES), F32),
                pltpu.VMEM((2 * states * count, LANES), F32),
                pltpu.SemaphoreType.DMA((2, SEGMENTS)),
            ],
        ),
        out_shape=[hbm(*out) for out in outs],
        compiler_params=params(52),
        cost_estimate=cost(0),
        name="scan_backward",
    )(place, *in_hbm((bc, decay, dt, act, sp, u, step, slope, dy, h)))


def tail_kernel(
    place_ref,
    len_ref,
    *refs,
    micros,
    count,
    taps,
    clusters,
    ranks,
    chunks,
    states,
):
    def take(number):
        nonlocal refs
        taken, refs = refs[:number], refs[number:]
        return taken

    code_own_ref, code_other_ref = take(2)
    sact_ref, dpre_ref, alog_sum_ref, back_ref = take(4)
    dtx_ref, bc_own_ref, bc_other_ref, decay_ref = take(4)
    dy_refs = take(micros)
    conved_ref, inner_ref, act_ref, high_ref, convw_ref, skip_ref = take(6)
    normed_ref, weight_ref, gate_part_ref, x_ref = take(4)
    keep_ref, send_ref, dnormed_ref = take(3)
    mask_ref, code_ref, wcode_ref, vec_ref, alog_ref, total_ref, win_ref, sems, low_ref = refs

    step = pl.program_id(0)
    rows = micros * count
    eighth = states // 2
    edge = LANES // 2
    half, core, cube, face = (place_ref[k] for k in range(4))
    pair = step ^ face
    span = LANES + 32

    def fetch(k):
        source = weight_ref.at[0, pl.ds(2 * (k ^ face), 2), half]
        return (pltpu.make_async_copy(source, win_ref.at[k], sems.at[k]),)

    stream(step, win_ref.shape[0], fetch)

    def pack_row(chunk):
        relative = chunk ^ cube
        return (relative & 3) * span + LANES + (relative >> 2) * 16

    def place_pair(start, size, cols, even, odd):
        keep_ref[aligned(start, size, 16), cols] = jnp.where(core == 0, even, odd).astype(BF16)
        send_ref[aligned(start, size, 16), cols] = jnp.where(core == 0, odd, even).astype(BF16)

    @pl.when(step == 0)
    def _():
        fill_masks(len_ref, mask_ref, micros, count, taps, clusters)
        total_ref[...] = gate_part_ref[...].astype(F32)
        code_ref[...] = (code_own_ref[...] + code_other_ref[...]).astype(BF16)
        alog_ref[...] = alog_sum_ref[...] * (decay_ref[...] * (1.0 / LOG2E))

    code = code_ref[...]
    lane = lax.broadcasted_iota(jnp.int32, (1, LANES), 1)
    code_rank = jnp.where(lane < ranks, code, jnp.zeros_like(code))
    dpre = dpre_ref[...]
    for part in range(2):
        source = lanes(2 * (2 * pair + part) + half)
        cols = slice(part * LANES, (part + 1) * LANES)
        wcode_ref[:ranks, cols] = dtx_ref[:, source]
        own = bc_own_ref[:, :, source].reshape(states, LANES)
        other = bc_other_ref[:, :, source].reshape(states, LANES)
        wcode_ref[ranks : ranks + states, cols] = jnp.where(half == 0, own, other)
        wcode_ref[ranks + states : ranks + 2 * states, cols] = jnp.where(half == 0, other, own)
        wcode_ref[ranks + 2 * states :, cols] = jnp.zeros(
            (LANES - ranks - 2 * states, LANES), BF16
        )
    for part in range(2):
        cols = slice(part * LANES, (part + 1) * LANES)
        chunk = 2 * pair + part
        source = 2 * chunk + half
        weights = convw_ref[:, lanes(source)]
        sact = sact_ref[:, cols]
        dy = jnp.concatenate([ref[pl.ds(part * count, count), :] for ref in dy_refs], axis=0)
        dact = sact + dot(code, wcode_ref[:, cols], 1, 0)
        dact = dact + dy * skip_ref[pl.ds(source, 1), :]
        conved = conved_ref[:, cols]
        sig = sigmoid(conved)
        dconv = dact * (sig * (1.0 + conved * (1.0 - sig)))
        inner = inner_ref[:, cols]
        dinner = weights[taps - 1 : taps] * dconv
        sums = [None] * (taps + 1)
        sums[taps - 1] = jnp.sum(dconv * inner, axis=0, keepdims=True)
        sums[taps] = jnp.sum(dconv, axis=0, keepdims=True)
        for back in range(1, taps):
            kept = dconv * mask_ref[back]
            dinner = dinner + weights[taps - 1 - back : taps - back] * pltpu.roll(
                kept, rows - back, 0
            )
            sums[taps - 1 - back] = jnp.sum(
                kept * pltpu.roll(inner, back, 0), axis=0, keepdims=True
            )
        for k in range(taps + 1):
            vec_ref[k : k + 1, lanes(chunk)] = sums[k]
        vec_ref[taps + 1 : taps + 3, lanes(chunk)] = back_ref[:, lanes(chunk)]
        low_ref[:, cols] = dinner.astype(BF16)

        act = act_ref[:, cols]
        start = pack_row(chunk)
        rows_now = dot(act, code_rank, 0, 0) + dot(dpre[:, cols], high_ref[...], 0, 0)
        for k in range(4):
            place_pair(
                start,
                16,
                slice(k * LANES, (k + 1) * LANES),
                rows_now[k * 16 : (k + 1) * 16],
                rows_now[edge + k * 16 : edge + (k + 1) * 16],
            )
        state_rows = dot(code, act, 0, 0)[ranks : ranks + 2 * states]
        place_pair(
            start, 16, slice(4 * LANES, 5 * LANES), state_rows[:states], state_rows[states:]
        )

    normed = normed_ref[...]
    for part in range(2):
        grad = dot(low_ref[:, lanes(core ^ part)], normed, 0, 0)
        out_ref = (keep_ref, send_ref)[part]
        out_ref[aligned(step * span, LANES, 16), :] = grad.astype(BF16)
    width = total_ref.shape[1]
    total_ref[...] += dot(low_ref[...], win_ref[step].reshape(2 * LANES, width), 1, 0)

    @pl.when(step == pl.num_programs(0) - 1)
    def _():
        total = total_ref[...]
        dnormed_ref[...] = total.astype(BF16)
        x = x_ref[...].astype(F32)
        unit = x * lax.rsqrt(jnp.mean(x * x, axis=1, keepdims=True) + EPSILON)
        vec_ref[taps + 3 : taps + 4, :] = jnp.sum(total * unit, axis=0, keepdims=True)
        is_gain = lax.broadcasted_iota(jnp.int32, (8, LANES), 0) == taps + 3
        for chunk in range(chunks):
            start = pack_row(chunk)
            vec = vec_ref[:, chunk * LANES : (chunk + 1) * LANES]
            far, farther = (pltpu.roll(vec, LANES - k * edge // 2, 1) for k in (1, 2))
            even = jnp.where(is_gain & (lane >= edge // 2), far, vec)
            odd = jnp.where(is_gain & (lane < edge // 2), far, farther)
            alog = [
                alog_ref[pl.ds(q * eighth * chunks + chunk, eighth, stride=chunks), :]
                for q in range(2)
            ]
            place_pair(
                start,
                16,
                slice(5 * LANES, 6 * LANES),
                jnp.concatenate([alog[0], even]),
                jnp.concatenate([alog[1], odd]),
            )
            blank = jnp.zeros((16, 2 * LANES), F32)
            place_pair(start, 16, slice(6 * LANES, 8 * LANES), blank, blank)


def tail(
    place,
    lengths,
    code_own,
    code_other,
    sact,
    dpre,
    alog,
    back,
    dtx,
    bc_own,
    bc_other,
    decay,
    dy,
    conved,
    inner,
    act,
    high,
    convw,
    skip,
    normed,
    w4,
    gate_part,
    x,
):
    rows, own = act.shape
    chunks = own // LANES
    width = normed.shape[1]
    micros, _, clusters = lengths.shape
    count = rows // micros
    taps = convw.shape[0]
    ranks = dtx.shape[0]
    states = decay.shape[0] // chunks
    cols = 2 * LANES
    extent = 4 * (LANES + 32)

    def by_cols(height):
        return pl.BlockSpec((height, cols), lambda i, p: (0, i ^ p[FACE]))

    def dy_spec(micro):
        return pl.BlockSpec(
            (2 * count, LANES), lambda i, p: (micro * (chunks // 2) + (i ^ p[FACE]), 0)
        )

    in_specs = (
        [pl.BlockSpec(memory_space=pltpu.SMEM)]
        + [whole((rows, LANES))] * 2
        + [by_cols(rows)] * 2
        + [whole(alog.shape), whole(back.shape)]
        + [whole(array.shape) for array in (dtx, bc_own, bc_other, decay)]
        + [dy_spec(micro) for micro in range(micros)]
        + [by_cols(rows)] * 3
        + [whole(array.shape) for array in (high, convw, skip, normed)]
        + [
            ANY,
            whole((rows, width)),
            whole((rows, width)),
        ]
    )
    return pl.pallas_call(
        functools.partial(
            tail_kernel,
            micros=micros,
            count=count,
            taps=taps,
            clusters=clusters,
            ranks=ranks,
            chunks=chunks,
            states=states,
        ),
        grid_spec=pltpu.PrefetchScalarGridSpec(
            num_scalar_prefetch=1,
            grid=(chunks // 2,),
            in_specs=in_specs,
            out_specs=[whole((extent, width)), whole((extent, width)), whole((rows, width))],
            scratch_shapes=[
                pltpu.VMEM((taps, rows, LANES), F32),
                pltpu.VMEM((rows, LANES), BF16),
                pltpu.VMEM((LANES, cols), BF16),
                pltpu.VMEM((8, own), F32),
                pltpu.VMEM((states * chunks, LANES), F32),
                pltpu.VMEM((rows, width), F32),
                pltpu.VMEM((chunks // 2, 2, LANES, width), BF16),
                pltpu.SemaphoreType.DMA((chunks // 2,)),
                pltpu.VMEM((rows, cols), BF16),
            ],
        ),
        out_shape=[
            hbm((extent, width), BF16),
            hbm((extent, width), BF16),
            hbm((rows, width), BF16),
        ],
        compiler_params=params(34),
        cost_estimate=cost(7),
        name="tail",
    )(
        place,
        lengths,
        *in_hbm([code_own]),
        code_other,
        *in_hbm(
            (
                sact,
                dpre,
                alog,
                back,
                dtx,
                bc_own,
                bc_other,
                decay,
                *([dy] * micros),
                conved,
                inner,
                act,
                high,
                convw,
                skip,
                normed,
                w4,
                gate_part,
                x,
            )
        ),
    )


def fetch_halves(source, which, half, target_ref, sems):
    copies = []
    for k in range(target_ref.shape[0]):
        pair = pl.ds(2 * k, 2)
        block = source.at[pair, half] if which is None else source.at[which, pair, half]
        copies.append(pltpu.make_async_copy(block, target_ref.at[k], sems.at[k]))
    for copy in copies:
        copy.start()
    return copies


def products_kernel(
    place_ref,
    gated_ref,
    dgate_ref,
    out_ref,
    weight_ref,
    mixed_ref,
    dnormed_ref,
    wout_ref,
    wgate_ref,
    out_sems,
    gate_sems,
):
    half = place_ref[HALF]
    width = mixed_ref.shape[1]
    jobs = (
        (fetch_halves(out_ref, None, half, wout_ref, out_sems), gated_ref, wout_ref, mixed_ref),
        (fetch_halves(weight_ref, 1, half, wgate_ref, gate_sems), dgate_ref, wgate_ref, dnormed_ref),
    )
    for copies, left_ref, right_ref, result_ref in jobs:
        total = None
        for k, copy in enumerate(copies):
            copy.wait()
            left = left_ref[:, 2 * k * LANES : 2 * (k + 1) * LANES]
            term = dot(left, right_ref[k].reshape(-1, width), 1, 0)
            total = term if total is None else total + term
        result_ref[...] = total.astype(BF16)


def products(place, gated, dgate, wout3, w4):
    rows, own = gated.shape
    width = w4.shape[-1]
    pairs = own // (2 * LANES)
    return pl.pallas_call(
        products_kernel,
        grid_spec=pltpu.PrefetchScalarGridSpec(
            num_scalar_prefetch=1,
            grid=(1,),
            in_specs=[whole((rows, own)), whole((rows, own)), ANY, ANY],
            out_specs=[whole((rows, width))] * 2,
            scratch_shapes=[
                pltpu.VMEM((pairs, 2, LANES, width), BF16),
                pltpu.VMEM((pairs, 2, LANES, width), BF16),
                pltpu.SemaphoreType.DMA((pairs,)),
                pltpu.SemaphoreType.DMA((pairs,)),
            ],
        ),
        out_shape=[hbm((rows, width), BF16)] * 2,
        compiler_params=params(20),
        cost_estimate=cost(4),
        name="products",
    )(place, *in_hbm((gated, dgate, wout3, w4)))


def finish_kernel(x_ref, mine_ref, theirs_ref, cotan_ref, gain_ref, grad_ref):
    x = x_ref[...].astype(F32)
    scale = lax.rsqrt(jnp.mean(x * x, axis=1, keepdims=True) + EPSILON)
    unit = x * scale
    dhat = (mine_ref[...].astype(F32) + theirs_ref[...].astype(F32)) * gain_ref[...]
    grad_ref[...] = cotan_ref[...].astype(F32) + scale * (
        dhat - unit * jnp.mean(dhat * unit, axis=1, keepdims=True)
    )


def finish(x, mine, theirs, cotan, gain):
    rows, width = x.shape
    by_rows = pl.BlockSpec((rows // 4, width), lambda i: (i, 0))
    return pl.pallas_call(
        finish_kernel,
        grid=(4,),
        in_specs=[by_rows] * 4 + [whole(gain.shape)],
        out_specs=by_rows,
        out_shape=jax.ShapeDtypeStruct((rows, width), F32),
        compiler_params=params(16),
        cost_estimate=cost(0),
        name="finish",
    )(*in_hbm((x, mine)), theirs, *in_hbm((cotan, gain)))


def unpack_kernel(
    near_ref,
    far_ref,
    out_ref,
    dtx_ref,
    dt_ref,
    bc_ref,
    alog_ref,
    convw_ref,
    convb_ref,
    bias_ref,
    skip_ref,
    out_grad_ref,
    *,
    eighth,
    taps,
    edge,
):
    pack = near_ref[...].astype(F32) + far_ref[...].astype(F32)
    for k in range(4):
        rows = pack[:, k * LANES : (k + 1) * LANES]
        dtx_ref[pl.ds(16 * k, 16), :] = rows[:, :edge]
        dt_ref[pl.ds(16 * k, 16), :] = pltpu.roll(rows, edge, 1)[:, :edge]
    rows = pack[:, 4 * LANES : 5 * LANES]
    bc_ref[0] = rows[:eighth]
    bc_ref[1] = rows[eighth:]
    rows = pack[:, 5 * LANES : 6 * LANES]
    alog_ref[...] = rows[:eighth]
    vec = rows[eighth:, :edge]
    convw_ref[...] = vec[:taps]
    convb_ref[...] = vec[taps : taps + 1]
    bias_ref[...] = vec[taps + 1 : taps + 2]
    skip_ref[...] = vec[taps + 2 : taps + 3]
    out_grad_ref[...] = out_ref[...].astype(F32)


def unpack(near, far, out, eighth, taps, ranks):
    edge = LANES // 2
    shapes = [
        (edge, ranks),
        (edge, ranks),
        (2, eighth, LANES),
        (eighth, LANES),
        (taps, edge),
        (1, edge),
        (1, edge),
        (1, edge),
        out.shape,
    ]
    return pl.pallas_call(
        functools.partial(unpack_kernel, eighth=eighth, taps=taps, edge=edge),
        grid=(1,),
        in_specs=[whole(array.shape) for array in (near, far, out)],
        out_specs=[whole(shape) for shape in shapes],
        out_shape=[jax.ShapeDtypeStruct(shape, F32) for shape in shapes],
        cost_estimate=cost(0),
        name="unpack",
    )(near, far, out)


def swap_pair(array):
    count = lax.axis_size("state")
    return lax.ppermute(array, "state", [(pos, pos ^ 1) for pos in range(count)])


def swap_bit(array, bits):
    return lax.ppermute(array, "dp", [(pos, pos ^ bits) for pos in range(lax.axis_size("dp"))])


def swap_both(array, bits=0):
    states = lax.axis_size("state")
    pairs = []
    for d in range(lax.axis_size("dp")):
        for s in range(states):
            pairs.append((d * states + s, (((d & ~1) | s) ^ bits) * states + (d & 1)))
    return lax.ppermute(array, ("dp", "state"), pairs)


def add_mixed(x, mine, theirs):
    return (x.astype(F32) + (mine.astype(F32) + theirs.astype(F32))).astype(BF16)


def add_quarters(kept, got, start=0, stop=None):
    extent = kept.shape[0] // 4
    stop = extent if stop is None else stop
    return [
        kept[k * extent + start : k * extent + stop] + got[k * extent + start : k * extent + stop]
        for k in range(4)
    ]


def trade_quarters(quarters):
    return [quarters[0]] + [swap_bit(quarters[k], k * X_BIT) for k in range(1, 4)]


def sum_quarters(quarters):
    left, right = (quarters[k].astype(F32) + quarters[k + 1].astype(F32) for k in (0, 2))
    return (left + right).astype(BF16)


CORE_BIT, X_BIT, ZH_BIT = 1, 2, 8


def shards(
    tokens,
    cluster_len,
    norm_gain,
    in_weight,
    conv_weight,
    conv_bias,
    dtx_weight,
    dt_weight,
    dt_bias,
    bc_weight,
    a_log,
    skip_gain,
    out_weight,
    cotangent,
):
    micros, count, width = tokens.shape
    inner = out_weight.shape[0]
    taps = conv_weight.shape[0]
    ranks = dtx_weight.shape[1]
    chunks = inner // (2 * LANES)
    own = chunks * LANES
    rows = micros * count
    edge = LANES // 2
    span = LANES + 32
    dp_parts = lax.axis_size("dp")
    state_count = lax.axis_size("state")
    dp_pos = lax.axis_index("dp")
    state_pos = lax.axis_index("state")
    half = state_pos & 1
    fast = state_count == 2 and dp_parts == 2 * chunks == 16
    if fast:
        place = jnp.stack([half, dp_pos & 1, dp_pos >> 1, (dp_pos >> 1) & 3])
        bc_own, alog_own = bc_weight, a_log
        bc_other, alog_other = swap_pair(bc_weight), swap_pair(a_log)
    else:
        place = jnp.stack([half, 0, 0, 0])
        bc_all = lax.all_gather(bc_weight, "state", axis=1, tiled=True)
        alog_all = lax.all_gather(a_log, "state", axis=0, tiled=True)
        eighth = alog_all.shape[0] // 2
        bc_own, bc_other = (
            lax.dynamic_slice_in_dim(bc_all, which * eighth, eighth, 1)
            for which in (half, 1 - half)
        )
        alog_own, alog_other = (
            lax.dynamic_slice_in_dim(alog_all, which * eighth, eighth, 0)
            for which in (half, 1 - half)
        )
    place = place.astype(jnp.int32)
    eighth = alog_own.shape[0]
    states = 2 * eighth

    x = tokens.reshape(rows, width)
    cotan = cotangent.reshape(rows, width)
    w4 = in_weight.reshape(2, chunks, 2, LANES, width)
    wout3 = out_weight.reshape(chunks, 2, LANES, width)
    dtx, dt = dtx_weight.T, dt_weight.T
    bias = dt_bias.reshape(-1, LANES)
    skip = skip_gain.reshape(-1, LANES)

    normed, act_all, act, inner_own, conved, gate = project(
        place, cluster_len, x, norm_gain[None], w4, conv_weight, conv_bias.reshape(-1, LANES)
    )
    bc, rank, high, decay, sp, u, step, slope, h, dy, gated, dgate, keep, send = scan_forward(
        place,
        cluster_len,
        act_all,
        bc_own,
        bc_other,
        alog_own,
        alog_other,
        dtx,
        dt,
        bias,
        skip,
        act,
        gate,
        wout3,
        cotan,
        normed,
    )
    if fast:
        early = swap_bit(send, CORE_BIT)
    mixed_part, dn_gate = products(place, gated, dgate, wout3, w4)
    if fast:
        *quarters, mixed_part, dn_gate, sp = lax.optimization_barrier(
            (*add_quarters(keep, early), mixed_part, dn_gate, sp)
        )
        early_got = trade_quarters(quarters)
    mixed_other = swap_pair(mixed_part)
    code_own, sact, dpre, alog, back = scan_backward(
        place, micros, bc, decay, dt, act, sp, u, step, slope, dy, h
    )
    code_other = swap_pair(code_own)
    if fast:
        block = sum_quarters(early_got)
        out_keep, out_send, gate_sum = block[:edge], block[edge:LANES], block[LANES:]
        mixed = add_mixed(x, mixed_part, mixed_other)
        out_send, gate_sum, mixed, conved = lax.optimization_barrier(
            (out_send, gate_sum, mixed, conved)
        )
        out_got = swap_bit(out_send, ZH_BIT)
    late_keep, late_send, dnormed_part = tail(
        place,
        cluster_len,
        code_own,
        code_other,
        sact,
        dpre,
        alog,
        back,
        dtx,
        bc_own,
        bc_other,
        decay,
        dy,
        conved,
        inner_own,
        act,
        high,
        conv_weight,
        skip,
        normed,
        w4,
        dn_gate,
        x,
    )
    if fast:
        late = swap_bit(late_send, CORE_BIT)
        late_got = trade_quarters(add_quarters(late_keep, late))
    dnormed_other = swap_pair(dnormed_part)
    tokens_grad = finish(x, dnormed_part, dnormed_other, cotan, norm_gain[None])
    if not fast:
        mixed = add_mixed(x, mixed_part, mixed_other)
    if fast:
        out_own = swap_both(out_keep + out_got)
        *late_got, out_own, tokens_grad = lax.optimization_barrier(
            (*late_got, out_own, tokens_grad)
        )
        block = sum_quarters(late_got)
        inner_sum = block[:LANES]
        upper = dp_pos >= dp_parts // 2
        crossing = jnp.where(upper, inner_sum, gate_sum)
        first, second = crossing[:edge], crossing[edge:]
        first, pack_far, pack_near = lax.optimization_barrier(
            (first, block[-16:], block[LANES:-16])
        )
        pack_far = swap_both(pack_far, ZH_BIT)
        first_got = swap_bit(first, ZH_BIT)
        pack_near = swap_both(pack_near)
        first_got, pack_far, pack_near = lax.optimization_barrier((first_got, pack_far, pack_near))
        second_got = swap_bit(second, ZH_BIT)
        gain_mine = (
            pack_near[:, 5 * LANES : 6 * LANES].astype(F32)
            + pack_far[:, 5 * LANES : 6 * LANES].astype(F32)
        ).astype(BF16)
        gain_both = gain_mine[-1].astype(F32) + swap_bit(gain_mine, CORE_BIT)[-1].astype(F32)
        extent = width // (dp_parts * state_count)
        gain_grad = lax.dynamic_slice_in_dim(gain_both, (dp_pos & 1) * extent, extent, 0)
        (
            dtx_grad,
            dt_grad,
            bc_grad,
            alog_grad,
            convw_grad,
            convb_grad,
            bias_grad,
            skip_grad,
            out_own,
        ) = unpack(pack_near, pack_far, out_own, eighth, taps, ranks)
        convb_grad, bias_grad, skip_grad = (
            array[0] for array in (convb_grad, bias_grad, skip_grad)
        )
        in_grad = jnp.where(upper, gate_sum, inner_sum).astype(F32) + jnp.concatenate(
            [first_got, second_got]
        ).astype(F32)
    mixed = mixed.reshape(micros, count, width)
    tokens_grad = tokens_grad.reshape(micros, count, width)

    if not fast:
        def total(array):
            return lax.psum(array.astype(F32), "dp")

        def both_rows(array):
            mine = array.reshape(chunks, 1, LANES, -1)
            other = swap_pair(mine)
            low = jnp.where(half == 0, mine, other)
            high = jnp.where(half == 0, other, mine)
            return jnp.concatenate([low, high], axis=1).reshape(2 * own, -1)

        every = dp_parts * state_count
        at = dp_pos * state_count + state_pos

        def cut_own(array):
            extent = array.shape[0] // every
            return lax.dynamic_slice_in_dim(array, at * extent, extent, 0)

        pair = total(jnp.stack([keep, send])).reshape(2, 2, 2, 2 * LANES, width)
        outs = pair[:, :, :, :LANES].reshape(2, 2, 2, 2, edge, width)
        outs = jnp.transpose(outs, (3, 1, 2, 0, 4, 5)).reshape(own, width)
        gates = jnp.moveaxis(pair[:, :, :, LANES:], 0, 2).reshape(own, width)
        pair = total(jnp.stack([late_keep, late_send])).reshape(2, 2, 2, span, width)
        inners = jnp.moveaxis(pair[:, :, :, :LANES], 0, 2).reshape(own, width)
        packs = pair[:, :, :, LANES:].reshape(2, 2, 2, 2, 16, width // LANES, LANES)
        packs = jnp.transpose(packs, (3, 1, 2, 0, 5, 4, 6)).reshape(chunks, 2, -1, 16, LANES)
        small = both_rows(packs[:, :, :4].reshape(own, LANES))
        in_grad = cut_own(jnp.concatenate([both_rows(inners), both_rows(gates)]))
        out_own = cut_own(both_rows(outs))
        mine = cut_own(small)
        dtx_grad, dt_grad = mine[:, :ranks], mine[:, ranks:]
        vec_rows = jnp.swapaxes(packs[:, :, 5, eighth:, :edge], 2, 3).reshape(own, -1)
        gain_sum = vec_rows[:, -1].reshape(chunks, 2, 2, -1).swapaxes(1, 2).reshape(-1)
        gain_grad = cut_own(gain_sum + swap_pair(gain_sum))
        vec = cut_own(both_rows(vec_rows)).T
        state_rows = jnp.concatenate([packs[:, :, 4], packs[:, :, 5, :eighth]], axis=2)
        state_rows = state_rows.reshape(chunks, 2, 3, eighth, LANES)
        state_rows = jnp.transpose(state_rows, (0, 4, 2, 1, 3)).reshape(own, -1)
        extent = inner // dp_parts
        state_part = lax.dynamic_slice_in_dim(both_rows(state_rows), dp_pos * extent, extent, 0)
        state_part = state_part.T.reshape(3, state_count, -1, extent)
        state_part = lax.dynamic_index_in_dim(state_part, state_pos, 1, keepdims=False)
        bc_grad, alog_grad = state_part[:2], state_part[2]
        convw_grad, convb_grad, bias_grad, skip_grad = (
            vec[:taps], vec[taps], vec[taps + 1], vec[taps + 2]
        )

    return (
        mixed,
        tokens_grad,
        gain_grad,
        in_grad,
        convw_grad,
        convb_grad,
        dtx_grad,
        dt_grad,
        bias_grad,
        bc_grad,
        alog_grad,
        skip_grad,
        out_own,
    )


def solution(mesh):
    return jax.shard_map(
        shards,
        mesh=mesh,
        in_specs=(
            P(None, "dp", None),
            P(None, "dp", None),
            P(),
            P(),
            P(),
            P(),
            P(),
            P(),
            P(),
            P(None, "state", None),
            P("state", None),
            P(),
            P(),
            P(None, "dp", None),
        ),
        out_specs=(
            P(None, "dp", None),
            P(None, "dp", None),
            P(("dp", "state")),
            P(("dp", "state"), None),
            P(None, ("dp", "state")),
            P(("dp", "state")),
            P(("dp", "state"), None),
            P(("dp", "state"), None),
            P(("dp", "state")),
            P(None, "state", "dp"),
            P("state", "dp"),
            P(("dp", "state")),
            P(("dp", "state"), None),
        ),
        check_vma=False,
    )
```

```python
import functools
import math

import jax
import jax.numpy as jnp
from jax import lax
from jax.experimental import pallas as pl
from jax.experimental.pallas import tpu as pltpu
from jax.sharding import PartitionSpec as P

EPSILON = 1e-05
LANES = 128
RESET = 1e4
LOG2E = math.log2(math.e)
F32 = jnp.float32
BF16 = jnp.bfloat16
MIB = 1024 * 1024


def dot(left, right, left_dim, right_dim):
    return lax.dot_general(
        left, right, (((left_dim,), (right_dim,)), ((), ())), preferred_element_type=F32
    )


def params(mib):
    return pltpu.CompilerParams(
        vmem_limit_bytes=mib * MIB, dimension_semantics=("arbitrary",)
    )


ANY = pl.BlockSpec(memory_space=pl.ANY)


def stream(step, steps, fetch):
    @pl.when(step == 0)
    def _():
        for k in range(steps):
            for copy in fetch(k):
                copy.start()

    for copy in fetch(step):
        copy.wait()


def whole(shape):
    return pl.BlockSpec(shape, lambda *_: (0,) * len(shape))


sigmoid = jax.nn.sigmoid


def log_one_plus(value):
    series = value * (1.0 - value * (0.5 - value * (1.0 / 3.0)))
    return jnp.where(value < 1e-3, series, jnp.log(1.0 + value))


def lanes(index):
    return pl.ds(pl.multiple_of(index * LANES, LANES), LANES)


def cost(micros):
    return pl.CostEstimate(
        flops=int(micros * 1e9), bytes_accessed=int(micros * 1e6), transcendentals=0
    )


def hbm(shape, dtype):
    return pltpu.HBM(shape, dtype)


def in_hbm(arrays):
    return [pltpu.with_memory_space_constraint(array, pltpu.HBM) for array in arrays]


def aligned(start, size, to=8):
    return pl.ds(pl.multiple_of(start, to), size)


SEGMENTS = 4

HALF, CORE, CUBE, FACE = range(4)


def fill_masks(len_ref, mask_ref, micros, count, taps, clusters):
    place = lax.broadcasted_iota(jnp.int32, (count, LANES), 0)
    for micro in range(micros):
        rows = pl.ds(micro * count, count)
        for back in range(1, taps):
            apart = place < back
            start = 0
            for cluster in range(clusters - 1):
                start = start + len_ref[micro, 0, cluster]
                apart = apart | ((place >= start) & (place < start + back))
            mask_ref[back, rows, :] = jnp.where(apart, 0.0, 1.0)
            if back == 1:
                mask_ref[0, rows, :] = jnp.where(apart, 1.0, 0.0)


def project_kernel(
    place_ref,
    len_ref,
    gain_ref,
    convw_ref,
    convb_ref,
    x_far,
    weight_far,
    normed_far,
    act_far,
    own_act_far,
    inner_far,
    conved_far,
    gate_far,
    mask_ref,
    x_ref,
    win_ref,
    wgate_ref,
    normed_ref,
    act_ref,
    own_act_ref,
    inner_ref,
    conved_ref,
    gate_ref,
    in_sems,
    out_sems,
    *,
    micros,
    count,
    taps,
    clusters,
):
    half = place_ref[HALF]
    chunks = win_ref.shape[0]
    inward = [pltpu.make_async_copy(x_far, x_ref, in_sems.at[2 * chunks])]
    for k in range(chunks):
        inward.append(pltpu.make_async_copy(weight_far.at[0, k], win_ref.at[k], in_sems.at[2 * k]))
        inward.append(
            pltpu.make_async_copy(
                weight_far.at[1, k, half], wgate_ref.at[k], in_sems.at[2 * k + 1]
            )
        )
    for copy in inward:
        copy.start()
    outward = []

    def put(source, target):
        outward.append(pltpu.make_async_copy(source, target, out_sems.at[len(outward)]))
        outward[-1].start()

    fill_masks(len_ref, mask_ref, micros, count, taps, clusters)
    inward[0].wait()
    rows = x_ref[...].astype(F32)
    scale = lax.rsqrt(jnp.mean(rows * rows, axis=1, keepdims=True) + EPSILON)
    normed = (rows * scale * gain_ref[...]).astype(BF16)
    normed_ref[...] = normed
    put(normed_ref, normed_far)
    for k in range(chunks):
        inward[2 * k + 1].wait()
        inward[2 * k + 2].wait()
        proj = dot(normed, win_ref[k].reshape(2 * LANES, -1), 1, 1)
        own = slice(k * LANES, (k + 1) * LANES)
        gate_ref[:, own] = dot(normed, wgate_ref[k], 1, 1)
        inners, conveds, acts = [], [], []
        for part in range(2):
            cols = slice((2 * k + part) * LANES, (2 * k + part + 1) * LANES)
            inner = proj[:, part * LANES : (part + 1) * LANES]
            conved = convb_ref[2 * k + part : 2 * k + part + 1, :]
            conved = conved + convw_ref[taps - 1 : taps, cols] * inner
            for back in range(1, taps):
                shifted = pltpu.roll(inner, back, 0) * mask_ref[back]
                conved = conved + convw_ref[taps - 1 - back : taps - back, cols] * shifted
            act = conved * sigmoid(conved)
            act_ref[:, cols] = act.astype(BF16)
            inners.append(inner)
            conveds.append(conved)
            acts.append(act)
        inner_ref[:, own] = jnp.where(half == 0, *inners)
        conved_ref[:, own] = jnp.where(half == 0, *conveds)
        own_act_ref[:, own] = jnp.where(half == 0, *acts).astype(BF16)
        if k % 2:
            group = pl.ds((k - 1) * LANES, 2 * LANES)
            wide = pl.ds(2 * (k - 1) * LANES, 4 * LANES)
            put(act_ref.at[:, wide], act_far.at[:, wide])
            for near, far in (
                (gate_ref, gate_far),
                (inner_ref, inner_far),
                (conved_ref, conved_far),
                (own_act_ref, own_act_far),
            ):
                put(near.at[:, group], far.at[:, group])
    for copy in outward:
        copy.wait()


def project(place, lengths, x, gain, w4, conv_weight, conv_bias):
    rows, width = x.shape
    chunks = w4.shape[1]
    micros, _, clusters = lengths.shape
    taps = conv_weight.shape[0]
    own = chunks * LANES
    outs = [
        ((rows, width), BF16),
        ((rows, 2 * own), BF16),
        ((rows, own), BF16),
        ((rows, own), F32),
        ((rows, own), F32),
        ((rows, own), F32),
    ]
    return pl.pallas_call(
        functools.partial(
            project_kernel, micros=micros, count=rows // micros, taps=taps, clusters=clusters
        ),
        grid_spec=pltpu.PrefetchScalarGridSpec(
            num_scalar_prefetch=1,
            grid=(1,),
            in_specs=[
                pl.BlockSpec(memory_space=pltpu.SMEM),
                whole(gain.shape),
                whole(conv_weight.shape),
                whole(conv_bias.shape),
                ANY,
                ANY,
            ],
            out_specs=[ANY] * len(outs),
            scratch_shapes=[
                pltpu.VMEM((taps, rows, LANES), F32),
                pltpu.VMEM((rows, width), BF16),
                pltpu.VMEM((chunks, 2, LANES, width), BF16),
                pltpu.VMEM((chunks, LANES, width), BF16),
            ]
            + [pltpu.VMEM(*out) for out in outs]
            + [
                pltpu.SemaphoreType.DMA((2 * chunks + 1,)),
                pltpu.SemaphoreType.DMA((1 + 5 * chunks // 2,)),
            ],
        ),
        out_shape=[hbm(*out) for out in outs],
        compiler_params=params(30),
        cost_estimate=cost(6),
        name="project",
    )(place, *in_hbm((lengths, gain, conv_weight, conv_bias, x, w4)))


def every_row(ref, row, height):
    return ref[pl.ds(row, height, stride=0), :]


def b_at(n, eighth):
    return (n // eighth) * 2 * eighth + n % eighth


def c_at(n, eighth):
    return b_at(n, eighth) + eighth


def forward_kernel(
    place_ref,
    len_ref,
    act_all_ref,
    bc_own_ref,
    bc_other_ref,
    alog_own_ref,
    alog_other_ref,
    dtx_ref,
    dt_ref,
    bias_ref,
    skip_ref,
    act_ref,
    *refs,
    micros,
    count,
    states,
    chunks,
    clusters,
):
    gate_far, wout_far, cotan_far, normed_far = refs[:4]
    bc_ref, rank_ref, rank_high_ref, decay_ref = refs[4:8]
    sp_far, u_far, step_far, slope_far, h_far, dy_far = refs[8:14]
    gated_far, dgate_far, keep_far, send_far = refs[14:18]
    mask_ref, y_ref, tmp_ref, wide_ref = refs[18:22]
    gate_ref, wout_ref, cotan_ref, normed_ref = refs[22:26]
    sp_ref, u_ref, step_ref, slope_ref, h_ref, dy_ref = refs[26:32]
    gated_ref, dgate_ref, keep_ref, send_ref = refs[32:36]
    in_sems, out_sems = refs[36:]
    rows = micros * count
    eighth = states // 2
    half, core, cube, face = (place_ref[k] for k in range(4))
    first = half == 0
    inward = [
        pltpu.make_async_copy(source, target, in_sems.at[k])
        for k, (source, target) in enumerate(
            (
                (gate_far, gate_ref),
                (wout_far.at[:, half], wout_ref),
                (cotan_far, cotan_ref),
                (normed_far, normed_ref),
            )
        )
    ]
    for copy in inward:
        copy.start()
    outward = []

    def put(source, target):
        outward.append(pltpu.make_async_copy(source, target, out_sems.at[len(outward)]))
        outward[-1].start()

    act_all = act_all_ref[...]
    own = dot(act_all, bc_own_ref[...].reshape(states, -1), 1, 1)
    other = dot(act_all, bc_other_ref[...].reshape(states, -1), 1, 1)
    bc_ref[:, :states] = jnp.where(first, own, other)
    bc_ref[:, states:] = jnp.where(first, other, own)
    spread_lanes(bc_ref, wide_ref)

    fill_masks(len_ref, mask_ref, micros, count, 2, clusters)
    for chunk in range(chunks):
        cols = lanes(2 * chunk + half)
        own, other = alog_own_ref[:, cols], alog_other_ref[:, cols]
        tmp_ref[pl.ds(chunk * states, eighth), :] = jnp.where(first, own, other)
        tmp_ref[pl.ds(chunk * states + eighth, eighth), :] = jnp.where(first, other, own)
    for n in range(states):
        decay_ref[pl.ds(n * chunks, chunks), :] = -LOG2E * jnp.exp(
            tmp_ref[pl.ds(n, chunks, stride=states), :]
        )

    rank = dot(act_all, dtx_ref[...], 1, 1).astype(BF16)
    rank_ref[...] = rank
    rank_high_ref[...] = jnp.concatenate([jnp.zeros_like(rank), rank], axis=1)
    for chunk in range(chunks):
        cols = slice(chunk * LANES, (chunk + 1) * LANES)
        bias = bias_ref[pl.ds(2 * chunk + half, 1), :]
        pre = dot(rank, dt_ref[:, lanes(2 * chunk + half)], 1, 0) + bias
        tail_part = jnp.exp(-jnp.abs(pre))
        step = jnp.maximum(pre, 0.0) + log_one_plus(tail_part)
        slope = jnp.where(pre >= 0.0, 1.0, tail_part) / (1.0 + tail_part)
        step_ref[:, cols] = step
        slope_ref[:, cols] = slope.astype(BF16)
        held = step + RESET * mask_ref[0]
        source = step * act_ref[:, cols].astype(F32)
        for micro in range(micros):
            span = slice(micro * count, (micro + 1) * count)
            place = pl.ds((micro * chunks + chunk) * count, count)
            sp_ref[place, :] = held[span]
            u_ref[place, :] = source[span]
    put(sp_ref, sp_far)
    put(u_ref, u_far)
    put(step_ref, step_far)
    put(slope_ref, slope_far)

    for micro in range(micros):

        def advance(t, h, micro=micro):
            row = micro * count + t
            span = pl.ds(micro * chunks * count + t, chunks, stride=count)
            sp = sp_ref[span, :]
            u = u_ref[span, :]
            out = []
            y = None
            for n in range(states):
                decay = jnp.exp2(sp * decay_ref[pl.ds(n * chunks, chunks), :])
                now = decay * h[n] + u * every_row(wide_ref, b_at(n, eighth) * rows + row, chunks)
                h_ref[aligned((row * states + n) * chunks, chunks), :] = now
                out.append(now)
                term = now * every_row(wide_ref, c_at(n, eighth) * rows + row, chunks)
                y = term if y is None else y + term
            y_ref[span, :] = y
            return tuple(out)

        h = (jnp.zeros((chunks, LANES), F32),) * states
        segment = count // SEGMENTS
        for k in range(SEGMENTS):
            h = lax.fori_loop(k * segment, (k + 1) * segment, advance, h, unroll=4)
            extent = segment * states * chunks
            place = pl.ds((micro * SEGMENTS + k) * extent, extent)
            put(h_ref.at[place], h_far.at[place])

    for copy in inward:
        copy.wait()
    cotan = cotan_ref[...]
    for chunk in range(chunks):
        cols = slice(chunk * LANES, (chunk + 1) * LANES)
        places = [pl.ds((micro * chunks + chunk) * count, count) for micro in range(micros)]
        y = jnp.concatenate([y_ref[place, :] for place in places])
        y = y + skip_ref[pl.ds(2 * chunk + half, 1), :] * act_ref[:, cols].astype(F32)
        gate = gate_ref[:, cols]
        sig = sigmoid(gate)
        gated_ref[:, cols] = (y * (gate * sig)).astype(BF16)
        dgated = dot(cotan, wout_ref[chunk], 1, 1)
        dy = dgated * (gate * sig)
        for micro in range(micros):
            dy_ref[places[micro], :] = dy[micro * count : (micro + 1) * count]
        dgate_ref[:, cols] = (dgated * y * (sig * (1.0 + gate * (1.0 - sig)))).astype(BF16)
    put(dy_ref, dy_far)
    put(gated_ref, gated_far)
    put(dgate_ref, dgate_far)
    normed = normed_ref[...]
    edge = LANES // 2
    for r in range(chunks // 2):
        for zh in range(2):
            grad = dot(gated_ref[:, lanes((r + 4 * zh) ^ cube)], cotan, 0, 0).astype(BF16)
            top, bottom = grad[:edge], grad[edge:]
            place = pl.ds(r * 2 * LANES + zh * edge, edge)
            keep_ref[place, :] = jnp.where(core == 0, top, bottom)
            send_ref[place, :] = jnp.where(core == 0, bottom, top)
        place = pl.ds((2 * r + 1) * LANES, LANES)
        pair = 2 * (r ^ face)
        for chunk, out_ref in ((pair + core, keep_ref), (pair + 1 - core, send_ref)):
            out_ref[place, :] = dot(dgate_ref[:, lanes(chunk)], normed, 0, 0).astype(BF16)
        place = pl.ds(r * 2 * LANES, 2 * LANES)
        put(send_ref.at[place], send_far.at[place])
        put(keep_ref.at[place], keep_far.at[place])
    for copy in outward:
        copy.wait()


def scan_forward(
    place,
    lengths,
    act_all,
    bc_own,
    bc_other,
    alog_own,
    alog_other,
    dtx,
    dt,
    bias,
    skip,
    act,
    gate,
    wout3,
    cotan,
    normed,
):
    rows, own = act.shape
    chunks = own // LANES
    states = 2 * alog_own.shape[0]
    width = cotan.shape[1]
    micros, _, clusters = lengths.shape
    ranks = dtx.shape[0]
    small = [
        ((rows, 2 * states), F32),
        ((rows, ranks), BF16),
        ((rows, 2 * ranks), BF16),
        ((states * chunks, LANES), F32),
    ]
    large = [
        ((chunks * rows, LANES), F32),
        ((chunks * rows, LANES), F32),
        ((rows, own), F32),
        ((rows, own), BF16),
        ((rows * states * chunks, LANES), F32),
        ((chunks * rows, LANES), F32),
        ((rows, own), BF16),
        ((rows, own), BF16),
        ((own, width), BF16),
        ((own, width), BF16),
    ]
    operands = (act_all, bc_own, bc_other, alog_own, alog_other, dtx, dt, bias, skip, act)
    streamed = (gate, wout3, cotan, normed)
    return pl.pallas_call(
        functools.partial(
            forward_kernel,
            micros=micros,
            count=rows // micros,
            states=states,
            chunks=chunks,
            clusters=clusters,
        ),
        grid_spec=pltpu.PrefetchScalarGridSpec(
            num_scalar_prefetch=1,
            grid=(1,),
            in_specs=[pl.BlockSpec(memory_space=pltpu.SMEM)]
            + [whole(operand.shape) for operand in operands]
            + [ANY] * len(streamed),
            out_specs=[whole(shape) for shape, _ in small] + [ANY] * len(large),
            scratch_shapes=[
                pltpu.VMEM((2, rows, LANES), F32),
                pltpu.VMEM((chunks * rows, LANES), F32),
                pltpu.VMEM((states * chunks, LANES), F32),
                pltpu.VMEM((2 * states * rows, LANES), F32),
                pltpu.VMEM((rows, own), F32),
                pltpu.VMEM((chunks, LANES, width), BF16),
                pltpu.VMEM((rows, width), BF16),
                pltpu.VMEM((rows, width), BF16),
            ]
            + [pltpu.VMEM(*out) for out in large]
            + [pltpu.SemaphoreType.DMA((4,)), pltpu.SemaphoreType.DMA((7 + chunks + micros * SEGMENTS,))],
        ),
        out_shape=[hbm(*out) for out in small + large],
        compiler_params=params(52),
        cost_estimate=cost(19),
        name="scan_forward",
    )(
        place,
        lengths,
        *in_hbm(operands[:1]),
        *operands[1:5],
        *in_hbm((*operands[5:], *streamed)),
    )


def spread_lanes(values_ref, wide_ref):
    rows, count = values_ref.shape
    for k in range(count):
        wide_ref[pl.ds(k * rows, rows), :] = jnp.broadcast_to(
            values_ref[:, k : k + 1], (rows, LANES)
        )


def backward_kernel(
    place_ref,
    bc_ref,
    decay_ref,
    dt_ref,
    act_ref,
    sp_ref,
    u_ref,
    step_ref,
    slope_ref,
    dy_ref,
    h_far,
    code_ref,
    sact_ref,
    dpre_ref,
    alog_ref,
    vec_ref,
    h_ref,
    s_ref,
    d_ref,
    terms_ref,
    sums_b_ref,
    sums_c_ref,
    wide_ref,
    sems,
    *,
    count,
    states,
    chunks,
):
    micro = pl.program_id(0)
    block = states * chunks
    segment = count // SEGMENTS

    def fetch(which, k):
        extent = segment * block
        buffer = h_ref.at[which % 2]
        return pltpu.make_async_copy(
            h_far.at[aligned((which * SEGMENTS + k) * extent, extent)],
            buffer.at[pl.ds(block + k * extent, extent)],
            sems.at[which % 2, k],
        )

    @pl.when(micro == 0)
    def _():
        for k in reversed(range(SEGMENTS)):
            fetch(0, k).start()
        for which in range(2):
            h_ref[which, pl.ds(0, block), :] = jnp.zeros((block, LANES), F32)
        alog_ref[...] = jnp.zeros_like(alog_ref)
        vec_ref[...] = jnp.zeros_like(vec_ref)

    half = place_ref[HALF]
    eighth = states // 2
    zero = (jnp.zeros((chunks, LANES), F32),) * states
    spread_lanes(bc_ref, wide_ref)

    @pl.when(micro + 1 < pl.num_programs(0))
    def _():
        for k in reversed(range(SEGMENTS)):
            fetch(micro + 1, k).start()

    side = micro % 2

    def put_terms(which, t, values, factor):
        factor = jnp.concatenate([factor, factor]).astype(BF16)
        for n in range(0, states, 2):
            pair = jnp.concatenate(values[n : n + 2]).astype(BF16) * factor
            place = aligned(t * block + n * chunks, 2 * chunks, 16)
            terms_ref[which, place, :] = pair

    def retreat(back, carry):
        flows, totals = carry
        for slot in range(2):
            t = count - 1 - (2 * back + slot)
            span = pl.ds(t, chunks, stride=count)
            sp = sp_ref[span, :]
            u = u_ref[span, :]
            dy = dy_ref[span, :]
            out_flows = []
            out_totals = []
            b_values, c_values = [], []
            d_sum = None
            s_sum = None
            for n in range(states):
                rate = decay_ref[pl.ds(n * chunks, chunks), :]
                dh = flows[n] + dy * every_row(wide_ref, c_at(n, eighth) * count + t, chunks)
                flow = jnp.exp2(sp * rate) * dh
                out_flows.append(flow)
                q = flow * h_ref[side, aligned(t * block + n * chunks, chunks), :]
                now = h_ref[side, aligned((t + 1) * block + n * chunks, chunks), :]
                out_totals.append(totals[n] + q * sp)
                d_term = q * rate
                s_term = dh * every_row(wide_ref, b_at(n, eighth) * count + t, chunks)
                d_sum = d_term if d_sum is None else d_sum + d_term
                s_sum = s_term if s_sum is None else s_sum + s_term
                b_values.append(dh)
                c_values.append(now)
            s_ref[span, :] = s_sum
            d_ref[span, :] = d_sum
            put_terms(0, t, b_values, u)
            put_terms(1, t, c_values, dy)
            flows, totals = tuple(out_flows), tuple(out_totals)
        return flows, totals

    carry = (zero, zero)
    for k in range(SEGMENTS):
        fetch(micro, SEGMENTS - 1 - k).wait()
        carry = lax.fori_loop(k * segment // 2, (k + 1) * segment // 2, retreat, carry)
    totals = carry[1]
    for n in range(states):
        alog_ref[pl.ds(n * chunks, chunks), :] += totals[n]

    shape = (2 * states, 2 * block)
    group = lax.broadcasted_iota(jnp.int32, shape, 1) // chunks
    gather = jnp.where(group == lax.broadcasted_iota(jnp.int32, shape, 0), 1.0, 0.0).astype(BF16)

    @pl.loop(0, count // 16)
    def _(step):
        for which, sums_ref in ((0, sums_b_ref), (1, sums_c_ref)):
            for k in range(8):
                at = 8 * step + k
                terms = terms_ref[which, aligned(at * 2 * block, 2 * block, 16), :]
                sums_ref[aligned(at * 2 * states, 2 * states), :] = dot(gather, terms, 1, 0)

    ranks = dt_ref.shape[0]
    drank = None
    for chunk in range(chunks):
        cols = slice(chunk * LANES, (chunk + 1) * LANES)
        place = pl.ds(chunk * count, count)
        act = act_ref[:, cols].astype(F32)
        weight = dt_ref[:, lanes(2 * chunk + half)]
        s_now = s_ref[place, :]
        dstep = d_ref[place, :] * (1.0 / LOG2E) + s_now * act
        sact_ref[:, cols] = s_now * step_ref[:, cols]
        dpre = dstep * slope_ref[:, cols].astype(F32)
        vec_ref[0:1, cols] += jnp.sum(dpre, axis=0, keepdims=True)
        vec_ref[1:2, cols] += jnp.sum(dy_ref[place, :] * act, axis=0, keepdims=True)
        low = dpre.astype(BF16)
        dpre_ref[:, cols] = low
        term = dot(low, weight, 1, 1)
        drank = term if drank is None else drank + term
    source = lax.broadcasted_iota(jnp.int32, (2 * LANES, LANES), 0)
    target = lax.broadcasted_iota(jnp.int32, (2 * LANES, LANES), 1)
    code = None
    for n in range(states):
        pair = jnp.concatenate(
            [ref[pl.ds(n, count, stride=states), :] for ref in (sums_b_ref, sums_c_ref)], axis=1
        )
        column = ranks + jnp.where(source < LANES, b_at(n, eighth), c_at(n, eighth))
        pick = jnp.where(target == column, 1.0, 0.0).astype(BF16)
        term = dot(pair.astype(BF16), pick, 1, 0)
        code = term if code is None else code + term
    drank = jnp.concatenate([drank, jnp.zeros((count, LANES - ranks), F32)], axis=1)
    code_ref[...] = (code + drank).astype(BF16)


def scan_backward(place, micros, bc, decay, dt, act, sp, u, step, slope, dy, h):
    rows, own = act.shape
    count = rows // micros
    chunks = own // LANES
    states = bc.shape[1] // 2
    outs = [
        ((rows, LANES), BF16),
        ((rows, own), F32),
        ((rows, own), BF16),
        ((states * chunks, LANES), F32),
        ((2, own), F32),
    ]

    def block(*shape):
        return pl.BlockSpec(shape, lambda i, p: (i, 0))

    return pl.pallas_call(
        functools.partial(backward_kernel, count=count, states=states, chunks=chunks),
        grid_spec=pltpu.PrefetchScalarGridSpec(
            num_scalar_prefetch=1,
            grid=(micros,),
            in_specs=[
                block(count, 2 * states),
                whole(decay.shape),
                whole(dt.shape),
                block(count, own),
                block(chunks * count, LANES),
                block(chunks * count, LANES),
                block(count, own),
                block(count, own),
                block(chunks * count, LANES),
                ANY,
            ],
            out_specs=[block(count, LANES), block(count, own), block(count, own)]
            + [whole(shape) for shape, _ in outs[3:]],
            scratch_shapes=[
                pltpu.VMEM((2, (count + 1) * states * chunks, LANES), F32),
                pltpu.VMEM((chunks * count, LANES), F32),
                pltpu.VMEM((chunks * count, LANES), F32),
                pltpu.VMEM((2, count * states * chunks, LANES), BF16),
                pltpu.VMEM((count * states, LANES), F32),
                pltpu.VMEM((count * states, LANES), F32),
                pltpu.VMEM((2 * states * count, LANES), F32),
                pltpu.SemaphoreType.DMA((2, SEGMENTS)),
            ],
        ),
        out_shape=[hbm(*out) for out in outs],
        compiler_params=params(52),
        cost_estimate=cost(0),
        name="scan_backward",
    )(place, *in_hbm((bc, decay, dt, act, sp, u, step, slope, dy, h)))


def tail_kernel(
    place_ref,
    len_ref,
    *refs,
    micros,
    count,
    taps,
    clusters,
    ranks,
    chunks,
    states,
):
    def take(number):
        nonlocal refs
        taken, refs = refs[:number], refs[number:]
        return taken

    code_own_ref, code_other_ref = take(2)
    sact_ref, dpre_ref, alog_sum_ref, back_ref = take(4)
    dtx_ref, bc_own_ref, bc_other_ref, decay_ref = take(4)
    dy_refs = take(micros)
    conved_ref, inner_ref, act_ref, high_ref, convw_ref, skip_ref = take(6)
    normed_ref, weight_ref, gate_part_ref, x_ref = take(4)
    keep_ref, send_ref, dnormed_ref = take(3)
    mask_ref, code_ref, wcode_ref, vec_ref, alog_ref, total_ref, win_ref, sems, low_ref = refs

    step = pl.program_id(0)
    rows = micros * count
    eighth = states // 2
    edge = LANES // 2
    half, core, cube, face = (place_ref[k] for k in range(4))
    pair = step ^ face
    span = LANES + 32

    def fetch(k):
        source = weight_ref.at[0, pl.ds(2 * (k ^ face), 2), half]
        return (pltpu.make_async_copy(source, win_ref.at[k], sems.at[k]),)

    stream(step, win_ref.shape[0], fetch)

    def pack_row(chunk):
        relative = chunk ^ cube
        return (relative & 3) * span + LANES + (relative >> 2) * 16

    def place_pair(start, size, cols, even, odd):
        keep_ref[aligned(start, size, 16), cols] = jnp.where(core == 0, even, odd).astype(BF16)
        send_ref[aligned(start, size, 16), cols] = jnp.where(core == 0, odd, even).astype(BF16)

    @pl.when(step == 0)
    def _():
        fill_masks(len_ref, mask_ref, micros, count, taps, clusters)
        total_ref[...] = gate_part_ref[...].astype(F32)
        code_ref[...] = (
            code_own_ref[...].astype(F32) + code_other_ref[...].astype(F32)
        ).astype(BF16)
        alog_ref[...] = alog_sum_ref[...] * (decay_ref[...] * (1.0 / LOG2E))

    code = code_ref[...]
    lane = lax.broadcasted_iota(jnp.int32, (1, LANES), 1)
    code_rank = jnp.where(lane < ranks, code, jnp.zeros_like(code))
    dpre = dpre_ref[...]
    for part in range(2):
        source = lanes(2 * (2 * pair + part) + half)
        cols = slice(part * LANES, (part + 1) * LANES)
        wcode_ref[:ranks, cols] = dtx_ref[:, source]
        own = bc_own_ref[:, :, source].reshape(states, LANES)
        other = bc_other_ref[:, :, source].reshape(states, LANES)
        wcode_ref[ranks : ranks + states, cols] = jnp.where(half == 0, own, other)
        wcode_ref[ranks + states : ranks + 2 * states, cols] = jnp.where(half == 0, other, own)
        wcode_ref[ranks + 2 * states :, cols] = jnp.zeros(
            (LANES - ranks - 2 * states, LANES), BF16
        )
    for part in range(2):
        cols = slice(part * LANES, (part + 1) * LANES)
        chunk = 2 * pair + part
        source = 2 * chunk + half
        weights = convw_ref[:, lanes(source)]
        sact = sact_ref[:, cols]
        dy = jnp.concatenate([ref[pl.ds(part * count, count), :] for ref in dy_refs], axis=0)
        dact = sact + dot(code, wcode_ref[:, cols], 1, 0)
        dact = dact + dy * skip_ref[pl.ds(source, 1), :]
        conved = conved_ref[:, cols]
        sig = sigmoid(conved)
        dconv = dact * (sig * (1.0 + conved * (1.0 - sig)))
        inner = inner_ref[:, cols]
        dinner = weights[taps - 1 : taps] * dconv
        sums = [None] * (taps + 1)
        sums[taps - 1] = jnp.sum(dconv * inner, axis=0, keepdims=True)
        sums[taps] = jnp.sum(dconv, axis=0, keepdims=True)
        for back in range(1, taps):
            kept = dconv * mask_ref[back]
            dinner = dinner + weights[taps - 1 - back : taps - back] * pltpu.roll(
                kept, rows - back, 0
            )
            sums[taps - 1 - back] = jnp.sum(
                kept * pltpu.roll(inner, back, 0), axis=0, keepdims=True
            )
        for k in range(taps + 1):
            vec_ref[k : k + 1, lanes(chunk)] = sums[k]
        vec_ref[taps + 1 : taps + 3, lanes(chunk)] = back_ref[:, lanes(chunk)]
        low_ref[:, cols] = dinner.astype(BF16)

        act = act_ref[:, cols]
        start = pack_row(chunk)
        rows_now = dot(act, code_rank, 0, 0) + dot(dpre[:, cols], high_ref[...], 0, 0)
        for k in range(4):
            place_pair(
                start,
                16,
                slice(k * LANES, (k + 1) * LANES),
                rows_now[k * 16 : (k + 1) * 16],
                rows_now[edge + k * 16 : edge + (k + 1) * 16],
            )
        state_rows = dot(code, act, 0, 0)[ranks : ranks + 2 * states]
        place_pair(
            start, 16, slice(4 * LANES, 5 * LANES), state_rows[:states], state_rows[states:]
        )

    normed = normed_ref[...]
    for part in range(2):
        grad = dot(low_ref[:, lanes(core ^ part)], normed, 0, 0)
        out_ref = (keep_ref, send_ref)[part]
        out_ref[aligned(step * span, LANES, 16), :] = grad.astype(BF16)
    width = total_ref.shape[1]
    total_ref[...] += dot(low_ref[...], win_ref[step].reshape(2 * LANES, width), 1, 0)

    @pl.when(step == pl.num_programs(0) - 1)
    def _():
        total = total_ref[...]
        dnormed_ref[...] = total.astype(BF16)
        x = x_ref[...].astype(F32)
        unit = x * lax.rsqrt(jnp.mean(x * x, axis=1, keepdims=True) + EPSILON)
        vec_ref[taps + 3 : taps + 4, :] = jnp.sum(total * unit, axis=0, keepdims=True)
        is_gain = lax.broadcasted_iota(jnp.int32, (8, LANES), 0) == taps + 3
        for chunk in range(chunks):
            start = pack_row(chunk)
            vec = vec_ref[:, chunk * LANES : (chunk + 1) * LANES]
            far, farther = (pltpu.roll(vec, LANES - k * edge // 2, 1) for k in (1, 2))
            even = jnp.where(is_gain & (lane >= edge // 2), far, vec)
            odd = jnp.where(is_gain & (lane < edge // 2), far, farther)
            alog = [
                alog_ref[pl.ds(q * eighth * chunks + chunk, eighth, stride=chunks), :]
                for q in range(2)
            ]
            place_pair(
                start,
                16,
                slice(5 * LANES, 6 * LANES),
                jnp.concatenate([alog[0], even]),
                jnp.concatenate([alog[1], odd]),
            )
            blank = jnp.zeros((16, 2 * LANES), F32)
            place_pair(start, 16, slice(6 * LANES, 8 * LANES), blank, blank)


def tail(
    place,
    lengths,
    code_own,
    code_other,
    sact,
    dpre,
    alog,
    back,
    dtx,
    bc_own,
    bc_other,
    decay,
    dy,
    conved,
    inner,
    act,
    high,
    convw,
    skip,
    normed,
    w4,
    gate_part,
    x,
):
    rows, own = act.shape
    chunks = own // LANES
    width = normed.shape[1]
    micros, _, clusters = lengths.shape
    count = rows // micros
    taps = convw.shape[0]
    ranks = dtx.shape[0]
    states = decay.shape[0] // chunks
    cols = 2 * LANES
    extent = 4 * (LANES + 32)

    def by_cols(height):
        return pl.BlockSpec((height, cols), lambda i, p: (0, i ^ p[FACE]))

    def dy_spec(micro):
        return pl.BlockSpec(
            (2 * count, LANES), lambda i, p: (micro * (chunks // 2) + (i ^ p[FACE]), 0)
        )

    in_specs = (
        [pl.BlockSpec(memory_space=pltpu.SMEM)]
        + [whole((rows, LANES))] * 2
        + [by_cols(rows)] * 2
        + [whole(alog.shape), whole(back.shape)]
        + [whole(array.shape) for array in (dtx, bc_own, bc_other, decay)]
        + [dy_spec(micro) for micro in range(micros)]
        + [by_cols(rows)] * 3
        + [whole(array.shape) for array in (high, convw, skip, normed)]
        + [
            ANY,
            whole((rows, width)),
            whole((rows, width)),
        ]
    )
    return pl.pallas_call(
        functools.partial(
            tail_kernel,
            micros=micros,
            count=count,
            taps=taps,
            clusters=clusters,
            ranks=ranks,
            chunks=chunks,
            states=states,
        ),
        grid_spec=pltpu.PrefetchScalarGridSpec(
            num_scalar_prefetch=1,
            grid=(chunks // 2,),
            in_specs=in_specs,
            out_specs=[whole((extent, width)), whole((extent, width)), whole((rows, width))],
            scratch_shapes=[
                pltpu.VMEM((taps, rows, LANES), F32),
                pltpu.VMEM((rows, LANES), BF16),
                pltpu.VMEM((LANES, cols), BF16),
                pltpu.VMEM((8, own), F32),
                pltpu.VMEM((states * chunks, LANES), F32),
                pltpu.VMEM((rows, width), F32),
                pltpu.VMEM((chunks // 2, 2, LANES, width), BF16),
                pltpu.SemaphoreType.DMA((chunks // 2,)),
                pltpu.VMEM((rows, cols), BF16),
            ],
        ),
        out_shape=[
            hbm((extent, width), BF16),
            hbm((extent, width), BF16),
            hbm((rows, width), BF16),
        ],
        compiler_params=params(34),
        cost_estimate=cost(7),
        name="tail",
    )(
        place,
        lengths,
        *in_hbm([code_own]),
        code_other,
        *in_hbm(
            (
                sact,
                dpre,
                alog,
                back,
                dtx,
                bc_own,
                bc_other,
                decay,
                *([dy] * micros),
                conved,
                inner,
                act,
                high,
                convw,
                skip,
                normed,
                w4,
                gate_part,
                x,
            )
        ),
    )


def fetch_halves(source, which, half, target_ref, sems):
    copies = []
    for k in range(target_ref.shape[0]):
        pair = pl.ds(2 * k, 2)
        block = source.at[pair, half] if which is None else source.at[which, pair, half]
        copies.append(pltpu.make_async_copy(block, target_ref.at[k], sems.at[k]))
    for copy in copies:
        copy.start()
    return copies


def products_kernel(
    place_ref,
    gated_ref,
    dgate_ref,
    out_ref,
    weight_ref,
    mixed_ref,
    dnormed_ref,
    wout_ref,
    wgate_ref,
    out_sems,
    gate_sems,
):
    half = place_ref[HALF]
    width = mixed_ref.shape[1]
    jobs = (
        (fetch_halves(out_ref, None, half, wout_ref, out_sems), gated_ref, wout_ref, mixed_ref),
        (fetch_halves(weight_ref, 1, half, wgate_ref, gate_sems), dgate_ref, wgate_ref, dnormed_ref),
    )
    for copies, left_ref, right_ref, result_ref in jobs:
        total = None
        for k, copy in enumerate(copies):
            copy.wait()
            left = left_ref[:, 2 * k * LANES : 2 * (k + 1) * LANES]
            term = dot(left, right_ref[k].reshape(-1, width), 1, 0)
            total = term if total is None else total + term
        result_ref[...] = total.astype(BF16)


def products(place, gated, dgate, wout3, w4):
    rows, own = gated.shape
    width = w4.shape[-1]
    pairs = own // (2 * LANES)
    return pl.pallas_call(
        products_kernel,
        grid_spec=pltpu.PrefetchScalarGridSpec(
            num_scalar_prefetch=1,
            grid=(1,),
            in_specs=[whole((rows, own)), whole((rows, own)), ANY, ANY],
            out_specs=[whole((rows, width))] * 2,
            scratch_shapes=[
                pltpu.VMEM((pairs, 2, LANES, width), BF16),
                pltpu.VMEM((pairs, 2, LANES, width), BF16),
                pltpu.SemaphoreType.DMA((pairs,)),
                pltpu.SemaphoreType.DMA((pairs,)),
            ],
        ),
        out_shape=[hbm((rows, width), BF16)] * 2,
        compiler_params=params(20),
        cost_estimate=cost(4),
        name="products",
    )(place, *in_hbm((gated, dgate, wout3, w4)))


def finish_kernel(x_ref, mine_ref, theirs_ref, cotan_ref, gain_ref, grad_ref):
    x = x_ref[...].astype(F32)
    scale = lax.rsqrt(jnp.mean(x * x, axis=1, keepdims=True) + EPSILON)
    unit = x * scale
    dhat = (mine_ref[...].astype(F32) + theirs_ref[...].astype(F32)) * gain_ref[...]
    grad_ref[...] = cotan_ref[...].astype(F32) + scale * (
        dhat - unit * jnp.mean(dhat * unit, axis=1, keepdims=True)
    )


def finish(x, mine, theirs, cotan, gain):
    rows, width = x.shape
    by_rows = pl.BlockSpec((rows // 4, width), lambda i: (i, 0))
    return pl.pallas_call(
        finish_kernel,
        grid=(4,),
        in_specs=[by_rows] * 4 + [whole(gain.shape)],
        out_specs=by_rows,
        out_shape=jax.ShapeDtypeStruct((rows, width), F32),
        compiler_params=params(16),
        cost_estimate=cost(0),
        name="finish",
    )(*in_hbm((x, mine)), theirs, *in_hbm((cotan, gain)))


def unpack_kernel(
    near_ref,
    far_ref,
    out_ref,
    dtx_ref,
    dt_ref,
    bc_ref,
    alog_ref,
    convw_ref,
    convb_ref,
    bias_ref,
    skip_ref,
    out_grad_ref,
    *,
    eighth,
    taps,
    edge,
):
    pack = near_ref[...].astype(F32) + far_ref[...].astype(F32)
    for k in range(4):
        rows = pack[:, k * LANES : (k + 1) * LANES]
        dtx_ref[pl.ds(16 * k, 16), :] = rows[:, :edge]
        dt_ref[pl.ds(16 * k, 16), :] = pltpu.roll(rows, edge, 1)[:, :edge]
    rows = pack[:, 4 * LANES : 5 * LANES]
    bc_ref[0] = rows[:eighth]
    bc_ref[1] = rows[eighth:]
    rows = pack[:, 5 * LANES : 6 * LANES]
    alog_ref[...] = rows[:eighth]
    vec = rows[eighth:, :edge]
    convw_ref[...] = vec[:taps]
    convb_ref[...] = vec[taps : taps + 1]
    bias_ref[...] = vec[taps + 1 : taps + 2]
    skip_ref[...] = vec[taps + 2 : taps + 3]
    out_grad_ref[...] = out_ref[...].astype(F32)


def unpack(near, far, out, eighth, taps, ranks):
    edge = LANES // 2
    shapes = [
        (edge, ranks),
        (edge, ranks),
        (2, eighth, LANES),
        (eighth, LANES),
        (taps, edge),
        (1, edge),
        (1, edge),
        (1, edge),
        out.shape,
    ]
    return pl.pallas_call(
        functools.partial(unpack_kernel, eighth=eighth, taps=taps, edge=edge),
        grid=(1,),
        in_specs=[whole(array.shape) for array in (near, far, out)],
        out_specs=[whole(shape) for shape in shapes],
        out_shape=[jax.ShapeDtypeStruct(shape, F32) for shape in shapes],
        cost_estimate=cost(0),
        name="unpack",
    )(near, far, out)


def swap_pair(array):
    count = lax.axis_size("state")
    return lax.ppermute(array, "state", [(pos, pos ^ 1) for pos in range(count)])


def swap_bit(array, bits):
    return lax.ppermute(array, "dp", [(pos, pos ^ bits) for pos in range(lax.axis_size("dp"))])


def swap_both(array, bits=0):
    states = lax.axis_size("state")
    pairs = []
    for d in range(lax.axis_size("dp")):
        for s in range(states):
            pairs.append((d * states + s, (((d & ~1) | s) ^ bits) * states + (d & 1)))
    return lax.ppermute(array, ("dp", "state"), pairs)


def add_mixed(x, mine, theirs):
    return (x.astype(F32) + (mine.astype(F32) + theirs.astype(F32))).astype(BF16)


def add_quarters(kept, got, start=0, stop=None):
    extent = kept.shape[0] // 4
    stop = extent if stop is None else stop
    return [
        kept[k * extent + start : k * extent + stop] + got[k * extent + start : k * extent + stop]
        for k in range(4)
    ]


def trade_quarters(quarters):
    return [quarters[0]] + [swap_bit(quarters[k], k * X_BIT) for k in range(1, 4)]


def sum_quarters(quarters):
    left, right = (quarters[k].astype(F32) + quarters[k + 1].astype(F32) for k in (0, 2))
    return (left + right).astype(BF16)


CORE_BIT, X_BIT, ZH_BIT = 1, 2, 8


def shards(
    tokens,
    cluster_len,
    norm_gain,
    in_weight,
    conv_weight,
    conv_bias,
    dtx_weight,
    dt_weight,
    dt_bias,
    bc_weight,
    a_log,
    skip_gain,
    out_weight,
    cotangent,
):
    micros, count, width = tokens.shape
    inner = out_weight.shape[0]
    taps = conv_weight.shape[0]
    ranks = dtx_weight.shape[1]
    chunks = inner // (2 * LANES)
    own = chunks * LANES
    rows = micros * count
    edge = LANES // 2
    span = LANES + 32
    dp_parts = lax.axis_size("dp")
    state_count = lax.axis_size("state")
    dp_pos = lax.axis_index("dp")
    state_pos = lax.axis_index("state")
    half = state_pos & 1
    fast = state_count == 2 and dp_parts == 2 * chunks == 16
    if fast:
        place = jnp.stack([half, dp_pos & 1, dp_pos >> 1, (dp_pos >> 1) & 3])
        bc_own, alog_own = bc_weight, a_log
        bc_other, alog_other = swap_pair(bc_weight), swap_pair(a_log)
    else:
        place = jnp.stack([half, 0, 0, 0])
        bc_all = lax.all_gather(bc_weight, "state", axis=1, tiled=True)
        alog_all = lax.all_gather(a_log, "state", axis=0, tiled=True)
        eighth = alog_all.shape[0] // 2
        bc_own, bc_other = (
            lax.dynamic_slice_in_dim(bc_all, which * eighth, eighth, 1)
            for which in (half, 1 - half)
        )
        alog_own, alog_other = (
            lax.dynamic_slice_in_dim(alog_all, which * eighth, eighth, 0)
            for which in (half, 1 - half)
        )
    place = place.astype(jnp.int32)
    eighth = alog_own.shape[0]
    states = 2 * eighth

    x = tokens.reshape(rows, width)
    cotan = cotangent.reshape(rows, width)
    w4 = in_weight.reshape(2, chunks, 2, LANES, width)
    wout3 = out_weight.reshape(chunks, 2, LANES, width)
    dtx, dt = dtx_weight.T, dt_weight.T
    bias = dt_bias.reshape(-1, LANES)
    skip = skip_gain.reshape(-1, LANES)

    normed, act_all, act, inner_own, conved, gate = project(
        place, cluster_len, x, norm_gain[None], w4, conv_weight, conv_bias.reshape(-1, LANES)
    )
    bc, rank, high, decay, sp, u, step, slope, h, dy, gated, dgate, keep, send = scan_forward(
        place,
        cluster_len,
        act_all,
        bc_own,
        bc_other,
        alog_own,
        alog_other,
        dtx,
        dt,
        bias,
        skip,
        act,
        gate,
        wout3,
        cotan,
        normed,
    )
    if fast:
        early = swap_bit(send, CORE_BIT)
    mixed_part, dn_gate = products(place, gated, dgate, wout3, w4)
    if fast:
        *quarters, mixed_part, dn_gate, sp = lax.optimization_barrier(
            (*add_quarters(keep, early), mixed_part, dn_gate, sp)
        )
        early_got = trade_quarters(quarters)
    code_own, sact, dpre, alog, back = scan_backward(
        place, micros, bc, decay, dt, act, sp, u, step, slope, dy, h
    )
    if fast:
        *early_got, code_own, mixed_part = lax.optimization_barrier(
            (*early_got, code_own, mixed_part)
        )
    code_other = swap_pair(code_own)
    mixed_other = swap_pair(mixed_part)
    if fast:
        block = sum_quarters(early_got)
        out_keep, out_send, gate_sum = block[:edge], block[edge:LANES], block[LANES:]
        out_send, gate_sum, conved = lax.optimization_barrier((out_send, gate_sum, conved))
        out_got = swap_bit(out_send, ZH_BIT)
    late_keep, late_send, dnormed_part = tail(
        place,
        cluster_len,
        code_own,
        code_other,
        sact,
        dpre,
        alog,
        back,
        dtx,
        bc_own,
        bc_other,
        decay,
        dy,
        conved,
        inner_own,
        act,
        high,
        conv_weight,
        skip,
        normed,
        w4,
        dn_gate,
        x,
    )
    mixed = add_mixed(x, mixed_part, mixed_other)
    if fast:
        late_send, mixed_other = lax.optimization_barrier((late_send, mixed_other))
        mixed = add_mixed(x, mixed_part, mixed_other)
        late = swap_bit(late_send, CORE_BIT)
        late_got = trade_quarters(add_quarters(late_keep, late))
    dnormed_other = swap_pair(dnormed_part)
    tokens_grad = finish(x, dnormed_part, dnormed_other, cotan, norm_gain[None])
    if fast:
        out_own = swap_both(out_keep + out_got)
        *late_got, out_own, tokens_grad, mixed = lax.optimization_barrier(
            (*late_got, out_own, tokens_grad, mixed)
        )
        block = sum_quarters(late_got)
        inner_sum = block[:LANES]
        upper = dp_pos >= dp_parts // 2
        crossing = jnp.where(upper, inner_sum, gate_sum)
        first, second = crossing[:edge], crossing[edge:]
        first, pack_far, pack_near = lax.optimization_barrier(
            (first, block[-16:], block[LANES:-16])
        )
        pack_far = swap_both(pack_far, ZH_BIT)
        first_got = swap_bit(first, ZH_BIT)
        pack_near = swap_both(pack_near)
        first_got, pack_far, pack_near = lax.optimization_barrier((first_got, pack_far, pack_near))
        second_got = swap_bit(second, ZH_BIT)
        gain_mine = (
            pack_near[:, 5 * LANES : 6 * LANES].astype(F32)
            + pack_far[:, 5 * LANES : 6 * LANES].astype(F32)
        ).astype(BF16)
        gain_both = gain_mine[-1].astype(F32) + swap_bit(gain_mine, CORE_BIT)[-1].astype(F32)
        extent = width // (dp_parts * state_count)
        gain_grad = lax.dynamic_slice_in_dim(gain_both, (dp_pos & 1) * extent, extent, 0)
        (
            dtx_grad,
            dt_grad,
            bc_grad,
            alog_grad,
            convw_grad,
            convb_grad,
            bias_grad,
            skip_grad,
            out_own,
        ) = unpack(pack_near, pack_far, out_own, eighth, taps, ranks)
        convb_grad, bias_grad, skip_grad = (
            array[0] for array in (convb_grad, bias_grad, skip_grad)
        )
        second_got, dtx_grad, dt_grad, out_own = lax.optimization_barrier(
            (second_got, dtx_grad, dt_grad, out_own)
        )
        in_grad = jnp.where(upper, gate_sum, inner_sum).astype(F32) + jnp.concatenate(
            [first_got, second_got]
        ).astype(F32)
    mixed = mixed.reshape(micros, count, width)
    tokens_grad = tokens_grad.reshape(micros, count, width)

    if not fast:
        def total(array):
            return lax.psum(array.astype(F32), "dp")

        def both_rows(array):
            mine = array.reshape(chunks, 1, LANES, -1)
            other = swap_pair(mine)
            low = jnp.where(half == 0, mine, other)
            high = jnp.where(half == 0, other, mine)
            return jnp.concatenate([low, high], axis=1).reshape(2 * own, -1)

        every = dp_parts * state_count
        at = dp_pos * state_count + state_pos

        def cut_own(array):
            extent = array.shape[0] // every
            return lax.dynamic_slice_in_dim(array, at * extent, extent, 0)

        pair = total(jnp.stack([keep, send])).reshape(2, 2, 2, 2 * LANES, width)
        outs = pair[:, :, :, :LANES].reshape(2, 2, 2, 2, edge, width)
        outs = jnp.transpose(outs, (3, 1, 2, 0, 4, 5)).reshape(own, width)
        gates = jnp.moveaxis(pair[:, :, :, LANES:], 0, 2).reshape(own, width)
        pair = total(jnp.stack([late_keep, late_send])).reshape(2, 2, 2, span, width)
        inners = jnp.moveaxis(pair[:, :, :, :LANES], 0, 2).reshape(own, width)
        packs = pair[:, :, :, LANES:].reshape(2, 2, 2, 2, 16, width // LANES, LANES)
        packs = jnp.transpose(packs, (3, 1, 2, 0, 5, 4, 6)).reshape(chunks, 2, -1, 16, LANES)
        small = both_rows(packs[:, :, :4].reshape(own, LANES))
        in_grad = cut_own(jnp.concatenate([both_rows(inners), both_rows(gates)]))
        out_own = cut_own(both_rows(outs))
        mine = cut_own(small)
        dtx_grad, dt_grad = mine[:, :ranks], mine[:, ranks:]
        vec_rows = jnp.swapaxes(packs[:, :, 5, eighth:, :edge], 2, 3).reshape(own, -1)
        gain_sum = vec_rows[:, -1].reshape(chunks, 2, 2, -1).swapaxes(1, 2).reshape(-1)
        gain_grad = cut_own(gain_sum + swap_pair(gain_sum))
        vec = cut_own(both_rows(vec_rows)).T
        state_rows = jnp.concatenate([packs[:, :, 4], packs[:, :, 5, :eighth]], axis=2)
        state_rows = state_rows.reshape(chunks, 2, 3, eighth, LANES)
        state_rows = jnp.transpose(state_rows, (0, 4, 2, 1, 3)).reshape(own, -1)
        extent = inner // dp_parts
        state_part = lax.dynamic_slice_in_dim(both_rows(state_rows), dp_pos * extent, extent, 0)
        state_part = state_part.T.reshape(3, state_count, -1, extent)
        state_part = lax.dynamic_index_in_dim(state_part, state_pos, 1, keepdims=False)
        bc_grad, alog_grad = state_part[:2], state_part[2]
        convw_grad, convb_grad, bias_grad, skip_grad = (
            vec[:taps], vec[taps], vec[taps + 1], vec[taps + 2]
        )

    return (
        mixed,
        tokens_grad,
        gain_grad,
        in_grad,
        convw_grad,
        convb_grad,
        dtx_grad,
        dt_grad,
        bias_grad,
        bc_grad,
        alog_grad,
        skip_grad,
        out_own,
    )


def solution(mesh):
    return jax.shard_map(
        shards,
        mesh=mesh,
        in_specs=(
            P(None, "dp", None),
            P(None, "dp", None),
            P(),
            P(),
            P(),
            P(),
            P(),
            P(),
            P(),
            P(None, "state", None),
            P("state", None),
            P(),
            P(),
            P(None, "dp", None),
        ),
        out_specs=(
            P(None, "dp", None),
            P(None, "dp", None),
            P(("dp", "state")),
            P(("dp", "state"), None),
            P(None, ("dp", "state")),
            P(("dp", "state")),
            P(("dp", "state"), None),
            P(("dp", "state"), None),
            P(("dp", "state")),
            P(None, "state", "dp"),
            P("state", "dp"),
            P(("dp", "state")),
            P(("dp", "state"), None),
        ),
        check_vma=False,
    )
```

```python
import functools
import math

import jax
import jax.numpy as jnp
from jax import lax
from jax.experimental import pallas as pl
from jax.experimental.pallas import tpu as pltpu
from jax.sharding import PartitionSpec as P

EPSILON = 1e-05
LANES = 128
RESET = 1e4
LOG2E = math.log2(math.e)
F32 = jnp.float32
BF16 = jnp.bfloat16
MIB = 1024 * 1024


def dot(left, right, left_dim, right_dim):
    return lax.dot_general(
        left, right, (((left_dim,), (right_dim,)), ((), ())), preferred_element_type=F32
    )


def params(mib):
    return pltpu.CompilerParams(
        vmem_limit_bytes=mib * MIB, dimension_semantics=("arbitrary",)
    )


ANY = pl.BlockSpec(memory_space=pl.ANY)


def stream(step, steps, fetch):
    @pl.when(step == 0)
    def _():
        for k in range(steps):
            for copy in fetch(k):
                copy.start()

    for copy in fetch(step):
        copy.wait()


def whole(shape):
    return pl.BlockSpec(shape, lambda *_: (0,) * len(shape))


sigmoid = jax.nn.sigmoid


def log_one_plus(value):
    series = value * (1.0 - value * (0.5 - value * (1.0 / 3.0)))
    return jnp.where(value < 1e-3, series, jnp.log(1.0 + value))


def lanes(index):
    return pl.ds(pl.multiple_of(index * LANES, LANES), LANES)


def cost(micros):
    return pl.CostEstimate(
        flops=int(micros * 1e9), bytes_accessed=int(micros * 1e6), transcendentals=0
    )


def hbm(shape, dtype):
    return pltpu.HBM(shape, dtype)


def in_hbm(arrays):
    return [pltpu.with_memory_space_constraint(array, pltpu.HBM) for array in arrays]


def aligned(start, size, to=8):
    return pl.ds(pl.multiple_of(start, to), size)


SEGMENTS = 4

HALF, CORE, CUBE, FACE = range(4)


def fill_masks(len_ref, mask_ref, micros, count, taps, clusters):
    place = lax.broadcasted_iota(jnp.int32, (count, LANES), 0)
    for micro in range(micros):
        rows = pl.ds(micro * count, count)
        for back in range(1, taps):
            apart = place < back
            start = 0
            for cluster in range(clusters - 1):
                start = start + len_ref[micro, 0, cluster]
                apart = apart | ((place >= start) & (place < start + back))
            mask_ref[back, rows, :] = jnp.where(apart, 0.0, 1.0)
            if back == 1:
                mask_ref[0, rows, :] = jnp.where(apart, 1.0, 0.0)


def project_kernel(
    place_ref,
    len_ref,
    gain_ref,
    convw_ref,
    convb_ref,
    x_far,
    weight_far,
    normed_far,
    act_far,
    own_act_far,
    inner_far,
    conved_far,
    gate_far,
    mask_ref,
    x_ref,
    win_ref,
    wgate_ref,
    normed_ref,
    act_ref,
    own_act_ref,
    inner_ref,
    conved_ref,
    gate_ref,
    in_sems,
    out_sems,
    *,
    micros,
    count,
    taps,
    clusters,
):
    half = place_ref[HALF]
    chunks = win_ref.shape[0]
    inward = [pltpu.make_async_copy(x_far, x_ref, in_sems.at[2 * chunks])]
    for k in range(chunks):
        inward.append(pltpu.make_async_copy(weight_far.at[0, k], win_ref.at[k], in_sems.at[2 * k]))
        inward.append(
            pltpu.make_async_copy(
                weight_far.at[1, k, half], wgate_ref.at[k], in_sems.at[2 * k + 1]
            )
        )
    for copy in inward:
        copy.start()
    outward = []

    def put(source, target):
        outward.append(pltpu.make_async_copy(source, target, out_sems.at[len(outward)]))
        outward[-1].start()

    fill_masks(len_ref, mask_ref, micros, count, taps, clusters)
    inward[0].wait()
    rows = x_ref[...].astype(F32)
    scale = lax.rsqrt(jnp.mean(rows * rows, axis=1, keepdims=True) + EPSILON)
    normed = (rows * scale * gain_ref[...]).astype(BF16)
    normed_ref[...] = normed
    put(normed_ref, normed_far)
    for k in range(chunks):
        inward[2 * k + 1].wait()
        inward[2 * k + 2].wait()
        proj = dot(normed, win_ref[k].reshape(2 * LANES, -1), 1, 1)
        own = slice(k * LANES, (k + 1) * LANES)
        gate_ref[:, own] = dot(normed, wgate_ref[k], 1, 1)
        inners, conveds, acts = [], [], []
        for part in range(2):
            cols = slice((2 * k + part) * LANES, (2 * k + part + 1) * LANES)
            inner = proj[:, part * LANES : (part + 1) * LANES]
            conved = convb_ref[2 * k + part : 2 * k + part + 1, :]
            conved = conved + convw_ref[taps - 1 : taps, cols] * inner
            for back in range(1, taps):
                shifted = pltpu.roll(inner, back, 0) * mask_ref[back]
                conved = conved + convw_ref[taps - 1 - back : taps - back, cols] * shifted
            act = conved * sigmoid(conved)
            act_ref[:, cols] = act.astype(BF16)
            inners.append(inner)
            conveds.append(conved)
            acts.append(act)
        inner_ref[:, own] = jnp.where(half == 0, *inners)
        conved_ref[:, own] = jnp.where(half == 0, *conveds)
        own_act_ref[:, own] = jnp.where(half == 0, *acts).astype(BF16)
        if k % 2:
            group = pl.ds((k - 1) * LANES, 2 * LANES)
            wide = pl.ds(2 * (k - 1) * LANES, 4 * LANES)
            put(act_ref.at[:, wide], act_far.at[:, wide])
            for near, far in (
                (gate_ref, gate_far),
                (inner_ref, inner_far),
                (conved_ref, conved_far),
                (own_act_ref, own_act_far),
            ):
                put(near.at[:, group], far.at[:, group])
    for copy in outward:
        copy.wait()


def project(place, lengths, x, gain, w4, conv_weight, conv_bias):
    rows, width = x.shape
    chunks = w4.shape[1]
    micros, _, clusters = lengths.shape
    taps = conv_weight.shape[0]
    own = chunks * LANES
    outs = [
        ((rows, width), BF16),
        ((rows, 2 * own), BF16),
        ((rows, own), BF16),
        ((rows, own), F32),
        ((rows, own), F32),
        ((rows, own), F32),
    ]
    return pl.pallas_call(
        functools.partial(
            project_kernel, micros=micros, count=rows // micros, taps=taps, clusters=clusters
        ),
        grid_spec=pltpu.PrefetchScalarGridSpec(
            num_scalar_prefetch=1,
            grid=(1,),
            in_specs=[
                pl.BlockSpec(memory_space=pltpu.SMEM),
                whole(gain.shape),
                whole(conv_weight.shape),
                whole(conv_bias.shape),
                ANY,
                ANY,
            ],
            out_specs=[ANY] * len(outs),
            scratch_shapes=[
                pltpu.VMEM((taps, rows, LANES), F32),
                pltpu.VMEM((rows, width), BF16),
                pltpu.VMEM((chunks, 2, LANES, width), BF16),
                pltpu.VMEM((chunks, LANES, width), BF16),
            ]
            + [pltpu.VMEM(*out) for out in outs]
            + [
                pltpu.SemaphoreType.DMA((2 * chunks + 1,)),
                pltpu.SemaphoreType.DMA((1 + 5 * chunks // 2,)),
            ],
        ),
        out_shape=[hbm(*out) for out in outs],
        compiler_params=params(30),
        cost_estimate=cost(6),
        name="project",
    )(place, *in_hbm((lengths, gain, conv_weight, conv_bias, x, w4)))


def every_row(ref, row, height):
    return ref[pl.ds(row, height, stride=0), :]


def b_at(n, eighth):
    return (n // eighth) * 2 * eighth + n % eighth


def c_at(n, eighth):
    return b_at(n, eighth) + eighth


def forward_kernel(
    place_ref,
    len_ref,
    act_all_ref,
    bc_own_ref,
    bc_other_ref,
    alog_own_ref,
    alog_other_ref,
    dtx_ref,
    dt_ref,
    bias_ref,
    skip_ref,
    act_ref,
    *refs,
    micros,
    count,
    states,
    chunks,
    clusters,
):
    gate_far, wout_far, cotan_far, normed_far = refs[:4]
    bc_ref, rank_ref, rank_high_ref, decay_ref = refs[4:8]
    sp_far, u_far, step_far, slope_far, h_far, dy_far = refs[8:14]
    gated_far, dgate_far, keep_far, send_far = refs[14:18]
    mask_ref, y_ref, tmp_ref, wide_ref = refs[18:22]
    gate_ref, wout_ref, cotan_ref, normed_ref = refs[22:26]
    sp_ref, u_ref, step_ref, slope_ref, h_ref, dy_ref = refs[26:32]
    gated_ref, dgate_ref, keep_ref, send_ref = refs[32:36]
    in_sems, out_sems = refs[36:]
    rows = micros * count
    eighth = states // 2
    half, core, cube, face = (place_ref[k] for k in range(4))
    first = half == 0
    inward = [
        pltpu.make_async_copy(source, target, in_sems.at[k])
        for k, (source, target) in enumerate(
            (
                (gate_far, gate_ref),
                (wout_far.at[:, half], wout_ref),
                (cotan_far, cotan_ref),
                (normed_far, normed_ref),
            )
        )
    ]
    for copy in inward:
        copy.start()
    outward = []

    def put(source, target):
        outward.append(pltpu.make_async_copy(source, target, out_sems.at[len(outward)]))
        outward[-1].start()

    ranks = dtx_ref.shape[0]
    weights = jnp.concatenate(
        [dtx_ref[...]] + [ref[...].reshape(states, -1) for ref in (bc_own_ref, bc_other_ref)]
    )
    product = dot(act_all_ref[...], weights, 1, 1)
    own, other = product[:, ranks : ranks + states], product[:, ranks + states :]
    bc_ref[:, :states] = jnp.where(first, own, other)
    bc_ref[:, states:] = jnp.where(first, other, own)
    spread_lanes(bc_ref, wide_ref)

    fill_masks(len_ref, mask_ref, micros, count, 2, clusters)
    for chunk in range(chunks):
        cols = lanes(2 * chunk + half)
        own, other = alog_own_ref[:, cols], alog_other_ref[:, cols]
        tmp_ref[pl.ds(chunk * states, eighth), :] = jnp.where(first, own, other)
        tmp_ref[pl.ds(chunk * states + eighth, eighth), :] = jnp.where(first, other, own)
    for n in range(states):
        decay_ref[pl.ds(n * chunks, chunks), :] = -LOG2E * jnp.exp(
            tmp_ref[pl.ds(n, chunks, stride=states), :]
        )

    rank = product[:, :ranks].astype(BF16)
    rank_ref[...] = rank
    rank_high_ref[...] = jnp.concatenate([jnp.zeros_like(rank), rank], axis=1)
    for chunk in range(chunks):
        cols = slice(chunk * LANES, (chunk + 1) * LANES)
        bias = bias_ref[pl.ds(2 * chunk + half, 1), :]
        pre = dot(rank, dt_ref[:, lanes(2 * chunk + half)], 1, 0) + bias
        tail_part = jnp.exp(-jnp.abs(pre))
        step = jnp.maximum(pre, 0.0) + log_one_plus(tail_part)
        slope = jnp.where(pre >= 0.0, 1.0, tail_part) / (1.0 + tail_part)
        step_ref[:, cols] = step
        slope_ref[:, cols] = slope.astype(BF16)
        held = step + RESET * mask_ref[0]
        source = step * act_ref[:, cols].astype(F32)
        for micro in range(micros):
            span = slice(micro * count, (micro + 1) * count)
            place = pl.ds((micro * chunks + chunk) * count, count)
            sp_ref[place, :] = held[span]
            u_ref[place, :] = source[span]
    put(sp_ref, sp_far)
    put(u_ref, u_far)
    put(step_ref, step_far)
    put(slope_ref, slope_far)

    for micro in range(micros):

        def advance(t, h, micro=micro):
            row = micro * count + t
            span = pl.ds(micro * chunks * count + t, chunks, stride=count)
            sp = sp_ref[span, :]
            u = u_ref[span, :]
            out = []
            y = None
            for n in range(states):
                decay = jnp.exp2(sp * decay_ref[pl.ds(n * chunks, chunks), :])
                now = decay * h[n] + u * every_row(wide_ref, b_at(n, eighth) * rows + row, chunks)
                h_ref[aligned((row * states + n) * chunks, chunks), :] = now
                out.append(now)
                term = now * every_row(wide_ref, c_at(n, eighth) * rows + row, chunks)
                y = term if y is None else y + term
            y_ref[span, :] = y
            return tuple(out)

        h = (jnp.zeros((chunks, LANES), F32),) * states
        segment = count // SEGMENTS
        for k in range(SEGMENTS):
            h = lax.fori_loop(k * segment, (k + 1) * segment, advance, h, unroll=4)
            extent = segment * states * chunks
            place = pl.ds((micro * SEGMENTS + k) * extent, extent)
            put(h_ref.at[place], h_far.at[place])

    for copy in inward:
        copy.wait()
    cotan = cotan_ref[...]
    for chunk in range(chunks):
        cols = slice(chunk * LANES, (chunk + 1) * LANES)
        places = [pl.ds((micro * chunks + chunk) * count, count) for micro in range(micros)]
        y = jnp.concatenate([y_ref[place, :] for place in places])
        y = y + skip_ref[pl.ds(2 * chunk + half, 1), :] * act_ref[:, cols].astype(F32)
        gate = gate_ref[:, cols]
        sig = sigmoid(gate)
        gated_ref[:, cols] = (y * (gate * sig)).astype(BF16)
        dgated = dot(cotan, wout_ref[chunk], 1, 1)
        dy = dgated * (gate * sig)
        for micro in range(micros):
            dy_ref[places[micro], :] = dy[micro * count : (micro + 1) * count]
        dgate_ref[:, cols] = (dgated * y * (sig * (1.0 + gate * (1.0 - sig)))).astype(BF16)
    put(dy_ref, dy_far)
    put(gated_ref, gated_far)
    put(dgate_ref, dgate_far)
    normed = normed_ref[...]
    edge = LANES // 2
    for r in range(chunks // 2):
        for zh in range(2):
            grad = dot(gated_ref[:, lanes((r + 4 * zh) ^ cube)], cotan, 0, 0).astype(BF16)
            top, bottom = grad[:edge], grad[edge:]
            place = pl.ds(r * 2 * LANES + zh * edge, edge)
            keep_ref[place, :] = jnp.where(core == 0, top, bottom)
            send_ref[place, :] = jnp.where(core == 0, bottom, top)
        place = pl.ds((2 * r + 1) * LANES, LANES)
        pair = 2 * (r ^ face)
        for chunk, out_ref in ((pair + core, keep_ref), (pair + 1 - core, send_ref)):
            out_ref[place, :] = dot(dgate_ref[:, lanes(chunk)], normed, 0, 0).astype(BF16)
        place = pl.ds(r * 2 * LANES, 2 * LANES)
        put(send_ref.at[place], send_far.at[place])
        put(keep_ref.at[place], keep_far.at[place])
    for copy in outward:
        copy.wait()


def scan_forward(
    place,
    lengths,
    act_all,
    bc_own,
    bc_other,
    alog_own,
    alog_other,
    dtx,
    dt,
    bias,
    skip,
    act,
    gate,
    wout3,
    cotan,
    normed,
):
    rows, own = act.shape
    chunks = own // LANES
    states = 2 * alog_own.shape[0]
    width = cotan.shape[1]
    micros, _, clusters = lengths.shape
    ranks = dtx.shape[0]
    small = [
        ((rows, 2 * states), F32),
        ((rows, ranks), BF16),
        ((rows, 2 * ranks), BF16),
        ((states * chunks, LANES), F32),
    ]
    large = [
        ((chunks * rows, LANES), F32),
        ((chunks * rows, LANES), F32),
        ((rows, own), F32),
        ((rows, own), BF16),
        ((rows * states * chunks, LANES), F32),
        ((chunks * rows, LANES), F32),
        ((rows, own), BF16),
        ((rows, own), BF16),
        ((own, width), BF16),
        ((own, width), BF16),
    ]
    operands = (act_all, bc_own, bc_other, alog_own, alog_other, dtx, dt, bias, skip, act)
    streamed = (gate, wout3, cotan, normed)
    return pl.pallas_call(
        functools.partial(
            forward_kernel,
            micros=micros,
            count=rows // micros,
            states=states,
            chunks=chunks,
            clusters=clusters,
        ),
        grid_spec=pltpu.PrefetchScalarGridSpec(
            num_scalar_prefetch=1,
            grid=(1,),
            in_specs=[pl.BlockSpec(memory_space=pltpu.SMEM)]
            + [whole(operand.shape) for operand in operands]
            + [ANY] * len(streamed),
            out_specs=[whole(shape) for shape, _ in small] + [ANY] * len(large),
            scratch_shapes=[
                pltpu.VMEM((2, rows, LANES), F32),
                pltpu.VMEM((chunks * rows, LANES), F32),
                pltpu.VMEM((states * chunks, LANES), F32),
                pltpu.VMEM((2 * states * rows, LANES), F32),
                pltpu.VMEM((rows, own), F32),
                pltpu.VMEM((chunks, LANES, width), BF16),
                pltpu.VMEM((rows, width), BF16),
                pltpu.VMEM((rows, width), BF16),
            ]
            + [pltpu.VMEM(*out) for out in large]
            + [pltpu.SemaphoreType.DMA((4,)), pltpu.SemaphoreType.DMA((7 + chunks + micros * SEGMENTS,))],
        ),
        out_shape=[hbm(*out) for out in small + large],
        compiler_params=params(52),
        cost_estimate=cost(19),
        name="scan_forward",
    )(
        place,
        lengths,
        *in_hbm(operands[:1]),
        *operands[1:5],
        *in_hbm((*operands[5:], *streamed)),
    )


def spread_lanes(values_ref, wide_ref):
    rows, count = values_ref.shape
    for k in range(count):
        wide_ref[pl.ds(k * rows, rows), :] = jnp.broadcast_to(
            values_ref[:, k : k + 1], (rows, LANES)
        )


def backward_kernel(
    place_ref,
    bc_ref,
    decay_ref,
    dt_ref,
    act_ref,
    sp_ref,
    u_ref,
    step_ref,
    slope_ref,
    dy_ref,
    h_far,
    code_ref,
    sact_ref,
    dpre_ref,
    alog_ref,
    vec_ref,
    h_ref,
    s_ref,
    d_ref,
    terms_ref,
    sums_b_ref,
    sums_c_ref,
    wide_ref,
    sems,
    *,
    count,
    states,
    chunks,
):
    micro = pl.program_id(0)
    block = states * chunks
    segment = count // SEGMENTS

    def fetch(which, k):
        extent = segment * block
        buffer = h_ref.at[which % 2]
        return pltpu.make_async_copy(
            h_far.at[aligned((which * SEGMENTS + k) * extent, extent)],
            buffer.at[pl.ds(block + k * extent, extent)],
            sems.at[which % 2, k],
        )

    @pl.when(micro == 0)
    def _():
        for k in reversed(range(SEGMENTS)):
            fetch(0, k).start()
        for which in range(2):
            h_ref[which, pl.ds(0, block), :] = jnp.zeros((block, LANES), F32)
        alog_ref[...] = jnp.zeros_like(alog_ref)
        vec_ref[...] = jnp.zeros_like(vec_ref)

    half = place_ref[HALF]
    eighth = states // 2
    zero = (jnp.zeros((chunks, LANES), F32),) * states
    spread_lanes(bc_ref, wide_ref)

    @pl.when(micro + 1 < pl.num_programs(0))
    def _():
        for k in reversed(range(SEGMENTS)):
            fetch(micro + 1, k).start()

    side = micro % 2

    def put_terms(which, t, terms):
        for n in range(0, states, 2):
            pair = jnp.concatenate(terms[n : n + 2]).astype(BF16)
            place = aligned(t * block + n * chunks, 2 * chunks, 16)
            terms_ref[which, place, :] = pair

    def retreat(back, carry):
        flows, totals = carry
        for slot in range(2):
            t = count - 1 - (2 * back + slot)
            span = pl.ds(t, chunks, stride=count)
            sp = sp_ref[span, :]
            u = u_ref[span, :]
            dy = dy_ref[span, :]
            out_flows = []
            out_totals = []
            b_terms, c_terms = [], []
            d_sum = None
            s_sum = None
            for n in range(states):
                rate = decay_ref[pl.ds(n * chunks, chunks), :]
                dh = flows[n] + dy * every_row(wide_ref, c_at(n, eighth) * count + t, chunks)
                flow = jnp.exp2(sp * rate) * dh
                out_flows.append(flow)
                q = flow * h_ref[side, aligned(t * block + n * chunks, chunks), :]
                now = h_ref[side, aligned((t + 1) * block + n * chunks, chunks), :]
                out_totals.append(totals[n] + q * sp)
                d_term = q * rate
                s_term = dh * every_row(wide_ref, b_at(n, eighth) * count + t, chunks)
                d_sum = d_term if d_sum is None else d_sum + d_term
                s_sum = s_term if s_sum is None else s_sum + s_term
                b_terms.append(dh * u)
                c_terms.append(dy * now)
            s_ref[span, :] = s_sum
            d_ref[span, :] = d_sum
            put_terms(0, t, b_terms)
            put_terms(1, t, c_terms)
            flows, totals = tuple(out_flows), tuple(out_totals)
        return flows, totals

    carry = (zero, zero)
    for k in range(SEGMENTS):
        fetch(micro, SEGMENTS - 1 - k).wait()
        carry = lax.fori_loop(k * segment // 2, (k + 1) * segment // 2, retreat, carry)
    totals = carry[1]
    for n in range(states):
        alog_ref[pl.ds(n * chunks, chunks), :] += totals[n]

    shape = (2 * states, 2 * block)
    group = lax.broadcasted_iota(jnp.int32, shape, 1) // chunks
    gather = jnp.where(group == lax.broadcasted_iota(jnp.int32, shape, 0), 1.0, 0.0).astype(BF16)

    @pl.loop(0, count // 64)
    def _(step):
        for which, sums_ref in ((0, sums_b_ref), (1, sums_c_ref)):
            for k in range(32):
                at = 32 * step + k
                terms = terms_ref[which, aligned(at * 2 * block, 2 * block, 16), :]
                sums_ref[aligned(at * 2 * states, 2 * states), :] = dot(gather, terms, 1, 0)

    ranks = dt_ref.shape[0]
    drank = None
    for chunk in range(chunks):
        cols = slice(chunk * LANES, (chunk + 1) * LANES)
        place = pl.ds(chunk * count, count)
        act = act_ref[:, cols].astype(F32)
        weight = dt_ref[:, lanes(2 * chunk + half)]
        s_now = s_ref[place, :]
        dstep = d_ref[place, :] * (1.0 / LOG2E) + s_now * act
        sact_ref[:, cols] = s_now * step_ref[:, cols]
        dpre = dstep * slope_ref[:, cols].astype(F32)
        vec_ref[0:1, cols] += jnp.sum(dpre, axis=0, keepdims=True)
        vec_ref[1:2, cols] += jnp.sum(dy_ref[place, :] * act, axis=0, keepdims=True)
        low = dpre.astype(BF16)
        dpre_ref[:, cols] = low
        term = dot(low, weight, 1, 1)
        drank = term if drank is None else drank + term
    source = lax.broadcasted_iota(jnp.int32, (2 * LANES, LANES), 0)
    target = lax.broadcasted_iota(jnp.int32, (2 * LANES, LANES), 1)
    code = None
    for n in range(states):
        pair = jnp.concatenate(
            [ref[pl.ds(n, count, stride=states), :] for ref in (sums_b_ref, sums_c_ref)], axis=1
        )
        column = ranks + jnp.where(source < LANES, b_at(n, eighth), c_at(n, eighth))
        pick = jnp.where(target == column, 1.0, 0.0).astype(BF16)
        term = dot(pair.astype(BF16), pick, 1, 0)
        code = term if code is None else code + term
    drank = jnp.concatenate([drank, jnp.zeros((count, LANES - ranks), F32)], axis=1)
    code_ref[...] = (code + drank).astype(BF16)


def scan_backward(place, micros, bc, decay, dt, act, sp, u, step, slope, dy, h):
    rows, own = act.shape
    count = rows // micros
    chunks = own // LANES
    states = bc.shape[1] // 2
    outs = [
        ((rows, LANES), BF16),
        ((rows, own), F32),
        ((rows, own), BF16),
        ((states * chunks, LANES), F32),
        ((2, own), F32),
    ]

    def block(*shape):
        return pl.BlockSpec(shape, lambda i, p: (i, 0))

    return pl.pallas_call(
        functools.partial(backward_kernel, count=count, states=states, chunks=chunks),
        grid_spec=pltpu.PrefetchScalarGridSpec(
            num_scalar_prefetch=1,
            grid=(micros,),
            in_specs=[
                block(count, 2 * states),
                whole(decay.shape),
                whole(dt.shape),
                block(count, own),
                block(chunks * count, LANES),
                block(chunks * count, LANES),
                block(count, own),
                block(count, own),
                block(chunks * count, LANES),
                ANY,
            ],
            out_specs=[block(count, LANES), block(count, own), block(count, own)]
            + [whole(shape) for shape, _ in outs[3:]],
            scratch_shapes=[
                pltpu.VMEM((2, (count + 1) * states * chunks, LANES), F32),
                pltpu.VMEM((chunks * count, LANES), F32),
                pltpu.VMEM((chunks * count, LANES), F32),
                pltpu.VMEM((2, count * states * chunks, LANES), BF16),
                pltpu.VMEM((count * states, LANES), F32),
                pltpu.VMEM((count * states, LANES), F32),
                pltpu.VMEM((2 * states * count, LANES), F32),
                pltpu.SemaphoreType.DMA((2, SEGMENTS)),
            ],
        ),
        out_shape=[hbm(*out) for out in outs],
        compiler_params=params(52),
        cost_estimate=cost(0),
        name="scan_backward",
    )(place, *in_hbm((bc, decay, dt, act, sp, u, step, slope, dy, h)))


def tail_kernel(
    place_ref,
    len_ref,
    *refs,
    micros,
    count,
    taps,
    clusters,
    ranks,
    chunks,
    states,
):
    def take(number):
        nonlocal refs
        taken, refs = refs[:number], refs[number:]
        return taken

    code_own_ref, code_other_ref = take(2)
    sact_ref, dpre_ref, alog_sum_ref, back_ref = take(4)
    dtx_ref, bc_own_ref, bc_other_ref, decay_ref = take(4)
    dy_refs = take(micros)
    conved_ref, inner_ref, act_ref, high_ref, convw_ref, skip_ref = take(6)
    normed_ref, weight_ref, gate_part_ref, x_ref = take(4)
    keep_ref, send_ref, dnormed_ref = take(3)
    mask_ref, code_ref, wcode_ref, vec_ref, alog_ref, total_ref, win_ref, sems, low_ref = refs[:9]
    code_turned_ref, rank_turned_ref = refs[9:]

    step = pl.program_id(0)
    rows = micros * count
    eighth = states // 2
    edge = LANES // 2
    half, core, cube, face = (place_ref[k] for k in range(4))
    pair = step ^ face
    span = LANES + 32

    def fetch(k):
        source = weight_ref.at[0, pl.ds(2 * (k ^ face), 2), half]
        return (pltpu.make_async_copy(source, win_ref.at[k], sems.at[k]),)

    stream(step, win_ref.shape[0], fetch)

    def pack_row(chunk):
        relative = chunk ^ cube
        return (relative & 3) * span + LANES + (relative >> 2) * 16

    def place_pair(start, size, cols, even, odd):
        keep_ref[aligned(start, size, 16), cols] = jnp.where(core == 0, even, odd).astype(BF16)
        send_ref[aligned(start, size, 16), cols] = jnp.where(core == 0, odd, even).astype(BF16)

    @pl.when(step == 0)
    def _():
        fill_masks(len_ref, mask_ref, micros, count, taps, clusters)
        total_ref[...] = gate_part_ref[...].astype(F32)
        code_ref[...] = (
            code_own_ref[...].astype(F32) + code_other_ref[...].astype(F32)
        ).astype(BF16)
        code_turned_ref[...] = code_ref[...].T
        rank_turned_ref[...] = high_ref[...].T
        alog_ref[...] = alog_sum_ref[...] * (decay_ref[...] * (1.0 / LOG2E))

    code = code_ref[...]
    lane = lax.broadcasted_iota(jnp.int32, (1, LANES), 1)
    for part in range(2):
        source = lanes(2 * (2 * pair + part) + half)
        cols = slice(part * LANES, (part + 1) * LANES)
        wcode_ref[:ranks, cols] = dtx_ref[:, source]
        own = bc_own_ref[:, :, source].reshape(states, LANES)
        other = bc_other_ref[:, :, source].reshape(states, LANES)
        wcode_ref[ranks : ranks + states, cols] = jnp.where(half == 0, own, other)
        wcode_ref[ranks + states : ranks + 2 * states, cols] = jnp.where(half == 0, other, own)
        wcode_ref[ranks + 2 * states :, cols] = jnp.zeros(
            (LANES - ranks - 2 * states, LANES), BF16
        )
    for part in range(2):
        cols = slice(part * LANES, (part + 1) * LANES)
        chunk = 2 * pair + part
        source = 2 * chunk + half
        weights = convw_ref[:, lanes(source)]
        sact = sact_ref[:, cols]
        dy = jnp.concatenate([ref[pl.ds(part * count, count), :] for ref in dy_refs], axis=0)
        dact = sact + dot(code, wcode_ref[:, cols], 1, 0)
        dact = dact + dy * skip_ref[pl.ds(source, 1), :]
        conved = conved_ref[:, cols]
        sig = sigmoid(conved)
        dconv = dact * (sig * (1.0 + conved * (1.0 - sig)))
        inner = inner_ref[:, cols]
        dinner = weights[taps - 1 : taps] * dconv
        sums = [None] * (taps + 1)
        sums[taps - 1] = jnp.sum(dconv * inner, axis=0, keepdims=True)
        sums[taps] = jnp.sum(dconv, axis=0, keepdims=True)
        for back in range(1, taps):
            kept = dconv * mask_ref[back]
            dinner = dinner + weights[taps - 1 - back : taps - back] * pltpu.roll(
                kept, rows - back, 0
            )
            sums[taps - 1 - back] = jnp.sum(
                kept * pltpu.roll(inner, back, 0), axis=0, keepdims=True
            )
        for k in range(taps + 1):
            vec_ref[k : k + 1, lanes(chunk)] = sums[k]
        vec_ref[taps + 1 : taps + 3, lanes(chunk)] = back_ref[:, lanes(chunk)]
        low_ref[:, cols] = dinner.astype(BF16)

        act = act_ref[:, cols]
        start = pack_row(chunk)
        code_rows = dot(code_turned_ref[...], act, 1, 0)
        rank_rows = dot(rank_turned_ref[...], dpre_ref[:, cols], 1, 0)[ranks:]
        dtx_rows = code_rows[:ranks]
        even = jnp.where(lane < edge, dtx_rows, pltpu.roll(rank_rows, edge, 1))
        odd = jnp.where(lane < edge, pltpu.roll(dtx_rows, edge, 1), rank_rows)
        for k in range(4):
            place = slice(k * 16, (k + 1) * 16)
            place_pair(
                start, 16, slice(k * LANES, (k + 1) * LANES), even[place], odd[place]
            )
        state_rows = code_rows[ranks : ranks + 2 * states]
        place_pair(
            start, 16, slice(4 * LANES, 5 * LANES), state_rows[:states], state_rows[states:]
        )

    normed = normed_ref[...]
    for part in range(2):
        grad = dot(low_ref[:, lanes(core ^ part)], normed, 0, 0)
        out_ref = (keep_ref, send_ref)[part]
        out_ref[aligned(step * span, LANES, 16), :] = grad.astype(BF16)
    width = total_ref.shape[1]
    total_ref[...] += dot(low_ref[...], win_ref[step].reshape(2 * LANES, width), 1, 0)

    @pl.when(step == pl.num_programs(0) - 1)
    def _():
        total = total_ref[...]
        dnormed_ref[...] = total.astype(BF16)
        x = x_ref[...].astype(F32)
        unit = x * lax.rsqrt(jnp.mean(x * x, axis=1, keepdims=True) + EPSILON)
        vec_ref[taps + 3 : taps + 4, :] = jnp.sum(total * unit, axis=0, keepdims=True)
        is_gain = lax.broadcasted_iota(jnp.int32, (8, LANES), 0) == taps + 3
        for chunk in range(chunks):
            start = pack_row(chunk)
            vec = vec_ref[:, chunk * LANES : (chunk + 1) * LANES]
            far, farther = (pltpu.roll(vec, LANES - k * edge // 2, 1) for k in (1, 2))
            even = jnp.where(is_gain & (lane >= edge // 2), far, vec)
            odd = jnp.where(is_gain & (lane < edge // 2), far, farther)
            alog = [
                alog_ref[pl.ds(q * eighth * chunks + chunk, eighth, stride=chunks), :]
                for q in range(2)
            ]
            place_pair(
                start,
                16,
                slice(5 * LANES, 6 * LANES),
                jnp.concatenate([alog[0], even]),
                jnp.concatenate([alog[1], odd]),
            )
            blank = jnp.zeros((16, 2 * LANES), F32)
            place_pair(start, 16, slice(6 * LANES, 8 * LANES), blank, blank)


def tail(
    place,
    lengths,
    code_own,
    code_other,
    sact,
    dpre,
    alog,
    back,
    dtx,
    bc_own,
    bc_other,
    decay,
    dy,
    conved,
    inner,
    act,
    high,
    convw,
    skip,
    normed,
    w4,
    gate_part,
    x,
):
    rows, own = act.shape
    chunks = own // LANES
    width = normed.shape[1]
    micros, _, clusters = lengths.shape
    count = rows // micros
    taps = convw.shape[0]
    ranks = dtx.shape[0]
    states = decay.shape[0] // chunks
    cols = 2 * LANES
    extent = 4 * (LANES + 32)

    def by_cols(height):
        return pl.BlockSpec((height, cols), lambda i, p: (0, i ^ p[FACE]))

    def dy_spec(micro):
        return pl.BlockSpec(
            (2 * count, LANES), lambda i, p: (micro * (chunks // 2) + (i ^ p[FACE]), 0)
        )

    in_specs = (
        [pl.BlockSpec(memory_space=pltpu.SMEM)]
        + [whole((rows, LANES))] * 2
        + [by_cols(rows)] * 2
        + [whole(alog.shape), whole(back.shape)]
        + [whole(array.shape) for array in (dtx, bc_own, bc_other, decay)]
        + [dy_spec(micro) for micro in range(micros)]
        + [by_cols(rows)] * 3
        + [whole(array.shape) for array in (high, convw, skip, normed)]
        + [
            ANY,
            whole((rows, width)),
            whole((rows, width)),
        ]
    )
    return pl.pallas_call(
        functools.partial(
            tail_kernel,
            micros=micros,
            count=count,
            taps=taps,
            clusters=clusters,
            ranks=ranks,
            chunks=chunks,
            states=states,
        ),
        grid_spec=pltpu.PrefetchScalarGridSpec(
            num_scalar_prefetch=1,
            grid=(chunks // 2,),
            in_specs=in_specs,
            out_specs=[whole((extent, width)), whole((extent, width)), whole((rows, width))],
            scratch_shapes=[
                pltpu.VMEM((taps, rows, LANES), F32),
                pltpu.VMEM((rows, LANES), BF16),
                pltpu.VMEM((LANES, cols), BF16),
                pltpu.VMEM((8, own), F32),
                pltpu.VMEM((states * chunks, LANES), F32),
                pltpu.VMEM((rows, width), F32),
                pltpu.VMEM((chunks // 2, 2, LANES, width), BF16),
                pltpu.SemaphoreType.DMA((chunks // 2,)),
                pltpu.VMEM((rows, cols), BF16),
                pltpu.VMEM((LANES, rows), BF16),
                pltpu.VMEM((2 * ranks, rows), BF16),
            ],
        ),
        out_shape=[
            hbm((extent, width), BF16),
            hbm((extent, width), BF16),
            hbm((rows, width), BF16),
        ],
        compiler_params=params(34),
        cost_estimate=cost(7),
        name="tail",
    )(
        place,
        lengths,
        *in_hbm([code_own]),
        code_other,
        *in_hbm(
            (
                sact,
                dpre,
                alog,
                back,
                dtx,
                bc_own,
                bc_other,
                decay,
                *([dy] * micros),
                conved,
                inner,
                act,
                high,
                convw,
                skip,
                normed,
                w4,
                gate_part,
                x,
            )
        ),
    )


def fetch_halves(source, which, half, target_ref, sems):
    copies = []
    for k in range(target_ref.shape[0]):
        pair = pl.ds(2 * k, 2)
        block = source.at[pair, half] if which is None else source.at[which, pair, half]
        copies.append(pltpu.make_async_copy(block, target_ref.at[k], sems.at[k]))
    for copy in copies:
        copy.start()
    return copies


def products_kernel(
    place_ref,
    gated_ref,
    dgate_ref,
    out_ref,
    weight_ref,
    mixed_ref,
    dnormed_ref,
    wout_ref,
    wgate_ref,
    out_sems,
    gate_sems,
):
    half = place_ref[HALF]
    width = mixed_ref.shape[1]
    jobs = (
        (fetch_halves(out_ref, None, half, wout_ref, out_sems), gated_ref, wout_ref, mixed_ref),
        (fetch_halves(weight_ref, 1, half, wgate_ref, gate_sems), dgate_ref, wgate_ref, dnormed_ref),
    )
    for copies, left_ref, right_ref, result_ref in jobs:
        total = None
        for k, copy in enumerate(copies):
            copy.wait()
            left = left_ref[:, 2 * k * LANES : 2 * (k + 1) * LANES]
            term = dot(left, right_ref[k].reshape(-1, width), 1, 0)
            total = term if total is None else total + term
        result_ref[...] = total.astype(BF16)


def products(place, gated, dgate, wout3, w4):
    rows, own = gated.shape
    width = w4.shape[-1]
    pairs = own // (2 * LANES)
    return pl.pallas_call(
        products_kernel,
        grid_spec=pltpu.PrefetchScalarGridSpec(
            num_scalar_prefetch=1,
            grid=(1,),
            in_specs=[whole((rows, own)), whole((rows, own)), ANY, ANY],
            out_specs=[whole((rows, width))] * 2,
            scratch_shapes=[
                pltpu.VMEM((pairs, 2, LANES, width), BF16),
                pltpu.VMEM((pairs, 2, LANES, width), BF16),
                pltpu.SemaphoreType.DMA((pairs,)),
                pltpu.SemaphoreType.DMA((pairs,)),
            ],
        ),
        out_shape=[hbm((rows, width), BF16)] * 2,
        compiler_params=params(20),
        cost_estimate=cost(4),
        name="products",
    )(place, *in_hbm((gated, dgate, wout3, w4)))


def finish_kernel(x_ref, mine_ref, theirs_ref, cotan_ref, gain_ref, grad_ref):
    x = x_ref[...].astype(F32)
    scale = lax.rsqrt(jnp.mean(x * x, axis=1, keepdims=True) + EPSILON)
    unit = x * scale
    dhat = (mine_ref[...].astype(F32) + theirs_ref[...].astype(F32)) * gain_ref[...]
    grad_ref[...] = cotan_ref[...].astype(F32) + scale * (
        dhat - unit * jnp.mean(dhat * unit, axis=1, keepdims=True)
    )


def finish(x, mine, theirs, cotan, gain):
    rows, width = x.shape
    by_rows = pl.BlockSpec((rows // 4, width), lambda i: (i, 0))
    return pl.pallas_call(
        finish_kernel,
        grid=(4,),
        in_specs=[by_rows] * 4 + [whole(gain.shape)],
        out_specs=by_rows,
        out_shape=jax.ShapeDtypeStruct((rows, width), F32),
        compiler_params=params(16),
        cost_estimate=cost(0),
        name="finish",
    )(*in_hbm((x, mine)), theirs, *in_hbm((cotan, gain)))


def unpack_kernel(
    near_ref,
    far_ref,
    out_ref,
    dtx_ref,
    dt_ref,
    bc_ref,
    alog_ref,
    convw_ref,
    convb_ref,
    bias_ref,
    skip_ref,
    out_grad_ref,
    *,
    eighth,
    taps,
    edge,
):
    pack = near_ref[...].astype(F32) + far_ref[...].astype(F32)
    turned = jnp.concatenate([pack[:, k * LANES : (k + 1) * LANES] for k in range(4)]).T
    dtx_ref[...] = turned[:edge]
    dt_ref[...] = turned[edge:]
    rows = pack[:, 4 * LANES : 5 * LANES]
    bc_ref[0] = rows[:eighth]
    bc_ref[1] = rows[eighth:]
    rows = pack[:, 5 * LANES : 6 * LANES]
    alog_ref[...] = rows[:eighth]
    vec = rows[eighth:, :edge]
    convw_ref[...] = vec[:taps]
    convb_ref[...] = vec[taps : taps + 1]
    bias_ref[...] = vec[taps + 1 : taps + 2]
    skip_ref[...] = vec[taps + 2 : taps + 3]
    out_grad_ref[...] = out_ref[...].astype(F32)


def unpack(near, far, out, eighth, taps, ranks):
    edge = LANES // 2
    shapes = [
        (edge, ranks),
        (edge, ranks),
        (2, eighth, LANES),
        (eighth, LANES),
        (taps, edge),
        (1, edge),
        (1, edge),
        (1, edge),
        out.shape,
    ]
    return pl.pallas_call(
        functools.partial(unpack_kernel, eighth=eighth, taps=taps, edge=edge),
        grid=(1,),
        in_specs=[whole(array.shape) for array in (near, far, out)],
        out_specs=[whole(shape) for shape in shapes],
        out_shape=[jax.ShapeDtypeStruct(shape, F32) for shape in shapes],
        cost_estimate=cost(0),
        name="unpack",
    )(near, far, out)


def swap_pair(array):
    count = lax.axis_size("state")
    return lax.ppermute(array, "state", [(pos, pos ^ 1) for pos in range(count)])


def swap_bit(array, bits):
    return lax.ppermute(array, "dp", [(pos, pos ^ bits) for pos in range(lax.axis_size("dp"))])


def swap_both(array, bits=0):
    states = lax.axis_size("state")
    pairs = []
    for d in range(lax.axis_size("dp")):
        for s in range(states):
            pairs.append((d * states + s, (((d & ~1) | s) ^ bits) * states + (d & 1)))
    return lax.ppermute(array, ("dp", "state"), pairs)


def add_mixed(x, mine, theirs):
    return (x.astype(F32) + (mine.astype(F32) + theirs.astype(F32))).astype(BF16)


def add_quarters(kept, got, start=0, stop=None):
    extent = kept.shape[0] // 4
    stop = extent if stop is None else stop
    return [
        kept[k * extent + start : k * extent + stop] + got[k * extent + start : k * extent + stop]
        for k in range(4)
    ]


def trade_quarters(quarters):
    return [quarters[0]] + [swap_bit(quarters[k], k * X_BIT) for k in range(1, 4)]


def sum_quarters(quarters):
    left, right = (quarters[k].astype(F32) + quarters[k + 1].astype(F32) for k in (0, 2))
    return (left + right).astype(BF16)


CORE_BIT, X_BIT, ZH_BIT = 1, 2, 8


def shards(
    tokens,
    cluster_len,
    norm_gain,
    in_weight,
    conv_weight,
    conv_bias,
    dtx_weight,
    dt_weight,
    dt_bias,
    bc_weight,
    a_log,
    skip_gain,
    out_weight,
    cotangent,
):
    micros, count, width = tokens.shape
    inner = out_weight.shape[0]
    taps = conv_weight.shape[0]
    ranks = dtx_weight.shape[1]
    chunks = inner // (2 * LANES)
    own = chunks * LANES
    rows = micros * count
    edge = LANES // 2
    span = LANES + 32
    dp_parts = lax.axis_size("dp")
    state_count = lax.axis_size("state")
    dp_pos = lax.axis_index("dp")
    state_pos = lax.axis_index("state")
    half = state_pos & 1
    fast = state_count == 2 and dp_parts == 2 * chunks == 16
    if fast:
        place = jnp.stack([half, dp_pos & 1, dp_pos >> 1, (dp_pos >> 1) & 3])
        bc_own, alog_own = bc_weight, a_log
        bc_other, alog_other = swap_pair(bc_weight), swap_pair(a_log)
    else:
        place = jnp.stack([half, 0, 0, 0])
        bc_all = lax.all_gather(bc_weight, "state", axis=1, tiled=True)
        alog_all = lax.all_gather(a_log, "state", axis=0, tiled=True)
        eighth = alog_all.shape[0] // 2
        bc_own, bc_other = (
            lax.dynamic_slice_in_dim(bc_all, which * eighth, eighth, 1)
            for which in (half, 1 - half)
        )
        alog_own, alog_other = (
            lax.dynamic_slice_in_dim(alog_all, which * eighth, eighth, 0)
            for which in (half, 1 - half)
        )
    place = place.astype(jnp.int32)
    eighth = alog_own.shape[0]
    states = 2 * eighth

    x = tokens.reshape(rows, width)
    cotan = cotangent.reshape(rows, width)
    w4 = in_weight.reshape(2, chunks, 2, LANES, width)
    wout3 = out_weight.reshape(chunks, 2, LANES, width)
    dtx, dt = dtx_weight.T, dt_weight.T
    bias = dt_bias.reshape(-1, LANES)
    skip = skip_gain.reshape(-1, LANES)

    normed, act_all, act, inner_own, conved, gate = project(
        place, cluster_len, x, norm_gain[None], w4, conv_weight, conv_bias.reshape(-1, LANES)
    )
    bc, rank, high, decay, sp, u, step, slope, h, dy, gated, dgate, keep, send = scan_forward(
        place,
        cluster_len,
        act_all,
        bc_own,
        bc_other,
        alog_own,
        alog_other,
        dtx,
        dt,
        bias,
        skip,
        act,
        gate,
        wout3,
        cotan,
        normed,
    )
    if fast:
        early = swap_bit(send, CORE_BIT)
    mixed_part, dn_gate = products(place, gated, dgate, wout3, w4)
    if fast:
        *quarters, mixed_part, dn_gate, sp = lax.optimization_barrier(
            (*add_quarters(keep, early), mixed_part, dn_gate, sp)
        )
        early_got = trade_quarters(quarters)
    code_own, sact, dpre, alog, back = scan_backward(
        place, micros, bc, decay, dt, act, sp, u, step, slope, dy, h
    )
    if fast:
        *early_got, code_own, mixed_part = lax.optimization_barrier(
            (*early_got, code_own, mixed_part)
        )
    code_other = swap_pair(code_own)
    mixed_other = swap_pair(mixed_part)
    if fast:
        block = sum_quarters(early_got)
        out_keep, out_send, gate_sum = block[:edge], block[edge:LANES], block[LANES:]
        out_send, gate_sum, conved = lax.optimization_barrier((out_send, gate_sum, conved))
        out_got = swap_bit(out_send, ZH_BIT)
    late_keep, late_send, dnormed_part = tail(
        place,
        cluster_len,
        code_own,
        code_other,
        sact,
        dpre,
        alog,
        back,
        dtx,
        bc_own,
        bc_other,
        decay,
        dy,
        conved,
        inner_own,
        act,
        high,
        conv_weight,
        skip,
        normed,
        w4,
        dn_gate,
        x,
    )
    mixed = add_mixed(x, mixed_part, mixed_other)
    if fast:
        late_send, mixed_other, out_got = lax.optimization_barrier(
            (late_send, mixed_other, out_got)
        )
        mixed = add_mixed(x, mixed_part, mixed_other)
        late = swap_bit(late_send, CORE_BIT)
        late_got = trade_quarters(add_quarters(late_keep, late))
    dnormed_other = swap_pair(dnormed_part)
    tokens_grad = finish(x, dnormed_part, dnormed_other, cotan, norm_gain[None])
    if fast:
        out_own = swap_both(out_keep + out_got)
        *late_got, out_own, tokens_grad, mixed = lax.optimization_barrier(
            (*late_got, out_own, tokens_grad, mixed)
        )
        block = sum_quarters(late_got)
        inner_sum = block[:LANES]
        upper = dp_pos >= dp_parts // 2
        crossing = jnp.where(upper, inner_sum, gate_sum)
        first, second = crossing[:edge], crossing[edge:]
        first, pack_far, pack_near = lax.optimization_barrier(
            (first, block[-16:], block[LANES:-16])
        )
        pack_far = swap_both(pack_far, ZH_BIT)
        first_got = swap_bit(first, ZH_BIT)
        pack_near = swap_both(pack_near)
        first_got, pack_far, pack_near = lax.optimization_barrier((first_got, pack_far, pack_near))
        second_got = swap_bit(second, ZH_BIT)
        gain_mine = (
            pack_near[:, 5 * LANES : 6 * LANES].astype(F32)
            + pack_far[:, 5 * LANES : 6 * LANES].astype(F32)
        ).astype(BF16)
        gain_both = gain_mine[-1].astype(F32) + swap_bit(gain_mine, CORE_BIT)[-1].astype(F32)
        extent = width // (dp_parts * state_count)
        gain_grad = lax.dynamic_slice_in_dim(gain_both, (dp_pos & 1) * extent, extent, 0)
        (
            dtx_grad,
            dt_grad,
            bc_grad,
            alog_grad,
            convw_grad,
            convb_grad,
            bias_grad,
            skip_grad,
            out_own,
        ) = unpack(pack_near, pack_far, out_own, eighth, taps, ranks)
        convb_grad, bias_grad, skip_grad = (
            array[0] for array in (convb_grad, bias_grad, skip_grad)
        )
        second_got, dtx_grad, dt_grad, out_own = lax.optimization_barrier(
            (second_got, dtx_grad, dt_grad, out_own)
        )
        in_grad = jnp.where(upper, gate_sum, inner_sum).astype(F32) + jnp.concatenate(
            [first_got, second_got]
        ).astype(F32)
    mixed = mixed.reshape(micros, count, width)
    tokens_grad = tokens_grad.reshape(micros, count, width)

    if not fast:
        def total(array):
            return lax.psum(array.astype(F32), "dp")

        def both_rows(array):
            mine = array.reshape(chunks, 1, LANES, -1)
            other = swap_pair(mine)
            low = jnp.where(half == 0, mine, other)
            high = jnp.where(half == 0, other, mine)
            return jnp.concatenate([low, high], axis=1).reshape(2 * own, -1)

        every = dp_parts * state_count
        at = dp_pos * state_count + state_pos

        def cut_own(array):
            extent = array.shape[0] // every
            return lax.dynamic_slice_in_dim(array, at * extent, extent, 0)

        pair = total(jnp.stack([keep, send])).reshape(2, 2, 2, 2 * LANES, width)
        outs = pair[:, :, :, :LANES].reshape(2, 2, 2, 2, edge, width)
        outs = jnp.transpose(outs, (3, 1, 2, 0, 4, 5)).reshape(own, width)
        gates = jnp.moveaxis(pair[:, :, :, LANES:], 0, 2).reshape(own, width)
        pair = total(jnp.stack([late_keep, late_send])).reshape(2, 2, 2, span, width)
        inners = jnp.moveaxis(pair[:, :, :, :LANES], 0, 2).reshape(own, width)
        packs = pair[:, :, :, LANES:].reshape(2, 2, 2, 2, 16, width // LANES, LANES)
        packs = jnp.transpose(packs, (3, 1, 2, 0, 5, 4, 6)).reshape(chunks, 2, -1, 16, LANES)
        small = packs[:, :, :4].reshape(chunks, 2, ranks, 2, edge)
        small = both_rows(jnp.transpose(small, (0, 1, 4, 3, 2)).reshape(own, 2 * ranks))
        in_grad = cut_own(jnp.concatenate([both_rows(inners), both_rows(gates)]))
        out_own = cut_own(both_rows(outs))
        mine = cut_own(small)
        dtx_grad, dt_grad = mine[:, :ranks], mine[:, ranks:]
        vec_rows = jnp.swapaxes(packs[:, :, 5, eighth:, :edge], 2, 3).reshape(own, -1)
        gain_sum = vec_rows[:, -1].reshape(chunks, 2, 2, -1).swapaxes(1, 2).reshape(-1)
        gain_grad = cut_own(gain_sum + swap_pair(gain_sum))
        vec = cut_own(both_rows(vec_rows)).T
        state_rows = jnp.concatenate([packs[:, :, 4], packs[:, :, 5, :eighth]], axis=2)
        state_rows = state_rows.reshape(chunks, 2, 3, eighth, LANES)
        state_rows = jnp.transpose(state_rows, (0, 4, 2, 1, 3)).reshape(own, -1)
        extent = inner // dp_parts
        state_part = lax.dynamic_slice_in_dim(both_rows(state_rows), dp_pos * extent, extent, 0)
        state_part = state_part.T.reshape(3, state_count, -1, extent)
        state_part = lax.dynamic_index_in_dim(state_part, state_pos, 1, keepdims=False)
        bc_grad, alog_grad = state_part[:2], state_part[2]
        convw_grad, convb_grad, bias_grad, skip_grad = (
            vec[:taps], vec[taps], vec[taps + 1], vec[taps + 2]
        )

    return (
        mixed,
        tokens_grad,
        gain_grad,
        in_grad,
        convw_grad,
        convb_grad,
        dtx_grad,
        dt_grad,
        bias_grad,
        bc_grad,
        alog_grad,
        skip_grad,
        out_own,
    )


def solution(mesh):
    return jax.shard_map(
        shards,
        mesh=mesh,
        in_specs=(
            P(None, "dp", None),
            P(None, "dp", None),
            P(),
            P(),
            P(),
            P(),
            P(),
            P(),
            P(),
            P(None, "state", None),
            P("state", None),
            P(),
            P(),
            P(None, "dp", None),
        ),
        out_specs=(
            P(None, "dp", None),
            P(None, "dp", None),
            P(("dp", "state")),
            P(("dp", "state"), None),
            P(None, ("dp", "state")),
            P(("dp", "state")),
            P(("dp", "state"), None),
            P(("dp", "state"), None),
            P(("dp", "state")),
            P(None, "state", "dp"),
            P("state", "dp"),
            P(("dp", "state")),
            P(("dp", "state"), None),
        ),
        check_vma=False,
    )
```

```python
import functools
import math

import jax
import jax.numpy as jnp
from jax import lax
from jax.experimental import pallas as pl
from jax.experimental.pallas import tpu as pltpu
from jax.sharding import PartitionSpec as P

EPSILON = 1e-05
LANES = 128
RESET = 1e4
LOG2E = math.log2(math.e)
F32 = jnp.float32
BF16 = jnp.bfloat16
MIB = 1024 * 1024


def dot(left, right, left_dim, right_dim):
    return lax.dot_general(
        left, right, (((left_dim,), (right_dim,)), ((), ())), preferred_element_type=F32
    )


def params(mib):
    return pltpu.CompilerParams(
        vmem_limit_bytes=mib * MIB, dimension_semantics=("arbitrary",)
    )


ANY = pl.BlockSpec(memory_space=pl.ANY)


def stream(step, steps, fetch):
    @pl.when(step == 0)
    def _():
        for k in range(steps):
            for copy in fetch(k):
                copy.start()

    for copy in fetch(step):
        copy.wait()


def whole(shape):
    return pl.BlockSpec(shape, lambda *_: (0,) * len(shape))


sigmoid = jax.nn.sigmoid


def log_one_plus(value):
    series = value * (1.0 - value * (0.5 - value * (1.0 / 3.0)))
    return jnp.where(value < 1e-3, series, jnp.log(1.0 + value))


def lanes(index):
    return pl.ds(pl.multiple_of(index * LANES, LANES), LANES)


def cost(micros):
    return pl.CostEstimate(
        flops=int(micros * 1e9), bytes_accessed=int(micros * 1e6), transcendentals=0
    )


def hbm(shape, dtype):
    return pltpu.HBM(shape, dtype)


def in_hbm(arrays):
    return [pltpu.with_memory_space_constraint(array, pltpu.HBM) for array in arrays]


def aligned(start, size, to=8):
    return pl.ds(pl.multiple_of(start, to), size)


SEGMENTS = 4

HALF, CORE, CUBE, FACE = range(4)


def fill_masks(len_ref, mask_ref, micros, count, taps, clusters):
    place = lax.broadcasted_iota(jnp.int32, (count, LANES), 0)
    for micro in range(micros):
        rows = pl.ds(micro * count, count)
        for back in range(1, taps):
            apart = place < back
            start = 0
            for cluster in range(clusters - 1):
                start = start + len_ref[micro, 0, cluster]
                apart = apart | ((place >= start) & (place < start + back))
            mask_ref[back, rows, :] = jnp.where(apart, 0.0, 1.0)
            if back == 1:
                mask_ref[0, rows, :] = jnp.where(apart, 1.0, 0.0)


def project_kernel(
    place_ref,
    len_ref,
    gain_ref,
    convw_ref,
    convb_ref,
    x_far,
    weight_far,
    normed_far,
    act_far,
    own_act_far,
    inner_far,
    bend_far,
    gate_far,
    mask_ref,
    x_ref,
    win_ref,
    wgate_ref,
    normed_ref,
    act_ref,
    own_act_ref,
    inner_ref,
    bend_ref,
    gate_ref,
    in_sems,
    out_sems,
    *,
    micros,
    count,
    taps,
    clusters,
):
    half = place_ref[HALF]
    chunks = win_ref.shape[0]
    inward = [pltpu.make_async_copy(x_far, x_ref, in_sems.at[2 * chunks])]
    for k in range(chunks):
        inward.append(pltpu.make_async_copy(weight_far.at[0, k], win_ref.at[k], in_sems.at[2 * k]))
        inward.append(
            pltpu.make_async_copy(
                weight_far.at[1, k, half], wgate_ref.at[k], in_sems.at[2 * k + 1]
            )
        )
    for copy in inward:
        copy.start()
    outward = []

    def put(source, target):
        outward.append(pltpu.make_async_copy(source, target, out_sems.at[len(outward)]))
        outward[-1].start()

    fill_masks(len_ref, mask_ref, micros, count, taps, clusters)
    inward[0].wait()
    rows = x_ref[...].astype(F32)
    scale = lax.rsqrt(jnp.mean(rows * rows, axis=1, keepdims=True) + EPSILON)
    normed = (rows * scale * gain_ref[...]).astype(BF16)
    normed_ref[...] = normed
    put(normed_ref, normed_far)
    for k in range(chunks):
        inward[2 * k + 1].wait()
        inward[2 * k + 2].wait()
        proj = dot(normed, win_ref[k].reshape(2 * LANES, -1), 1, 1)
        own = slice(k * LANES, (k + 1) * LANES)
        gate_ref[:, own] = dot(normed, wgate_ref[k], 1, 1)
        inners, sigs, acts = [], [], []
        for part in range(2):
            cols = slice((2 * k + part) * LANES, (2 * k + part + 1) * LANES)
            inner = proj[:, part * LANES : (part + 1) * LANES]
            conved = convb_ref[2 * k + part : 2 * k + part + 1, :]
            conved = conved + convw_ref[taps - 1 : taps, cols] * inner
            for back in range(1, taps):
                shifted = pltpu.roll(inner, back, 0) * mask_ref[back]
                conved = conved + convw_ref[taps - 1 - back : taps - back, cols] * shifted
            sig = sigmoid(conved)
            act = conved * sig
            act_ref[:, cols] = act.astype(BF16)
            inners.append(inner)
            sigs.append(sig)
            acts.append(act)
        inner_ref[:, own] = jnp.where(half == 0, *inners)
        act, sig = jnp.where(half == 0, *acts), jnp.where(half == 0, *sigs)
        bend_ref[:, own] = (sig + act * (1.0 - sig)).astype(BF16)
        own_act_ref[:, own] = act.astype(BF16)
        if k % 2:
            group = pl.ds((k - 1) * LANES, 2 * LANES)
            wide = pl.ds(2 * (k - 1) * LANES, 4 * LANES)
            put(act_ref.at[:, wide], act_far.at[:, wide])
            for near, far in (
                (gate_ref, gate_far),
                (inner_ref, inner_far),
                (bend_ref, bend_far),
                (own_act_ref, own_act_far),
            ):
                put(near.at[:, group], far.at[:, group])
    for copy in outward:
        copy.wait()


def project(place, lengths, x, gain, w4, conv_weight, conv_bias):
    rows, width = x.shape
    chunks = w4.shape[1]
    micros, _, clusters = lengths.shape
    taps = conv_weight.shape[0]
    own = chunks * LANES
    outs = [
        ((rows, width), BF16),
        ((rows, 2 * own), BF16),
        ((rows, own), BF16),
        ((rows, own), F32),
        ((rows, own), BF16),
        ((rows, own), F32),
    ]
    return pl.pallas_call(
        functools.partial(
            project_kernel, micros=micros, count=rows // micros, taps=taps, clusters=clusters
        ),
        grid_spec=pltpu.PrefetchScalarGridSpec(
            num_scalar_prefetch=1,
            grid=(1,),
            in_specs=[
                pl.BlockSpec(memory_space=pltpu.SMEM),
                whole(gain.shape),
                whole(conv_weight.shape),
                whole(conv_bias.shape),
                ANY,
                ANY,
            ],
            out_specs=[ANY] * len(outs),
            scratch_shapes=[
                pltpu.VMEM((taps, rows, LANES), F32),
                pltpu.VMEM((rows, width), BF16),
                pltpu.VMEM((chunks, 2, LANES, width), BF16),
                pltpu.VMEM((chunks, LANES, width), BF16),
            ]
            + [pltpu.VMEM(*out) for out in outs]
            + [
                pltpu.SemaphoreType.DMA((2 * chunks + 1,)),
                pltpu.SemaphoreType.DMA((1 + 5 * chunks // 2,)),
            ],
        ),
        out_shape=[hbm(*out) for out in outs],
        compiler_params=params(30),
        cost_estimate=cost(6),
        name="project",
    )(place, *in_hbm((lengths, gain, conv_weight, conv_bias, x, w4)))


def every_row(ref, row, height):
    return ref[pl.ds(row, height, stride=0), :]


def b_at(n, eighth):
    return (n // eighth) * 2 * eighth + n % eighth


def c_at(n, eighth):
    return b_at(n, eighth) + eighth


def forward_kernel(
    place_ref,
    len_ref,
    act_all_ref,
    bc_own_ref,
    bc_other_ref,
    alog_own_ref,
    alog_other_ref,
    dtx_ref,
    dt_ref,
    bias_ref,
    skip_ref,
    act_ref,
    *refs,
    micros,
    count,
    states,
    chunks,
    clusters,
):
    gate_far, wout_far, cotan_far, normed_far = refs[:4]
    bc_ref, rank_ref, rank_high_ref, decay_ref = refs[4:8]
    sp_far, u_far, step_far, slope_far, h_far, dy_far = refs[8:14]
    gated_far, dgate_far, keep_far, send_far = refs[14:18]
    mask_ref, y_ref, tmp_ref, wide_ref = refs[18:22]
    gate_ref, wout_ref, cotan_ref, normed_ref = refs[22:26]
    sp_ref, u_ref, step_ref, slope_ref, h_ref, dy_ref = refs[26:32]
    gated_ref, dgate_ref, keep_ref, send_ref = refs[32:36]
    in_sems, out_sems = refs[36:]
    rows = micros * count
    eighth = states // 2
    half, core, cube, face = (place_ref[k] for k in range(4))
    first = half == 0
    inward = [
        pltpu.make_async_copy(source, target, in_sems.at[k])
        for k, (source, target) in enumerate(
            (
                (gate_far, gate_ref),
                (wout_far.at[:, half], wout_ref),
                (cotan_far, cotan_ref),
                (normed_far, normed_ref),
            )
        )
    ]
    for copy in inward:
        copy.start()
    outward = []

    def put(source, target):
        outward.append(pltpu.make_async_copy(source, target, out_sems.at[len(outward)]))
        outward[-1].start()

    ranks = dtx_ref.shape[0]
    weights = jnp.concatenate(
        [dtx_ref[...]] + [ref[...].reshape(states, -1) for ref in (bc_own_ref, bc_other_ref)]
    )
    product = dot(act_all_ref[...], weights, 1, 1)
    own, other = product[:, ranks : ranks + states], product[:, ranks + states :]
    bc_ref[:, :states] = jnp.where(first, own, other)
    bc_ref[:, states:] = jnp.where(first, other, own)
    spread_lanes(bc_ref, wide_ref)

    fill_masks(len_ref, mask_ref, micros, count, 2, clusters)
    for chunk in range(chunks):
        cols = lanes(2 * chunk + half)
        own, other = alog_own_ref[:, cols], alog_other_ref[:, cols]
        tmp_ref[pl.ds(chunk * states, eighth), :] = jnp.where(first, own, other)
        tmp_ref[pl.ds(chunk * states + eighth, eighth), :] = jnp.where(first, other, own)
    for n in range(states):
        decay_ref[pl.ds(n * chunks, chunks), :] = -LOG2E * jnp.exp(
            tmp_ref[pl.ds(n, chunks, stride=states), :]
        )

    rank = product[:, :ranks].astype(BF16)
    rank_ref[...] = rank
    rank_high_ref[...] = jnp.concatenate([jnp.zeros_like(rank), rank], axis=1)
    for chunk in range(chunks):
        cols = slice(chunk * LANES, (chunk + 1) * LANES)
        bias = bias_ref[pl.ds(2 * chunk + half, 1), :]
        pre = dot(rank, dt_ref[:, lanes(2 * chunk + half)], 1, 0) + bias
        tail_part = jnp.exp(-jnp.abs(pre))
        step = jnp.maximum(pre, 0.0) + log_one_plus(tail_part)
        slope = jnp.where(pre >= 0.0, 1.0, tail_part) / (1.0 + tail_part)
        step_ref[:, cols] = step
        slope_ref[:, cols] = slope.astype(BF16)
        held = step + RESET * mask_ref[0]
        source = step * act_ref[:, cols].astype(F32)
        for micro in range(micros):
            span = slice(micro * count, (micro + 1) * count)
            place = pl.ds((micro * chunks + chunk) * count, count)
            sp_ref[place, :] = held[span]
            u_ref[place, :] = source[span]
    put(sp_ref, sp_far)
    put(u_ref, u_far)
    put(step_ref, step_far)
    put(slope_ref, slope_far)

    for micro in range(micros):

        def advance(t, h, micro=micro):
            row = micro * count + t
            span = pl.ds(micro * chunks * count + t, chunks, stride=count)
            sp = sp_ref[span, :]
            u = u_ref[span, :]
            out = []
            y = None
            for n in range(states):
                decay = jnp.exp2(sp * decay_ref[pl.ds(n * chunks, chunks), :])
                now = decay * h[n] + u * every_row(wide_ref, b_at(n, eighth) * rows + row, chunks)
                h_ref[aligned((row * states + n) * chunks, chunks), :] = now
                out.append(now)
                term = now * every_row(wide_ref, c_at(n, eighth) * rows + row, chunks)
                y = term if y is None else y + term
            y_ref[span, :] = y
            return tuple(out)

        h = (jnp.zeros((chunks, LANES), F32),) * states
        segment = count // SEGMENTS
        for k in range(SEGMENTS):
            h = lax.fori_loop(k * segment, (k + 1) * segment, advance, h, unroll=8)
            extent = segment * states * chunks
            place = pl.ds((micro * SEGMENTS + k) * extent, extent)
            put(h_ref.at[place], h_far.at[place])

    for copy in inward:
        copy.wait()
    cotan = cotan_ref[...]
    for chunk in range(chunks):
        cols = slice(chunk * LANES, (chunk + 1) * LANES)
        places = [pl.ds((micro * chunks + chunk) * count, count) for micro in range(micros)]
        y = jnp.concatenate([y_ref[place, :] for place in places])
        y = y + skip_ref[pl.ds(2 * chunk + half, 1), :] * act_ref[:, cols].astype(F32)
        gate = gate_ref[:, cols]
        sig = sigmoid(gate)
        gated_ref[:, cols] = (y * (gate * sig)).astype(BF16)
        dgated = dot(cotan, wout_ref[chunk], 1, 1)
        dy = dgated * (gate * sig)
        for micro in range(micros):
            dy_ref[places[micro], :] = dy[micro * count : (micro + 1) * count]
        dgate_ref[:, cols] = (dgated * y * (sig * (1.0 + gate * (1.0 - sig)))).astype(BF16)
    put(dy_ref, dy_far)
    put(gated_ref, gated_far)
    put(dgate_ref, dgate_far)
    normed = normed_ref[...]
    edge = LANES // 2
    for r in range(chunks // 2):
        for zh in range(2):
            grad = dot(gated_ref[:, lanes((r + 4 * zh) ^ cube)], cotan, 0, 0).astype(BF16)
            top, bottom = grad[:edge], grad[edge:]
            place = pl.ds(r * 2 * LANES + zh * edge, edge)
            keep_ref[place, :] = jnp.where(core == 0, top, bottom)
            send_ref[place, :] = jnp.where(core == 0, bottom, top)
        place = pl.ds((2 * r + 1) * LANES, LANES)
        pair = 2 * (r ^ face)
        for chunk, out_ref in ((pair + core, keep_ref), (pair + 1 - core, send_ref)):
            out_ref[place, :] = dot(dgate_ref[:, lanes(chunk)], normed, 0, 0).astype(BF16)
        place = pl.ds(r * 2 * LANES, 2 * LANES)
        put(send_ref.at[place], send_far.at[place])
        put(keep_ref.at[place], keep_far.at[place])
    for copy in outward:
        copy.wait()


def scan_forward(
    place,
    lengths,
    act_all,
    bc_own,
    bc_other,
    alog_own,
    alog_other,
    dtx,
    dt,
    bias,
    skip,
    act,
    gate,
    wout3,
    cotan,
    normed,
):
    rows, own = act.shape
    chunks = own // LANES
    states = 2 * alog_own.shape[0]
    width = cotan.shape[1]
    micros, _, clusters = lengths.shape
    ranks = dtx.shape[0]
    small = [
        ((rows, 2 * states), F32),
        ((rows, ranks), BF16),
        ((rows, 2 * ranks), BF16),
        ((states * chunks, LANES), F32),
    ]
    large = [
        ((chunks * rows, LANES), F32),
        ((chunks * rows, LANES), F32),
        ((rows, own), F32),
        ((rows, own), BF16),
        ((rows * states * chunks, LANES), F32),
        ((chunks * rows, LANES), F32),
        ((rows, own), BF16),
        ((rows, own), BF16),
        ((own, width), BF16),
        ((own, width), BF16),
    ]
    operands = (act_all, bc_own, bc_other, alog_own, alog_other, dtx, dt, bias, skip, act)
    streamed = (gate, wout3, cotan, normed)
    return pl.pallas_call(
        functools.partial(
            forward_kernel,
            micros=micros,
            count=rows // micros,
            states=states,
            chunks=chunks,
            clusters=clusters,
        ),
        grid_spec=pltpu.PrefetchScalarGridSpec(
            num_scalar_prefetch=1,
            grid=(1,),
            in_specs=[pl.BlockSpec(memory_space=pltpu.SMEM)]
            + [whole(operand.shape) for operand in operands]
            + [ANY] * len(streamed),
            out_specs=[whole(shape) for shape, _ in small] + [ANY] * len(large),
            scratch_shapes=[
                pltpu.VMEM((2, rows, LANES), F32),
                pltpu.VMEM((chunks * rows, LANES), F32),
                pltpu.VMEM((states * chunks, LANES), F32),
                pltpu.VMEM((2 * states * rows, LANES), F32),
                pltpu.VMEM((rows, own), F32),
                pltpu.VMEM((chunks, LANES, width), BF16),
                pltpu.VMEM((rows, width), BF16),
                pltpu.VMEM((rows, width), BF16),
            ]
            + [pltpu.VMEM(*out) for out in large]
            + [pltpu.SemaphoreType.DMA((4,)), pltpu.SemaphoreType.DMA((7 + chunks + micros * SEGMENTS,))],
        ),
        out_shape=[hbm(*out) for out in small + large],
        compiler_params=params(52),
        cost_estimate=cost(19),
        name="scan_forward",
    )(
        place,
        lengths,
        *in_hbm(operands[:1]),
        *operands[1:5],
        *in_hbm((*operands[5:], *streamed)),
    )


def spread_lanes(values_ref, wide_ref):
    rows, count = values_ref.shape
    for k in range(count):
        wide_ref[pl.ds(k * rows, rows), :] = jnp.broadcast_to(
            values_ref[:, k : k + 1], (rows, LANES)
        )


def backward_kernel(
    place_ref,
    bc_ref,
    decay_ref,
    dt_ref,
    skip_ref,
    act_ref,
    sp_ref,
    u_ref,
    step_ref,
    slope_ref,
    dy_ref,
    h_far,
    code_ref,
    sact_ref,
    dpre_ref,
    alog_ref,
    vec_ref,
    h_ref,
    s_ref,
    d_ref,
    terms_ref,
    sums_b_ref,
    sums_c_ref,
    wide_ref,
    sems,
    *,
    count,
    states,
    chunks,
):
    micro = pl.program_id(0)
    block = states * chunks
    segment = count // SEGMENTS

    def fetch(which, k):
        extent = segment * block
        buffer = h_ref.at[which % 2]
        return pltpu.make_async_copy(
            h_far.at[aligned((which * SEGMENTS + k) * extent, extent)],
            buffer.at[pl.ds(block + k * extent, extent)],
            sems.at[which % 2, k],
        )

    @pl.when(micro == 0)
    def _():
        for k in reversed(range(SEGMENTS)):
            fetch(0, k).start()
        for which in range(2):
            h_ref[which, pl.ds(0, block), :] = jnp.zeros((block, LANES), F32)
        alog_ref[...] = jnp.zeros_like(alog_ref)
        vec_ref[...] = jnp.zeros_like(vec_ref)

    half = place_ref[HALF]
    eighth = states // 2
    zero = (jnp.zeros((chunks, LANES), F32),) * states
    spread_lanes(bc_ref, wide_ref)

    @pl.when(micro + 1 < pl.num_programs(0))
    def _():
        for k in reversed(range(SEGMENTS)):
            fetch(micro + 1, k).start()

    side = micro % 2

    def put_terms(which, t, terms):
        for n in range(0, states, 2):
            pair = jnp.concatenate(terms[n : n + 2]).astype(BF16)
            place = aligned(t * block + n * chunks, 2 * chunks, 16)
            terms_ref[which, place, :] = pair

    def retreat(back, carry):
        flows, totals = carry
        for slot in range(4):
            t = count - 1 - (4 * back + slot)
            span = pl.ds(t, chunks, stride=count)
            sp = sp_ref[span, :]
            u = u_ref[span, :]
            dy = dy_ref[span, :]
            out_flows = []
            out_totals = []
            b_terms, c_terms = [], []
            d_sum = None
            s_sum = None
            for n in range(states):
                rate = decay_ref[pl.ds(n * chunks, chunks), :]
                dh = flows[n] + dy * every_row(wide_ref, c_at(n, eighth) * count + t, chunks)
                flow = jnp.exp2(sp * rate) * dh
                out_flows.append(flow)
                q = flow * h_ref[side, aligned(t * block + n * chunks, chunks), :]
                now = h_ref[side, aligned((t + 1) * block + n * chunks, chunks), :]
                out_totals.append(totals[n] + q * sp)
                d_term = q * rate
                s_term = dh * every_row(wide_ref, b_at(n, eighth) * count + t, chunks)
                d_sum = d_term if d_sum is None else d_sum + d_term
                s_sum = s_term if s_sum is None else s_sum + s_term
                b_terms.append(dh * u)
                c_terms.append(dy * now)
            s_ref[span, :] = s_sum
            d_ref[span, :] = d_sum
            put_terms(0, t, b_terms)
            put_terms(1, t, c_terms)
            flows, totals = tuple(out_flows), tuple(out_totals)
        return flows, totals

    carry = (zero, zero)
    for k in range(SEGMENTS):
        fetch(micro, SEGMENTS - 1 - k).wait()
        carry = lax.fori_loop(k * segment // 4, (k + 1) * segment // 4, retreat, carry)
    totals = carry[1]
    for n in range(states):
        alog_ref[pl.ds(n * chunks, chunks), :] += totals[n]

    shape = (2 * states, 2 * block)
    group = lax.broadcasted_iota(jnp.int32, shape, 1) // chunks
    gather = jnp.where(group == lax.broadcasted_iota(jnp.int32, shape, 0), 1.0, 0.0).astype(BF16)

    @pl.loop(0, count // 64)
    def _(step):
        for which, sums_ref in ((0, sums_b_ref), (1, sums_c_ref)):
            for k in range(32):
                at = 32 * step + k
                terms = terms_ref[which, aligned(at * 2 * block, 2 * block, 16), :]
                sums_ref[aligned(at * 2 * states, 2 * states), :] = dot(gather, terms, 1, 0)

    ranks = dt_ref.shape[0]
    drank = None
    for chunk in range(chunks):
        cols = slice(chunk * LANES, (chunk + 1) * LANES)
        place = pl.ds(chunk * count, count)
        act = act_ref[:, cols].astype(F32)
        weight = dt_ref[:, lanes(2 * chunk + half)]
        s_now = s_ref[place, :]
        dstep = d_ref[place, :] * (1.0 / LOG2E) + s_now * act
        dy = dy_ref[place, :]
        skip = skip_ref[pl.ds(2 * chunk + half, 1), :]
        sact_ref[:, cols] = s_now * step_ref[:, cols] + dy * skip
        dpre = dstep * slope_ref[:, cols].astype(F32)
        vec_ref[0:1, cols] += jnp.sum(dpre, axis=0, keepdims=True)
        vec_ref[1:2, cols] += jnp.sum(dy * act, axis=0, keepdims=True)
        low = dpre.astype(BF16)
        dpre_ref[:, cols] = low
        term = dot(low, weight, 1, 1)
        drank = term if drank is None else drank + term
    source = lax.broadcasted_iota(jnp.int32, (2 * LANES, LANES), 0)
    target = lax.broadcasted_iota(jnp.int32, (2 * LANES, LANES), 1)
    code = None
    for n in range(states):
        pair = jnp.concatenate(
            [ref[pl.ds(n, count, stride=states), :] for ref in (sums_b_ref, sums_c_ref)], axis=1
        )
        column = ranks + jnp.where(source < LANES, b_at(n, eighth), c_at(n, eighth))
        pick = jnp.where(target == column, 1.0, 0.0).astype(BF16)
        term = dot(pair.astype(BF16), pick, 1, 0)
        code = term if code is None else code + term
    drank = jnp.concatenate([drank, jnp.zeros((count, LANES - ranks), F32)], axis=1)
    code_ref[...] = (code + drank).astype(BF16)


def scan_backward(place, micros, bc, decay, dt, skip, act, sp, u, step, slope, dy, h):
    rows, own = act.shape
    count = rows // micros
    chunks = own // LANES
    states = bc.shape[1] // 2
    outs = [
        ((rows, LANES), BF16),
        ((rows, own), F32),
        ((rows, own), BF16),
        ((states * chunks, LANES), F32),
        ((2, own), F32),
    ]

    def block(*shape):
        return pl.BlockSpec(shape, lambda i, p: (i, 0))

    return pl.pallas_call(
        functools.partial(backward_kernel, count=count, states=states, chunks=chunks),
        grid_spec=pltpu.PrefetchScalarGridSpec(
            num_scalar_prefetch=1,
            grid=(micros,),
            in_specs=[
                block(count, 2 * states),
                whole(decay.shape),
                whole(dt.shape),
                whole(skip.shape),
                block(count, own),
                block(chunks * count, LANES),
                block(chunks * count, LANES),
                block(count, own),
                block(count, own),
                block(chunks * count, LANES),
                ANY,
            ],
            out_specs=[block(count, LANES), block(count, own), block(count, own)]
            + [whole(shape) for shape, _ in outs[3:]],
            scratch_shapes=[
                pltpu.VMEM((2, (count + 1) * states * chunks, LANES), F32),
                pltpu.VMEM((chunks * count, LANES), F32),
                pltpu.VMEM((chunks * count, LANES), F32),
                pltpu.VMEM((2, count * states * chunks, LANES), BF16),
                pltpu.VMEM((count * states, LANES), F32),
                pltpu.VMEM((count * states, LANES), F32),
                pltpu.VMEM((2 * states * count, LANES), F32),
                pltpu.SemaphoreType.DMA((2, SEGMENTS)),
            ],
        ),
        out_shape=[hbm(*out) for out in outs],
        compiler_params=params(52),
        cost_estimate=cost(0),
        name="scan_backward",
    )(place, *in_hbm((bc, decay, dt, skip, act, sp, u, step, slope, dy, h)))


def tail_kernel(
    place_ref,
    len_ref,
    *refs,
    micros,
    count,
    taps,
    clusters,
    ranks,
    chunks,
    states,
):
    def take(number):
        nonlocal refs
        taken, refs = refs[:number], refs[number:]
        return taken

    code_own_ref, code_other_ref = take(2)
    sact_ref, dpre_ref, alog_sum_ref, back_ref = take(4)
    dtx_ref, bc_own_ref, bc_other_ref, decay_ref = take(4)
    bend_ref, inner_ref, act_ref, high_ref, convw_ref = take(5)
    normed_ref, weight_ref, gate_part_ref, x_ref = take(4)
    keep_ref, send_ref, dnormed_ref = take(3)
    mask_ref, code_ref, wcode_ref, vec_ref, alog_ref, total_ref, win_ref, sems, low_ref = refs[:9]
    code_turned_ref, rank_turned_ref = refs[9:]

    step = pl.program_id(0)
    rows = micros * count
    eighth = states // 2
    edge = LANES // 2
    half, core, cube, face = (place_ref[k] for k in range(4))
    pair = step ^ face
    span = LANES + 32

    def fetch(k):
        source = weight_ref.at[0, pl.ds(2 * (k ^ face), 2), half]
        return (pltpu.make_async_copy(source, win_ref.at[k], sems.at[k]),)

    stream(step, win_ref.shape[0], fetch)

    def pack_row(chunk):
        relative = chunk ^ cube
        return (relative & 3) * span + LANES + (relative >> 2) * 16

    def place_pair(start, size, cols, even, odd):
        keep_ref[aligned(start, size, 16), cols] = jnp.where(core == 0, even, odd).astype(BF16)
        send_ref[aligned(start, size, 16), cols] = jnp.where(core == 0, odd, even).astype(BF16)

    @pl.when(step == 0)
    def _():
        fill_masks(len_ref, mask_ref, micros, count, taps, clusters)
        total_ref[...] = gate_part_ref[...].astype(F32)
        code_ref[...] = (
            code_own_ref[...].astype(F32) + code_other_ref[...].astype(F32)
        ).astype(BF16)
        code_turned_ref[...] = code_ref[...].T
        rank_turned_ref[...] = high_ref[...].T
        alog_ref[...] = alog_sum_ref[...] * (decay_ref[...] * (1.0 / LOG2E))

    code = code_ref[...]
    lane = lax.broadcasted_iota(jnp.int32, (1, LANES), 1)
    for part in range(2):
        source = lanes(2 * (2 * pair + part) + half)
        cols = slice(part * LANES, (part + 1) * LANES)
        wcode_ref[:ranks, cols] = dtx_ref[:, source]
        own = bc_own_ref[:, :, source].reshape(states, LANES)
        other = bc_other_ref[:, :, source].reshape(states, LANES)
        wcode_ref[ranks : ranks + states, cols] = jnp.where(half == 0, own, other)
        wcode_ref[ranks + states : ranks + 2 * states, cols] = jnp.where(half == 0, other, own)
        wcode_ref[ranks + 2 * states :, cols] = jnp.zeros(
            (LANES - ranks - 2 * states, LANES), BF16
        )
    for part in range(2):
        cols = slice(part * LANES, (part + 1) * LANES)
        chunk = 2 * pair + part
        source = 2 * chunk + half
        weights = convw_ref[:, lanes(source)]
        dact = sact_ref[:, cols] + dot(code, wcode_ref[:, cols], 1, 0)
        dconv = dact * bend_ref[:, cols].astype(F32)
        inner = inner_ref[:, cols]
        dinner = weights[taps - 1 : taps] * dconv
        sums = [None] * (taps + 1)
        sums[taps - 1] = jnp.sum(dconv * inner, axis=0, keepdims=True)
        sums[taps] = jnp.sum(dconv, axis=0, keepdims=True)
        for back in range(1, taps):
            kept = dconv * mask_ref[back]
            dinner = dinner + weights[taps - 1 - back : taps - back] * pltpu.roll(
                kept, rows - back, 0
            )
            sums[taps - 1 - back] = jnp.sum(
                kept * pltpu.roll(inner, back, 0), axis=0, keepdims=True
            )
        for k in range(taps + 1):
            vec_ref[k : k + 1, lanes(chunk)] = sums[k]
        vec_ref[taps + 1 : taps + 3, lanes(chunk)] = back_ref[:, lanes(chunk)]
        low_ref[:, cols] = dinner.astype(BF16)

        act = act_ref[:, cols]
        start = pack_row(chunk)
        code_rows = dot(code_turned_ref[...], act, 1, 0)
        rank_rows = dot(rank_turned_ref[...], dpre_ref[:, cols], 1, 0)[ranks:]
        dtx_rows = code_rows[:ranks]
        even = jnp.where(lane < edge, dtx_rows, pltpu.roll(rank_rows, edge, 1))
        odd = jnp.where(lane < edge, pltpu.roll(dtx_rows, edge, 1), rank_rows)
        for k in range(4):
            place = slice(k * 16, (k + 1) * 16)
            place_pair(
                start, 16, slice(k * LANES, (k + 1) * LANES), even[place], odd[place]
            )
        state_rows = code_rows[ranks : ranks + 2 * states]
        place_pair(
            start, 16, slice(4 * LANES, 5 * LANES), state_rows[:states], state_rows[states:]
        )

    normed = normed_ref[...]
    for part in range(2):
        grad = dot(low_ref[:, lanes(core ^ part)], normed, 0, 0)
        out_ref = (keep_ref, send_ref)[part]
        out_ref[aligned(step * span, LANES, 16), :] = grad.astype(BF16)
    width = total_ref.shape[1]
    total_ref[...] += dot(low_ref[...], win_ref[step].reshape(2 * LANES, width), 1, 0)

    @pl.when(step == pl.num_programs(0) - 1)
    def _():
        total = total_ref[...]
        dnormed_ref[...] = total.astype(BF16)
        x = x_ref[...].astype(F32)
        unit = x * lax.rsqrt(jnp.mean(x * x, axis=1, keepdims=True) + EPSILON)
        vec_ref[taps + 3 : taps + 4, :] = jnp.sum(total * unit, axis=0, keepdims=True)
        is_gain = lax.broadcasted_iota(jnp.int32, (8, LANES), 0) == taps + 3
        for chunk in range(chunks):
            start = pack_row(chunk)
            vec = vec_ref[:, chunk * LANES : (chunk + 1) * LANES]
            far, farther = (pltpu.roll(vec, LANES - k * edge // 2, 1) for k in (1, 2))
            even = jnp.where(is_gain & (lane >= edge // 2), far, vec)
            odd = jnp.where(is_gain & (lane < edge // 2), far, farther)
            alog = [
                alog_ref[pl.ds(q * eighth * chunks + chunk, eighth, stride=chunks), :]
                for q in range(2)
            ]
            place_pair(
                start,
                16,
                slice(5 * LANES, 6 * LANES),
                jnp.concatenate([alog[0], even]),
                jnp.concatenate([alog[1], odd]),
            )
            blank = jnp.zeros((16, 2 * LANES), F32)
            place_pair(start, 16, slice(6 * LANES, 8 * LANES), blank, blank)


def tail(
    place,
    lengths,
    code_own,
    code_other,
    sact,
    dpre,
    alog,
    back,
    dtx,
    bc_own,
    bc_other,
    decay,
    bend,
    inner,
    act,
    high,
    convw,
    normed,
    w4,
    gate_part,
    x,
):
    rows, own = act.shape
    chunks = own // LANES
    width = normed.shape[1]
    micros, _, clusters = lengths.shape
    count = rows // micros
    taps = convw.shape[0]
    ranks = dtx.shape[0]
    states = decay.shape[0] // chunks
    cols = 2 * LANES
    extent = 4 * (LANES + 32)

    def by_cols(height):
        return pl.BlockSpec((height, cols), lambda i, p: (0, i ^ p[FACE]))

    in_specs = (
        [pl.BlockSpec(memory_space=pltpu.SMEM)]
        + [whole((rows, LANES))] * 2
        + [by_cols(rows)] * 2
        + [whole(alog.shape), whole(back.shape)]
        + [whole(array.shape) for array in (dtx, bc_own, bc_other, decay)]
        + [by_cols(rows)] * 3
        + [whole(array.shape) for array in (high, convw, normed)]
        + [
            ANY,
            whole((rows, width)),
            whole((rows, width)),
        ]
    )
    return pl.pallas_call(
        functools.partial(
            tail_kernel,
            micros=micros,
            count=count,
            taps=taps,
            clusters=clusters,
            ranks=ranks,
            chunks=chunks,
            states=states,
        ),
        grid_spec=pltpu.PrefetchScalarGridSpec(
            num_scalar_prefetch=1,
            grid=(chunks // 2,),
            in_specs=in_specs,
            out_specs=[whole((extent, width)), whole((extent, width)), whole((rows, width))],
            scratch_shapes=[
                pltpu.VMEM((taps, rows, LANES), F32),
                pltpu.VMEM((rows, LANES), BF16),
                pltpu.VMEM((LANES, cols), BF16),
                pltpu.VMEM((8, own), F32),
                pltpu.VMEM((states * chunks, LANES), F32),
                pltpu.VMEM((rows, width), F32),
                pltpu.VMEM((chunks // 2, 2, LANES, width), BF16),
                pltpu.SemaphoreType.DMA((chunks // 2,)),
                pltpu.VMEM((rows, cols), BF16),
                pltpu.VMEM((LANES, rows), BF16),
                pltpu.VMEM((2 * ranks, rows), BF16),
            ],
        ),
        out_shape=[
            hbm((extent, width), BF16),
            hbm((extent, width), BF16),
            hbm((rows, width), BF16),
        ],
        compiler_params=params(34),
        cost_estimate=cost(7),
        name="tail",
    )(
        place,
        lengths,
        *in_hbm([code_own]),
        code_other,
        *in_hbm(
            (
                sact,
                dpre,
                alog,
                back,
                dtx,
                bc_own,
                bc_other,
                decay,
                bend,
                inner,
                act,
                high,
                convw,
                normed,
                w4,
                gate_part,
                x,
            )
        ),
    )


def fetch_halves(source, which, half, target_ref, sems):
    copies = []
    for k in range(target_ref.shape[0]):
        pair = pl.ds(2 * k, 2)
        block = source.at[pair, half] if which is None else source.at[which, pair, half]
        copies.append(pltpu.make_async_copy(block, target_ref.at[k], sems.at[k]))
    for copy in copies:
        copy.start()
    return copies


def products_kernel(
    place_ref,
    gated_ref,
    dgate_ref,
    out_ref,
    weight_ref,
    mixed_ref,
    dnormed_ref,
    wout_ref,
    wgate_ref,
    out_sems,
    gate_sems,
):
    half = place_ref[HALF]
    width = mixed_ref.shape[1]
    jobs = (
        (fetch_halves(out_ref, None, half, wout_ref, out_sems), gated_ref, wout_ref, mixed_ref),
        (fetch_halves(weight_ref, 1, half, wgate_ref, gate_sems), dgate_ref, wgate_ref, dnormed_ref),
    )
    for copies, left_ref, right_ref, result_ref in jobs:
        total = None
        for k, copy in enumerate(copies):
            copy.wait()
            left = left_ref[:, 2 * k * LANES : 2 * (k + 1) * LANES]
            term = dot(left, right_ref[k].reshape(-1, width), 1, 0)
            total = term if total is None else total + term
        result_ref[...] = total.astype(BF16)


def products(place, gated, dgate, wout3, w4):
    rows, own = gated.shape
    width = w4.shape[-1]
    pairs = own // (2 * LANES)
    return pl.pallas_call(
        products_kernel,
        grid_spec=pltpu.PrefetchScalarGridSpec(
            num_scalar_prefetch=1,
            grid=(1,),
            in_specs=[whole((rows, own)), whole((rows, own)), ANY, ANY],
            out_specs=[whole((rows, width))] * 2,
            scratch_shapes=[
                pltpu.VMEM((pairs, 2, LANES, width), BF16),
                pltpu.VMEM((pairs, 2, LANES, width), BF16),
                pltpu.SemaphoreType.DMA((pairs,)),
                pltpu.SemaphoreType.DMA((pairs,)),
            ],
        ),
        out_shape=[hbm((rows, width), BF16)] * 2,
        compiler_params=params(20),
        cost_estimate=cost(4),
        name="products",
    )(place, *in_hbm((gated, dgate, wout3, w4)))


def finish_kernel(x_ref, mine_ref, theirs_ref, cotan_ref, gain_ref, grad_ref):
    x = x_ref[...].astype(F32)
    scale = lax.rsqrt(jnp.mean(x * x, axis=1, keepdims=True) + EPSILON)
    unit = x * scale
    dhat = (mine_ref[...].astype(F32) + theirs_ref[...].astype(F32)) * gain_ref[...]
    grad_ref[...] = cotan_ref[...].astype(F32) + scale * (
        dhat - unit * jnp.mean(dhat * unit, axis=1, keepdims=True)
    )


def finish(x, mine, theirs, cotan, gain):
    rows, width = x.shape
    by_rows = pl.BlockSpec((rows // 4, width), lambda i: (i, 0))
    return pl.pallas_call(
        finish_kernel,
        grid=(4,),
        in_specs=[by_rows] * 4 + [whole(gain.shape)],
        out_specs=by_rows,
        out_shape=jax.ShapeDtypeStruct((rows, width), F32),
        compiler_params=params(16),
        cost_estimate=cost(0),
        name="finish",
    )(*in_hbm((x, mine)), theirs, *in_hbm((cotan, gain)))


def unpack_kernel(
    near_ref,
    far_ref,
    out_ref,
    dtx_ref,
    dt_ref,
    bc_ref,
    alog_ref,
    convw_ref,
    convb_ref,
    bias_ref,
    skip_ref,
    out_grad_ref,
    *,
    eighth,
    taps,
    edge,
):
    pack = near_ref[...].astype(F32) + far_ref[...].astype(F32)
    turned = jnp.concatenate([pack[:, k * LANES : (k + 1) * LANES] for k in range(4)]).T
    dtx_ref[...] = turned[:edge]
    dt_ref[...] = turned[edge:]
    rows = pack[:, 4 * LANES : 5 * LANES]
    bc_ref[0] = rows[:eighth]
    bc_ref[1] = rows[eighth:]
    rows = pack[:, 5 * LANES : 6 * LANES]
    alog_ref[...] = rows[:eighth]
    vec = rows[eighth:, :edge]
    convw_ref[...] = vec[:taps]
    convb_ref[...] = vec[taps : taps + 1]
    bias_ref[...] = vec[taps + 1 : taps + 2]
    skip_ref[...] = vec[taps + 2 : taps + 3]
    out_grad_ref[...] = out_ref[...].astype(F32)


def unpack(near, far, out, eighth, taps, ranks):
    edge = LANES // 2
    shapes = [
        (edge, ranks),
        (edge, ranks),
        (2, eighth, LANES),
        (eighth, LANES),
        (taps, edge),
        (1, edge),
        (1, edge),
        (1, edge),
        out.shape,
    ]
    return pl.pallas_call(
        functools.partial(unpack_kernel, eighth=eighth, taps=taps, edge=edge),
        grid=(1,),
        in_specs=[whole(array.shape) for array in (near, far, out)],
        out_specs=[whole(shape) for shape in shapes],
        out_shape=[jax.ShapeDtypeStruct(shape, F32) for shape in shapes],
        cost_estimate=cost(0),
        name="unpack",
    )(near, far, out)


def swap_pair(array):
    count = lax.axis_size("state")
    return lax.ppermute(array, "state", [(pos, pos ^ 1) for pos in range(count)])


def swap_bit(array, bits):
    return lax.ppermute(array, "dp", [(pos, pos ^ bits) for pos in range(lax.axis_size("dp"))])


def swap_both(array, bits=0):
    states = lax.axis_size("state")
    pairs = []
    for d in range(lax.axis_size("dp")):
        for s in range(states):
            pairs.append((d * states + s, (((d & ~1) | s) ^ bits) * states + (d & 1)))
    return lax.ppermute(array, ("dp", "state"), pairs)


def add_mixed(x, mine, theirs):
    return (x.astype(F32) + (mine.astype(F32) + theirs.astype(F32))).astype(BF16)


def add_quarters(kept, got, start=0, stop=None):
    extent = kept.shape[0] // 4
    stop = extent if stop is None else stop
    return [
        kept[k * extent + start : k * extent + stop] + got[k * extent + start : k * extent + stop]
        for k in range(4)
    ]


def trade_quarters(quarters):
    return [quarters[0]] + [swap_bit(quarters[k], k * X_BIT) for k in range(1, 4)]


def sum_quarters(quarters):
    left, right = (quarters[k].astype(F32) + quarters[k + 1].astype(F32) for k in (0, 2))
    return (left + right).astype(BF16)


CORE_BIT, X_BIT, ZH_BIT = 1, 2, 8


def shards(
    tokens,
    cluster_len,
    norm_gain,
    in_weight,
    conv_weight,
    conv_bias,
    dtx_weight,
    dt_weight,
    dt_bias,
    bc_weight,
    a_log,
    skip_gain,
    out_weight,
    cotangent,
):
    micros, count, width = tokens.shape
    inner = out_weight.shape[0]
    taps = conv_weight.shape[0]
    ranks = dtx_weight.shape[1]
    chunks = inner // (2 * LANES)
    own = chunks * LANES
    rows = micros * count
    edge = LANES // 2
    span = LANES + 32
    dp_parts = lax.axis_size("dp")
    state_count = lax.axis_size("state")
    dp_pos = lax.axis_index("dp")
    state_pos = lax.axis_index("state")
    half = state_pos & 1
    fast = state_count == 2 and dp_parts == 2 * chunks == 16
    if fast:
        place = jnp.stack([half, dp_pos & 1, dp_pos >> 1, (dp_pos >> 1) & 3])
        bc_own, alog_own = bc_weight, a_log
        bc_other, alog_other = swap_pair(bc_weight), swap_pair(a_log)
    else:
        place = jnp.stack([half, 0, 0, 0])
        bc_all = lax.all_gather(bc_weight, "state", axis=1, tiled=True)
        alog_all = lax.all_gather(a_log, "state", axis=0, tiled=True)
        eighth = alog_all.shape[0] // 2
        bc_own, bc_other = (
            lax.dynamic_slice_in_dim(bc_all, which * eighth, eighth, 1)
            for which in (half, 1 - half)
        )
        alog_own, alog_other = (
            lax.dynamic_slice_in_dim(alog_all, which * eighth, eighth, 0)
            for which in (half, 1 - half)
        )
    place = place.astype(jnp.int32)
    eighth = alog_own.shape[0]
    states = 2 * eighth

    x = tokens.reshape(rows, width)
    cotan = cotangent.reshape(rows, width)
    w4 = in_weight.reshape(2, chunks, 2, LANES, width)
    wout3 = out_weight.reshape(chunks, 2, LANES, width)
    dtx, dt = dtx_weight.T, dt_weight.T
    bias = dt_bias.reshape(-1, LANES)
    skip = skip_gain.reshape(-1, LANES)

    normed, act_all, act, inner_own, bend, gate = project(
        place, cluster_len, x, norm_gain[None], w4, conv_weight, conv_bias.reshape(-1, LANES)
    )
    bc, rank, high, decay, sp, u, step, slope, h, dy, gated, dgate, keep, send = scan_forward(
        place,
        cluster_len,
        act_all,
        bc_own,
        bc_other,
        alog_own,
        alog_other,
        dtx,
        dt,
        bias,
        skip,
        act,
        gate,
        wout3,
        cotan,
        normed,
    )
    if fast:
        early = swap_bit(send, CORE_BIT)
    mixed_part, dn_gate = products(place, gated, dgate, wout3, w4)
    if fast:
        *quarters, mixed_part, dn_gate, sp = lax.optimization_barrier(
            (*add_quarters(keep, early), mixed_part, dn_gate, sp)
        )
        early_got = trade_quarters(quarters)
    code_own, sact, dpre, alog, back = scan_backward(
        place, micros, bc, decay, dt, skip, act, sp, u, step, slope, dy, h
    )
    if fast:
        *early_got, code_own, mixed_part = lax.optimization_barrier(
            (*early_got, code_own, mixed_part)
        )
    code_other = swap_pair(code_own)
    mixed_other = swap_pair(mixed_part)
    if fast:
        block = sum_quarters(early_got)
        out_keep, out_send, gate_sum = block[:edge], block[edge:LANES], block[LANES:]
        out_send, gate_sum, bend = lax.optimization_barrier((out_send, gate_sum, bend))
        out_got = swap_bit(out_send, ZH_BIT)
    late_keep, late_send, dnormed_part = tail(
        place,
        cluster_len,
        code_own,
        code_other,
        sact,
        dpre,
        alog,
        back,
        dtx,
        bc_own,
        bc_other,
        decay,
        bend,
        inner_own,
        act,
        high,
        conv_weight,
        normed,
        w4,
        dn_gate,
        x,
    )
    mixed = add_mixed(x, mixed_part, mixed_other)
    if fast:
        late_send, mixed_other = lax.optimization_barrier((late_send, mixed_other))
        mixed = add_mixed(x, mixed_part, mixed_other)
        late = swap_bit(late_send, CORE_BIT)
        late_got = trade_quarters(add_quarters(late_keep, late))
    dnormed_other = swap_pair(dnormed_part)
    tokens_grad = finish(x, dnormed_part, dnormed_other, cotan, norm_gain[None])
    if fast:
        out_own = swap_both(out_keep + out_got)
        *late_got, out_own, tokens_grad, mixed = lax.optimization_barrier(
            (*late_got, out_own, tokens_grad, mixed)
        )
        block = sum_quarters(late_got)
        inner_sum = block[:LANES]
        upper = dp_pos >= dp_parts // 2
        crossing = jnp.where(upper, inner_sum, gate_sum)
        first, second = crossing[:edge], crossing[edge:]
        first, pack_far, pack_near = lax.optimization_barrier(
            (first, block[-16:], block[LANES:-16])
        )
        pack_far = swap_both(pack_far, ZH_BIT)
        first_got = swap_bit(first, ZH_BIT)
        pack_near = swap_both(pack_near)
        first_got, pack_far, pack_near = lax.optimization_barrier((first_got, pack_far, pack_near))
        second_got = swap_bit(second, ZH_BIT)
        gain_mine = (
            pack_near[:, 5 * LANES : 6 * LANES].astype(F32)
            + pack_far[:, 5 * LANES : 6 * LANES].astype(F32)
        ).astype(BF16)
        gain_both = gain_mine[-1].astype(F32) + swap_bit(gain_mine, CORE_BIT)[-1].astype(F32)
        extent = width // (dp_parts * state_count)
        gain_grad = lax.dynamic_slice_in_dim(gain_both, (dp_pos & 1) * extent, extent, 0)
        (
            dtx_grad,
            dt_grad,
            bc_grad,
            alog_grad,
            convw_grad,
            convb_grad,
            bias_grad,
            skip_grad,
            out_own,
        ) = unpack(pack_near, pack_far, out_own, eighth, taps, ranks)
        convb_grad, bias_grad, skip_grad = (
            array[0] for array in (convb_grad, bias_grad, skip_grad)
        )
        second_got, dtx_grad, dt_grad, out_own = lax.optimization_barrier(
            (second_got, dtx_grad, dt_grad, out_own)
        )
        in_grad = jnp.where(upper, gate_sum, inner_sum).astype(F32) + jnp.concatenate(
            [first_got, second_got]
        ).astype(F32)
    mixed = mixed.reshape(micros, count, width)
    tokens_grad = tokens_grad.reshape(micros, count, width)

    if not fast:
        def total(array):
            return lax.psum(array.astype(F32), "dp")

        def both_rows(array):
            mine = array.reshape(chunks, 1, LANES, -1)
            other = swap_pair(mine)
            low = jnp.where(half == 0, mine, other)
            high = jnp.where(half == 0, other, mine)
            return jnp.concatenate([low, high], axis=1).reshape(2 * own, -1)

        every = dp_parts * state_count
        at = dp_pos * state_count + state_pos

        def cut_own(array):
            extent = array.shape[0] // every
            return lax.dynamic_slice_in_dim(array, at * extent, extent, 0)

        pair = total(jnp.stack([keep, send])).reshape(2, 2, 2, 2 * LANES, width)
        outs = pair[:, :, :, :LANES].reshape(2, 2, 2, 2, edge, width)
        outs = jnp.transpose(outs, (3, 1, 2, 0, 4, 5)).reshape(own, width)
        gates = jnp.moveaxis(pair[:, :, :, LANES:], 0, 2).reshape(own, width)
        pair = total(jnp.stack([late_keep, late_send])).reshape(2, 2, 2, span, width)
        inners = jnp.moveaxis(pair[:, :, :, :LANES], 0, 2).reshape(own, width)
        packs = pair[:, :, :, LANES:].reshape(2, 2, 2, 2, 16, width // LANES, LANES)
        packs = jnp.transpose(packs, (3, 1, 2, 0, 5, 4, 6)).reshape(chunks, 2, -1, 16, LANES)
        small = packs[:, :, :4].reshape(chunks, 2, ranks, 2, edge)
        small = both_rows(jnp.transpose(small, (0, 1, 4, 3, 2)).reshape(own, 2 * ranks))
        in_grad = cut_own(jnp.concatenate([both_rows(inners), both_rows(gates)]))
        out_own = cut_own(both_rows(outs))
        mine = cut_own(small)
        dtx_grad, dt_grad = mine[:, :ranks], mine[:, ranks:]
        vec_rows = jnp.swapaxes(packs[:, :, 5, eighth:, :edge], 2, 3).reshape(own, -1)
        gain_sum = vec_rows[:, -1].reshape(chunks, 2, 2, -1).swapaxes(1, 2).reshape(-1)
        gain_grad = cut_own(gain_sum + swap_pair(gain_sum))
        vec = cut_own(both_rows(vec_rows)).T
        state_rows = jnp.concatenate([packs[:, :, 4], packs[:, :, 5, :eighth]], axis=2)
        state_rows = state_rows.reshape(chunks, 2, 3, eighth, LANES)
        state_rows = jnp.transpose(state_rows, (0, 4, 2, 1, 3)).reshape(own, -1)
        extent = inner // dp_parts
        state_part = lax.dynamic_slice_in_dim(both_rows(state_rows), dp_pos * extent, extent, 0)
        state_part = state_part.T.reshape(3, state_count, -1, extent)
        state_part = lax.dynamic_index_in_dim(state_part, state_pos, 1, keepdims=False)
        bc_grad, alog_grad = state_part[:2], state_part[2]
        convw_grad, convb_grad, bias_grad, skip_grad = (
            vec[:taps], vec[taps], vec[taps + 1], vec[taps + 2]
        )

    return (
        mixed,
        tokens_grad,
        gain_grad,
        in_grad,
        convw_grad,
        convb_grad,
        dtx_grad,
        dt_grad,
        bias_grad,
        bc_grad,
        alog_grad,
        skip_grad,
        out_own,
    )


def solution(mesh):
    return jax.shard_map(
        shards,
        mesh=mesh,
        in_specs=(
            P(None, "dp", None),
            P(None, "dp", None),
            P(),
            P(),
            P(),
            P(),
            P(),
            P(),
            P(),
            P(None, "state", None),
            P("state", None),
            P(),
            P(),
            P(None, "dp", None),
        ),
        out_specs=(
            P(None, "dp", None),
            P(None, "dp", None),
            P(("dp", "state")),
            P(("dp", "state"), None),
            P(None, ("dp", "state")),
            P(("dp", "state")),
            P(("dp", "state"), None),
            P(("dp", "state"), None),
            P(("dp", "state")),
            P(None, "state", "dp"),
            P("state", "dp"),
            P(("dp", "state")),
            P(("dp", "state"), None),
        ),
        check_vma=False,
    )
```

```python
import functools
import math

import jax
import jax.numpy as jnp
from jax import lax
from jax.experimental import pallas as pl
from jax.experimental.pallas import tpu as pltpu
from jax.sharding import PartitionSpec as P

EPSILON = 1e-05
LANES = 128
RESET = 1e4
LOG2E = math.log2(math.e)
F32 = jnp.float32
BF16 = jnp.bfloat16
MIB = 1024 * 1024


def dot(left, right, left_dim, right_dim):
    return lax.dot_general(
        left, right, (((left_dim,), (right_dim,)), ((), ())), preferred_element_type=F32
    )


def params(mib):
    return pltpu.CompilerParams(
        vmem_limit_bytes=mib * MIB, dimension_semantics=("arbitrary",)
    )


ANY = pl.BlockSpec(memory_space=pl.ANY)


def stream(step, steps, fetch):
    @pl.when(step == 0)
    def _():
        for k in range(steps):
            for copy in fetch(k):
                copy.start()

    for copy in fetch(step):
        copy.wait()


def whole(shape):
    return pl.BlockSpec(shape, lambda *_: (0,) * len(shape))


sigmoid = jax.nn.sigmoid


def log_one_plus(value):
    series = value * (1.0 - value * (0.5 - value * (1.0 / 3.0)))
    return jnp.where(value < 1e-3, series, jnp.log(1.0 + value))


def lanes(index):
    return pl.ds(pl.multiple_of(index * LANES, LANES), LANES)


def cost(micros):
    return pl.CostEstimate(
        flops=int(micros * 1e9), bytes_accessed=int(micros * 1e6), transcendentals=0
    )


def hbm(shape, dtype):
    return pltpu.HBM(shape, dtype)


def in_hbm(arrays):
    return [pltpu.with_memory_space_constraint(array, pltpu.HBM) for array in arrays]


def two_lanes(index):
    return pl.ds(pl.multiple_of(index * 2 * LANES, 2 * LANES), 2 * LANES)


def aligned(start, size, to=8):
    return pl.ds(pl.multiple_of(start, to), size)


SEGMENTS = 4

HALF, CORE, CUBE, FACE = range(4)


def fill_masks(len_ref, mask_ref, micros, count, taps, clusters):
    place = lax.broadcasted_iota(jnp.int32, (count, LANES), 0)
    for micro in range(micros):
        rows = pl.ds(micro * count, count)
        for back in range(1, taps):
            apart = place < back
            start = 0
            for cluster in range(clusters - 1):
                start = start + len_ref[micro, 0, cluster]
                apart = apart | ((place >= start) & (place < start + back))
            mask_ref[back, rows, :] = jnp.where(apart, 0.0, 1.0)
            if back == 1:
                mask_ref[0, rows, :] = jnp.where(apart, 1.0, 0.0)


def project_kernel(
    place_ref,
    len_ref,
    gain_ref,
    convw_ref,
    convb_ref,
    x_far,
    weight_far,
    normed_far,
    act_far,
    own_act_far,
    inner_far,
    bend_far,
    gate_far,
    mask_ref,
    x_ref,
    win_ref,
    wgate_ref,
    normed_ref,
    act_ref,
    own_act_ref,
    inner_ref,
    bend_ref,
    gate_ref,
    in_sems,
    out_sems,
    *,
    micros,
    count,
    taps,
    clusters,
):
    half = place_ref[HALF]
    chunks = win_ref.shape[0]
    inward = [pltpu.make_async_copy(x_far, x_ref, in_sems.at[2 * chunks])]
    for k in range(chunks):
        inward.append(pltpu.make_async_copy(weight_far.at[0, k], win_ref.at[k], in_sems.at[2 * k]))
        inward.append(
            pltpu.make_async_copy(
                weight_far.at[1, k, half], wgate_ref.at[k], in_sems.at[2 * k + 1]
            )
        )
    for copy in inward:
        copy.start()
    outward = []

    def put(source, target):
        outward.append(pltpu.make_async_copy(source, target, out_sems.at[len(outward)]))
        outward[-1].start()

    fill_masks(len_ref, mask_ref, micros, count, taps, clusters)
    inward[0].wait()
    rows = x_ref[...].astype(F32)
    scale = lax.rsqrt(jnp.mean(rows * rows, axis=1, keepdims=True) + EPSILON)
    normed = (rows * scale * gain_ref[...]).astype(BF16)
    normed_ref[...] = normed
    put(normed_ref, normed_far)
    for k in range(chunks):
        inward[2 * k + 1].wait()
        inward[2 * k + 2].wait()
        proj = dot(normed, win_ref[k].reshape(2 * LANES, -1), 1, 1)
        own = slice(k * LANES, (k + 1) * LANES)
        gate_ref[:, own] = dot(normed, wgate_ref[k], 1, 1)
        inners, sigs, acts = [], [], []
        for part in range(2):
            cols = slice((2 * k + part) * LANES, (2 * k + part + 1) * LANES)
            inner = proj[:, part * LANES : (part + 1) * LANES]
            conved = convb_ref[2 * k + part : 2 * k + part + 1, :]
            conved = conved + convw_ref[taps - 1 : taps, cols] * inner
            for back in range(1, taps):
                shifted = pltpu.roll(inner, back, 0) * mask_ref[back]
                conved = conved + convw_ref[taps - 1 - back : taps - back, cols] * shifted
            sig = sigmoid(conved)
            act = conved * sig
            act_ref[:, cols] = act.astype(BF16)
            inners.append(inner)
            sigs.append(sig)
            acts.append(act)
        inner_ref[:, own] = jnp.where(half == 0, *inners)
        act, sig = jnp.where(half == 0, *acts), jnp.where(half == 0, *sigs)
        bend_ref[:, own] = (sig + act * (1.0 - sig)).astype(BF16)
        own_act_ref[:, own] = act.astype(BF16)
        if k % 2:
            group = pl.ds((k - 1) * LANES, 2 * LANES)
            wide = pl.ds(2 * (k - 1) * LANES, 4 * LANES)
            put(act_ref.at[:, wide], act_far.at[:, wide])
            for near, far in (
                (gate_ref, gate_far),
                (inner_ref, inner_far),
                (bend_ref, bend_far),
                (own_act_ref, own_act_far),
            ):
                put(near.at[:, group], far.at[:, group])
    for copy in outward:
        copy.wait()


def project(place, lengths, x, gain, w4, conv_weight, conv_bias):
    rows, width = x.shape
    chunks = w4.shape[1]
    micros, _, clusters = lengths.shape
    taps = conv_weight.shape[0]
    own = chunks * LANES
    outs = [
        ((rows, width), BF16),
        ((rows, 2 * own), BF16),
        ((rows, own), BF16),
        ((rows, own), F32),
        ((rows, own), BF16),
        ((rows, own), F32),
    ]
    return pl.pallas_call(
        functools.partial(
            project_kernel, micros=micros, count=rows // micros, taps=taps, clusters=clusters
        ),
        grid_spec=pltpu.PrefetchScalarGridSpec(
            num_scalar_prefetch=1,
            grid=(1,),
            in_specs=[
                pl.BlockSpec(memory_space=pltpu.SMEM),
                whole(gain.shape),
                whole(conv_weight.shape),
                whole(conv_bias.shape),
                ANY,
                ANY,
            ],
            out_specs=[ANY] * len(outs),
            scratch_shapes=[
                pltpu.VMEM((taps, rows, LANES), F32),
                pltpu.VMEM((rows, width), BF16),
                pltpu.VMEM((chunks, 2, LANES, width), BF16),
                pltpu.VMEM((chunks, LANES, width), BF16),
            ]
            + [pltpu.VMEM(*out) for out in outs]
            + [
                pltpu.SemaphoreType.DMA((2 * chunks + 1,)),
                pltpu.SemaphoreType.DMA((1 + 5 * chunks // 2,)),
            ],
        ),
        out_shape=[hbm(*out) for out in outs],
        compiler_params=params(30),
        cost_estimate=cost(6),
        name="project",
    )(place, *in_hbm((lengths, gain, conv_weight, conv_bias, x, w4)))


def every_row(ref, row, height):
    return ref[pl.ds(row, height, stride=0), :]


def b_at(n, eighth):
    return (n // eighth) * 2 * eighth + n % eighth


def c_at(n, eighth):
    return b_at(n, eighth) + eighth


def forward_kernel(
    place_ref,
    len_ref,
    act_all_ref,
    bc_own_ref,
    bc_other_ref,
    alog_own_ref,
    alog_other_ref,
    dtx_ref,
    dt_ref,
    bias_ref,
    skip_ref,
    act_ref,
    *refs,
    micros,
    count,
    states,
    chunks,
    clusters,
):
    gate_far, wout_far, cotan_far, normed_far = refs[:4]
    bc_ref, rank_ref, rank_high_ref, decay_ref = refs[4:8]
    sp_far, u_far, step_far, slope_far, h_far, dy_far = refs[8:14]
    gated_far, dgate_far, keep_far, send_far = refs[14:18]
    mask_ref, y_ref, tmp_ref, wide_ref = refs[18:22]
    gate_ref, wout_ref, cotan_ref, normed_ref = refs[22:26]
    sp_ref, u_ref, step_ref, slope_ref, h_ref, dy_ref = refs[26:32]
    gated_ref, dgate_ref, keep_ref, send_ref = refs[32:36]
    in_sems, out_sems = refs[36:]
    rows = micros * count
    eighth = states // 2
    half, core, cube, face = (place_ref[k] for k in range(4))
    first = half == 0
    inward = [
        pltpu.make_async_copy(source, target, in_sems.at[k])
        for k, (source, target) in enumerate(
            (
                (gate_far, gate_ref),
                (wout_far.at[:, half], wout_ref),
                (cotan_far, cotan_ref),
                (normed_far, normed_ref),
            )
        )
    ]
    for copy in inward:
        copy.start()
    outward = []

    def put(source, target):
        outward.append(pltpu.make_async_copy(source, target, out_sems.at[len(outward)]))
        outward[-1].start()

    ranks = dtx_ref.shape[0]
    weights = jnp.concatenate(
        [dtx_ref[...]] + [ref[...].reshape(states, -1) for ref in (bc_own_ref, bc_other_ref)]
    )
    product = dot(act_all_ref[...], weights, 1, 1)
    own, other = product[:, ranks : ranks + states], product[:, ranks + states :]
    bc_ref[:, :states] = jnp.where(first, own, other)
    bc_ref[:, states:] = jnp.where(first, other, own)
    spread_lanes(bc_ref, wide_ref)

    fill_masks(len_ref, mask_ref, micros, count, 2, clusters)
    for chunk in range(chunks):
        cols = lanes(2 * chunk + half)
        own, other = alog_own_ref[:, cols], alog_other_ref[:, cols]
        tmp_ref[pl.ds(chunk * states, eighth), :] = jnp.where(first, own, other)
        tmp_ref[pl.ds(chunk * states + eighth, eighth), :] = jnp.where(first, other, own)
    for n in range(states):
        decay_ref[pl.ds(n * chunks, chunks), :] = -LOG2E * jnp.exp(
            tmp_ref[pl.ds(n, chunks, stride=states), :]
        )

    rank = product[:, :ranks].astype(BF16)
    rank_ref[...] = rank
    rank_high_ref[...] = jnp.concatenate([jnp.zeros_like(rank), rank], axis=1)
    for chunk in range(chunks):
        cols = slice(chunk * LANES, (chunk + 1) * LANES)
        bias = bias_ref[pl.ds(2 * chunk + half, 1), :]
        pre = dot(rank, dt_ref[:, lanes(2 * chunk + half)], 1, 0) + bias
        tail_part = jnp.exp(-jnp.abs(pre))
        step = jnp.maximum(pre, 0.0) + log_one_plus(tail_part)
        slope = jnp.where(pre >= 0.0, 1.0, tail_part) / (1.0 + tail_part)
        step_ref[:, cols] = step
        slope_ref[:, cols] = slope.astype(BF16)
        held = step + RESET * mask_ref[0]
        source = step * act_ref[:, cols].astype(F32)
        for micro in range(micros):
            span = slice(micro * count, (micro + 1) * count)
            place = pl.ds((micro * chunks + chunk) * count, count)
            sp_ref[place, :] = held[span]
            u_ref[place, :] = source[span]
    put(sp_ref, sp_far)
    put(u_ref, u_far)
    put(step_ref, step_far)
    put(slope_ref, slope_far)

    for micro in range(micros):

        def advance(t, h, micro=micro):
            row = micro * count + t
            span = pl.ds(micro * chunks * count + t, chunks, stride=count)
            sp = sp_ref[span, :]
            u = u_ref[span, :]
            out = []
            y = None
            for n in range(states):
                decay = jnp.exp2(sp * decay_ref[pl.ds(n * chunks, chunks), :])
                now = decay * h[n] + u * every_row(wide_ref, b_at(n, eighth) * rows + row, chunks)
                h_ref[aligned((row * states + n) * chunks, chunks), :] = now
                out.append(now)
                term = now * every_row(wide_ref, c_at(n, eighth) * rows + row, chunks)
                y = term if y is None else y + term
            y_ref[span, :] = y
            return tuple(out)

        h = (jnp.zeros((chunks, LANES), F32),) * states
        segment = count // SEGMENTS
        for k in range(SEGMENTS):
            h = lax.fori_loop(k * segment, (k + 1) * segment, advance, h, unroll=8)
            extent = segment * states * chunks
            place = pl.ds((micro * SEGMENTS + k) * extent, extent)
            put(h_ref.at[place], h_far.at[place])

    for copy in inward:
        copy.wait()
    cotan = cotan_ref[...]
    for chunk in range(chunks):
        cols = slice(chunk * LANES, (chunk + 1) * LANES)
        places = [pl.ds((micro * chunks + chunk) * count, count) for micro in range(micros)]
        y = jnp.concatenate([y_ref[place, :] for place in places])
        y = y + skip_ref[pl.ds(2 * chunk + half, 1), :] * act_ref[:, cols].astype(F32)
        gate = gate_ref[:, cols]
        sig = sigmoid(gate)
        gated_ref[:, cols] = (y * (gate * sig)).astype(BF16)
        dgated = dot(cotan, wout_ref[chunk], 1, 1)
        dy = dgated * (gate * sig)
        for micro in range(micros):
            dy_ref[places[micro], :] = dy[micro * count : (micro + 1) * count]
        dgate_ref[:, cols] = (dgated * y * (sig * (1.0 + gate * (1.0 - sig)))).astype(BF16)
    put(dy_ref, dy_far)
    put(gated_ref, gated_far)
    put(dgate_ref, dgate_far)
    normed = normed_ref[...]
    edge = LANES // 2
    straight, first_core = (cube & 1) == 0, core == 0
    for r in range(0, chunks // 2, 2):
        for zh in range(2):
            pair = ((r + 4 * zh) ^ cube) >> 1
            grad = dot(gated_ref[:, two_lanes(pair)], cotan, 0, 0).astype(BF16)
            parts = grad[:LANES], grad[LANES:]
            for k in range(2):
                one = jnp.where(straight, parts[k], parts[1 - k])
                top, bottom = one[:edge], one[edge:]
                place = pl.ds((r + k) * 2 * LANES + zh * edge, edge)
                keep_ref[place, :] = jnp.where(first_core, top, bottom)
                send_ref[place, :] = jnp.where(first_core, bottom, top)
        for k in range(r, r + 2):
            grad = dot(dgate_ref[:, two_lanes(k ^ face)], normed, 0, 0).astype(BF16)
            place = pl.ds((2 * k + 1) * LANES, LANES)
            keep_ref[place, :] = jnp.where(first_core, grad[:LANES], grad[LANES:])
            send_ref[place, :] = jnp.where(first_core, grad[LANES:], grad[:LANES])
            place = pl.ds(k * 2 * LANES, 2 * LANES)
            put(send_ref.at[place], send_far.at[place])
            put(keep_ref.at[place], keep_far.at[place])
    for copy in outward:
        copy.wait()


def scan_forward(
    place,
    lengths,
    act_all,
    bc_own,
    bc_other,
    alog_own,
    alog_other,
    dtx,
    dt,
    bias,
    skip,
    act,
    gate,
    wout3,
    cotan,
    normed,
):
    rows, own = act.shape
    chunks = own // LANES
    states = 2 * alog_own.shape[0]
    width = cotan.shape[1]
    micros, _, clusters = lengths.shape
    ranks = dtx.shape[0]
    small = [
        ((rows, 2 * states), F32),
        ((rows, ranks), BF16),
        ((rows, 2 * ranks), BF16),
        ((states * chunks, LANES), F32),
    ]
    large = [
        ((chunks * rows, LANES), F32),
        ((chunks * rows, LANES), F32),
        ((rows, own), F32),
        ((rows, own), BF16),
        ((rows * states * chunks, LANES), F32),
        ((chunks * rows, LANES), F32),
        ((rows, own), BF16),
        ((rows, own), BF16),
        ((own, width), BF16),
        ((own, width), BF16),
    ]
    operands = (act_all, bc_own, bc_other, alog_own, alog_other, dtx, dt, bias, skip, act)
    streamed = (gate, wout3, cotan, normed)
    return pl.pallas_call(
        functools.partial(
            forward_kernel,
            micros=micros,
            count=rows // micros,
            states=states,
            chunks=chunks,
            clusters=clusters,
        ),
        grid_spec=pltpu.PrefetchScalarGridSpec(
            num_scalar_prefetch=1,
            grid=(1,),
            in_specs=[pl.BlockSpec(memory_space=pltpu.SMEM)]
            + [whole(operand.shape) for operand in operands]
            + [ANY] * len(streamed),
            out_specs=[whole(shape) for shape, _ in small] + [ANY] * len(large),
            scratch_shapes=[
                pltpu.VMEM((2, rows, LANES), F32),
                pltpu.VMEM((chunks * rows, LANES), F32),
                pltpu.VMEM((states * chunks, LANES), F32),
                pltpu.VMEM((2 * states * rows, LANES), F32),
                pltpu.VMEM((rows, own), F32),
                pltpu.VMEM((chunks, LANES, width), BF16),
                pltpu.VMEM((rows, width), BF16),
                pltpu.VMEM((rows, width), BF16),
            ]
            + [pltpu.VMEM(*out) for out in large]
            + [pltpu.SemaphoreType.DMA((4,)), pltpu.SemaphoreType.DMA((7 + chunks + micros * SEGMENTS,))],
        ),
        out_shape=[hbm(*out) for out in small + large],
        compiler_params=params(52),
        cost_estimate=cost(19),
        name="scan_forward",
    )(
        place,
        lengths,
        *in_hbm(operands[:1]),
        *operands[1:5],
        *in_hbm((*operands[5:], *streamed)),
    )


def spread_lanes(values_ref, wide_ref):
    rows, count = values_ref.shape
    for k in range(count):
        wide_ref[pl.ds(k * rows, rows), :] = jnp.broadcast_to(
            values_ref[:, k : k + 1], (rows, LANES)
        )


def backward_kernel(
    place_ref,
    bc_ref,
    decay_ref,
    dt_ref,
    skip_ref,
    act_ref,
    sp_ref,
    u_ref,
    step_ref,
    slope_ref,
    dy_ref,
    h_far,
    code_ref,
    sact_ref,
    dpre_ref,
    alog_ref,
    vec_ref,
    h_ref,
    s_ref,
    d_ref,
    terms_ref,
    sums_b_ref,
    sums_c_ref,
    wide_ref,
    sems,
    *,
    count,
    states,
    chunks,
):
    micro = pl.program_id(0)
    block = states * chunks
    segment = count // SEGMENTS

    def fetch(which, k):
        extent = segment * block
        buffer = h_ref.at[which % 2]
        return pltpu.make_async_copy(
            h_far.at[aligned((which * SEGMENTS + k) * extent, extent)],
            buffer.at[pl.ds(block + k * extent, extent)],
            sems.at[which % 2, k],
        )

    @pl.when(micro == 0)
    def _():
        for k in reversed(range(SEGMENTS)):
            fetch(0, k).start()
        for which in range(2):
            h_ref[which, pl.ds(0, block), :] = jnp.zeros((block, LANES), F32)
        alog_ref[...] = jnp.zeros_like(alog_ref)
        vec_ref[...] = jnp.zeros_like(vec_ref)

    half = place_ref[HALF]
    eighth = states // 2
    zero = (jnp.zeros((chunks, LANES), F32),) * states
    spread_lanes(bc_ref, wide_ref)

    @pl.when(micro + 1 < pl.num_programs(0))
    def _():
        for k in reversed(range(SEGMENTS)):
            fetch(micro + 1, k).start()

    side = micro % 2

    def put_terms(which, t, terms):
        for n in range(0, states, 2):
            pair = jnp.concatenate(terms[n : n + 2]).astype(BF16)
            place = aligned(t * block + n * chunks, 2 * chunks, 16)
            terms_ref[which, place, :] = pair

    def retreat(back, carry):
        flows, totals = carry
        for slot in range(4):
            t = count - 1 - (4 * back + slot)
            span = pl.ds(t, chunks, stride=count)
            sp = sp_ref[span, :]
            u = u_ref[span, :]
            dy = dy_ref[span, :]
            out_flows = []
            out_totals = []
            b_terms, c_terms = [], []
            d_sum = None
            s_sum = None
            for n in range(states):
                rate = decay_ref[pl.ds(n * chunks, chunks), :]
                dh = flows[n] + dy * every_row(wide_ref, c_at(n, eighth) * count + t, chunks)
                flow = jnp.exp2(sp * rate) * dh
                out_flows.append(flow)
                q = flow * h_ref[side, aligned(t * block + n * chunks, chunks), :]
                now = h_ref[side, aligned((t + 1) * block + n * chunks, chunks), :]
                out_totals.append(totals[n] + q * sp)
                d_term = q * rate
                s_term = dh * every_row(wide_ref, b_at(n, eighth) * count + t, chunks)
                d_sum = d_term if d_sum is None else d_sum + d_term
                s_sum = s_term if s_sum is None else s_sum + s_term
                b_terms.append(dh * u)
                c_terms.append(dy * now)
            s_ref[span, :] = s_sum
            d_ref[span, :] = d_sum
            put_terms(0, t, b_terms)
            put_terms(1, t, c_terms)
            flows, totals = tuple(out_flows), tuple(out_totals)
        return flows, totals

    carry = (zero, zero)
    for k in range(SEGMENTS):
        fetch(micro, SEGMENTS - 1 - k).wait()
        carry = lax.fori_loop(k * segment // 4, (k + 1) * segment // 4, retreat, carry)
    totals = carry[1]
    for n in range(states):
        alog_ref[pl.ds(n * chunks, chunks), :] += totals[n]

    shape = (2 * states, 2 * block)
    group = lax.broadcasted_iota(jnp.int32, shape, 1) // chunks
    gather = jnp.where(group == lax.broadcasted_iota(jnp.int32, shape, 0), 1.0, 0.0).astype(BF16)

    for which, sums_ref in ((0, sums_b_ref), (1, sums_c_ref)):
        for at in range(count // 2):
            terms = terms_ref[which, pl.ds(at * 2 * block, 2 * block), :]
            sums_ref[pl.ds(at * 2 * states, 2 * states), :] = dot(gather, terms, 1, 0)

    ranks = dt_ref.shape[0]
    drank = None
    for chunk in range(chunks):
        cols = slice(chunk * LANES, (chunk + 1) * LANES)
        place = pl.ds(chunk * count, count)
        act = act_ref[:, cols].astype(F32)
        weight = dt_ref[:, lanes(2 * chunk + half)]
        s_now = s_ref[place, :]
        dstep = d_ref[place, :] * (1.0 / LOG2E) + s_now * act
        dy = dy_ref[place, :]
        skip = skip_ref[pl.ds(2 * chunk + half, 1), :]
        sact_ref[:, cols] = s_now * step_ref[:, cols] + dy * skip
        dpre = dstep * slope_ref[:, cols].astype(F32)
        vec_ref[0:1, cols] += jnp.sum(dpre, axis=0, keepdims=True)
        vec_ref[1:2, cols] += jnp.sum(dy * act, axis=0, keepdims=True)
        low = dpre.astype(BF16)
        dpre_ref[:, cols] = low
        term = dot(low, weight, 1, 1)
        drank = term if drank is None else drank + term
    source = lax.broadcasted_iota(jnp.int32, (2 * LANES, LANES), 0)
    target = lax.broadcasted_iota(jnp.int32, (2 * LANES, LANES), 1)
    code = None
    for n in range(states):
        pair = jnp.concatenate(
            [ref[pl.ds(n, count, stride=states), :] for ref in (sums_b_ref, sums_c_ref)], axis=1
        )
        column = ranks + jnp.where(source < LANES, b_at(n, eighth), c_at(n, eighth))
        pick = jnp.where(target == column, 1.0, 0.0).astype(BF16)
        term = dot(pair.astype(BF16), pick, 1, 0)
        code = term if code is None else code + term
    drank = jnp.concatenate([drank, jnp.zeros((count, LANES - ranks), F32)], axis=1)
    code_ref[...] = (code + drank).astype(BF16)


def scan_backward(place, micros, bc, decay, dt, skip, act, sp, u, step, slope, dy, h):
    rows, own = act.shape
    count = rows // micros
    chunks = own // LANES
    states = bc.shape[1] // 2
    outs = [
        ((rows, LANES), BF16),
        ((rows, own), F32),
        ((rows, own), BF16),
        ((states * chunks, LANES), F32),
        ((2, own), F32),
    ]

    def block(*shape):
        return pl.BlockSpec(shape, lambda i, p: (i, 0))

    return pl.pallas_call(
        functools.partial(backward_kernel, count=count, states=states, chunks=chunks),
        grid_spec=pltpu.PrefetchScalarGridSpec(
            num_scalar_prefetch=1,
            grid=(micros,),
            in_specs=[
                block(count, 2 * states),
                whole(decay.shape),
                whole(dt.shape),
                whole(skip.shape),
                block(count, own),
                block(chunks * count, LANES),
                block(chunks * count, LANES),
                block(count, own),
                block(count, own),
                block(chunks * count, LANES),
                ANY,
            ],
            out_specs=[block(count, LANES), block(count, own), block(count, own)]
            + [whole(shape) for shape, _ in outs[3:]],
            scratch_shapes=[
                pltpu.VMEM((2, (count + 1) * states * chunks, LANES), F32),
                pltpu.VMEM((chunks * count, LANES), F32),
                pltpu.VMEM((chunks * count, LANES), F32),
                pltpu.VMEM((2, count * states * chunks, LANES), BF16),
                pltpu.VMEM((count * states, LANES), F32),
                pltpu.VMEM((count * states, LANES), F32),
                pltpu.VMEM((2 * states * count, LANES), F32),
                pltpu.SemaphoreType.DMA((2, SEGMENTS)),
            ],
        ),
        out_shape=[hbm(*out) for out in outs],
        compiler_params=params(52),
        cost_estimate=cost(0),
        name="scan_backward",
    )(place, *in_hbm((bc, decay, dt, skip, act, sp, u, step, slope, dy, h)))


def tail_kernel(
    place_ref,
    len_ref,
    *refs,
    micros,
    count,
    taps,
    clusters,
    ranks,
    chunks,
    states,
):
    def take(number):
        nonlocal refs
        taken, refs = refs[:number], refs[number:]
        return taken

    code_own_ref, code_other_ref = take(2)
    sact_ref, dpre_ref, alog_sum_ref, back_ref = take(4)
    dtx_ref, bc_own_ref, bc_other_ref, decay_ref = take(4)
    bend_ref, inner_ref, act_ref, high_ref, convw_ref = take(5)
    normed_ref, weight_ref, gate_part_ref, x_ref = take(4)
    keep_ref, send_ref, dnormed_ref = take(3)
    mask_ref, code_ref, wcode_ref, vec_ref, alog_ref, total_ref, win_ref, sems, low_ref = refs[:9]
    code_turned_ref, rank_turned_ref = refs[9:]

    step = pl.program_id(0)
    rows = micros * count
    eighth = states // 2
    edge = LANES // 2
    half, core, cube, face = (place_ref[k] for k in range(4))
    pair = step ^ face
    span = LANES + 32

    def fetch(k):
        source = weight_ref.at[0, pl.ds(2 * (k ^ face), 2), half]
        return (pltpu.make_async_copy(source, win_ref.at[k], sems.at[k]),)

    stream(step, win_ref.shape[0], fetch)

    def pack_row(chunk):
        relative = chunk ^ cube
        return (relative & 3) * span + LANES + (relative >> 2) * 16

    def place_pair(start, size, cols, even, odd):
        keep_ref[aligned(start, size, 16), cols] = jnp.where(core == 0, even, odd).astype(BF16)
        send_ref[aligned(start, size, 16), cols] = jnp.where(core == 0, odd, even).astype(BF16)

    @pl.when(step == 0)
    def _():
        fill_masks(len_ref, mask_ref, micros, count, taps, clusters)
        total_ref[...] = gate_part_ref[...].astype(F32)
        code_ref[...] = (
            code_own_ref[...].astype(F32) + code_other_ref[...].astype(F32)
        ).astype(BF16)
        code_turned_ref[...] = code_ref[...].T
        rank_turned_ref[...] = high_ref[...].T
        alog_ref[...] = alog_sum_ref[...] * (decay_ref[...] * (1.0 / LOG2E))

    code = code_ref[...]
    lane = lax.broadcasted_iota(jnp.int32, (1, LANES), 1)
    for part in range(2):
        source = lanes(2 * (2 * pair + part) + half)
        cols = slice(part * LANES, (part + 1) * LANES)
        wcode_ref[:ranks, cols] = dtx_ref[:, source]
        own = bc_own_ref[:, :, source].reshape(states, LANES)
        other = bc_other_ref[:, :, source].reshape(states, LANES)
        wcode_ref[ranks : ranks + states, cols] = jnp.where(half == 0, own, other)
        wcode_ref[ranks + states : ranks + 2 * states, cols] = jnp.where(half == 0, other, own)
        wcode_ref[ranks + 2 * states :, cols] = jnp.zeros(
            (LANES - ranks - 2 * states, LANES), BF16
        )
    for part in range(2):
        cols = slice(part * LANES, (part + 1) * LANES)
        chunk = 2 * pair + part
        source = 2 * chunk + half
        weights = convw_ref[:, lanes(source)]
        dact = sact_ref[:, cols] + dot(code, wcode_ref[:, cols], 1, 0)
        dconv = dact * bend_ref[:, cols].astype(F32)
        inner = inner_ref[:, cols]
        dinner = weights[taps - 1 : taps] * dconv
        sums = [None] * (taps + 1)
        sums[taps - 1] = jnp.sum(dconv * inner, axis=0, keepdims=True)
        sums[taps] = jnp.sum(dconv, axis=0, keepdims=True)
        for back in range(1, taps):
            kept = dconv * mask_ref[back]
            dinner = dinner + weights[taps - 1 - back : taps - back] * pltpu.roll(
                kept, rows - back, 0
            )
            sums[taps - 1 - back] = jnp.sum(
                kept * pltpu.roll(inner, back, 0), axis=0, keepdims=True
            )
        for k in range(taps + 1):
            vec_ref[k : k + 1, lanes(chunk)] = sums[k]
        vec_ref[taps + 1 : taps + 3, lanes(chunk)] = back_ref[:, lanes(chunk)]
        low_ref[:, cols] = dinner.astype(BF16)

        act = act_ref[:, cols]
        start = pack_row(chunk)
        code_rows = dot(code_turned_ref[...], act, 1, 0)
        rank_rows = dot(rank_turned_ref[...], dpre_ref[:, cols], 1, 0)[ranks:]
        dtx_rows = code_rows[:ranks]
        even = jnp.where(lane < edge, dtx_rows, pltpu.roll(rank_rows, edge, 1))
        odd = jnp.where(lane < edge, pltpu.roll(dtx_rows, edge, 1), rank_rows)
        for k in range(4):
            place = slice(k * 16, (k + 1) * 16)
            place_pair(
                start, 16, slice(k * LANES, (k + 1) * LANES), even[place], odd[place]
            )
        state_rows = code_rows[ranks : ranks + 2 * states]
        place_pair(
            start, 16, slice(4 * LANES, 5 * LANES), state_rows[:states], state_rows[states:]
        )

    normed = normed_ref[...]
    grad = dot(low_ref[...], normed, 0, 0).astype(BF16)
    place = aligned(step * span, LANES, 16)
    keep_ref[place, :] = jnp.where(core == 0, grad[:LANES], grad[LANES:])
    send_ref[place, :] = jnp.where(core == 0, grad[LANES:], grad[:LANES])
    width = total_ref.shape[1]
    total_ref[...] += dot(low_ref[...], win_ref[step].reshape(2 * LANES, width), 1, 0)

    @pl.when(step == pl.num_programs(0) - 1)
    def _():
        total = total_ref[...]
        dnormed_ref[...] = total.astype(BF16)
        x = x_ref[...].astype(F32)
        unit = x * lax.rsqrt(jnp.mean(x * x, axis=1, keepdims=True) + EPSILON)
        vec_ref[taps + 3 : taps + 4, :] = jnp.sum(total * unit, axis=0, keepdims=True)
        is_gain = lax.broadcasted_iota(jnp.int32, (8, LANES), 0) == taps + 3
        for chunk in range(chunks):
            start = pack_row(chunk)
            vec = vec_ref[:, chunk * LANES : (chunk + 1) * LANES]
            far, farther = (pltpu.roll(vec, LANES - k * edge // 2, 1) for k in (1, 2))
            even = jnp.where(is_gain & (lane >= edge // 2), far, vec)
            odd = jnp.where(is_gain & (lane < edge // 2), far, farther)
            alog = [
                alog_ref[pl.ds(q * eighth * chunks + chunk, eighth, stride=chunks), :]
                for q in range(2)
            ]
            place_pair(
                start,
                16,
                slice(5 * LANES, 6 * LANES),
                jnp.concatenate([alog[0], even]),
                jnp.concatenate([alog[1], odd]),
            )
            blank = jnp.zeros((16, 2 * LANES), F32)
            place_pair(start, 16, slice(6 * LANES, 8 * LANES), blank, blank)


def tail(
    place,
    lengths,
    code_own,
    code_other,
    sact,
    dpre,
    alog,
    back,
    dtx,
    bc_own,
    bc_other,
    decay,
    bend,
    inner,
    act,
    high,
    convw,
    normed,
    w4,
    gate_part,
    x,
):
    rows, own = act.shape
    chunks = own // LANES
    width = normed.shape[1]
    micros, _, clusters = lengths.shape
    count = rows // micros
    taps = convw.shape[0]
    ranks = dtx.shape[0]
    states = decay.shape[0] // chunks
    cols = 2 * LANES
    extent = 4 * (LANES + 32)

    def by_cols(height):
        return pl.BlockSpec((height, cols), lambda i, p: (0, i ^ p[FACE]))

    in_specs = (
        [pl.BlockSpec(memory_space=pltpu.SMEM)]
        + [whole((rows, LANES))] * 2
        + [by_cols(rows)] * 2
        + [whole(alog.shape), whole(back.shape)]
        + [whole(array.shape) for array in (dtx, bc_own, bc_other, decay)]
        + [by_cols(rows)] * 3
        + [whole(array.shape) for array in (high, convw, normed)]
        + [
            ANY,
            whole((rows, width)),
            whole((rows, width)),
        ]
    )
    return pl.pallas_call(
        functools.partial(
            tail_kernel,
            micros=micros,
            count=count,
            taps=taps,
            clusters=clusters,
            ranks=ranks,
            chunks=chunks,
            states=states,
        ),
        grid_spec=pltpu.PrefetchScalarGridSpec(
            num_scalar_prefetch=1,
            grid=(chunks // 2,),
            in_specs=in_specs,
            out_specs=[whole((extent, width)), whole((extent, width)), whole((rows, width))],
            scratch_shapes=[
                pltpu.VMEM((taps, rows, LANES), F32),
                pltpu.VMEM((rows, LANES), BF16),
                pltpu.VMEM((LANES, cols), BF16),
                pltpu.VMEM((8, own), F32),
                pltpu.VMEM((states * chunks, LANES), F32),
                pltpu.VMEM((rows, width), F32),
                pltpu.VMEM((chunks // 2, 2, LANES, width), BF16),
                pltpu.SemaphoreType.DMA((chunks // 2,)),
                pltpu.VMEM((rows, cols), BF16),
                pltpu.VMEM((LANES, rows), BF16),
                pltpu.VMEM((2 * ranks, rows), BF16),
            ],
        ),
        out_shape=[
            hbm((extent, width), BF16),
            hbm((extent, width), BF16),
            hbm((rows, width), BF16),
        ],
        compiler_params=params(34),
        cost_estimate=cost(7),
        name="tail",
    )(
        place,
        lengths,
        *in_hbm([code_own]),
        code_other,
        *in_hbm(
            (
                sact,
                dpre,
                alog,
                back,
                dtx,
                bc_own,
                bc_other,
                decay,
                bend,
                inner,
                act,
                high,
                convw,
                normed,
                w4,
                gate_part,
                x,
            )
        ),
    )


def fetch_halves(source, which, half, target_ref, sems):
    copies = []
    for k in range(target_ref.shape[0]):
        pair = pl.ds(2 * k, 2)
        block = source.at[pair, half] if which is None else source.at[which, pair, half]
        copies.append(pltpu.make_async_copy(block, target_ref.at[k], sems.at[k]))
    for copy in copies:
        copy.start()
    return copies


def products_kernel(
    place_ref,
    gated_ref,
    dgate_ref,
    out_ref,
    weight_ref,
    mixed_ref,
    dnormed_ref,
    wout_ref,
    wgate_ref,
    out_sems,
    gate_sems,
):
    half = place_ref[HALF]
    width = mixed_ref.shape[1]
    jobs = (
        (fetch_halves(out_ref, None, half, wout_ref, out_sems), gated_ref, wout_ref, mixed_ref),
        (fetch_halves(weight_ref, 1, half, wgate_ref, gate_sems), dgate_ref, wgate_ref, dnormed_ref),
    )
    for copies, left_ref, right_ref, result_ref in jobs:
        total = None
        for k, copy in enumerate(copies):
            copy.wait()
            left = left_ref[:, 2 * k * LANES : 2 * (k + 1) * LANES]
            term = dot(left, right_ref[k].reshape(-1, width), 1, 0)
            total = term if total is None else total + term
        result_ref[...] = total.astype(BF16)


def products(place, gated, dgate, wout3, w4):
    rows, own = gated.shape
    width = w4.shape[-1]
    pairs = own // (2 * LANES)
    return pl.pallas_call(
        products_kernel,
        grid_spec=pltpu.PrefetchScalarGridSpec(
            num_scalar_prefetch=1,
            grid=(1,),
            in_specs=[whole((rows, own)), whole((rows, own)), ANY, ANY],
            out_specs=[whole((rows, width))] * 2,
            scratch_shapes=[
                pltpu.VMEM((pairs, 2, LANES, width), BF16),
                pltpu.VMEM((pairs, 2, LANES, width), BF16),
                pltpu.SemaphoreType.DMA((pairs,)),
                pltpu.SemaphoreType.DMA((pairs,)),
            ],
        ),
        out_shape=[hbm((rows, width), BF16)] * 2,
        compiler_params=params(20),
        cost_estimate=cost(4),
        name="products",
    )(place, *in_hbm((gated, dgate, wout3, w4)))


def finish_kernel(x_ref, mine_ref, theirs_ref, cotan_ref, gain_ref, grad_ref):
    x = x_ref[...].astype(F32)
    scale = lax.rsqrt(jnp.mean(x * x, axis=1, keepdims=True) + EPSILON)
    unit = x * scale
    dhat = (mine_ref[...].astype(F32) + theirs_ref[...].astype(F32)) * gain_ref[...]
    grad_ref[...] = cotan_ref[...].astype(F32) + scale * (
        dhat - unit * jnp.mean(dhat * unit, axis=1, keepdims=True)
    )


def finish(x, mine, theirs, cotan, gain):
    rows, width = x.shape
    by_rows = pl.BlockSpec((rows // 4, width), lambda i: (i, 0))
    return pl.pallas_call(
        finish_kernel,
        grid=(4,),
        in_specs=[by_rows] * 4 + [whole(gain.shape)],
        out_specs=by_rows,
        out_shape=jax.ShapeDtypeStruct((rows, width), F32),
        compiler_params=params(16),
        cost_estimate=cost(0),
        name="finish",
    )(*in_hbm((x, mine)), theirs, *in_hbm((cotan, gain)))


def unpack_kernel(
    near_ref,
    far_ref,
    out_ref,
    dtx_ref,
    dt_ref,
    bc_ref,
    alog_ref,
    convw_ref,
    convb_ref,
    bias_ref,
    skip_ref,
    out_grad_ref,
    *,
    eighth,
    taps,
    edge,
):
    pack = near_ref[...].astype(F32) + far_ref[...].astype(F32)
    turned = jnp.concatenate([pack[:, k * LANES : (k + 1) * LANES] for k in range(4)]).T
    dtx_ref[...] = turned[:edge]
    dt_ref[...] = turned[edge:]
    rows = pack[:, 4 * LANES : 5 * LANES]
    bc_ref[0] = rows[:eighth]
    bc_ref[1] = rows[eighth:]
    rows = pack[:, 5 * LANES : 6 * LANES]
    alog_ref[...] = rows[:eighth]
    vec = rows[eighth:, :edge]
    convw_ref[...] = vec[:taps]
    convb_ref[...] = vec[taps : taps + 1]
    bias_ref[...] = vec[taps + 1 : taps + 2]
    skip_ref[...] = vec[taps + 2 : taps + 3]
    out_grad_ref[...] = out_ref[...].astype(F32)


def unpack(near, far, out, eighth, taps, ranks):
    edge = LANES // 2
    shapes = [
        (edge, ranks),
        (edge, ranks),
        (2, eighth, LANES),
        (eighth, LANES),
        (taps, edge),
        (1, edge),
        (1, edge),
        (1, edge),
        out.shape,
    ]
    return pl.pallas_call(
        functools.partial(unpack_kernel, eighth=eighth, taps=taps, edge=edge),
        grid=(1,),
        in_specs=[whole(array.shape) for array in (near, far, out)],
        out_specs=[whole(shape) for shape in shapes],
        out_shape=[jax.ShapeDtypeStruct(shape, F32) for shape in shapes],
        cost_estimate=cost(0),
        name="unpack",
    )(near, far, out)


def swap_pair(array):
    count = lax.axis_size("state")
    return lax.ppermute(array, "state", [(pos, pos ^ 1) for pos in range(count)])


def swap_bit(array, bits):
    return lax.ppermute(array, "dp", [(pos, pos ^ bits) for pos in range(lax.axis_size("dp"))])


def swap_both(array, bits=0):
    states = lax.axis_size("state")
    pairs = []
    for d in range(lax.axis_size("dp")):
        for s in range(states):
            pairs.append((d * states + s, (((d & ~1) | s) ^ bits) * states + (d & 1)))
    return lax.ppermute(array, ("dp", "state"), pairs)


def add_mixed(x, mine, theirs):
    return (x.astype(F32) + (mine.astype(F32) + theirs.astype(F32))).astype(BF16)


def add_quarters(kept, got, start=0, stop=None):
    extent = kept.shape[0] // 4
    stop = extent if stop is None else stop
    return [
        kept[k * extent + start : k * extent + stop] + got[k * extent + start : k * extent + stop]
        for k in range(4)
    ]


def trade_quarters(quarters):
    return [quarters[0]] + [swap_bit(quarters[k], k * X_BIT) for k in range(1, 4)]


def sum_quarters(quarters):
    left, right = (quarters[k].astype(F32) + quarters[k + 1].astype(F32) for k in (0, 2))
    return (left + right).astype(BF16)


CORE_BIT, X_BIT, ZH_BIT = 1, 2, 8


def shards(
    tokens,
    cluster_len,
    norm_gain,
    in_weight,
    conv_weight,
    conv_bias,
    dtx_weight,
    dt_weight,
    dt_bias,
    bc_weight,
    a_log,
    skip_gain,
    out_weight,
    cotangent,
):
    micros, count, width = tokens.shape
    inner = out_weight.shape[0]
    taps = conv_weight.shape[0]
    ranks = dtx_weight.shape[1]
    chunks = inner // (2 * LANES)
    own = chunks * LANES
    rows = micros * count
    edge = LANES // 2
    span = LANES + 32
    dp_parts = lax.axis_size("dp")
    state_count = lax.axis_size("state")
    dp_pos = lax.axis_index("dp")
    state_pos = lax.axis_index("state")
    half = state_pos & 1
    fast = state_count == 2 and dp_parts == 2 * chunks == 16
    if fast:
        place = jnp.stack([half, dp_pos & 1, dp_pos >> 1, (dp_pos >> 1) & 3])
        bc_own, alog_own = bc_weight, a_log
        bc_other, alog_other = swap_pair(bc_weight), swap_pair(a_log)
    else:
        place = jnp.stack([half, 0, 0, 0])
        bc_all = lax.all_gather(bc_weight, "state", axis=1, tiled=True)
        alog_all = lax.all_gather(a_log, "state", axis=0, tiled=True)
        eighth = alog_all.shape[0] // 2
        bc_own, bc_other = (
            lax.dynamic_slice_in_dim(bc_all, which * eighth, eighth, 1)
            for which in (half, 1 - half)
        )
        alog_own, alog_other = (
            lax.dynamic_slice_in_dim(alog_all, which * eighth, eighth, 0)
            for which in (half, 1 - half)
        )
    place = place.astype(jnp.int32)
    eighth = alog_own.shape[0]
    states = 2 * eighth

    x = tokens.reshape(rows, width)
    cotan = cotangent.reshape(rows, width)
    w4 = in_weight.reshape(2, chunks, 2, LANES, width)
    wout3 = out_weight.reshape(chunks, 2, LANES, width)
    dtx, dt = dtx_weight.T, dt_weight.T
    bias = dt_bias.reshape(-1, LANES)
    skip = skip_gain.reshape(-1, LANES)

    normed, act_all, act, inner_own, bend, gate = project(
        place, cluster_len, x, norm_gain[None], w4, conv_weight, conv_bias.reshape(-1, LANES)
    )
    bc, rank, high, decay, sp, u, step, slope, h, dy, gated, dgate, keep, send = scan_forward(
        place,
        cluster_len,
        act_all,
        bc_own,
        bc_other,
        alog_own,
        alog_other,
        dtx,
        dt,
        bias,
        skip,
        act,
        gate,
        wout3,
        cotan,
        normed,
    )
    if fast:
        early = swap_bit(send, CORE_BIT)
    mixed_part, dn_gate = products(place, gated, dgate, wout3, w4)
    if fast:
        *quarters, mixed_part, dn_gate, sp = lax.optimization_barrier(
            (*add_quarters(keep, early), mixed_part, dn_gate, sp)
        )
        early_got = trade_quarters(quarters)
    code_own, sact, dpre, alog, back = scan_backward(
        place, micros, bc, decay, dt, skip, act, sp, u, step, slope, dy, h
    )
    if fast:
        *early_got, code_own, mixed_part = lax.optimization_barrier(
            (*early_got, code_own, mixed_part)
        )
    code_other = swap_pair(code_own)
    mixed_other = swap_pair(mixed_part)
    if fast:
        block = sum_quarters(early_got)
        out_keep, out_send, gate_sum = block[:edge], block[edge:LANES], block[LANES:]
        out_send, gate_sum, bend = lax.optimization_barrier((out_send, gate_sum, bend))
        out_got = swap_bit(out_send, ZH_BIT)
    late_keep, late_send, dnormed_part = tail(
        place,
        cluster_len,
        code_own,
        code_other,
        sact,
        dpre,
        alog,
        back,
        dtx,
        bc_own,
        bc_other,
        decay,
        bend,
        inner_own,
        act,
        high,
        conv_weight,
        normed,
        w4,
        dn_gate,
        x,
    )
    mixed = add_mixed(x, mixed_part, mixed_other)
    if fast:
        late_send, mixed_other = lax.optimization_barrier((late_send, mixed_other))
        mixed = add_mixed(x, mixed_part, mixed_other)
        late = swap_bit(late_send, CORE_BIT)
        late_got = trade_quarters(add_quarters(late_keep, late))
    dnormed_other = swap_pair(dnormed_part)
    tokens_grad = finish(x, dnormed_part, dnormed_other, cotan, norm_gain[None])
    if fast:
        out_own = swap_both(out_keep + out_got)
        *late_got, out_own, tokens_grad, mixed = lax.optimization_barrier(
            (*late_got, out_own, tokens_grad, mixed)
        )
        block = sum_quarters(late_got)
        inner_sum = block[:LANES]
        upper = dp_pos >= dp_parts // 2
        crossing = jnp.where(upper, inner_sum, gate_sum)
        first, second = crossing[:edge], crossing[edge:]
        first, pack_far, pack_near = lax.optimization_barrier(
            (first, block[-16:], block[LANES:-16])
        )
        pack_far = swap_both(pack_far, ZH_BIT)
        first_got = swap_bit(first, ZH_BIT)
        pack_near = swap_both(pack_near)
        first_got, pack_far, pack_near = lax.optimization_barrier((first_got, pack_far, pack_near))
        second_got = swap_bit(second, ZH_BIT)
        gain_mine = (
            pack_near[:, 5 * LANES : 6 * LANES].astype(F32)
            + pack_far[:, 5 * LANES : 6 * LANES].astype(F32)
        ).astype(BF16)
        gain_both = gain_mine[-1].astype(F32) + swap_bit(gain_mine, CORE_BIT)[-1].astype(F32)
        extent = width // (dp_parts * state_count)
        gain_grad = lax.dynamic_slice_in_dim(gain_both, (dp_pos & 1) * extent, extent, 0)
        (
            dtx_grad,
            dt_grad,
            bc_grad,
            alog_grad,
            convw_grad,
            convb_grad,
            bias_grad,
            skip_grad,
            out_own,
        ) = unpack(pack_near, pack_far, out_own, eighth, taps, ranks)
        convb_grad, bias_grad, skip_grad = (
            array[0] for array in (convb_grad, bias_grad, skip_grad)
        )
        second_got, dtx_grad, dt_grad, out_own = lax.optimization_barrier(
            (second_got, dtx_grad, dt_grad, out_own)
        )
        in_grad = jnp.where(upper, gate_sum, inner_sum).astype(F32) + jnp.concatenate(
            [first_got, second_got]
        ).astype(F32)
    mixed = mixed.reshape(micros, count, width)
    tokens_grad = tokens_grad.reshape(micros, count, width)

    if not fast:
        def total(array):
            return lax.psum(array.astype(F32), "dp")

        def both_rows(array):
            mine = array.reshape(chunks, 1, LANES, -1)
            other = swap_pair(mine)
            low = jnp.where(half == 0, mine, other)
            high = jnp.where(half == 0, other, mine)
            return jnp.concatenate([low, high], axis=1).reshape(2 * own, -1)

        every = dp_parts * state_count
        at = dp_pos * state_count + state_pos

        def cut_own(array):
            extent = array.shape[0] // every
            return lax.dynamic_slice_in_dim(array, at * extent, extent, 0)

        pair = total(jnp.stack([keep, send])).reshape(2, 2, 2, 2 * LANES, width)
        outs = pair[:, :, :, :LANES].reshape(2, 2, 2, 2, edge, width)
        outs = jnp.transpose(outs, (3, 1, 2, 0, 4, 5)).reshape(own, width)
        gates = jnp.moveaxis(pair[:, :, :, LANES:], 0, 2).reshape(own, width)
        pair = total(jnp.stack([late_keep, late_send])).reshape(2, 2, 2, span, width)
        inners = jnp.moveaxis(pair[:, :, :, :LANES], 0, 2).reshape(own, width)
        packs = pair[:, :, :, LANES:].reshape(2, 2, 2, 2, 16, width // LANES, LANES)
        packs = jnp.transpose(packs, (3, 1, 2, 0, 5, 4, 6)).reshape(chunks, 2, -1, 16, LANES)
        small = packs[:, :, :4].reshape(chunks, 2, ranks, 2, edge)
        small = both_rows(jnp.transpose(small, (0, 1, 4, 3, 2)).reshape(own, 2 * ranks))
        in_grad = cut_own(jnp.concatenate([both_rows(inners), both_rows(gates)]))
        out_own = cut_own(both_rows(outs))
        mine = cut_own(small)
        dtx_grad, dt_grad = mine[:, :ranks], mine[:, ranks:]
        vec_rows = jnp.swapaxes(packs[:, :, 5, eighth:, :edge], 2, 3).reshape(own, -1)
        gain_sum = vec_rows[:, -1].reshape(chunks, 2, 2, -1).swapaxes(1, 2).reshape(-1)
        gain_grad = cut_own(gain_sum + swap_pair(gain_sum))
        vec = cut_own(both_rows(vec_rows)).T
        state_rows = jnp.concatenate([packs[:, :, 4], packs[:, :, 5, :eighth]], axis=2)
        state_rows = state_rows.reshape(chunks, 2, 3, eighth, LANES)
        state_rows = jnp.transpose(state_rows, (0, 4, 2, 1, 3)).reshape(own, -1)
        extent = inner // dp_parts
        state_part = lax.dynamic_slice_in_dim(both_rows(state_rows), dp_pos * extent, extent, 0)
        state_part = state_part.T.reshape(3, state_count, -1, extent)
        state_part = lax.dynamic_index_in_dim(state_part, state_pos, 1, keepdims=False)
        bc_grad, alog_grad = state_part[:2], state_part[2]
        convw_grad, convb_grad, bias_grad, skip_grad = (
            vec[:taps], vec[taps], vec[taps + 1], vec[taps + 2]
        )

    return (
        mixed,
        tokens_grad,
        gain_grad,
        in_grad,
        convw_grad,
        convb_grad,
        dtx_grad,
        dt_grad,
        bias_grad,
        bc_grad,
        alog_grad,
        skip_grad,
        out_own,
    )


def solution(mesh):
    return jax.shard_map(
        shards,
        mesh=mesh,
        in_specs=(
            P(None, "dp", None),
            P(None, "dp", None),
            P(),
            P(),
            P(),
            P(),
            P(),
            P(),
            P(),
            P(None, "state", None),
            P("state", None),
            P(),
            P(),
            P(None, "dp", None),
        ),
        out_specs=(
            P(None, "dp", None),
            P(None, "dp", None),
            P(("dp", "state")),
            P(("dp", "state"), None),
            P(None, ("dp", "state")),
            P(("dp", "state")),
            P(("dp", "state"), None),
            P(("dp", "state"), None),
            P(("dp", "state")),
            P(None, "state", "dp"),
            P("state", "dp"),
            P(("dp", "state")),
            P(("dp", "state"), None),
        ),
        check_vma=False,
    )
```

```python
import functools
import math

import jax
import jax.numpy as jnp
from jax import lax
from jax.experimental import pallas as pl
from jax.experimental.pallas import tpu as pltpu
from jax.sharding import PartitionSpec as P

EPSILON = 1e-05
LANES = 128
RESET = 1e4
LOG2E = math.log2(math.e)
F32 = jnp.float32
BF16 = jnp.bfloat16
MIB = 1024 * 1024


def dot(left, right, left_dim, right_dim):
    return lax.dot_general(
        left, right, (((left_dim,), (right_dim,)), ((), ())), preferred_element_type=F32
    )


def params(mib):
    return pltpu.CompilerParams(
        vmem_limit_bytes=mib * MIB, dimension_semantics=("arbitrary",)
    )


ANY = pl.BlockSpec(memory_space=pl.ANY)


def stream(step, steps, fetch):
    @pl.when(step == 0)
    def _():
        for k in range(steps):
            for copy in fetch(k):
                copy.start()

    for copy in fetch(step):
        copy.wait()


def whole(shape):
    return pl.BlockSpec(shape, lambda *_: (0,) * len(shape))


sigmoid = jax.nn.sigmoid


def log_one_plus(value):
    series = value * (1.0 - value * (0.5 - value * (1.0 / 3.0)))
    return jnp.where(value < 1e-3, series, jnp.log(1.0 + value))


def lanes(index):
    return pl.ds(pl.multiple_of(index * LANES, LANES), LANES)


def cost(micros):
    return pl.CostEstimate(
        flops=int(micros * 1e9), bytes_accessed=int(micros * 1e6), transcendentals=0
    )


def hbm(shape, dtype):
    return pltpu.HBM(shape, dtype)


def in_hbm(arrays):
    return [pltpu.with_memory_space_constraint(array, pltpu.HBM) for array in arrays]


def two_lanes(index):
    return pl.ds(pl.multiple_of(index * 2 * LANES, 2 * LANES), 2 * LANES)


def aligned(start, size, to=8):
    return pl.ds(pl.multiple_of(start, to), size)


SEGMENTS = 4

HALF, CORE, CUBE, FACE = range(4)


def fill_masks(len_ref, mask_ref, micros, count, taps, clusters):
    place = lax.broadcasted_iota(jnp.int32, (count, LANES), 0)
    for micro in range(micros):
        rows = pl.ds(micro * count, count)
        for back in range(1, taps):
            apart = place < back
            start = 0
            for cluster in range(clusters - 1):
                start = start + len_ref[micro, 0, cluster]
                apart = apart | ((place >= start) & (place < start + back))
            mask_ref[back, rows, :] = jnp.where(apart, 0.0, 1.0)
            if back == 1:
                mask_ref[0, rows, :] = jnp.where(apart, 1.0, 0.0)


def project_kernel(
    place_ref,
    len_ref,
    gain_ref,
    convw_ref,
    convb_ref,
    x_far,
    weight_far,
    normed_far,
    act_far,
    own_act_far,
    inner_far,
    bend_far,
    gate_far,
    mask_ref,
    x_ref,
    win_ref,
    wgate_ref,
    normed_ref,
    act_ref,
    own_act_ref,
    inner_ref,
    bend_ref,
    gate_ref,
    in_sems,
    out_sems,
    *,
    micros,
    count,
    taps,
    clusters,
):
    half = place_ref[HALF]
    chunks = win_ref.shape[0]
    inward = [pltpu.make_async_copy(x_far, x_ref, in_sems.at[2 * chunks])]
    for k in range(chunks):
        inward.append(pltpu.make_async_copy(weight_far.at[0, k], win_ref.at[k], in_sems.at[2 * k]))
        inward.append(
            pltpu.make_async_copy(
                weight_far.at[1, k, half], wgate_ref.at[k], in_sems.at[2 * k + 1]
            )
        )
    for copy in inward:
        copy.start()
    outward = []

    def put(source, target):
        outward.append(pltpu.make_async_copy(source, target, out_sems.at[len(outward)]))
        outward[-1].start()

    fill_masks(len_ref, mask_ref, micros, count, taps, clusters)
    inward[0].wait()
    rows = x_ref[...].astype(F32)
    scale = lax.rsqrt(jnp.mean(rows * rows, axis=1, keepdims=True) + EPSILON)
    normed = (rows * scale * gain_ref[...]).astype(BF16)
    normed_ref[...] = normed
    put(normed_ref, normed_far)
    for k in range(chunks):
        inward[2 * k + 1].wait()
        inward[2 * k + 2].wait()
        proj = dot(normed, win_ref[k].reshape(2 * LANES, -1), 1, 1)
        own = slice(k * LANES, (k + 1) * LANES)
        gate_ref[:, own] = dot(normed, wgate_ref[k], 1, 1)
        inners, sigs, acts = [], [], []
        for part in range(2):
            cols = slice((2 * k + part) * LANES, (2 * k + part + 1) * LANES)
            inner = proj[:, part * LANES : (part + 1) * LANES]
            conved = convb_ref[2 * k + part : 2 * k + part + 1, :]
            conved = conved + convw_ref[taps - 1 : taps, cols] * inner
            for back in range(1, taps):
                shifted = pltpu.roll(inner, back, 0) * mask_ref[back]
                conved = conved + convw_ref[taps - 1 - back : taps - back, cols] * shifted
            sig = sigmoid(conved)
            act = conved * sig
            act_ref[:, cols] = act.astype(BF16)
            inners.append(inner)
            sigs.append(sig)
            acts.append(act)
        inner_ref[:, own] = jnp.where(half == 0, *inners)
        act, sig = jnp.where(half == 0, *acts), jnp.where(half == 0, *sigs)
        bend_ref[:, own] = (sig + act * (1.0 - sig)).astype(BF16)
        own_act_ref[:, own] = act.astype(BF16)
        if k % 2:
            group = pl.ds((k - 1) * LANES, 2 * LANES)
            wide = pl.ds(2 * (k - 1) * LANES, 4 * LANES)
            put(act_ref.at[:, wide], act_far.at[:, wide])
            for near, far in (
                (gate_ref, gate_far),
                (inner_ref, inner_far),
                (bend_ref, bend_far),
                (own_act_ref, own_act_far),
            ):
                put(near.at[:, group], far.at[:, group])
    for copy in outward:
        copy.wait()


def project(place, lengths, x, gain, w4, conv_weight, conv_bias):
    rows, width = x.shape
    chunks = w4.shape[1]
    micros, _, clusters = lengths.shape
    taps = conv_weight.shape[0]
    own = chunks * LANES
    outs = [
        ((rows, width), BF16),
        ((rows, 2 * own), BF16),
        ((rows, own), BF16),
        ((rows, own), F32),
        ((rows, own), BF16),
        ((rows, own), F32),
    ]
    return pl.pallas_call(
        functools.partial(
            project_kernel, micros=micros, count=rows // micros, taps=taps, clusters=clusters
        ),
        grid_spec=pltpu.PrefetchScalarGridSpec(
            num_scalar_prefetch=1,
            grid=(1,),
            in_specs=[
                pl.BlockSpec(memory_space=pltpu.SMEM),
                whole(gain.shape),
                whole(conv_weight.shape),
                whole(conv_bias.shape),
                ANY,
                ANY,
            ],
            out_specs=[ANY] * len(outs),
            scratch_shapes=[
                pltpu.VMEM((taps, rows, LANES), F32),
                pltpu.VMEM((rows, width), BF16),
                pltpu.VMEM((chunks, 2, LANES, width), BF16),
                pltpu.VMEM((chunks, LANES, width), BF16),
            ]
            + [pltpu.VMEM(*out) for out in outs]
            + [
                pltpu.SemaphoreType.DMA((2 * chunks + 1,)),
                pltpu.SemaphoreType.DMA((1 + 5 * chunks // 2,)),
            ],
        ),
        out_shape=[hbm(*out) for out in outs],
        compiler_params=params(30),
        cost_estimate=cost(6),
        name="project",
    )(place, *in_hbm((lengths, gain, conv_weight, conv_bias, x, w4)))


def every_row(ref, row, height):
    return ref[pl.ds(row, height, stride=0), :]


def b_at(n, eighth):
    return (n // eighth) * 2 * eighth + n % eighth


def c_at(n, eighth):
    return b_at(n, eighth) + eighth


def forward_kernel(
    place_ref,
    len_ref,
    act_all_ref,
    bc_own_ref,
    bc_other_ref,
    alog_own_ref,
    alog_other_ref,
    dtx_ref,
    dt_ref,
    bias_ref,
    skip_ref,
    act_ref,
    *refs,
    micros,
    count,
    states,
    chunks,
    clusters,
):
    gate_far, wout_far, cotan_far, normed_far = refs[:4]
    bc_ref, rank_ref, rank_high_ref, decay_ref = refs[4:8]
    sp_far, u_far, step_far, slope_far, h_far, dy_far = refs[8:14]
    gated_far, dgate_far, keep_far, send_far = refs[14:18]
    mask_ref, y_ref, tmp_ref, wide_ref = refs[18:22]
    gate_ref, wout_ref, cotan_ref, normed_ref = refs[22:26]
    sp_ref, u_ref, step_ref, slope_ref, h_ref, dy_ref = refs[26:32]
    gated_ref, dgate_ref, keep_ref, send_ref = refs[32:36]
    in_sems, out_sems = refs[36:]
    rows = micros * count
    eighth = states // 2
    half, core, cube, face = (place_ref[k] for k in range(4))
    first = half == 0
    inward = [
        pltpu.make_async_copy(source, target, in_sems.at[k])
        for k, (source, target) in enumerate(
            (
                (gate_far, gate_ref),
                (wout_far.at[:, half], wout_ref),
                (cotan_far, cotan_ref),
                (normed_far, normed_ref),
            )
        )
    ]
    for copy in inward:
        copy.start()
    outward = []

    def put(source, target):
        outward.append(pltpu.make_async_copy(source, target, out_sems.at[len(outward)]))
        outward[-1].start()

    ranks = dtx_ref.shape[0]
    weights = jnp.concatenate(
        [dtx_ref[...]] + [ref[...].reshape(states, -1) for ref in (bc_own_ref, bc_other_ref)]
    )
    product = dot(act_all_ref[...], weights, 1, 1)
    own, other = product[:, ranks : ranks + states], product[:, ranks + states :]
    bc_ref[:, :states] = jnp.where(first, own, other)
    bc_ref[:, states:] = jnp.where(first, other, own)
    spread_lanes(bc_ref, wide_ref)

    fill_masks(len_ref, mask_ref, micros, count, 2, clusters)
    for chunk in range(chunks):
        cols = lanes(2 * chunk + half)
        own, other = alog_own_ref[:, cols], alog_other_ref[:, cols]
        tmp_ref[pl.ds(chunk * states, eighth), :] = jnp.where(first, own, other)
        tmp_ref[pl.ds(chunk * states + eighth, eighth), :] = jnp.where(first, other, own)
    for n in range(states):
        decay_ref[pl.ds(n * chunks, chunks), :] = -LOG2E * jnp.exp(
            tmp_ref[pl.ds(n, chunks, stride=states), :]
        )

    rank = product[:, :ranks].astype(BF16)
    rank_ref[...] = rank
    rank_high_ref[...] = jnp.concatenate([jnp.zeros_like(rank), rank], axis=1)
    for chunk in range(chunks):
        cols = slice(chunk * LANES, (chunk + 1) * LANES)
        bias = bias_ref[pl.ds(2 * chunk + half, 1), :]
        pre = dot(rank, dt_ref[:, lanes(2 * chunk + half)], 1, 0) + bias
        tail_part = jnp.exp(-jnp.abs(pre))
        step = jnp.maximum(pre, 0.0) + log_one_plus(tail_part)
        slope = jnp.where(pre >= 0.0, 1.0, tail_part) / (1.0 + tail_part)
        step_ref[:, cols] = step
        slope_ref[:, cols] = slope.astype(BF16)
        held = step + RESET * mask_ref[0]
        source = step * act_ref[:, cols].astype(F32)
        for micro in range(micros):
            span = slice(micro * count, (micro + 1) * count)
            place = pl.ds((micro * chunks + chunk) * count, count)
            sp_ref[place, :] = held[span]
            u_ref[place, :] = source[span]
    put(sp_ref, sp_far)
    put(u_ref, u_far)
    put(step_ref, step_far)
    put(slope_ref, slope_far)

    for micro in range(micros):

        def advance(t, h, micro=micro):
            row = micro * count + t
            span = pl.ds(micro * chunks * count + t, chunks, stride=count)
            sp = sp_ref[span, :]
            u = u_ref[span, :]
            out = []
            y = None
            for n in range(states):
                decay = jnp.exp2(sp * decay_ref[pl.ds(n * chunks, chunks), :])
                now = decay * h[n] + u * every_row(wide_ref, b_at(n, eighth) * rows + row, chunks)
                h_ref[aligned((row * states + n) * chunks, chunks), :] = now
                out.append(now)
                term = now * every_row(wide_ref, c_at(n, eighth) * rows + row, chunks)
                y = term if y is None else y + term
            y_ref[span, :] = y
            return tuple(out)

        h = (jnp.zeros((chunks, LANES), F32),) * states
        segment = count // SEGMENTS
        for k in range(SEGMENTS):
            h = lax.fori_loop(k * segment, (k + 1) * segment, advance, h, unroll=8)
            extent = segment * states * chunks
            place = pl.ds((micro * SEGMENTS + k) * extent, extent)
            put(h_ref.at[place], h_far.at[place])

    for copy in inward:
        copy.wait()
    cotan = cotan_ref[...]
    for chunk in range(chunks):
        cols = slice(chunk * LANES, (chunk + 1) * LANES)
        places = [pl.ds((micro * chunks + chunk) * count, count) for micro in range(micros)]
        y = jnp.concatenate([y_ref[place, :] for place in places])
        y = y + skip_ref[pl.ds(2 * chunk + half, 1), :] * act_ref[:, cols].astype(F32)
        gate = gate_ref[:, cols]
        sig = sigmoid(gate)
        gated_ref[:, cols] = (y * (gate * sig)).astype(BF16)
        dgated = dot(cotan, wout_ref[chunk], 1, 1)
        dy = dgated * (gate * sig)
        for micro in range(micros):
            dy_ref[places[micro], :] = dy[micro * count : (micro + 1) * count]
        dgate_ref[:, cols] = (dgated * y * (sig * (1.0 + gate * (1.0 - sig)))).astype(BF16)
    put(dy_ref, dy_far)
    put(gated_ref, gated_far)
    put(dgate_ref, dgate_far)
    normed = normed_ref[...]
    edge = LANES // 2
    straight, first_core = (cube & 1) == 0, core == 0
    for r in range(0, chunks // 2, 2):
        for zh in range(2):
            pair = ((r + 4 * zh) ^ cube) >> 1
            grad = dot(gated_ref[:, two_lanes(pair)], cotan, 0, 0).astype(BF16)
            parts = grad[:LANES], grad[LANES:]
            for k in range(2):
                one = jnp.where(straight, parts[k], parts[1 - k])
                top, bottom = one[:edge], one[edge:]
                place = pl.ds((r + k) * 2 * LANES + zh * edge, edge)
                keep_ref[place, :] = jnp.where(first_core, top, bottom)
                send_ref[place, :] = jnp.where(first_core, bottom, top)
        for k in range(r, r + 2):
            grad = dot(dgate_ref[:, two_lanes(k ^ face)], normed, 0, 0).astype(BF16)
            place = pl.ds((2 * k + 1) * LANES, LANES)
            keep_ref[place, :] = jnp.where(first_core, grad[:LANES], grad[LANES:])
            send_ref[place, :] = jnp.where(first_core, grad[LANES:], grad[:LANES])
            place = pl.ds(k * 2 * LANES, 2 * LANES)
            put(send_ref.at[place], send_far.at[place])
            put(keep_ref.at[place], keep_far.at[place])
    for copy in outward:
        copy.wait()


def scan_forward(
    place,
    lengths,
    act_all,
    bc_own,
    bc_other,
    alog_own,
    alog_other,
    dtx,
    dt,
    bias,
    skip,
    act,
    gate,
    wout3,
    cotan,
    normed,
):
    rows, own = act.shape
    chunks = own // LANES
    states = 2 * alog_own.shape[0]
    width = cotan.shape[1]
    micros, _, clusters = lengths.shape
    ranks = dtx.shape[0]
    small = [
        ((rows, 2 * states), F32),
        ((rows, ranks), BF16),
        ((rows, 2 * ranks), BF16),
        ((states * chunks, LANES), F32),
    ]
    large = [
        ((chunks * rows, LANES), F32),
        ((chunks * rows, LANES), F32),
        ((rows, own), F32),
        ((rows, own), BF16),
        ((rows * states * chunks, LANES), F32),
        ((chunks * rows, LANES), F32),
        ((rows, own), BF16),
        ((rows, own), BF16),
        ((own, width), BF16),
        ((own, width), BF16),
    ]
    operands = (act_all, bc_own, bc_other, alog_own, alog_other, dtx, dt, bias, skip, act)
    streamed = (gate, wout3, cotan, normed)
    return pl.pallas_call(
        functools.partial(
            forward_kernel,
            micros=micros,
            count=rows // micros,
            states=states,
            chunks=chunks,
            clusters=clusters,
        ),
        grid_spec=pltpu.PrefetchScalarGridSpec(
            num_scalar_prefetch=1,
            grid=(1,),
            in_specs=[pl.BlockSpec(memory_space=pltpu.SMEM)]
            + [whole(operand.shape) for operand in operands]
            + [ANY] * len(streamed),
            out_specs=[whole(shape) for shape, _ in small] + [ANY] * len(large),
            scratch_shapes=[
                pltpu.VMEM((2, rows, LANES), F32),
                pltpu.VMEM((chunks * rows, LANES), F32),
                pltpu.VMEM((states * chunks, LANES), F32),
                pltpu.VMEM((2 * states * rows, LANES), F32),
                pltpu.VMEM((rows, own), F32),
                pltpu.VMEM((chunks, LANES, width), BF16),
                pltpu.VMEM((rows, width), BF16),
                pltpu.VMEM((rows, width), BF16),
            ]
            + [pltpu.VMEM(*out) for out in large]
            + [pltpu.SemaphoreType.DMA((4,)), pltpu.SemaphoreType.DMA((7 + chunks + micros * SEGMENTS,))],
        ),
        out_shape=[hbm(*out) for out in small + large],
        compiler_params=params(52),
        cost_estimate=cost(19),
        name="scan_forward",
    )(
        place,
        lengths,
        *in_hbm(operands[:1]),
        *operands[1:5],
        *in_hbm((*operands[5:], *streamed)),
    )


def spread_lanes(values_ref, wide_ref):
    rows, count = values_ref.shape
    for k in range(count):
        wide_ref[pl.ds(k * rows, rows), :] = jnp.broadcast_to(
            values_ref[:, k : k + 1], (rows, LANES)
        )


def backward_kernel(
    place_ref,
    bc_ref,
    decay_ref,
    dt_ref,
    skip_ref,
    act_ref,
    sp_ref,
    u_ref,
    step_ref,
    slope_ref,
    dy_ref,
    h_far,
    code_ref,
    sact_ref,
    dpre_ref,
    alog_ref,
    vec_ref,
    h_ref,
    s_ref,
    d_ref,
    terms_ref,
    sums_b_ref,
    sums_c_ref,
    wide_ref,
    sems,
    *,
    count,
    states,
    chunks,
):
    micro = pl.program_id(0)
    block = states * chunks
    segment = count // SEGMENTS

    def fetch(which, k):
        extent = segment * block
        buffer = h_ref.at[which % 2]
        return pltpu.make_async_copy(
            h_far.at[aligned((which * SEGMENTS + k) * extent, extent)],
            buffer.at[pl.ds(block + k * extent, extent)],
            sems.at[which % 2, k],
        )

    @pl.when(micro == 0)
    def _():
        for k in reversed(range(SEGMENTS)):
            fetch(0, k).start()
        for which in range(2):
            h_ref[which, pl.ds(0, block), :] = jnp.zeros((block, LANES), F32)
        alog_ref[...] = jnp.zeros_like(alog_ref)
        vec_ref[...] = jnp.zeros_like(vec_ref)

    half = place_ref[HALF]
    eighth = states // 2
    zero = (jnp.zeros((chunks, LANES), F32),) * states
    spread_lanes(bc_ref, wide_ref)

    @pl.when(micro + 1 < pl.num_programs(0))
    def _():
        for k in reversed(range(SEGMENTS)):
            fetch(micro + 1, k).start()

    side = micro % 2

    def put_terms(which, t, terms):
        for n in range(0, states, 2):
            pair = jnp.concatenate(terms[n : n + 2]).astype(BF16)
            place = aligned(t * block + n * chunks, 2 * chunks, 16)
            terms_ref[which, place, :] = pair

    def retreat(back, carry):
        flows, totals = carry
        for slot in range(4):
            t = count - 1 - (4 * back + slot)
            span = pl.ds(t, chunks, stride=count)
            sp = sp_ref[span, :]
            u = u_ref[span, :]
            dy = dy_ref[span, :]
            out_flows = []
            out_totals = []
            b_terms, c_terms = [], []
            d_sum = None
            s_sum = None
            for n in range(states):
                rate = decay_ref[pl.ds(n * chunks, chunks), :]
                dh = flows[n] + dy * every_row(wide_ref, c_at(n, eighth) * count + t, chunks)
                flow = jnp.exp2(sp * rate) * dh
                out_flows.append(flow)
                q = flow * h_ref[side, aligned(t * block + n * chunks, chunks), :]
                now = h_ref[side, aligned((t + 1) * block + n * chunks, chunks), :]
                out_totals.append(totals[n] + q * sp)
                d_term = q * rate
                s_term = dh * every_row(wide_ref, b_at(n, eighth) * count + t, chunks)
                d_sum = d_term if d_sum is None else d_sum + d_term
                s_sum = s_term if s_sum is None else s_sum + s_term
                b_terms.append(dh * u)
                c_terms.append(dy * now)
            s_ref[span, :] = s_sum
            d_ref[span, :] = d_sum
            put_terms(0, t, b_terms)
            put_terms(1, t, c_terms)
            flows, totals = tuple(out_flows), tuple(out_totals)
        return flows, totals

    carry = (zero, zero)
    for k in range(SEGMENTS):
        fetch(micro, SEGMENTS - 1 - k).wait()
        carry = lax.fori_loop(k * segment // 4, (k + 1) * segment // 4, retreat, carry)
    totals = carry[1]
    for n in range(states):
        alog_ref[pl.ds(n * chunks, chunks), :] += totals[n]

    shape = (2 * states, 2 * block)
    group = lax.broadcasted_iota(jnp.int32, shape, 1) // chunks
    gather = jnp.where(group == lax.broadcasted_iota(jnp.int32, shape, 0), 1.0, 0.0).astype(BF16)

    for which, sums_ref in ((0, sums_b_ref), (1, sums_c_ref)):
        for at in range(count // 2):
            terms = terms_ref[which, pl.ds(at * 2 * block, 2 * block), :]
            sums_ref[pl.ds(at * 2 * states, 2 * states), :] = dot(gather, terms, 1, 0)

    ranks = dt_ref.shape[0]
    drank = None
    for chunk in range(chunks):
        cols = slice(chunk * LANES, (chunk + 1) * LANES)
        place = pl.ds(chunk * count, count)
        act = act_ref[:, cols].astype(F32)
        weight = dt_ref[:, lanes(2 * chunk + half)]
        s_now = s_ref[place, :]
        dstep = d_ref[place, :] * (1.0 / LOG2E) + s_now * act
        dy = dy_ref[place, :]
        skip = skip_ref[pl.ds(2 * chunk + half, 1), :]
        sact_ref[:, cols] = s_now * step_ref[:, cols] + dy * skip
        dpre = dstep * slope_ref[:, cols].astype(F32)
        vec_ref[0:1, cols] += jnp.sum(dpre, axis=0, keepdims=True)
        vec_ref[1:2, cols] += jnp.sum(dy * act, axis=0, keepdims=True)
        low = dpre.astype(BF16)
        dpre_ref[:, cols] = low
        term = dot(low, weight, 1, 1)
        drank = term if drank is None else drank + term
    source = lax.broadcasted_iota(jnp.int32, (2 * LANES, LANES), 0)
    target = lax.broadcasted_iota(jnp.int32, (2 * LANES, LANES), 1)
    code = None
    for n in range(states):
        pair = jnp.concatenate(
            [ref[pl.ds(n, count, stride=states), :] for ref in (sums_b_ref, sums_c_ref)], axis=1
        )
        column = ranks + jnp.where(source < LANES, b_at(n, eighth), c_at(n, eighth))
        pick = jnp.where(target == column, 1.0, 0.0).astype(BF16)
        term = dot(pair.astype(BF16), pick, 1, 0)
        code = term if code is None else code + term
    drank = jnp.concatenate([drank, jnp.zeros((count, LANES - ranks), F32)], axis=1)
    code_ref[...] = (code + drank).astype(BF16)


def scan_backward(place, micros, bc, decay, dt, skip, act, sp, u, step, slope, dy, h):
    rows, own = act.shape
    count = rows // micros
    chunks = own // LANES
    states = bc.shape[1] // 2
    outs = [
        ((rows, LANES), BF16),
        ((rows, own), F32),
        ((rows, own), BF16),
        ((states * chunks, LANES), F32),
        ((2, own), F32),
    ]

    def block(*shape):
        return pl.BlockSpec(shape, lambda i, p: (i, 0))

    return pl.pallas_call(
        functools.partial(backward_kernel, count=count, states=states, chunks=chunks),
        grid_spec=pltpu.PrefetchScalarGridSpec(
            num_scalar_prefetch=1,
            grid=(micros,),
            in_specs=[
                block(count, 2 * states),
                whole(decay.shape),
                whole(dt.shape),
                whole(skip.shape),
                block(count, own),
                block(chunks * count, LANES),
                block(chunks * count, LANES),
                block(count, own),
                block(count, own),
                block(chunks * count, LANES),
                ANY,
            ],
            out_specs=[block(count, LANES), block(count, own), block(count, own)]
            + [whole(shape) for shape, _ in outs[3:]],
            scratch_shapes=[
                pltpu.VMEM((2, (count + 1) * states * chunks, LANES), F32),
                pltpu.VMEM((chunks * count, LANES), F32),
                pltpu.VMEM((chunks * count, LANES), F32),
                pltpu.VMEM((2, count * states * chunks, LANES), BF16),
                pltpu.VMEM((count * states, LANES), F32),
                pltpu.VMEM((count * states, LANES), F32),
                pltpu.VMEM((2 * states * count, LANES), F32),
                pltpu.SemaphoreType.DMA((2, SEGMENTS)),
            ],
        ),
        out_shape=[hbm(*out) for out in outs],
        compiler_params=params(52),
        cost_estimate=cost(0),
        name="scan_backward",
    )(place, *in_hbm((bc, decay, dt, skip, act, sp, u, step, slope, dy, h)))


def tail_kernel(
    place_ref,
    len_ref,
    *refs,
    micros,
    count,
    taps,
    clusters,
    ranks,
    chunks,
    states,
):
    def take(number):
        nonlocal refs
        taken, refs = refs[:number], refs[number:]
        return taken

    code_own_ref, code_other_ref = take(2)
    sact_ref, dpre_ref, alog_sum_ref, back_ref = take(4)
    dtx_ref, bc_own_ref, bc_other_ref, decay_ref = take(4)
    bend_ref, inner_ref, act_ref, high_ref, convw_ref = take(5)
    normed_ref, weight_ref, gate_part_ref, x_ref = take(4)
    keep_ref, send_ref, dnormed_ref = take(3)
    mask_ref, code_ref, wcode_ref, vec_ref, alog_ref, total_ref, win_ref, sems, low_ref = refs[:9]
    code_turned_ref, rank_turned_ref = refs[9:]

    step = pl.program_id(0)
    rows = micros * count
    eighth = states // 2
    edge = LANES // 2
    half, core, cube, face = (place_ref[k] for k in range(4))
    pair = step ^ face
    span = LANES + 32

    def fetch(k):
        source = weight_ref.at[0, pl.ds(2 * (k ^ face), 2), half]
        return (pltpu.make_async_copy(source, win_ref.at[k], sems.at[k]),)

    stream(step, win_ref.shape[0], fetch)

    def pack_row(chunk):
        relative = chunk ^ cube
        return (relative & 3) * span + LANES + (relative >> 2) * 16

    def place_pair(start, size, cols, even, odd):
        keep_ref[aligned(start, size, 16), cols] = jnp.where(core == 0, even, odd).astype(BF16)
        send_ref[aligned(start, size, 16), cols] = jnp.where(core == 0, odd, even).astype(BF16)

    @pl.when(step == 0)
    def _():
        fill_masks(len_ref, mask_ref, micros, count, taps, clusters)
        total_ref[...] = gate_part_ref[...].astype(F32)
        code_ref[...] = (
            code_own_ref[...].astype(F32) + code_other_ref[...].astype(F32)
        ).astype(BF16)
        code_turned_ref[...] = code_ref[...].T
        rank_turned_ref[...] = high_ref[...].T
        alog_ref[...] = alog_sum_ref[...] * (decay_ref[...] * (1.0 / LOG2E))

    code = code_ref[...]
    lane = lax.broadcasted_iota(jnp.int32, (1, LANES), 1)
    for part in range(2):
        source = lanes(2 * (2 * pair + part) + half)
        cols = slice(part * LANES, (part + 1) * LANES)
        wcode_ref[:ranks, cols] = dtx_ref[:, source]
        own = bc_own_ref[:, :, source].reshape(states, LANES)
        other = bc_other_ref[:, :, source].reshape(states, LANES)
        wcode_ref[ranks : ranks + states, cols] = jnp.where(half == 0, own, other)
        wcode_ref[ranks + states : ranks + 2 * states, cols] = jnp.where(half == 0, other, own)
        wcode_ref[ranks + 2 * states :, cols] = jnp.zeros(
            (LANES - ranks - 2 * states, LANES), BF16
        )
    for part in range(2):
        cols = slice(part * LANES, (part + 1) * LANES)
        chunk = 2 * pair + part
        source = 2 * chunk + half
        weights = convw_ref[:, lanes(source)]
        dact = sact_ref[:, cols] + dot(code, wcode_ref[:, cols], 1, 0)
        dconv = dact * bend_ref[:, cols].astype(F32)
        inner = inner_ref[:, cols]
        dinner = weights[taps - 1 : taps] * dconv
        sums = [None] * (taps + 1)
        sums[taps - 1] = jnp.sum(dconv * inner, axis=0, keepdims=True)
        sums[taps] = jnp.sum(dconv, axis=0, keepdims=True)
        for back in range(1, taps):
            kept = dconv * mask_ref[back]
            dinner = dinner + weights[taps - 1 - back : taps - back] * pltpu.roll(
                kept, rows - back, 0
            )
            sums[taps - 1 - back] = jnp.sum(
                kept * pltpu.roll(inner, back, 0), axis=0, keepdims=True
            )
        for k in range(taps + 1):
            vec_ref[k : k + 1, lanes(chunk)] = sums[k]
        vec_ref[taps + 1 : taps + 3, lanes(chunk)] = back_ref[:, lanes(chunk)]
        low_ref[:, cols] = dinner.astype(BF16)

        act = act_ref[:, cols]
        start = pack_row(chunk)
        code_rows = dot(code_turned_ref[...], act, 1, 0)
        rank_rows = dot(rank_turned_ref[...], dpre_ref[:, cols], 1, 0)[ranks:]
        dtx_rows = code_rows[:ranks]
        even = jnp.where(lane < edge, dtx_rows, pltpu.roll(rank_rows, edge, 1))
        odd = jnp.where(lane < edge, pltpu.roll(dtx_rows, edge, 1), rank_rows)
        for k in range(4):
            place = slice(k * 16, (k + 1) * 16)
            place_pair(
                start, 16, slice(k * LANES, (k + 1) * LANES), even[place], odd[place]
            )
        state_rows = code_rows[ranks : ranks + 2 * states]
        place_pair(
            start, 16, slice(4 * LANES, 5 * LANES), state_rows[:states], state_rows[states:]
        )

    normed = normed_ref[...]
    grad = dot(low_ref[...], normed, 0, 0).astype(BF16)
    place = aligned(step * span, LANES, 16)
    keep_ref[place, :] = jnp.where(core == 0, grad[:LANES], grad[LANES:])
    send_ref[place, :] = jnp.where(core == 0, grad[LANES:], grad[:LANES])
    width = total_ref.shape[1]
    total_ref[...] += dot(low_ref[...], win_ref[step].reshape(2 * LANES, width), 1, 0)

    @pl.when(step == pl.num_programs(0) - 1)
    def _():
        total = total_ref[...]
        dnormed_ref[...] = total.astype(BF16)
        x = x_ref[...].astype(F32)
        unit = x * lax.rsqrt(jnp.mean(x * x, axis=1, keepdims=True) + EPSILON)
        vec_ref[taps + 3 : taps + 4, :] = jnp.sum(total * unit, axis=0, keepdims=True)
        is_gain = lax.broadcasted_iota(jnp.int32, (8, LANES), 0) == taps + 3
        for chunk in range(chunks):
            start = pack_row(chunk)
            vec = vec_ref[:, chunk * LANES : (chunk + 1) * LANES]
            far, farther = (pltpu.roll(vec, LANES - k * edge // 2, 1) for k in (1, 2))
            even = jnp.where(is_gain & (lane >= edge // 2), far, vec)
            odd = jnp.where(is_gain & (lane < edge // 2), far, farther)
            alog = [
                alog_ref[pl.ds(q * eighth * chunks + chunk, eighth, stride=chunks), :]
                for q in range(2)
            ]
            place_pair(
                start,
                16,
                slice(5 * LANES, 6 * LANES),
                jnp.concatenate([alog[0], even]),
                jnp.concatenate([alog[1], odd]),
            )
            blank = jnp.zeros((16, 2 * LANES), F32)
            place_pair(start, 16, slice(6 * LANES, 8 * LANES), blank, blank)


def tail(
    place,
    lengths,
    code_own,
    code_other,
    sact,
    dpre,
    alog,
    back,
    dtx,
    bc_own,
    bc_other,
    decay,
    bend,
    inner,
    act,
    high,
    convw,
    normed,
    w4,
    gate_part,
    x,
):
    rows, own = act.shape
    chunks = own // LANES
    width = normed.shape[1]
    micros, _, clusters = lengths.shape
    count = rows // micros
    taps = convw.shape[0]
    ranks = dtx.shape[0]
    states = decay.shape[0] // chunks
    cols = 2 * LANES
    extent = 4 * (LANES + 32)

    def by_cols(height):
        return pl.BlockSpec((height, cols), lambda i, p: (0, i ^ p[FACE]))

    in_specs = (
        [pl.BlockSpec(memory_space=pltpu.SMEM)]
        + [whole((rows, LANES))] * 2
        + [by_cols(rows)] * 2
        + [whole(alog.shape), whole(back.shape)]
        + [whole(array.shape) for array in (dtx, bc_own, bc_other, decay)]
        + [by_cols(rows)] * 3
        + [whole(array.shape) for array in (high, convw, normed)]
        + [
            ANY,
            whole((rows, width)),
            whole((rows, width)),
        ]
    )
    return pl.pallas_call(
        functools.partial(
            tail_kernel,
            micros=micros,
            count=count,
            taps=taps,
            clusters=clusters,
            ranks=ranks,
            chunks=chunks,
            states=states,
        ),
        grid_spec=pltpu.PrefetchScalarGridSpec(
            num_scalar_prefetch=1,
            grid=(chunks // 2,),
            in_specs=in_specs,
            out_specs=[whole((extent, width)), whole((extent, width)), whole((rows, width))],
            scratch_shapes=[
                pltpu.VMEM((taps, rows, LANES), F32),
                pltpu.VMEM((rows, LANES), BF16),
                pltpu.VMEM((LANES, cols), BF16),
                pltpu.VMEM((8, own), F32),
                pltpu.VMEM((states * chunks, LANES), F32),
                pltpu.VMEM((rows, width), F32),
                pltpu.VMEM((chunks // 2, 2, LANES, width), BF16),
                pltpu.SemaphoreType.DMA((chunks // 2,)),
                pltpu.VMEM((rows, cols), BF16),
                pltpu.VMEM((LANES, rows), BF16),
                pltpu.VMEM((2 * ranks, rows), BF16),
            ],
        ),
        out_shape=[
            hbm((extent, width), BF16),
            hbm((extent, width), BF16),
            hbm((rows, width), BF16),
        ],
        compiler_params=params(34),
        cost_estimate=cost(7),
        name="tail",
    )(
        place,
        lengths,
        *in_hbm([code_own]),
        code_other,
        *in_hbm(
            (
                sact,
                dpre,
                alog,
                back,
                dtx,
                bc_own,
                bc_other,
                decay,
                bend,
                inner,
                act,
                high,
                convw,
                normed,
                w4,
                gate_part,
                x,
            )
        ),
    )


def fetch_halves(source, which, half, target_ref, sems):
    copies = []
    for k in range(target_ref.shape[0]):
        pair = pl.ds(2 * k, 2)
        block = source.at[pair, half] if which is None else source.at[which, pair, half]
        copies.append(pltpu.make_async_copy(block, target_ref.at[k], sems.at[k]))
    for copy in copies:
        copy.start()
    return copies


def products_kernel(
    place_ref,
    gated_ref,
    dgate_ref,
    out_ref,
    weight_ref,
    mixed_ref,
    dnormed_ref,
    wout_ref,
    wgate_ref,
    out_sems,
    gate_sems,
):
    half = place_ref[HALF]
    width = mixed_ref.shape[1]
    jobs = (
        (fetch_halves(out_ref, None, half, wout_ref, out_sems), gated_ref, wout_ref, mixed_ref),
        (fetch_halves(weight_ref, 1, half, wgate_ref, gate_sems), dgate_ref, wgate_ref, dnormed_ref),
    )
    for copies, left_ref, right_ref, result_ref in jobs:
        total = None
        for k, copy in enumerate(copies):
            copy.wait()
            left = left_ref[:, 2 * k * LANES : 2 * (k + 1) * LANES]
            term = dot(left, right_ref[k].reshape(-1, width), 1, 0)
            total = term if total is None else total + term
        result_ref[...] = total.astype(BF16)


def products(place, gated, dgate, wout3, w4):
    rows, own = gated.shape
    width = w4.shape[-1]
    pairs = own // (2 * LANES)
    return pl.pallas_call(
        products_kernel,
        grid_spec=pltpu.PrefetchScalarGridSpec(
            num_scalar_prefetch=1,
            grid=(1,),
            in_specs=[whole((rows, own)), whole((rows, own)), ANY, ANY],
            out_specs=[whole((rows, width))] * 2,
            scratch_shapes=[
                pltpu.VMEM((pairs, 2, LANES, width), BF16),
                pltpu.VMEM((pairs, 2, LANES, width), BF16),
                pltpu.SemaphoreType.DMA((pairs,)),
                pltpu.SemaphoreType.DMA((pairs,)),
            ],
        ),
        out_shape=[hbm((rows, width), BF16)] * 2,
        compiler_params=params(20),
        cost_estimate=cost(4),
        name="products",
    )(place, *in_hbm((gated, dgate, wout3, w4)))


def finish_kernel(x_ref, mine_ref, theirs_ref, cotan_ref, gain_ref, grad_ref):
    x = x_ref[...].astype(F32)
    scale = lax.rsqrt(jnp.mean(x * x, axis=1, keepdims=True) + EPSILON)
    unit = x * scale
    dhat = (mine_ref[...].astype(F32) + theirs_ref[...].astype(F32)) * gain_ref[...]
    grad_ref[...] = cotan_ref[...].astype(F32) + scale * (
        dhat - unit * jnp.mean(dhat * unit, axis=1, keepdims=True)
    )


def finish(x, mine, theirs, cotan, gain):
    rows, width = x.shape
    by_rows = pl.BlockSpec((rows // 4, width), lambda i: (i, 0))
    return pl.pallas_call(
        finish_kernel,
        grid=(4,),
        in_specs=[by_rows] * 4 + [whole(gain.shape)],
        out_specs=by_rows,
        out_shape=jax.ShapeDtypeStruct((rows, width), F32),
        compiler_params=params(16),
        cost_estimate=cost(0),
        name="finish",
    )(*in_hbm((x, mine)), theirs, *in_hbm((cotan, gain)))


def unpack_kernel(
    near_ref,
    far_ref,
    out_ref,
    dtx_ref,
    dt_ref,
    bc_ref,
    alog_ref,
    convw_ref,
    convb_ref,
    bias_ref,
    skip_ref,
    out_grad_ref,
    *,
    eighth,
    taps,
    edge,
):
    pack = near_ref[...].astype(F32) + far_ref[...].astype(F32)
    turned = jnp.concatenate([pack[:, k * LANES : (k + 1) * LANES] for k in range(4)]).T
    dtx_ref[...] = turned[:edge]
    dt_ref[...] = turned[edge:]
    rows = pack[:, 4 * LANES : 5 * LANES]
    bc_ref[0] = rows[:eighth]
    bc_ref[1] = rows[eighth:]
    rows = pack[:, 5 * LANES : 6 * LANES]
    alog_ref[...] = rows[:eighth]
    vec = rows[eighth:, :edge]
    convw_ref[...] = vec[:taps]
    convb_ref[...] = vec[taps : taps + 1]
    bias_ref[...] = vec[taps + 1 : taps + 2]
    skip_ref[...] = vec[taps + 2 : taps + 3]
    out_grad_ref[...] = out_ref[...].astype(F32)


def unpack(near, far, out, eighth, taps, ranks):
    edge = LANES // 2
    shapes = [
        (edge, ranks),
        (edge, ranks),
        (2, eighth, LANES),
        (eighth, LANES),
        (taps, edge),
        (1, edge),
        (1, edge),
        (1, edge),
        out.shape,
    ]
    return pl.pallas_call(
        functools.partial(unpack_kernel, eighth=eighth, taps=taps, edge=edge),
        grid=(1,),
        in_specs=[whole(array.shape) for array in (near, far, out)],
        out_specs=[whole(shape) for shape in shapes],
        out_shape=[jax.ShapeDtypeStruct(shape, F32) for shape in shapes],
        cost_estimate=cost(0),
        name="unpack",
    )(near, far, out)


def swap_pair(array):
    count = lax.axis_size("state")
    return lax.ppermute(array, "state", [(pos, pos ^ 1) for pos in range(count)])


def swap_bit(array, bits):
    return lax.ppermute(array, "dp", [(pos, pos ^ bits) for pos in range(lax.axis_size("dp"))])


def swap_both(array, bits=0):
    states = lax.axis_size("state")
    pairs = []
    for d in range(lax.axis_size("dp")):
        for s in range(states):
            pairs.append((d * states + s, (((d & ~1) | s) ^ bits) * states + (d & 1)))
    return lax.ppermute(array, ("dp", "state"), pairs)


def add_mixed(x, mine, theirs):
    return (x.astype(F32) + (mine.astype(F32) + theirs.astype(F32))).astype(BF16)


def add_quarters(kept, got):
    extent = kept.shape[0] // 4
    return [kept[k * extent :][:extent] + got[k * extent :][:extent] for k in range(1, 4)]


def trade_quarters(quarters):
    return [swap_bit(quarters[k - 1], k * X_BIT) for k in range(1, 4)]


def sum_quarters(kept, got, quarters):
    extent = kept.shape[0] // 4
    own = kept[:extent].astype(F32) + got[:extent].astype(F32)
    first, second, third = (quarter.astype(F32) for quarter in quarters)
    return ((own + first) + (second + third)).astype(BF16)


CORE_BIT, X_BIT, ZH_BIT = 1, 2, 8


def shards(
    tokens,
    cluster_len,
    norm_gain,
    in_weight,
    conv_weight,
    conv_bias,
    dtx_weight,
    dt_weight,
    dt_bias,
    bc_weight,
    a_log,
    skip_gain,
    out_weight,
    cotangent,
):
    micros, count, width = tokens.shape
    inner = out_weight.shape[0]
    taps = conv_weight.shape[0]
    ranks = dtx_weight.shape[1]
    chunks = inner // (2 * LANES)
    own = chunks * LANES
    rows = micros * count
    edge = LANES // 2
    span = LANES + 32
    dp_parts = lax.axis_size("dp")
    state_count = lax.axis_size("state")
    dp_pos = lax.axis_index("dp")
    state_pos = lax.axis_index("state")
    half = state_pos & 1
    fast = state_count == 2 and dp_parts == 2 * chunks == 16
    if fast:
        place = jnp.stack([half, dp_pos & 1, dp_pos >> 1, (dp_pos >> 1) & 3])
        bc_own, alog_own = bc_weight, a_log
        bc_other, alog_other = swap_pair(bc_weight), swap_pair(a_log)
    else:
        place = jnp.stack([half, 0, 0, 0])
        bc_all = lax.all_gather(bc_weight, "state", axis=1, tiled=True)
        alog_all = lax.all_gather(a_log, "state", axis=0, tiled=True)
        eighth = alog_all.shape[0] // 2
        bc_own, bc_other = (
            lax.dynamic_slice_in_dim(bc_all, which * eighth, eighth, 1)
            for which in (half, 1 - half)
        )
        alog_own, alog_other = (
            lax.dynamic_slice_in_dim(alog_all, which * eighth, eighth, 0)
            for which in (half, 1 - half)
        )
    place = place.astype(jnp.int32)
    eighth = alog_own.shape[0]
    states = 2 * eighth

    x = tokens.reshape(rows, width)
    cotan = cotangent.reshape(rows, width)
    w4 = in_weight.reshape(2, chunks, 2, LANES, width)
    wout3 = out_weight.reshape(chunks, 2, LANES, width)
    dtx, dt = dtx_weight.T, dt_weight.T
    bias = dt_bias.reshape(-1, LANES)
    skip = skip_gain.reshape(-1, LANES)

    normed, act_all, act, inner_own, bend, gate = project(
        place, cluster_len, x, norm_gain[None], w4, conv_weight, conv_bias.reshape(-1, LANES)
    )
    bc, rank, high, decay, sp, u, step, slope, h, dy, gated, dgate, keep, send = scan_forward(
        place,
        cluster_len,
        act_all,
        bc_own,
        bc_other,
        alog_own,
        alog_other,
        dtx,
        dt,
        bias,
        skip,
        act,
        gate,
        wout3,
        cotan,
        normed,
    )
    if fast:
        early = swap_bit(send, CORE_BIT)
    mixed_part, dn_gate = products(place, gated, dgate, wout3, w4)
    if fast:
        *quarters, mixed_part, dn_gate, sp = lax.optimization_barrier(
            (*add_quarters(keep, early), mixed_part, dn_gate, sp)
        )
        early_got = trade_quarters(quarters)
    code_own, sact, dpre, alog, back = scan_backward(
        place, micros, bc, decay, dt, skip, act, sp, u, step, slope, dy, h
    )
    if fast:
        *early_got, code_own, mixed_part = lax.optimization_barrier(
            (*early_got, code_own, mixed_part)
        )
    code_other = swap_pair(code_own)
    mixed_other = swap_pair(mixed_part)
    if fast:
        block = sum_quarters(keep, early, early_got)
        out_keep, out_send, gate_sum = block[:edge], block[edge:LANES], block[LANES:]
        out_send, gate_sum, bend = lax.optimization_barrier((out_send, gate_sum, bend))
    late_keep, late_send, dnormed_part = tail(
        place,
        cluster_len,
        code_own,
        code_other,
        sact,
        dpre,
        alog,
        back,
        dtx,
        bc_own,
        bc_other,
        decay,
        bend,
        inner_own,
        act,
        high,
        conv_weight,
        normed,
        w4,
        dn_gate,
        x,
    )
    mixed = add_mixed(x, mixed_part, mixed_other)
    if fast:
        late_send, mixed_other = lax.optimization_barrier((late_send, mixed_other))
        mixed = add_mixed(x, mixed_part, mixed_other)
        late = swap_bit(late_send, CORE_BIT)
        late_got = trade_quarters(add_quarters(late_keep, late))
        out_got = swap_bit(out_send, ZH_BIT)
    dnormed_other = swap_pair(dnormed_part)
    tokens_grad = finish(x, dnormed_part, dnormed_other, cotan, norm_gain[None])
    if fast:
        *late_got, out_got, tokens_grad, mixed = lax.optimization_barrier(
            (*late_got, out_got, tokens_grad, mixed)
        )
        out_own = swap_both(out_keep + out_got)
        block = sum_quarters(late_keep, late, late_got)
        inner_sum = block[:LANES]
        upper = dp_pos >= dp_parts // 2
        crossing = jnp.where(upper, inner_sum, gate_sum)
        first, second = crossing[:edge], crossing[edge:]
        first, pack_far, pack_near = lax.optimization_barrier(
            (first, block[-16:], block[LANES:-16])
        )
        pack_far = swap_both(pack_far, ZH_BIT)
        first_got = swap_bit(first, ZH_BIT)
        pack_near = swap_both(pack_near)
        first_got, pack_far, pack_near = lax.optimization_barrier((first_got, pack_far, pack_near))
        second_got = swap_bit(second, ZH_BIT)
        gain_mine = (
            pack_near[:, 5 * LANES : 6 * LANES].astype(F32)
            + pack_far[:, 5 * LANES : 6 * LANES].astype(F32)
        ).astype(BF16)
        gain_both = gain_mine[-1].astype(F32) + swap_bit(gain_mine, CORE_BIT)[-1].astype(F32)
        extent = width // (dp_parts * state_count)
        gain_grad = lax.dynamic_slice_in_dim(gain_both, (dp_pos & 1) * extent, extent, 0)
        (
            dtx_grad,
            dt_grad,
            bc_grad,
            alog_grad,
            convw_grad,
            convb_grad,
            bias_grad,
            skip_grad,
            out_own,
        ) = unpack(pack_near, pack_far, out_own, eighth, taps, ranks)
        convb_grad, bias_grad, skip_grad = (
            array[0] for array in (convb_grad, bias_grad, skip_grad)
        )
        second_got, dtx_grad, dt_grad, out_own = lax.optimization_barrier(
            (second_got, dtx_grad, dt_grad, out_own)
        )
        in_grad = jnp.where(upper, gate_sum, inner_sum).astype(F32) + jnp.concatenate(
            [first_got, second_got]
        ).astype(F32)
    mixed = mixed.reshape(micros, count, width)
    tokens_grad = tokens_grad.reshape(micros, count, width)

    if not fast:
        def total(array):
            return lax.psum(array.astype(F32), "dp")

        def both_rows(array):
            mine = array.reshape(chunks, 1, LANES, -1)
            other = swap_pair(mine)
            low = jnp.where(half == 0, mine, other)
            high = jnp.where(half == 0, other, mine)
            return jnp.concatenate([low, high], axis=1).reshape(2 * own, -1)

        every = dp_parts * state_count
        at = dp_pos * state_count + state_pos

        def cut_own(array):
            extent = array.shape[0] // every
            return lax.dynamic_slice_in_dim(array, at * extent, extent, 0)

        pair = total(jnp.stack([keep, send])).reshape(2, 2, 2, 2 * LANES, width)
        outs = pair[:, :, :, :LANES].reshape(2, 2, 2, 2, edge, width)
        outs = jnp.transpose(outs, (3, 1, 2, 0, 4, 5)).reshape(own, width)
        gates = jnp.moveaxis(pair[:, :, :, LANES:], 0, 2).reshape(own, width)
        pair = total(jnp.stack([late_keep, late_send])).reshape(2, 2, 2, span, width)
        inners = jnp.moveaxis(pair[:, :, :, :LANES], 0, 2).reshape(own, width)
        packs = pair[:, :, :, LANES:].reshape(2, 2, 2, 2, 16, width // LANES, LANES)
        packs = jnp.transpose(packs, (3, 1, 2, 0, 5, 4, 6)).reshape(chunks, 2, -1, 16, LANES)
        small = packs[:, :, :4].reshape(chunks, 2, ranks, 2, edge)
        small = both_rows(jnp.transpose(small, (0, 1, 4, 3, 2)).reshape(own, 2 * ranks))
        in_grad = cut_own(jnp.concatenate([both_rows(inners), both_rows(gates)]))
        out_own = cut_own(both_rows(outs))
        mine = cut_own(small)
        dtx_grad, dt_grad = mine[:, :ranks], mine[:, ranks:]
        vec_rows = jnp.swapaxes(packs[:, :, 5, eighth:, :edge], 2, 3).reshape(own, -1)
        gain_sum = vec_rows[:, -1].reshape(chunks, 2, 2, -1).swapaxes(1, 2).reshape(-1)
        gain_grad = cut_own(gain_sum + swap_pair(gain_sum))
        vec = cut_own(both_rows(vec_rows)).T
        state_rows = jnp.concatenate([packs[:, :, 4], packs[:, :, 5, :eighth]], axis=2)
        state_rows = state_rows.reshape(chunks, 2, 3, eighth, LANES)
        state_rows = jnp.transpose(state_rows, (0, 4, 2, 1, 3)).reshape(own, -1)
        extent = inner // dp_parts
        state_part = lax.dynamic_slice_in_dim(both_rows(state_rows), dp_pos * extent, extent, 0)
        state_part = state_part.T.reshape(3, state_count, -1, extent)
        state_part = lax.dynamic_index_in_dim(state_part, state_pos, 1, keepdims=False)
        bc_grad, alog_grad = state_part[:2], state_part[2]
        convw_grad, convb_grad, bias_grad, skip_grad = (
            vec[:taps], vec[taps], vec[taps + 1], vec[taps + 2]
        )

    return (
        mixed,
        tokens_grad,
        gain_grad,
        in_grad,
        convw_grad,
        convb_grad,
        dtx_grad,
        dt_grad,
        bias_grad,
        bc_grad,
        alog_grad,
        skip_grad,
        out_own,
    )


def solution(mesh):
    return jax.shard_map(
        shards,
        mesh=mesh,
        in_specs=(
            P(None, "dp", None),
            P(None, "dp", None),
            P(),
            P(),
            P(),
            P(),
            P(),
            P(),
            P(),
            P(None, "state", None),
            P("state", None),
            P(),
            P(),
            P(None, "dp", None),
        ),
        out_specs=(
            P(None, "dp", None),
            P(None, "dp", None),
            P(("dp", "state")),
            P(("dp", "state"), None),
            P(None, ("dp", "state")),
            P(("dp", "state")),
            P(("dp", "state"), None),
            P(("dp", "state"), None),
            P(("dp", "state")),
            P(None, "state", "dp"),
            P("state", "dp"),
            P(("dp", "state")),
            P(("dp", "state"), None),
        ),
        check_vma=False,
    )
```

```python
import functools
import math

import jax
import jax.numpy as jnp
from jax import lax
from jax.experimental import pallas as pl
from jax.experimental.pallas import tpu as pltpu
from jax.sharding import PartitionSpec as P

EPSILON = 1e-05
LANES = 128
RESET = 1e4
LOG2E = math.log2(math.e)
F32 = jnp.float32
BF16 = jnp.bfloat16
MIB = 1024 * 1024


def dot(left, right, left_dim, right_dim):
    return lax.dot_general(
        left, right, (((left_dim,), (right_dim,)), ((), ())), preferred_element_type=F32
    )


def params(mib):
    return pltpu.CompilerParams(
        vmem_limit_bytes=mib * MIB, dimension_semantics=("arbitrary",)
    )


ANY = pl.BlockSpec(memory_space=pl.ANY)


def stream(step, steps, fetch):
    @pl.when(step == 0)
    def _():
        for k in range(steps):
            for copy in fetch(k):
                copy.start()

    for copy in fetch(step):
        copy.wait()


def whole(shape):
    return pl.BlockSpec(shape, lambda *_: (0,) * len(shape))


sigmoid = jax.nn.sigmoid


def log_one_plus(value):
    series = value * (1.0 - value * (0.5 - value * (1.0 / 3.0)))
    return jnp.where(value < 1e-3, series, jnp.log(1.0 + value))


def lanes(index):
    return pl.ds(pl.multiple_of(index * LANES, LANES), LANES)


def cost(micros):
    return pl.CostEstimate(
        flops=int(micros * 1e9), bytes_accessed=int(micros * 1e6), transcendentals=0
    )


def hbm(shape, dtype):
    return pltpu.HBM(shape, dtype)


def in_hbm(arrays):
    return [pltpu.with_memory_space_constraint(array, pltpu.HBM) for array in arrays]


def aligned(start, size, to=8):
    return pl.ds(pl.multiple_of(start, to), size)


SEGMENTS = 4

HALF, CORE, CUBE, FACE = range(4)


def fill_masks(len_ref, mask_ref, micros, count, taps, clusters):
    place = lax.broadcasted_iota(jnp.int32, (count, LANES), 0)
    for micro in range(micros):
        rows = pl.ds(micro * count, count)
        for back in range(1, taps):
            apart = place < back
            start = 0
            for cluster in range(clusters - 1):
                start = start + len_ref[micro, 0, cluster]
                apart = apart | ((place >= start) & (place < start + back))
            mask_ref[back, rows, :] = jnp.where(apart, 0.0, 1.0)
            if back == 1:
                mask_ref[0, rows, :] = jnp.where(apart, 1.0, 0.0)


def project_kernel(
    place_ref,
    len_ref,
    gain_ref,
    convw_ref,
    convb_ref,
    x_far,
    weight_far,
    normed_far,
    act_far,
    own_act_far,
    inner_far,
    bend_far,
    gate_far,
    mask_ref,
    x_ref,
    win_ref,
    wgate_ref,
    normed_ref,
    act_ref,
    own_act_ref,
    inner_ref,
    bend_ref,
    gate_ref,
    in_sems,
    out_sems,
    *,
    micros,
    count,
    taps,
    clusters,
):
    half = place_ref[HALF]
    chunks = win_ref.shape[0]
    inward = [pltpu.make_async_copy(x_far, x_ref, in_sems.at[2 * chunks])]
    for k in range(chunks):
        inward.append(pltpu.make_async_copy(weight_far.at[0, k], win_ref.at[k], in_sems.at[2 * k]))
        inward.append(
            pltpu.make_async_copy(
                weight_far.at[1, k, half], wgate_ref.at[k], in_sems.at[2 * k + 1]
            )
        )
    for copy in inward:
        copy.start()
    outward = []

    def put(source, target):
        outward.append(pltpu.make_async_copy(source, target, out_sems.at[len(outward)]))
        outward[-1].start()

    fill_masks(len_ref, mask_ref, micros, count, taps, clusters)
    inward[0].wait()
    rows = x_ref[...].astype(F32)
    scale = lax.rsqrt(jnp.mean(rows * rows, axis=1, keepdims=True) + EPSILON)
    normed = (rows * scale * gain_ref[...]).astype(BF16)
    normed_ref[...] = normed
    put(normed_ref, normed_far)
    for k in range(chunks):
        inward[2 * k + 1].wait()
        inward[2 * k + 2].wait()
        proj = dot(normed, win_ref[k].reshape(2 * LANES, -1), 1, 1)
        own = slice(k * LANES, (k + 1) * LANES)
        gate_ref[:, own] = dot(normed, wgate_ref[k], 1, 1)
        inners, sigs, acts = [], [], []
        for part in range(2):
            cols = slice((2 * k + part) * LANES, (2 * k + part + 1) * LANES)
            inner = proj[:, part * LANES : (part + 1) * LANES]
            conved = convb_ref[2 * k + part : 2 * k + part + 1, :]
            conved = conved + convw_ref[taps - 1 : taps, cols] * inner
            for back in range(1, taps):
                shifted = pltpu.roll(inner, back, 0) * mask_ref[back]
                conved = conved + convw_ref[taps - 1 - back : taps - back, cols] * shifted
            sig = sigmoid(conved)
            act = conved * sig
            act_ref[:, cols] = act.astype(BF16)
            inners.append(inner)
            sigs.append(sig)
            acts.append(act)
        inner_ref[:, own] = jnp.where(half == 0, *inners)
        act, sig = jnp.where(half == 0, *acts), jnp.where(half == 0, *sigs)
        bend_ref[:, own] = (sig + act * (1.0 - sig)).astype(BF16)
        own_act_ref[:, own] = act.astype(BF16)
        if k % 2:
            group = pl.ds((k - 1) * LANES, 2 * LANES)
            wide = pl.ds(2 * (k - 1) * LANES, 4 * LANES)
            put(act_ref.at[:, wide], act_far.at[:, wide])
            for near, far in (
                (gate_ref, gate_far),
                (inner_ref, inner_far),
                (bend_ref, bend_far),
                (own_act_ref, own_act_far),
            ):
                put(near.at[:, group], far.at[:, group])
    for copy in outward:
        copy.wait()


def project(place, lengths, x, gain, w4, conv_weight, conv_bias):
    rows, width = x.shape
    chunks = w4.shape[1]
    micros, _, clusters = lengths.shape
    taps = conv_weight.shape[0]
    own = chunks * LANES
    outs = [
        ((rows, width), BF16),
        ((rows, 2 * own), BF16),
        ((rows, own), BF16),
        ((rows, own), F32),
        ((rows, own), BF16),
        ((rows, own), F32),
    ]
    return pl.pallas_call(
        functools.partial(
            project_kernel, micros=micros, count=rows // micros, taps=taps, clusters=clusters
        ),
        grid_spec=pltpu.PrefetchScalarGridSpec(
            num_scalar_prefetch=1,
            grid=(1,),
            in_specs=[
                pl.BlockSpec(memory_space=pltpu.SMEM),
                whole(gain.shape),
                whole(conv_weight.shape),
                whole(conv_bias.shape),
                ANY,
                ANY,
            ],
            out_specs=[ANY] * len(outs),
            scratch_shapes=[
                pltpu.VMEM((taps, rows, LANES), F32),
                pltpu.VMEM((rows, width), BF16),
                pltpu.VMEM((chunks, 2, LANES, width), BF16),
                pltpu.VMEM((chunks, LANES, width), BF16),
            ]
            + [pltpu.VMEM(*out) for out in outs]
            + [
                pltpu.SemaphoreType.DMA((2 * chunks + 1,)),
                pltpu.SemaphoreType.DMA((1 + 5 * chunks // 2,)),
            ],
        ),
        out_shape=[hbm(*out) for out in outs],
        compiler_params=params(30),
        cost_estimate=cost(6),
        name="project",
    )(place, *in_hbm((lengths, gain, conv_weight, conv_bias, x, w4)))


def every_row(ref, row, height):
    return ref[pl.ds(row, height, stride=0), :]


def b_at(n, eighth):
    return (n // eighth) * 2 * eighth + n % eighth


def c_at(n, eighth):
    return b_at(n, eighth) + eighth


def forward_kernel(
    place_ref,
    len_ref,
    act_all_ref,
    bc_own_ref,
    bc_other_ref,
    alog_own_ref,
    alog_other_ref,
    dtx_ref,
    dt_ref,
    bias_ref,
    skip_ref,
    act_ref,
    *refs,
    micros,
    count,
    states,
    chunks,
    clusters,
):
    gate_far, wout_far, cotan_far, normed_far = refs[:4]
    bc_ref, rank_ref, rank_high_ref, decay_ref = refs[4:8]
    sp_far, u_far, step_far, slope_far, h_far, dy_far = refs[8:14]
    gated_far, dgate_far, keep_far, send_far = refs[14:18]
    mask_ref, y_ref, tmp_ref, wide_ref = refs[18:22]
    gate_ref, wout_ref, cotan_ref, normed_ref = refs[22:26]
    sp_ref, u_ref, step_ref, slope_ref, h_ref, dy_ref = refs[26:32]
    gated_ref, dgate_ref, keep_ref, send_ref = refs[32:36]
    in_sems, out_sems = refs[36:]
    rows = micros * count
    eighth = states // 2
    half, core, cube, face = (place_ref[k] for k in range(4))
    first = half == 0
    inward = [
        pltpu.make_async_copy(source, target, in_sems.at[k])
        for k, (source, target) in enumerate(
            (
                (gate_far, gate_ref),
                (wout_far.at[:, half], wout_ref),
                (cotan_far, cotan_ref),
                (normed_far, normed_ref),
            )
        )
    ]
    for copy in inward:
        copy.start()
    outward = []

    def put(source, target):
        outward.append(pltpu.make_async_copy(source, target, out_sems.at[len(outward)]))
        outward[-1].start()

    ranks = dtx_ref.shape[0]
    weights = jnp.concatenate(
        [dtx_ref[...]] + [ref[...].reshape(states, -1) for ref in (bc_own_ref, bc_other_ref)]
    )
    product = dot(act_all_ref[...], weights, 1, 1)
    own, other = product[:, ranks : ranks + states], product[:, ranks + states :]
    bc_ref[:, :states] = jnp.where(first, own, other)
    bc_ref[:, states:] = jnp.where(first, other, own)
    spread_lanes(bc_ref, wide_ref)

    fill_masks(len_ref, mask_ref, micros, count, 2, clusters)
    for chunk in range(chunks):
        cols = lanes(2 * chunk + half)
        own, other = alog_own_ref[:, cols], alog_other_ref[:, cols]
        tmp_ref[pl.ds(chunk * states, eighth), :] = jnp.where(first, own, other)
        tmp_ref[pl.ds(chunk * states + eighth, eighth), :] = jnp.where(first, other, own)
    for n in range(states):
        decay_ref[pl.ds(n * chunks, chunks), :] = -LOG2E * jnp.exp(
            tmp_ref[pl.ds(n, chunks, stride=states), :]
        )

    rank = product[:, :ranks].astype(BF16)
    rank_ref[...] = rank
    rank_high_ref[...] = jnp.concatenate([jnp.zeros_like(rank), rank], axis=1)
    for chunk in range(chunks):
        cols = slice(chunk * LANES, (chunk + 1) * LANES)
        bias = bias_ref[pl.ds(2 * chunk + half, 1), :]
        pre = dot(rank, dt_ref[:, lanes(2 * chunk + half)], 1, 0) + bias
        tail_part = jnp.exp(-jnp.abs(pre))
        step = jnp.maximum(pre, 0.0) + log_one_plus(tail_part)
        slope = jnp.where(pre >= 0.0, 1.0, tail_part) / (1.0 + tail_part)
        step_ref[:, cols] = step
        slope_ref[:, cols] = slope.astype(BF16)
        held = step + RESET * mask_ref[0]
        source = step * act_ref[:, cols].astype(F32)
        for micro in range(micros):
            span = slice(micro * count, (micro + 1) * count)
            place = pl.ds((micro * chunks + chunk) * count, count)
            sp_ref[place, :] = held[span]
            u_ref[place, :] = source[span]
    put(sp_ref, sp_far)
    put(u_ref, u_far)
    put(step_ref, step_far)
    put(slope_ref, slope_far)

    for micro in range(micros):

        def advance(t, h, micro=micro):
            row = micro * count + t
            span = pl.ds(micro * chunks * count + t, chunks, stride=count)
            sp = sp_ref[span, :]
            u = u_ref[span, :]
            out = []
            y = None
            for n in range(states):
                decay = jnp.exp2(sp * decay_ref[pl.ds(n * chunks, chunks), :])
                now = decay * h[n] + u * every_row(wide_ref, b_at(n, eighth) * rows + row, chunks)
                h_ref[aligned((row * states + n) * chunks, chunks), :] = now
                out.append(now)
                term = now * every_row(wide_ref, c_at(n, eighth) * rows + row, chunks)
                y = term if y is None else y + term
            y_ref[span, :] = y
            return tuple(out)

        h = (jnp.zeros((chunks, LANES), F32),) * states
        segment = count // SEGMENTS
        for k in range(SEGMENTS):
            h = lax.fori_loop(k * segment, (k + 1) * segment, advance, h, unroll=8)
            extent = segment * states * chunks
            place = pl.ds((micro * SEGMENTS + k) * extent, extent)
            put(h_ref.at[place], h_far.at[place])

    for copy in inward:
        copy.wait()
    cotan = cotan_ref[...]
    for chunk in range(chunks):
        cols = slice(chunk * LANES, (chunk + 1) * LANES)
        places = [pl.ds((micro * chunks + chunk) * count, count) for micro in range(micros)]
        y = jnp.concatenate([y_ref[place, :] for place in places])
        y = y + skip_ref[pl.ds(2 * chunk + half, 1), :] * act_ref[:, cols].astype(F32)
        gate = gate_ref[:, cols]
        sig = sigmoid(gate)
        gated_ref[:, cols] = (y * (gate * sig)).astype(BF16)
        dgated = dot(cotan, wout_ref[chunk], 1, 1)
        dy = dgated * (gate * sig)
        for micro in range(micros):
            dy_ref[places[micro], :] = dy[micro * count : (micro + 1) * count]
        dgate_ref[:, cols] = (dgated * y * (sig * (1.0 + gate * (1.0 - sig)))).astype(BF16)
    put(dy_ref, dy_far)
    put(gated_ref, gated_far)
    put(dgate_ref, dgate_far)
    normed = normed_ref[...]
    edge = LANES // 2
    for r in range(chunks // 2):
        for zh in range(2):
            grad = dot(gated_ref[:, lanes((r + 4 * zh) ^ cube)], cotan, 0, 0).astype(BF16)
            top, bottom = grad[:edge], grad[edge:]
            place = pl.ds(r * 2 * LANES + zh * edge, edge)
            keep_ref[place, :] = jnp.where(core == 0, top, bottom)
            send_ref[place, :] = jnp.where(core == 0, bottom, top)
        place = pl.ds((2 * r + 1) * LANES, LANES)
        pair = 2 * (r ^ face)
        for chunk, out_ref in ((pair + core, keep_ref), (pair + 1 - core, send_ref)):
            out_ref[place, :] = dot(dgate_ref[:, lanes(chunk)], normed, 0, 0).astype(BF16)
        place = pl.ds(r * 2 * LANES, 2 * LANES)
        put(send_ref.at[place], send_far.at[place])
        put(keep_ref.at[place], keep_far.at[place])
    for copy in outward:
        copy.wait()


def scan_forward(
    place,
    lengths,
    act_all,
    bc_own,
    bc_other,
    alog_own,
    alog_other,
    dtx,
    dt,
    bias,
    skip,
    act,
    gate,
    wout3,
    cotan,
    normed,
):
    rows, own = act.shape
    chunks = own // LANES
    states = 2 * alog_own.shape[0]
    width = cotan.shape[1]
    micros, _, clusters = lengths.shape
    ranks = dtx.shape[0]
    small = [
        ((rows, 2 * states), F32),
        ((rows, ranks), BF16),
        ((rows, 2 * ranks), BF16),
        ((states * chunks, LANES), F32),
    ]
    large = [
        ((chunks * rows, LANES), F32),
        ((chunks * rows, LANES), F32),
        ((rows, own), F32),
        ((rows, own), BF16),
        ((rows * states * chunks, LANES), F32),
        ((chunks * rows, LANES), F32),
        ((rows, own), BF16),
        ((rows, own), BF16),
        ((own, width), BF16),
        ((own, width), BF16),
    ]
    operands = (act_all, bc_own, bc_other, alog_own, alog_other, dtx, dt, bias, skip, act)
    streamed = (gate, wout3, cotan, normed)
    return pl.pallas_call(
        functools.partial(
            forward_kernel,
            micros=micros,
            count=rows // micros,
            states=states,
            chunks=chunks,
            clusters=clusters,
        ),
        grid_spec=pltpu.PrefetchScalarGridSpec(
            num_scalar_prefetch=1,
            grid=(1,),
            in_specs=[pl.BlockSpec(memory_space=pltpu.SMEM)]
            + [whole(operand.shape) for operand in operands]
            + [ANY] * len(streamed),
            out_specs=[whole(shape) for shape, _ in small] + [ANY] * len(large),
            scratch_shapes=[
                pltpu.VMEM((2, rows, LANES), F32),
                pltpu.VMEM((chunks * rows, LANES), F32),
                pltpu.VMEM((states * chunks, LANES), F32),
                pltpu.VMEM((2 * states * rows + 8, LANES), F32),
                pltpu.VMEM((rows, own), F32),
                pltpu.VMEM((chunks, LANES, width), BF16),
                pltpu.VMEM((rows, width), BF16),
                pltpu.VMEM((rows, width), BF16),
            ]
            + [pltpu.VMEM(*out) for out in large]
            + [pltpu.SemaphoreType.DMA((4,)), pltpu.SemaphoreType.DMA((7 + chunks + micros * SEGMENTS,))],
        ),
        out_shape=[hbm(*out) for out in small + large],
        compiler_params=params(52),
        cost_estimate=cost(19),
        name="scan_forward",
    )(
        place,
        lengths,
        *in_hbm(operands[:1]),
        *operands[1:5],
        *in_hbm((*operands[5:], *streamed)),
    )


def spread_lanes(values_ref, wide_ref):
    rows, count = values_ref.shape
    for k in range(count):
        wide_ref[pl.ds(k * rows, rows), :] = jnp.broadcast_to(
            values_ref[:, k : k + 1], (rows, LANES)
        )


def backward_kernel(
    place_ref,
    bc_ref,
    decay_ref,
    dt_ref,
    skip_ref,
    act_ref,
    sp_ref,
    u_ref,
    step_ref,
    slope_ref,
    dy_ref,
    h_far,
    code_ref,
    sact_ref,
    dpre_ref,
    alog_ref,
    vec_ref,
    h_ref,
    s_ref,
    d_ref,
    terms_ref,
    sums_b_ref,
    sums_c_ref,
    wide_ref,
    sems,
    *,
    count,
    states,
    chunks,
):
    micro = pl.program_id(0)
    block = states * chunks
    segment = count // SEGMENTS

    def fetch(which, k):
        extent = segment * block
        buffer = h_ref.at[which % 2]
        return pltpu.make_async_copy(
            h_far.at[aligned((which * SEGMENTS + k) * extent, extent)],
            buffer.at[pl.ds(block + k * extent, extent)],
            sems.at[which % 2, k],
        )

    @pl.when(micro == 0)
    def _():
        for k in reversed(range(SEGMENTS)):
            fetch(0, k).start()
        for which in range(2):
            h_ref[which, pl.ds(0, block), :] = jnp.zeros((block, LANES), F32)
        alog_ref[...] = jnp.zeros_like(alog_ref)
        vec_ref[...] = jnp.zeros_like(vec_ref)

    half = place_ref[HALF]
    eighth = states // 2
    zero = (jnp.zeros((chunks, LANES), F32),) * states
    spread_lanes(bc_ref, wide_ref)

    @pl.when(micro + 1 < pl.num_programs(0))
    def _():
        for k in reversed(range(SEGMENTS)):
            fetch(micro + 1, k).start()

    side = micro % 2

    def put_terms(which, t, terms):
        for n in range(0, states, 2):
            pair = jnp.concatenate(terms[n : n + 2]).astype(BF16)
            place = aligned(t * block + n * chunks, 2 * chunks, 16)
            terms_ref[which, place, :] = pair

    def retreat(back, carry):
        flows, totals = carry
        for slot in range(4):
            t = count - 1 - (4 * back + slot)
            span = pl.ds(t, chunks, stride=count)
            sp = sp_ref[span, :]
            u = u_ref[span, :]
            dy = dy_ref[span, :]
            out_flows = []
            out_totals = []
            b_terms, c_terms = [], []
            d_sum = None
            s_sum = None
            for n in range(states):
                rate = decay_ref[pl.ds(n * chunks, chunks), :]
                dh = flows[n] + dy * every_row(wide_ref, c_at(n, eighth) * count + t, chunks)
                flow = jnp.exp2(sp * rate) * dh
                out_flows.append(flow)
                q = flow * h_ref[side, aligned(t * block + n * chunks, chunks), :]
                now = h_ref[side, aligned((t + 1) * block + n * chunks, chunks), :]
                out_totals.append(totals[n] + q * sp)
                d_term = q * rate
                s_term = dh * every_row(wide_ref, b_at(n, eighth) * count + t, chunks)
                d_sum = d_term if d_sum is None else d_sum + d_term
                s_sum = s_term if s_sum is None else s_sum + s_term
                b_terms.append(dh * u)
                c_terms.append(dy * now)
            s_ref[span, :] = s_sum
            d_ref[span, :] = d_sum
            put_terms(0, t, b_terms)
            put_terms(1, t, c_terms)
            flows, totals = tuple(out_flows), tuple(out_totals)
        return flows, totals

    carry = (zero, zero)
    for k in range(SEGMENTS):
        fetch(micro, SEGMENTS - 1 - k).wait()
        carry = lax.fori_loop(k * segment // 4, (k + 1) * segment // 4, retreat, carry)
    totals = carry[1]
    for n in range(states):
        alog_ref[pl.ds(n * chunks, chunks), :] += totals[n]

    shape = (2 * states, 2 * block)
    group = lax.broadcasted_iota(jnp.int32, shape, 1) // chunks
    gather = jnp.where(group == lax.broadcasted_iota(jnp.int32, shape, 0), 1.0, 0.0).astype(BF16)

    @pl.loop(0, count // 64)
    def _(step):
        for which, sums_ref in ((0, sums_b_ref), (1, sums_c_ref)):
            for k in range(32):
                at = 32 * step + k
                terms = terms_ref[which, aligned(at * 2 * block, 2 * block, 16), :]
                sums_ref[aligned(at * 2 * states, 2 * states), :] = dot(gather, terms, 1, 0)

    ranks = dt_ref.shape[0]
    drank = None
    for chunk in range(chunks):
        cols = slice(chunk * LANES, (chunk + 1) * LANES)
        place = pl.ds(chunk * count, count)
        act = act_ref[:, cols].astype(F32)
        weight = dt_ref[:, lanes(2 * chunk + half)]
        s_now = s_ref[place, :]
        dstep = d_ref[place, :] * (1.0 / LOG2E) + s_now * act
        dy = dy_ref[place, :]
        skip = skip_ref[pl.ds(2 * chunk + half, 1), :]
        sact_ref[:, cols] = s_now * step_ref[:, cols] + dy * skip
        dpre = dstep * slope_ref[:, cols].astype(F32)
        vec_ref[0:1, cols] += jnp.sum(dpre, axis=0, keepdims=True)
        vec_ref[1:2, cols] += jnp.sum(dy * act, axis=0, keepdims=True)
        low = dpre.astype(BF16)
        dpre_ref[:, cols] = low
        term = dot(low, weight, 1, 1)
        drank = term if drank is None else drank + term
    source = lax.broadcasted_iota(jnp.int32, (2 * LANES, LANES), 0)
    target = lax.broadcasted_iota(jnp.int32, (2 * LANES, LANES), 1)
    code = None
    for n in range(states):
        pair = jnp.concatenate(
            [ref[pl.ds(n, count, stride=states), :] for ref in (sums_b_ref, sums_c_ref)], axis=1
        )
        column = ranks + jnp.where(source < LANES, b_at(n, eighth), c_at(n, eighth))
        pick = jnp.where(target == column, 1.0, 0.0).astype(BF16)
        term = dot(pair.astype(BF16), pick, 1, 0)
        code = term if code is None else code + term
    drank = jnp.concatenate([drank, jnp.zeros((count, LANES - ranks), F32)], axis=1)
    code_ref[...] = (code + drank).astype(BF16)


def scan_backward(place, micros, bc, decay, dt, skip, act, sp, u, step, slope, dy, h):
    rows, own = act.shape
    count = rows // micros
    chunks = own // LANES
    states = bc.shape[1] // 2
    outs = [
        ((rows, LANES), BF16),
        ((rows, own), F32),
        ((rows, own), BF16),
        ((states * chunks, LANES), F32),
        ((2, own), F32),
    ]

    def block(*shape):
        return pl.BlockSpec(shape, lambda i, p: (i, 0))

    return pl.pallas_call(
        functools.partial(backward_kernel, count=count, states=states, chunks=chunks),
        grid_spec=pltpu.PrefetchScalarGridSpec(
            num_scalar_prefetch=1,
            grid=(micros,),
            in_specs=[
                block(count, 2 * states),
                whole(decay.shape),
                whole(dt.shape),
                whole(skip.shape),
                block(count, own),
                block(chunks * count, LANES),
                block(chunks * count, LANES),
                block(count, own),
                block(count, own),
                block(chunks * count, LANES),
                ANY,
            ],
            out_specs=[block(count, LANES), block(count, own), block(count, own)]
            + [whole(shape) for shape, _ in outs[3:]],
            scratch_shapes=[
                pltpu.VMEM((2, (count + 1) * states * chunks, LANES), F32),
                pltpu.VMEM((chunks * count, LANES), F32),
                pltpu.VMEM((chunks * count, LANES), F32),
                pltpu.VMEM((2, count * states * chunks, LANES), BF16),
                pltpu.VMEM((count * states, LANES), F32),
                pltpu.VMEM((count * states, LANES), F32),
                pltpu.VMEM((2 * states * count + 8, LANES), F32),
                pltpu.SemaphoreType.DMA((2, SEGMENTS)),
            ],
        ),
        out_shape=[hbm(*out) for out in outs],
        compiler_params=params(52),
        cost_estimate=cost(0),
        name="scan_backward",
    )(place, *in_hbm((bc, decay, dt, skip, act, sp, u, step, slope, dy, h)))


def tail_kernel(
    place_ref,
    len_ref,
    *refs,
    micros,
    count,
    taps,
    clusters,
    ranks,
    chunks,
    states,
):
    def take(number):
        nonlocal refs
        taken, refs = refs[:number], refs[number:]
        return taken

    code_own_ref, code_other_ref = take(2)
    sact_ref, dpre_ref, alog_sum_ref, back_ref = take(4)
    dtx_ref, bc_own_ref, bc_other_ref, decay_ref = take(4)
    bend_ref, inner_ref, act_ref, high_ref, convw_ref = take(5)
    normed_ref, weight_ref, gate_part_ref, x_ref = take(4)
    keep_ref, send_ref, dnormed_ref = take(3)
    mask_ref, code_ref, wcode_ref, vec_ref, alog_ref, total_ref, win_ref, sems, low_ref = refs[:9]
    code_turned_ref, rank_turned_ref = refs[9:]

    step = pl.program_id(0)
    rows = micros * count
    eighth = states // 2
    edge = LANES // 2
    half, core, cube, face = (place_ref[k] for k in range(4))
    pair = step ^ face
    span = LANES + 32

    def fetch(k):
        source = weight_ref.at[0, pl.ds(2 * (k ^ face), 2), half]
        return (pltpu.make_async_copy(source, win_ref.at[k], sems.at[k]),)

    stream(step, win_ref.shape[0], fetch)

    def pack_row(chunk):
        relative = chunk ^ cube
        return (relative & 3) * span + LANES + (relative >> 2) * 16

    def place_pair(start, size, cols, even, odd):
        keep_ref[aligned(start, size, 16), cols] = jnp.where(core == 0, even, odd).astype(BF16)
        send_ref[aligned(start, size, 16), cols] = jnp.where(core == 0, odd, even).astype(BF16)

    @pl.when(step == 0)
    def _():
        fill_masks(len_ref, mask_ref, micros, count, taps, clusters)
        total_ref[...] = gate_part_ref[...].astype(F32)
        code_ref[...] = (
            code_own_ref[...].astype(F32) + code_other_ref[...].astype(F32)
        ).astype(BF16)
        code_turned_ref[...] = code_ref[...].T
        rank_turned_ref[...] = high_ref[...].T
        alog_ref[...] = alog_sum_ref[...] * (decay_ref[...] * (1.0 / LOG2E))

    code = code_ref[...]
    lane = lax.broadcasted_iota(jnp.int32, (1, LANES), 1)
    for part in range(2):
        source = lanes(2 * (2 * pair + part) + half)
        cols = slice(part * LANES, (part + 1) * LANES)
        wcode_ref[:ranks, cols] = dtx_ref[:, source]
        own = bc_own_ref[:, :, source].reshape(states, LANES)
        other = bc_other_ref[:, :, source].reshape(states, LANES)
        wcode_ref[ranks : ranks + states, cols] = jnp.where(half == 0, own, other)
        wcode_ref[ranks + states : ranks + 2 * states, cols] = jnp.where(half == 0, other, own)
        wcode_ref[ranks + 2 * states :, cols] = jnp.zeros(
            (LANES - ranks - 2 * states, LANES), BF16
        )
    for part in range(2):
        cols = slice(part * LANES, (part + 1) * LANES)
        chunk = 2 * pair + part
        source = 2 * chunk + half
        weights = convw_ref[:, lanes(source)]
        dact = sact_ref[:, cols] + dot(code, wcode_ref[:, cols], 1, 0)
        dconv = dact * bend_ref[:, cols].astype(F32)
        inner = inner_ref[:, cols]
        dinner = weights[taps - 1 : taps] * dconv
        sums = [None] * (taps + 1)
        sums[taps - 1] = jnp.sum(dconv * inner, axis=0, keepdims=True)
        sums[taps] = jnp.sum(dconv, axis=0, keepdims=True)
        for back in range(1, taps):
            kept = dconv * mask_ref[back]
            dinner = dinner + weights[taps - 1 - back : taps - back] * pltpu.roll(
                kept, rows - back, 0
            )
            sums[taps - 1 - back] = jnp.sum(
                kept * pltpu.roll(inner, back, 0), axis=0, keepdims=True
            )
        for k in range(taps + 1):
            vec_ref[k : k + 1, lanes(chunk)] = sums[k]
        vec_ref[taps + 1 : taps + 3, lanes(chunk)] = back_ref[:, lanes(chunk)]
        low_ref[:, cols] = dinner.astype(BF16)

        act = act_ref[:, cols]
        start = pack_row(chunk)
        code_rows = dot(code_turned_ref[...], act, 1, 0)
        rank_rows = dot(rank_turned_ref[...], dpre_ref[:, cols], 1, 0)[ranks:]
        dtx_rows = code_rows[:ranks]
        even = jnp.where(lane < edge, dtx_rows, pltpu.roll(rank_rows, edge, 1))
        odd = jnp.where(lane < edge, pltpu.roll(dtx_rows, edge, 1), rank_rows)
        for k in range(4):
            place = slice(k * 16, (k + 1) * 16)
            place_pair(
                start, 16, slice(k * LANES, (k + 1) * LANES), even[place], odd[place]
            )
        state_rows = code_rows[ranks : ranks + 2 * states]
        place_pair(
            start, 16, slice(4 * LANES, 5 * LANES), state_rows[:states], state_rows[states:]
        )

    normed = normed_ref[...]
    for part in range(2):
        grad = dot(low_ref[:, lanes(core ^ part)], normed, 0, 0)
        out_ref = (keep_ref, send_ref)[part]
        out_ref[aligned(step * span, LANES, 16), :] = grad.astype(BF16)
    width = total_ref.shape[1]
    total_ref[...] += dot(low_ref[...], win_ref[step].reshape(2 * LANES, width), 1, 0)

    @pl.when(step == pl.num_programs(0) - 1)
    def _():
        total = total_ref[...]
        dnormed_ref[...] = total.astype(BF16)
        x = x_ref[...].astype(F32)
        unit = x * lax.rsqrt(jnp.mean(x * x, axis=1, keepdims=True) + EPSILON)
        vec_ref[taps + 3 : taps + 4, :] = jnp.sum(total * unit, axis=0, keepdims=True)
        is_gain = lax.broadcasted_iota(jnp.int32, (8, LANES), 0) == taps + 3
        for chunk in range(chunks):
            start = pack_row(chunk)
            vec = vec_ref[:, chunk * LANES : (chunk + 1) * LANES]
            far, farther = (pltpu.roll(vec, LANES - k * edge // 2, 1) for k in (1, 2))
            even = jnp.where(is_gain & (lane >= edge // 2), far, vec)
            odd = jnp.where(is_gain & (lane < edge // 2), far, farther)
            alog = [
                alog_ref[pl.ds(q * eighth * chunks + chunk, eighth, stride=chunks), :]
                for q in range(2)
            ]
            place_pair(
                start,
                16,
                slice(5 * LANES, 6 * LANES),
                jnp.concatenate([alog[0], even]),
                jnp.concatenate([alog[1], odd]),
            )
            blank = jnp.zeros((16, 2 * LANES), F32)
            place_pair(start, 16, slice(6 * LANES, 8 * LANES), blank, blank)


def tail(
    place,
    lengths,
    code_own,
    code_other,
    sact,
    dpre,
    alog,
    back,
    dtx,
    bc_own,
    bc_other,
    decay,
    bend,
    inner,
    act,
    high,
    convw,
    normed,
    w4,
    gate_part,
    x,
):
    rows, own = act.shape
    chunks = own // LANES
    width = normed.shape[1]
    micros, _, clusters = lengths.shape
    count = rows // micros
    taps = convw.shape[0]
    ranks = dtx.shape[0]
    states = decay.shape[0] // chunks
    cols = 2 * LANES
    extent = 4 * (LANES + 32)

    def by_cols(height):
        return pl.BlockSpec((height, cols), lambda i, p: (0, i ^ p[FACE]))

    in_specs = (
        [pl.BlockSpec(memory_space=pltpu.SMEM)]
        + [whole((rows, LANES))] * 2
        + [by_cols(rows)] * 2
        + [whole(alog.shape), whole(back.shape)]
        + [whole(array.shape) for array in (dtx, bc_own, bc_other, decay)]
        + [by_cols(rows)] * 3
        + [whole(array.shape) for array in (high, convw, normed)]
        + [
            ANY,
            whole((rows, width)),
            whole((rows, width)),
        ]
    )
    return pl.pallas_call(
        functools.partial(
            tail_kernel,
            micros=micros,
            count=count,
            taps=taps,
            clusters=clusters,
            ranks=ranks,
            chunks=chunks,
            states=states,
        ),
        grid_spec=pltpu.PrefetchScalarGridSpec(
            num_scalar_prefetch=1,
            grid=(chunks // 2,),
            in_specs=in_specs,
            out_specs=[whole((extent, width)), whole((extent, width)), whole((rows, width))],
            scratch_shapes=[
                pltpu.VMEM((taps, rows, LANES), F32),
                pltpu.VMEM((rows, LANES), BF16),
                pltpu.VMEM((LANES, cols), BF16),
                pltpu.VMEM((8, own), F32),
                pltpu.VMEM((states * chunks, LANES), F32),
                pltpu.VMEM((rows, width), F32),
                pltpu.VMEM((chunks // 2, 2, LANES, width), BF16),
                pltpu.SemaphoreType.DMA((chunks // 2,)),
                pltpu.VMEM((rows, cols), BF16),
                pltpu.VMEM((LANES, rows), BF16),
                pltpu.VMEM((2 * ranks, rows), BF16),
            ],
        ),
        out_shape=[
            hbm((extent, width), BF16),
            hbm((extent, width), BF16),
            hbm((rows, width), BF16),
        ],
        compiler_params=params(34),
        cost_estimate=cost(7),
        name="tail",
    )(
        place,
        lengths,
        *in_hbm([code_own]),
        code_other,
        *in_hbm(
            (
                sact,
                dpre,
                alog,
                back,
                dtx,
                bc_own,
                bc_other,
                decay,
                bend,
                inner,
                act,
                high,
                convw,
                normed,
                w4,
                gate_part,
                x,
            )
        ),
    )


def fetch_halves(source, which, half, target_ref, sems):
    copies = []
    for k in range(target_ref.shape[0]):
        pair = pl.ds(2 * k, 2)
        block = source.at[pair, half] if which is None else source.at[which, pair, half]
        copies.append(pltpu.make_async_copy(block, target_ref.at[k], sems.at[k]))
    for copy in copies:
        copy.start()
    return copies


def products_kernel(
    place_ref,
    gated_ref,
    dgate_ref,
    out_ref,
    weight_ref,
    mixed_ref,
    dnormed_ref,
    wout_ref,
    wgate_ref,
    out_sems,
    gate_sems,
):
    half = place_ref[HALF]
    width = mixed_ref.shape[1]
    jobs = (
        (fetch_halves(out_ref, None, half, wout_ref, out_sems), gated_ref, wout_ref, mixed_ref),
        (fetch_halves(weight_ref, 1, half, wgate_ref, gate_sems), dgate_ref, wgate_ref, dnormed_ref),
    )
    for copies, left_ref, right_ref, result_ref in jobs:
        total = None
        for k, copy in enumerate(copies):
            copy.wait()
            left = left_ref[:, 2 * k * LANES : 2 * (k + 1) * LANES]
            term = dot(left, right_ref[k].reshape(-1, width), 1, 0)
            total = term if total is None else total + term
        result_ref[...] = total.astype(BF16)


def products(place, gated, dgate, wout3, w4):
    rows, own = gated.shape
    width = w4.shape[-1]
    pairs = own // (2 * LANES)
    return pl.pallas_call(
        products_kernel,
        grid_spec=pltpu.PrefetchScalarGridSpec(
            num_scalar_prefetch=1,
            grid=(1,),
            in_specs=[whole((rows, own)), whole((rows, own)), ANY, ANY],
            out_specs=[whole((rows, width))] * 2,
            scratch_shapes=[
                pltpu.VMEM((pairs, 2, LANES, width), BF16),
                pltpu.VMEM((pairs, 2, LANES, width), BF16),
                pltpu.SemaphoreType.DMA((pairs,)),
                pltpu.SemaphoreType.DMA((pairs,)),
            ],
        ),
        out_shape=[hbm((rows, width), BF16)] * 2,
        compiler_params=params(20),
        cost_estimate=cost(4),
        name="products",
    )(place, *in_hbm((gated, dgate, wout3, w4)))


def finish_kernel(x_ref, mine_ref, theirs_ref, cotan_ref, gain_ref, grad_ref):
    x = x_ref[...].astype(F32)
    scale = lax.rsqrt(jnp.mean(x * x, axis=1, keepdims=True) + EPSILON)
    unit = x * scale
    dhat = (mine_ref[...].astype(F32) + theirs_ref[...].astype(F32)) * gain_ref[...]
    grad_ref[...] = cotan_ref[...].astype(F32) + scale * (
        dhat - unit * jnp.mean(dhat * unit, axis=1, keepdims=True)
    )


def finish(x, mine, theirs, cotan, gain):
    rows, width = x.shape
    by_rows = pl.BlockSpec((rows // 4, width), lambda i: (i, 0))
    return pl.pallas_call(
        finish_kernel,
        grid=(4,),
        in_specs=[by_rows] * 4 + [whole(gain.shape)],
        out_specs=by_rows,
        out_shape=jax.ShapeDtypeStruct((rows, width), F32),
        compiler_params=params(16),
        cost_estimate=cost(0),
        name="finish",
    )(*in_hbm((x, mine)), theirs, *in_hbm((cotan, gain)))


def unpack_kernel(
    near_ref,
    far_ref,
    out_ref,
    dtx_ref,
    dt_ref,
    bc_ref,
    alog_ref,
    convw_ref,
    convb_ref,
    bias_ref,
    skip_ref,
    out_grad_ref,
    *,
    eighth,
    taps,
    edge,
):
    pack = near_ref[...].astype(F32) + far_ref[...].astype(F32)
    turned = jnp.concatenate([pack[:, k * LANES : (k + 1) * LANES] for k in range(4)]).T
    dtx_ref[...] = turned[:edge]
    dt_ref[...] = turned[edge:]
    rows = pack[:, 4 * LANES : 5 * LANES]
    bc_ref[0] = rows[:eighth]
    bc_ref[1] = rows[eighth:]
    rows = pack[:, 5 * LANES : 6 * LANES]
    alog_ref[...] = rows[:eighth]
    vec = rows[eighth:, :edge]
    convw_ref[...] = vec[:taps]
    convb_ref[...] = vec[taps : taps + 1]
    bias_ref[...] = vec[taps + 1 : taps + 2]
    skip_ref[...] = vec[taps + 2 : taps + 3]
    out_grad_ref[...] = out_ref[...].astype(F32)


def unpack(near, far, out, eighth, taps, ranks):
    edge = LANES // 2
    shapes = [
        (edge, ranks),
        (edge, ranks),
        (2, eighth, LANES),
        (eighth, LANES),
        (taps, edge),
        (1, edge),
        (1, edge),
        (1, edge),
        out.shape,
    ]
    return pl.pallas_call(
        functools.partial(unpack_kernel, eighth=eighth, taps=taps, edge=edge),
        grid=(1,),
        in_specs=[whole(array.shape) for array in (near, far, out)],
        out_specs=[whole(shape) for shape in shapes],
        out_shape=[jax.ShapeDtypeStruct(shape, F32) for shape in shapes],
        cost_estimate=cost(0),
        name="unpack",
    )(near, far, out)


def swap_pair(array):
    count = lax.axis_size("state")
    return lax.ppermute(array, "state", [(pos, pos ^ 1) for pos in range(count)])


def swap_bit(array, bits):
    return lax.ppermute(array, "dp", [(pos, pos ^ bits) for pos in range(lax.axis_size("dp"))])


def swap_both(array, bits=0):
    states = lax.axis_size("state")
    pairs = []
    for d in range(lax.axis_size("dp")):
        for s in range(states):
            pairs.append((d * states + s, (((d & ~1) | s) ^ bits) * states + (d & 1)))
    return lax.ppermute(array, ("dp", "state"), pairs)


def add_mixed(x, mine, theirs):
    return (x.astype(F32) + (mine.astype(F32) + theirs.astype(F32))).astype(BF16)


def add_quarters(kept, got, start=0, stop=None):
    extent = kept.shape[0] // 4
    stop = extent if stop is None else stop
    return [
        kept[k * extent + start : k * extent + stop] + got[k * extent + start : k * extent + stop]
        for k in range(4)
    ]


def trade_quarters(quarters):
    return [quarters[0]] + [swap_bit(quarters[k], k * X_BIT) for k in range(1, 4)]


def sum_quarters(quarters):
    left, right = (quarters[k].astype(F32) + quarters[k + 1].astype(F32) for k in (0, 2))
    return (left + right).astype(BF16)


CORE_BIT, X_BIT, ZH_BIT = 1, 2, 8


def shards(
    tokens,
    cluster_len,
    norm_gain,
    in_weight,
    conv_weight,
    conv_bias,
    dtx_weight,
    dt_weight,
    dt_bias,
    bc_weight,
    a_log,
    skip_gain,
    out_weight,
    cotangent,
):
    micros, count, width = tokens.shape
    inner = out_weight.shape[0]
    taps = conv_weight.shape[0]
    ranks = dtx_weight.shape[1]
    chunks = inner // (2 * LANES)
    own = chunks * LANES
    rows = micros * count
    edge = LANES // 2
    span = LANES + 32
    dp_parts = lax.axis_size("dp")
    state_count = lax.axis_size("state")
    dp_pos = lax.axis_index("dp")
    state_pos = lax.axis_index("state")
    half = state_pos & 1
    fast = state_count == 2 and dp_parts == 2 * chunks == 16
    if fast:
        place = jnp.stack([half, dp_pos & 1, dp_pos >> 1, (dp_pos >> 1) & 3])
        bc_own, alog_own = bc_weight, a_log
        bc_other, alog_other = swap_pair(bc_weight), swap_pair(a_log)
    else:
        place = jnp.stack([half, 0, 0, 0])
        bc_all = lax.all_gather(bc_weight, "state", axis=1, tiled=True)
        alog_all = lax.all_gather(a_log, "state", axis=0, tiled=True)
        eighth = alog_all.shape[0] // 2
        bc_own, bc_other = (
            lax.dynamic_slice_in_dim(bc_all, which * eighth, eighth, 1)
            for which in (half, 1 - half)
        )
        alog_own, alog_other = (
            lax.dynamic_slice_in_dim(alog_all, which * eighth, eighth, 0)
            for which in (half, 1 - half)
        )
    place = place.astype(jnp.int32)
    eighth = alog_own.shape[0]
    states = 2 * eighth

    x = tokens.reshape(rows, width)
    cotan = cotangent.reshape(rows, width)
    w4 = in_weight.reshape(2, chunks, 2, LANES, width)
    wout3 = out_weight.reshape(chunks, 2, LANES, width)
    dtx, dt = dtx_weight.T, dt_weight.T
    bias = dt_bias.reshape(-1, LANES)
    skip = skip_gain.reshape(-1, LANES)

    normed, act_all, act, inner_own, bend, gate = project(
        place, cluster_len, x, norm_gain[None], w4, conv_weight, conv_bias.reshape(-1, LANES)
    )
    bc, rank, high, decay, sp, u, step, slope, h, dy, gated, dgate, keep, send = scan_forward(
        place,
        cluster_len,
        act_all,
        bc_own,
        bc_other,
        alog_own,
        alog_other,
        dtx,
        dt,
        bias,
        skip,
        act,
        gate,
        wout3,
        cotan,
        normed,
    )
    if fast:
        early = swap_bit(send, CORE_BIT)
    mixed_part, dn_gate = products(place, gated, dgate, wout3, w4)
    if fast:
        *quarters, mixed_part, dn_gate, sp = lax.optimization_barrier(
            (*add_quarters(keep, early), mixed_part, dn_gate, sp)
        )
        early_got = trade_quarters(quarters)
    code_own, sact, dpre, alog, back = scan_backward(
        place, micros, bc, decay, dt, skip, act, sp, u, step, slope, dy, h
    )
    if fast:
        *early_got, code_own, mixed_part = lax.optimization_barrier(
            (*early_got, code_own, mixed_part)
        )
    code_other = swap_pair(code_own)
    mixed_other = swap_pair(mixed_part)
    if fast:
        block = sum_quarters(early_got)
        out_keep, out_send, gate_sum = block[:edge], block[edge:LANES], block[LANES:]
        out_send, gate_sum, bend = lax.optimization_barrier((out_send, gate_sum, bend))
        out_got = swap_bit(out_send, ZH_BIT)
    late_keep, late_send, dnormed_part = tail(
        place,
        cluster_len,
        code_own,
        code_other,
        sact,
        dpre,
        alog,
        back,
        dtx,
        bc_own,
        bc_other,
        decay,
        bend,
        inner_own,
        act,
        high,
        conv_weight,
        normed,
        w4,
        dn_gate,
        x,
    )
    mixed = add_mixed(x, mixed_part, mixed_other)
    if fast:
        late_send, mixed_other = lax.optimization_barrier((late_send, mixed_other))
        mixed = add_mixed(x, mixed_part, mixed_other)
        late = swap_bit(late_send, CORE_BIT)
        late_got = trade_quarters(add_quarters(late_keep, late))
    dnormed_other = swap_pair(dnormed_part)
    tokens_grad = finish(x, dnormed_part, dnormed_other, cotan, norm_gain[None])
    if fast:
        out_own = swap_both(out_keep + out_got)
        *late_got, out_own, tokens_grad, mixed = lax.optimization_barrier(
            (*late_got, out_own, tokens_grad, mixed)
        )
        block = sum_quarters(late_got)
        inner_sum = block[:LANES]
        upper = dp_pos >= dp_parts // 2
        crossing = jnp.where(upper, inner_sum, gate_sum)
        first, second = crossing[:edge], crossing[edge:]
        first, pack_far, pack_near = lax.optimization_barrier(
            (first, block[-16:], block[LANES:-16])
        )
        pack_far = swap_both(pack_far, ZH_BIT)
        first_got = swap_bit(first, ZH_BIT)
        pack_near = swap_both(pack_near)
        first_got, pack_far, pack_near = lax.optimization_barrier((first_got, pack_far, pack_near))
        second_got = swap_bit(second, ZH_BIT)
        gain_mine = (
            pack_near[:, 5 * LANES : 6 * LANES].astype(F32)
            + pack_far[:, 5 * LANES : 6 * LANES].astype(F32)
        ).astype(BF16)
        gain_both = gain_mine[-1].astype(F32) + swap_bit(gain_mine, CORE_BIT)[-1].astype(F32)
        extent = width // (dp_parts * state_count)
        gain_grad = lax.dynamic_slice_in_dim(gain_both, (dp_pos & 1) * extent, extent, 0)
        (
            dtx_grad,
            dt_grad,
            bc_grad,
            alog_grad,
            convw_grad,
            convb_grad,
            bias_grad,
            skip_grad,
            out_own,
        ) = unpack(pack_near, pack_far, out_own, eighth, taps, ranks)
        convb_grad, bias_grad, skip_grad = (
            array[0] for array in (convb_grad, bias_grad, skip_grad)
        )
        second_got, dtx_grad, dt_grad, out_own = lax.optimization_barrier(
            (second_got, dtx_grad, dt_grad, out_own)
        )
        in_grad = jnp.where(upper, gate_sum, inner_sum).astype(F32) + jnp.concatenate(
            [first_got, second_got]
        ).astype(F32)
    mixed = mixed.reshape(micros, count, width)
    tokens_grad = tokens_grad.reshape(micros, count, width)

    if not fast:
        def total(array):
            return lax.psum(array.astype(F32), "dp")

        def both_rows(array):
            mine = array.reshape(chunks, 1, LANES, -1)
            other = swap_pair(mine)
            low = jnp.where(half == 0, mine, other)
            high = jnp.where(half == 0, other, mine)
            return jnp.concatenate([low, high], axis=1).reshape(2 * own, -1)

        every = dp_parts * state_count
        at = dp_pos * state_count + state_pos

        def cut_own(array):
            extent = array.shape[0] // every
            return lax.dynamic_slice_in_dim(array, at * extent, extent, 0)

        pair = total(jnp.stack([keep, send])).reshape(2, 2, 2, 2 * LANES, width)
        outs = pair[:, :, :, :LANES].reshape(2, 2, 2, 2, edge, width)
        outs = jnp.transpose(outs, (3, 1, 2, 0, 4, 5)).reshape(own, width)
        gates = jnp.moveaxis(pair[:, :, :, LANES:], 0, 2).reshape(own, width)
        pair = total(jnp.stack([late_keep, late_send])).reshape(2, 2, 2, span, width)
        inners = jnp.moveaxis(pair[:, :, :, :LANES], 0, 2).reshape(own, width)
        packs = pair[:, :, :, LANES:].reshape(2, 2, 2, 2, 16, width // LANES, LANES)
        packs = jnp.transpose(packs, (3, 1, 2, 0, 5, 4, 6)).reshape(chunks, 2, -1, 16, LANES)
        small = packs[:, :, :4].reshape(chunks, 2, ranks, 2, edge)
        small = both_rows(jnp.transpose(small, (0, 1, 4, 3, 2)).reshape(own, 2 * ranks))
        in_grad = cut_own(jnp.concatenate([both_rows(inners), both_rows(gates)]))
        out_own = cut_own(both_rows(outs))
        mine = cut_own(small)
        dtx_grad, dt_grad = mine[:, :ranks], mine[:, ranks:]
        vec_rows = jnp.swapaxes(packs[:, :, 5, eighth:, :edge], 2, 3).reshape(own, -1)
        gain_sum = vec_rows[:, -1].reshape(chunks, 2, 2, -1).swapaxes(1, 2).reshape(-1)
        gain_grad = cut_own(gain_sum + swap_pair(gain_sum))
        vec = cut_own(both_rows(vec_rows)).T
        state_rows = jnp.concatenate([packs[:, :, 4], packs[:, :, 5, :eighth]], axis=2)
        state_rows = state_rows.reshape(chunks, 2, 3, eighth, LANES)
        state_rows = jnp.transpose(state_rows, (0, 4, 2, 1, 3)).reshape(own, -1)
        extent = inner // dp_parts
        state_part = lax.dynamic_slice_in_dim(both_rows(state_rows), dp_pos * extent, extent, 0)
        state_part = state_part.T.reshape(3, state_count, -1, extent)
        state_part = lax.dynamic_index_in_dim(state_part, state_pos, 1, keepdims=False)
        bc_grad, alog_grad = state_part[:2], state_part[2]
        convw_grad, convb_grad, bias_grad, skip_grad = (
            vec[:taps], vec[taps], vec[taps + 1], vec[taps + 2]
        )

    return (
        mixed,
        tokens_grad,
        gain_grad,
        in_grad,
        convw_grad,
        convb_grad,
        dtx_grad,
        dt_grad,
        bias_grad,
        bc_grad,
        alog_grad,
        skip_grad,
        out_own,
    )


def solution(mesh):
    return jax.shard_map(
        shards,
        mesh=mesh,
        in_specs=(
            P(None, "dp", None),
            P(None, "dp", None),
            P(),
            P(),
            P(),
            P(),
            P(),
            P(),
            P(),
            P(None, "state", None),
            P("state", None),
            P(),
            P(),
            P(None, "dp", None),
        ),
        out_specs=(
            P(None, "dp", None),
            P(None, "dp", None),
            P(("dp", "state")),
            P(("dp", "state"), None),
            P(None, ("dp", "state")),
            P(("dp", "state")),
            P(("dp", "state"), None),
            P(("dp", "state"), None),
            P(("dp", "state")),
            P(None, "state", "dp"),
            P("state", "dp"),
            P(("dp", "state")),
            P(("dp", "state"), None),
        ),
        check_vma=False,
    )
```

```python
import functools
import math

import jax
import jax.numpy as jnp
from jax import lax
from jax.experimental import pallas as pl
from jax.experimental.pallas import tpu as pltpu
from jax.sharding import PartitionSpec as P

EPSILON = 1e-05
LANES = 128
RESET = 1e4
LOG2E = math.log2(math.e)
F32 = jnp.float32
BF16 = jnp.bfloat16
MIB = 1024 * 1024


def dot(left, right, left_dim, right_dim):
    return lax.dot_general(
        left, right, (((left_dim,), (right_dim,)), ((), ())), preferred_element_type=F32
    )


def params(mib):
    return pltpu.CompilerParams(
        vmem_limit_bytes=mib * MIB, dimension_semantics=("arbitrary",)
    )


ANY = pl.BlockSpec(memory_space=pl.ANY)


def stream(step, steps, fetch):
    @pl.when(step == 0)
    def _():
        for k in range(steps):
            for copy in fetch(k):
                copy.start()

    for copy in fetch(step):
        copy.wait()


def whole(shape):
    return pl.BlockSpec(shape, lambda *_: (0,) * len(shape))


sigmoid = jax.nn.sigmoid


def log_one_plus(value):
    series = value * (1.0 - value * (0.5 - value * (1.0 / 3.0)))
    return jnp.where(value < 1e-3, series, jnp.log(1.0 + value))


def lanes(index):
    return pl.ds(pl.multiple_of(index * LANES, LANES), LANES)


def cost(micros):
    return pl.CostEstimate(
        flops=int(micros * 1e9), bytes_accessed=int(micros * 1e6), transcendentals=0
    )


def hbm(shape, dtype):
    return pltpu.HBM(shape, dtype)


def in_hbm(arrays):
    return [pltpu.with_memory_space_constraint(array, pltpu.HBM) for array in arrays]


def aligned(start, size, to=8):
    return pl.ds(pl.multiple_of(start, to), size)


SEGMENTS = 4

HALF, CORE, CUBE, FACE = range(4)


def fill_masks(len_ref, mask_ref, micros, count, taps, clusters):
    place = lax.broadcasted_iota(jnp.int32, (count, LANES), 0)
    for micro in range(micros):
        rows = pl.ds(micro * count, count)
        for back in range(1, taps):
            apart = place < back
            start = 0
            for cluster in range(clusters - 1):
                start = start + len_ref[micro, 0, cluster]
                apart = apart | ((place >= start) & (place < start + back))
            mask_ref[back, rows, :] = jnp.where(apart, 0.0, 1.0)
            if back == 1:
                mask_ref[0, rows, :] = jnp.where(apart, 1.0, 0.0)


def project_kernel(
    place_ref,
    len_ref,
    gain_ref,
    convw_ref,
    convb_ref,
    x_far,
    weight_far,
    normed_far,
    act_far,
    own_act_far,
    inner_far,
    bend_far,
    gate_far,
    mask_ref,
    x_ref,
    win_ref,
    wgate_ref,
    normed_ref,
    act_ref,
    own_act_ref,
    inner_ref,
    bend_ref,
    gate_ref,
    in_sems,
    out_sems,
    *,
    micros,
    count,
    taps,
    clusters,
):
    half = place_ref[HALF]
    chunks = win_ref.shape[0]
    inward = [pltpu.make_async_copy(x_far, x_ref, in_sems.at[2 * chunks])]
    for k in range(chunks):
        inward.append(pltpu.make_async_copy(weight_far.at[0, k], win_ref.at[k], in_sems.at[2 * k]))
        inward.append(
            pltpu.make_async_copy(
                weight_far.at[1, k, half], wgate_ref.at[k], in_sems.at[2 * k + 1]
            )
        )
    for copy in inward:
        copy.start()
    outward = []

    def put(source, target):
        outward.append(pltpu.make_async_copy(source, target, out_sems.at[len(outward)]))
        outward[-1].start()

    fill_masks(len_ref, mask_ref, micros, count, taps, clusters)
    inward[0].wait()
    rows = x_ref[...].astype(F32)
    scale = lax.rsqrt(jnp.mean(rows * rows, axis=1, keepdims=True) + EPSILON)
    normed = (rows * scale * gain_ref[...]).astype(BF16)
    normed_ref[...] = normed
    put(normed_ref, normed_far)
    for k in range(chunks):
        inward[2 * k + 1].wait()
        inward[2 * k + 2].wait()
        proj = dot(normed, win_ref[k].reshape(2 * LANES, -1), 1, 1)
        own = slice(k * LANES, (k + 1) * LANES)
        gate_ref[:, own] = dot(normed, wgate_ref[k], 1, 1)
        inners, sigs, acts = [], [], []
        for part in range(2):
            cols = slice((2 * k + part) * LANES, (2 * k + part + 1) * LANES)
            inner = proj[:, part * LANES : (part + 1) * LANES]
            conved = convb_ref[2 * k + part : 2 * k + part + 1, :]
            conved = conved + convw_ref[taps - 1 : taps, cols] * inner
            for back in range(1, taps):
                shifted = pltpu.roll(inner, back, 0) * mask_ref[back]
                conved = conved + convw_ref[taps - 1 - back : taps - back, cols] * shifted
            sig = sigmoid(conved)
            act = conved * sig
            act_ref[:, cols] = act.astype(BF16)
            inners.append(inner)
            sigs.append(sig)
            acts.append(act)
        inner_ref[:, own] = jnp.where(half == 0, *inners)
        act, sig = jnp.where(half == 0, *acts), jnp.where(half == 0, *sigs)
        bend_ref[:, own] = (sig + act * (1.0 - sig)).astype(BF16)
        own_act_ref[:, own] = act.astype(BF16)
        if k % 2:
            group = pl.ds((k - 1) * LANES, 2 * LANES)
            wide = pl.ds(2 * (k - 1) * LANES, 4 * LANES)
            put(act_ref.at[:, wide], act_far.at[:, wide])
            for near, far in (
                (gate_ref, gate_far),
                (inner_ref, inner_far),
                (bend_ref, bend_far),
                (own_act_ref, own_act_far),
            ):
                put(near.at[:, group], far.at[:, group])
    for copy in outward:
        copy.wait()


def project(place, lengths, x, gain, w4, conv_weight, conv_bias):
    rows, width = x.shape
    chunks = w4.shape[1]
    micros, _, clusters = lengths.shape
    taps = conv_weight.shape[0]
    own = chunks * LANES
    outs = [
        ((rows, width), BF16),
        ((rows, 2 * own), BF16),
        ((rows, own), BF16),
        ((rows, own), F32),
        ((rows, own), BF16),
        ((rows, own), F32),
    ]
    return pl.pallas_call(
        functools.partial(
            project_kernel, micros=micros, count=rows // micros, taps=taps, clusters=clusters
        ),
        grid_spec=pltpu.PrefetchScalarGridSpec(
            num_scalar_prefetch=1,
            grid=(1,),
            in_specs=[
                pl.BlockSpec(memory_space=pltpu.SMEM),
                whole(gain.shape),
                whole(conv_weight.shape),
                whole(conv_bias.shape),
                ANY,
                ANY,
            ],
            out_specs=[ANY] * len(outs),
            scratch_shapes=[
                pltpu.VMEM((taps, rows, LANES), F32),
                pltpu.VMEM((rows, width), BF16),
                pltpu.VMEM((chunks, 2, LANES, width), BF16),
                pltpu.VMEM((chunks, LANES, width), BF16),
            ]
            + [pltpu.VMEM(*out) for out in outs]
            + [
                pltpu.SemaphoreType.DMA((2 * chunks + 1,)),
                pltpu.SemaphoreType.DMA((1 + 5 * chunks // 2,)),
            ],
        ),
        out_shape=[hbm(*out) for out in outs],
        compiler_params=params(30),
        cost_estimate=cost(6),
        name="project",
    )(place, *in_hbm((lengths, gain, conv_weight, conv_bias, x, w4)))


def every_row(ref, row, height):
    return ref[pl.ds(row, height, stride=0), :]


def b_at(n, eighth):
    return (n // eighth) * 2 * eighth + n % eighth


def c_at(n, eighth):
    return b_at(n, eighth) + eighth


def forward_kernel(
    place_ref,
    len_ref,
    act_all_ref,
    bc_own_ref,
    bc_other_ref,
    alog_own_ref,
    alog_other_ref,
    dtx_ref,
    dt_ref,
    bias_ref,
    skip_ref,
    act_ref,
    *refs,
    micros,
    count,
    states,
    chunks,
    clusters,
):
    gate_far, wout_far, cotan_far, normed_far = refs[:4]
    bc_ref, rank_ref, rank_high_ref, decay_ref = refs[4:8]
    sp_far, u_far, step_far, slope_far, h_far, dy_far = refs[8:14]
    gated_far, dgate_far, keep_far, send_far = refs[14:18]
    mask_ref, y_ref, tmp_ref, wide_ref = refs[18:22]
    gate_ref, wout_ref, cotan_ref, normed_ref = refs[22:26]
    sp_ref, u_ref, step_ref, slope_ref, h_ref, dy_ref = refs[26:32]
    gated_ref, dgate_ref, keep_ref, send_ref = refs[32:36]
    in_sems, out_sems = refs[36:]
    rows = micros * count
    eighth = states // 2
    half, core, cube, face = (place_ref[k] for k in range(4))
    first = half == 0
    inward = [
        pltpu.make_async_copy(source, target, in_sems.at[k])
        for k, (source, target) in enumerate(
            (
                (gate_far, gate_ref),
                (wout_far.at[:, half], wout_ref),
                (cotan_far, cotan_ref),
                (normed_far, normed_ref),
            )
        )
    ]
    for copy in inward:
        copy.start()
    outward = []

    def put(source, target):
        outward.append(pltpu.make_async_copy(source, target, out_sems.at[len(outward)]))
        outward[-1].start()

    ranks = dtx_ref.shape[0]
    weights = jnp.concatenate(
        [dtx_ref[...]] + [ref[...].reshape(states, -1) for ref in (bc_own_ref, bc_other_ref)]
    )
    product = dot(act_all_ref[...], weights, 1, 1)
    own, other = product[:, ranks : ranks + states], product[:, ranks + states :]
    bc_ref[:, :states] = jnp.where(first, own, other)
    bc_ref[:, states:] = jnp.where(first, other, own)
    spread_lanes(bc_ref, wide_ref)

    fill_masks(len_ref, mask_ref, micros, count, 2, clusters)
    for chunk in range(chunks):
        cols = lanes(2 * chunk + half)
        own, other = alog_own_ref[:, cols], alog_other_ref[:, cols]
        tmp_ref[pl.ds(chunk * states, eighth), :] = jnp.where(first, own, other)
        tmp_ref[pl.ds(chunk * states + eighth, eighth), :] = jnp.where(first, other, own)
    for n in range(states):
        decay_ref[pl.ds(n * chunks, chunks), :] = -LOG2E * jnp.exp(
            tmp_ref[pl.ds(n, chunks, stride=states), :]
        )

    rank = product[:, :ranks].astype(BF16)
    rank_ref[...] = rank
    rank_high_ref[...] = jnp.concatenate([jnp.zeros_like(rank), rank], axis=1)
    for chunk in range(chunks):
        cols = slice(chunk * LANES, (chunk + 1) * LANES)
        bias = bias_ref[pl.ds(2 * chunk + half, 1), :]
        pre = dot(rank, dt_ref[:, lanes(2 * chunk + half)], 1, 0) + bias
        tail_part = jnp.exp(-jnp.abs(pre))
        step = jnp.maximum(pre, 0.0) + log_one_plus(tail_part)
        slope = jnp.where(pre >= 0.0, 1.0, tail_part) / (1.0 + tail_part)
        step_ref[:, cols] = step
        slope_ref[:, cols] = slope.astype(BF16)
        held = step + RESET * mask_ref[0]
        source = step * act_ref[:, cols].astype(F32)
        for micro in range(micros):
            span = slice(micro * count, (micro + 1) * count)
            place = pl.ds((micro * chunks + chunk) * count, count)
            sp_ref[place, :] = held[span]
            u_ref[place, :] = source[span]
    put(sp_ref, sp_far)
    put(u_ref, u_far)
    put(step_ref, step_far)
    put(slope_ref, slope_far)

    for micro in range(micros):

        def advance(t, h, micro=micro):
            row = micro * count + t
            span = pl.ds(micro * chunks * count + t, chunks, stride=count)
            sp = sp_ref[span, :]
            u = u_ref[span, :]
            out = []
            y = None
            for n in range(states):
                decay = jnp.exp2(sp * decay_ref[pl.ds(n * chunks, chunks), :])
                now = decay * h[n] + u * every_row(wide_ref, b_at(n, eighth) * rows + row, chunks)
                h_ref[aligned((row * states + n) * chunks, chunks), :] = now
                out.append(now)
                term = now * every_row(wide_ref, c_at(n, eighth) * rows + row, chunks)
                y = term if y is None else y + term
            y_ref[span, :] = y
            return tuple(out)

        h = (jnp.zeros((chunks, LANES), F32),) * states
        segment = count // SEGMENTS
        for k in range(SEGMENTS):
            h = lax.fori_loop(k * segment, (k + 1) * segment, advance, h, unroll=8)
            extent = segment * states * chunks
            place = pl.ds((micro * SEGMENTS + k) * extent, extent)
            put(h_ref.at[place], h_far.at[place])

    for copy in inward:
        copy.wait()
    cotan = cotan_ref[...]
    for chunk in range(chunks):
        cols = slice(chunk * LANES, (chunk + 1) * LANES)
        places = [pl.ds((micro * chunks + chunk) * count, count) for micro in range(micros)]
        y = jnp.concatenate([y_ref[place, :] for place in places])
        y = y + skip_ref[pl.ds(2 * chunk + half, 1), :] * act_ref[:, cols].astype(F32)
        gate = gate_ref[:, cols]
        sig = sigmoid(gate)
        gated_ref[:, cols] = (y * (gate * sig)).astype(BF16)
        dgated = dot(cotan, wout_ref[chunk], 1, 1)
        dy = dgated * (gate * sig)
        for micro in range(micros):
            dy_ref[places[micro], :] = dy[micro * count : (micro + 1) * count]
        dgate_ref[:, cols] = (dgated * y * (sig * (1.0 + gate * (1.0 - sig)))).astype(BF16)
    put(dy_ref, dy_far)
    put(gated_ref, gated_far)
    put(dgate_ref, dgate_far)
    normed = normed_ref[...]
    edge = LANES // 2
    for r in range(chunks // 2):
        for zh in range(2):
            grad = dot(gated_ref[:, lanes((r + 4 * zh) ^ cube)], cotan, 0, 0).astype(BF16)
            top, bottom = grad[:edge], grad[edge:]
            place = pl.ds(r * 2 * LANES + zh * edge, edge)
            keep_ref[place, :] = jnp.where(core == 0, top, bottom)
            send_ref[place, :] = jnp.where(core == 0, bottom, top)
        place = pl.ds((2 * r + 1) * LANES, LANES)
        pair = 2 * (r ^ face)
        for chunk, out_ref in ((pair + core, keep_ref), (pair + 1 - core, send_ref)):
            out_ref[place, :] = dot(dgate_ref[:, lanes(chunk)], normed, 0, 0).astype(BF16)
        place = pl.ds(r * 2 * LANES, 2 * LANES)
        put(send_ref.at[place], send_far.at[place])
        put(keep_ref.at[place], keep_far.at[place])
    for copy in outward:
        copy.wait()


def scan_forward(
    place,
    lengths,
    act_all,
    bc_own,
    bc_other,
    alog_own,
    alog_other,
    dtx,
    dt,
    bias,
    skip,
    act,
    gate,
    wout3,
    cotan,
    normed,
):
    rows, own = act.shape
    chunks = own // LANES
    states = 2 * alog_own.shape[0]
    width = cotan.shape[1]
    micros, _, clusters = lengths.shape
    ranks = dtx.shape[0]
    small = [
        ((rows, 2 * states), F32),
        ((rows, ranks), BF16),
        ((rows, 2 * ranks), BF16),
        ((states * chunks, LANES), F32),
    ]
    large = [
        ((chunks * rows, LANES), F32),
        ((chunks * rows, LANES), F32),
        ((rows, own), F32),
        ((rows, own), BF16),
        ((rows * states * chunks, LANES), F32),
        ((chunks * rows, LANES), F32),
        ((rows, own), BF16),
        ((rows, own), BF16),
        ((own, width), BF16),
        ((own, width), BF16),
    ]
    operands = (act_all, bc_own, bc_other, alog_own, alog_other, dtx, dt, bias, skip, act)
    streamed = (gate, wout3, cotan, normed)
    return pl.pallas_call(
        functools.partial(
            forward_kernel,
            micros=micros,
            count=rows // micros,
            states=states,
            chunks=chunks,
            clusters=clusters,
        ),
        grid_spec=pltpu.PrefetchScalarGridSpec(
            num_scalar_prefetch=1,
            grid=(1,),
            in_specs=[pl.BlockSpec(memory_space=pltpu.SMEM)]
            + [whole(operand.shape) for operand in operands]
            + [ANY] * len(streamed),
            out_specs=[whole(shape) for shape, _ in small] + [ANY] * len(large),
            scratch_shapes=[
                pltpu.VMEM((2, rows, LANES), F32),
                pltpu.VMEM((chunks * rows, LANES), F32),
                pltpu.VMEM((states * chunks, LANES), F32),
                pltpu.VMEM((2 * states * rows + 8, LANES), F32),
                pltpu.VMEM((rows, own), F32),
                pltpu.VMEM((chunks, LANES, width), BF16),
                pltpu.VMEM((rows, width), BF16),
                pltpu.VMEM((rows, width), BF16),
            ]
            + [pltpu.VMEM(*out) for out in large]
            + [pltpu.SemaphoreType.DMA((4,)), pltpu.SemaphoreType.DMA((7 + chunks + micros * SEGMENTS,))],
        ),
        out_shape=[hbm(*out) for out in small + large],
        compiler_params=params(52),
        cost_estimate=cost(19),
        name="scan_forward",
    )(
        place,
        lengths,
        *in_hbm(operands[:1]),
        *operands[1:5],
        *in_hbm((*operands[5:], *streamed)),
    )


def spread_lanes(values_ref, wide_ref):
    rows, count = values_ref.shape
    for k in range(count):
        wide_ref[pl.ds(k * rows, rows), :] = jnp.broadcast_to(
            values_ref[:, k : k + 1], (rows, LANES)
        )


def backward_kernel(
    place_ref,
    bc_ref,
    decay_ref,
    dt_ref,
    skip_ref,
    act_ref,
    sp_ref,
    u_ref,
    step_ref,
    slope_ref,
    dy_ref,
    h_far,
    code_ref,
    sact_ref,
    dpre_ref,
    alog_ref,
    vec_ref,
    h_ref,
    s_ref,
    d_ref,
    terms_ref,
    sums_b_ref,
    sums_c_ref,
    wide_ref,
    sems,
    *,
    count,
    states,
    chunks,
):
    micro = pl.program_id(0)
    block = states * chunks
    segment = count // SEGMENTS

    def fetch(which, k):
        extent = segment * block
        buffer = h_ref.at[which % 2]
        return pltpu.make_async_copy(
            h_far.at[aligned((which * SEGMENTS + k) * extent, extent)],
            buffer.at[pl.ds(block + k * extent, extent)],
            sems.at[which % 2, k],
        )

    @pl.when(micro == 0)
    def _():
        for k in reversed(range(SEGMENTS)):
            fetch(0, k).start()
        for which in range(2):
            h_ref[which, pl.ds(0, block), :] = jnp.zeros((block, LANES), F32)
        alog_ref[...] = jnp.zeros_like(alog_ref)
        vec_ref[...] = jnp.zeros_like(vec_ref)

    half = place_ref[HALF]
    eighth = states // 2
    zero = (jnp.zeros((chunks, LANES), F32),) * states
    spread_lanes(bc_ref, wide_ref)

    @pl.when(micro + 1 < pl.num_programs(0))
    def _():
        for k in reversed(range(SEGMENTS)):
            fetch(micro + 1, k).start()

    side = micro % 2

    def put_terms(which, t, terms):
        for n in range(0, states, 2):
            pair = jnp.concatenate(terms[n : n + 2]).astype(BF16)
            place = aligned(t * block + n * chunks, 2 * chunks, 16)
            terms_ref[which, place, :] = pair

    def retreat(back, carry):
        flows, totals = carry
        for slot in range(8):
            t = count - 1 - (8 * back + slot)
            span = pl.ds(t, chunks, stride=count)
            sp = sp_ref[span, :]
            u = u_ref[span, :]
            dy = dy_ref[span, :]
            out_flows = []
            out_totals = []
            b_terms, c_terms = [], []
            d_sum = None
            s_sum = None
            for n in range(states):
                rate = decay_ref[pl.ds(n * chunks, chunks), :]
                dh = flows[n] + dy * every_row(wide_ref, c_at(n, eighth) * count + t, chunks)
                flow = jnp.exp2(sp * rate) * dh
                out_flows.append(flow)
                q = flow * h_ref[side, aligned(t * block + n * chunks, chunks), :]
                now = h_ref[side, aligned((t + 1) * block + n * chunks, chunks), :]
                out_totals.append(totals[n] + q * sp)
                d_term = q * rate
                s_term = dh * every_row(wide_ref, b_at(n, eighth) * count + t, chunks)
                d_sum = d_term if d_sum is None else d_sum + d_term
                s_sum = s_term if s_sum is None else s_sum + s_term
                b_terms.append(dh * u)
                c_terms.append(dy * now)
            s_ref[span, :] = s_sum
            d_ref[span, :] = d_sum
            put_terms(0, t, b_terms)
            put_terms(1, t, c_terms)
            flows, totals = tuple(out_flows), tuple(out_totals)
        return flows, totals

    carry = (zero, zero)
    for k in range(SEGMENTS):
        fetch(micro, SEGMENTS - 1 - k).wait()
        carry = lax.fori_loop(k * segment // 8, (k + 1) * segment // 8, retreat, carry)
    totals = carry[1]
    for n in range(states):
        alog_ref[pl.ds(n * chunks, chunks), :] += totals[n]

    shape = (2 * states, 2 * block)
    group = lax.broadcasted_iota(jnp.int32, shape, 1) // chunks
    gather = jnp.where(group == lax.broadcasted_iota(jnp.int32, shape, 0), 1.0, 0.0).astype(BF16)

    @pl.loop(0, count // 64)
    def _(step):
        for which, sums_ref in ((0, sums_b_ref), (1, sums_c_ref)):
            for k in range(32):
                at = 32 * step + k
                terms = terms_ref[which, aligned(at * 2 * block, 2 * block, 16), :]
                sums_ref[aligned(at * 2 * states, 2 * states), :] = dot(gather, terms, 1, 0)

    ranks = dt_ref.shape[0]
    drank = None
    for chunk in range(chunks):
        cols = slice(chunk * LANES, (chunk + 1) * LANES)
        place = pl.ds(chunk * count, count)
        act = act_ref[:, cols].astype(F32)
        weight = dt_ref[:, lanes(2 * chunk + half)]
        s_now = s_ref[place, :]
        dstep = d_ref[place, :] * (1.0 / LOG2E) + s_now * act
        dy = dy_ref[place, :]
        skip = skip_ref[pl.ds(2 * chunk + half, 1), :]
        sact_ref[:, cols] = s_now * step_ref[:, cols] + dy * skip
        dpre = dstep * slope_ref[:, cols].astype(F32)
        vec_ref[0:1, cols] += jnp.sum(dpre, axis=0, keepdims=True)
        vec_ref[1:2, cols] += jnp.sum(dy * act, axis=0, keepdims=True)
        low = dpre.astype(BF16)
        dpre_ref[:, cols] = low
        term = dot(low, weight, 1, 1)
        drank = term if drank is None else drank + term
    source = lax.broadcasted_iota(jnp.int32, (2 * LANES, LANES), 0)
    target = lax.broadcasted_iota(jnp.int32, (2 * LANES, LANES), 1)
    code = None
    for n in range(states):
        pair = jnp.concatenate(
            [ref[pl.ds(n, count, stride=states), :] for ref in (sums_b_ref, sums_c_ref)], axis=1
        )
        column = ranks + jnp.where(source < LANES, b_at(n, eighth), c_at(n, eighth))
        pick = jnp.where(target == column, 1.0, 0.0).astype(BF16)
        term = dot(pair.astype(BF16), pick, 1, 0)
        code = term if code is None else code + term
    drank = jnp.concatenate([drank, jnp.zeros((count, LANES - ranks), F32)], axis=1)
    code_ref[...] = (code + drank).astype(BF16)


def scan_backward(place, micros, bc, decay, dt, skip, act, sp, u, step, slope, dy, h):
    rows, own = act.shape
    count = rows // micros
    chunks = own // LANES
    states = bc.shape[1] // 2
    outs = [
        ((rows, LANES), BF16),
        ((rows, own), F32),
        ((rows, own), BF16),
        ((states * chunks, LANES), F32),
        ((2, own), F32),
    ]

    def block(*shape):
        return pl.BlockSpec(shape, lambda i, p: (i, 0))

    return pl.pallas_call(
        functools.partial(backward_kernel, count=count, states=states, chunks=chunks),
        grid_spec=pltpu.PrefetchScalarGridSpec(
            num_scalar_prefetch=1,
            grid=(micros,),
            in_specs=[
                block(count, 2 * states),
                whole(decay.shape),
                whole(dt.shape),
                whole(skip.shape),
                block(count, own),
                block(chunks * count, LANES),
                block(chunks * count, LANES),
                block(count, own),
                block(count, own),
                block(chunks * count, LANES),
                ANY,
            ],
            out_specs=[block(count, LANES), block(count, own), block(count, own)]
            + [whole(shape) for shape, _ in outs[3:]],
            scratch_shapes=[
                pltpu.VMEM((2, (count + 1) * states * chunks, LANES), F32),
                pltpu.VMEM((chunks * count, LANES), F32),
                pltpu.VMEM((chunks * count, LANES), F32),
                pltpu.VMEM((2, count * states * chunks, LANES), BF16),
                pltpu.VMEM((count * states, LANES), F32),
                pltpu.VMEM((count * states, LANES), F32),
                pltpu.VMEM((2 * states * count + 8, LANES), F32),
                pltpu.SemaphoreType.DMA((2, SEGMENTS)),
            ],
        ),
        out_shape=[hbm(*out) for out in outs],
        compiler_params=params(52),
        cost_estimate=cost(0),
        name="scan_backward",
    )(place, *in_hbm((bc, decay, dt, skip, act, sp, u, step, slope, dy, h)))


def tail_kernel(
    place_ref,
    len_ref,
    *refs,
    micros,
    count,
    taps,
    clusters,
    ranks,
    chunks,
    states,
):
    def take(number):
        nonlocal refs
        taken, refs = refs[:number], refs[number:]
        return taken

    code_own_ref, code_other_ref = take(2)
    sact_ref, dpre_ref, alog_sum_ref, back_ref = take(4)
    dtx_ref, bc_own_ref, bc_other_ref, decay_ref = take(4)
    bend_ref, inner_ref, act_ref, high_ref, convw_ref = take(5)
    normed_ref, weight_ref, gate_part_ref, x_ref = take(4)
    keep_ref, send_ref, dnormed_ref = take(3)
    mask_ref, code_ref, wcode_ref, vec_ref, alog_ref, total_ref, win_ref, sems, low_ref = refs[:9]
    code_turned_ref, rank_turned_ref = refs[9:]

    step = pl.program_id(0)
    rows = micros * count
    eighth = states // 2
    edge = LANES // 2
    half, core, cube, face = (place_ref[k] for k in range(4))
    pair = step ^ face
    span = LANES + 32

    def fetch(k):
        source = weight_ref.at[0, pl.ds(2 * (k ^ face), 2), half]
        return (pltpu.make_async_copy(source, win_ref.at[k], sems.at[k]),)

    stream(step, win_ref.shape[0], fetch)

    def pack_row(chunk):
        relative = chunk ^ cube
        return (relative & 3) * span + LANES + (relative >> 2) * 16

    def place_pair(start, size, cols, even, odd):
        keep_ref[aligned(start, size, 16), cols] = jnp.where(core == 0, even, odd).astype(BF16)
        send_ref[aligned(start, size, 16), cols] = jnp.where(core == 0, odd, even).astype(BF16)

    @pl.when(step == 0)
    def _():
        fill_masks(len_ref, mask_ref, micros, count, taps, clusters)
        total_ref[...] = gate_part_ref[...].astype(F32)
        code_ref[...] = (
            code_own_ref[...].astype(F32) + code_other_ref[...].astype(F32)
        ).astype(BF16)
        code_turned_ref[...] = code_ref[...].T
        rank_turned_ref[...] = high_ref[...].T
        alog_ref[...] = alog_sum_ref[...] * (decay_ref[...] * (1.0 / LOG2E))

    code = code_ref[...]
    lane = lax.broadcasted_iota(jnp.int32, (1, LANES), 1)
    for part in range(2):
        source = lanes(2 * (2 * pair + part) + half)
        cols = slice(part * LANES, (part + 1) * LANES)
        wcode_ref[:ranks, cols] = dtx_ref[:, source]
        own = bc_own_ref[:, :, source].reshape(states, LANES)
        other = bc_other_ref[:, :, source].reshape(states, LANES)
        wcode_ref[ranks : ranks + states, cols] = jnp.where(half == 0, own, other)
        wcode_ref[ranks + states : ranks + 2 * states, cols] = jnp.where(half == 0, other, own)
        wcode_ref[ranks + 2 * states :, cols] = jnp.zeros(
            (LANES - ranks - 2 * states, LANES), BF16
        )
    for part in range(2):
        cols = slice(part * LANES, (part + 1) * LANES)
        chunk = 2 * pair + part
        source = 2 * chunk + half
        weights = convw_ref[:, lanes(source)]
        dact = sact_ref[:, cols] + dot(code, wcode_ref[:, cols], 1, 0)
        dconv = dact * bend_ref[:, cols].astype(F32)
        inner = inner_ref[:, cols]
        dinner = weights[taps - 1 : taps] * dconv
        sums = [None] * (taps + 1)
        sums[taps - 1] = jnp.sum(dconv * inner, axis=0, keepdims=True)
        sums[taps] = jnp.sum(dconv, axis=0, keepdims=True)
        for back in range(1, taps):
            kept = dconv * mask_ref[back]
            dinner = dinner + weights[taps - 1 - back : taps - back] * pltpu.roll(
                kept, rows - back, 0
            )
            sums[taps - 1 - back] = jnp.sum(
                kept * pltpu.roll(inner, back, 0), axis=0, keepdims=True
            )
        for k in range(taps + 1):
            vec_ref[k : k + 1, lanes(chunk)] = sums[k]
        vec_ref[taps + 1 : taps + 3, lanes(chunk)] = back_ref[:, lanes(chunk)]
        low_ref[:, cols] = dinner.astype(BF16)

        act = act_ref[:, cols]
        start = pack_row(chunk)
        code_rows = dot(code_turned_ref[...], act, 1, 0)
        rank_rows = dot(rank_turned_ref[...], dpre_ref[:, cols], 1, 0)[ranks:]
        dtx_rows = code_rows[:ranks]
        even = jnp.where(lane < edge, dtx_rows, pltpu.roll(rank_rows, edge, 1))
        odd = jnp.where(lane < edge, pltpu.roll(dtx_rows, edge, 1), rank_rows)
        for k in range(4):
            place = slice(k * 16, (k + 1) * 16)
            place_pair(
                start, 16, slice(k * LANES, (k + 1) * LANES), even[place], odd[place]
            )
        state_rows = code_rows[ranks : ranks + 2 * states]
        place_pair(
            start, 16, slice(4 * LANES, 5 * LANES), state_rows[:states], state_rows[states:]
        )

    normed = normed_ref[...]
    for part in range(2):
        grad = dot(low_ref[:, lanes(core ^ part)], normed, 0, 0)
        out_ref = (keep_ref, send_ref)[part]
        out_ref[aligned(step * span, LANES, 16), :] = grad.astype(BF16)
    width = total_ref.shape[1]
    total_ref[...] += dot(low_ref[...], win_ref[step].reshape(2 * LANES, width), 1, 0)

    @pl.when(step == pl.num_programs(0) - 1)
    def _():
        total = total_ref[...]
        dnormed_ref[...] = total.astype(BF16)
        x = x_ref[...].astype(F32)
        unit = x * lax.rsqrt(jnp.mean(x * x, axis=1, keepdims=True) + EPSILON)
        vec_ref[taps + 3 : taps + 4, :] = jnp.sum(total * unit, axis=0, keepdims=True)
        is_gain = lax.broadcasted_iota(jnp.int32, (8, LANES), 0) == taps + 3
        for chunk in range(chunks):
            start = pack_row(chunk)
            vec = vec_ref[:, chunk * LANES : (chunk + 1) * LANES]
            far, farther = (pltpu.roll(vec, LANES - k * edge // 2, 1) for k in (1, 2))
            even = jnp.where(is_gain & (lane >= edge // 2), far, vec)
            odd = jnp.where(is_gain & (lane < edge // 2), far, farther)
            alog = [
                alog_ref[pl.ds(q * eighth * chunks + chunk, eighth, stride=chunks), :]
                for q in range(2)
            ]
            place_pair(
                start,
                16,
                slice(5 * LANES, 6 * LANES),
                jnp.concatenate([alog[0], even]),
                jnp.concatenate([alog[1], odd]),
            )
            blank = jnp.zeros((16, 2 * LANES), F32)
            place_pair(start, 16, slice(6 * LANES, 8 * LANES), blank, blank)


def tail(
    place,
    lengths,
    code_own,
    code_other,
    sact,
    dpre,
    alog,
    back,
    dtx,
    bc_own,
    bc_other,
    decay,
    bend,
    inner,
    act,
    high,
    convw,
    normed,
    w4,
    gate_part,
    x,
):
    rows, own = act.shape
    chunks = own // LANES
    width = normed.shape[1]
    micros, _, clusters = lengths.shape
    count = rows // micros
    taps = convw.shape[0]
    ranks = dtx.shape[0]
    states = decay.shape[0] // chunks
    cols = 2 * LANES
    extent = 4 * (LANES + 32)

    def by_cols(height):
        return pl.BlockSpec((height, cols), lambda i, p: (0, i ^ p[FACE]))

    in_specs = (
        [pl.BlockSpec(memory_space=pltpu.SMEM)]
        + [whole((rows, LANES))] * 2
        + [by_cols(rows)] * 2
        + [whole(alog.shape), whole(back.shape)]
        + [whole(array.shape) for array in (dtx, bc_own, bc_other, decay)]
        + [by_cols(rows)] * 3
        + [whole(array.shape) for array in (high, convw, normed)]
        + [
            ANY,
            whole((rows, width)),
            whole((rows, width)),
        ]
    )
    return pl.pallas_call(
        functools.partial(
            tail_kernel,
            micros=micros,
            count=count,
            taps=taps,
            clusters=clusters,
            ranks=ranks,
            chunks=chunks,
            states=states,
        ),
        grid_spec=pltpu.PrefetchScalarGridSpec(
            num_scalar_prefetch=1,
            grid=(chunks // 2,),
            in_specs=in_specs,
            out_specs=[whole((extent, width)), whole((extent, width)), whole((rows, width))],
            scratch_shapes=[
                pltpu.VMEM((taps, rows, LANES), F32),
                pltpu.VMEM((rows, LANES), BF16),
                pltpu.VMEM((LANES, cols), BF16),
                pltpu.VMEM((8, own), F32),
                pltpu.VMEM((states * chunks, LANES), F32),
                pltpu.VMEM((rows, width), F32),
                pltpu.VMEM((chunks // 2, 2, LANES, width), BF16),
                pltpu.SemaphoreType.DMA((chunks // 2,)),
                pltpu.VMEM((rows, cols), BF16),
                pltpu.VMEM((LANES, rows), BF16),
                pltpu.VMEM((2 * ranks, rows), BF16),
            ],
        ),
        out_shape=[
            hbm((extent, width), BF16),
            hbm((extent, width), BF16),
            hbm((rows, width), BF16),
        ],
        compiler_params=params(34),
        cost_estimate=cost(7),
        name="tail",
    )(
        place,
        lengths,
        *in_hbm([code_own]),
        code_other,
        *in_hbm(
            (
                sact,
                dpre,
                alog,
                back,
                dtx,
                bc_own,
                bc_other,
                decay,
                bend,
                inner,
                act,
                high,
                convw,
                normed,
                w4,
                gate_part,
                x,
            )
        ),
    )


def fetch_halves(source, which, half, target_ref, sems):
    copies = []
    for k in range(target_ref.shape[0]):
        pair = pl.ds(2 * k, 2)
        block = source.at[pair, half] if which is None else source.at[which, pair, half]
        copies.append(pltpu.make_async_copy(block, target_ref.at[k], sems.at[k]))
    for copy in copies:
        copy.start()
    return copies


def products_kernel(
    place_ref,
    gated_ref,
    dgate_ref,
    out_ref,
    weight_ref,
    mixed_ref,
    dnormed_ref,
    wout_ref,
    wgate_ref,
    out_sems,
    gate_sems,
):
    half = place_ref[HALF]
    width = mixed_ref.shape[1]
    jobs = (
        (fetch_halves(out_ref, None, half, wout_ref, out_sems), gated_ref, wout_ref, mixed_ref),
        (fetch_halves(weight_ref, 1, half, wgate_ref, gate_sems), dgate_ref, wgate_ref, dnormed_ref),
    )
    for copies, left_ref, right_ref, result_ref in jobs:
        total = None
        for k, copy in enumerate(copies):
            copy.wait()
            left = left_ref[:, 2 * k * LANES : 2 * (k + 1) * LANES]
            term = dot(left, right_ref[k].reshape(-1, width), 1, 0)
            total = term if total is None else total + term
        result_ref[...] = total.astype(BF16)


def products(place, gated, dgate, wout3, w4):
    rows, own = gated.shape
    width = w4.shape[-1]
    pairs = own // (2 * LANES)
    return pl.pallas_call(
        products_kernel,
        grid_spec=pltpu.PrefetchScalarGridSpec(
            num_scalar_prefetch=1,
            grid=(1,),
            in_specs=[whole((rows, own)), whole((rows, own)), ANY, ANY],
            out_specs=[whole((rows, width))] * 2,
            scratch_shapes=[
                pltpu.VMEM((pairs, 2, LANES, width), BF16),
                pltpu.VMEM((pairs, 2, LANES, width), BF16),
                pltpu.SemaphoreType.DMA((pairs,)),
                pltpu.SemaphoreType.DMA((pairs,)),
            ],
        ),
        out_shape=[hbm((rows, width), BF16)] * 2,
        compiler_params=params(20),
        cost_estimate=cost(4),
        name="products",
    )(place, *in_hbm((gated, dgate, wout3, w4)))


def finish_kernel(x_ref, mine_ref, theirs_ref, cotan_ref, gain_ref, grad_ref):
    x = x_ref[...].astype(F32)
    scale = lax.rsqrt(jnp.mean(x * x, axis=1, keepdims=True) + EPSILON)
    unit = x * scale
    dhat = (mine_ref[...].astype(F32) + theirs_ref[...].astype(F32)) * gain_ref[...]
    grad_ref[...] = cotan_ref[...].astype(F32) + scale * (
        dhat - unit * jnp.mean(dhat * unit, axis=1, keepdims=True)
    )


def finish(x, mine, theirs, cotan, gain):
    rows, width = x.shape
    by_rows = pl.BlockSpec((rows // 4, width), lambda i: (i, 0))
    return pl.pallas_call(
        finish_kernel,
        grid=(4,),
        in_specs=[by_rows] * 4 + [whole(gain.shape)],
        out_specs=by_rows,
        out_shape=jax.ShapeDtypeStruct((rows, width), F32),
        compiler_params=params(16),
        cost_estimate=cost(0),
        name="finish",
    )(*in_hbm((x, mine)), theirs, *in_hbm((cotan, gain)))


def unpack_kernel(
    near_ref,
    far_ref,
    out_ref,
    dtx_ref,
    dt_ref,
    bc_ref,
    alog_ref,
    convw_ref,
    convb_ref,
    bias_ref,
    skip_ref,
    out_grad_ref,
    *,
    eighth,
    taps,
    edge,
):
    pack = near_ref[...].astype(F32) + far_ref[...].astype(F32)
    turned = jnp.concatenate([pack[:, k * LANES : (k + 1) * LANES] for k in range(4)]).T
    dtx_ref[...] = turned[:edge]
    dt_ref[...] = turned[edge:]
    rows = pack[:, 4 * LANES : 5 * LANES]
    bc_ref[0] = rows[:eighth]
    bc_ref[1] = rows[eighth:]
    rows = pack[:, 5 * LANES : 6 * LANES]
    alog_ref[...] = rows[:eighth]
    vec = rows[eighth:, :edge]
    convw_ref[...] = vec[:taps]
    convb_ref[...] = vec[taps : taps + 1]
    bias_ref[...] = vec[taps + 1 : taps + 2]
    skip_ref[...] = vec[taps + 2 : taps + 3]
    out_grad_ref[...] = out_ref[...].astype(F32)


def unpack(near, far, out, eighth, taps, ranks):
    edge = LANES // 2
    shapes = [
        (edge, ranks),
        (edge, ranks),
        (2, eighth, LANES),
        (eighth, LANES),
        (taps, edge),
        (1, edge),
        (1, edge),
        (1, edge),
        out.shape,
    ]
    return pl.pallas_call(
        functools.partial(unpack_kernel, eighth=eighth, taps=taps, edge=edge),
        grid=(1,),
        in_specs=[whole(array.shape) for array in (near, far, out)],
        out_specs=[whole(shape) for shape in shapes],
        out_shape=[jax.ShapeDtypeStruct(shape, F32) for shape in shapes],
        cost_estimate=cost(0),
        name="unpack",
    )(near, far, out)


def swap_pair(array):
    count = lax.axis_size("state")
    return lax.ppermute(array, "state", [(pos, pos ^ 1) for pos in range(count)])


def swap_bit(array, bits):
    return lax.ppermute(array, "dp", [(pos, pos ^ bits) for pos in range(lax.axis_size("dp"))])


def swap_both(array, bits=0):
    states = lax.axis_size("state")
    pairs = []
    for d in range(lax.axis_size("dp")):
        for s in range(states):
            pairs.append((d * states + s, (((d & ~1) | s) ^ bits) * states + (d & 1)))
    return lax.ppermute(array, ("dp", "state"), pairs)


def add_mixed(x, mine, theirs):
    return (x.astype(F32) + (mine.astype(F32) + theirs.astype(F32))).astype(BF16)


def add_quarters(kept, got, start=0, stop=None):
    extent = kept.shape[0] // 4
    stop = extent if stop is None else stop
    return [
        kept[k * extent + start : k * extent + stop] + got[k * extent + start : k * extent + stop]
        for k in range(4)
    ]


def trade_quarters(quarters):
    return [quarters[0]] + [swap_bit(quarters[k], k * X_BIT) for k in range(1, 4)]


def sum_quarters(quarters):
    left, right = (quarters[k].astype(F32) + quarters[k + 1].astype(F32) for k in (0, 2))
    return (left + right).astype(BF16)


CORE_BIT, X_BIT, ZH_BIT = 1, 2, 8


def shards(
    tokens,
    cluster_len,
    norm_gain,
    in_weight,
    conv_weight,
    conv_bias,
    dtx_weight,
    dt_weight,
    dt_bias,
    bc_weight,
    a_log,
    skip_gain,
    out_weight,
    cotangent,
):
    micros, count, width = tokens.shape
    inner = out_weight.shape[0]
    taps = conv_weight.shape[0]
    ranks = dtx_weight.shape[1]
    chunks = inner // (2 * LANES)
    own = chunks * LANES
    rows = micros * count
    edge = LANES // 2
    span = LANES + 32
    dp_parts = lax.axis_size("dp")
    state_count = lax.axis_size("state")
    dp_pos = lax.axis_index("dp")
    state_pos = lax.axis_index("state")
    half = state_pos & 1
    fast = state_count == 2 and dp_parts == 2 * chunks == 16
    if fast:
        place = jnp.stack([half, dp_pos & 1, dp_pos >> 1, (dp_pos >> 1) & 3])
        bc_own, alog_own = bc_weight, a_log
        bc_other, alog_other = swap_pair(bc_weight), swap_pair(a_log)
    else:
        place = jnp.stack([half, 0, 0, 0])
        bc_all = lax.all_gather(bc_weight, "state", axis=1, tiled=True)
        alog_all = lax.all_gather(a_log, "state", axis=0, tiled=True)
        eighth = alog_all.shape[0] // 2
        bc_own, bc_other = (
            lax.dynamic_slice_in_dim(bc_all, which * eighth, eighth, 1)
            for which in (half, 1 - half)
        )
        alog_own, alog_other = (
            lax.dynamic_slice_in_dim(alog_all, which * eighth, eighth, 0)
            for which in (half, 1 - half)
        )
    place = place.astype(jnp.int32)
    eighth = alog_own.shape[0]
    states = 2 * eighth

    x = tokens.reshape(rows, width)
    cotan = cotangent.reshape(rows, width)
    w4 = in_weight.reshape(2, chunks, 2, LANES, width)
    wout3 = out_weight.reshape(chunks, 2, LANES, width)
    dtx, dt = dtx_weight.T, dt_weight.T
    bias = dt_bias.reshape(-1, LANES)
    skip = skip_gain.reshape(-1, LANES)

    normed, act_all, act, inner_own, bend, gate = project(
        place, cluster_len, x, norm_gain[None], w4, conv_weight, conv_bias.reshape(-1, LANES)
    )
    bc, rank, high, decay, sp, u, step, slope, h, dy, gated, dgate, keep, send = scan_forward(
        place,
        cluster_len,
        act_all,
        bc_own,
        bc_other,
        alog_own,
        alog_other,
        dtx,
        dt,
        bias,
        skip,
        act,
        gate,
        wout3,
        cotan,
        normed,
    )
    if fast:
        early = swap_bit(send, CORE_BIT)
    mixed_part, dn_gate = products(place, gated, dgate, wout3, w4)
    if fast:
        *quarters, mixed_part, dn_gate, sp = lax.optimization_barrier(
            (*add_quarters(keep, early), mixed_part, dn_gate, sp)
        )
        early_got = trade_quarters(quarters)
    code_own, sact, dpre, alog, back = scan_backward(
        place, micros, bc, decay, dt, skip, act, sp, u, step, slope, dy, h
    )
    if fast:
        *early_got, code_own, mixed_part = lax.optimization_barrier(
            (*early_got, code_own, mixed_part)
        )
    code_other = swap_pair(code_own)
    mixed_other = swap_pair(mixed_part)
    if fast:
        block = sum_quarters(early_got)
        out_keep, out_send, gate_sum = block[:edge], block[edge:LANES], block[LANES:]
        out_send, gate_sum, bend = lax.optimization_barrier((out_send, gate_sum, bend))
        out_got = swap_bit(out_send, ZH_BIT)
    late_keep, late_send, dnormed_part = tail(
        place,
        cluster_len,
        code_own,
        code_other,
        sact,
        dpre,
        alog,
        back,
        dtx,
        bc_own,
        bc_other,
        decay,
        bend,
        inner_own,
        act,
        high,
        conv_weight,
        normed,
        w4,
        dn_gate,
        x,
    )
    mixed = add_mixed(x, mixed_part, mixed_other)
    if fast:
        late_send, mixed_other = lax.optimization_barrier((late_send, mixed_other))
        mixed = add_mixed(x, mixed_part, mixed_other)
        late = swap_bit(late_send, CORE_BIT)
        late_got = trade_quarters(add_quarters(late_keep, late))
    dnormed_other = swap_pair(dnormed_part)
    tokens_grad = finish(x, dnormed_part, dnormed_other, cotan, norm_gain[None])
    if fast:
        out_own = swap_both(out_keep + out_got)
        *late_got, out_own, tokens_grad, mixed = lax.optimization_barrier(
            (*late_got, out_own, tokens_grad, mixed)
        )
        block = sum_quarters(late_got)
        inner_sum = block[:LANES]
        upper = dp_pos >= dp_parts // 2
        crossing = jnp.where(upper, inner_sum, gate_sum)
        first, second = crossing[:edge], crossing[edge:]
        first, pack_far, pack_near = lax.optimization_barrier(
            (first, block[-16:], block[LANES:-16])
        )
        pack_far = swap_both(pack_far, ZH_BIT)
        first_got = swap_bit(first, ZH_BIT)
        pack_near = swap_both(pack_near)
        first_got, pack_far, pack_near = lax.optimization_barrier((first_got, pack_far, pack_near))
        second_got = swap_bit(second, ZH_BIT)
        gain_mine = (
            pack_near[:, 5 * LANES : 6 * LANES].astype(F32)
            + pack_far[:, 5 * LANES : 6 * LANES].astype(F32)
        ).astype(BF16)
        gain_both = gain_mine[-1].astype(F32) + swap_bit(gain_mine, CORE_BIT)[-1].astype(F32)
        extent = width // (dp_parts * state_count)
        gain_grad = lax.dynamic_slice_in_dim(gain_both, (dp_pos & 1) * extent, extent, 0)
        (
            dtx_grad,
            dt_grad,
            bc_grad,
            alog_grad,
            convw_grad,
            convb_grad,
            bias_grad,
            skip_grad,
            out_own,
        ) = unpack(pack_near, pack_far, out_own, eighth, taps, ranks)
        convb_grad, bias_grad, skip_grad = (
            array[0] for array in (convb_grad, bias_grad, skip_grad)
        )
        second_got, dtx_grad, dt_grad, out_own = lax.optimization_barrier(
            (second_got, dtx_grad, dt_grad, out_own)
        )
        in_grad = jnp.where(upper, gate_sum, inner_sum).astype(F32) + jnp.concatenate(
            [first_got, second_got]
        ).astype(F32)
    mixed = mixed.reshape(micros, count, width)
    tokens_grad = tokens_grad.reshape(micros, count, width)

    if not fast:
        def total(array):
            return lax.psum(array.astype(F32), "dp")

        def both_rows(array):
            mine = array.reshape(chunks, 1, LANES, -1)
            other = swap_pair(mine)
            low = jnp.where(half == 0, mine, other)
            high = jnp.where(half == 0, other, mine)
            return jnp.concatenate([low, high], axis=1).reshape(2 * own, -1)

        every = dp_parts * state_count
        at = dp_pos * state_count + state_pos

        def cut_own(array):
            extent = array.shape[0] // every
            return lax.dynamic_slice_in_dim(array, at * extent, extent, 0)

        pair = total(jnp.stack([keep, send])).reshape(2, 2, 2, 2 * LANES, width)
        outs = pair[:, :, :, :LANES].reshape(2, 2, 2, 2, edge, width)
        outs = jnp.transpose(outs, (3, 1, 2, 0, 4, 5)).reshape(own, width)
        gates = jnp.moveaxis(pair[:, :, :, LANES:], 0, 2).reshape(own, width)
        pair = total(jnp.stack([late_keep, late_send])).reshape(2, 2, 2, span, width)
        inners = jnp.moveaxis(pair[:, :, :, :LANES], 0, 2).reshape(own, width)
        packs = pair[:, :, :, LANES:].reshape(2, 2, 2, 2, 16, width // LANES, LANES)
        packs = jnp.transpose(packs, (3, 1, 2, 0, 5, 4, 6)).reshape(chunks, 2, -1, 16, LANES)
        small = packs[:, :, :4].reshape(chunks, 2, ranks, 2, edge)
        small = both_rows(jnp.transpose(small, (0, 1, 4, 3, 2)).reshape(own, 2 * ranks))
        in_grad = cut_own(jnp.concatenate([both_rows(inners), both_rows(gates)]))
        out_own = cut_own(both_rows(outs))
        mine = cut_own(small)
        dtx_grad, dt_grad = mine[:, :ranks], mine[:, ranks:]
        vec_rows = jnp.swapaxes(packs[:, :, 5, eighth:, :edge], 2, 3).reshape(own, -1)
        gain_sum = vec_rows[:, -1].reshape(chunks, 2, 2, -1).swapaxes(1, 2).reshape(-1)
        gain_grad = cut_own(gain_sum + swap_pair(gain_sum))
        vec = cut_own(both_rows(vec_rows)).T
        state_rows = jnp.concatenate([packs[:, :, 4], packs[:, :, 5, :eighth]], axis=2)
        state_rows = state_rows.reshape(chunks, 2, 3, eighth, LANES)
        state_rows = jnp.transpose(state_rows, (0, 4, 2, 1, 3)).reshape(own, -1)
        extent = inner // dp_parts
        state_part = lax.dynamic_slice_in_dim(both_rows(state_rows), dp_pos * extent, extent, 0)
        state_part = state_part.T.reshape(3, state_count, -1, extent)
        state_part = lax.dynamic_index_in_dim(state_part, state_pos, 1, keepdims=False)
        bc_grad, alog_grad = state_part[:2], state_part[2]
        convw_grad, convb_grad, bias_grad, skip_grad = (
            vec[:taps], vec[taps], vec[taps + 1], vec[taps + 2]
        )

    return (
        mixed,
        tokens_grad,
        gain_grad,
        in_grad,
        convw_grad,
        convb_grad,
        dtx_grad,
        dt_grad,
        bias_grad,
        bc_grad,
        alog_grad,
        skip_grad,
        out_own,
    )


def solution(mesh):
    return jax.shard_map(
        shards,
        mesh=mesh,
        in_specs=(
            P(None, "dp", None),
            P(None, "dp", None),
            P(),
            P(),
            P(),
            P(),
            P(),
            P(),
            P(),
            P(None, "state", None),
            P("state", None),
            P(),
            P(),
            P(None, "dp", None),
        ),
        out_specs=(
            P(None, "dp", None),
            P(None, "dp", None),
            P(("dp", "state")),
            P(("dp", "state"), None),
            P(None, ("dp", "state")),
            P(("dp", "state")),
            P(("dp", "state"), None),
            P(("dp", "state"), None),
            P(("dp", "state")),
            P(None, "state", "dp"),
            P("state", "dp"),
            P(("dp", "state")),
            P(("dp", "state"), None),
        ),
        check_vma=False,
    )
```
